32 devices in a mesh: seq: 4 (over z), res: 8 (over y, x, core).
Axes of the slice: x: 2, y: 2, z: 4, core: 2. Of those that a mesh axis runs over, the one named last changes fastest.
Arguments:
- alignment_rows: bfloat16 [32, 512, 256], P('seq', 'res'), may hold values from -6 to 6
- pair_entries: bfloat16 [512, 512, 128], P('res', 'seq'), may hold values from -6 to 6
- combined_weight: bfloat16 [256, 1024], replicated, may hold values from -0.375 to 0.375
- output_weight: bfloat16 [256, 256], replicated, may hold values from -0.375 to 0.375
- pair_weight: float32 [128, 8], replicated, may hold values from -9 to 9
- updated_gradient: bfloat16 [32, 512, 256], P('seq', 'res'), may hold values from -6 to 6
Outputs:
- updated: bfloat16 [32, 512, 256], P('seq', 'res')
- alignment_gradient: bfloat16 [32, 512, 256], P('seq', 'res')
- pair_gradient: bfloat16 [512, 512, 128], P('res', 'seq')
- combined_weight_gradient: float32 [256, 1024], replicated
- output_weight_gradient: float32 [256, 256], replicated
- pair_weight_gradient: float32 [128, 8], replicated
The draws below stay inside these ranges and needn't reach their ends.
All inputs are finite; a program needn't handle non-finite values.
Results may differ from the reference program's by a relative error of at most 0.011.
Values may be sent and summed in bfloat16 or wider, within the bound.
No kernel may reach another device: no remote copies, remote signals or barrier semaphores. Data moves between devices by JAX's collectives and lax.ppermute only.
A program may use at most 128 MiB of HBM per device.

```python
import math
import jax
import jax.numpy as jnp
from jax import lax

ALIGNMENT_WIDTH = 256
PAIR_WIDTH = 128
HEAD_COUNT = 8
HEAD_DIM = 32
QUERY_CHANNELS = 256
SEQUENCE_TOTAL = 32
RESIDUE_TOTAL = 512


def shared_pair(key):
    basis_rows = jnp.clip(jax.random.normal(jax.random.fold_in(key, 5), (PAIR_WIDTH, HEAD_COUNT), jnp.float32), -5.0, 5.0)
    return basis_rows


def draw_pair_weight(key, part):
    basis_rows = shared_pair(key)
    drawn = basis_rows / math.sqrt(PAIR_WIDTH)
    return drawn


def draw_pair_entries(key, part):
    key = jax.random.fold_in(key, 22)
    noise_draw = jnp.clip(jax.random.normal(jax.random.fold_in(key, 1), (RESIDUE_TOTAL, RESIDUE_TOTAL, PAIR_WIDTH), jnp.float32), -6.0, 6.0)
    return noise_draw.astype(jnp.bfloat16)


def levels(own_key, extent, split, low, top_value):
    def one(dim, blocks):
        heights = jax.random.uniform(jax.random.fold_in(jax.random.fold_in(own_key, 6), dim), (blocks,), jnp.float32, low / len(split), top_value / len(split))
        return jnp.repeat(jnp.exp(heights), extent[dim] // blocks).reshape((-1,) + (1,) * (len(extent) - dim - 1))

    loudness = one(*split[0])
    for cut in split[1:]:
        loudness = loudness * one(*cut)
    return loudness


def gaussian(own_key, shape, deviation, reach, shards=(), kind=jnp.bfloat16):
    factor_of = levels(own_key, shape, shards, -0.22, 0.18) if shards else 1.0
    result = jax.random.normal(own_key, shape, jnp.float32) * deviation * factor_of
    return jnp.minimum(jnp.maximum(result, -reach), reach).astype(kind)


def setup_inputs(seed: int = 0) -> dict:
    streams_of = jax.random.split(jax.random.key(seed), 7)
    return {
        "alignment_rows": gaussian(streams_of[0], (SEQUENCE_TOTAL, RESIDUE_TOTAL, ALIGNMENT_WIDTH), 1.0, 6.0, ((0, 4), (1, 8))),
        "pair_entries": draw_pair_entries(jax.random.fold_in(streams_of[6], 71), 0),
        "combined_weight": gaussian(streams_of[2], (ALIGNMENT_WIDTH, 4 * QUERY_CHANNELS), ALIGNMENT_WIDTH ** -0.5, 0.375),
        "output_weight": gaussian(streams_of[3], (QUERY_CHANNELS, ALIGNMENT_WIDTH), QUERY_CHANNELS ** -0.5, 0.375),
        "pair_weight": draw_pair_weight(jax.random.fold_in(streams_of[6], 71), 0),
        "updated_gradient": gaussian(streams_of[5], (SEQUENCE_TOTAL, RESIDUE_TOTAL, ALIGNMENT_WIDTH), 1.0, 6.0, ((0, 4), (1, 8))),
    }


eps_norm = 1e-05

def layer_normalize(values):
    values = values.astype(jnp.float32)
    center = values - lax.optimization_barrier(jnp.mean(values, axis=-1, keepdims=True))
    broadcast_pair = lax.rsqrt(lax.optimization_barrier(jnp.mean(center * center, axis=-1, keepdims=True)) + eps_norm)
    return (center * broadcast_pair, broadcast_pair)

def layer_norm_backward(normalized_gradient, normalized_rows, broadcast_pair):
    mean_grad = lax.optimization_barrier(jnp.mean(normalized_gradient, axis=-1, keepdims=True))
    mean_cross = lax.optimization_barrier(jnp.mean(normalized_gradient * normalized_rows, axis=-1, keepdims=True))
    return broadcast_pair * (normalized_gradient - mean_grad - normalized_rows * mean_cross)

def split_heads(tensor):
    return tensor.reshape(tensor.shape[0], tensor.shape[1], HEAD_COUNT, HEAD_DIM).astype(jnp.float32)

def lowered(tensor):
    return lax.optimization_barrier(tensor.astype(jnp.bfloat16)).astype(jnp.float32)

def reference(alignment_rows, pair_entries, combined_weight, output_weight, pair_weight, updated_gradient):
    token_count = SEQUENCE_TOTAL * RESIDUE_TOTAL
    query_width = QUERY_CHANNELS
    score_scale = 1.0 / math.sqrt(HEAD_DIM * SEQUENCE_TOTAL)
    normalized_rows, broadcast_pair = layer_normalize(alignment_rows)
    normalized_rows_backward = normalized_rows.astype(jnp.bfloat16).reshape(token_count, ALIGNMENT_WIDTH)
    projected = jnp.dot(normalized_rows_backward, combined_weight, preferred_element_type=jnp.float32).reshape(SEQUENCE_TOTAL, RESIDUE_TOTAL, 4 * query_width)
    queries = (projected[..., :query_width] * score_scale).astype(jnp.bfloat16)
    key_rows = projected[..., query_width:2 * query_width].astype(jnp.bfloat16)
    value_rows = projected[..., 2 * query_width:3 * query_width].astype(jnp.bfloat16)
    gate_open = jax.nn.sigmoid(projected[..., 3 * query_width:])
    pair_normed, pair_spread = layer_normalize(pair_entries)
    pair_bias = jnp.einsum('ijc,ch->hij', pair_normed, pair_weight, precision=lax.Precision.HIGHEST)
    logits = jnp.einsum('sihd,sjhd->hij', split_heads(queries), split_heads(key_rows)) + pair_bias
    row_top = lax.optimization_barrier(jnp.max(logits, axis=-1, keepdims=True))
    lifted = jnp.exp(logits - row_top)
    softmax_out = lifted / lax.optimization_barrier(jnp.sum(lifted, axis=-1, keepdims=True))
    softmax_low = lowered(softmax_out)
    attended = jnp.einsum('hij,sjhd->sihd', softmax_low, split_heads(value_rows)).reshape(SEQUENCE_TOTAL, RESIDUE_TOTAL, query_width)
    gated_out = (gate_open * attended).astype(jnp.bfloat16)
    flattened_gated = gated_out.reshape(token_count, query_width)
    updated = jnp.dot(flattened_gated, output_weight, preferred_element_type=jnp.float32).astype(jnp.bfloat16).reshape(SEQUENCE_TOTAL, RESIDUE_TOTAL, ALIGNMENT_WIDTH)
    flattened_gradient = updated_gradient.reshape(token_count, ALIGNMENT_WIDTH)
    grad_gated = jnp.dot(flattened_gradient, output_weight.T, preferred_element_type=jnp.float32).reshape(SEQUENCE_TOTAL, RESIDUE_TOTAL, query_width)
    output_weight_gradient = jnp.dot(flattened_gated.T, flattened_gradient, preferred_element_type=jnp.float32)
    grad_attended = (grad_gated * gate_open).astype(jnp.bfloat16)
    grad_gate_logit = grad_gated * attended * gate_open * (1.0 - gate_open)
    grad_probs = jnp.einsum('sihd,sjhd->hij', split_heads(grad_attended), split_heads(value_rows))
    row_dot = lax.optimization_barrier(jnp.sum(softmax_out * grad_probs, axis=-1, keepdims=True))
    grad_logits = softmax_out * (grad_probs - row_dot)
    grad_logits_b = lowered(grad_logits)
    grad_queries = jnp.einsum('hij,sjhd->sihd', grad_logits_b, split_heads(key_rows)) * score_scale
    grad_keys = jnp.einsum('hij,sihd->sjhd', grad_logits_b, split_heads(queries))
    grad_values = jnp.einsum('hij,sihd->sjhd', softmax_low, split_heads(grad_attended))
    projected_gradient = jnp.concatenate([grad_queries.reshape(SEQUENCE_TOTAL, RESIDUE_TOTAL, query_width), grad_keys.reshape(SEQUENCE_TOTAL, RESIDUE_TOTAL, query_width), grad_values.reshape(SEQUENCE_TOTAL, RESIDUE_TOTAL, query_width), grad_gate_logit], axis=-1).astype(jnp.bfloat16).reshape(token_count, 4 * query_width)
    combined_weight_gradient = jnp.dot(normalized_rows_backward.T, projected_gradient, preferred_element_type=jnp.float32)
    normalized_gradient = jnp.dot(projected_gradient, combined_weight.T, preferred_element_type=jnp.float32).reshape(SEQUENCE_TOTAL, RESIDUE_TOTAL, ALIGNMENT_WIDTH)
    alignment_gradient = layer_norm_backward(normalized_gradient, normalized_rows, broadcast_pair).astype(jnp.bfloat16)
    pair_weight_gradient = jnp.einsum('ijc,hij->ch', pair_normed, grad_logits, precision=lax.Precision.HIGHEST)
    grad_pair_normed = jnp.einsum('hij,ch->ijc', grad_logits, pair_weight, precision=lax.Precision.HIGHEST)
    pair_gradient = layer_norm_backward(grad_pair_normed, pair_normed, pair_spread).astype(jnp.bfloat16)
    return (updated, alignment_gradient, pair_gradient, combined_weight_gradient, output_weight_gradient, pair_weight_gradient)
```

```python
import math

import jax
import jax.numpy as jnp
from jax import lax
from jax.sharding import PartitionSpec as P

eps_norm = 1e-05


def layer_normalize(values):
    values = values.astype(jnp.float32)
    center = values - jnp.mean(values, axis=-1, keepdims=True)
    broadcast_pair = lax.rsqrt(jnp.mean(center * center, axis=-1, keepdims=True) + eps_norm)
    return (center * broadcast_pair, broadcast_pair)


def layer_norm_backward(normalized_gradient, normalized_rows, broadcast_pair):
    mean_grad = jnp.mean(normalized_gradient, axis=-1, keepdims=True)
    mean_cross = jnp.mean(normalized_gradient * normalized_rows, axis=-1, keepdims=True)
    return broadcast_pair * (normalized_gradient - mean_grad - normalized_rows * mean_cross)


def split_heads(tensor, head_count):
    return tensor.reshape(
        tensor.shape[0], tensor.shape[1], head_count, tensor.shape[2] // head_count
    )


def merge_heads(tensor):
    return tensor.reshape(tensor.shape[0], tensor.shape[1], tensor.shape[2] * tensor.shape[3])


def gathered_body(
    alignment_rows, pair_entries, combined_weight, output_weight, pair_weight, updated_gradient
):
    sequence_count, residue_count, alignment_width = alignment_rows.shape
    head_count = pair_weight.shape[1]
    query_width = output_weight.shape[0]
    head_dim = query_width // head_count
    column_count = pair_entries.shape[1]
    token_count = sequence_count * residue_count
    score_scale = 1.0 / math.sqrt(head_dim * sequence_count * lax.axis_size("seq"))
    normalized_rows, broadcast_pair = layer_normalize(alignment_rows)
    normalized_rows_backward = normalized_rows.astype(jnp.bfloat16).reshape(
        token_count, alignment_width
    )
    projected = jnp.dot(
        normalized_rows_backward, combined_weight, preferred_element_type=jnp.float32
    ).reshape(sequence_count, residue_count, 4 * query_width)
    queries = (projected[..., :query_width] * score_scale).astype(jnp.bfloat16)
    key_rows = projected[..., query_width : 2 * query_width].astype(jnp.bfloat16)
    value_rows = projected[..., 2 * query_width : 3 * query_width].astype(jnp.bfloat16)
    gate_open = jax.nn.sigmoid(projected[..., 3 * query_width :])
    all_keys, all_values = (
        lax.all_gather(key_rows, "res", axis=1, tiled=True),
        lax.all_gather(value_rows, "res", axis=1, tiled=True),
    )
    query_heads = split_heads(queries, head_count)
    key_heads = split_heads(all_keys, head_count)
    value_heads = split_heads(all_values, head_count)
    score_terms = jnp.einsum(
        "sihd,sjhd->hij", query_heads, key_heads, preferred_element_type=jnp.float32
    )
    pair_normed, pair_spread = layer_normalize(pair_entries)
    pair_bias = jnp.einsum("ijc,ch->hij", pair_normed, pair_weight, precision=lax.Precision.HIGHEST)
    col_start = lax.axis_index("seq") * column_count
    own_block = lax.dynamic_slice_in_dim(score_terms, col_start, column_count, 2) + pair_bias
    logits = lax.psum(lax.dynamic_update_slice_in_dim(score_terms, own_block, col_start, 2), "seq")
    row_top = jnp.max(logits, axis=-1, keepdims=True)
    lifted = jnp.exp(logits - row_top)
    softmax_out = lifted / jnp.sum(lifted, axis=-1, keepdims=True)
    softmax_low = softmax_out.astype(jnp.bfloat16)
    attended = merge_heads(
        jnp.einsum("hij,sjhd->sihd", softmax_low, value_heads, preferred_element_type=jnp.float32)
    )
    gated_out = (gate_open * attended).astype(jnp.bfloat16)
    flattened_gated = gated_out.reshape(token_count, query_width)
    updated = (
        jnp.dot(flattened_gated, output_weight, preferred_element_type=jnp.float32)
        .astype(jnp.bfloat16)
        .reshape(sequence_count, residue_count, alignment_width)
    )
    flattened_gradient = updated_gradient.reshape(token_count, alignment_width)
    grad_gated = jnp.dot(
        flattened_gradient, output_weight.T, preferred_element_type=jnp.float32
    ).reshape(sequence_count, residue_count, query_width)
    out_local = jnp.dot(flattened_gated.T, flattened_gradient, preferred_element_type=jnp.float32)
    grad_attended = (grad_gated * gate_open).astype(jnp.bfloat16)
    grad_gate_logit = grad_gated * attended * gate_open * (1.0 - gate_open)
    attended_grad_heads = split_heads(grad_attended, head_count)
    grad_terms = jnp.einsum(
        "sihd,sjhd->hij", attended_grad_heads, value_heads, preferred_element_type=jnp.float32
    )
    grad_probs = lax.psum(grad_terms, "seq")
    row_dot = jnp.sum(softmax_out * grad_probs, axis=-1, keepdims=True)
    grad_logits = softmax_out * (grad_probs - row_dot)
    grad_logits_b = grad_logits.astype(jnp.bfloat16)
    logit_share = lax.dynamic_slice_in_dim(grad_logits, col_start, column_count, 2)
    grad_query_heads = (
        jnp.einsum("hij,sjhd->sihd", grad_logits_b, key_heads, preferred_element_type=jnp.float32)
        * score_scale
    )
    key_part = jnp.einsum(
        "hij,sihd->jshd", grad_logits_b, query_heads, preferred_element_type=jnp.float32
    )
    value_part = jnp.einsum(
        "hij,sihd->jshd", softmax_low, attended_grad_heads, preferred_element_type=jnp.float32
    )
    summed = lax.psum_scatter(
        jnp.concatenate([merge_heads(key_part), merge_heads(value_part)], axis=-1),
        "res",
        scatter_dimension=0,
        tiled=True,
    )
    key_value_grads = jnp.transpose(summed, (1, 0, 2))
    projected_gradient = jnp.concatenate(
        [merge_heads(grad_query_heads), key_value_grads, grad_gate_logit], axis=-1
    )
    projected_gradient = projected_gradient.astype(jnp.bfloat16).reshape(
        token_count, 4 * query_width
    )
    qkvg_local = jnp.dot(
        normalized_rows_backward.T, projected_gradient, preferred_element_type=jnp.float32
    )
    normalized_gradient = jnp.dot(
        projected_gradient, combined_weight.T, preferred_element_type=jnp.float32
    ).reshape(sequence_count, residue_count, alignment_width)
    alignment_gradient = layer_norm_backward(
        normalized_gradient, normalized_rows, broadcast_pair
    ).astype(jnp.bfloat16)
    pair_w_local = jnp.einsum(
        "ijc,hij->ch", pair_normed, logit_share, precision=lax.Precision.HIGHEST
    )
    grad_pair_normed = jnp.einsum(
        "hij,ch->ijc", logit_share, pair_weight, precision=lax.Precision.HIGHEST
    )
    pair_gradient = layer_norm_backward(grad_pair_normed, pair_normed, pair_spread).astype(
        jnp.bfloat16
    )
    combined_weight_gradient, output_weight_gradient, pair_weight_gradient = lax.psum(
        (qkvg_local, out_local, pair_w_local), ("seq", "res")
    )
    return (
        updated,
        alignment_gradient,
        pair_gradient,
        combined_weight_gradient,
        output_weight_gradient,
        pair_weight_gradient,
    )


def shifted_rows(mine, axis_size, axis_name):
    return [
        lax.ppermute(mine[k], axis_name, [(a, (a + k) % axis_size) for a in range(axis_size)])
        for k in range(1, axis_size)
    ]


def gathered(mine, seq_size, seq_index):
    rows = jnp.zeros((seq_size,) + mine.shape, mine.dtype)
    rows = lax.dynamic_update_index_in_dim(rows, mine, seq_index, 0)
    for k, t in enumerate(shifted_rows([mine] * seq_size, seq_size, "seq"), 1):
        rows = lax.dynamic_update_index_in_dim(rows, t, (seq_index - k) % seq_size, 0)
    return rows


def head_body(
    alignment_rows, pair_entries, combined_weight, output_weight, pair_weight, updated_gradient
):
    sequence_count, residue_count, alignment_width = alignment_rows.shape
    head_count = pair_weight.shape[1]
    query_width = output_weight.shape[0]
    head_dim = query_width // head_count
    column_count = pair_entries.shape[1]
    pair_width = pair_entries.shape[2]
    token_count = sequence_count * residue_count
    seq_size = lax.axis_size("seq")
    seq_index = lax.axis_index("seq")
    residue_total = residue_count * head_count
    row_count = residue_total // seq_size
    depth = sequence_count * head_dim
    score_scale = 1.0 / math.sqrt(head_dim * sequence_count * seq_size)

    normalized_rows, broadcast_pair = layer_normalize(alignment_rows)
    normed_b = normalized_rows.astype(jnp.bfloat16).reshape(token_count, alignment_width)
    projected = jnp.dot(normed_b, combined_weight, preferred_element_type=jnp.float32)
    gate_open = jax.nn.sigmoid(projected[:, 3 * query_width :])
    flattened_gradient = updated_gradient.reshape(token_count, alignment_width)
    grad_gated = jnp.dot(flattened_gradient, output_weight.T, preferred_element_type=jnp.float32)

    def to_heads(tensors):
        blocks = jnp.stack(
            [
                t.astype(jnp.bfloat16).reshape(sequence_count, residue_count, head_count, head_dim)
                for t in tensors
            ]
        )
        blocks = jnp.transpose(blocks, (3, 0, 2, 1, 4)).reshape(
            head_count, len(tensors), residue_count, depth
        )
        blocks = lax.all_to_all(blocks, "res", 0, 0, tiled=True)
        return [
            blocks[:, t].reshape(residue_total, depth) for t in range(len(tensors))
        ]

    queries, keys = to_heads(
        [projected[:, :query_width] * score_scale, projected[:, query_width : 2 * query_width]]
    )
    values, grad_attended = to_heads(
        [projected[:, 2 * query_width : 3 * query_width], grad_gated * gate_open]
    )

    pair_normed, pair_spread = layer_normalize(pair_entries)
    pair_bias = jnp.einsum("ijc,ch->hij", pair_normed, pair_weight, precision=lax.Precision.HIGHEST)
    bias = lax.all_to_all(pair_bias, "res", 0, 0, tiled=True).reshape(residue_total, column_count)

    col_start = seq_index * column_count
    score_terms = jnp.dot(queries, keys.T, preferred_element_type=jnp.float32)
    own_block = lax.dynamic_slice_in_dim(score_terms, col_start, column_count, 1) + bias
    score_terms = lax.dynamic_update_slice_in_dim(score_terms, own_block, col_start, 1)
    grad_terms = jnp.dot(grad_attended, values.T, preferred_element_type=jnp.float32)

    def row_sums(terms, kind):
        blocks = terms.reshape(seq_size, row_count, residue_total)
        pick = lambda k: lax.dynamic_index_in_dim(blocks, (seq_index + k) % seq_size, 0, False)
        sent = [pick(k).astype(kind) for k in range(seq_size)]
        return sum((t.astype(jnp.float32) for t in shifted_rows(sent, seq_size, "seq")), pick(0))

    def all_rows(mine):
        return gathered(mine, seq_size, seq_index).reshape(residue_total, residue_total)

    logits = row_sums(score_terms, jnp.float32)
    grad_probs = row_sums(grad_terms, jnp.bfloat16)
    row_top = jnp.max(logits, axis=-1, keepdims=True)
    lifted = jnp.exp(logits - row_top)
    softmax_out = lifted / jnp.sum(lifted, axis=-1, keepdims=True)
    probs = all_rows(softmax_out.astype(jnp.bfloat16))
    row_dot = jnp.sum(softmax_out * grad_probs, axis=-1, keepdims=True)
    grad_logits = all_rows((softmax_out * (grad_probs - row_dot)).astype(jnp.bfloat16))

    def to_residues(tensors):
        blocks = jnp.stack(
            [t.astype(jnp.bfloat16).reshape(head_count, residue_count, depth) for t in tensors], 1
        )
        blocks = lax.all_to_all(blocks, "res", 0, 0, tiled=True)
        blocks = blocks.reshape(
            head_count, len(tensors), residue_count, sequence_count, head_dim
        )
        blocks = jnp.transpose(blocks, (1, 3, 2, 0, 4))
        return [blocks[t].reshape(token_count, query_width) for t in range(len(tensors))]

    attended, grad_values = to_residues(
        [
            jnp.dot(probs, values, preferred_element_type=jnp.float32),
            jnp.dot(probs.T, grad_attended, preferred_element_type=jnp.float32),
        ]
    )
    grad_queries, grad_keys = to_residues(
        [
            jnp.dot(grad_logits, keys, preferred_element_type=jnp.float32) * score_scale,
            jnp.dot(grad_logits.T, queries, preferred_element_type=jnp.float32),
        ]
    )
    logit_share = lax.dynamic_slice_in_dim(grad_logits, col_start, column_count, 1).reshape(
        head_count, residue_count, column_count
    )
    logit_share = lax.all_to_all(logit_share, "res", 0, 0, tiled=True).astype(jnp.float32)

    attended = attended.astype(jnp.float32)
    gated_out = (gate_open * attended).astype(jnp.bfloat16)
    updated = jnp.dot(gated_out, output_weight, preferred_element_type=jnp.float32).astype(
        jnp.bfloat16
    )
    out_local = jnp.dot(gated_out.T, flattened_gradient, preferred_element_type=jnp.float32)
    grad_gate_logit = grad_gated * attended * gate_open * (1.0 - gate_open)
    projected_gradient = jnp.concatenate(
        [grad_queries, grad_keys, grad_values, grad_gate_logit.astype(jnp.bfloat16)], axis=-1
    )
    qkvg_local = jnp.dot(normed_b.T, projected_gradient, preferred_element_type=jnp.float32)
    normalized_gradient = jnp.dot(
        projected_gradient, combined_weight.T, preferred_element_type=jnp.float32
    ).reshape(alignment_rows.shape)
    alignment_gradient = layer_norm_backward(
        normalized_gradient, normalized_rows, broadcast_pair
    ).astype(jnp.bfloat16)
    pair_w_local = jnp.einsum(
        "ijc,hij->hc", pair_normed, logit_share, precision=lax.Precision.HIGHEST
    )

    weight_rows = alignment_width // head_count
    parts = jnp.concatenate(
        [
            qkvg_local.reshape(head_count, weight_rows, 4 * query_width),
            out_local.reshape(head_count, weight_rows, alignment_width),
            jnp.pad(pair_w_local[:, None, :], ((0, 0), (0, weight_rows - 1), (0, 0))),
        ],
        axis=-1,
    ).astype(jnp.bfloat16)
    part = jnp.sum(lax.all_to_all(parts, "res", 0, 0, tiled=True).astype(jnp.float32), axis=0)
    sent = part.astype(jnp.bfloat16)
    part = jnp.sum(gathered(sent, seq_size, seq_index).astype(jnp.float32), axis=0)
    whole = lax.all_gather(part.astype(jnp.bfloat16), "res", axis=0).astype(jnp.float32)
    wide = 4 * query_width + alignment_width
    combined_weight_gradient = whole[:, :, : 4 * query_width].reshape(combined_weight.shape)
    output_weight_gradient = whole[:, :, 4 * query_width : wide].reshape(output_weight.shape)
    pair_weight_gradient = whole[:, 0, wide:].T

    grad_pair_normed = jnp.einsum(
        "hij,ch->ijc", logit_share, pair_weight, precision=lax.Precision.HIGHEST
    )
    pair_gradient = layer_norm_backward(grad_pair_normed, pair_normed, pair_spread).astype(
        jnp.bfloat16
    )
    return (
        updated.reshape(alignment_rows.shape),
        alignment_gradient,
        pair_gradient,
        combined_weight_gradient,
        output_weight_gradient,
        pair_weight_gradient,
    )


def body(alignment_rows, pair_entries, combined_weight, output_weight, pair_weight, updated_gradient):
    one_head = pair_weight.shape[1] == lax.axis_size("res")
    chosen = head_body if one_head else gathered_body
    return chosen(
        alignment_rows, pair_entries, combined_weight, output_weight, pair_weight, updated_gradient
    )


def solution(mesh):
    return jax.shard_map(
        body,
        mesh=mesh,
        in_specs=(
            P("seq", "res", None),
            P("res", "seq", None),
            P(),
            P(),
            P(),
            P("seq", "res", None),
        ),
        out_specs=(
            P("seq", "res", None),
            P("seq", "res", None),
            P("res", "seq", None),
            P(),
            P(),
            P(),
        ),
        check_vma=False,
    )
```

```python
import math

import jax
import jax.numpy as jnp
from jax import lax
from jax.sharding import PartitionSpec as P

eps_norm = 1e-05


def layer_normalize(values):
    values = values.astype(jnp.float32)
    center = values - jnp.mean(values, axis=-1, keepdims=True)
    broadcast_pair = lax.rsqrt(jnp.mean(center * center, axis=-1, keepdims=True) + eps_norm)
    return (center * broadcast_pair, broadcast_pair)


def layer_norm_backward(normalized_gradient, normalized_rows, broadcast_pair):
    mean_grad = jnp.mean(normalized_gradient, axis=-1, keepdims=True)
    mean_cross = jnp.mean(normalized_gradient * normalized_rows, axis=-1, keepdims=True)
    return broadcast_pair * (normalized_gradient - mean_grad - normalized_rows * mean_cross)


def split_heads(tensor, head_count):
    return tensor.reshape(
        tensor.shape[0], tensor.shape[1], head_count, tensor.shape[2] // head_count
    )


def merge_heads(tensor):
    return tensor.reshape(tensor.shape[0], tensor.shape[1], tensor.shape[2] * tensor.shape[3])


def gathered_body(
    alignment_rows, pair_entries, combined_weight, output_weight, pair_weight, updated_gradient
):
    sequence_count, residue_count, alignment_width = alignment_rows.shape
    head_count = pair_weight.shape[1]
    query_width = output_weight.shape[0]
    head_dim = query_width // head_count
    column_count = pair_entries.shape[1]
    token_count = sequence_count * residue_count
    score_scale = 1.0 / math.sqrt(head_dim * sequence_count * lax.axis_size("seq"))
    normalized_rows, broadcast_pair = layer_normalize(alignment_rows)
    normalized_rows_backward = normalized_rows.astype(jnp.bfloat16).reshape(
        token_count, alignment_width
    )
    projected = jnp.dot(
        normalized_rows_backward, combined_weight, preferred_element_type=jnp.float32
    ).reshape(sequence_count, residue_count, 4 * query_width)
    queries = (projected[..., :query_width] * score_scale).astype(jnp.bfloat16)
    key_rows = projected[..., query_width : 2 * query_width].astype(jnp.bfloat16)
    value_rows = projected[..., 2 * query_width : 3 * query_width].astype(jnp.bfloat16)
    gate_open = jax.nn.sigmoid(projected[..., 3 * query_width :])
    all_keys, all_values = (
        lax.all_gather(key_rows, "res", axis=1, tiled=True),
        lax.all_gather(value_rows, "res", axis=1, tiled=True),
    )
    query_heads = split_heads(queries, head_count)
    key_heads = split_heads(all_keys, head_count)
    value_heads = split_heads(all_values, head_count)
    score_terms = jnp.einsum(
        "sihd,sjhd->hij", query_heads, key_heads, preferred_element_type=jnp.float32
    )
    pair_normed, pair_spread = layer_normalize(pair_entries)
    pair_bias = jnp.einsum("ijc,ch->hij", pair_normed, pair_weight, precision=lax.Precision.HIGHEST)
    col_start = lax.axis_index("seq") * column_count
    own_block = lax.dynamic_slice_in_dim(score_terms, col_start, column_count, 2) + pair_bias
    logits = lax.psum(lax.dynamic_update_slice_in_dim(score_terms, own_block, col_start, 2), "seq")
    row_top = jnp.max(logits, axis=-1, keepdims=True)
    lifted = jnp.exp(logits - row_top)
    softmax_out = lifted / jnp.sum(lifted, axis=-1, keepdims=True)
    softmax_low = softmax_out.astype(jnp.bfloat16)
    attended = merge_heads(
        jnp.einsum("hij,sjhd->sihd", softmax_low, value_heads, preferred_element_type=jnp.float32)
    )
    gated_out = (gate_open * attended).astype(jnp.bfloat16)
    flattened_gated = gated_out.reshape(token_count, query_width)
    updated = (
        jnp.dot(flattened_gated, output_weight, preferred_element_type=jnp.float32)
        .astype(jnp.bfloat16)
        .reshape(sequence_count, residue_count, alignment_width)
    )
    flattened_gradient = updated_gradient.reshape(token_count, alignment_width)
    grad_gated = jnp.dot(
        flattened_gradient, output_weight.T, preferred_element_type=jnp.float32
    ).reshape(sequence_count, residue_count, query_width)
    out_local = jnp.dot(flattened_gated.T, flattened_gradient, preferred_element_type=jnp.float32)
    grad_attended = (grad_gated * gate_open).astype(jnp.bfloat16)
    grad_gate_logit = grad_gated * attended * gate_open * (1.0 - gate_open)
    attended_grad_heads = split_heads(grad_attended, head_count)
    grad_terms = jnp.einsum(
        "sihd,sjhd->hij", attended_grad_heads, value_heads, preferred_element_type=jnp.float32
    )
    grad_probs = lax.psum(grad_terms, "seq")
    row_dot = jnp.sum(softmax_out * grad_probs, axis=-1, keepdims=True)
    grad_logits = softmax_out * (grad_probs - row_dot)
    grad_logits_b = grad_logits.astype(jnp.bfloat16)
    logit_share = lax.dynamic_slice_in_dim(grad_logits, col_start, column_count, 2)
    grad_query_heads = (
        jnp.einsum("hij,sjhd->sihd", grad_logits_b, key_heads, preferred_element_type=jnp.float32)
        * score_scale
    )
    key_part = jnp.einsum(
        "hij,sihd->jshd", grad_logits_b, query_heads, preferred_element_type=jnp.float32
    )
    value_part = jnp.einsum(
        "hij,sihd->jshd", softmax_low, attended_grad_heads, preferred_element_type=jnp.float32
    )
    summed = lax.psum_scatter(
        jnp.concatenate([merge_heads(key_part), merge_heads(value_part)], axis=-1),
        "res",
        scatter_dimension=0,
        tiled=True,
    )
    key_value_grads = jnp.transpose(summed, (1, 0, 2))
    projected_gradient = jnp.concatenate(
        [merge_heads(grad_query_heads), key_value_grads, grad_gate_logit], axis=-1
    )
    projected_gradient = projected_gradient.astype(jnp.bfloat16).reshape(
        token_count, 4 * query_width
    )
    qkvg_local = jnp.dot(
        normalized_rows_backward.T, projected_gradient, preferred_element_type=jnp.float32
    )
    normalized_gradient = jnp.dot(
        projected_gradient, combined_weight.T, preferred_element_type=jnp.float32
    ).reshape(sequence_count, residue_count, alignment_width)
    alignment_gradient = layer_norm_backward(
        normalized_gradient, normalized_rows, broadcast_pair
    ).astype(jnp.bfloat16)
    pair_w_local = jnp.einsum(
        "ijc,hij->ch", pair_normed, logit_share, precision=lax.Precision.HIGHEST
    )
    grad_pair_normed = jnp.einsum(
        "hij,ch->ijc", logit_share, pair_weight, precision=lax.Precision.HIGHEST
    )
    pair_gradient = layer_norm_backward(grad_pair_normed, pair_normed, pair_spread).astype(
        jnp.bfloat16
    )
    combined_weight_gradient, output_weight_gradient, pair_weight_gradient = lax.psum(
        (qkvg_local, out_local, pair_w_local), ("seq", "res")
    )
    return (
        updated,
        alignment_gradient,
        pair_gradient,
        combined_weight_gradient,
        output_weight_gradient,
        pair_weight_gradient,
    )


def swapped(mine, axis_name, distance):
    size = lax.axis_size(axis_name)
    return lax.ppermute(mine, axis_name, [(a, a ^ distance) for a in range(size)])


def gathered_seq(mine):
    size, index = lax.axis_size("seq"), lax.axis_index("seq")
    rows = jnp.zeros((size,) + mine.shape, mine.dtype)
    rows = lax.dynamic_update_index_in_dim(rows, mine, index, 0)
    for k in range(1, size):
        t = lax.ppermute(mine, "seq", [(a, (a + k) % size) for a in range(size)])
        rows = lax.dynamic_update_index_in_dim(rows, t, (index - k) % size, 0)
    return rows


def summed_everywhere(parts):
    parts = lax.all_to_all(parts.astype(jnp.bfloat16), "res", 0, 0, tiled=True)
    part = jnp.sum(parts.astype(jnp.float32), axis=0).astype(jnp.bfloat16)
    part = jnp.sum(gathered_seq(part).astype(jnp.float32), axis=0).astype(jnp.bfloat16)
    return lax.all_gather(part, "res", axis=0).astype(jnp.float32)


def head_body(
    alignment_rows, pair_entries, combined_weight, output_weight, pair_weight, updated_gradient
):
    sequence_count, residue_count, alignment_width = alignment_rows.shape
    head_count = pair_weight.shape[1]
    query_width = output_weight.shape[0]
    head_dim = query_width // head_count
    column_count = pair_entries.shape[1]
    token_count = sequence_count * residue_count
    seq_size, res_size = lax.axis_size("seq"), lax.axis_size("res")
    seq_index = lax.axis_index("seq")
    core = lax.axis_index("res") % 2
    half = seq_index // 2
    residue_total = residue_count * res_size
    half_seqs = sequence_count // 2
    half_rows = residue_count // 2
    depth = half_seqs * head_dim
    group = 2 * res_size
    groups = [[g * group + k for k in range(group)] for g in range(seq_size // 2)]
    score_scale = 1.0 / math.sqrt(head_dim * sequence_count * seq_size)

    def across(blocks):
        return lax.all_to_all(
            blocks, ("seq", "res"), 0, 0, axis_index_groups=groups, tiled=True
        )

    normalized_rows, broadcast_pair = layer_normalize(alignment_rows)
    normed_b = normalized_rows.astype(jnp.bfloat16).reshape(token_count, alignment_width)
    projected = jnp.dot(normed_b, combined_weight, preferred_element_type=jnp.float32)
    gate_open = jax.nn.sigmoid(projected[:, 3 * query_width :])
    flattened_gradient = updated_gradient.reshape(token_count, alignment_width)
    grad_gated = jnp.dot(flattened_gradient, output_weight.T, preferred_element_type=jnp.float32)

    def to_heads(tensors):
        blocks = jnp.stack(
            [
                t.astype(jnp.bfloat16).reshape(2, half_seqs, residue_count, head_count, head_dim)
                for t in tensors
            ]
        )
        blocks = jnp.transpose(blocks, (4, 1, 0, 3, 2, 5)).reshape(
            group, len(tensors), residue_count, depth
        )
        blocks = across(blocks).reshape(2, res_size, len(tensors), residue_count, depth)
        blocks = jnp.transpose(blocks, (2, 1, 3, 0, 4))
        return [blocks[t].reshape(residue_total, 2 * depth) for t in range(len(tensors))]

    def rows_of(tensor, which):
        blocks = tensor.reshape(res_size, 2, half_rows, tensor.shape[1])
        return lax.dynamic_index_in_dim(blocks, which, 1, False).reshape(
            residue_total // 2, tensor.shape[1]
        )

    def products(left, right):
        own = jnp.dot(rows_of(left, core), right.T, preferred_element_type=jnp.float32)
        other_rows = swapped(rows_of(left, 1 - core), "res", 1)
        other = swapped(right, "res", 1)
        return own + jnp.dot(other_rows, other.T, preferred_element_type=jnp.float32)

    queries, keys = to_heads(
        [projected[:, :query_width] * score_scale, projected[:, query_width : 2 * query_width]]
    )
    values, grad_attended = to_heads(
        [projected[:, 2 * query_width : 3 * query_width], grad_gated * gate_open]
    )

    pair_normed, pair_spread = layer_normalize(pair_entries)
    pair_bias = jnp.einsum("ijc,ch->hij", pair_normed, pair_weight, precision=lax.Precision.HIGHEST)
    bias = across(pair_bias.reshape(group, half_rows, column_count))
    bias = jnp.transpose(bias.reshape(2, res_size * half_rows, column_count), (1, 0, 2)).reshape(
        residue_total // 2, 2 * column_count
    )

    score_terms = products(queries, keys)
    bias_start = half * 2 * column_count
    own_block = lax.dynamic_slice_in_dim(score_terms, bias_start, 2 * column_count, 1) + bias
    score_terms = lax.dynamic_update_slice_in_dim(score_terms, own_block, bias_start, 1)
    grad_terms = products(grad_attended, values)

    def row_sums(terms, kind):
        blocks = terms.reshape(2, residue_total // 4, residue_total)
        mine = lax.dynamic_index_in_dim(blocks, half, 0, False)
        sent = lax.dynamic_index_in_dim(blocks, 1 - half, 0, False).astype(kind)
        return mine + swapped(sent, "seq", seq_size // 2).astype(jnp.float32)

    def half_gathered(mine):
        other = swapped(mine, "seq", seq_size // 2)
        low = jnp.where(half == 0, mine, other)
        high = jnp.where(half == 0, other, mine)
        return jnp.concatenate([low, high], axis=0)

    def all_rows(mine):
        other = swapped(mine, "res", 1)
        even = jnp.where(core == 0, mine, other).reshape(res_size, half_rows, residue_total)
        odd = jnp.where(core == 0, other, mine).reshape(res_size, half_rows, residue_total)
        return jnp.stack([even, odd], 1).reshape(residue_total, residue_total)

    logits = row_sums(score_terms, jnp.float32)
    grad_probs = row_sums(grad_terms, jnp.bfloat16)
    row_top = jnp.max(logits, axis=-1, keepdims=True)
    lifted = jnp.exp(logits - row_top)
    softmax_out = lifted / jnp.sum(lifted, axis=-1, keepdims=True)
    probs = all_rows(half_gathered(softmax_out.astype(jnp.bfloat16)))
    row_dot = jnp.sum(softmax_out * grad_probs, axis=-1, keepdims=True)
    grad_logits_half = half_gathered((softmax_out * (grad_probs - row_dot)).astype(jnp.bfloat16))
    logit_share = lax.dynamic_slice_in_dim(grad_logits_half, bias_start, 2 * column_count, 1)
    logit_share = jnp.transpose(
        logit_share.reshape(res_size, half_rows, 2, column_count), (2, 0, 1, 3)
    ).reshape(group, half_rows, column_count)
    logit_share = (
        across(logit_share)
        .reshape(head_count, residue_count, column_count)
        .astype(jnp.float32)
    )
    grad_logits = all_rows(grad_logits_half)

    def to_residues(tensors):
        blocks = jnp.stack(
            [
                t.astype(jnp.bfloat16).reshape(res_size, residue_count, 2, depth)
                for t in tensors
            ]
        )
        blocks = jnp.transpose(blocks, (3, 1, 0, 2, 4)).reshape(
            group, len(tensors), residue_count, depth
        )
        blocks = across(blocks).reshape(
            head_count, 2, len(tensors), residue_count, half_seqs, head_dim
        )
        blocks = jnp.transpose(blocks, (2, 1, 4, 3, 0, 5))
        return [blocks[t].reshape(token_count, query_width) for t in range(len(tensors))]

    attended, grad_values = to_residues(
        [
            jnp.dot(probs, values, preferred_element_type=jnp.float32),
            jnp.dot(probs.T, grad_attended, preferred_element_type=jnp.float32),
        ]
    )
    grad_queries, grad_keys = to_residues(
        [
            jnp.dot(grad_logits, keys, preferred_element_type=jnp.float32) * score_scale,
            jnp.dot(grad_logits.T, queries, preferred_element_type=jnp.float32),
        ]
    )

    attended = attended.astype(jnp.float32)
    gated_out = (gate_open * attended).astype(jnp.bfloat16)
    updated = jnp.dot(gated_out, output_weight, preferred_element_type=jnp.float32).astype(
        jnp.bfloat16
    )
    grad_gate_logit = grad_gated * attended * gate_open * (1.0 - gate_open)
    projected_gradient = jnp.concatenate(
        [grad_queries, grad_keys, grad_values, grad_gate_logit.astype(jnp.bfloat16)], axis=-1
    )

    weight_rows = alignment_width // res_size

    def row_blocks(matrix):
        return matrix.reshape(res_size, weight_rows, matrix.shape[-1])

    value_gate = projected_gradient[:, 2 * query_width :]
    query_key = projected_gradient[:, : 2 * query_width]
    early = summed_everywhere(
        jnp.concatenate(
            [
                row_blocks(jnp.dot(normed_b.T, value_gate, preferred_element_type=jnp.float32)),
                row_blocks(
                    jnp.dot(gated_out.T, flattened_gradient, preferred_element_type=jnp.float32)
                ),
            ],
            axis=-1,
        )
    )
    pair_w_local = jnp.einsum(
        "ijc,hij->hc", pair_normed, logit_share, precision=lax.Precision.HIGHEST
    )
    late = summed_everywhere(
        jnp.concatenate(
            [
                row_blocks(jnp.dot(normed_b.T, query_key, preferred_element_type=jnp.float32)),
                jnp.pad(pair_w_local[:, None, :], ((0, 0), (0, weight_rows - 1), (0, 0))),
            ],
            axis=-1,
        )
    )
    combined_weight_gradient = jnp.concatenate(
        [late[:, :, : 2 * query_width], early[:, :, : 2 * query_width]], axis=-1
    ).reshape(combined_weight.shape)
    output_weight_gradient = early[:, :, 2 * query_width :].reshape(output_weight.shape)
    pair_weight_gradient = late[:, 0, 2 * query_width :].T

    normalized_gradient = jnp.dot(
        projected_gradient, combined_weight.T, preferred_element_type=jnp.float32
    ).reshape(alignment_rows.shape)
    alignment_gradient = layer_norm_backward(
        normalized_gradient, normalized_rows, broadcast_pair
    ).astype(jnp.bfloat16)
    grad_pair_normed = jnp.einsum(
        "hij,ch->ijc", logit_share, pair_weight, precision=lax.Precision.HIGHEST
    )
    pair_gradient = layer_norm_backward(grad_pair_normed, pair_normed, pair_spread).astype(
        jnp.bfloat16
    )
    return (
        updated.reshape(alignment_rows.shape),
        alignment_gradient,
        pair_gradient,
        combined_weight_gradient,
        output_weight_gradient,
        pair_weight_gradient,
    )


def body(alignment_rows, pair_entries, combined_weight, output_weight, pair_weight, updated_gradient):
    head_count = pair_weight.shape[1]
    one_head = head_count == lax.axis_size("res") and lax.axis_size("seq") == 4
    chosen = head_body if one_head else gathered_body
    return chosen(
        alignment_rows, pair_entries, combined_weight, output_weight, pair_weight, updated_gradient
    )


def solution(mesh):
    return jax.shard_map(
        body,
        mesh=mesh,
        in_specs=(
            P("seq", "res", None),
            P("res", "seq", None),
            P(),
            P(),
            P(),
            P("seq", "res", None),
        ),
        out_specs=(
            P("seq", "res", None),
            P("seq", "res", None),
            P("res", "seq", None),
            P(),
            P(),
            P(),
        ),
        check_vma=False,
    )
```

```python
import functools
import math

import jax
import jax.numpy as jnp
from jax import lax
from jax.experimental import pallas as pl
from jax.experimental.pallas import tpu as pltpu
from jax.sharding import PartitionSpec as P

eps_norm = 1e-05


def layer_normalize(values):
    values = values.astype(jnp.float32)
    center = values - jnp.mean(values, axis=-1, keepdims=True)
    broadcast_pair = lax.rsqrt(jnp.mean(center * center, axis=-1, keepdims=True) + eps_norm)
    return (center * broadcast_pair, broadcast_pair)


def layer_norm_backward(normalized_gradient, normalized_rows, broadcast_pair):
    mean_grad = jnp.mean(normalized_gradient, axis=-1, keepdims=True)
    mean_cross = jnp.mean(normalized_gradient * normalized_rows, axis=-1, keepdims=True)
    return broadcast_pair * (normalized_gradient - mean_grad - normalized_rows * mean_cross)


def split_heads(tensor, head_count):
    return tensor.reshape(
        tensor.shape[0], tensor.shape[1], head_count, tensor.shape[2] // head_count
    )


def merge_heads(tensor):
    return tensor.reshape(tensor.shape[0], tensor.shape[1], tensor.shape[2] * tensor.shape[3])


def gathered_body(
    alignment_rows, pair_entries, combined_weight, output_weight, pair_weight, updated_gradient
):
    sequence_count, residue_count, alignment_width = alignment_rows.shape
    head_count = pair_weight.shape[1]
    query_width = output_weight.shape[0]
    head_dim = query_width // head_count
    column_count = pair_entries.shape[1]
    token_count = sequence_count * residue_count
    score_scale = 1.0 / math.sqrt(head_dim * sequence_count * lax.axis_size("seq"))
    normalized_rows, broadcast_pair = layer_normalize(alignment_rows)
    normalized_rows_backward = normalized_rows.astype(jnp.bfloat16).reshape(
        token_count, alignment_width
    )
    projected = jnp.dot(
        normalized_rows_backward, combined_weight, preferred_element_type=jnp.float32
    ).reshape(sequence_count, residue_count, 4 * query_width)
    queries = (projected[..., :query_width] * score_scale).astype(jnp.bfloat16)
    key_rows = projected[..., query_width : 2 * query_width].astype(jnp.bfloat16)
    value_rows = projected[..., 2 * query_width : 3 * query_width].astype(jnp.bfloat16)
    gate_open = jax.nn.sigmoid(projected[..., 3 * query_width :])
    all_keys, all_values = (
        lax.all_gather(key_rows, "res", axis=1, tiled=True),
        lax.all_gather(value_rows, "res", axis=1, tiled=True),
    )
    query_heads = split_heads(queries, head_count)
    key_heads = split_heads(all_keys, head_count)
    value_heads = split_heads(all_values, head_count)
    score_terms = jnp.einsum(
        "sihd,sjhd->hij", query_heads, key_heads, preferred_element_type=jnp.float32
    )
    pair_normed, pair_spread = layer_normalize(pair_entries)
    pair_bias = jnp.einsum("ijc,ch->hij", pair_normed, pair_weight, precision=lax.Precision.HIGHEST)
    col_start = lax.axis_index("seq") * column_count
    own_block = lax.dynamic_slice_in_dim(score_terms, col_start, column_count, 2) + pair_bias
    logits = lax.psum(lax.dynamic_update_slice_in_dim(score_terms, own_block, col_start, 2), "seq")
    row_top = jnp.max(logits, axis=-1, keepdims=True)
    lifted = jnp.exp(logits - row_top)
    softmax_out = lifted / jnp.sum(lifted, axis=-1, keepdims=True)
    softmax_low = softmax_out.astype(jnp.bfloat16)
    attended = merge_heads(
        jnp.einsum("hij,sjhd->sihd", softmax_low, value_heads, preferred_element_type=jnp.float32)
    )
    gated_out = (gate_open * attended).astype(jnp.bfloat16)
    flattened_gated = gated_out.reshape(token_count, query_width)
    updated = (
        jnp.dot(flattened_gated, output_weight, preferred_element_type=jnp.float32)
        .astype(jnp.bfloat16)
        .reshape(sequence_count, residue_count, alignment_width)
    )
    flattened_gradient = updated_gradient.reshape(token_count, alignment_width)
    grad_gated = jnp.dot(
        flattened_gradient, output_weight.T, preferred_element_type=jnp.float32
    ).reshape(sequence_count, residue_count, query_width)
    out_local = jnp.dot(flattened_gated.T, flattened_gradient, preferred_element_type=jnp.float32)
    grad_attended = (grad_gated * gate_open).astype(jnp.bfloat16)
    grad_gate_logit = grad_gated * attended * gate_open * (1.0 - gate_open)
    attended_grad_heads = split_heads(grad_attended, head_count)
    grad_terms = jnp.einsum(
        "sihd,sjhd->hij", attended_grad_heads, value_heads, preferred_element_type=jnp.float32
    )
    grad_probs = lax.psum(grad_terms, "seq")
    row_dot = jnp.sum(softmax_out * grad_probs, axis=-1, keepdims=True)
    grad_logits = softmax_out * (grad_probs - row_dot)
    grad_logits_b = grad_logits.astype(jnp.bfloat16)
    logit_share = lax.dynamic_slice_in_dim(grad_logits, col_start, column_count, 2)
    grad_query_heads = (
        jnp.einsum("hij,sjhd->sihd", grad_logits_b, key_heads, preferred_element_type=jnp.float32)
        * score_scale
    )
    key_part = jnp.einsum(
        "hij,sihd->jshd", grad_logits_b, query_heads, preferred_element_type=jnp.float32
    )
    value_part = jnp.einsum(
        "hij,sihd->jshd", softmax_low, attended_grad_heads, preferred_element_type=jnp.float32
    )
    summed = lax.psum_scatter(
        jnp.concatenate([merge_heads(key_part), merge_heads(value_part)], axis=-1),
        "res",
        scatter_dimension=0,
        tiled=True,
    )
    key_value_grads = jnp.transpose(summed, (1, 0, 2))
    projected_gradient = jnp.concatenate(
        [merge_heads(grad_query_heads), key_value_grads, grad_gate_logit], axis=-1
    )
    projected_gradient = projected_gradient.astype(jnp.bfloat16).reshape(
        token_count, 4 * query_width
    )
    qkvg_local = jnp.dot(
        normalized_rows_backward.T, projected_gradient, preferred_element_type=jnp.float32
    )
    normalized_gradient = jnp.dot(
        projected_gradient, combined_weight.T, preferred_element_type=jnp.float32
    ).reshape(sequence_count, residue_count, alignment_width)
    alignment_gradient = layer_norm_backward(
        normalized_gradient, normalized_rows, broadcast_pair
    ).astype(jnp.bfloat16)
    pair_w_local = jnp.einsum(
        "ijc,hij->ch", pair_normed, logit_share, precision=lax.Precision.HIGHEST
    )
    grad_pair_normed = jnp.einsum(
        "hij,ch->ijc", logit_share, pair_weight, precision=lax.Precision.HIGHEST
    )
    pair_gradient = layer_norm_backward(grad_pair_normed, pair_normed, pair_spread).astype(
        jnp.bfloat16
    )
    combined_weight_gradient, output_weight_gradient, pair_weight_gradient = lax.psum(
        (qkvg_local, out_local, pair_w_local), ("seq", "res")
    )
    return (
        updated,
        alignment_gradient,
        pair_gradient,
        combined_weight_gradient,
        output_weight_gradient,
        pair_weight_gradient,
    )


VMEM_LIMIT = 48 * 1024 * 1024
LANES = 128
SLOTS = 4
NT = (((1,), (1,)), ((), ()))
TN = (((0,), (0,)), ((), ()))


def f32_dot(left, right, dims=None):
    if dims is None:
        return jnp.dot(left, right, preferred_element_type=jnp.float32)
    return lax.dot_general(left, right, dims, preferred_element_type=jnp.float32)


def two_terms(values):
    high = values.astype(jnp.bfloat16)
    return high, (values - high.astype(jnp.float32)).astype(jnp.bfloat16)


def slot_select(pieces):
    slot = lax.broadcasted_iota(jnp.int32, pieces[0].shape, 1) // (LANES // SLOTS)
    result = pieces[0]
    for k in range(1, SLOTS):
        result = jnp.where(slot == k, pieces[k], result)
    return result


def pack_heads(out_ref, row, tensor, residues):
    for core in range(2):
        for tile in range(tensor.shape[1] // LANES):
            rolled = []
            for s in range(SLOTS):
                start = (core * SLOTS + s) * residues
                piece = tensor[start : start + residues, tile * LANES : (tile + 1) * LANES]
                rolled.append(pltpu.roll(piece, s * LANES // SLOTS, 1) if s else piece)
            for j in range(SLOTS):
                block = slot_select([rolled[(k - j) % SLOTS] for k in range(SLOTS)])
                out_ref[(tile * SLOTS + j) * 2 + core, row : row + residues, :] = block.astype(
                    jnp.bfloat16
                )


def unpack_heads(in_ref, row, residues, tiles):
    rows = []
    for core in range(2):
        for s in range(SLOTS):
            pieces = []
            for tile in range(tiles):
                blocks = [
                    in_ref[
                        (tile * SLOTS + (k - s) % SLOTS) * 2 + core, row : row + residues, :
                    ].astype(jnp.float32)
                    for k in range(SLOTS)
                ]
                block = slot_select(blocks)
                pieces.append(pltpu.roll(block, LANES - s * LANES // SLOTS, 1) if s else block)
            rows.append(jnp.concatenate(pieces, axis=1))
    return jnp.concatenate(rows, axis=0)


def normalized(x_ref):
    width = x_ref.shape[-1]
    values = x_ref[...].reshape(-1, width).astype(jnp.float32)
    return layer_normalize(values)


def gate_of(logits):
    return 1.0 / (1.0 + jnp.exp(-logits))


def value_kernel(x_ref, grad_ref, wc_ref, wo_ref, out_ref):
    residues, width = x_ref.shape[1], x_ref.shape[2]
    normed = normalized(x_ref)[0].astype(jnp.bfloat16)
    values = f32_dot(normed, wc_ref[:, 2 * width : 3 * width])
    gate = gate_of(f32_dot(normed, wc_ref[:, 3 * width :]))
    grad_gated = f32_dot(grad_ref[...].reshape(-1, width), wo_ref[...], NT)
    pack_heads(out_ref, 0, values, residues)
    pack_heads(out_ref, residues, grad_gated * gate, residues)


def query_kernel(scale, x_ref, wc_ref, pair_ref, weight_ref, out_ref, bias_ref, mean_ref, spread_ref):
    residues, width = x_ref.shape[1], x_ref.shape[2]
    heads = weight_ref.shape[0]
    normed = normalized(x_ref)[0].astype(jnp.bfloat16)
    pack_heads(out_ref, 0, f32_dot(normed, wc_ref[:, :width]) * scale, residues)
    pack_heads(out_ref, residues, f32_dot(normed, wc_ref[:, width : 2 * width]), residues)

    columns, channels = pair_ref.shape[1], pair_ref.shape[2]
    first = weight_ref[...].astype(jnp.bfloat16)
    rest = weight_ref[...] - first.astype(jnp.float32)
    second, third = two_terms(rest)
    share = jnp.full((heads, channels), 1.0 / channels, jnp.bfloat16)
    left = jnp.concatenate([first, second, third, share], axis=0)
    ones = jnp.full((heads, channels), 1.0 / channels, jnp.bfloat16)
    average = jnp.full((channels, channels), 1.0 / channels, jnp.bfloat16)

    def rows(step, carry):
        for k in range(8):
            i = step * 8 + k
            entries = pair_ref[i]
            center = entries.astype(jnp.float32) - f32_dot(entries, average)
            high, low = two_terms(center * center)
            variance = f32_dot(ones, high, NT) + f32_dot(ones, low, NT)
            spread = lax.rsqrt(variance + eps_norm)
            raw = f32_dot(left, entries, NT)
            bias = spread * (raw[:heads] + raw[heads : 2 * heads] + raw[2 * heads : 3 * heads])
            bias_ref[:, i, :] = bias
            mean_ref[pl.ds(i, 1), :] = raw[3 * heads : 3 * heads + 1]
            spread_ref[pl.ds(i, 1), :] = spread[:1]
        return carry

    lax.fori_loop(0, pair_ref.shape[0] // 8, rows, 0)
    half = residues // 2
    for h in range(heads):
        for core in range(2):
            high, low = two_terms(bias_ref[h, core * half : (core + 1) * half, :])
            out_ref[h * 2 + core, 2 * residues : 2 * residues + half, :] = high
            out_ref[h * 2 + core, 2 * residues + half : 3 * residues, :] = low


def lanes_of(blocks_ref, row, residues):
    count = blocks_ref.shape[0] // 2
    planes = [
        blocks_ref[p * count : (p + 1) * count, row : row + residues, :].reshape(-1, LANES)
        for p in range(2)
    ]
    return jnp.concatenate(planes, axis=1)


def score_kernel(
    residues, left_row, right_row, with_bias, place_ref, own_ref, other_ref, mine_ref, sent_ref
):
    core, half = place_ref[0], place_ref[1]
    count = own_ref.shape[0] // 2
    part = residues // 2
    right = jnp.concatenate(
        [lanes_of(own_ref, right_row, residues), lanes_of(other_ref, right_row, residues)], axis=1
    )
    for which, ref in ((half, mine_ref), (1 - half, sent_ref)):
        left = []
        for k in range(count // 2):
            block = which * (count // 2) + k
            rows = pl.ds(pl.multiple_of(left_row + core * part, part), part)
            left.append(
                jnp.concatenate(
                    [
                        r[p * count + block, rows, :]
                        for r in (own_ref, other_ref)
                        for p in range(2)
                    ],
                    axis=1,
                )
            )
        ref[...] = f32_dot(jnp.concatenate(left, axis=0), right, NT).astype(ref.dtype)
        if with_bias:
            for p in range(2):
                columns = pl.ds(pl.multiple_of((half * 2 + p) * LANES, LANES), LANES)
                for k in range(count // 2):
                    block = p * count + which * (count // 2) + k
                    high = own_ref[block, 2 * residues : 2 * residues + part, :]
                    low = own_ref[block, 2 * residues + part : 3 * residues, :]
                    bias = high.astype(jnp.float32) + low.astype(jnp.float32)
                    ref[k * part : (k + 1) * part, columns] += bias


def softmax_kernel(logit_ref, logit_other_ref, grad_ref, grad_other_ref, prob_ref, out_ref):
    logits = logit_ref[...] + logit_other_ref[...]
    lifted = jnp.exp(logits - jnp.max(logits, axis=-1, keepdims=True))
    softmax_out = lifted / jnp.sum(lifted, axis=-1, keepdims=True)
    prob_ref[...] = softmax_out.astype(jnp.bfloat16)
    grad_probs = grad_ref[...] + grad_other_ref[...].astype(jnp.float32)
    row_dot = jnp.sum(softmax_out * grad_probs, axis=-1, keepdims=True)
    out_ref[...] = (softmax_out * (grad_probs - row_dot)).astype(jnp.bfloat16)


def product_kernel(
    residues, scale, first_row, second_row, with_share,
    place_ref, own_ref, far_ref, near_ref, corner_ref, blocks_ref, out_ref, whole_ref,
):
    core, half = place_ref[0], place_ref[1]
    count = blocks_ref.shape[0] // 2
    part = residues // 2
    quarters = (
        (own_ref, core, half), (far_ref, core, 1 - half),
        (near_ref, 1 - core, half), (corner_ref, 1 - core, 1 - half),
    )
    for ref, c, z in quarters:
        for k in range(count // 2):
            start = (z * (count // 2) + k) * residues + c * part
            whole_ref[pl.ds(pl.multiple_of(start, part), part), :] = ref[k * part : (k + 1) * part, :]
    whole = whole_ref[...]
    if with_share:
        for p in range(2):
            columns = pl.ds(pl.multiple_of((half * 2 + p) * LANES, LANES), LANES)
            for q in range(count):
                rows = pl.ds(pl.multiple_of(q * residues + core * part, part), part)
                out_ref[p * count + q, 2 * residues : 2 * residues + part, :] = whole_ref[rows, columns]
    first = f32_dot(whole, lanes_of(blocks_ref, first_row, residues)) * scale
    second = f32_dot(whole, lanes_of(blocks_ref, second_row, residues), TN)
    for row, product in ((0, first), (residues, second)):
        for p in range(2):
            out_ref[p * count : (p + 1) * count, row : row + residues, :] = (
                product[:, p * LANES : (p + 1) * LANES]
                .astype(jnp.bfloat16)
                .reshape(count, residues, LANES)
            )


def gate_kernel(x_ref, grad_ref, wc_ref, wo_ref, blocks_ref, updated_ref, value_gate_ref, weight_ref):
    residues, width = x_ref.shape[1], x_ref.shape[2]
    tiles = width // LANES
    normed = normalized(x_ref)[0].astype(jnp.bfloat16)
    gate = gate_of(f32_dot(normed, wc_ref[:, 3 * width :]))
    grad = grad_ref[...].reshape(-1, width)
    grad_gated = f32_dot(grad, wo_ref[...], NT)
    attended = unpack_heads(blocks_ref, 0, residues, tiles)
    gated = (gate * attended).astype(jnp.bfloat16)
    updated_ref[...] = f32_dot(gated, wo_ref[...]).astype(jnp.bfloat16).reshape(updated_ref.shape)
    value_gate_ref[:, :width] = unpack_heads(blocks_ref, residues, residues, tiles).astype(
        jnp.bfloat16
    )
    value_gate_ref[:, width:] = (grad_gated * attended * gate * (1.0 - gate)).astype(jnp.bfloat16)
    weight_ref[:, : 2 * width] = f32_dot(normed, value_gate_ref[...], TN).astype(jnp.bfloat16)
    weight_ref[:, 2 * width :] = f32_dot(gated, grad, TN).astype(jnp.bfloat16)


def share_of(blocks_ref, row, part, heads):
    return jnp.concatenate(
        [
            blocks_ref[:, row : row + part, :]
            .astype(jnp.float32)
            .reshape(heads, 2 * part, LANES)
        ],
        axis=0,
    )


def weight_kernel(
    x_ref, blocks_ref, pair_ref, mean_ref, spread_ref, query_key_ref, weight_ref, share_ref
):
    residues, width = x_ref.shape[1], x_ref.shape[2]
    tiles = width // LANES
    heads = share_ref.shape[0]
    part = residues // 2
    share_ref[...] = share_of(blocks_ref, 2 * residues, part, heads)

    def rows(step, carry):
        total, shift = carry
        for k in range(8):
            i = step * 8 + k
            scaled = share_ref[:, i, :] * spread_ref[pl.ds(i, 1), :]
            high, low = two_terms(scaled)
            total += f32_dot(jnp.concatenate([high, low], axis=0), pair_ref[i])
            shift += (high.astype(jnp.float32) + low.astype(jnp.float32)) * mean_ref[pl.ds(i, 1), :]
        return total, shift

    channels = pair_ref.shape[2]
    total, shift = lax.fori_loop(
        0,
        pair_ref.shape[0] // 8,
        rows,
        (jnp.zeros((2 * heads, channels), jnp.float32), jnp.zeros((heads, LANES), jnp.float32)),
    )
    pair_weight = total[:heads] + total[heads:] - jnp.sum(shift, axis=1, keepdims=True)
    normed = normalized(x_ref)[0].astype(jnp.bfloat16)
    for t in range(2):
        query_key_ref[:, t * width : (t + 1) * width] = unpack_heads(
            blocks_ref, t * residues, residues, tiles
        ).astype(jnp.bfloat16)
    weight_ref[:, : 2 * width] = f32_dot(normed, query_key_ref[...], TN).astype(jnp.bfloat16)
    rows_each = weight_ref.shape[0] // heads
    first = lax.broadcasted_iota(jnp.int32, (rows_each, channels), 0) == 0
    for h in range(heads):
        row = jnp.broadcast_to(pair_weight[h : h + 1], (rows_each, channels))
        weight_ref[h * rows_each : (h + 1) * rows_each, 2 * width :] = jnp.where(
            first, row, 0.0
        ).astype(jnp.bfloat16)


def alignment_kernel(x_ref, wc_ref, query_key_ref, value_gate_ref, out_ref):
    width = x_ref.shape[2]
    normed, spread = normalized(x_ref)
    gradient = f32_dot(query_key_ref[...], wc_ref[:, : 2 * width], NT) + f32_dot(
        value_gate_ref[...], wc_ref[:, 2 * width :], NT
    )
    out_ref[...] = (
        layer_norm_backward(gradient, normed, spread).astype(jnp.bfloat16).reshape(out_ref.shape)
    )


def pair_kernel(blocks_row, blocks_ref, pair_ref, weight_ref, bias_ref, mean_ref, spread_ref, out_ref, share_ref):
    heads, channels = weight_ref.shape
    part = pair_ref.shape[0] // 2
    share_ref[...] = share_of(blocks_ref, blocks_row, part, heads)
    first, second = two_terms(weight_ref[...])
    zero = jnp.zeros((heads, channels), jnp.bfloat16)
    top = lax.broadcasted_iota(jnp.int32, (heads, channels), 0) < 2
    ones = jnp.where(top, 1.0, 0.0).astype(jnp.bfloat16)
    right = jnp.concatenate(
        [
            jnp.concatenate([first, first, second, ones, zero], axis=0),
            jnp.concatenate([zero, zero, zero, zero, ones], axis=0),
        ],
        axis=1,
    )
    row = lax.broadcasted_iota(jnp.int32, (heads, LANES), 0)

    def rows_of_two(value):
        high, low = two_terms(value)
        high, low = high.astype(jnp.float32), low.astype(jnp.float32)
        return jnp.where(row == 0, high, jnp.where(row == 1, low, 0.0)).astype(jnp.bfloat16)

    def rows(step, carry):
        for k in range(8):
            i = step * 8 + k
            gradient = share_ref[:, i, :]
            spread = spread_ref[pl.ds(i, 1), :]
            cross = jnp.sum(gradient * bias_ref[:, i, :], axis=0, keepdims=True) / channels
            slope = spread * spread * cross
            high, low = two_terms(gradient * spread)
            left = jnp.concatenate(
                [
                    high, low, high,
                    rows_of_two(jnp.broadcast_to(slope * mean_ref[pl.ds(i, 1), :], row.shape)),
                    rows_of_two(jnp.broadcast_to(slope, row.shape)),
                ],
                axis=0,
            )
            terms = f32_dot(left, right, TN)
            entries = pair_ref[i].astype(jnp.float32)
            out_ref[i] = (terms[:, :channels] - terms[:, channels:] * entries).astype(jnp.bfloat16)
        return carry

    lax.fori_loop(0, pair_ref.shape[0] // 8, rows, 0)


def call(kernel, outs, *args, scratch=(), place=None, flops=0):
    whole = pl.BlockSpec(memory_space=pltpu.VMEM)
    specs = [whole] * len(args)
    if place is not None:
        specs = [pl.BlockSpec(memory_space=pltpu.SMEM)] + specs
        args = (place,) + args
    shapes = [jax.ShapeDtypeStruct(*o) for o in outs]
    moved = sum(math.prod(a.shape) * a.dtype.itemsize for a in list(args) + shapes)
    result = pl.pallas_call(
        kernel,
        out_shape=shapes,
        in_specs=specs,
        out_specs=[whole] * len(shapes),
        scratch_shapes=scratch,
        compiler_params=pltpu.CompilerParams(vmem_limit_bytes=VMEM_LIMIT),
        cost_estimate=pl.CostEstimate(flops=flops, bytes_accessed=moved, transcendentals=0),
    )(*args)
    return result


def swapped(mine, axis_name, distance):
    size = lax.axis_size(axis_name)
    return lax.ppermute(mine, axis_name, [(a, a ^ distance) for a in range(size)])


def gathered_seq(mine):
    size, index = lax.axis_size("seq"), lax.axis_index("seq")
    rows = jnp.zeros((size,) + mine.shape, mine.dtype)
    rows = lax.dynamic_update_index_in_dim(rows, mine, index, 0)
    for k in range(1, size):
        t = lax.ppermute(mine, "seq", [(a, (a + k) % size) for a in range(size)])
        rows = lax.dynamic_update_index_in_dim(rows, t, (index - k) % size, 0)
    return rows


def summed_everywhere(parts):
    size = lax.axis_size("res")
    rows, columns = parts.shape
    parts = lax.all_to_all(parts.reshape(size, rows // size, columns), "res", 0, 0, tiled=True)
    part = jnp.sum(parts.astype(jnp.float32), axis=0).astype(jnp.bfloat16)
    part = jnp.sum(gathered_seq(part).astype(jnp.float32), axis=0).astype(jnp.bfloat16)
    return lax.all_gather(part, "res", axis=0)


def fits_heads(alignment_rows, pair_entries, pair_weight):
    channels, heads = pair_weight.shape
    return (
        lax.axis_size("seq") == 4
        and lax.axis_size("res") == heads == 8
        and alignment_rows.shape[0] == 2 * SLOTS
        and alignment_rows.shape[1] == pair_entries.shape[0] == 64
        and alignment_rows.shape[2] == 2 * LANES
        and pair_entries.shape[1] == channels == LANES
    )


def head_body(
    alignment_rows, pair_entries, combined_weight, output_weight, pair_weight, updated_gradient
):
    sequences, residues, width = alignment_rows.shape
    channels, heads = pair_weight.shape
    tokens = sequences * residues
    seq_size, res_size = lax.axis_size("seq"), lax.axis_size("res")
    seq_half = seq_size // 2
    total = residues * res_size
    group = 2 * res_size
    groups = [[g * group + k for k in range(group)] for g in range(seq_half)]
    scale = 1.0 / math.sqrt(width // heads * sequences * seq_size)
    place = jnp.stack([lax.axis_index("res") % 2, lax.axis_index("seq") // 2]).astype(jnp.int32)
    bf16, f32 = jnp.bfloat16, jnp.float32

    def across(blocks):
        return lax.all_to_all(blocks, ("seq", "res"), 0, 0, axis_index_groups=groups, tiled=True)

    def all_quarters(mine):
        far = swapped(mine, "seq", seq_half)
        return mine, far, swapped(mine, "res", 1), swapped(far, "res", 1)

    x, grad, wc, wo = alignment_rows, updated_gradient, combined_weight, output_weight
    (value_blocks,) = call(
        value_kernel, [((group, 2 * residues, LANES), bf16)], x, grad, wc, wo,
        flops=8 * tokens * width * width,
    )
    value_blocks = across(value_blocks)
    centred = (pair_weight - jnp.mean(pair_weight, axis=0, keepdims=True)).T
    query_blocks, bias, mean, spread = call(
        functools.partial(query_kernel, scale),
        [
            ((group, 3 * residues, LANES), bf16),
            ((heads, residues, LANES), f32),
            ((residues, LANES), f32),
            ((residues, LANES), f32),
        ],
        x, wc, pair_entries, centred,
        flops=8 * tokens * width * width,
    )
    query_blocks = across(query_blocks)

    def scores(blocks, left_row, right_row, with_bias, kind):
        return call(
            functools.partial(score_kernel, residues, left_row, right_row, with_bias),
            [((total // 4, total), f32), ((total // 4, total), kind)],
            blocks, swapped(blocks, "res", 1),
            place=place, flops=2 * total * total * width,
        )

    grad_mine, grad_sent = scores(value_blocks, residues, 0, False, bf16)
    grad_other = swapped(grad_sent, "seq", seq_half)
    logit_mine, logit_sent = scores(query_blocks, 0, residues, True, f32)
    logit_other = swapped(logit_sent, "seq", seq_half)
    quarter = ((total // 4, total), bf16)
    probs, grad_logits = call(
        softmax_kernel, [quarter, quarter], logit_mine, logit_other, grad_mine, grad_other,
        flops=total * total,
    )

    def products(quarters, blocks, first_row, second_row, with_share, factor):
        rows = 2 * residues + (residues // 2 if with_share else 0)
        (out,) = call(
            functools.partial(
                product_kernel, residues, factor, first_row, second_row, with_share
            ),
            [((group, rows, LANES), bf16)],
            *quarters, blocks,
            scratch=[pltpu.VMEM((total, total), bf16)],
            place=place, flops=4 * total * total * width,
        )
        return across(out)

    attended_blocks = products(all_quarters(probs), value_blocks, 0, residues, False, 1.0)
    grad_blocks = products(all_quarters(grad_logits), query_blocks, residues, 0, True, scale)

    updated, value_gate, early = call(
        gate_kernel,
        [(x.shape, bf16), ((tokens, 2 * width), bf16), ((width, 3 * width), bf16)],
        x, grad, wc, wo, attended_blocks,
        flops=12 * tokens * width * width,
    )
    early = summed_everywhere(early)
    query_key, late = call(
        weight_kernel,
        [((tokens, 2 * width), bf16), ((width, 2 * width + channels), bf16)],
        x, grad_blocks, pair_entries, mean, spread,
        scratch=[pltpu.VMEM((heads, residues, LANES), f32)],
        flops=4 * tokens * width * width,
    )
    late = summed_everywhere(late)
    (alignment_gradient,) = call(
        alignment_kernel, [(x.shape, bf16)], x, wc, query_key, value_gate,
        flops=8 * tokens * width * width,
    )
    (pair_gradient,) = call(
        functools.partial(pair_kernel, 2 * residues),
        [(pair_entries.shape, bf16)],
        grad_blocks, pair_entries, centred, bias, mean, spread,
        scratch=[pltpu.VMEM((heads, residues, LANES), f32)],
        flops=8 * tokens * width * width,
    )

    combined_weight_gradient = (
        jnp.concatenate([late[:, :, : 2 * width], early[:, :, : 2 * width]], axis=-1)
        .reshape(wc.shape)
        .astype(f32)
    )
    output_weight_gradient = early[:, :, 2 * width :].reshape(wo.shape).astype(f32)
    pair_weight_gradient = late[:, 0, 2 * width :].T.astype(f32)
    return (
        updated,
        alignment_gradient,
        pair_gradient,
        combined_weight_gradient,
        output_weight_gradient,
        pair_weight_gradient,
    )


def body(alignment_rows, pair_entries, combined_weight, output_weight, pair_weight, updated_gradient):
    chosen = head_body if fits_heads(alignment_rows, pair_entries, pair_weight) else gathered_body
    return chosen(
        alignment_rows, pair_entries, combined_weight, output_weight, pair_weight, updated_gradient
    )


def solution(mesh):
    return jax.shard_map(
        body,
        mesh=mesh,
        in_specs=(
            P("seq", "res", None),
            P("res", "seq", None),
            P(),
            P(),
            P(),
            P("seq", "res", None),
        ),
        out_specs=(
            P("seq", "res", None),
            P("seq", "res", None),
            P("res", "seq", None),
            P(),
            P(),
            P(),
        ),
        check_vma=False,
    )
```

```python
import functools
import math

import jax
import jax.numpy as jnp
from jax import lax
from jax.experimental import pallas as pl
from jax.experimental.pallas import tpu as pltpu
from jax.sharding import PartitionSpec as P

eps_norm = 1e-05


def layer_normalize(values):
    values = values.astype(jnp.float32)
    center = values - jnp.mean(values, axis=-1, keepdims=True)
    broadcast_pair = lax.rsqrt(jnp.mean(center * center, axis=-1, keepdims=True) + eps_norm)
    return (center * broadcast_pair, broadcast_pair)


def layer_norm_backward(normalized_gradient, normalized_rows, broadcast_pair):
    mean_grad = jnp.mean(normalized_gradient, axis=-1, keepdims=True)
    mean_cross = jnp.mean(normalized_gradient * normalized_rows, axis=-1, keepdims=True)
    return broadcast_pair * (normalized_gradient - mean_grad - normalized_rows * mean_cross)


def split_heads(tensor, head_count):
    return tensor.reshape(
        tensor.shape[0], tensor.shape[1], head_count, tensor.shape[2] // head_count
    )


def merge_heads(tensor):
    return tensor.reshape(tensor.shape[0], tensor.shape[1], tensor.shape[2] * tensor.shape[3])


def gathered_body(
    alignment_rows, pair_entries, combined_weight, output_weight, pair_weight, updated_gradient
):
    sequence_count, residue_count, alignment_width = alignment_rows.shape
    head_count = pair_weight.shape[1]
    query_width = output_weight.shape[0]
    head_dim = query_width // head_count
    column_count = pair_entries.shape[1]
    token_count = sequence_count * residue_count
    score_scale = 1.0 / math.sqrt(head_dim * sequence_count * lax.axis_size("seq"))
    normalized_rows, broadcast_pair = layer_normalize(alignment_rows)
    normalized_rows_backward = normalized_rows.astype(jnp.bfloat16).reshape(
        token_count, alignment_width
    )
    projected = jnp.dot(
        normalized_rows_backward, combined_weight, preferred_element_type=jnp.float32
    ).reshape(sequence_count, residue_count, 4 * query_width)
    queries = (projected[..., :query_width] * score_scale).astype(jnp.bfloat16)
    key_rows = projected[..., query_width : 2 * query_width].astype(jnp.bfloat16)
    value_rows = projected[..., 2 * query_width : 3 * query_width].astype(jnp.bfloat16)
    gate_open = jax.nn.sigmoid(projected[..., 3 * query_width :])
    all_keys, all_values = (
        lax.all_gather(key_rows, "res", axis=1, tiled=True),
        lax.all_gather(value_rows, "res", axis=1, tiled=True),
    )
    query_heads = split_heads(queries, head_count)
    key_heads = split_heads(all_keys, head_count)
    value_heads = split_heads(all_values, head_count)
    score_terms = jnp.einsum(
        "sihd,sjhd->hij", query_heads, key_heads, preferred_element_type=jnp.float32
    )
    pair_normed, pair_spread = layer_normalize(pair_entries)
    pair_bias = jnp.einsum("ijc,ch->hij", pair_normed, pair_weight, precision=lax.Precision.HIGHEST)
    col_start = lax.axis_index("seq") * column_count
    own_block = lax.dynamic_slice_in_dim(score_terms, col_start, column_count, 2) + pair_bias
    logits = lax.psum(lax.dynamic_update_slice_in_dim(score_terms, own_block, col_start, 2), "seq")
    row_top = jnp.max(logits, axis=-1, keepdims=True)
    lifted = jnp.exp(logits - row_top)
    softmax_out = lifted / jnp.sum(lifted, axis=-1, keepdims=True)
    softmax_low = softmax_out.astype(jnp.bfloat16)
    attended = merge_heads(
        jnp.einsum("hij,sjhd->sihd", softmax_low, value_heads, preferred_element_type=jnp.float32)
    )
    gated_out = (gate_open * attended).astype(jnp.bfloat16)
    flattened_gated = gated_out.reshape(token_count, query_width)
    updated = (
        jnp.dot(flattened_gated, output_weight, preferred_element_type=jnp.float32)
        .astype(jnp.bfloat16)
        .reshape(sequence_count, residue_count, alignment_width)
    )
    flattened_gradient = updated_gradient.reshape(token_count, alignment_width)
    grad_gated = jnp.dot(
        flattened_gradient, output_weight.T, preferred_element_type=jnp.float32
    ).reshape(sequence_count, residue_count, query_width)
    out_local = jnp.dot(flattened_gated.T, flattened_gradient, preferred_element_type=jnp.float32)
    grad_attended = (grad_gated * gate_open).astype(jnp.bfloat16)
    grad_gate_logit = grad_gated * attended * gate_open * (1.0 - gate_open)
    attended_grad_heads = split_heads(grad_attended, head_count)
    grad_terms = jnp.einsum(
        "sihd,sjhd->hij", attended_grad_heads, value_heads, preferred_element_type=jnp.float32
    )
    grad_probs = lax.psum(grad_terms, "seq")
    row_dot = jnp.sum(softmax_out * grad_probs, axis=-1, keepdims=True)
    grad_logits = softmax_out * (grad_probs - row_dot)
    grad_logits_b = grad_logits.astype(jnp.bfloat16)
    logit_share = lax.dynamic_slice_in_dim(grad_logits, col_start, column_count, 2)
    grad_query_heads = (
        jnp.einsum("hij,sjhd->sihd", grad_logits_b, key_heads, preferred_element_type=jnp.float32)
        * score_scale
    )
    key_part = jnp.einsum(
        "hij,sihd->jshd", grad_logits_b, query_heads, preferred_element_type=jnp.float32
    )
    value_part = jnp.einsum(
        "hij,sihd->jshd", softmax_low, attended_grad_heads, preferred_element_type=jnp.float32
    )
    summed = lax.psum_scatter(
        jnp.concatenate([merge_heads(key_part), merge_heads(value_part)], axis=-1),
        "res",
        scatter_dimension=0,
        tiled=True,
    )
    key_value_grads = jnp.transpose(summed, (1, 0, 2))
    projected_gradient = jnp.concatenate(
        [merge_heads(grad_query_heads), key_value_grads, grad_gate_logit], axis=-1
    )
    projected_gradient = projected_gradient.astype(jnp.bfloat16).reshape(
        token_count, 4 * query_width
    )
    qkvg_local = jnp.dot(
        normalized_rows_backward.T, projected_gradient, preferred_element_type=jnp.float32
    )
    normalized_gradient = jnp.dot(
        projected_gradient, combined_weight.T, preferred_element_type=jnp.float32
    ).reshape(sequence_count, residue_count, alignment_width)
    alignment_gradient = layer_norm_backward(
        normalized_gradient, normalized_rows, broadcast_pair
    ).astype(jnp.bfloat16)
    pair_w_local = jnp.einsum(
        "ijc,hij->ch", pair_normed, logit_share, precision=lax.Precision.HIGHEST
    )
    grad_pair_normed = jnp.einsum(
        "hij,ch->ijc", logit_share, pair_weight, precision=lax.Precision.HIGHEST
    )
    pair_gradient = layer_norm_backward(grad_pair_normed, pair_normed, pair_spread).astype(
        jnp.bfloat16
    )
    combined_weight_gradient, output_weight_gradient, pair_weight_gradient = lax.psum(
        (qkvg_local, out_local, pair_w_local), ("seq", "res")
    )
    return (
        updated,
        alignment_gradient,
        pair_gradient,
        combined_weight_gradient,
        output_weight_gradient,
        pair_weight_gradient,
    )


VMEM_LIMIT = 48 * 1024 * 1024
LANES = 128
SLOTS = 4
NT = (((1,), (1,)), ((), ()))
TN = (((0,), (0,)), ((), ()))


def f32_dot(left, right, dims=None):
    if dims is None:
        return jnp.dot(left, right, preferred_element_type=jnp.float32)
    return lax.dot_general(left, right, dims, preferred_element_type=jnp.float32)


def two_terms(values):
    high = values.astype(jnp.bfloat16)
    return high, (values - high.astype(jnp.float32)).astype(jnp.bfloat16)


def slot_select(pieces):
    slot = lax.broadcasted_iota(jnp.int32, pieces[0].shape, 1) // (LANES // SLOTS)
    result = pieces[0]
    for k in range(1, SLOTS):
        result = jnp.where(slot == k, pieces[k], result)
    return result


def pack_heads(out_ref, row, tensor, residues):
    for core in range(2):
        for tile in range(tensor.shape[1] // LANES):
            rolled = []
            for s in range(SLOTS):
                start = (core * SLOTS + s) * residues
                piece = tensor[start : start + residues, tile * LANES : (tile + 1) * LANES]
                rolled.append(pltpu.roll(piece, s * LANES // SLOTS, 1) if s else piece)
            for j in range(SLOTS):
                block = slot_select([rolled[(k - j) % SLOTS] for k in range(SLOTS)])
                out_ref[(tile * SLOTS + j) * 2 + core, row : row + residues, :] = block.astype(
                    jnp.bfloat16
                )


def unpack_heads(in_ref, row, residues, tiles):
    rows = []
    for core in range(2):
        for s in range(SLOTS):
            pieces = []
            for tile in range(tiles):
                blocks = [
                    in_ref[
                        (tile * SLOTS + (k - s) % SLOTS) * 2 + core, row : row + residues, :
                    ].astype(jnp.float32)
                    for k in range(SLOTS)
                ]
                block = slot_select(blocks)
                pieces.append(pltpu.roll(block, LANES - s * LANES // SLOTS, 1) if s else block)
            rows.append(jnp.concatenate(pieces, axis=1))
    return jnp.concatenate(rows, axis=0)


def normalized(x_ref):
    width = x_ref.shape[-1]
    values = x_ref[...].reshape(-1, width).astype(jnp.float32)
    return layer_normalize(values)


def gate_of(logits):
    return 1.0 / (1.0 + jnp.exp(-logits))


def value_kernel(x_ref, grad_ref, wc_ref, wo_ref, out_ref, normed_ref):
    residues, width = x_ref.shape[1], x_ref.shape[2]
    normed = normalized(x_ref)[0].astype(jnp.bfloat16)
    normed_ref[...] = normed.reshape(normed_ref.shape)
    values = f32_dot(normed, wc_ref[:, 2 * width : 3 * width])
    gate = gate_of(f32_dot(normed, wc_ref[:, 3 * width :]))
    grad_gated = f32_dot(grad_ref[...].reshape(-1, width), wo_ref[...], NT)
    pack_heads(out_ref, 0, values, residues)
    pack_heads(out_ref, residues, grad_gated * gate, residues)


def query_kernel(scale, normed_ref, wc_ref, pair_ref, weight_ref, out_ref, bias_ref, mean_ref, spread_ref):
    residues, width = normed_ref.shape[1], normed_ref.shape[2]
    heads = weight_ref.shape[0]
    normed = normed_ref[...].reshape(-1, width)
    pack_heads(out_ref, 0, f32_dot(normed, wc_ref[:, :width]) * scale, residues)
    pack_heads(out_ref, residues, f32_dot(normed, wc_ref[:, width : 2 * width]), residues)

    columns, channels = pair_ref.shape[1], pair_ref.shape[2]
    first = weight_ref[...].astype(jnp.bfloat16)
    rest = weight_ref[...] - first.astype(jnp.float32)
    second, third = two_terms(rest)
    share = jnp.full((heads, channels), 1.0 / channels, jnp.bfloat16)
    left = jnp.concatenate([first, second, third, share], axis=0)
    ones = jnp.full((heads, channels), 1.0 / channels, jnp.bfloat16)
    average = jnp.full((channels, channels), 1.0 / channels, jnp.bfloat16)

    def rows(step, carry):
        for k in range(8):
            i = step * 8 + k
            entries = pair_ref[i]
            center = entries.astype(jnp.float32) - f32_dot(entries, average)
            high, low = two_terms(center * center)
            variance = f32_dot(ones, high, NT) + f32_dot(ones, low, NT)
            spread = lax.rsqrt(variance + eps_norm)
            raw = f32_dot(left, entries, NT)
            bias = spread * (raw[:heads] + raw[heads : 2 * heads] + raw[2 * heads : 3 * heads])
            bias_ref[:, i, :] = bias
            mean_ref[pl.ds(i, 1), :] = raw[3 * heads : 3 * heads + 1]
            spread_ref[pl.ds(i, 1), :] = spread[:1]
        return carry

    lax.fori_loop(0, pair_ref.shape[0] // 8, rows, 0)
    half = residues // 2
    for h in range(heads):
        for core in range(2):
            high, low = two_terms(bias_ref[h, core * half : (core + 1) * half, :])
            out_ref[h * 2 + core, 2 * residues : 2 * residues + half, :] = high
            out_ref[h * 2 + core, 2 * residues + half : 3 * residues, :] = low


def lanes_of(blocks_ref, row, residues):
    count = blocks_ref.shape[0] // 2
    planes = [
        blocks_ref[p * count : (p + 1) * count, row : row + residues, :].reshape(-1, LANES)
        for p in range(2)
    ]
    return jnp.concatenate(planes, axis=1)


def score_kernel(
    residues, left_row, right_row, with_bias, place_ref, own_ref, other_ref, mine_ref, sent_ref
):
    core, half = place_ref[0], place_ref[1]
    count = own_ref.shape[0] // 2
    part = residues // 2
    right = jnp.concatenate(
        [lanes_of(own_ref, right_row, residues), lanes_of(other_ref, right_row, residues)], axis=1
    )
    for which, ref in ((half, mine_ref), (1 - half, sent_ref)):
        left = []
        for k in range(count // 2):
            block = which * (count // 2) + k
            rows = pl.ds(pl.multiple_of(left_row + core * part, part), part)
            left.append(
                jnp.concatenate(
                    [
                        r[p * count + block, rows, :]
                        for r in (own_ref, other_ref)
                        for p in range(2)
                    ],
                    axis=1,
                )
            )
        ref[...] = f32_dot(jnp.concatenate(left, axis=0), right, NT).astype(ref.dtype)
        if with_bias:
            for p in range(2):
                columns = pl.ds(pl.multiple_of((half * 2 + p) * LANES, LANES), LANES)
                for k in range(count // 2):
                    block = p * count + which * (count // 2) + k
                    high = own_ref[block, 2 * residues : 2 * residues + part, :]
                    low = own_ref[block, 2 * residues + part : 3 * residues, :]
                    bias = high.astype(jnp.float32) + low.astype(jnp.float32)
                    ref[k * part : (k + 1) * part, columns] += bias


def split_kernel(place_ref, normed_ref, grad_ref, after_ref, keep_ref, send_ref):
    core = place_ref[0]
    for which, ref in ((core, keep_ref), (1 - core, send_ref)):
        for s in range(SLOTS):
            ref[0, s] = normed_ref[which * SLOTS + s]
            ref[1, s] = grad_ref[which * SLOTS + s]


def softmax_kernel(logit_ref, logit_other_ref, grad_ref, grad_other_ref, out_ref, prob_ref):
    logits = logit_ref[...] + logit_other_ref[...]
    lifted = jnp.exp(logits - jnp.max(logits, axis=-1, keepdims=True))
    softmax_out = lifted / jnp.sum(lifted, axis=-1, keepdims=True)
    prob_ref[...] = softmax_out.astype(jnp.bfloat16)
    grad_probs = grad_ref[...] + grad_other_ref[...].astype(jnp.float32)
    row_dot = jnp.sum(softmax_out * grad_probs, axis=-1, keepdims=True)
    out_ref[...] = (softmax_out * (grad_probs - row_dot)).astype(jnp.bfloat16)


def product_kernel(
    residues, scale, first_row, second_row, with_share,
    place_ref, own_ref, far_ref, near_ref, corner_ref, blocks_ref, out_ref, whole_ref,
):
    core, half = place_ref[0], place_ref[1]
    count = blocks_ref.shape[0] // 2
    part = residues // 2
    quarters = (
        (own_ref, core, half), (far_ref, core, 1 - half),
        (near_ref, 1 - core, half), (corner_ref, 1 - core, 1 - half),
    )
    for ref, c, z in quarters:
        for k in range(count // 2):
            start = (z * (count // 2) + k) * residues + c * part
            whole_ref[pl.ds(pl.multiple_of(start, part), part), :] = ref[k * part : (k + 1) * part, :]
    whole = whole_ref[...]
    if with_share:
        for p in range(2):
            columns = pl.ds(pl.multiple_of((half * 2 + p) * LANES, LANES), LANES)
            for q in range(count):
                rows = pl.ds(pl.multiple_of(q * residues + core * part, part), part)
                out_ref[p * count + q, 2 * residues : 2 * residues + part, :] = whole_ref[rows, columns]
    first = f32_dot(whole, lanes_of(blocks_ref, first_row, residues)) * scale
    second = f32_dot(whole, lanes_of(blocks_ref, second_row, residues), TN)
    for row, product in ((0, first), (residues, second)):
        for p in range(2):
            out_ref[p * count : (p + 1) * count, row : row + residues, :] = (
                product[:, p * LANES : (p + 1) * LANES]
                .astype(jnp.bfloat16)
                .reshape(count, residues, LANES)
            )


def share_of(blocks_ref, row, part, heads):
    return jnp.concatenate(
        [
            blocks_ref[:, row : row + part, :]
            .astype(jnp.float32)
            .reshape(heads, 2 * part, LANES)
        ],
        axis=0,
    )


def final_kernel(x_ref, grad_ref, wc_ref, wo_ref, attended_ref, blocks_ref, updated_ref, out_ref):
    residues, width = x_ref.shape[1], x_ref.shape[2]
    tiles = width // LANES
    normed, spread = normalized(x_ref)
    gate = gate_of(f32_dot(normed.astype(jnp.bfloat16), wc_ref[:, 3 * width :]))
    grad_gated = f32_dot(grad_ref[...].reshape(-1, width), wo_ref[...], NT)
    attended = unpack_heads(attended_ref, 0, residues, tiles)
    gated = (gate * attended).astype(jnp.bfloat16)
    updated_ref[...] = f32_dot(gated, wo_ref[...]).astype(jnp.bfloat16).reshape(updated_ref.shape)
    parts = [
        unpack_heads(blocks_ref, 0, residues, tiles),
        unpack_heads(blocks_ref, residues, residues, tiles),
        unpack_heads(attended_ref, residues, residues, tiles),
        grad_gated * attended * gate * (1.0 - gate),
    ]
    gradient = f32_dot(
        jnp.concatenate([p.astype(jnp.bfloat16) for p in parts], axis=1), wc_ref[...], NT
    )
    out_ref[...] = (
        layer_norm_backward(gradient, normed, spread).astype(jnp.bfloat16).reshape(out_ref.shape)
    )


def head_weight_kernel(
    place_ref, same_ref, cross_ref, gate_weight_ref, out_weight_ref, attended_ref, blocks_ref, sum_ref
):
    core, turn = place_ref[0], place_ref[2]
    count, residues = blocks_ref.shape[0] // 2, same_ref.shape[3]
    width = same_ref.shape[4]
    slot = lax.broadcasted_iota(jnp.int32, (2 * count * residues, LANES), 1) // (LANES // SLOTS)

    def tokens_of(t, s):
        rows = []
        for block in range(count):
            a, b = same_ref[block, t, s], cross_ref[block, t, s]
            rows += [jnp.where(core == 0, a, b), jnp.where(core == 0, b, a)]
        return jnp.concatenate(rows, axis=0)

    def tile_of(ref, row):
        return ref[:, row : row + residues, :].reshape(-1, LANES)

    attended = tile_of(attended_ref, 0).astype(jnp.float32)
    sums = [jnp.zeros((width, LANES), jnp.float32)] * 5
    for s in range(SLOTS):
        chosen = slot == lax.rem(turn + s, SLOTS)
        normed, grad = tokens_of(0, s), tokens_of(1, s)
        gate = gate_of(f32_dot(normed, gate_weight_ref[...]))
        grad_gated = f32_dot(grad, out_weight_ref[...], NT)
        gated = (gate * attended).astype(jnp.bfloat16)
        gate_logit = (grad_gated * attended * gate * (1.0 - gate)).astype(jnp.bfloat16)
        pieces = [
            tile_of(blocks_ref, 0),
            tile_of(blocks_ref, residues),
            tile_of(attended_ref, residues),
            gate_logit,
            gated,
        ]
        zero = jnp.zeros_like(gated)
        pieces = [jnp.where(chosen, p, zero) for p in pieces]
        products = f32_dot(normed, jnp.concatenate(pieces[:4], axis=1), TN)
        for t in range(4):
            sums[t] += products[:, t * LANES : (t + 1) * LANES]
        sums[4] += f32_dot(grad, pieces[4], TN)
    totals = []
    for part in sums:
        part = part + pltpu.roll(part, LANES // 2, 1)
        totals.append(part + pltpu.roll(part, LANES // 4, 1))
    sum_ref[:width, :] = slot_select(totals[:4])
    quarter = width // SLOTS
    sum_ref[width:, :] = slot_select(
        [totals[4][k * quarter : (k + 1) * quarter] for k in range(SLOTS)]
    )


def pair_weight_kernel(blocks_ref, pair_ref, mean_ref, spread_ref, sums_ref, out_ref, share_ref):
    heads, part = share_ref.shape[0], pair_ref.shape[0] // 2
    share_ref[...] = share_of(blocks_ref, blocks_ref.shape[1] - part, part, heads)

    def rows(step, carry):
        total, shift = carry
        for k in range(8):
            i = step * 8 + k
            scaled = share_ref[:, i, :] * spread_ref[pl.ds(i, 1), :]
            high, low = two_terms(scaled)
            total += f32_dot(jnp.concatenate([high, low], axis=0), pair_ref[i])
            shift += (high.astype(jnp.float32) + low.astype(jnp.float32)) * mean_ref[pl.ds(i, 1), :]
        return total, shift

    channels = pair_ref.shape[2]
    total, shift = lax.fori_loop(
        0,
        pair_ref.shape[0] // 8,
        rows,
        (jnp.zeros((2 * heads, channels), jnp.float32), jnp.zeros((heads, LANES), jnp.float32)),
    )
    count = sums_ref.shape[0]
    out_ref[:count, :] = sums_ref[...]
    out_ref[count:, :] = total[:heads] + total[heads:] - jnp.sum(shift, axis=1, keepdims=True)


def add_kernel(mine_ref, other_ref, out_ref):
    count = mine_ref.shape[0]
    out_ref[:count, :] = (
        mine_ref[...].astype(jnp.float32) + other_ref[:count, :].astype(jnp.float32)
    ).astype(out_ref.dtype)
    if out_ref.shape[0] > count:
        out_ref[count:, :] = jnp.zeros((out_ref.shape[0] - count, LANES), out_ref.dtype)


def spread_kernel(parts_ref, combined_ref, out_weight_ref, pair_weight_ref):
    heads, width = parts_ref.shape[0], combined_ref.shape[0]
    slot_lanes = LANES // SLOTS
    quarter = width // SLOTS
    for tile in range(heads // SLOTS):
        parts = [parts_ref[tile * SLOTS + j, :width, :].astype(jnp.float32) for j in range(SLOTS)]
        for t in range(4):
            moved = []
            for j in range(SLOTS):
                shift = (j - t) % SLOTS * slot_lanes
                moved.append(pltpu.roll(parts[j], shift, 1) if shift else parts[j])
            start = t * width + tile * LANES
            combined_ref[:, start : start + LANES] = slot_select(moved)
    for h in range(heads):
        turned = parts_ref[h, width : width + quarter, :].astype(jnp.float32).T
        out_weight_ref[h * slot_lanes : (h + 1) * slot_lanes, :] = jnp.concatenate(
            [turned[k * slot_lanes : (k + 1) * slot_lanes, :] for k in range(SLOTS)], axis=1
        )
    total = jnp.zeros(pair_weight_ref.shape, jnp.float32)
    for h in range(heads):
        total += parts_ref[h, width + quarter :, :].astype(jnp.float32)[:heads]
    pair_weight_ref[...] = total


def pair_kernel(blocks_row, blocks_ref, pair_ref, weight_ref, bias_ref, mean_ref, spread_ref, out_ref, share_ref):
    heads, channels = weight_ref.shape
    part = pair_ref.shape[0] // 2
    share_ref[...] = share_of(blocks_ref, blocks_row, part, heads)
    first, second = two_terms(weight_ref[...])
    zero = jnp.zeros((heads, channels), jnp.bfloat16)
    top = lax.broadcasted_iota(jnp.int32, (heads, channels), 0) < 2
    ones = jnp.where(top, 1.0, 0.0).astype(jnp.bfloat16)
    right = jnp.concatenate(
        [
            jnp.concatenate([first, first, second, ones, zero], axis=0),
            jnp.concatenate([zero, zero, zero, zero, ones], axis=0),
        ],
        axis=1,
    )
    row = lax.broadcasted_iota(jnp.int32, (heads, LANES), 0)

    def rows_of_two(value):
        high, low = two_terms(value)
        high, low = high.astype(jnp.float32), low.astype(jnp.float32)
        return jnp.where(row == 0, high, jnp.where(row == 1, low, 0.0)).astype(jnp.bfloat16)

    def rows(step, carry):
        for k in range(8):
            i = step * 8 + k
            gradient = share_ref[:, i, :]
            spread = spread_ref[pl.ds(i, 1), :]
            cross = jnp.sum(gradient * bias_ref[:, i, :], axis=0, keepdims=True) / channels
            slope = spread * spread * cross
            high, low = two_terms(gradient * spread)
            left = jnp.concatenate(
                [
                    high, low, high,
                    rows_of_two(jnp.broadcast_to(slope * mean_ref[pl.ds(i, 1), :], row.shape)),
                    rows_of_two(jnp.broadcast_to(slope, row.shape)),
                ],
                axis=0,
            )
            terms = f32_dot(left, right, TN)
            entries = pair_ref[i].astype(jnp.float32)
            out_ref[i] = (terms[:, :channels] - terms[:, channels:] * entries).astype(jnp.bfloat16)
        return carry

    lax.fori_loop(0, pair_ref.shape[0] // 8, rows, 0)


def call(kernel, outs, *args, scratch=(), place=None, flops=0):
    whole = pl.BlockSpec(memory_space=pltpu.VMEM)
    specs = [whole] * len(args)
    if place is not None:
        specs = [pl.BlockSpec(memory_space=pltpu.SMEM)] + specs
        args = (place,) + args
    shapes = [jax.ShapeDtypeStruct(*o) for o in outs]
    moved = sum(math.prod(a.shape) * a.dtype.itemsize for a in list(args) + shapes)
    result = pl.pallas_call(
        kernel,
        out_shape=shapes,
        in_specs=specs,
        out_specs=[whole] * len(shapes),
        scratch_shapes=scratch,
        compiler_params=pltpu.CompilerParams(vmem_limit_bytes=VMEM_LIMIT),
        cost_estimate=pl.CostEstimate(flops=flops, bytes_accessed=moved, transcendentals=0),
    )(*args)
    return result


def swapped(mine, axis_name, distance):
    size = lax.axis_size(axis_name)
    return lax.ppermute(mine, axis_name, [(a, a ^ distance) for a in range(size)])


def fits_heads(alignment_rows, pair_entries, pair_weight):
    channels, heads = pair_weight.shape
    return (
        lax.axis_size("seq") == 4
        and lax.axis_size("res") == heads == 8
        and alignment_rows.shape[0] == 2 * SLOTS
        and alignment_rows.shape[1] == pair_entries.shape[0] == 64
        and alignment_rows.shape[2] == 2 * LANES
        and pair_entries.shape[1] == channels == LANES
    )


def head_body(
    alignment_rows, pair_entries, combined_weight, output_weight, pair_weight, updated_gradient
):
    sequences, residues, width = alignment_rows.shape
    channels, heads = pair_weight.shape
    tokens = sequences * residues
    seq_size, res_size = lax.axis_size("seq"), lax.axis_size("res")
    seq_half = seq_size // 2
    total = residues * res_size
    group = 2 * res_size
    groups = [[g * group + k for k in range(group)] for g in range(seq_half)]
    scale = 1.0 / math.sqrt(width // heads * sequences * seq_size)
    res_index, seq_index = lax.axis_index("res"), lax.axis_index("seq")
    head = seq_index % 2 * (res_size // 2) + res_index // 2
    place = jnp.stack([res_index % 2, seq_index // 2, head % SLOTS]).astype(jnp.int32)
    bf16, f32 = jnp.bfloat16, jnp.float32

    def across(blocks):
        return lax.all_to_all(blocks, ("seq", "res"), 0, 0, axis_index_groups=groups, tiled=True)

    core_groups = [
        [g * group + 2 * k + core for k in range(res_size)]
        for g in range(seq_half)
        for core in range(2)
    ]

    def over_heads(mine):
        return lax.all_gather(mine, ("seq", "res"), axis=0, axis_index_groups=core_groups)

    def all_quarters(mine):
        far = swapped(mine, "seq", seq_half)
        return mine, far, swapped(mine, "res", 1), swapped(far, "res", 1)

    x, grad, wc, wo = alignment_rows, updated_gradient, combined_weight, output_weight
    value_blocks, normed = call(
        value_kernel, [((group, 2 * residues, LANES), bf16), (x.shape, bf16)], x, grad, wc, wo,
        flops=8 * tokens * width * width,
    )
    value_blocks = across(value_blocks)
    centred = (pair_weight - jnp.mean(pair_weight, axis=0, keepdims=True)).T
    query_blocks, bias, mean, spread = call(
        functools.partial(query_kernel, scale),
        [
            ((group, 3 * residues, LANES), bf16),
            ((heads, residues, LANES), f32),
            ((residues, LANES), f32),
            ((residues, LANES), f32),
        ],
        normed, wc, pair_entries, centred,
        flops=8 * tokens * width * width,
    )
    query_blocks = across(query_blocks)

    def scores(blocks, left_row, right_row, with_bias, kind):
        return call(
            functools.partial(score_kernel, residues, left_row, right_row, with_bias),
            [((total // 4, total), f32), ((total // 4, total), kind)],
            blocks, swapped(blocks, "res", 1),
            place=place, flops=2 * total * total * width,
        )

    grad_mine, grad_sent = scores(value_blocks, residues, 0, False, bf16)
    grad_other = swapped(grad_sent, "seq", seq_half)
    half_tokens = ((2, sequences // 2, residues, width), bf16)
    keep, send = call(
        split_kernel, [half_tokens, half_tokens], normed, grad, grad_mine, place=place
    )
    same_tokens, cross_tokens = over_heads(keep), over_heads(swapped(send, "res", 1))

    logit_mine, logit_sent = scores(query_blocks, 0, residues, True, f32)
    logit_other = swapped(logit_sent, "seq", seq_half)
    quarter = ((total // 4, total), bf16)
    grad_logits, probs = call(
        softmax_kernel, [quarter, quarter], logit_mine, logit_other, grad_mine, grad_other,
        flops=total * total,
    )

    def products(quarters, blocks, first_row, second_row, with_share, factor):
        rows = 2 * residues + (residues // 2 if with_share else 0)
        (out,) = call(
            functools.partial(
                product_kernel, residues, factor, first_row, second_row, with_share
            ),
            [((group, rows, LANES), bf16)],
            *quarters, blocks,
            scratch=[pltpu.VMEM((total, total), bf16)],
            place=place, flops=4 * total * total * width,
        )
        return out

    grad_sums = products(all_quarters(grad_logits), query_blocks, residues, 0, True, scale)
    grad_blocks = across(grad_sums)
    attended = products(all_quarters(probs), value_blocks, 0, residues, False, 1.0)
    attended_blocks = across(attended)

    head_dim = width // heads
    gate_weight = jnp.tile(
        lax.dynamic_slice_in_dim(wc, 3 * width + head * head_dim, head_dim, 1), (1, SLOTS)
    )
    out_weight = jnp.tile(
        lax.dynamic_slice_in_dim(wo, head * head_dim, head_dim, 0), (SLOTS, 1)
    )
    rows = width + width // SLOTS
    (sums,) = call(
        head_weight_kernel, [((rows, LANES), f32)],
        same_tokens, cross_tokens, gate_weight, out_weight, attended, grad_sums,
        place=place, flops=20 * 4 * tokens * width * LANES,
    )
    (sums,) = call(
        pair_weight_kernel, [((rows + heads, LANES), f32)],
        grad_blocks, pair_entries, mean, spread, sums,
        scratch=[pltpu.VMEM((heads, residues, LANES), f32)],
        flops=4 * tokens * width * width,
    )
    wire = ((rows + 2 * heads, LANES), bf16)
    (sums,) = call(add_kernel, [wire], sums, swapped(sums, "res", 1))
    (sums,) = call(add_kernel, [wire], sums, swapped(sums, "seq", seq_half))
    parts = over_heads(sums)
    combined_weight_gradient, output_weight_gradient, pair_weight_gradient = call(
        spread_kernel, [(wc.shape, f32), (wo.shape, f32), ((heads, channels), f32)], parts
    )

    updated, alignment_gradient = call(
        final_kernel, [(x.shape, bf16), (x.shape, bf16)],
        x, grad, wc, wo, attended_blocks, grad_blocks,
        flops=14 * tokens * width * width,
    )
    (pair_gradient,) = call(
        functools.partial(pair_kernel, 2 * residues),
        [(pair_entries.shape, bf16)],
        grad_blocks, pair_entries, centred, bias, mean, spread,
        scratch=[pltpu.VMEM((heads, residues, LANES), f32)],
        flops=8 * tokens * width * width,
    )
    return (
        updated,
        alignment_gradient,
        pair_gradient,
        combined_weight_gradient,
        output_weight_gradient,
        pair_weight_gradient.T,
    )


def body(alignment_rows, pair_entries, combined_weight, output_weight, pair_weight, updated_gradient):
    chosen = head_body if fits_heads(alignment_rows, pair_entries, pair_weight) else gathered_body
    return chosen(
        alignment_rows, pair_entries, combined_weight, output_weight, pair_weight, updated_gradient
    )


def solution(mesh):
    return jax.shard_map(
        body,
        mesh=mesh,
        in_specs=(
            P("seq", "res", None),
            P("res", "seq", None),
            P(),
            P(),
            P(),
            P("seq", "res", None),
        ),
        out_specs=(
            P("seq", "res", None),
            P("seq", "res", None),
            P("res", "seq", None),
            P(),
            P(),
            P(),
        ),
        check_vma=False,
    )
```

```python
import functools
import math

import jax
import jax.numpy as jnp
from jax import lax
from jax.experimental import pallas as pl
from jax.experimental.pallas import tpu as pltpu
from jax.sharding import PartitionSpec as P

eps_norm = 1e-05


def layer_normalize(values):
    values = values.astype(jnp.float32)
    center = values - jnp.mean(values, axis=-1, keepdims=True)
    broadcast_pair = lax.rsqrt(jnp.mean(center * center, axis=-1, keepdims=True) + eps_norm)
    return (center * broadcast_pair, broadcast_pair)


def layer_norm_backward(normalized_gradient, normalized_rows, broadcast_pair):
    mean_grad = jnp.mean(normalized_gradient, axis=-1, keepdims=True)
    mean_cross = jnp.mean(normalized_gradient * normalized_rows, axis=-1, keepdims=True)
    return broadcast_pair * (normalized_gradient - mean_grad - normalized_rows * mean_cross)


def split_heads(tensor, head_count):
    return tensor.reshape(
        tensor.shape[0], tensor.shape[1], head_count, tensor.shape[2] // head_count
    )


def merge_heads(tensor):
    return tensor.reshape(tensor.shape[0], tensor.shape[1], tensor.shape[2] * tensor.shape[3])


def gathered_body(
    alignment_rows, pair_entries, combined_weight, output_weight, pair_weight, updated_gradient
):
    sequence_count, residue_count, alignment_width = alignment_rows.shape
    head_count = pair_weight.shape[1]
    query_width = output_weight.shape[0]
    head_dim = query_width // head_count
    column_count = pair_entries.shape[1]
    token_count = sequence_count * residue_count
    score_scale = 1.0 / math.sqrt(head_dim * sequence_count * lax.axis_size("seq"))
    normalized_rows, broadcast_pair = layer_normalize(alignment_rows)
    normalized_rows_backward = normalized_rows.astype(jnp.bfloat16).reshape(
        token_count, alignment_width
    )
    projected = jnp.dot(
        normalized_rows_backward, combined_weight, preferred_element_type=jnp.float32
    ).reshape(sequence_count, residue_count, 4 * query_width)
    queries = (projected[..., :query_width] * score_scale).astype(jnp.bfloat16)
    key_rows = projected[..., query_width : 2 * query_width].astype(jnp.bfloat16)
    value_rows = projected[..., 2 * query_width : 3 * query_width].astype(jnp.bfloat16)
    gate_open = jax.nn.sigmoid(projected[..., 3 * query_width :])
    all_keys, all_values = (
        lax.all_gather(key_rows, "res", axis=1, tiled=True),
        lax.all_gather(value_rows, "res", axis=1, tiled=True),
    )
    query_heads = split_heads(queries, head_count)
    key_heads = split_heads(all_keys, head_count)
    value_heads = split_heads(all_values, head_count)
    score_terms = jnp.einsum(
        "sihd,sjhd->hij", query_heads, key_heads, preferred_element_type=jnp.float32
    )
    pair_normed, pair_spread = layer_normalize(pair_entries)
    pair_bias = jnp.einsum("ijc,ch->hij", pair_normed, pair_weight, precision=lax.Precision.HIGHEST)
    col_start = lax.axis_index("seq") * column_count
    own_block = lax.dynamic_slice_in_dim(score_terms, col_start, column_count, 2) + pair_bias
    logits = lax.psum(lax.dynamic_update_slice_in_dim(score_terms, own_block, col_start, 2), "seq")
    row_top = jnp.max(logits, axis=-1, keepdims=True)
    lifted = jnp.exp(logits - row_top)
    softmax_out = lifted / jnp.sum(lifted, axis=-1, keepdims=True)
    softmax_low = softmax_out.astype(jnp.bfloat16)
    attended = merge_heads(
        jnp.einsum("hij,sjhd->sihd", softmax_low, value_heads, preferred_element_type=jnp.float32)
    )
    gated_out = (gate_open * attended).astype(jnp.bfloat16)
    flattened_gated = gated_out.reshape(token_count, query_width)
    updated = (
        jnp.dot(flattened_gated, output_weight, preferred_element_type=jnp.float32)
        .astype(jnp.bfloat16)
        .reshape(sequence_count, residue_count, alignment_width)
    )
    flattened_gradient = updated_gradient.reshape(token_count, alignment_width)
    grad_gated = jnp.dot(
        flattened_gradient, output_weight.T, preferred_element_type=jnp.float32
    ).reshape(sequence_count, residue_count, query_width)
    out_local = jnp.dot(flattened_gated.T, flattened_gradient, preferred_element_type=jnp.float32)
    grad_attended = (grad_gated * gate_open).astype(jnp.bfloat16)
    grad_gate_logit = grad_gated * attended * gate_open * (1.0 - gate_open)
    attended_grad_heads = split_heads(grad_attended, head_count)
    grad_terms = jnp.einsum(
        "sihd,sjhd->hij", attended_grad_heads, value_heads, preferred_element_type=jnp.float32
    )
    grad_probs = lax.psum(grad_terms, "seq")
    row_dot = jnp.sum(softmax_out * grad_probs, axis=-1, keepdims=True)
    grad_logits = softmax_out * (grad_probs - row_dot)
    grad_logits_b = grad_logits.astype(jnp.bfloat16)
    logit_share = lax.dynamic_slice_in_dim(grad_logits, col_start, column_count, 2)
    grad_query_heads = (
        jnp.einsum("hij,sjhd->sihd", grad_logits_b, key_heads, preferred_element_type=jnp.float32)
        * score_scale
    )
    key_part = jnp.einsum(
        "hij,sihd->jshd", grad_logits_b, query_heads, preferred_element_type=jnp.float32
    )
    value_part = jnp.einsum(
        "hij,sihd->jshd", softmax_low, attended_grad_heads, preferred_element_type=jnp.float32
    )
    summed = lax.psum_scatter(
        jnp.concatenate([merge_heads(key_part), merge_heads(value_part)], axis=-1),
        "res",
        scatter_dimension=0,
        tiled=True,
    )
    key_value_grads = jnp.transpose(summed, (1, 0, 2))
    projected_gradient = jnp.concatenate(
        [merge_heads(grad_query_heads), key_value_grads, grad_gate_logit], axis=-1
    )
    projected_gradient = projected_gradient.astype(jnp.bfloat16).reshape(
        token_count, 4 * query_width
    )
    qkvg_local = jnp.dot(
        normalized_rows_backward.T, projected_gradient, preferred_element_type=jnp.float32
    )
    normalized_gradient = jnp.dot(
        projected_gradient, combined_weight.T, preferred_element_type=jnp.float32
    ).reshape(sequence_count, residue_count, alignment_width)
    alignment_gradient = layer_norm_backward(
        normalized_gradient, normalized_rows, broadcast_pair
    ).astype(jnp.bfloat16)
    pair_w_local = jnp.einsum(
        "ijc,hij->ch", pair_normed, logit_share, precision=lax.Precision.HIGHEST
    )
    grad_pair_normed = jnp.einsum(
        "hij,ch->ijc", logit_share, pair_weight, precision=lax.Precision.HIGHEST
    )
    pair_gradient = layer_norm_backward(grad_pair_normed, pair_normed, pair_spread).astype(
        jnp.bfloat16
    )
    combined_weight_gradient, output_weight_gradient, pair_weight_gradient = lax.psum(
        (qkvg_local, out_local, pair_w_local), ("seq", "res")
    )
    return (
        updated,
        alignment_gradient,
        pair_gradient,
        combined_weight_gradient,
        output_weight_gradient,
        pair_weight_gradient,
    )


VMEM_LIMIT = 48 * 1024 * 1024
LANES = 128
SLOTS = 4
NT = (((1,), (1,)), ((), ()))
TN = (((0,), (0,)), ((), ()))


def f32_dot(left, right, dims=None):
    if dims is None:
        return jnp.dot(left, right, preferred_element_type=jnp.float32)
    return lax.dot_general(left, right, dims, preferred_element_type=jnp.float32)


def two_terms(values):
    high = values.astype(jnp.bfloat16)
    return high, (values - high.astype(jnp.float32)).astype(jnp.bfloat16)


def slot_select(pieces):
    slot = lax.broadcasted_iota(jnp.int32, pieces[0].shape, 1) // (LANES // SLOTS)
    result = pieces[0]
    for k in range(1, SLOTS):
        result = jnp.where(slot == k, pieces[k], result)
    return result


def pack_heads(out_ref, row, tensor, residues):
    for core in range(2):
        for tile in range(tensor.shape[1] // LANES):
            rolled = []
            for s in range(SLOTS):
                start = (core * SLOTS + s) * residues
                piece = tensor[start : start + residues, tile * LANES : (tile + 1) * LANES]
                rolled.append(pltpu.roll(piece, s * LANES // SLOTS, 1) if s else piece)
            for j in range(SLOTS):
                block = slot_select([rolled[(k - j) % SLOTS] for k in range(SLOTS)])
                out_ref[(tile * SLOTS + j) * 2 + core, row : row + residues, :] = block.astype(
                    jnp.bfloat16
                )


def unpack_heads(in_ref, row, residues, tiles):
    rows = []
    for core in range(2):
        for s in range(SLOTS):
            pieces = []
            for tile in range(tiles):
                blocks = [
                    in_ref[
                        (tile * SLOTS + (k - s) % SLOTS) * 2 + core, row : row + residues, :
                    ].astype(jnp.float32)
                    for k in range(SLOTS)
                ]
                block = slot_select(blocks)
                pieces.append(pltpu.roll(block, LANES - s * LANES // SLOTS, 1) if s else block)
            rows.append(jnp.concatenate(pieces, axis=1))
    return jnp.concatenate(rows, axis=0)


def normalized(x_ref):
    width = x_ref.shape[-1]
    values = x_ref[...].reshape(-1, width).astype(jnp.float32)
    return layer_normalize(values)


def gate_of(logits):
    return 1.0 / (1.0 + jnp.exp(-logits))


def value_kernel(
    place_ref, x_ref, grad_ref, wc_ref, wo_ref, out_ref, normed_ref, keep_ref, send_ref
):
    residues, width = x_ref.shape[1], x_ref.shape[2]
    core = place_ref[0]
    normed = normalized(x_ref)[0].astype(jnp.bfloat16)
    normed_ref[...] = normed.reshape(normed_ref.shape)
    values = f32_dot(normed, wc_ref[:, 2 * width : 3 * width])
    gate = gate_of(f32_dot(normed, wc_ref[:, 3 * width :]))
    grad_gated = f32_dot(grad_ref[...].reshape(-1, width), wo_ref[...], NT)
    pack_heads(out_ref, 0, values, residues)
    pack_heads(out_ref, residues, grad_gated * gate, residues)
    for which, ref in ((core, keep_ref), (1 - core, send_ref)):
        for s in range(SLOTS):
            ref[0, s] = normed_ref[which * SLOTS + s]
            ref[1, s] = grad_ref[which * SLOTS + s]


def merge_kernel(place_ref, keep_ref, other_ref, normed_ref, grad_ref):
    core = place_ref[0]
    for t, ref in ((0, normed_ref), (1, grad_ref)):
        ref[core] = keep_ref[t]
        ref[1 - core] = other_ref[t]


def query_kernel(scale, normed_ref, wc_ref, pair_ref, weight_ref, out_ref, bias_ref, mean_ref, spread_ref):
    residues, width = normed_ref.shape[1], normed_ref.shape[2]
    heads = weight_ref.shape[0]
    normed = normed_ref[...].reshape(-1, width)
    pack_heads(out_ref, 0, f32_dot(normed, wc_ref[:, :width]) * scale, residues)
    pack_heads(out_ref, residues, f32_dot(normed, wc_ref[:, width : 2 * width]), residues)

    columns, channels = pair_ref.shape[1], pair_ref.shape[2]
    first = weight_ref[...].astype(jnp.bfloat16)
    rest = weight_ref[...] - first.astype(jnp.float32)
    second, third = two_terms(rest)
    share = jnp.full((heads, channels), 1.0 / channels, jnp.bfloat16)
    left = jnp.concatenate([first, second, third, share], axis=0)
    ones = jnp.full((heads, channels), 1.0 / channels, jnp.bfloat16)
    average = jnp.full((channels, channels), 1.0 / channels, jnp.bfloat16)

    def rows(step, carry):
        for k in range(8):
            i = step * 8 + k
            entries = pair_ref[i]
            center = entries.astype(jnp.float32) - f32_dot(entries, average)
            high, low = two_terms(center * center)
            variance = f32_dot(ones, high, NT) + f32_dot(ones, low, NT)
            spread = lax.rsqrt(variance + eps_norm)
            raw = f32_dot(left, entries, NT)
            bias = spread * (raw[:heads] + raw[heads : 2 * heads] + raw[2 * heads : 3 * heads])
            bias_ref[:, i, :] = bias
            mean_ref[pl.ds(i, 1), :] = raw[3 * heads : 3 * heads + 1]
            spread_ref[pl.ds(i, 1), :] = spread[:1]
        return carry

    lax.fori_loop(0, pair_ref.shape[0] // 8, rows, 0)
    half = residues // 2
    for h in range(heads):
        for core in range(2):
            high, low = two_terms(bias_ref[h, core * half : (core + 1) * half, :])
            out_ref[h * 2 + core, 2 * residues : 2 * residues + half, :] = high
            out_ref[h * 2 + core, 2 * residues + half : 3 * residues, :] = low


def lanes_of(blocks_ref, row, residues):
    count = blocks_ref.shape[0] // 2
    planes = [
        blocks_ref[p * count : (p + 1) * count, row : row + residues, :].reshape(-1, LANES)
        for p in range(2)
    ]
    return jnp.concatenate(planes, axis=1)


def score_kernel(
    residues, left_row, right_row, with_bias, place_ref, own_ref, other_ref, mine_ref, sent_ref
):
    core, half = place_ref[0], place_ref[1]
    count = own_ref.shape[0] // 2
    part = residues // 2
    right = jnp.concatenate(
        [lanes_of(own_ref, right_row, residues), lanes_of(other_ref, right_row, residues)], axis=1
    )
    for which, ref in ((half, mine_ref), (1 - half, sent_ref)):
        left = []
        for k in range(count // 2):
            block = which * (count // 2) + k
            rows = pl.ds(pl.multiple_of(left_row + core * part, part), part)
            left.append(
                jnp.concatenate(
                    [
                        r[p * count + block, rows, :]
                        for r in (own_ref, other_ref)
                        for p in range(2)
                    ],
                    axis=1,
                )
            )
        ref[...] = f32_dot(jnp.concatenate(left, axis=0), right, NT).astype(ref.dtype)
        if with_bias:
            for p in range(2):
                columns = pl.ds(pl.multiple_of((half * 2 + p) * LANES, LANES), LANES)
                for k in range(count // 2):
                    block = p * count + which * (count // 2) + k
                    high = own_ref[block, 2 * residues : 2 * residues + part, :]
                    low = own_ref[block, 2 * residues + part : 3 * residues, :]
                    bias = high.astype(jnp.float32) + low.astype(jnp.float32)
                    ref[k * part : (k + 1) * part, columns] += bias


def softmax_kernel(logit_ref, logit_other_ref, grad_ref, grad_other_ref, out_ref, prob_ref):
    logits = logit_ref[...] + logit_other_ref[...]
    lifted = jnp.exp(logits - jnp.max(logits, axis=-1, keepdims=True))
    softmax_out = lifted / jnp.sum(lifted, axis=-1, keepdims=True)
    prob_ref[...] = softmax_out.astype(jnp.bfloat16)
    grad_probs = grad_ref[...] + grad_other_ref[...].astype(jnp.float32)
    row_dot = jnp.sum(softmax_out * grad_probs, axis=-1, keepdims=True)
    out_ref[...] = (softmax_out * (grad_probs - row_dot)).astype(jnp.bfloat16)


def product_kernel(
    residues, scale, first_row, second_row, with_share,
    place_ref, own_ref, far_ref, near_ref, corner_ref, blocks_ref, out_ref, whole_ref,
):
    core, half = place_ref[0], place_ref[1]
    count = blocks_ref.shape[0] // 2
    part = residues // 2
    quarters = (
        (own_ref, core, half), (far_ref, core, 1 - half),
        (near_ref, 1 - core, half), (corner_ref, 1 - core, 1 - half),
    )
    for ref, c, z in quarters:
        for k in range(count // 2):
            start = (z * (count // 2) + k) * residues + c * part
            whole_ref[pl.ds(pl.multiple_of(start, part), part), :] = ref[k * part : (k + 1) * part, :]
    whole = whole_ref[...]
    if with_share:
        for p in range(2):
            columns = pl.ds(pl.multiple_of((half * 2 + p) * LANES, LANES), LANES)
            for q in range(count):
                rows = pl.ds(pl.multiple_of(q * residues + core * part, part), part)
                out_ref[p * count + q, 2 * residues : 2 * residues + part, :] = whole_ref[rows, columns]
    first = f32_dot(whole, lanes_of(blocks_ref, first_row, residues)) * scale
    second = f32_dot(whole, lanes_of(blocks_ref, second_row, residues), TN)
    for row, product in ((0, first), (residues, second)):
        for p in range(2):
            out_ref[p * count : (p + 1) * count, row : row + residues, :] = (
                product[:, p * LANES : (p + 1) * LANES]
                .astype(jnp.bfloat16)
                .reshape(count, residues, LANES)
            )


def share_of(blocks_ref, row, part, heads):
    return jnp.concatenate(
        [
            blocks_ref[:, row : row + part, :]
            .astype(jnp.float32)
            .reshape(heads, 2 * part, LANES)
        ],
        axis=0,
    )


def final_kernel(x_ref, grad_ref, wc_ref, wo_ref, attended_ref, blocks_ref, updated_ref, out_ref):
    residues, width = x_ref.shape[1], x_ref.shape[2]
    tiles = width // LANES
    normed, spread = normalized(x_ref)
    gate = gate_of(f32_dot(normed.astype(jnp.bfloat16), wc_ref[:, 3 * width :]))
    grad_gated = f32_dot(grad_ref[...].reshape(-1, width), wo_ref[...], NT)
    attended = unpack_heads(attended_ref, 0, residues, tiles)
    gated = (gate * attended).astype(jnp.bfloat16)
    updated_ref[...] = f32_dot(gated, wo_ref[...]).astype(jnp.bfloat16).reshape(updated_ref.shape)
    parts = [
        unpack_heads(blocks_ref, 0, residues, tiles),
        unpack_heads(blocks_ref, residues, residues, tiles),
        unpack_heads(attended_ref, residues, residues, tiles),
        grad_gated * attended * gate * (1.0 - gate),
    ]
    gradient = f32_dot(
        jnp.concatenate([p.astype(jnp.bfloat16) for p in parts], axis=1), wc_ref[...], NT
    )
    out_ref[...] = (
        layer_norm_backward(gradient, normed, spread).astype(jnp.bfloat16).reshape(out_ref.shape)
    )


def head_weight_kernel(place_ref, *refs):
    turn, chip = place_ref[2], place_ref[3]
    flips = (len(refs) - 5) // 2
    normed_refs, grad_refs = refs[:flips], refs[flips : 2 * flips]
    gate_weight_ref, out_weight_ref, attended_ref, blocks_ref, sum_ref = refs[2 * flips :]
    residues, width = normed_refs[0].shape[2], normed_refs[0].shape[3]
    slot = lax.broadcasted_iota(jnp.int32, (2 * flips * residues, LANES), 1) // (LANES // SLOTS)

    def tokens_of(arrays, s):
        return jnp.concatenate([r[c, s] for r in arrays for c in range(2)], axis=0)

    def tile_of(ref, row):
        rows = []
        for flip in range(flips):
            block = jnp.bitwise_xor(chip, flip) * 2
            rows += [ref[block + c, row : row + residues, :] for c in range(2)]
        return jnp.concatenate(rows, axis=0)

    attended = tile_of(attended_ref, 0).astype(jnp.float32)
    sums = [jnp.zeros((width, LANES), jnp.float32)] * 5
    for s in range(SLOTS):
        chosen = slot == lax.rem(turn + s, SLOTS)
        normed, grad = tokens_of(normed_refs, s), tokens_of(grad_refs, s)
        gate = gate_of(f32_dot(normed, gate_weight_ref[...]))
        grad_gated = f32_dot(grad, out_weight_ref[...], NT)
        gated = (gate * attended).astype(jnp.bfloat16)
        gate_logit = (grad_gated * attended * gate * (1.0 - gate)).astype(jnp.bfloat16)
        pieces = [
            tile_of(blocks_ref, 0),
            tile_of(blocks_ref, residues),
            tile_of(attended_ref, residues),
            gate_logit,
            gated,
        ]
        zero = jnp.zeros_like(gated)
        pieces = [jnp.where(chosen, p, zero) for p in pieces]
        products = f32_dot(normed, jnp.concatenate(pieces[:4], axis=1), TN)
        for t in range(4):
            sums[t] += products[:, t * LANES : (t + 1) * LANES]
        sums[4] += f32_dot(grad, pieces[4], TN)
    totals = []
    for part in sums:
        part = part + pltpu.roll(part, LANES // 2, 1)
        totals.append(part + pltpu.roll(part, LANES // 4, 1))
    sum_ref[:width, :] = slot_select(totals[:4])
    quarter = width // SLOTS
    sum_ref[width:, :] = slot_select(
        [totals[4][k * quarter : (k + 1) * quarter] for k in range(SLOTS)]
    )


def pair_weight_kernel(blocks_ref, pair_ref, mean_ref, spread_ref, sums_ref, out_ref, share_ref):
    heads, part = share_ref.shape[0], pair_ref.shape[0] // 2
    share_ref[...] = share_of(blocks_ref, blocks_ref.shape[1] - part, part, heads)

    def rows(step, carry):
        total, shift = carry
        for k in range(8):
            i = step * 8 + k
            scaled = share_ref[:, i, :] * spread_ref[pl.ds(i, 1), :]
            high, low = two_terms(scaled)
            total += f32_dot(jnp.concatenate([high, low], axis=0), pair_ref[i])
            shift += (high.astype(jnp.float32) + low.astype(jnp.float32)) * mean_ref[pl.ds(i, 1), :]
        return total, shift

    channels = pair_ref.shape[2]
    total, shift = lax.fori_loop(
        0,
        pair_ref.shape[0] // 8,
        rows,
        (jnp.zeros((2 * heads, channels), jnp.float32), jnp.zeros((heads, LANES), jnp.float32)),
    )
    count = sums_ref.shape[0]
    out_ref[:count, :] = sums_ref[...]
    out_ref[count:, :] = total[:heads] + total[heads:] - jnp.sum(shift, axis=1, keepdims=True)


def add_kernel(mine_ref, other_ref, out_ref):
    count = mine_ref.shape[0]
    out_ref[:count, :] = (
        mine_ref[...].astype(jnp.float32) + other_ref[:count, :].astype(jnp.float32)
    ).astype(out_ref.dtype)
    if out_ref.shape[0] > count:
        out_ref[count:, :] = jnp.zeros((out_ref.shape[0] - count, LANES), out_ref.dtype)


def spread_kernel(parts_ref, combined_ref, out_weight_ref, pair_weight_ref):
    heads, width = parts_ref.shape[0], combined_ref.shape[0]
    slot_lanes = LANES // SLOTS
    quarter = width // SLOTS
    for tile in range(heads // SLOTS):
        parts = [parts_ref[2 * j + tile, :width, :].astype(jnp.float32) for j in range(SLOTS)]
        for t in range(4):
            moved = []
            for j in range(SLOTS):
                shift = (j - t) % SLOTS * slot_lanes
                moved.append(pltpu.roll(parts[j], shift, 1) if shift else parts[j])
            start = t * width + tile * LANES
            combined_ref[:, start : start + LANES] = slot_select(moved)
    for h in range(heads):
        turned = parts_ref[2 * (h % SLOTS) + h // SLOTS, width : width + quarter, :].astype(jnp.float32).T
        out_weight_ref[h * slot_lanes : (h + 1) * slot_lanes, :] = jnp.concatenate(
            [turned[k * slot_lanes : (k + 1) * slot_lanes, :] for k in range(SLOTS)], axis=1
        )
    total = jnp.zeros(pair_weight_ref.shape, jnp.float32)
    for h in range(heads):
        total += parts_ref[h, width + quarter :, :].astype(jnp.float32)[:heads]
    pair_weight_ref[...] = total


def pair_kernel(blocks_row, blocks_ref, pair_ref, weight_ref, bias_ref, mean_ref, spread_ref, out_ref, share_ref):
    heads, channels = weight_ref.shape
    part = pair_ref.shape[0] // 2
    share_ref[...] = share_of(blocks_ref, blocks_row, part, heads)
    first, second = two_terms(weight_ref[...])
    zero = jnp.zeros((heads, channels), jnp.bfloat16)
    top = lax.broadcasted_iota(jnp.int32, (heads, channels), 0) < 2
    ones = jnp.where(top, 1.0, 0.0).astype(jnp.bfloat16)
    right = jnp.concatenate(
        [
            jnp.concatenate([first, first, second, ones, zero], axis=0),
            jnp.concatenate([zero, zero, zero, zero, ones], axis=0),
        ],
        axis=1,
    )
    row = lax.broadcasted_iota(jnp.int32, (heads, LANES), 0)

    def rows_of_two(value):
        high, low = two_terms(value)
        high, low = high.astype(jnp.float32), low.astype(jnp.float32)
        return jnp.where(row == 0, high, jnp.where(row == 1, low, 0.0)).astype(jnp.bfloat16)

    def rows(step, carry):
        for k in range(8):
            i = step * 8 + k
            gradient = share_ref[:, i, :]
            spread = spread_ref[pl.ds(i, 1), :]
            cross = jnp.sum(gradient * bias_ref[:, i, :], axis=0, keepdims=True) / channels
            slope = spread * spread * cross
            high, low = two_terms(gradient * spread)
            left = jnp.concatenate(
                [
                    high, low, high,
                    rows_of_two(jnp.broadcast_to(slope * mean_ref[pl.ds(i, 1), :], row.shape)),
                    rows_of_two(jnp.broadcast_to(slope, row.shape)),
                ],
                axis=0,
            )
            terms = f32_dot(left, right, TN)
            entries = pair_ref[i].astype(jnp.float32)
            out_ref[i] = (terms[:, :channels] - terms[:, channels:] * entries).astype(jnp.bfloat16)
        return carry

    lax.fori_loop(0, pair_ref.shape[0] // 8, rows, 0)


def call(kernel, outs, *args, scratch=(), place=None, flops=0, after=()):
    whole = pl.BlockSpec(memory_space=pltpu.VMEM)
    specs = [whole] * len(args)
    if place is not None:
        specs = [pl.BlockSpec(memory_space=pltpu.SMEM)] + specs
        args = (place,) + args
    shapes = [jax.ShapeDtypeStruct(*o) for o in outs]
    moved = sum(math.prod(a.shape) * a.dtype.itemsize for a in list(args) + shapes)
    first, last = len(args), len(args) + len(after)
    return pl.pallas_call(
        lambda *refs: kernel(*refs[:first], *refs[last:]),
        out_shape=shapes,
        in_specs=specs + [pl.BlockSpec(memory_space=pl.ANY)] * len(after),
        out_specs=[whole] * len(shapes),
        scratch_shapes=scratch,
        compiler_params=pltpu.CompilerParams(vmem_limit_bytes=VMEM_LIMIT),
        cost_estimate=pl.CostEstimate(flops=flops, bytes_accessed=moved, transcendentals=0),
    )(*args, *after)


def swapped(mine, axis_name, distance):
    size = lax.axis_size(axis_name)
    return lax.ppermute(mine, axis_name, [(a, a ^ distance) for a in range(size)])


def fits_heads(alignment_rows, pair_entries, pair_weight):
    channels, heads = pair_weight.shape
    return (
        lax.axis_size("seq") == 4
        and lax.axis_size("res") == heads == 8
        and alignment_rows.shape[0] == 2 * SLOTS
        and alignment_rows.shape[1] == pair_entries.shape[0] == 64
        and alignment_rows.shape[2] == 2 * LANES
        and pair_entries.shape[1] == channels == LANES
    )


def head_body(
    alignment_rows, pair_entries, combined_weight, output_weight, pair_weight, updated_gradient
):
    sequences, residues, width = alignment_rows.shape
    channels, heads = pair_weight.shape
    tokens = sequences * residues
    seq_size, res_size = lax.axis_size("seq"), lax.axis_size("res")
    seq_half = seq_size // 2
    total = residues * res_size
    group = 2 * res_size
    groups = [[g * group + k for k in range(group)] for g in range(seq_half)]
    scale = 1.0 / math.sqrt(width // heads * sequences * seq_size)
    res_index, seq_index = lax.axis_index("res"), lax.axis_index("seq")
    head = seq_index % 2 * (res_size // 2) + res_index // 2
    core, plane = res_index % 2, seq_index % 2
    place = jnp.stack([core, seq_index // 2, head % SLOTS, head]).astype(jnp.int32)
    bf16, f32 = jnp.bfloat16, jnp.float32

    def across(blocks):
        return lax.all_to_all(blocks, ("seq", "res"), 0, 0, axis_index_groups=groups, tiled=True)

    def doubled(mine, steps):
        arrays = {0: mine}
        for axis_name, distance, bit in steps:
            arrays |= {
                flip | bit: swapped(t, axis_name, distance) for flip, t in arrays.items()
            }
        return [arrays[flip] for flip in range(len(arrays))]

    def all_quarters(mine):
        far = swapped(mine, "seq", seq_half)
        return mine, far, swapped(mine, "res", 1), swapped(far, "res", 1)

    x, grad, wc, wo = alignment_rows, updated_gradient, combined_weight, output_weight
    half_tokens = ((2, sequences // 2, residues, width), bf16)
    value_blocks, normed, keep, send = call(
        value_kernel,
        [((group, 2 * residues, LANES), bf16), (x.shape, bf16), half_tokens, half_tokens],
        x, grad, wc, wo,
        place=place, flops=8 * tokens * width * width,
    )
    value_blocks = across(value_blocks)
    centred = (pair_weight - jnp.mean(pair_weight, axis=0, keepdims=True)).T
    query_blocks, bias, mean, spread = call(
        functools.partial(query_kernel, scale),
        [
            ((group, 3 * residues, LANES), bf16),
            ((heads, residues, LANES), f32),
            ((residues, LANES), f32),
            ((residues, LANES), f32),
        ],
        normed, wc, pair_entries, centred,
        flops=8 * tokens * width * width,
    )
    query_blocks = across(query_blocks)

    def scores(blocks, left_row, right_row, with_bias, kind, after=()):
        return call(
            functools.partial(score_kernel, residues, left_row, right_row, with_bias),
            [((total // 4, total), f32), ((total // 4, total), kind)],
            blocks, swapped(blocks, "res", 1),
            place=place, flops=2 * total * total * width, after=after,
        )

    grad_mine, grad_sent = scores(value_blocks, residues, 0, False, bf16, after=(mean,))
    grad_other = swapped(grad_sent, "seq", seq_half)
    normed_tokens, grad_tokens = call(
        merge_kernel, [half_tokens, half_tokens], keep, swapped(send, "res", 1),
        place=place, after=(mean,),
    )
    x_step, y_step, z_step = ("res", 2, 1), ("res", 4, 2), ("seq", 1, 4)
    normed_tokens = doubled(normed_tokens, (x_step, y_step, z_step))
    grad_tokens = doubled(grad_tokens, (y_step, z_step, x_step))

    logit_mine, logit_sent = scores(query_blocks, 0, residues, True, f32)
    logit_other = swapped(logit_sent, "seq", seq_half)
    quarter = ((total // 4, total), bf16)
    grad_logits, probs = call(
        softmax_kernel, [quarter, quarter], logit_mine, logit_other, grad_mine, grad_other,
        flops=total * total,
    )

    def products(quarters, blocks, first_row, second_row, with_share, factor):
        rows = 2 * residues + (residues // 2 if with_share else 0)
        (out,) = call(
            functools.partial(
                product_kernel, residues, factor, first_row, second_row, with_share
            ),
            [((group, rows, LANES), bf16)],
            *quarters, blocks,
            scratch=[pltpu.VMEM((total, total), bf16)],
            place=place, flops=4 * total * total * width,
        )
        return out

    grad_sums = products(all_quarters(grad_logits), query_blocks, residues, 0, True, scale)
    grad_blocks = across(grad_sums)
    attended = products(all_quarters(probs), value_blocks, 0, residues, False, 1.0)
    attended_blocks = across(attended)

    head_dim = width // heads
    gate_weight = jnp.tile(
        lax.dynamic_slice_in_dim(wc, 3 * width + head * head_dim, head_dim, 1), (1, SLOTS)
    )
    out_weight = jnp.tile(
        lax.dynamic_slice_in_dim(wo, head * head_dim, head_dim, 0), (SLOTS, 1)
    )
    rows = width + width // SLOTS
    (sums,) = call(
        head_weight_kernel, [((rows, LANES), f32)],
        *normed_tokens, *grad_tokens, gate_weight, out_weight, attended, grad_sums,
        place=place, flops=20 * 4 * tokens * width * LANES,
    )
    (sums,) = call(
        pair_weight_kernel, [((rows + heads, LANES), f32)],
        grad_blocks, pair_entries, mean, spread, sums,
        scratch=[pltpu.VMEM((heads, residues, LANES), f32)],
        flops=4 * tokens * width * width,
    )
    wire = ((rows + 2 * heads, LANES), bf16)
    (sums,) = call(add_kernel, [wire], sums, swapped(sums, "res", 1))
    (sums,) = call(add_kernel, [wire], sums, swapped(sums, "seq", seq_half))
    sums = jnp.where(plane == core, sums, swapped(sums, "seq", 1))
    parts = lax.all_gather(sums, "res", axis=0)
    combined_weight_gradient, output_weight_gradient, pair_weight_gradient = call(
        spread_kernel, [(wc.shape, f32), (wo.shape, f32), ((heads, channels), f32)], parts
    )

    updated, alignment_gradient = call(
        final_kernel, [(x.shape, bf16), (x.shape, bf16)],
        x, grad, wc, wo, attended_blocks, grad_blocks,
        flops=14 * tokens * width * width,
    )
    (pair_gradient,) = call(
        functools.partial(pair_kernel, 2 * residues),
        [(pair_entries.shape, bf16)],
        grad_blocks, pair_entries, centred, bias, mean, spread,
        scratch=[pltpu.VMEM((heads, residues, LANES), f32)],
        flops=8 * tokens * width * width,
    )
    return (
        updated,
        alignment_gradient,
        pair_gradient,
        combined_weight_gradient,
        output_weight_gradient,
        pair_weight_gradient.T,
    )


def body(alignment_rows, pair_entries, combined_weight, output_weight, pair_weight, updated_gradient):
    chosen = head_body if fits_heads(alignment_rows, pair_entries, pair_weight) else gathered_body
    return chosen(
        alignment_rows, pair_entries, combined_weight, output_weight, pair_weight, updated_gradient
    )


def solution(mesh):
    return jax.shard_map(
        body,
        mesh=mesh,
        in_specs=(
            P("seq", "res", None),
            P("res", "seq", None),
            P(),
            P(),
            P(),
            P("seq", "res", None),
        ),
        out_specs=(
            P("seq", "res", None),
            P("seq", "res", None),
            P("res", "seq", None),
            P(),
            P(),
            P(),
        ),
        check_vma=False,
    )
```

```python
import functools
import math

import jax
import jax.numpy as jnp
from jax import lax
from jax.experimental import pallas as pl
from jax.experimental.pallas import tpu as pltpu
from jax.sharding import PartitionSpec as P

eps_norm = 1e-05


def layer_normalize(values):
    values = values.astype(jnp.float32)
    center = values - jnp.mean(values, axis=-1, keepdims=True)
    broadcast_pair = lax.rsqrt(jnp.mean(center * center, axis=-1, keepdims=True) + eps_norm)
    return (center * broadcast_pair, broadcast_pair)


def layer_norm_backward(normalized_gradient, normalized_rows, broadcast_pair):
    mean_grad = jnp.mean(normalized_gradient, axis=-1, keepdims=True)
    mean_cross = jnp.mean(normalized_gradient * normalized_rows, axis=-1, keepdims=True)
    return broadcast_pair * (normalized_gradient - mean_grad - normalized_rows * mean_cross)


def split_heads(tensor, head_count):
    return tensor.reshape(
        tensor.shape[0], tensor.shape[1], head_count, tensor.shape[2] // head_count
    )


def merge_heads(tensor):
    return tensor.reshape(tensor.shape[0], tensor.shape[1], tensor.shape[2] * tensor.shape[3])


def gathered_body(
    alignment_rows, pair_entries, combined_weight, output_weight, pair_weight, updated_gradient
):
    sequence_count, residue_count, alignment_width = alignment_rows.shape
    head_count = pair_weight.shape[1]
    query_width = output_weight.shape[0]
    head_dim = query_width // head_count
    column_count = pair_entries.shape[1]
    token_count = sequence_count * residue_count
    score_scale = 1.0 / math.sqrt(head_dim * sequence_count * lax.axis_size("seq"))
    normalized_rows, broadcast_pair = layer_normalize(alignment_rows)
    normalized_rows_backward = normalized_rows.astype(jnp.bfloat16).reshape(
        token_count, alignment_width
    )
    projected = jnp.dot(
        normalized_rows_backward, combined_weight, preferred_element_type=jnp.float32
    ).reshape(sequence_count, residue_count, 4 * query_width)
    queries = (projected[..., :query_width] * score_scale).astype(jnp.bfloat16)
    key_rows = projected[..., query_width : 2 * query_width].astype(jnp.bfloat16)
    value_rows = projected[..., 2 * query_width : 3 * query_width].astype(jnp.bfloat16)
    gate_open = jax.nn.sigmoid(projected[..., 3 * query_width :])
    all_keys, all_values = (
        lax.all_gather(key_rows, "res", axis=1, tiled=True),
        lax.all_gather(value_rows, "res", axis=1, tiled=True),
    )
    query_heads = split_heads(queries, head_count)
    key_heads = split_heads(all_keys, head_count)
    value_heads = split_heads(all_values, head_count)
    score_terms = jnp.einsum(
        "sihd,sjhd->hij", query_heads, key_heads, preferred_element_type=jnp.float32
    )
    pair_normed, pair_spread = layer_normalize(pair_entries)
    pair_bias = jnp.einsum("ijc,ch->hij", pair_normed, pair_weight, precision=lax.Precision.HIGHEST)
    col_start = lax.axis_index("seq") * column_count
    own_block = lax.dynamic_slice_in_dim(score_terms, col_start, column_count, 2) + pair_bias
    logits = lax.psum(lax.dynamic_update_slice_in_dim(score_terms, own_block, col_start, 2), "seq")
    row_top = jnp.max(logits, axis=-1, keepdims=True)
    lifted = jnp.exp(logits - row_top)
    softmax_out = lifted / jnp.sum(lifted, axis=-1, keepdims=True)
    softmax_low = softmax_out.astype(jnp.bfloat16)
    attended = merge_heads(
        jnp.einsum("hij,sjhd->sihd", softmax_low, value_heads, preferred_element_type=jnp.float32)
    )
    gated_out = (gate_open * attended).astype(jnp.bfloat16)
    flattened_gated = gated_out.reshape(token_count, query_width)
    updated = (
        jnp.dot(flattened_gated, output_weight, preferred_element_type=jnp.float32)
        .astype(jnp.bfloat16)
        .reshape(sequence_count, residue_count, alignment_width)
    )
    flattened_gradient = updated_gradient.reshape(token_count, alignment_width)
    grad_gated = jnp.dot(
        flattened_gradient, output_weight.T, preferred_element_type=jnp.float32
    ).reshape(sequence_count, residue_count, query_width)
    out_local = jnp.dot(flattened_gated.T, flattened_gradient, preferred_element_type=jnp.float32)
    grad_attended = (grad_gated * gate_open).astype(jnp.bfloat16)
    grad_gate_logit = grad_gated * attended * gate_open * (1.0 - gate_open)
    attended_grad_heads = split_heads(grad_attended, head_count)
    grad_terms = jnp.einsum(
        "sihd,sjhd->hij", attended_grad_heads, value_heads, preferred_element_type=jnp.float32
    )
    grad_probs = lax.psum(grad_terms, "seq")
    row_dot = jnp.sum(softmax_out * grad_probs, axis=-1, keepdims=True)
    grad_logits = softmax_out * (grad_probs - row_dot)
    grad_logits_b = grad_logits.astype(jnp.bfloat16)
    logit_share = lax.dynamic_slice_in_dim(grad_logits, col_start, column_count, 2)
    grad_query_heads = (
        jnp.einsum("hij,sjhd->sihd", grad_logits_b, key_heads, preferred_element_type=jnp.float32)
        * score_scale
    )
    key_part = jnp.einsum(
        "hij,sihd->jshd", grad_logits_b, query_heads, preferred_element_type=jnp.float32
    )
    value_part = jnp.einsum(
        "hij,sihd->jshd", softmax_low, attended_grad_heads, preferred_element_type=jnp.float32
    )
    summed = lax.psum_scatter(
        jnp.concatenate([merge_heads(key_part), merge_heads(value_part)], axis=-1),
        "res",
        scatter_dimension=0,
        tiled=True,
    )
    key_value_grads = jnp.transpose(summed, (1, 0, 2))
    projected_gradient = jnp.concatenate(
        [merge_heads(grad_query_heads), key_value_grads, grad_gate_logit], axis=-1
    )
    projected_gradient = projected_gradient.astype(jnp.bfloat16).reshape(
        token_count, 4 * query_width
    )
    qkvg_local = jnp.dot(
        normalized_rows_backward.T, projected_gradient, preferred_element_type=jnp.float32
    )
    normalized_gradient = jnp.dot(
        projected_gradient, combined_weight.T, preferred_element_type=jnp.float32
    ).reshape(sequence_count, residue_count, alignment_width)
    alignment_gradient = layer_norm_backward(
        normalized_gradient, normalized_rows, broadcast_pair
    ).astype(jnp.bfloat16)
    pair_w_local = jnp.einsum(
        "ijc,hij->ch", pair_normed, logit_share, precision=lax.Precision.HIGHEST
    )
    grad_pair_normed = jnp.einsum(
        "hij,ch->ijc", logit_share, pair_weight, precision=lax.Precision.HIGHEST
    )
    pair_gradient = layer_norm_backward(grad_pair_normed, pair_normed, pair_spread).astype(
        jnp.bfloat16
    )
    combined_weight_gradient, output_weight_gradient, pair_weight_gradient = lax.psum(
        (qkvg_local, out_local, pair_w_local), ("seq", "res")
    )
    return (
        updated,
        alignment_gradient,
        pair_gradient,
        combined_weight_gradient,
        output_weight_gradient,
        pair_weight_gradient,
    )


VMEM_LIMIT = 20 * 1024 * 1024
LANES = 128
SLOTS = 4
NT = (((1,), (1,)), ((), ()))
TN = (((0,), (0,)), ((), ()))


def f32_dot(left, right, dims=None):
    if dims is None:
        return jnp.dot(left, right, preferred_element_type=jnp.float32)
    return lax.dot_general(left, right, dims, preferred_element_type=jnp.float32)


def two_terms(values):
    high = values.astype(jnp.bfloat16)
    return high, (values - high.astype(jnp.float32)).astype(jnp.bfloat16)


def slot_select(pieces):
    slot = lax.broadcasted_iota(jnp.int32, pieces[0].shape, 1) // (LANES // SLOTS)
    result = pieces[0]
    for k in range(1, SLOTS):
        result = jnp.where(slot == k, pieces[k], result)
    return result


def pack_heads(out_ref, row, tensor, residues):
    for core in range(2):
        for tile in range(tensor.shape[1] // LANES):
            rolled = []
            for s in range(SLOTS):
                start = (core * SLOTS + s) * residues
                piece = tensor[start : start + residues, tile * LANES : (tile + 1) * LANES]
                rolled.append(pltpu.roll(piece, s * LANES // SLOTS, 1) if s else piece)
            for j in range(SLOTS):
                block = slot_select([rolled[(k - j) % SLOTS] for k in range(SLOTS)])
                out_ref[(tile * SLOTS + j) * 2 + core, row : row + residues, :] = block.astype(
                    jnp.bfloat16
                )


def unpack_heads(in_ref, row, residues, tiles):
    rows = []
    for core in range(2):
        for s in range(SLOTS):
            pieces = []
            for tile in range(tiles):
                blocks = [
                    in_ref[
                        (tile * SLOTS + (k - s) % SLOTS) * 2 + core, row : row + residues, :
                    ].astype(jnp.float32)
                    for k in range(SLOTS)
                ]
                block = slot_select(blocks)
                pieces.append(pltpu.roll(block, LANES - s * LANES // SLOTS, 1) if s else block)
            rows.append(jnp.concatenate(pieces, axis=1))
    return jnp.concatenate(rows, axis=0)


def normalized(x_ref):
    width = x_ref.shape[-1]
    values = x_ref[...].reshape(-1, width).astype(jnp.float32)
    return layer_normalize(values)


def gate_of(logits):
    return 1.0 / (1.0 + jnp.exp(-logits))


def value_kernel(
    place_ref, x_ref, grad_ref, wc_ref, wo_ref, out_ref, keep_ref, send_ref, normed_ref
):
    residues, width = x_ref.shape[1], x_ref.shape[2]
    core = place_ref[0]
    normed = normalized(x_ref)[0].astype(jnp.bfloat16)
    normed_ref[...] = normed.reshape(normed_ref.shape)
    values = f32_dot(normed, wc_ref[:, 2 * width : 3 * width])
    gate = gate_of(f32_dot(normed, wc_ref[:, 3 * width :]))
    grad_gated = f32_dot(grad_ref[...].reshape(-1, width), wo_ref[...], NT)
    pack_heads(out_ref, 0, values, residues)
    pack_heads(out_ref, residues, grad_gated * gate, residues)
    for which, ref in ((core, keep_ref), (1 - core, send_ref)):
        for s in range(SLOTS):
            ref[0, s] = normed_ref[which * SLOTS + s]
            ref[1, s] = grad_ref[which * SLOTS + s]


def merge_kernel(place_ref, keep_ref, other_ref, normed_ref, grad_ref):
    core = place_ref[0]
    for t, ref in ((0, normed_ref), (1, grad_ref)):
        ref[core] = keep_ref[t]
        ref[1 - core] = other_ref[t]


def centred(weight):
    return weight - jnp.mean(weight, axis=1, keepdims=True)


def query_kernel(scale, x_ref, wc_ref, pair_ref, weight_ref, out_ref, bias_ref, mean_ref, spread_ref):
    residues, width = x_ref.shape[1], x_ref.shape[2]
    heads = weight_ref.shape[0]
    normed = normalized(x_ref)[0].astype(jnp.bfloat16)
    pack_heads(out_ref, 0, f32_dot(normed, wc_ref[:, :width]) * scale, residues)
    pack_heads(out_ref, residues, f32_dot(normed, wc_ref[:, width : 2 * width]), residues)

    columns, channels = pair_ref.shape[1], pair_ref.shape[2]
    weight = centred(weight_ref[...])
    first = weight.astype(jnp.bfloat16)
    second, third = two_terms(weight - first.astype(jnp.float32))
    share = jnp.full((heads, channels), 1.0 / channels, jnp.bfloat16)
    left = jnp.concatenate([first, second, third, share], axis=0)
    average = jnp.full((channels, channels), 1.0 / channels, jnp.bfloat16)
    step_rows = 8

    def rows(step, carry):
        start = pl.multiple_of(step * step_rows, step_rows)
        entries = pair_ref[pl.ds(start, step_rows)].reshape(step_rows * columns, channels)
        center = entries.astype(jnp.float32) - f32_dot(entries, average)
        high, low = two_terms(center * center)
        variance = f32_dot(share, high, NT) + f32_dot(share, low, NT)
        spread = lax.rsqrt(variance + eps_norm)
        raw = f32_dot(left, entries, NT)
        bias = spread * (raw[:heads] + raw[heads : 2 * heads] + raw[2 * heads : 3 * heads])
        for k in range(step_rows):
            lanes = slice(k * columns, (k + 1) * columns)
            bias_ref[:, start + k, :] = bias[:, lanes]
            mean_ref[pl.ds(start + k, 1), :] = raw[3 * heads : 3 * heads + 1, lanes]
            spread_ref[pl.ds(start + k, 1), :] = spread[:1, lanes]
        return carry

    lax.fori_loop(0, pair_ref.shape[0] // step_rows, rows, 0)
    half = residues // 2
    for h in range(heads):
        for core in range(2):
            high, low = two_terms(bias_ref[h, core * half : (core + 1) * half, :])
            out_ref[h * 2 + core, 2 * residues : 2 * residues + half, :] = high
            out_ref[h * 2 + core, 2 * residues + half : 3 * residues, :] = low


def lanes_of(blocks_ref, row, residues):
    count = blocks_ref.shape[0] // 2
    planes = [
        blocks_ref[p * count : (p + 1) * count, row : row + residues, :].reshape(-1, LANES)
        for p in range(2)
    ]
    return jnp.concatenate(planes, axis=1)


def score_kernel(
    residues, left_row, right_row, with_bias, place_ref, own_ref, other_ref, mine_ref, sent_ref
):
    core, half = place_ref[0], place_ref[1]
    count = own_ref.shape[0] // 2
    part = residues // 2
    right = jnp.concatenate(
        [lanes_of(own_ref, right_row, residues), lanes_of(other_ref, right_row, residues)], axis=1
    )
    for which, ref in ((half, mine_ref), (1 - half, sent_ref)):
        left = []
        for k in range(count // 2):
            block = which * (count // 2) + k
            rows = pl.ds(pl.multiple_of(left_row + core * part, part), part)
            left.append(
                jnp.concatenate(
                    [
                        r[p * count + block, rows, :]
                        for r in (own_ref, other_ref)
                        for p in range(2)
                    ],
                    axis=1,
                )
            )
        ref[...] = f32_dot(jnp.concatenate(left, axis=0), right, NT).astype(ref.dtype)
        if with_bias:
            for p in range(2):
                columns = pl.ds(pl.multiple_of((half * 2 + p) * LANES, LANES), LANES)
                for k in range(count // 2):
                    block = p * count + which * (count // 2) + k
                    high = own_ref[block, 2 * residues : 2 * residues + part, :]
                    low = own_ref[block, 2 * residues + part : 3 * residues, :]
                    bias = high.astype(jnp.float32) + low.astype(jnp.float32)
                    ref[k * part : (k + 1) * part, columns] += bias


def softmax_kernel(logit_ref, logit_other_ref, grad_ref, grad_other_ref, out_ref, prob_ref):
    logits = logit_ref[...] + logit_other_ref[...]
    lifted = jnp.exp(logits - jnp.max(logits, axis=-1, keepdims=True))
    softmax_out = lifted / jnp.sum(lifted, axis=-1, keepdims=True)
    prob_ref[...] = softmax_out.astype(jnp.bfloat16)
    grad_probs = grad_ref[...] + grad_other_ref[...].astype(jnp.float32)
    row_dot = jnp.sum(softmax_out * grad_probs, axis=-1, keepdims=True)
    out_ref[...] = (softmax_out * (grad_probs - row_dot)).astype(jnp.bfloat16)


def product_kernel(
    residues, scale, first_row, second_row, with_share,
    place_ref, own_ref, far_ref, near_ref, corner_ref, blocks_ref, out_ref, whole_ref,
):
    core, half = place_ref[0], place_ref[1]
    count = blocks_ref.shape[0] // 2
    part = residues // 2
    quarters = (
        (own_ref, core, half), (far_ref, core, 1 - half),
        (near_ref, 1 - core, half), (corner_ref, 1 - core, 1 - half),
    )
    for ref, c, z in quarters:
        for k in range(count // 2):
            start = (z * (count // 2) + k) * residues + c * part
            whole_ref[pl.ds(pl.multiple_of(start, part), part), :] = ref[k * part : (k + 1) * part, :]
    whole = whole_ref[...]
    if with_share:
        for p in range(2):
            columns = pl.ds(pl.multiple_of((half * 2 + p) * LANES, LANES), LANES)
            for q in range(count):
                rows = pl.ds(pl.multiple_of(q * residues + core * part, part), part)
                out_ref[p * count + q, 2 * residues : 2 * residues + part, :] = whole_ref[rows, columns]
    first = f32_dot(whole, lanes_of(blocks_ref, first_row, residues)) * scale
    second = f32_dot(whole, lanes_of(blocks_ref, second_row, residues), TN)
    for row, product in ((0, first), (residues, second)):
        for p in range(2):
            out_ref[p * count : (p + 1) * count, row : row + residues, :] = (
                product[:, p * LANES : (p + 1) * LANES]
                .astype(jnp.bfloat16)
                .reshape(count, residues, LANES)
            )


def share_of(blocks_ref, row, part, heads):
    return jnp.concatenate(
        [
            blocks_ref[:, row : row + part, :]
            .astype(jnp.float32)
            .reshape(heads, 2 * part, LANES)
        ],
        axis=0,
    )


def final_kernel(x_ref, grad_ref, wc_ref, wo_ref, attended_ref, blocks_ref, updated_ref, out_ref):
    residues, width = x_ref.shape[1], x_ref.shape[2]
    tiles = width // LANES
    normed, spread = normalized(x_ref)
    gate = gate_of(f32_dot(normed.astype(jnp.bfloat16), wc_ref[:, 3 * width :]))
    grad_gated = f32_dot(grad_ref[...].reshape(-1, width), wo_ref[...], NT)
    attended = unpack_heads(attended_ref, 0, residues, tiles)
    gated = (gate * attended).astype(jnp.bfloat16)
    updated_ref[...] = f32_dot(gated, wo_ref[...]).astype(jnp.bfloat16).reshape(updated_ref.shape)
    parts = [
        unpack_heads(blocks_ref, 0, residues, tiles),
        unpack_heads(blocks_ref, residues, residues, tiles),
        unpack_heads(attended_ref, residues, residues, tiles),
        grad_gated * attended * gate * (1.0 - gate),
    ]
    gradient = f32_dot(
        jnp.concatenate([p.astype(jnp.bfloat16) for p in parts], axis=1), wc_ref[...], NT
    )
    out_ref[...] = (
        layer_norm_backward(gradient, normed, spread).astype(jnp.bfloat16).reshape(out_ref.shape)
    )


def head_weight_kernel(place_ref, *refs):
    turn, chip = place_ref[2], place_ref[3]
    flips = (len(refs) - 5) // 2
    normed_refs, grad_refs = refs[:flips], refs[flips : 2 * flips]
    gate_weight_ref, out_weight_ref, attended_ref, blocks_ref, sum_ref = refs[2 * flips :]
    residues, width = normed_refs[0].shape[2], normed_refs[0].shape[3]
    slot = lax.broadcasted_iota(jnp.int32, (2 * flips * residues, LANES), 1) // (LANES // SLOTS)

    def tokens_of(arrays, s):
        return jnp.concatenate([r[c, s] for r in arrays for c in range(2)], axis=0)

    def tile_of(ref, row):
        rows = []
        for flip in range(flips):
            block = jnp.bitwise_xor(chip, flip) * 2
            rows += [ref[block + c, row : row + residues, :] for c in range(2)]
        return jnp.concatenate(rows, axis=0)

    attended = tile_of(attended_ref, 0).astype(jnp.float32)
    sums = [jnp.zeros((width, LANES), jnp.float32)] * 5
    for s in range(SLOTS):
        chosen = slot == lax.rem(turn + s, SLOTS)
        normed, grad = tokens_of(normed_refs, s), tokens_of(grad_refs, s)
        gate = gate_of(f32_dot(normed, gate_weight_ref[...]))
        grad_gated = f32_dot(grad, out_weight_ref[...], NT)
        gated = (gate * attended).astype(jnp.bfloat16)
        gate_logit = (grad_gated * attended * gate * (1.0 - gate)).astype(jnp.bfloat16)
        pieces = [
            tile_of(blocks_ref, 0),
            tile_of(blocks_ref, residues),
            tile_of(attended_ref, residues),
            gate_logit,
            gated,
        ]
        zero = jnp.zeros_like(gated)
        pieces = [jnp.where(chosen, p, zero) for p in pieces]
        products = f32_dot(normed, jnp.concatenate(pieces[:4], axis=1), TN)
        for t in range(4):
            sums[t] += products[:, t * LANES : (t + 1) * LANES]
        sums[4] += f32_dot(grad, pieces[4], TN)
    totals = []
    for part in sums:
        part = part + pltpu.roll(part, LANES // 2, 1)
        totals.append(part + pltpu.roll(part, LANES // 4, 1))
    sum_ref[:width, :] = slot_select(totals[:4])
    quarter = width // SLOTS
    sum_ref[width:, :] = slot_select(
        [totals[4][k * quarter : (k + 1) * quarter] for k in range(SLOTS)]
    )


def pair_weight_kernel(blocks_ref, pair_ref, mean_ref, spread_ref, sums_ref, out_ref, share_ref):
    heads, part = share_ref.shape[0], pair_ref.shape[0] // 2
    share_ref[...] = share_of(blocks_ref, blocks_ref.shape[1] - part, part, heads)

    def rows(step, carry):
        total, shift = carry
        for k in range(8):
            i = step * 8 + k
            scaled = share_ref[:, i, :] * spread_ref[pl.ds(i, 1), :]
            high, low = two_terms(scaled)
            total += f32_dot(jnp.concatenate([high, low], axis=0), pair_ref[i])
            shift += (high.astype(jnp.float32) + low.astype(jnp.float32)) * mean_ref[pl.ds(i, 1), :]
        return total, shift

    channels = pair_ref.shape[2]
    total, shift = lax.fori_loop(
        0,
        pair_ref.shape[0] // 8,
        rows,
        (jnp.zeros((2 * heads, channels), jnp.float32), jnp.zeros((heads, LANES), jnp.float32)),
    )
    count = sums_ref.shape[0]
    out_ref[:count, :] = sums_ref[...]
    out_ref[count:, :] = total[:heads] + total[heads:] - jnp.sum(shift, axis=1, keepdims=True)


def add_kernel(mine_ref, other_ref, out_ref):
    count = mine_ref.shape[0]
    out_ref[:count, :] = (
        mine_ref[...].astype(jnp.float32) + other_ref[:count, :].astype(jnp.float32)
    ).astype(out_ref.dtype)
    if out_ref.shape[0] > count:
        out_ref[count:, :] = jnp.zeros((out_ref.shape[0] - count, LANES), out_ref.dtype)


def spread_kernel(parts_ref, combined_ref, out_weight_ref, pair_weight_ref):
    heads, width = parts_ref.shape[0], combined_ref.shape[0]
    slot_lanes = LANES // SLOTS
    quarter = width // SLOTS
    for tile in range(heads // SLOTS):
        parts = [parts_ref[2 * j + tile, :width, :].astype(jnp.float32) for j in range(SLOTS)]
        for t in range(4):
            moved = []
            for j in range(SLOTS):
                shift = (j - t) % SLOTS * slot_lanes
                moved.append(pltpu.roll(parts[j], shift, 1) if shift else parts[j])
            start = t * width + tile * LANES
            combined_ref[:, start : start + LANES] = slot_select(moved)
    for h in range(heads):
        turned = parts_ref[2 * (h % SLOTS) + h // SLOTS, width : width + quarter, :].astype(jnp.float32).T
        out_weight_ref[h * slot_lanes : (h + 1) * slot_lanes, :] = jnp.concatenate(
            [turned[k * slot_lanes : (k + 1) * slot_lanes, :] for k in range(SLOTS)], axis=1
        )
    total = jnp.zeros(pair_weight_ref.shape, jnp.float32)
    for h in range(heads):
        total += parts_ref[h, width + quarter :, :].astype(jnp.float32)[:heads]
    pair_weight_ref[...] = total


def pair_kernel(blocks_row, blocks_ref, pair_ref, weight_ref, bias_ref, mean_ref, spread_ref, out_ref, share_ref):
    heads, channels = weight_ref.shape
    part = pair_ref.shape[0] // 2
    share_ref[...] = share_of(blocks_ref, blocks_row, part, heads)
    first, second = two_terms(centred(weight_ref[...]))
    zero = jnp.zeros((heads, channels), jnp.bfloat16)
    top = lax.broadcasted_iota(jnp.int32, (heads, channels), 0) < 2
    ones = jnp.where(top, 1.0, 0.0).astype(jnp.bfloat16)
    right = jnp.concatenate(
        [
            jnp.concatenate([first, first, second, ones, zero], axis=0),
            jnp.concatenate([zero, zero, zero, zero, ones], axis=0),
        ],
        axis=1,
    )
    row = lax.broadcasted_iota(jnp.int32, (heads, LANES), 0)

    def rows_of_two(value):
        high, low = two_terms(value)
        high, low = high.astype(jnp.float32), low.astype(jnp.float32)
        return jnp.where(row == 0, high, jnp.where(row == 1, low, 0.0)).astype(jnp.bfloat16)

    def rows(step, carry):
        for k in range(8):
            i = step * 8 + k
            gradient = share_ref[:, i, :]
            spread = spread_ref[pl.ds(i, 1), :]
            cross = jnp.sum(gradient * bias_ref[:, i, :], axis=0, keepdims=True) / channels
            slope = spread * spread * cross
            high, low = two_terms(gradient * spread)
            left = jnp.concatenate(
                [
                    high, low, high,
                    rows_of_two(jnp.broadcast_to(slope * mean_ref[pl.ds(i, 1), :], row.shape)),
                    rows_of_two(jnp.broadcast_to(slope, row.shape)),
                ],
                axis=0,
            )
            terms = f32_dot(left, right, TN)
            entries = pair_ref[i].astype(jnp.float32)
            out_ref[i] = (terms[:, :channels] - terms[:, channels:] * entries).astype(jnp.bfloat16)
        return carry

    lax.fori_loop(0, pair_ref.shape[0] // 8, rows, 0)


def call(kernel, outs, *args, scratch=(), place=None, flops=0, after=()):
    whole = pl.BlockSpec(memory_space=pltpu.VMEM)
    specs = [whole] * len(args)
    if place is not None:
        specs = [pl.BlockSpec(memory_space=pltpu.SMEM)] + specs
        args = (place,) + args
    shapes = [jax.ShapeDtypeStruct(*o) for o in outs]
    moved = sum(math.prod(a.shape) * a.dtype.itemsize for a in list(args) + shapes)
    first, last = len(args), len(args) + len(after)
    return pl.pallas_call(
        lambda *refs: kernel(*refs[:first], *refs[last:]),
        out_shape=shapes,
        in_specs=specs + [pl.BlockSpec(memory_space=pl.ANY)] * len(after),
        out_specs=[whole] * len(shapes),
        scratch_shapes=scratch,
        compiler_params=pltpu.CompilerParams(vmem_limit_bytes=VMEM_LIMIT),
        cost_estimate=pl.CostEstimate(flops=flops, bytes_accessed=moved, transcendentals=0),
    )(*args, *after)


def swapped(mine, axis_name, distance):
    size = lax.axis_size(axis_name)
    return lax.ppermute(mine, axis_name, [(a, a ^ distance) for a in range(size)])


def fits_heads(alignment_rows, pair_entries, pair_weight):
    channels, heads = pair_weight.shape
    return (
        lax.axis_size("seq") == 4
        and lax.axis_size("res") == heads == 8
        and alignment_rows.shape[0] == 2 * SLOTS
        and alignment_rows.shape[1] == pair_entries.shape[0] == 64
        and alignment_rows.shape[2] == 2 * LANES
        and pair_entries.shape[1] == channels == LANES
    )


def head_body(
    alignment_rows, pair_entries, combined_weight, output_weight, pair_weight, updated_gradient
):
    sequences, residues, width = alignment_rows.shape
    channels, heads = pair_weight.shape
    tokens = sequences * residues
    seq_size, res_size = lax.axis_size("seq"), lax.axis_size("res")
    seq_half = seq_size // 2
    total = residues * res_size
    group = 2 * res_size
    groups = [[g * group + k for k in range(group)] for g in range(seq_half)]
    scale = 1.0 / math.sqrt(width // heads * sequences * seq_size)
    res_index, seq_index = lax.axis_index("res"), lax.axis_index("seq")
    head = seq_index % 2 * (res_size // 2) + res_index // 2
    core, plane = res_index % 2, seq_index % 2
    place = jnp.stack([core, seq_index // 2, head % SLOTS, head]).astype(jnp.int32)
    bf16, f32 = jnp.bfloat16, jnp.float32

    def across(blocks):
        return lax.all_to_all(blocks, ("seq", "res"), 0, 0, axis_index_groups=groups, tiled=True)

    def doubled(mine, steps):
        arrays = {0: mine}
        for axis_name, distance, bit in steps:
            arrays |= {
                flip | bit: swapped(t, axis_name, distance) for flip, t in arrays.items()
            }
        return [arrays[flip] for flip in range(len(arrays))]

    def all_quarters(mine):
        far = swapped(mine, "seq", seq_half)
        return mine, far, swapped(mine, "res", 1), swapped(far, "res", 1)

    x, grad, wc, wo = alignment_rows, updated_gradient, combined_weight, output_weight
    half_tokens = ((2, sequences // 2, residues, width), bf16)
    value_blocks, keep, send = call(
        value_kernel,
        [((group, 2 * residues, LANES), bf16), half_tokens, half_tokens],
        x, grad, wc, wo,
        scratch=[pltpu.VMEM(x.shape, bf16)],
        place=place, flops=8 * tokens * width * width,
    )
    value_blocks = across(value_blocks)
    query_blocks, bias, mean, spread = call(
        functools.partial(query_kernel, scale),
        [
            ((group, 3 * residues, LANES), bf16),
            ((heads, residues, LANES), f32),
            ((residues, LANES), f32),
            ((residues, LANES), f32),
        ],
        x, wc, pair_entries, pair_weight.T,
        flops=8 * tokens * width * width,
    )
    query_blocks = across(query_blocks)

    def scores(blocks, left_row, right_row, with_bias, kind, after=()):
        return call(
            functools.partial(score_kernel, residues, left_row, right_row, with_bias),
            [((total // 4, total), f32), ((total // 4, total), kind)],
            blocks, swapped(blocks, "res", 1),
            place=place, flops=2 * total * total * width, after=after,
        )

    grad_mine, grad_sent = scores(value_blocks, residues, 0, False, bf16, after=(mean,))
    grad_other = swapped(grad_sent, "seq", seq_half)
    normed_tokens, grad_tokens = call(
        merge_kernel, [half_tokens, half_tokens], keep, swapped(send, "res", 1),
        place=place,
    )
    x_step, y_step, z_step = ("res", 2, 1), ("res", 4, 2), ("seq", 1, 4)
    normed_tokens = doubled(normed_tokens, (x_step, y_step, z_step))
    grad_tokens = doubled(grad_tokens, (y_step, z_step, x_step))

    logit_mine, logit_sent = scores(
        query_blocks, 0, residues, True, f32, after=(normed_tokens[1], grad_tokens[2])
    )
    logit_other = swapped(logit_sent, "seq", seq_half)
    quarter = ((total // 4, total), bf16)
    grad_logits, probs = call(
        softmax_kernel, [quarter, quarter], logit_mine, logit_other, grad_mine, grad_other,
        flops=total * total,
        after=(normed_tokens[2], normed_tokens[3], grad_tokens[4], grad_tokens[6]),
    )

    def products(quarters, blocks, first_row, second_row, with_share, factor, after=()):
        rows = 2 * residues + (residues // 2 if with_share else 0)
        (out,) = call(
            functools.partial(
                product_kernel, residues, factor, first_row, second_row, with_share
            ),
            [((group, rows, LANES), bf16)],
            *quarters, blocks,
            scratch=[pltpu.VMEM((total, total), bf16)],
            place=place, flops=4 * total * total * width, after=after,
        )
        return out

    grad_sums = products(all_quarters(grad_logits), query_blocks, residues, 0, True, scale)
    grad_blocks = across(grad_sums)
    attended = products(
        all_quarters(probs), value_blocks, 0, residues, False, 1.0,
        after=(*normed_tokens[4:], *grad_tokens[1::2]),
    )
    attended_blocks = across(attended)

    head_dim = width // heads
    gate_weight = jnp.tile(
        lax.dynamic_slice_in_dim(wc, 3 * width + head * head_dim, head_dim, 1), (1, SLOTS)
    )
    out_weight = jnp.tile(
        lax.dynamic_slice_in_dim(wo, head * head_dim, head_dim, 0), (SLOTS, 1)
    )
    rows = width + width // SLOTS
    (sums,) = call(
        head_weight_kernel, [((rows, LANES), f32)],
        *normed_tokens, *grad_tokens, gate_weight, out_weight, attended, grad_sums,
        place=place, flops=20 * 4 * tokens * width * LANES,
    )
    (sums,) = call(
        pair_weight_kernel, [((rows + heads, LANES), f32)],
        grad_blocks, pair_entries, mean, spread, sums,
        scratch=[pltpu.VMEM((heads, residues, LANES), f32)],
        flops=4 * tokens * width * width,
    )
    wire = ((rows + 2 * heads, LANES), bf16)
    (sums,) = call(add_kernel, [wire], sums, swapped(sums, "res", 1))
    (sums,) = call(add_kernel, [wire], sums, swapped(sums, "seq", seq_half))
    sums = jnp.where(plane == core, sums, swapped(sums, "seq", 1))
    parts = lax.all_gather(sums, "res", axis=0)
    combined_weight_gradient, output_weight_gradient, pair_weight_gradient = call(
        spread_kernel, [(wc.shape, f32), (wo.shape, f32), ((heads, channels), f32)], parts
    )

    updated, alignment_gradient = call(
        final_kernel, [(x.shape, bf16), (x.shape, bf16)],
        x, grad, wc, wo, attended_blocks, grad_blocks,
        flops=14 * tokens * width * width,
    )
    (pair_gradient,) = call(
        functools.partial(pair_kernel, 2 * residues),
        [(pair_entries.shape, bf16)],
        grad_blocks, pair_entries, pair_weight.T, bias, mean, spread,
        scratch=[pltpu.VMEM((heads, residues, LANES), f32)],
        flops=8 * tokens * width * width,
    )
    return (
        updated,
        alignment_gradient,
        pair_gradient,
        combined_weight_gradient,
        output_weight_gradient,
        pair_weight_gradient.T,
    )


def body(alignment_rows, pair_entries, combined_weight, output_weight, pair_weight, updated_gradient):
    chosen = head_body if fits_heads(alignment_rows, pair_entries, pair_weight) else gathered_body
    return chosen(
        alignment_rows, pair_entries, combined_weight, output_weight, pair_weight, updated_gradient
    )


def solution(mesh):
    return jax.shard_map(
        body,
        mesh=mesh,
        in_specs=(
            P("seq", "res", None),
            P("res", "seq", None),
            P(),
            P(),
            P(),
            P("seq", "res", None),
        ),
        out_specs=(
            P("seq", "res", None),
            P("seq", "res", None),
            P("res", "seq", None),
            P(),
            P(),
            P(),
        ),
        check_vma=False,
    )
```

```python
import functools
import math

import jax
import jax.numpy as jnp
from jax import lax
from jax.experimental import pallas as pl
from jax.experimental.pallas import tpu as pltpu
from jax.sharding import PartitionSpec as P

eps_norm = 1e-05


def layer_normalize(values):
    values = values.astype(jnp.float32)
    center = values - jnp.mean(values, axis=-1, keepdims=True)
    broadcast_pair = lax.rsqrt(jnp.mean(center * center, axis=-1, keepdims=True) + eps_norm)
    return (center * broadcast_pair, broadcast_pair)


def layer_norm_backward(normalized_gradient, normalized_rows, broadcast_pair):
    mean_grad = jnp.mean(normalized_gradient, axis=-1, keepdims=True)
    mean_cross = jnp.mean(normalized_gradient * normalized_rows, axis=-1, keepdims=True)
    return broadcast_pair * (normalized_gradient - mean_grad - normalized_rows * mean_cross)


def split_heads(tensor, head_count):
    return tensor.reshape(
        tensor.shape[0], tensor.shape[1], head_count, tensor.shape[2] // head_count
    )


def merge_heads(tensor):
    return tensor.reshape(tensor.shape[0], tensor.shape[1], tensor.shape[2] * tensor.shape[3])


def gathered_body(
    alignment_rows, pair_entries, combined_weight, output_weight, pair_weight, updated_gradient
):
    sequence_count, residue_count, alignment_width = alignment_rows.shape
    head_count = pair_weight.shape[1]
    query_width = output_weight.shape[0]
    head_dim = query_width // head_count
    column_count = pair_entries.shape[1]
    token_count = sequence_count * residue_count
    score_scale = 1.0 / math.sqrt(head_dim * sequence_count * lax.axis_size("seq"))
    normalized_rows, broadcast_pair = layer_normalize(alignment_rows)
    normalized_rows_backward = normalized_rows.astype(jnp.bfloat16).reshape(
        token_count, alignment_width
    )
    projected = jnp.dot(
        normalized_rows_backward, combined_weight, preferred_element_type=jnp.float32
    ).reshape(sequence_count, residue_count, 4 * query_width)
    queries = (projected[..., :query_width] * score_scale).astype(jnp.bfloat16)
    key_rows = projected[..., query_width : 2 * query_width].astype(jnp.bfloat16)
    value_rows = projected[..., 2 * query_width : 3 * query_width].astype(jnp.bfloat16)
    gate_open = jax.nn.sigmoid(projected[..., 3 * query_width :])
    all_keys, all_values = (
        lax.all_gather(key_rows, "res", axis=1, tiled=True),
        lax.all_gather(value_rows, "res", axis=1, tiled=True),
    )
    query_heads = split_heads(queries, head_count)
    key_heads = split_heads(all_keys, head_count)
    value_heads = split_heads(all_values, head_count)
    score_terms = jnp.einsum(
        "sihd,sjhd->hij", query_heads, key_heads, preferred_element_type=jnp.float32
    )
    pair_normed, pair_spread = layer_normalize(pair_entries)
    pair_bias = jnp.einsum("ijc,ch->hij", pair_normed, pair_weight, precision=lax.Precision.HIGHEST)
    col_start = lax.axis_index("seq") * column_count
    own_block = lax.dynamic_slice_in_dim(score_terms, col_start, column_count, 2) + pair_bias
    logits = lax.psum(lax.dynamic_update_slice_in_dim(score_terms, own_block, col_start, 2), "seq")
    row_top = jnp.max(logits, axis=-1, keepdims=True)
    lifted = jnp.exp(logits - row_top)
    softmax_out = lifted / jnp.sum(lifted, axis=-1, keepdims=True)
    softmax_low = softmax_out.astype(jnp.bfloat16)
    attended = merge_heads(
        jnp.einsum("hij,sjhd->sihd", softmax_low, value_heads, preferred_element_type=jnp.float32)
    )
    gated_out = (gate_open * attended).astype(jnp.bfloat16)
    flattened_gated = gated_out.reshape(token_count, query_width)
    updated = (
        jnp.dot(flattened_gated, output_weight, preferred_element_type=jnp.float32)
        .astype(jnp.bfloat16)
        .reshape(sequence_count, residue_count, alignment_width)
    )
    flattened_gradient = updated_gradient.reshape(token_count, alignment_width)
    grad_gated = jnp.dot(
        flattened_gradient, output_weight.T, preferred_element_type=jnp.float32
    ).reshape(sequence_count, residue_count, query_width)
    out_local = jnp.dot(flattened_gated.T, flattened_gradient, preferred_element_type=jnp.float32)
    grad_attended = (grad_gated * gate_open).astype(jnp.bfloat16)
    grad_gate_logit = grad_gated * attended * gate_open * (1.0 - gate_open)
    attended_grad_heads = split_heads(grad_attended, head_count)
    grad_terms = jnp.einsum(
        "sihd,sjhd->hij", attended_grad_heads, value_heads, preferred_element_type=jnp.float32
    )
    grad_probs = lax.psum(grad_terms, "seq")
    row_dot = jnp.sum(softmax_out * grad_probs, axis=-1, keepdims=True)
    grad_logits = softmax_out * (grad_probs - row_dot)
    grad_logits_b = grad_logits.astype(jnp.bfloat16)
    logit_share = lax.dynamic_slice_in_dim(grad_logits, col_start, column_count, 2)
    grad_query_heads = (
        jnp.einsum("hij,sjhd->sihd", grad_logits_b, key_heads, preferred_element_type=jnp.float32)
        * score_scale
    )
    key_part = jnp.einsum(
        "hij,sihd->jshd", grad_logits_b, query_heads, preferred_element_type=jnp.float32
    )
    value_part = jnp.einsum(
        "hij,sihd->jshd", softmax_low, attended_grad_heads, preferred_element_type=jnp.float32
    )
    summed = lax.psum_scatter(
        jnp.concatenate([merge_heads(key_part), merge_heads(value_part)], axis=-1),
        "res",
        scatter_dimension=0,
        tiled=True,
    )
    key_value_grads = jnp.transpose(summed, (1, 0, 2))
    projected_gradient = jnp.concatenate(
        [merge_heads(grad_query_heads), key_value_grads, grad_gate_logit], axis=-1
    )
    projected_gradient = projected_gradient.astype(jnp.bfloat16).reshape(
        token_count, 4 * query_width
    )
    qkvg_local = jnp.dot(
        normalized_rows_backward.T, projected_gradient, preferred_element_type=jnp.float32
    )
    normalized_gradient = jnp.dot(
        projected_gradient, combined_weight.T, preferred_element_type=jnp.float32
    ).reshape(sequence_count, residue_count, alignment_width)
    alignment_gradient = layer_norm_backward(
        normalized_gradient, normalized_rows, broadcast_pair
    ).astype(jnp.bfloat16)
    pair_w_local = jnp.einsum(
        "ijc,hij->ch", pair_normed, logit_share, precision=lax.Precision.HIGHEST
    )
    grad_pair_normed = jnp.einsum(
        "hij,ch->ijc", logit_share, pair_weight, precision=lax.Precision.HIGHEST
    )
    pair_gradient = layer_norm_backward(grad_pair_normed, pair_normed, pair_spread).astype(
        jnp.bfloat16
    )
    combined_weight_gradient, output_weight_gradient, pair_weight_gradient = lax.psum(
        (qkvg_local, out_local, pair_w_local), ("seq", "res")
    )
    return (
        updated,
        alignment_gradient,
        pair_gradient,
        combined_weight_gradient,
        output_weight_gradient,
        pair_weight_gradient,
    )


VMEM_LIMIT = 20 * 1024 * 1024
LANES = 128
SLOTS = 4
NT = (((1,), (1,)), ((), ()))
TN = (((0,), (0,)), ((), ()))


def f32_dot(left, right, dims=None):
    if dims is None:
        return jnp.dot(left, right, preferred_element_type=jnp.float32)
    return lax.dot_general(left, right, dims, preferred_element_type=jnp.float32)


def two_terms(values):
    high = values.astype(jnp.bfloat16)
    return high, (values - high.astype(jnp.float32)).astype(jnp.bfloat16)


def slot_select(pieces):
    slot = lax.broadcasted_iota(jnp.int32, pieces[0].shape, 1) // (LANES // SLOTS)
    result = pieces[0]
    for k in range(1, SLOTS):
        result = jnp.where(slot == k, pieces[k], result)
    return result


def pack_heads(out_ref, row, tensor, residues):
    for core in range(2):
        for tile in range(tensor.shape[1] // LANES):
            rolled = []
            for s in range(SLOTS):
                start = (core * SLOTS + s) * residues
                piece = tensor[start : start + residues, tile * LANES : (tile + 1) * LANES]
                rolled.append(pltpu.roll(piece, s * LANES // SLOTS, 1) if s else piece)
            for j in range(SLOTS):
                block = slot_select([rolled[(k - j) % SLOTS] for k in range(SLOTS)])
                out_ref[(tile * SLOTS + j) * 2 + core, row : row + residues, :] = block.astype(
                    jnp.bfloat16
                )


def unpack_heads(in_ref, row, residues, tiles):
    rows = []
    for core in range(2):
        for s in range(SLOTS):
            pieces = []
            for tile in range(tiles):
                blocks = [
                    in_ref[
                        (tile * SLOTS + (k - s) % SLOTS) * 2 + core, row : row + residues, :
                    ].astype(jnp.float32)
                    for k in range(SLOTS)
                ]
                block = slot_select(blocks)
                pieces.append(pltpu.roll(block, LANES - s * LANES // SLOTS, 1) if s else block)
            rows.append(jnp.concatenate(pieces, axis=1))
    return jnp.concatenate(rows, axis=0)


def normalized(x_ref):
    width = x_ref.shape[-1]
    values = x_ref[...].reshape(-1, width).astype(jnp.float32)
    return layer_normalize(values)


def gate_of(logits):
    return 1.0 / (1.0 + jnp.exp(-logits))


def value_kernel(x_ref, grad_ref, wc_ref, wo_ref, out_ref):
    residues, width = x_ref.shape[1], x_ref.shape[2]
    normed = normalized(x_ref)[0].astype(jnp.bfloat16)
    values = f32_dot(normed, wc_ref[:, 2 * width : 3 * width])
    gate = gate_of(f32_dot(normed, wc_ref[:, 3 * width :]))
    grad_gated = f32_dot(grad_ref[...].reshape(-1, width), wo_ref[...], NT)
    pack_heads(out_ref, 0, values, residues)
    pack_heads(out_ref, residues, grad_gated * gate, residues)


def centred(weight):
    return weight - jnp.mean(weight, axis=1, keepdims=True)


def query_kernel(scale, x_ref, wc_ref, pair_ref, weight_ref, out_ref, bias_ref, mean_ref, spread_ref):
    residues, width = x_ref.shape[1], x_ref.shape[2]
    heads = weight_ref.shape[0]
    normed = normalized(x_ref)[0].astype(jnp.bfloat16)
    pack_heads(out_ref, 0, f32_dot(normed, wc_ref[:, :width]) * scale, residues)
    pack_heads(out_ref, residues, f32_dot(normed, wc_ref[:, width : 2 * width]), residues)

    columns, channels = pair_ref.shape[1], pair_ref.shape[2]
    weight = centred(weight_ref[...])
    first = weight.astype(jnp.bfloat16)
    second, third = two_terms(weight - first.astype(jnp.float32))
    share = jnp.full((heads, channels), 1.0 / channels, jnp.bfloat16)
    left = jnp.concatenate([first, second, third, share], axis=0)
    average = jnp.full((channels, channels), 1.0 / channels, jnp.bfloat16)
    step_rows = 8

    def rows(step, carry):
        start = pl.multiple_of(step * step_rows, step_rows)
        entries = pair_ref[pl.ds(start, step_rows)].reshape(step_rows * columns, channels)
        center = entries.astype(jnp.float32) - f32_dot(entries, average)
        high, low = two_terms(center * center)
        variance = f32_dot(share, high, NT) + f32_dot(share, low, NT)
        spread = lax.rsqrt(variance + eps_norm)
        raw = f32_dot(left, entries, NT)
        bias = spread * (raw[:heads] + raw[heads : 2 * heads] + raw[2 * heads : 3 * heads])
        for k in range(step_rows):
            lanes = slice(k * columns, (k + 1) * columns)
            bias_ref[:, start + k, :] = bias[:, lanes]
            mean_ref[pl.ds(start + k, 1), :] = raw[3 * heads : 3 * heads + 1, lanes]
            spread_ref[pl.ds(start + k, 1), :] = spread[:1, lanes]
        return carry

    lax.fori_loop(0, pair_ref.shape[0] // step_rows, rows, 0)
    half = residues // 2
    for h in range(heads):
        for core in range(2):
            high, low = two_terms(bias_ref[h, core * half : (core + 1) * half, :])
            out_ref[h * 2 + core, 2 * residues : 2 * residues + half, :] = high
            out_ref[h * 2 + core, 2 * residues + half : 3 * residues, :] = low


def lanes_of(blocks_ref, row, residues):
    count = blocks_ref.shape[0] // 2
    planes = [
        blocks_ref[p * count : (p + 1) * count, row : row + residues, :].reshape(-1, LANES)
        for p in range(2)
    ]
    return jnp.concatenate(planes, axis=1)


def score_kernel(
    residues, left_row, right_row, with_bias, place_ref, own_ref, other_ref, mine_ref, sent_ref
):
    core, half = place_ref[0], place_ref[1]
    count = own_ref.shape[0] // 2
    part = residues // 2
    right = jnp.concatenate(
        [lanes_of(own_ref, right_row, residues), lanes_of(other_ref, right_row, residues)], axis=1
    )
    for which, ref in ((half, mine_ref), (1 - half, sent_ref)):
        left = []
        for k in range(count // 2):
            block = which * (count // 2) + k
            rows = pl.ds(pl.multiple_of(left_row + core * part, part), part)
            left.append(
                jnp.concatenate(
                    [
                        r[p * count + block, rows, :]
                        for r in (own_ref, other_ref)
                        for p in range(2)
                    ],
                    axis=1,
                )
            )
        ref[...] = f32_dot(jnp.concatenate(left, axis=0), right, NT).astype(ref.dtype)
        if with_bias:
            for p in range(2):
                columns = pl.ds(pl.multiple_of((half * 2 + p) * LANES, LANES), LANES)
                for k in range(count // 2):
                    block = p * count + which * (count // 2) + k
                    high = own_ref[block, 2 * residues : 2 * residues + part, :]
                    low = own_ref[block, 2 * residues + part : 3 * residues, :]
                    bias = high.astype(jnp.float32) + low.astype(jnp.float32)
                    ref[k * part : (k + 1) * part, columns] += bias


def softmax_kernel(logit_ref, logit_other_ref, grad_ref, grad_other_ref, out_ref, prob_ref):
    logits = logit_ref[...] + logit_other_ref[...]
    lifted = jnp.exp(logits - jnp.max(logits, axis=-1, keepdims=True))
    softmax_out = lifted / jnp.sum(lifted, axis=-1, keepdims=True)
    prob_ref[...] = softmax_out.astype(jnp.bfloat16)
    grad_probs = grad_ref[...] + grad_other_ref[...].astype(jnp.float32)
    row_dot = jnp.sum(softmax_out * grad_probs, axis=-1, keepdims=True)
    out_ref[...] = (softmax_out * (grad_probs - row_dot)).astype(jnp.bfloat16)


def product_kernel(
    residues, scale, first_row, second_row, with_share,
    place_ref, own_ref, far_ref, near_ref, corner_ref, blocks_ref, out_ref, whole_ref,
):
    core, half = place_ref[0], place_ref[1]
    count = blocks_ref.shape[0] // 2
    part = residues // 2
    quarters = (
        (own_ref, core, half), (far_ref, core, 1 - half),
        (near_ref, 1 - core, half), (corner_ref, 1 - core, 1 - half),
    )
    for ref, c, z in quarters:
        for k in range(count // 2):
            start = (z * (count // 2) + k) * residues + c * part
            whole_ref[pl.ds(pl.multiple_of(start, part), part), :] = ref[k * part : (k + 1) * part, :]
    whole = whole_ref[...]
    if with_share:
        for p in range(2):
            columns = pl.ds(pl.multiple_of((half * 2 + p) * LANES, LANES), LANES)
            for q in range(count):
                rows = pl.ds(pl.multiple_of(q * residues + core * part, part), part)
                out_ref[p * count + q, 2 * residues : 2 * residues + part, :] = whole_ref[rows, columns]
    first = f32_dot(whole, lanes_of(blocks_ref, first_row, residues)) * scale
    second = f32_dot(whole, lanes_of(blocks_ref, second_row, residues), TN)
    for row, product in ((0, first), (residues, second)):
        for p in range(2):
            out_ref[p * count : (p + 1) * count, row : row + residues, :] = (
                product[:, p * LANES : (p + 1) * LANES]
                .astype(jnp.bfloat16)
                .reshape(count, residues, LANES)
            )


def share_of(blocks_ref, row, part, heads):
    return jnp.concatenate(
        [
            blocks_ref[:, row : row + part, :]
            .astype(jnp.float32)
            .reshape(heads, 2 * part, LANES)
        ],
        axis=0,
    )


def weight_kernel(
    place_ref, x_ref, grad_ref, wc_ref, wo_ref, attended_ref, blocks_ref, pair_weight_ref,
    updated_ref, projected_ref, keep_ref, send_ref, sums_ref,
):
    residues, width = x_ref.shape[1], x_ref.shape[2]
    tiles = width // LANES
    core = place_ref[0]
    normed = normalized(x_ref)[0].astype(jnp.bfloat16)
    gate = gate_of(f32_dot(normed, wc_ref[:, 3 * width :]))
    grad = grad_ref[...].reshape(-1, width)
    grad_gated = f32_dot(grad, wo_ref[...], NT)
    attended = unpack_heads(attended_ref, 0, residues, tiles)
    gated = (gate * attended).astype(jnp.bfloat16)
    updated_ref[...] = f32_dot(gated, wo_ref[...]).astype(jnp.bfloat16).reshape(updated_ref.shape)
    parts = [
        unpack_heads(blocks_ref, 0, residues, tiles),
        unpack_heads(blocks_ref, residues, residues, tiles),
        unpack_heads(attended_ref, residues, residues, tiles),
        grad_gated * attended * gate * (1.0 - gate),
    ]
    for t in range(4):
        projected_ref[:, t * width : (t + 1) * width] = parts[t].astype(jnp.bfloat16)
    sums_ref[:, : 4 * width] = f32_dot(normed, projected_ref[...], TN).astype(jnp.bfloat16)
    sums_ref[:, 4 * width : 5 * width] = f32_dot(gated, grad, TN).astype(jnp.bfloat16)
    heads, channels = pair_weight_ref.shape
    rows = sums_ref.shape[0] // heads
    first = lax.broadcasted_iota(jnp.int32, (rows, channels), 0) == 0
    for h in range(heads):
        row = jnp.broadcast_to(pair_weight_ref[h : h + 1], (rows, channels))
        sums_ref[h * rows : (h + 1) * rows, 5 * width :] = jnp.where(first, row, 0.0).astype(
            jnp.bfloat16
        )
    for which, ref in ((core, keep_ref), (1 - core, send_ref)):
        for block in range(heads // 2):
            start = pl.multiple_of((2 * block + which) * rows, rows)
            ref[block] = sums_ref[pl.ds(start, rows), :]


def pair_weight_kernel(blocks_ref, pair_ref, mean_ref, spread_ref, out_ref, share_ref):
    heads, part = share_ref.shape[0], pair_ref.shape[0] // 2
    share_ref[...] = share_of(blocks_ref, blocks_ref.shape[1] - part, part, heads)

    def rows(step, carry):
        total, shift = carry
        for k in range(8):
            i = step * 8 + k
            scaled = share_ref[:, i, :] * spread_ref[pl.ds(i, 1), :]
            high, low = two_terms(scaled)
            total += f32_dot(jnp.concatenate([high, low], axis=0), pair_ref[i])
            shift += (high.astype(jnp.float32) + low.astype(jnp.float32)) * mean_ref[pl.ds(i, 1), :]
        return total, shift

    channels = pair_ref.shape[2]
    total, shift = lax.fori_loop(
        0,
        pair_ref.shape[0] // 8,
        rows,
        (jnp.zeros((2 * heads, channels), jnp.float32), jnp.zeros((heads, LANES), jnp.float32)),
    )
    out_ref[...] = total[:heads] + total[heads:] - jnp.sum(shift, axis=1, keepdims=True)


def alignment_kernel(x_ref, wc_ref, projected_ref, out_ref):
    normed, spread = normalized(x_ref)
    gradient = f32_dot(projected_ref[...], wc_ref[...], NT)
    out_ref[...] = (
        layer_norm_backward(gradient, normed, spread).astype(jnp.bfloat16).reshape(out_ref.shape)
    )


def pair_kernel(blocks_row, blocks_ref, pair_ref, weight_ref, bias_ref, mean_ref, spread_ref, out_ref, share_ref):
    heads, channels = weight_ref.shape
    part = pair_ref.shape[0] // 2
    share_ref[...] = share_of(blocks_ref, blocks_row, part, heads)
    first, second = two_terms(centred(weight_ref[...]))
    zero = jnp.zeros((heads, channels), jnp.bfloat16)
    top = lax.broadcasted_iota(jnp.int32, (heads, channels), 0) < 2
    ones = jnp.where(top, 1.0, 0.0).astype(jnp.bfloat16)
    right = jnp.concatenate(
        [
            jnp.concatenate([first, first, second, ones, zero], axis=0),
            jnp.concatenate([zero, zero, zero, zero, ones], axis=0),
        ],
        axis=1,
    )
    row = lax.broadcasted_iota(jnp.int32, (heads, LANES), 0)

    def rows_of_two(value):
        high, low = two_terms(value)
        high, low = high.astype(jnp.float32), low.astype(jnp.float32)
        return jnp.where(row == 0, high, jnp.where(row == 1, low, 0.0)).astype(jnp.bfloat16)

    def rows(step, carry):
        for k in range(8):
            i = step * 8 + k
            gradient = share_ref[:, i, :]
            spread = spread_ref[pl.ds(i, 1), :]
            cross = jnp.sum(gradient * bias_ref[:, i, :], axis=0, keepdims=True) / channels
            slope = spread * spread * cross
            high, low = two_terms(gradient * spread)
            left = jnp.concatenate(
                [
                    high, low, high,
                    rows_of_two(jnp.broadcast_to(slope * mean_ref[pl.ds(i, 1), :], row.shape)),
                    rows_of_two(jnp.broadcast_to(slope, row.shape)),
                ],
                axis=0,
            )
            terms = f32_dot(left, right, TN)
            entries = pair_ref[i].astype(jnp.float32)
            out_ref[i] = (terms[:, :channels] - terms[:, channels:] * entries).astype(jnp.bfloat16)
        return carry

    lax.fori_loop(0, pair_ref.shape[0] // 8, rows, 0)


def call(kernel, outs, *args, scratch=(), place=None, flops=0, after=()):
    whole = pl.BlockSpec(memory_space=pltpu.VMEM)
    specs = [whole] * len(args)
    if place is not None:
        specs = [pl.BlockSpec(memory_space=pltpu.SMEM)] + specs
        args = (place,) + args
    shapes = [jax.ShapeDtypeStruct(*o) for o in outs]
    moved = sum(math.prod(a.shape) * a.dtype.itemsize for a in list(args) + shapes)
    first, last = len(args), len(args) + len(after)
    return pl.pallas_call(
        lambda *refs: kernel(*refs[:first], *refs[last:]),
        out_shape=shapes,
        in_specs=specs + [pl.BlockSpec(memory_space=pl.ANY)] * len(after),
        out_specs=[whole] * len(shapes),
        scratch_shapes=scratch,
        compiler_params=pltpu.CompilerParams(vmem_limit_bytes=VMEM_LIMIT),
        cost_estimate=pl.CostEstimate(flops=flops, bytes_accessed=moved, transcendentals=0),
    )(*args, *after)


def swapped(mine, axis_name, distance):
    size = lax.axis_size(axis_name)
    return lax.ppermute(mine, axis_name, [(a, a ^ distance) for a in range(size)])


def fits_heads(alignment_rows, pair_entries, pair_weight):
    channels, heads = pair_weight.shape
    return (
        lax.axis_size("seq") == 4
        and lax.axis_size("res") == heads == 8
        and alignment_rows.shape[0] == 2 * SLOTS
        and alignment_rows.shape[1] == pair_entries.shape[0] == 64
        and alignment_rows.shape[2] == 2 * LANES
        and pair_entries.shape[1] == channels == LANES
    )


def head_body(
    alignment_rows, pair_entries, combined_weight, output_weight, pair_weight, updated_gradient
):
    sequences, residues, width = alignment_rows.shape
    channels, heads = pair_weight.shape
    tokens = sequences * residues
    seq_size, res_size = lax.axis_size("seq"), lax.axis_size("res")
    seq_half = seq_size // 2
    total = residues * res_size
    group = 2 * res_size
    groups = [[g * group + k for k in range(group)] for g in range(seq_half)]
    scale = 1.0 / math.sqrt(width // heads * sequences * seq_size)
    res_index, seq_index = lax.axis_index("res"), lax.axis_index("seq")
    place = jnp.stack([res_index % 2, seq_index // 2]).astype(jnp.int32)
    bf16, f32 = jnp.bfloat16, jnp.float32

    def across(blocks):
        return lax.all_to_all(blocks, ("seq", "res"), 0, 0, axis_index_groups=groups, tiled=True)

    def all_quarters(mine):
        far = swapped(mine, "seq", seq_half)
        return mine, far, swapped(mine, "res", 1), swapped(far, "res", 1)

    x, grad, wc, wo = alignment_rows, updated_gradient, combined_weight, output_weight
    query_blocks, bias, mean, spread = call(
        functools.partial(query_kernel, scale),
        [
            ((group, 3 * residues, LANES), bf16),
            ((heads, residues, LANES), f32),
            ((residues, LANES), f32),
            ((residues, LANES), f32),
        ],
        x, wc, pair_entries, pair_weight.T,
        flops=8 * tokens * width * width,
    )
    query_blocks = across(query_blocks)
    (value_blocks,) = call(
        value_kernel, [((group, 2 * residues, LANES), bf16)], x, grad, wc, wo,
        flops=8 * tokens * width * width,
    )
    value_blocks = across(value_blocks)

    def scores(blocks, left_row, right_row, with_bias, kind, after=()):
        return call(
            functools.partial(score_kernel, residues, left_row, right_row, with_bias),
            [((total // 4, total), f32), ((total // 4, total), kind)],
            blocks, swapped(blocks, "res", 1),
            place=place, flops=2 * total * total * width, after=after,
        )

    logit_mine, logit_sent = scores(query_blocks, 0, residues, True, f32)
    logit_other = swapped(logit_sent, "seq", seq_half)
    grad_mine, grad_sent = scores(value_blocks, residues, 0, False, bf16, after=(logit_mine,))
    grad_other = swapped(grad_sent, "seq", seq_half)
    quarter = ((total // 4, total), bf16)
    grad_logits, probs = call(
        softmax_kernel, [quarter, quarter], logit_mine, logit_other, grad_mine, grad_other,
        flops=total * total,
    )

    def products(quarters, blocks, first_row, second_row, with_share, factor):
        rows = 2 * residues + (residues // 2 if with_share else 0)
        (out,) = call(
            functools.partial(
                product_kernel, residues, factor, first_row, second_row, with_share
            ),
            [((group, rows, LANES), bf16)],
            *quarters, blocks,
            scratch=[pltpu.VMEM((total, total), bf16)],
            place=place, flops=4 * total * total * width,
        )
        return across(out)

    grad_blocks = products(all_quarters(grad_logits), query_blocks, residues, 0, True, scale)
    attended_blocks = products(all_quarters(probs), value_blocks, 0, residues, False, 1.0)

    share = pltpu.VMEM((heads, residues, LANES), f32)
    (pair_weight_part,) = call(
        pair_weight_kernel, [((heads, channels), f32)],
        grad_blocks, pair_entries, mean, spread,
        scratch=[share], flops=4 * tokens * width * width,
    )
    (pair_gradient,) = call(
        functools.partial(pair_kernel, 2 * residues),
        [(pair_entries.shape, bf16)],
        grad_blocks, pair_entries, pair_weight.T, bias, mean, spread,
        scratch=[share], flops=8 * tokens * width * width,
    )
    columns = 5 * width + channels
    rows = width // res_size
    part_rows = ((res_size // 2, rows, columns), bf16)
    updated, projected, keep, send = call(
        weight_kernel,
        [(x.shape, bf16), ((tokens, 4 * width), bf16), part_rows, part_rows],
        x, grad, wc, wo, attended_blocks, grad_blocks, pair_weight_part,
        scratch=[pltpu.VMEM((width, columns), bf16)],
        place=place, flops=24 * tokens * width * width,
    )
    (alignment_gradient,) = call(
        alignment_kernel, [(x.shape, bf16)], x, wc, projected,
        flops=8 * tokens * width * width,
    )

    def added(mine, other):
        return (mine.astype(f32) + other.astype(f32)).astype(bf16)

    parts = added(keep, swapped(send, "res", 1))
    chips = [[2 * k + core for k in range(res_size // 2)] for core in range(2)]
    parts = lax.all_to_all(parts, "res", 0, 0, axis_index_groups=chips, tiled=True)
    part = jnp.sum(parts.astype(f32), axis=0).astype(bf16)
    part = added(part, swapped(part, "seq", 1))
    part = added(part, swapped(part, "seq", seq_half))
    whole = lax.all_gather(part, "res", axis=0)
    return (
        updated,
        alignment_gradient,
        pair_gradient,
        whole[:, :, : 4 * width].reshape(wc.shape).astype(f32),
        whole[:, :, 4 * width : 5 * width].reshape(wo.shape).astype(f32),
        whole[:, 0, 5 * width :].T.astype(f32),
    )


def body(alignment_rows, pair_entries, combined_weight, output_weight, pair_weight, updated_gradient):
    chosen = head_body if fits_heads(alignment_rows, pair_entries, pair_weight) else gathered_body
    return chosen(
        alignment_rows, pair_entries, combined_weight, output_weight, pair_weight, updated_gradient
    )


def solution(mesh):
    return jax.shard_map(
        body,
        mesh=mesh,
        in_specs=(
            P("seq", "res", None),
            P("res", "seq", None),
            P(),
            P(),
            P(),
            P("seq", "res", None),
        ),
        out_specs=(
            P("seq", "res", None),
            P("seq", "res", None),
            P("res", "seq", None),
            P(),
            P(),
            P(),
        ),
        check_vma=False,
    )
```

```python
import functools
import math

import jax
import jax.numpy as jnp
from jax import lax
from jax.experimental import pallas as pl
from jax.experimental.pallas import tpu as pltpu
from jax.sharding import PartitionSpec as P

eps_norm = 1e-05


def layer_normalize(values):
    values = values.astype(jnp.float32)
    center = values - jnp.mean(values, axis=-1, keepdims=True)
    broadcast_pair = lax.rsqrt(jnp.mean(center * center, axis=-1, keepdims=True) + eps_norm)
    return (center * broadcast_pair, broadcast_pair)


def layer_norm_backward(normalized_gradient, normalized_rows, broadcast_pair):
    mean_grad = jnp.mean(normalized_gradient, axis=-1, keepdims=True)
    mean_cross = jnp.mean(normalized_gradient * normalized_rows, axis=-1, keepdims=True)
    return broadcast_pair * (normalized_gradient - mean_grad - normalized_rows * mean_cross)


def split_heads(tensor, head_count):
    return tensor.reshape(
        tensor.shape[0], tensor.shape[1], head_count, tensor.shape[2] // head_count
    )


def merge_heads(tensor):
    return tensor.reshape(tensor.shape[0], tensor.shape[1], tensor.shape[2] * tensor.shape[3])


def gathered_body(
    alignment_rows, pair_entries, combined_weight, output_weight, pair_weight, updated_gradient
):
    sequence_count, residue_count, alignment_width = alignment_rows.shape
    head_count = pair_weight.shape[1]
    query_width = output_weight.shape[0]
    head_dim = query_width // head_count
    column_count = pair_entries.shape[1]
    token_count = sequence_count * residue_count
    score_scale = 1.0 / math.sqrt(head_dim * sequence_count * lax.axis_size("seq"))
    normalized_rows, broadcast_pair = layer_normalize(alignment_rows)
    normalized_rows_backward = normalized_rows.astype(jnp.bfloat16).reshape(
        token_count, alignment_width
    )
    projected = jnp.dot(
        normalized_rows_backward, combined_weight, preferred_element_type=jnp.float32
    ).reshape(sequence_count, residue_count, 4 * query_width)
    queries = (projected[..., :query_width] * score_scale).astype(jnp.bfloat16)
    key_rows = projected[..., query_width : 2 * query_width].astype(jnp.bfloat16)
    value_rows = projected[..., 2 * query_width : 3 * query_width].astype(jnp.bfloat16)
    gate_open = jax.nn.sigmoid(projected[..., 3 * query_width :])
    all_keys, all_values = (
        lax.all_gather(key_rows, "res", axis=1, tiled=True),
        lax.all_gather(value_rows, "res", axis=1, tiled=True),
    )
    query_heads = split_heads(queries, head_count)
    key_heads = split_heads(all_keys, head_count)
    value_heads = split_heads(all_values, head_count)
    score_terms = jnp.einsum(
        "sihd,sjhd->hij", query_heads, key_heads, preferred_element_type=jnp.float32
    )
    pair_normed, pair_spread = layer_normalize(pair_entries)
    pair_bias = jnp.einsum("ijc,ch->hij", pair_normed, pair_weight, precision=lax.Precision.HIGHEST)
    col_start = lax.axis_index("seq") * column_count
    own_block = lax.dynamic_slice_in_dim(score_terms, col_start, column_count, 2) + pair_bias
    logits = lax.psum(lax.dynamic_update_slice_in_dim(score_terms, own_block, col_start, 2), "seq")
    row_top = jnp.max(logits, axis=-1, keepdims=True)
    lifted = jnp.exp(logits - row_top)
    softmax_out = lifted / jnp.sum(lifted, axis=-1, keepdims=True)
    softmax_low = softmax_out.astype(jnp.bfloat16)
    attended = merge_heads(
        jnp.einsum("hij,sjhd->sihd", softmax_low, value_heads, preferred_element_type=jnp.float32)
    )
    gated_out = (gate_open * attended).astype(jnp.bfloat16)
    flattened_gated = gated_out.reshape(token_count, query_width)
    updated = (
        jnp.dot(flattened_gated, output_weight, preferred_element_type=jnp.float32)
        .astype(jnp.bfloat16)
        .reshape(sequence_count, residue_count, alignment_width)
    )
    flattened_gradient = updated_gradient.reshape(token_count, alignment_width)
    grad_gated = jnp.dot(
        flattened_gradient, output_weight.T, preferred_element_type=jnp.float32
    ).reshape(sequence_count, residue_count, query_width)
    out_local = jnp.dot(flattened_gated.T, flattened_gradient, preferred_element_type=jnp.float32)
    grad_attended = (grad_gated * gate_open).astype(jnp.bfloat16)
    grad_gate_logit = grad_gated * attended * gate_open * (1.0 - gate_open)
    attended_grad_heads = split_heads(grad_attended, head_count)
    grad_terms = jnp.einsum(
        "sihd,sjhd->hij", attended_grad_heads, value_heads, preferred_element_type=jnp.float32
    )
    grad_probs = lax.psum(grad_terms, "seq")
    row_dot = jnp.sum(softmax_out * grad_probs, axis=-1, keepdims=True)
    grad_logits = softmax_out * (grad_probs - row_dot)
    grad_logits_b = grad_logits.astype(jnp.bfloat16)
    logit_share = lax.dynamic_slice_in_dim(grad_logits, col_start, column_count, 2)
    grad_query_heads = (
        jnp.einsum("hij,sjhd->sihd", grad_logits_b, key_heads, preferred_element_type=jnp.float32)
        * score_scale
    )
    key_part = jnp.einsum(
        "hij,sihd->jshd", grad_logits_b, query_heads, preferred_element_type=jnp.float32
    )
    value_part = jnp.einsum(
        "hij,sihd->jshd", softmax_low, attended_grad_heads, preferred_element_type=jnp.float32
    )
    summed = lax.psum_scatter(
        jnp.concatenate([merge_heads(key_part), merge_heads(value_part)], axis=-1),
        "res",
        scatter_dimension=0,
        tiled=True,
    )
    key_value_grads = jnp.transpose(summed, (1, 0, 2))
    projected_gradient = jnp.concatenate(
        [merge_heads(grad_query_heads), key_value_grads, grad_gate_logit], axis=-1
    )
    projected_gradient = projected_gradient.astype(jnp.bfloat16).reshape(
        token_count, 4 * query_width
    )
    qkvg_local = jnp.dot(
        normalized_rows_backward.T, projected_gradient, preferred_element_type=jnp.float32
    )
    normalized_gradient = jnp.dot(
        projected_gradient, combined_weight.T, preferred_element_type=jnp.float32
    ).reshape(sequence_count, residue_count, alignment_width)
    alignment_gradient = layer_norm_backward(
        normalized_gradient, normalized_rows, broadcast_pair
    ).astype(jnp.bfloat16)
    pair_w_local = jnp.einsum(
        "ijc,hij->ch", pair_normed, logit_share, precision=lax.Precision.HIGHEST
    )
    grad_pair_normed = jnp.einsum(
        "hij,ch->ijc", logit_share, pair_weight, precision=lax.Precision.HIGHEST
    )
    pair_gradient = layer_norm_backward(grad_pair_normed, pair_normed, pair_spread).astype(
        jnp.bfloat16
    )
    combined_weight_gradient, output_weight_gradient, pair_weight_gradient = lax.psum(
        (qkvg_local, out_local, pair_w_local), ("seq", "res")
    )
    return (
        updated,
        alignment_gradient,
        pair_gradient,
        combined_weight_gradient,
        output_weight_gradient,
        pair_weight_gradient,
    )


VMEM_LIMIT = 20 * 1024 * 1024
ARGUMENT_VMEM_LIMIT = 56 * 1024 * 1024
LANES = 128
SLOTS = 4
NT = (((1,), (1,)), ((), ()))
TN = (((0,), (0,)), ((), ()))


def f32_dot(left, right, dims=None):
    if dims is None:
        return jnp.dot(left, right, preferred_element_type=jnp.float32)
    return lax.dot_general(left, right, dims, preferred_element_type=jnp.float32)


def two_terms(values):
    high = values.astype(jnp.bfloat16)
    return high, (values - high.astype(jnp.float32)).astype(jnp.bfloat16)


def slot_select(pieces):
    slot = lax.broadcasted_iota(jnp.int32, pieces[0].shape, 1) // (LANES // SLOTS)
    result = pieces[0]
    for k in range(1, SLOTS):
        result = jnp.where(slot == k, pieces[k], result)
    return result


def pack_heads(out_ref, row, tensor, residues):
    for core in range(2):
        for tile in range(tensor.shape[1] // LANES):
            rolled = []
            for s in range(SLOTS):
                start = (core * SLOTS + s) * residues
                piece = tensor[start : start + residues, tile * LANES : (tile + 1) * LANES]
                rolled.append(pltpu.roll(piece, s * LANES // SLOTS, 1) if s else piece)
            for j in range(SLOTS):
                block = slot_select([rolled[(k - j) % SLOTS] for k in range(SLOTS)])
                out_ref[(tile * SLOTS + j) * 2 + core, row : row + residues, :] = block.astype(
                    jnp.bfloat16
                )


def unpack_heads(in_ref, row, residues, tiles):
    rows = []
    for core in range(2):
        for s in range(SLOTS):
            pieces = []
            for tile in range(tiles):
                blocks = [
                    in_ref[
                        (tile * SLOTS + (k - s) % SLOTS) * 2 + core, row : row + residues, :
                    ].astype(jnp.float32)
                    for k in range(SLOTS)
                ]
                block = slot_select(blocks)
                pieces.append(pltpu.roll(block, LANES - s * LANES // SLOTS, 1) if s else block)
            rows.append(jnp.concatenate(pieces, axis=1))
    return jnp.concatenate(rows, axis=0)


def normalized(x_ref):
    width = x_ref.shape[-1]
    values = x_ref[...].reshape(-1, width).astype(jnp.float32)
    return layer_normalize(values)


def gate_of(logits):
    return 1.0 / (1.0 + jnp.exp(-logits))


def value_kernel(x_ref, grad_ref, wc_ref, wo_ref, out_ref):
    residues, width = x_ref.shape[1], x_ref.shape[2]
    normed = normalized(x_ref)[0].astype(jnp.bfloat16)
    values = f32_dot(normed, wc_ref[:, 2 * width : 3 * width])
    gate = gate_of(f32_dot(normed, wc_ref[:, 3 * width :]))
    grad_gated = f32_dot(grad_ref[...].reshape(-1, width), wo_ref[...], NT)
    pack_heads(out_ref, 0, values, residues)
    pack_heads(out_ref, residues, grad_gated * gate, residues)


def centred(weight):
    return weight - jnp.mean(weight, axis=1, keepdims=True)


def query_kernel(
    scale, arrive, x_ref, wc_ref, pair_ref, weight_ref, out_ref, bias_ref, mean_ref, spread_ref
):
    residues, width = x_ref.shape[1], x_ref.shape[2]
    heads = weight_ref.shape[0]
    normed = normalized(x_ref)[0].astype(jnp.bfloat16)
    pack_heads(out_ref, 0, f32_dot(normed, wc_ref[:, :width]) * scale, residues)
    pack_heads(out_ref, residues, f32_dot(normed, wc_ref[:, width : 2 * width]), residues)

    arrive()
    columns, channels = pair_ref.shape[1], pair_ref.shape[2]
    weight = centred(weight_ref[...])
    first = weight.astype(jnp.bfloat16)
    second, third = two_terms(weight - first.astype(jnp.float32))
    share = jnp.full((heads, channels), 1.0 / channels, jnp.bfloat16)
    left = jnp.concatenate([first, second, third, share], axis=0)
    average = jnp.full((channels, channels), 1.0 / channels, jnp.bfloat16)
    step_rows = 8

    def rows(step, carry):
        start = pl.multiple_of(step * step_rows, step_rows)
        entries = pair_ref[pl.ds(start, step_rows)].reshape(step_rows * columns, channels)
        center = entries.astype(jnp.float32) - f32_dot(entries, average)
        high, low = two_terms(center * center)
        variance = f32_dot(share, high, NT) + f32_dot(share, low, NT)
        spread = lax.rsqrt(variance + eps_norm)
        raw = f32_dot(left, entries, NT)
        bias = spread * (raw[:heads] + raw[heads : 2 * heads] + raw[2 * heads : 3 * heads])
        for k in range(step_rows):
            lanes = slice(k * columns, (k + 1) * columns)
            bias_ref[:, start + k, :] = bias[:, lanes]
            mean_ref[pl.ds(start + k, 1), :] = raw[3 * heads : 3 * heads + 1, lanes]
            spread_ref[pl.ds(start + k, 1), :] = spread[:1, lanes]
        return carry

    lax.fori_loop(0, pair_ref.shape[0] // step_rows, rows, 0)
    half = residues // 2
    for h in range(heads):
        for core in range(2):
            high, low = two_terms(bias_ref[h, core * half : (core + 1) * half, :])
            out_ref[h * 2 + core, 2 * residues : 2 * residues + half, :] = high
            out_ref[h * 2 + core, 2 * residues + half : 3 * residues, :] = low


def lanes_of(blocks_ref, row, residues):
    count = blocks_ref.shape[0] // 2
    planes = [
        blocks_ref[p * count : (p + 1) * count, row : row + residues, :].reshape(-1, LANES)
        for p in range(2)
    ]
    return jnp.concatenate(planes, axis=1)


def score_kernel(
    residues, left_row, right_row, with_bias, place_ref, own_ref, other_ref, mine_ref, sent_ref
):
    core, half = place_ref[0], place_ref[1]
    count = own_ref.shape[0] // 2
    part = residues // 2
    right = jnp.concatenate(
        [lanes_of(own_ref, right_row, residues), lanes_of(other_ref, right_row, residues)], axis=1
    )
    for which, ref in ((half, mine_ref), (1 - half, sent_ref)):
        left = []
        for k in range(count // 2):
            block = which * (count // 2) + k
            rows = pl.ds(pl.multiple_of(left_row + core * part, part), part)
            left.append(
                jnp.concatenate(
                    [
                        r[p * count + block, rows, :]
                        for r in (own_ref, other_ref)
                        for p in range(2)
                    ],
                    axis=1,
                )
            )
        ref[...] = f32_dot(jnp.concatenate(left, axis=0), right, NT).astype(ref.dtype)
        if with_bias:
            for p in range(2):
                columns = pl.ds(pl.multiple_of((half * 2 + p) * LANES, LANES), LANES)
                for k in range(count // 2):
                    block = p * count + which * (count // 2) + k
                    high = own_ref[block, 2 * residues : 2 * residues + part, :]
                    low = own_ref[block, 2 * residues + part : 3 * residues, :]
                    bias = high.astype(jnp.float32) + low.astype(jnp.float32)
                    ref[k * part : (k + 1) * part, columns] += bias


def softmax_kernel(logit_ref, other_ref, out_ref, low_ref):
    logits = logit_ref[...] + other_ref[...]
    lifted = jnp.exp(logits - jnp.max(logits, axis=-1, keepdims=True))
    softmax_out = lifted / jnp.sum(lifted, axis=-1, keepdims=True)
    out_ref[...] = softmax_out
    low_ref[...] = softmax_out.astype(jnp.bfloat16)


def softmax_gradient_kernel(softmax_ref, grad_ref, other_ref, out_ref):
    softmax_out = softmax_ref[...]
    grad_probs = grad_ref[...] + other_ref[...].astype(jnp.float32)
    row_dot = jnp.sum(softmax_out * grad_probs, axis=-1, keepdims=True)
    out_ref[...] = (softmax_out * (grad_probs - row_dot)).astype(jnp.bfloat16)


def product_kernel(
    residues, scale, first_row, second_row, with_share,
    place_ref, own_ref, far_ref, near_ref, corner_ref, blocks_ref, out_ref, whole_ref,
):
    core, half = place_ref[0], place_ref[1]
    count = blocks_ref.shape[0] // 2
    part = residues // 2
    quarters = (
        (own_ref, core, half), (far_ref, core, 1 - half),
        (near_ref, 1 - core, half), (corner_ref, 1 - core, 1 - half),
    )
    for ref, c, z in quarters:
        for k in range(count // 2):
            start = (z * (count // 2) + k) * residues + c * part
            whole_ref[pl.ds(pl.multiple_of(start, part), part), :] = ref[k * part : (k + 1) * part, :]
    whole = whole_ref[...]
    if with_share:
        for p in range(2):
            columns = pl.ds(pl.multiple_of((half * 2 + p) * LANES, LANES), LANES)
            for q in range(count):
                rows = pl.ds(pl.multiple_of(q * residues + core * part, part), part)
                out_ref[p * count + q, 2 * residues : 2 * residues + part, :] = whole_ref[rows, columns]
    first = f32_dot(whole, lanes_of(blocks_ref, first_row, residues)) * scale
    second = f32_dot(whole, lanes_of(blocks_ref, second_row, residues), TN)
    for row, product in ((0, first), (residues, second)):
        for p in range(2):
            out_ref[p * count : (p + 1) * count, row : row + residues, :] = (
                product[:, p * LANES : (p + 1) * LANES]
                .astype(jnp.bfloat16)
                .reshape(count, residues, LANES)
            )


def share_of(blocks_ref, row, part, heads):
    return jnp.concatenate(
        [
            blocks_ref[:, row : row + part, :]
            .astype(jnp.float32)
            .reshape(heads, 2 * part, LANES)
        ],
        axis=0,
    )


def weight_kernel(
    place_ref, x_ref, grad_ref, wc_ref, wo_ref, attended_ref, blocks_ref, pair_weight_ref,
    updated_ref, projected_ref, keep_ref, send_ref, sums_ref,
):
    residues, width = x_ref.shape[1], x_ref.shape[2]
    tiles = width // LANES
    core = place_ref[0]
    normed = normalized(x_ref)[0].astype(jnp.bfloat16)
    gate = gate_of(f32_dot(normed, wc_ref[:, 3 * width :]))
    grad = grad_ref[...].reshape(-1, width)
    grad_gated = f32_dot(grad, wo_ref[...], NT)
    attended = unpack_heads(attended_ref, 0, residues, tiles)
    gated = (gate * attended).astype(jnp.bfloat16)
    updated_ref[...] = f32_dot(gated, wo_ref[...]).astype(jnp.bfloat16).reshape(updated_ref.shape)
    parts = [
        unpack_heads(blocks_ref, 0, residues, tiles),
        unpack_heads(blocks_ref, residues, residues, tiles),
        unpack_heads(attended_ref, residues, residues, tiles),
        grad_gated * attended * gate * (1.0 - gate),
    ]
    for t in range(4):
        projected_ref[:, t * width : (t + 1) * width] = parts[t].astype(jnp.bfloat16)
    sums_ref[:, : 4 * width] = f32_dot(normed, projected_ref[...], TN).astype(jnp.bfloat16)
    sums_ref[:, 4 * width : 5 * width] = f32_dot(gated, grad, TN).astype(jnp.bfloat16)
    heads, channels = pair_weight_ref.shape
    rows = sums_ref.shape[0] // heads
    first = lax.broadcasted_iota(jnp.int32, (rows, channels), 0) == 0
    for h in range(heads):
        row = jnp.broadcast_to(pair_weight_ref[h : h + 1], (rows, channels))
        sums_ref[h * rows : (h + 1) * rows, 5 * width :] = jnp.where(first, row, 0.0).astype(
            jnp.bfloat16
        )
    for which, ref in ((core, keep_ref), (1 - core, send_ref)):
        for block in range(heads // 2):
            start = pl.multiple_of((2 * block + which) * rows, rows)
            ref[block] = sums_ref[pl.ds(start, rows), :]


def pair_weight_kernel(blocks_ref, pair_ref, mean_ref, spread_ref, out_ref, share_ref):
    heads, part = share_ref.shape[0], pair_ref.shape[0] // 2
    share_ref[...] = share_of(blocks_ref, blocks_ref.shape[1] - part, part, heads)

    def rows(step, carry):
        total, shift = carry
        for k in range(8):
            i = step * 8 + k
            scaled = share_ref[:, i, :] * spread_ref[pl.ds(i, 1), :]
            high, low = two_terms(scaled)
            total += f32_dot(jnp.concatenate([high, low], axis=0), pair_ref[i])
            shift += (high.astype(jnp.float32) + low.astype(jnp.float32)) * mean_ref[pl.ds(i, 1), :]
        return total, shift

    channels = pair_ref.shape[2]
    total, shift = lax.fori_loop(
        0,
        pair_ref.shape[0] // 8,
        rows,
        (jnp.zeros((2 * heads, channels), jnp.float32), jnp.zeros((heads, LANES), jnp.float32)),
    )
    out_ref[...] = total[:heads] + total[heads:] - jnp.sum(shift, axis=1, keepdims=True)


def alignment_kernel(x_ref, wc_ref, projected_ref, out_ref):
    normed, spread = normalized(x_ref)
    gradient = f32_dot(projected_ref[...], wc_ref[...], NT)
    out_ref[...] = (
        layer_norm_backward(gradient, normed, spread).astype(jnp.bfloat16).reshape(out_ref.shape)
    )


def pair_kernel(blocks_row, blocks_ref, pair_ref, weight_ref, bias_ref, mean_ref, spread_ref, out_ref, share_ref):
    heads, channels = weight_ref.shape
    part = pair_ref.shape[0] // 2
    share_ref[...] = share_of(blocks_ref, blocks_row, part, heads)
    first, second = two_terms(centred(weight_ref[...]))
    zero = jnp.zeros((heads, channels), jnp.bfloat16)
    top = lax.broadcasted_iota(jnp.int32, (heads, channels), 0) < 2
    ones = jnp.where(top, 1.0, 0.0).astype(jnp.bfloat16)
    right = jnp.concatenate(
        [
            jnp.concatenate([first, first, second, ones, zero], axis=0),
            jnp.concatenate([zero, zero, zero, zero, ones], axis=0),
        ],
        axis=1,
    )
    row = lax.broadcasted_iota(jnp.int32, (heads, LANES), 0)

    def rows_of_two(value):
        high, low = two_terms(value)
        high, low = high.astype(jnp.float32), low.astype(jnp.float32)
        return jnp.where(row == 0, high, jnp.where(row == 1, low, 0.0)).astype(jnp.bfloat16)

    def rows(step, carry):
        for k in range(8):
            i = step * 8 + k
            gradient = share_ref[:, i, :]
            spread = spread_ref[pl.ds(i, 1), :]
            cross = jnp.sum(gradient * bias_ref[:, i, :], axis=0, keepdims=True) / channels
            slope = spread * spread * cross
            high, low = two_terms(gradient * spread)
            left = jnp.concatenate(
                [
                    high, low, high,
                    rows_of_two(jnp.broadcast_to(slope * mean_ref[pl.ds(i, 1), :], row.shape)),
                    rows_of_two(jnp.broadcast_to(slope, row.shape)),
                ],
                axis=0,
            )
            terms = f32_dot(left, right, TN)
            entries = pair_ref[i].astype(jnp.float32)
            out_ref[i] = (terms[:, :channels] - terms[:, channels:] * entries).astype(jnp.bfloat16)
        return carry

    lax.fori_loop(0, pair_ref.shape[0] // 8, rows, 0)


def call(kernel, outs, *args, scratch=(), place=None, flops=0, after=(), outside=0, late=0):
    whole, anywhere = pl.BlockSpec(memory_space=pltpu.VMEM), pl.BlockSpec(memory_space=pl.ANY)
    specs = [anywhere] * outside + [whole] * (len(args) - outside)
    ahead = () if place is None else (place,)
    shapes = [jax.ShapeDtypeStruct(*o) for o in outs]
    moved = sum(math.prod(a.shape) * a.dtype.itemsize for a in list(args) + shapes)
    first = len(ahead) + len(args)
    last = first + len(after)

    def wrapped(*refs):
        given, rest = list(refs[:first]), refs[last:]
        if outside:
            *rest, arrived = rest
            held = rest[len(rest) - outside :]
            rest = rest[: len(rest) - outside]
            copies = []
            for k in range(outside):
                copies.append(
                    pltpu.make_async_copy(given[len(ahead) + k], held[k], arrived.at[k])
                )
                given[len(ahead) + k] = held[k]
            for copy in copies:
                copy.start()
            for copy in copies[: outside - late]:
                copy.wait()
            if late:
                given.insert(0, lambda: [copy.wait() for copy in copies[outside - late :]])
        kernel(*given, *rest)

    held = [pltpu.VMEM(a.shape, a.dtype) for a in args[:outside]]
    if outside:
        held.append(pltpu.SemaphoreType.DMA((outside,)))
    return pl.pallas_call(
        wrapped,
        out_shape=shapes,
        in_specs=[pl.BlockSpec(memory_space=pltpu.SMEM)] * len(ahead)
        + specs
        + [anywhere] * len(after),
        out_specs=[whole] * len(shapes),
        scratch_shapes=[*scratch, *held],
        compiler_params=pltpu.CompilerParams(
            vmem_limit_bytes=ARGUMENT_VMEM_LIMIT if outside else VMEM_LIMIT
        ),
        cost_estimate=pl.CostEstimate(flops=flops, bytes_accessed=moved, transcendentals=0),
    )(*ahead, *args, *after)


def swapped(mine, axis_name, distance):
    size = lax.axis_size(axis_name)
    return lax.ppermute(mine, axis_name, [(a, a ^ distance) for a in range(size)])


def fits_heads(alignment_rows, pair_entries, pair_weight):
    channels, heads = pair_weight.shape
    return (
        lax.axis_size("seq") == 4
        and lax.axis_size("res") == heads == 8
        and alignment_rows.shape[0] == 2 * SLOTS
        and alignment_rows.shape[1] == pair_entries.shape[0] == 64
        and alignment_rows.shape[2] == 2 * LANES
        and pair_entries.shape[1] == channels == LANES
    )


def head_body(
    alignment_rows, pair_entries, combined_weight, output_weight, pair_weight, updated_gradient
):
    sequences, residues, width = alignment_rows.shape
    channels, heads = pair_weight.shape
    tokens = sequences * residues
    seq_size, res_size = lax.axis_size("seq"), lax.axis_size("res")
    seq_half = seq_size // 2
    total = residues * res_size
    group = 2 * res_size
    groups = [[g * group + k for k in range(group)] for g in range(seq_half)]
    scale = 1.0 / math.sqrt(width // heads * sequences * seq_size)
    res_index, seq_index = lax.axis_index("res"), lax.axis_index("seq")
    place = jnp.stack([res_index % 2, seq_index // 2]).astype(jnp.int32)
    bf16, f32 = jnp.bfloat16, jnp.float32

    def across(blocks):
        return lax.all_to_all(blocks, ("seq", "res"), 0, 0, axis_index_groups=groups, tiled=True)

    def all_quarters(mine):
        far = swapped(mine, "seq", seq_half)
        return mine, far, swapped(mine, "res", 1), swapped(far, "res", 1)

    x, grad, wc, wo = alignment_rows, updated_gradient, combined_weight, output_weight
    query_blocks, bias, mean, spread = call(
        functools.partial(query_kernel, scale),
        [
            ((group, 3 * residues, LANES), bf16),
            ((heads, residues, LANES), f32),
            ((residues, LANES), f32),
            ((residues, LANES), f32),
        ],
        x, wc, pair_entries, pair_weight.T,
        flops=8 * tokens * width * width, outside=3, late=1,
    )
    query_blocks = across(query_blocks)
    def scores(blocks, left_row, right_row, with_bias, kind):
        return call(
            functools.partial(score_kernel, residues, left_row, right_row, with_bias),
            [((total // 4, total), f32), ((total // 4, total), kind)],
            blocks, swapped(blocks, "res", 1),
            place=place, flops=2 * total * total * width,
        )

    logit_mine, logit_sent = scores(query_blocks, 0, residues, True, f32)
    logit_other = swapped(logit_sent, "seq", seq_half)
    (value_blocks,) = call(
        value_kernel, [((group, 2 * residues, LANES), bf16)], x, grad, wc, wo,
        flops=8 * tokens * width * width, outside=4, after=(logit_sent,),
    )
    value_blocks = across(value_blocks)

    quarter = (total // 4, total)
    softmax_out, probs = call(
        softmax_kernel, [(quarter, f32), (quarter, bf16)], logit_mine, logit_other,
        flops=total * total,
    )
    value_blocks, probs = lax.optimization_barrier((value_blocks, probs))
    def products(quarters, blocks, first_row, second_row, with_share, factor):
        rows = 2 * residues + (residues // 2 if with_share else 0)
        (out,) = call(
            functools.partial(
                product_kernel, residues, factor, first_row, second_row, with_share
            ),
            [((group, rows, LANES), bf16)],
            *quarters, blocks,
            scratch=[pltpu.VMEM((total, total), bf16)],
            place=place, flops=4 * total * total * width,
        )
        return out

    grad_mine, grad_sent = scores(value_blocks, residues, 0, False, bf16)
    grad_other = swapped(grad_sent, "seq", seq_half)
    attended = products(all_quarters(probs), value_blocks, 0, residues, False, 1.0)
    attended, grad_other = lax.optimization_barrier((attended, grad_other))
    attended_blocks = across(attended)
    (grad_logits,) = call(
        softmax_gradient_kernel, [(quarter, bf16)], softmax_out, grad_mine, grad_other,
        flops=total * total,
    )

    grad_blocks = across(
        products(all_quarters(grad_logits), query_blocks, residues, 0, True, scale)
    )

    share = pltpu.VMEM((heads, residues, LANES), f32)
    (pair_weight_part,) = call(
        pair_weight_kernel, [((heads, channels), f32)],
        grad_blocks, pair_entries, mean, spread,
        scratch=[share], flops=4 * tokens * width * width,
    )
    (pair_gradient,) = call(
        functools.partial(pair_kernel, 2 * residues),
        [(pair_entries.shape, bf16)],
        grad_blocks, pair_entries, pair_weight.T, bias, mean, spread,
        scratch=[share], flops=8 * tokens * width * width,
    )
    columns = 5 * width + channels
    rows = width // res_size
    part_rows = ((res_size // 2, rows, columns), bf16)
    updated, projected, keep, send = call(
        weight_kernel,
        [(x.shape, bf16), ((tokens, 4 * width), bf16), part_rows, part_rows],
        x, grad, wc, wo, attended_blocks, grad_blocks, pair_weight_part,
        scratch=[pltpu.VMEM((width, columns), bf16)],
        place=place, flops=24 * tokens * width * width, outside=4,
    )
    (alignment_gradient,) = call(
        alignment_kernel, [(x.shape, bf16)], x, wc, projected,
        flops=8 * tokens * width * width,
    )

    def added(mine, other):
        return (mine.astype(f32) + other.astype(f32)).astype(bf16)

    parts = added(keep, swapped(send, "res", 1))
    chips = [[2 * k + core for k in range(res_size // 2)] for core in range(2)]
    parts = lax.all_to_all(parts, "res", 0, 0, axis_index_groups=chips, tiled=True)
    part = jnp.sum(parts.astype(f32), axis=0).astype(bf16)
    part = added(part, swapped(part, "seq", 1))
    part = added(part, swapped(part, "seq", seq_half))
    whole = lax.all_gather(part, "res", axis=0)
    return (
        updated,
        alignment_gradient,
        pair_gradient,
        whole[:, :, : 4 * width].reshape(wc.shape).astype(f32),
        whole[:, :, 4 * width : 5 * width].reshape(wo.shape).astype(f32),
        whole[:, 0, 5 * width :].T.astype(f32),
    )


def body(alignment_rows, pair_entries, combined_weight, output_weight, pair_weight, updated_gradient):
    chosen = head_body if fits_heads(alignment_rows, pair_entries, pair_weight) else gathered_body
    return chosen(
        alignment_rows, pair_entries, combined_weight, output_weight, pair_weight, updated_gradient
    )


def solution(mesh):
    return jax.shard_map(
        body,
        mesh=mesh,
        in_specs=(
            P("seq", "res", None),
            P("res", "seq", None),
            P(),
            P(),
            P(),
            P("seq", "res", None),
        ),
        out_specs=(
            P("seq", "res", None),
            P("seq", "res", None),
            P("res", "seq", None),
            P(),
            P(),
            P(),
        ),
        check_vma=False,
    )
```

```python
import functools
import math

import jax
import jax.numpy as jnp
from jax import lax
from jax.experimental import pallas as pl
from jax.experimental.pallas import tpu as pltpu
from jax.sharding import PartitionSpec as P

eps_norm = 1e-05


def layer_normalize(values):
    values = values.astype(jnp.float32)
    center = values - jnp.mean(values, axis=-1, keepdims=True)
    broadcast_pair = lax.rsqrt(jnp.mean(center * center, axis=-1, keepdims=True) + eps_norm)
    return (center * broadcast_pair, broadcast_pair)


def layer_norm_backward(normalized_gradient, normalized_rows, broadcast_pair):
    mean_grad = jnp.mean(normalized_gradient, axis=-1, keepdims=True)
    mean_cross = jnp.mean(normalized_gradient * normalized_rows, axis=-1, keepdims=True)
    return broadcast_pair * (normalized_gradient - mean_grad - normalized_rows * mean_cross)


def split_heads(tensor, head_count):
    return tensor.reshape(
        tensor.shape[0], tensor.shape[1], head_count, tensor.shape[2] // head_count
    )


def merge_heads(tensor):
    return tensor.reshape(tensor.shape[0], tensor.shape[1], tensor.shape[2] * tensor.shape[3])


def gathered_body(
    alignment_rows, pair_entries, combined_weight, output_weight, pair_weight, updated_gradient
):
    sequence_count, residue_count, alignment_width = alignment_rows.shape
    head_count = pair_weight.shape[1]
    query_width = output_weight.shape[0]
    head_dim = query_width // head_count
    column_count = pair_entries.shape[1]
    token_count = sequence_count * residue_count
    score_scale = 1.0 / math.sqrt(head_dim * sequence_count * lax.axis_size("seq"))
    normalized_rows, broadcast_pair = layer_normalize(alignment_rows)
    normalized_rows_backward = normalized_rows.astype(jnp.bfloat16).reshape(
        token_count, alignment_width
    )
    projected = jnp.dot(
        normalized_rows_backward, combined_weight, preferred_element_type=jnp.float32
    ).reshape(sequence_count, residue_count, 4 * query_width)
    queries = (projected[..., :query_width] * score_scale).astype(jnp.bfloat16)
    key_rows = projected[..., query_width : 2 * query_width].astype(jnp.bfloat16)
    value_rows = projected[..., 2 * query_width : 3 * query_width].astype(jnp.bfloat16)
    gate_open = jax.nn.sigmoid(projected[..., 3 * query_width :])
    all_keys, all_values = (
        lax.all_gather(key_rows, "res", axis=1, tiled=True),
        lax.all_gather(value_rows, "res", axis=1, tiled=True),
    )
    query_heads = split_heads(queries, head_count)
    key_heads = split_heads(all_keys, head_count)
    value_heads = split_heads(all_values, head_count)
    score_terms = jnp.einsum(
        "sihd,sjhd->hij", query_heads, key_heads, preferred_element_type=jnp.float32
    )
    pair_normed, pair_spread = layer_normalize(pair_entries)
    pair_bias = jnp.einsum("ijc,ch->hij", pair_normed, pair_weight, precision=lax.Precision.HIGHEST)
    col_start = lax.axis_index("seq") * column_count
    own_block = lax.dynamic_slice_in_dim(score_terms, col_start, column_count, 2) + pair_bias
    logits = lax.psum(lax.dynamic_update_slice_in_dim(score_terms, own_block, col_start, 2), "seq")
    row_top = jnp.max(logits, axis=-1, keepdims=True)
    lifted = jnp.exp(logits - row_top)
    softmax_out = lifted / jnp.sum(lifted, axis=-1, keepdims=True)
    softmax_low = softmax_out.astype(jnp.bfloat16)
    attended = merge_heads(
        jnp.einsum("hij,sjhd->sihd", softmax_low, value_heads, preferred_element_type=jnp.float32)
    )
    gated_out = (gate_open * attended).astype(jnp.bfloat16)
    flattened_gated = gated_out.reshape(token_count, query_width)
    updated = (
        jnp.dot(flattened_gated, output_weight, preferred_element_type=jnp.float32)
        .astype(jnp.bfloat16)
        .reshape(sequence_count, residue_count, alignment_width)
    )
    flattened_gradient = updated_gradient.reshape(token_count, alignment_width)
    grad_gated = jnp.dot(
        flattened_gradient, output_weight.T, preferred_element_type=jnp.float32
    ).reshape(sequence_count, residue_count, query_width)
    out_local = jnp.dot(flattened_gated.T, flattened_gradient, preferred_element_type=jnp.float32)
    grad_attended = (grad_gated * gate_open).astype(jnp.bfloat16)
    grad_gate_logit = grad_gated * attended * gate_open * (1.0 - gate_open)
    attended_grad_heads = split_heads(grad_attended, head_count)
    grad_terms = jnp.einsum(
        "sihd,sjhd->hij", attended_grad_heads, value_heads, preferred_element_type=jnp.float32
    )
    grad_probs = lax.psum(grad_terms, "seq")
    row_dot = jnp.sum(softmax_out * grad_probs, axis=-1, keepdims=True)
    grad_logits = softmax_out * (grad_probs - row_dot)
    grad_logits_b = grad_logits.astype(jnp.bfloat16)
    logit_share = lax.dynamic_slice_in_dim(grad_logits, col_start, column_count, 2)
    grad_query_heads = (
        jnp.einsum("hij,sjhd->sihd", grad_logits_b, key_heads, preferred_element_type=jnp.float32)
        * score_scale
    )
    key_part = jnp.einsum(
        "hij,sihd->jshd", grad_logits_b, query_heads, preferred_element_type=jnp.float32
    )
    value_part = jnp.einsum(
        "hij,sihd->jshd", softmax_low, attended_grad_heads, preferred_element_type=jnp.float32
    )
    summed = lax.psum_scatter(
        jnp.concatenate([merge_heads(key_part), merge_heads(value_part)], axis=-1),
        "res",
        scatter_dimension=0,
        tiled=True,
    )
    key_value_grads = jnp.transpose(summed, (1, 0, 2))
    projected_gradient = jnp.concatenate(
        [merge_heads(grad_query_heads), key_value_grads, grad_gate_logit], axis=-1
    )
    projected_gradient = projected_gradient.astype(jnp.bfloat16).reshape(
        token_count, 4 * query_width
    )
    qkvg_local = jnp.dot(
        normalized_rows_backward.T, projected_gradient, preferred_element_type=jnp.float32
    )
    normalized_gradient = jnp.dot(
        projected_gradient, combined_weight.T, preferred_element_type=jnp.float32
    ).reshape(sequence_count, residue_count, alignment_width)
    alignment_gradient = layer_norm_backward(
        normalized_gradient, normalized_rows, broadcast_pair
    ).astype(jnp.bfloat16)
    pair_w_local = jnp.einsum(
        "ijc,hij->ch", pair_normed, logit_share, precision=lax.Precision.HIGHEST
    )
    grad_pair_normed = jnp.einsum(
        "hij,ch->ijc", logit_share, pair_weight, precision=lax.Precision.HIGHEST
    )
    pair_gradient = layer_norm_backward(grad_pair_normed, pair_normed, pair_spread).astype(
        jnp.bfloat16
    )
    combined_weight_gradient, output_weight_gradient, pair_weight_gradient = lax.psum(
        (qkvg_local, out_local, pair_w_local), ("seq", "res")
    )
    return (
        updated,
        alignment_gradient,
        pair_gradient,
        combined_weight_gradient,
        output_weight_gradient,
        pair_weight_gradient,
    )


VMEM_LIMIT = 20 * 1024 * 1024
ARGUMENT_VMEM_LIMIT = 56 * 1024 * 1024
LANES = 128
SLOTS = 4
NT = (((1,), (1,)), ((), ()))
TN = (((0,), (0,)), ((), ()))


def f32_dot(left, right, dims=None):
    if dims is None:
        return jnp.dot(left, right, preferred_element_type=jnp.float32)
    return lax.dot_general(left, right, dims, preferred_element_type=jnp.float32)


def two_terms(values):
    high = values.astype(jnp.bfloat16)
    return high, (values - high.astype(jnp.float32)).astype(jnp.bfloat16)


def slot_select(pieces):
    slot = lax.broadcasted_iota(jnp.int32, pieces[0].shape, 1) // (LANES // SLOTS)
    result = pieces[0]
    for k in range(1, SLOTS):
        result = jnp.where(slot == k, pieces[k], result)
    return result


def pack_heads(out_ref, row, tensor, residues):
    for core in range(2):
        for tile in range(tensor.shape[1] // LANES):
            rolled = []
            for s in range(SLOTS):
                start = (core * SLOTS + s) * residues
                piece = tensor[start : start + residues, tile * LANES : (tile + 1) * LANES]
                rolled.append(pltpu.roll(piece, s * LANES // SLOTS, 1) if s else piece)
            for j in range(SLOTS):
                block = slot_select([rolled[(k - j) % SLOTS] for k in range(SLOTS)])
                out_ref[(tile * SLOTS + j) * 2 + core, row : row + residues, :] = block.astype(
                    jnp.bfloat16
                )


def unpack_heads(in_ref, row, residues, tiles):
    rows = []
    for core in range(2):
        for s in range(SLOTS):
            pieces = []
            for tile in range(tiles):
                blocks = [
                    in_ref[
                        (tile * SLOTS + (k - s) % SLOTS) * 2 + core, row : row + residues, :
                    ].astype(jnp.float32)
                    for k in range(SLOTS)
                ]
                block = slot_select(blocks)
                pieces.append(pltpu.roll(block, LANES - s * LANES // SLOTS, 1) if s else block)
            rows.append(jnp.concatenate(pieces, axis=1))
    return jnp.concatenate(rows, axis=0)


def normalized(x_ref):
    width = x_ref.shape[-1]
    values = x_ref[...].reshape(-1, width).astype(jnp.float32)
    return layer_normalize(values)


def gate_of(logits):
    return 1.0 / (1.0 + jnp.exp(-logits))


def value_kernel(x_ref, grad_ref, wc_ref, wo_ref, out_ref):
    residues, width = x_ref.shape[1], x_ref.shape[2]
    normed = normalized(x_ref)[0].astype(jnp.bfloat16)
    values = f32_dot(normed, wc_ref[:, 2 * width : 3 * width])
    gate = gate_of(f32_dot(normed, wc_ref[:, 3 * width :]))
    grad_gated = f32_dot(grad_ref[...].reshape(-1, width), wo_ref[...], NT)
    pack_heads(out_ref, 0, values, residues)
    pack_heads(out_ref, residues, grad_gated * gate, residues)


def centred(weight):
    return weight - jnp.mean(weight, axis=1, keepdims=True)


def query_kernel(
    scale, arrive, x_ref, wc_ref, pair_ref, weight_ref, out_ref, bias_ref, mean_ref, spread_ref
):
    residues, width = x_ref.shape[1], x_ref.shape[2]
    heads = weight_ref.shape[0]
    normed = normalized(x_ref)[0].astype(jnp.bfloat16)
    pack_heads(out_ref, 0, f32_dot(normed, wc_ref[:, :width]) * scale, residues)
    pack_heads(out_ref, residues, f32_dot(normed, wc_ref[:, width : 2 * width]), residues)

    arrive()
    columns, channels = pair_ref.shape[1], pair_ref.shape[2]
    weight = centred(weight_ref[...])
    first = weight.astype(jnp.bfloat16)
    second, third = two_terms(weight - first.astype(jnp.float32))
    share = jnp.full((heads, channels), 1.0 / channels, jnp.bfloat16)
    left = jnp.concatenate([first, second, third, share], axis=0)
    average = jnp.full((channels, channels), 1.0 / channels, jnp.bfloat16)
    step_rows = 8

    def rows(step, carry):
        start = pl.multiple_of(step * step_rows, step_rows)
        entries = pair_ref[pl.ds(start, step_rows)].reshape(step_rows * columns, channels)
        center = entries.astype(jnp.float32) - f32_dot(entries, average)
        high, low = two_terms(center * center)
        variance = f32_dot(share, high, NT) + f32_dot(share, low, NT)
        spread = lax.rsqrt(variance + eps_norm)
        raw = f32_dot(left, entries, NT)
        bias = spread * (raw[:heads] + raw[heads : 2 * heads] + raw[2 * heads : 3 * heads])
        for k in range(step_rows):
            lanes = slice(k * columns, (k + 1) * columns)
            bias_ref[:, start + k, :] = bias[:, lanes]
            mean_ref[pl.ds(start + k, 1), :] = raw[3 * heads : 3 * heads + 1, lanes]
            spread_ref[pl.ds(start + k, 1), :] = spread[:1, lanes]
        return carry

    lax.fori_loop(0, pair_ref.shape[0] // step_rows, rows, 0)
    half = residues // 2
    for h in range(heads):
        for core in range(2):
            high, low = two_terms(bias_ref[h, core * half : (core + 1) * half, :])
            out_ref[h * 2 + core, 2 * residues : 2 * residues + half, :] = high
            out_ref[h * 2 + core, 2 * residues + half : 3 * residues, :] = low


def lanes_of(blocks_ref, row, residues):
    count = blocks_ref.shape[0] // 2
    planes = [
        blocks_ref[p * count : (p + 1) * count, row : row + residues, :].reshape(-1, LANES)
        for p in range(2)
    ]
    return jnp.concatenate(planes, axis=1)


def score_kernel(
    residues, left_row, right_row, with_bias, place_ref, own_ref, other_ref, mine_ref, sent_ref
):
    core, half = place_ref[0], place_ref[1]
    count = own_ref.shape[0] // 2
    part = residues // 2
    right = jnp.concatenate(
        [lanes_of(own_ref, right_row, residues), lanes_of(other_ref, right_row, residues)], axis=1
    )
    for which, ref in ((half, mine_ref), (1 - half, sent_ref)):
        left = []
        for k in range(count // 2):
            block = which * (count // 2) + k
            rows = pl.ds(pl.multiple_of(left_row + core * part, part), part)
            left.append(
                jnp.concatenate(
                    [
                        r[p * count + block, rows, :]
                        for r in (own_ref, other_ref)
                        for p in range(2)
                    ],
                    axis=1,
                )
            )
        ref[...] = f32_dot(jnp.concatenate(left, axis=0), right, NT).astype(ref.dtype)
        if with_bias:
            for p in range(2):
                columns = pl.ds(pl.multiple_of((half * 2 + p) * LANES, LANES), LANES)
                for k in range(count // 2):
                    block = p * count + which * (count // 2) + k
                    high = own_ref[block, 2 * residues : 2 * residues + part, :]
                    low = own_ref[block, 2 * residues + part : 3 * residues, :]
                    bias = high.astype(jnp.float32) + low.astype(jnp.float32)
                    ref[k * part : (k + 1) * part, columns] += bias


def softmax_kernel(logit_ref, other_ref, out_ref, low_ref):
    logits = logit_ref[...] + other_ref[...]
    lifted = jnp.exp(logits - jnp.max(logits, axis=-1, keepdims=True))
    softmax_out = lifted / jnp.sum(lifted, axis=-1, keepdims=True)
    out_ref[...] = softmax_out
    low_ref[...] = softmax_out.astype(jnp.bfloat16)


def softmax_gradient_kernel(softmax_ref, grad_ref, other_ref, out_ref):
    softmax_out = softmax_ref[...]
    grad_probs = grad_ref[...] + other_ref[...].astype(jnp.float32)
    row_dot = jnp.sum(softmax_out * grad_probs, axis=-1, keepdims=True)
    out_ref[...] = (softmax_out * (grad_probs - row_dot)).astype(jnp.bfloat16)


def product_kernel(
    residues, scale, first_row, second_row, with_share,
    place_ref, own_ref, far_ref, near_ref, corner_ref, blocks_ref, out_ref, whole_ref,
):
    core, half = place_ref[0], place_ref[1]
    count = blocks_ref.shape[0] // 2
    part = residues // 2
    quarters = (
        (own_ref, core, half), (far_ref, core, 1 - half),
        (near_ref, 1 - core, half), (corner_ref, 1 - core, 1 - half),
    )
    for ref, c, z in quarters:
        for k in range(count // 2):
            start = (z * (count // 2) + k) * residues + c * part
            whole_ref[pl.ds(pl.multiple_of(start, part), part), :] = ref[k * part : (k + 1) * part, :]
    whole = whole_ref[...]
    if with_share:
        for p in range(2):
            columns = pl.ds(pl.multiple_of((half * 2 + p) * LANES, LANES), LANES)
            for q in range(count):
                rows = pl.ds(pl.multiple_of(q * residues + core * part, part), part)
                out_ref[p * count + q, 2 * residues : 2 * residues + part, :] = whole_ref[rows, columns]
    first = f32_dot(whole, lanes_of(blocks_ref, first_row, residues)) * scale
    second = f32_dot(whole, lanes_of(blocks_ref, second_row, residues), TN)
    for row, product in ((0, first), (residues, second)):
        for p in range(2):
            out_ref[p * count : (p + 1) * count, row : row + residues, :] = (
                product[:, p * LANES : (p + 1) * LANES]
                .astype(jnp.bfloat16)
                .reshape(count, residues, LANES)
            )


def share_of(blocks_ref, row, part, heads):
    return jnp.concatenate(
        [
            blocks_ref[:, row : row + part, :]
            .astype(jnp.float32)
            .reshape(heads, 2 * part, LANES)
        ],
        axis=0,
    )


def attended_weight_kernel(
    x_ref, grad_ref, wc_ref, wo_ref, blocks_ref, updated_ref, projected_ref, normed_ref, sums_ref
):
    residues, width = x_ref.shape[1], x_ref.shape[2]
    tiles = width // LANES
    normed = normalized(x_ref)[0].astype(jnp.bfloat16)
    normed_ref[...] = normed
    gate = gate_of(f32_dot(normed, wc_ref[:, 3 * width :]))
    grad = grad_ref[...].reshape(-1, width)
    grad_gated = f32_dot(grad, wo_ref[...], NT)
    attended = unpack_heads(blocks_ref, 0, residues, tiles)
    gated = (gate * attended).astype(jnp.bfloat16)
    updated_ref[...] = f32_dot(gated, wo_ref[...]).astype(jnp.bfloat16).reshape(updated_ref.shape)
    projected_ref[:, :width] = unpack_heads(blocks_ref, residues, residues, tiles).astype(
        jnp.bfloat16
    )
    projected_ref[:, width:] = (grad_gated * attended * gate * (1.0 - gate)).astype(jnp.bfloat16)
    sums_ref[:, : 2 * width] = f32_dot(normed, projected_ref[...], TN).astype(jnp.bfloat16)
    sums_ref[:, 2 * width :] = f32_dot(gated, grad, TN).astype(jnp.bfloat16)


def query_weight_kernel(
    place_ref, normed_ref, blocks_ref, pair_weight_ref, attended_sums_ref,
    projected_ref, keep_ref, send_ref, sums_ref,
):
    width = normed_ref.shape[1]
    tiles, residues = width // LANES, (blocks_ref.shape[1] * 2) // 5
    core = place_ref[0]
    for t in range(2):
        projected_ref[:, t * width : (t + 1) * width] = unpack_heads(
            blocks_ref, t * residues, residues, tiles
        ).astype(jnp.bfloat16)
    sums_ref[:, : 2 * width] = f32_dot(normed_ref[...], projected_ref[...], TN).astype(
        jnp.bfloat16
    )
    sums_ref[:, 2 * width : 5 * width] = attended_sums_ref[...]
    heads, channels = pair_weight_ref.shape
    rows = sums_ref.shape[0] // heads
    first = lax.broadcasted_iota(jnp.int32, (rows, channels), 0) == 0
    for h in range(heads):
        row = jnp.broadcast_to(pair_weight_ref[h : h + 1], (rows, channels))
        sums_ref[h * rows : (h + 1) * rows, 5 * width :] = jnp.where(first, row, 0.0).astype(
            jnp.bfloat16
        )
    for which, ref in ((core, keep_ref), (1 - core, send_ref)):
        for block in range(heads // 2):
            start = pl.multiple_of((2 * block + which) * rows, rows)
            ref[block] = sums_ref[pl.ds(start, rows), :]


def core_sum_kernel(place_ref, keep_ref, other_ref, own_ref, *send_refs):
    chip = place_ref[2]
    for flip, ref in enumerate((own_ref, *send_refs)):
        block = jnp.bitwise_xor(chip, flip)
        total = keep_ref[block].astype(jnp.float32) + other_ref[block].astype(jnp.float32)
        ref[...] = total.astype(ref.dtype)


def plane_sum_kernel(own_ref, *refs):
    total = own_ref[...]
    for ref in refs[:-1]:
        total += ref[...].astype(jnp.float32)
    refs[-1][...] = total.astype(refs[-1].dtype)


def pair_weight_kernel(blocks_ref, pair_ref, mean_ref, spread_ref, out_ref, share_ref):
    heads, part = share_ref.shape[0], pair_ref.shape[0] // 2
    share_ref[...] = share_of(blocks_ref, blocks_ref.shape[1] - part, part, heads)

    def rows(step, carry):
        total, shift = carry
        for k in range(8):
            i = step * 8 + k
            scaled = share_ref[:, i, :] * spread_ref[pl.ds(i, 1), :]
            high, low = two_terms(scaled)
            total += f32_dot(jnp.concatenate([high, low], axis=0), pair_ref[i])
            shift += (high.astype(jnp.float32) + low.astype(jnp.float32)) * mean_ref[pl.ds(i, 1), :]
        return total, shift

    channels = pair_ref.shape[2]
    total, shift = lax.fori_loop(
        0,
        pair_ref.shape[0] // 8,
        rows,
        (jnp.zeros((2 * heads, channels), jnp.float32), jnp.zeros((heads, LANES), jnp.float32)),
    )
    out_ref[...] = total[:heads] + total[heads:] - jnp.sum(shift, axis=1, keepdims=True)


def alignment_kernel(x_ref, wc_ref, query_key_ref, value_gate_ref, out_ref):
    normed, spread = normalized(x_ref)
    width = x_ref.shape[2]
    gradient = f32_dot(query_key_ref[...], wc_ref[:, : 2 * width], NT) + f32_dot(
        value_gate_ref[...], wc_ref[:, 2 * width :], NT
    )
    out_ref[...] = (
        layer_norm_backward(gradient, normed, spread).astype(jnp.bfloat16).reshape(out_ref.shape)
    )


def pair_kernel(blocks_row, blocks_ref, pair_ref, weight_ref, bias_ref, mean_ref, spread_ref, out_ref, share_ref):
    heads, channels = weight_ref.shape
    part = pair_ref.shape[0] // 2
    share_ref[...] = share_of(blocks_ref, blocks_row, part, heads)
    first, second = two_terms(centred(weight_ref[...]))
    zero = jnp.zeros((heads, channels), jnp.bfloat16)
    top = lax.broadcasted_iota(jnp.int32, (heads, channels), 0) < 2
    ones = jnp.where(top, 1.0, 0.0).astype(jnp.bfloat16)
    right = jnp.concatenate(
        [
            jnp.concatenate([first, first, second, ones, zero], axis=0),
            jnp.concatenate([zero, zero, zero, zero, ones], axis=0),
        ],
        axis=1,
    )
    row = lax.broadcasted_iota(jnp.int32, (heads, LANES), 0)

    def rows_of_two(value):
        high, low = two_terms(value)
        high, low = high.astype(jnp.float32), low.astype(jnp.float32)
        return jnp.where(row == 0, high, jnp.where(row == 1, low, 0.0)).astype(jnp.bfloat16)

    def rows(step, carry):
        for k in range(8):
            i = step * 8 + k
            gradient = share_ref[:, i, :]
            spread = spread_ref[pl.ds(i, 1), :]
            cross = jnp.sum(gradient * bias_ref[:, i, :], axis=0, keepdims=True) / channels
            slope = spread * spread * cross
            high, low = two_terms(gradient * spread)
            left = jnp.concatenate(
                [
                    high, low, high,
                    rows_of_two(jnp.broadcast_to(slope * mean_ref[pl.ds(i, 1), :], row.shape)),
                    rows_of_two(jnp.broadcast_to(slope, row.shape)),
                ],
                axis=0,
            )
            terms = f32_dot(left, right, TN)
            entries = pair_ref[i].astype(jnp.float32)
            out_ref[i] = (terms[:, :channels] - terms[:, channels:] * entries).astype(jnp.bfloat16)
        return carry

    lax.fori_loop(0, pair_ref.shape[0] // 8, rows, 0)


def call(kernel, outs, *args, scratch=(), place=None, flops=0, after=(), outside=0, late=0):
    whole, anywhere = pl.BlockSpec(memory_space=pltpu.VMEM), pl.BlockSpec(memory_space=pl.ANY)
    specs = [anywhere] * outside + [whole] * (len(args) - outside)
    ahead = () if place is None else (place,)
    shapes = [jax.ShapeDtypeStruct(*o) for o in outs]
    moved = sum(math.prod(a.shape) * a.dtype.itemsize for a in list(args) + shapes)
    first = len(ahead) + len(args)
    last = first + len(after)

    def wrapped(*refs):
        given, rest = list(refs[:first]), refs[last:]
        if outside:
            *rest, arrived = rest
            held = rest[len(rest) - outside :]
            rest = rest[: len(rest) - outside]
            copies = []
            for k in range(outside):
                copies.append(
                    pltpu.make_async_copy(given[len(ahead) + k], held[k], arrived.at[k])
                )
                given[len(ahead) + k] = held[k]
            for copy in copies:
                copy.start()
            for copy in copies[: outside - late]:
                copy.wait()
            if late:
                given.insert(0, lambda: [copy.wait() for copy in copies[outside - late :]])
        kernel(*given, *rest)

    held = [pltpu.VMEM(a.shape, a.dtype) for a in args[:outside]]
    if outside:
        held.append(pltpu.SemaphoreType.DMA((outside,)))
    return pl.pallas_call(
        wrapped,
        out_shape=shapes,
        in_specs=[pl.BlockSpec(memory_space=pltpu.SMEM)] * len(ahead)
        + specs
        + [anywhere] * len(after),
        out_specs=[whole] * len(shapes),
        scratch_shapes=[*scratch, *held],
        compiler_params=pltpu.CompilerParams(
            vmem_limit_bytes=ARGUMENT_VMEM_LIMIT if outside else VMEM_LIMIT
        ),
        cost_estimate=pl.CostEstimate(flops=flops, bytes_accessed=moved, transcendentals=0),
    )(*ahead, *args, *after)


def swapped(mine, axis_name, distance):
    size = lax.axis_size(axis_name)
    return lax.ppermute(mine, axis_name, [(a, a ^ distance) for a in range(size)])


def fits_heads(alignment_rows, pair_entries, pair_weight):
    channels, heads = pair_weight.shape
    return (
        lax.axis_size("seq") == 4
        and lax.axis_size("res") == heads == 8
        and alignment_rows.shape[0] == 2 * SLOTS
        and alignment_rows.shape[1] == pair_entries.shape[0] == 64
        and alignment_rows.shape[2] == 2 * LANES
        and pair_entries.shape[1] == channels == LANES
    )


def head_body(
    alignment_rows, pair_entries, combined_weight, output_weight, pair_weight, updated_gradient
):
    sequences, residues, width = alignment_rows.shape
    channels, heads = pair_weight.shape
    tokens = sequences * residues
    seq_size, res_size = lax.axis_size("seq"), lax.axis_size("res")
    seq_half = seq_size // 2
    total = residues * res_size
    group = 2 * res_size
    groups = [[g * group + k for k in range(group)] for g in range(seq_half)]
    scale = 1.0 / math.sqrt(width // heads * sequences * seq_size)
    res_index, seq_index = lax.axis_index("res"), lax.axis_index("seq")
    place = jnp.stack([res_index % 2, seq_index // 2, res_index // 2]).astype(jnp.int32)
    bf16, f32 = jnp.bfloat16, jnp.float32

    def across(blocks):
        return lax.all_to_all(blocks, ("seq", "res"), 0, 0, axis_index_groups=groups, tiled=True)

    x, grad, wc, wo = alignment_rows, updated_gradient, combined_weight, output_weight
    query_blocks, bias, mean, spread = call(
        functools.partial(query_kernel, scale),
        [
            ((group, 3 * residues, LANES), bf16),
            ((heads, residues, LANES), f32),
            ((residues, LANES), f32),
            ((residues, LANES), f32),
        ],
        x, wc, pair_entries, pair_weight.T,
        flops=8 * tokens * width * width, outside=3, late=1,
    )
    query_blocks = across(query_blocks)
    def scores(blocks, left_row, right_row, with_bias, kind):
        return call(
            functools.partial(score_kernel, residues, left_row, right_row, with_bias),
            [((total // 4, total), f32), ((total // 4, total), kind)],
            blocks, swapped(blocks, "res", 1),
            place=place, flops=2 * total * total * width,
        )

    (value_blocks,) = call(
        value_kernel, [((group, 2 * residues, LANES), bf16)], x, grad, wc, wo,
        flops=8 * tokens * width * width, outside=4,
    )
    logit_mine, logit_sent = scores(query_blocks, 0, residues, True, f32)
    value_blocks, logit_sent = lax.optimization_barrier((value_blocks, logit_sent))
    logit_other = swapped(logit_sent, "seq", seq_half)
    value_blocks = across(value_blocks)
    quarter = (total // 4, total)
    softmax_out, probs = call(
        softmax_kernel, [(quarter, f32), (quarter, bf16)], logit_mine, logit_other,
        flops=total * total,
    )
    probs_far = swapped(probs, "seq", seq_half)
    value_blocks, probs_far = lax.optimization_barrier((value_blocks, probs_far))
    grad_mine, grad_sent = scores(value_blocks, residues, 0, False, bf16)
    grad_other = swapped(grad_sent, "seq", seq_half)

    def products(quarters, blocks, first_row, second_row, with_share, factor):
        rows = 2 * residues + (residues // 2 if with_share else 0)
        (out,) = call(
            functools.partial(
                product_kernel, residues, factor, first_row, second_row, with_share
            ),
            [((group, rows, LANES), bf16)],
            *quarters, blocks,
            scratch=[pltpu.VMEM((total, total), bf16)],
            place=place, flops=4 * total * total * width,
        )
        return out

    def with_near(mine, far):
        return mine, far, swapped(mine, "res", 1), swapped(far, "res", 1)

    attended = products(with_near(probs, probs_far), value_blocks, 0, residues, False, 1.0)
    attended, grad_other = lax.optimization_barrier((attended, grad_other))
    attended_blocks = across(attended)
    (grad_logits,) = call(
        softmax_gradient_kernel, [(quarter, bf16)], softmax_out, grad_mine, grad_other,
        flops=total * total,
    )
    grad_quarters = with_near(grad_logits, swapped(grad_logits, "seq", seq_half))
    grad_quarters, attended_blocks = lax.optimization_barrier((grad_quarters, attended_blocks))
    grad_blocks = across(products(grad_quarters, query_blocks, residues, 0, True, scale))

    updated, value_gate, normed, attended_sums = call(
        attended_weight_kernel,
        [
            (x.shape, bf16),
            ((tokens, 2 * width), bf16),
            ((tokens, width), bf16),
            ((width, 3 * width), bf16),
        ],
        x, grad, wc, wo, attended_blocks,
        flops=14 * tokens * width * width, outside=4,
    )
    share = pltpu.VMEM((heads, residues, LANES), f32)
    (pair_weight_part,) = call(
        pair_weight_kernel, [((heads, channels), f32)],
        grad_blocks, pair_entries, mean, spread,
        scratch=[share], flops=4 * tokens * width * width,
    )
    columns = 5 * width + channels
    rows = width // res_size
    part_rows = ((res_size // 2, rows, columns), bf16)
    query_key, keep, send = call(
        query_weight_kernel,
        [((tokens, 2 * width), bf16), part_rows, part_rows],
        normed, grad_blocks, pair_weight_part, attended_sums,
        scratch=[pltpu.VMEM((width, columns), bf16)],
        place=place, flops=4 * tokens * width * width,
    )
    own, *sent = call(
        core_sum_kernel,
        [((rows, columns), f32)] + [((rows, columns), bf16)] * 3,
        keep, swapped(send, "res", 1), place=place,
    )
    received = [swapped(t, "res", 2 * flip) for flip, t in enumerate(sent, 1)]
    (pair_gradient,) = call(
        functools.partial(pair_kernel, 2 * residues),
        [(pair_entries.shape, bf16)],
        grad_blocks, pair_entries, pair_weight.T, bias, mean, spread,
        scratch=[share], flops=8 * tokens * width * width,
    )
    received, pair_gradient = lax.optimization_barrier((received, pair_gradient))
    (part,) = call(plane_sum_kernel, [((rows, columns), bf16)], own, *received)
    (alignment_gradient,) = call(
        alignment_kernel, [(x.shape, bf16)], x, wc, query_key, value_gate,
        flops=8 * tokens * width * width,
    )

    def added(mine, other):
        return (mine.astype(f32) + other.astype(f32)).astype(bf16)

    part = added(part, swapped(part, "seq", 1))
    part = added(part, swapped(part, "seq", seq_half))
    whole = lax.all_gather(part, "res", axis=0)
    return (
        updated,
        alignment_gradient,
        pair_gradient,
        whole[:, :, : 4 * width].reshape(wc.shape).astype(f32),
        whole[:, :, 4 * width : 5 * width].reshape(wo.shape).astype(f32),
        whole[:, 0, 5 * width :].T.astype(f32),
    )


def body(alignment_rows, pair_entries, combined_weight, output_weight, pair_weight, updated_gradient):
    chosen = head_body if fits_heads(alignment_rows, pair_entries, pair_weight) else gathered_body
    return chosen(
        alignment_rows, pair_entries, combined_weight, output_weight, pair_weight, updated_gradient
    )


def solution(mesh):
    return jax.shard_map(
        body,
        mesh=mesh,
        in_specs=(
            P("seq", "res", None),
            P("res", "seq", None),
            P(),
            P(),
            P(),
            P("seq", "res", None),
        ),
        out_specs=(
            P("seq", "res", None),
            P("seq", "res", None),
            P("res", "seq", None),
            P(),
            P(),
            P(),
        ),
        check_vma=False,
    )
```

```python
import functools
import math

import jax
import jax.numpy as jnp
from jax import lax
from jax.experimental import pallas as pl
from jax.experimental.pallas import tpu as pltpu
from jax.sharding import PartitionSpec as P

eps_norm = 1e-05


def layer_normalize(values):
    values = values.astype(jnp.float32)
    center = values - jnp.mean(values, axis=-1, keepdims=True)
    broadcast_pair = lax.rsqrt(jnp.mean(center * center, axis=-1, keepdims=True) + eps_norm)
    return (center * broadcast_pair, broadcast_pair)


def layer_norm_backward(normalized_gradient, normalized_rows, broadcast_pair):
    mean_grad = jnp.mean(normalized_gradient, axis=-1, keepdims=True)
    mean_cross = jnp.mean(normalized_gradient * normalized_rows, axis=-1, keepdims=True)
    return broadcast_pair * (normalized_gradient - mean_grad - normalized_rows * mean_cross)


def split_heads(tensor, head_count):
    return tensor.reshape(
        tensor.shape[0], tensor.shape[1], head_count, tensor.shape[2] // head_count
    )


def merge_heads(tensor):
    return tensor.reshape(tensor.shape[0], tensor.shape[1], tensor.shape[2] * tensor.shape[3])


def gathered_body(
    alignment_rows, pair_entries, combined_weight, output_weight, pair_weight, updated_gradient
):
    sequence_count, residue_count, alignment_width = alignment_rows.shape
    head_count = pair_weight.shape[1]
    query_width = output_weight.shape[0]
    head_dim = query_width // head_count
    column_count = pair_entries.shape[1]
    token_count = sequence_count * residue_count
    score_scale = 1.0 / math.sqrt(head_dim * sequence_count * lax.axis_size("seq"))
    normalized_rows, broadcast_pair = layer_normalize(alignment_rows)
    normalized_rows_backward = normalized_rows.astype(jnp.bfloat16).reshape(
        token_count, alignment_width
    )
    projected = jnp.dot(
        normalized_rows_backward, combined_weight, preferred_element_type=jnp.float32
    ).reshape(sequence_count, residue_count, 4 * query_width)
    queries = (projected[..., :query_width] * score_scale).astype(jnp.bfloat16)
    key_rows = projected[..., query_width : 2 * query_width].astype(jnp.bfloat16)
    value_rows = projected[..., 2 * query_width : 3 * query_width].astype(jnp.bfloat16)
    gate_open = jax.nn.sigmoid(projected[..., 3 * query_width :])
    all_keys, all_values = (
        lax.all_gather(key_rows, "res", axis=1, tiled=True),
        lax.all_gather(value_rows, "res", axis=1, tiled=True),
    )
    query_heads = split_heads(queries, head_count)
    key_heads = split_heads(all_keys, head_count)
    value_heads = split_heads(all_values, head_count)
    score_terms = jnp.einsum(
        "sihd,sjhd->hij", query_heads, key_heads, preferred_element_type=jnp.float32
    )
    pair_normed, pair_spread = layer_normalize(pair_entries)
    pair_bias = jnp.einsum("ijc,ch->hij", pair_normed, pair_weight, precision=lax.Precision.HIGHEST)
    col_start = lax.axis_index("seq") * column_count
    own_block = lax.dynamic_slice_in_dim(score_terms, col_start, column_count, 2) + pair_bias
    logits = lax.psum(lax.dynamic_update_slice_in_dim(score_terms, own_block, col_start, 2), "seq")
    row_top = jnp.max(logits, axis=-1, keepdims=True)
    lifted = jnp.exp(logits - row_top)
    softmax_out = lifted / jnp.sum(lifted, axis=-1, keepdims=True)
    softmax_low = softmax_out.astype(jnp.bfloat16)
    attended = merge_heads(
        jnp.einsum("hij,sjhd->sihd", softmax_low, value_heads, preferred_element_type=jnp.float32)
    )
    gated_out = (gate_open * attended).astype(jnp.bfloat16)
    flattened_gated = gated_out.reshape(token_count, query_width)
    updated = (
        jnp.dot(flattened_gated, output_weight, preferred_element_type=jnp.float32)
        .astype(jnp.bfloat16)
        .reshape(sequence_count, residue_count, alignment_width)
    )
    flattened_gradient = updated_gradient.reshape(token_count, alignment_width)
    grad_gated = jnp.dot(
        flattened_gradient, output_weight.T, preferred_element_type=jnp.float32
    ).reshape(sequence_count, residue_count, query_width)
    out_local = jnp.dot(flattened_gated.T, flattened_gradient, preferred_element_type=jnp.float32)
    grad_attended = (grad_gated * gate_open).astype(jnp.bfloat16)
    grad_gate_logit = grad_gated * attended * gate_open * (1.0 - gate_open)
    attended_grad_heads = split_heads(grad_attended, head_count)
    grad_terms = jnp.einsum(
        "sihd,sjhd->hij", attended_grad_heads, value_heads, preferred_element_type=jnp.float32
    )
    grad_probs = lax.psum(grad_terms, "seq")
    row_dot = jnp.sum(softmax_out * grad_probs, axis=-1, keepdims=True)
    grad_logits = softmax_out * (grad_probs - row_dot)
    grad_logits_b = grad_logits.astype(jnp.bfloat16)
    logit_share = lax.dynamic_slice_in_dim(grad_logits, col_start, column_count, 2)
    grad_query_heads = (
        jnp.einsum("hij,sjhd->sihd", grad_logits_b, key_heads, preferred_element_type=jnp.float32)
        * score_scale
    )
    key_part = jnp.einsum(
        "hij,sihd->jshd", grad_logits_b, query_heads, preferred_element_type=jnp.float32
    )
    value_part = jnp.einsum(
        "hij,sihd->jshd", softmax_low, attended_grad_heads, preferred_element_type=jnp.float32
    )
    summed = lax.psum_scatter(
        jnp.concatenate([merge_heads(key_part), merge_heads(value_part)], axis=-1),
        "res",
        scatter_dimension=0,
        tiled=True,
    )
    key_value_grads = jnp.transpose(summed, (1, 0, 2))
    projected_gradient = jnp.concatenate(
        [merge_heads(grad_query_heads), key_value_grads, grad_gate_logit], axis=-1
    )
    projected_gradient = projected_gradient.astype(jnp.bfloat16).reshape(
        token_count, 4 * query_width
    )
    qkvg_local = jnp.dot(
        normalized_rows_backward.T, projected_gradient, preferred_element_type=jnp.float32
    )
    normalized_gradient = jnp.dot(
        projected_gradient, combined_weight.T, preferred_element_type=jnp.float32
    ).reshape(sequence_count, residue_count, alignment_width)
    alignment_gradient = layer_norm_backward(
        normalized_gradient, normalized_rows, broadcast_pair
    ).astype(jnp.bfloat16)
    pair_w_local = jnp.einsum(
        "ijc,hij->ch", pair_normed, logit_share, precision=lax.Precision.HIGHEST
    )
    grad_pair_normed = jnp.einsum(
        "hij,ch->ijc", logit_share, pair_weight, precision=lax.Precision.HIGHEST
    )
    pair_gradient = layer_norm_backward(grad_pair_normed, pair_normed, pair_spread).astype(
        jnp.bfloat16
    )
    combined_weight_gradient, output_weight_gradient, pair_weight_gradient = lax.psum(
        (qkvg_local, out_local, pair_w_local), ("seq", "res")
    )
    return (
        updated,
        alignment_gradient,
        pair_gradient,
        combined_weight_gradient,
        output_weight_gradient,
        pair_weight_gradient,
    )


VMEM_LIMIT = 20 * 1024 * 1024
ARGUMENT_VMEM_LIMIT = 56 * 1024 * 1024
LANES = 128
SLOTS = 4
NT = (((1,), (1,)), ((), ()))
TN = (((0,), (0,)), ((), ()))


def f32_dot(left, right, dims=None):
    if dims is None:
        return jnp.dot(left, right, preferred_element_type=jnp.float32)
    return lax.dot_general(left, right, dims, preferred_element_type=jnp.float32)


def two_terms(values):
    high = values.astype(jnp.bfloat16)
    return high, (values - high.astype(jnp.float32)).astype(jnp.bfloat16)


def slot_select(pieces):
    slot = lax.broadcasted_iota(jnp.int32, pieces[0].shape, 1) // (LANES // SLOTS)
    result = pieces[0]
    for k in range(1, SLOTS):
        result = jnp.where(slot == k, pieces[k], result)
    return result


def pack_heads(out_ref, row, tensor, residues):
    for core in range(2):
        for tile in range(tensor.shape[1] // LANES):
            rolled = []
            for s in range(SLOTS):
                start = (core * SLOTS + s) * residues
                piece = tensor[start : start + residues, tile * LANES : (tile + 1) * LANES]
                rolled.append(pltpu.roll(piece, s * LANES // SLOTS, 1) if s else piece)
            for j in range(SLOTS):
                block = slot_select([rolled[(k - j) % SLOTS] for k in range(SLOTS)])
                out_ref[(tile * SLOTS + j) * 2 + core, row : row + residues, :] = block.astype(
                    jnp.bfloat16
                )


def unpack_heads(in_ref, row, residues, tiles):
    rows = []
    for core in range(2):
        for s in range(SLOTS):
            pieces = []
            for tile in range(tiles):
                blocks = [
                    in_ref[
                        (tile * SLOTS + (k - s) % SLOTS) * 2 + core, row : row + residues, :
                    ].astype(jnp.float32)
                    for k in range(SLOTS)
                ]
                block = slot_select(blocks)
                pieces.append(pltpu.roll(block, LANES - s * LANES // SLOTS, 1) if s else block)
            rows.append(jnp.concatenate(pieces, axis=1))
    return jnp.concatenate(rows, axis=0)


def normalized(x_ref):
    width = x_ref.shape[-1]
    values = x_ref[...].reshape(-1, width).astype(jnp.float32)
    return layer_normalize(values)


def gate_of(logits):
    return 1.0 / (1.0 + jnp.exp(-logits))


def value_kernel(x_ref, grad_ref, wc_ref, wo_ref, out_ref):
    residues, width = x_ref.shape[1], x_ref.shape[2]
    normed = normalized(x_ref)[0].astype(jnp.bfloat16)
    values = f32_dot(normed, wc_ref[:, 2 * width : 3 * width])
    gate = gate_of(f32_dot(normed, wc_ref[:, 3 * width :]))
    grad_gated = f32_dot(grad_ref[...].reshape(-1, width), wo_ref[...], NT)
    pack_heads(out_ref, 0, values, residues)
    pack_heads(out_ref, residues, grad_gated * gate, residues)


def centred(weight):
    return weight - jnp.mean(weight, axis=1, keepdims=True)


def query_kernel(scale, x_ref, wc_ref, out_ref):
    residues, width = x_ref.shape[1], x_ref.shape[2]
    normed = normalized(x_ref)[0].astype(jnp.bfloat16)
    pack_heads(out_ref, 0, f32_dot(normed, wc_ref[:, :width]) * scale, residues)
    pack_heads(out_ref, residues, f32_dot(normed, wc_ref[:, width : 2 * width]), residues)


def bias_kernel(pair_ref, weight_ref, out_ref, bias_ref, mean_ref, spread_ref):
    heads = weight_ref.shape[0]
    residues, columns, channels = pair_ref.shape
    weight = centred(weight_ref[...])
    first = weight.astype(jnp.bfloat16)
    second, third = two_terms(weight - first.astype(jnp.float32))
    share = jnp.full((heads, channels), 1.0 / channels, jnp.bfloat16)
    left = jnp.concatenate([first, second, third, share], axis=0)
    shares = jnp.concatenate([share, share], axis=1)
    row = lax.broadcasted_iota(jnp.int32, (channels, channels), 0)
    column = lax.broadcasted_iota(jnp.int32, (channels, channels), 1)
    less_mean = (jnp.where(row == column, 1.0, 0.0) - 1.0 / channels).astype(jnp.bfloat16)
    step_rows = 8

    def rows(step, carry):
        start = pl.multiple_of(step * step_rows, step_rows)
        entries = pair_ref[pl.ds(start, step_rows)].reshape(step_rows * columns, channels)
        center = f32_dot(entries, less_mean)
        variance = f32_dot(shares, jnp.concatenate(two_terms(center * center), axis=1), NT)
        spread = lax.rsqrt(variance + eps_norm)
        raw = f32_dot(left, entries, NT)
        bias = spread * (raw[:heads] + raw[heads : 2 * heads] + raw[2 * heads : 3 * heads])
        for k in range(step_rows):
            lanes = slice(k * columns, (k + 1) * columns)
            bias_ref[:, start + k, :] = bias[:, lanes]
            mean_ref[pl.ds(start + k, 1), :] = raw[3 * heads : 3 * heads + 1, lanes]
            spread_ref[pl.ds(start + k, 1), :] = spread[:1, lanes]
        return carry

    lax.fori_loop(0, residues // step_rows, rows, 0)
    half = residues // 2
    for h in range(heads):
        for core in range(2):
            high, low = two_terms(bias_ref[h, core * half : (core + 1) * half, :])
            out_ref[h * 2 + core, :half, :] = high
            out_ref[h * 2 + core, half:, :] = low


def lanes_of(blocks_ref, row, residues):
    count = blocks_ref.shape[0] // 2
    planes = [
        blocks_ref[p * count : (p + 1) * count, row : row + residues, :].reshape(-1, LANES)
        for p in range(2)
    ]
    return jnp.concatenate(planes, axis=1)


def score_kernel(
    residues, left_row, right_row, place_ref, own_ref, other_ref, mine_ref, sent_ref
):
    core, half = place_ref[0], place_ref[1]
    count = own_ref.shape[0] // 2
    part = residues // 2
    right = jnp.concatenate(
        [lanes_of(own_ref, right_row, residues), lanes_of(other_ref, right_row, residues)], axis=1
    )
    for which, ref in ((half, mine_ref), (1 - half, sent_ref)):
        left = []
        for k in range(count // 2):
            block = which * (count // 2) + k
            rows = pl.ds(pl.multiple_of(left_row + core * part, part), part)
            left.append(
                jnp.concatenate(
                    [
                        r[p * count + block, rows, :]
                        for r in (own_ref, other_ref)
                        for p in range(2)
                    ],
                    axis=1,
                )
            )
        ref[...] = f32_dot(jnp.concatenate(left, axis=0), right, NT).astype(ref.dtype)


def add_bias(place_ref, blocks_ref, which, ref):
    half = place_ref[1]
    count, part = blocks_ref.shape[0] // 2, blocks_ref.shape[1] // 2
    for p in range(2):
        columns = pl.ds(pl.multiple_of((half * 2 + p) * LANES, LANES), LANES)
        for k in range(count // 2):
            block = p * count + which * (count // 2) + k
            bias = blocks_ref[block, :part, :].astype(jnp.float32) + blocks_ref[
                block, part:, :
            ].astype(jnp.float32)
            ref[k * part : (k + 1) * part, columns] += bias


def sent_bias_kernel(place_ref, blocks_ref, sent_ref, out_ref):
    out_ref[...] = sent_ref[...]
    add_bias(place_ref, blocks_ref, 1 - place_ref[1], out_ref)


def softmax_kernel(place_ref, blocks_ref, logit_ref, other_ref, out_ref, low_ref):
    out_ref[...] = logit_ref[...] + other_ref[...]
    add_bias(place_ref, blocks_ref, place_ref[1], out_ref)
    logits = out_ref[...]
    lifted = jnp.exp(logits - jnp.max(logits, axis=-1, keepdims=True))
    softmax_out = lifted / jnp.sum(lifted, axis=-1, keepdims=True)
    out_ref[...] = softmax_out
    low_ref[...] = softmax_out.astype(jnp.bfloat16)


def softmax_gradient_kernel(softmax_ref, grad_ref, other_ref, out_ref):
    softmax_out = softmax_ref[...]
    grad_probs = grad_ref[...] + other_ref[...].astype(jnp.float32)
    row_dot = jnp.sum(softmax_out * grad_probs, axis=-1, keepdims=True)
    out_ref[...] = (softmax_out * (grad_probs - row_dot)).astype(jnp.bfloat16)


def product_kernel(
    residues, scale, first_row, second_row, with_share,
    place_ref, own_ref, far_ref, near_ref, corner_ref, blocks_ref, out_ref, whole_ref,
):
    core, half = place_ref[0], place_ref[1]
    count = blocks_ref.shape[0] // 2
    part = residues // 2
    quarters = (
        (own_ref, core, half), (far_ref, core, 1 - half),
        (near_ref, 1 - core, half), (corner_ref, 1 - core, 1 - half),
    )
    for ref, c, z in quarters:
        for k in range(count // 2):
            start = (z * (count // 2) + k) * residues + c * part
            whole_ref[pl.ds(pl.multiple_of(start, part), part), :] = ref[k * part : (k + 1) * part, :]
    whole = whole_ref[...]
    if with_share:
        for p in range(2):
            columns = pl.ds(pl.multiple_of((half * 2 + p) * LANES, LANES), LANES)
            for q in range(count):
                rows = pl.ds(pl.multiple_of(q * residues + core * part, part), part)
                out_ref[p * count + q, 2 * residues : 2 * residues + part, :] = whole_ref[rows, columns]
    first = f32_dot(whole, lanes_of(blocks_ref, first_row, residues)) * scale
    second = f32_dot(whole, lanes_of(blocks_ref, second_row, residues), TN)
    for row, product in ((0, first), (residues, second)):
        for p in range(2):
            out_ref[p * count : (p + 1) * count, row : row + residues, :] = (
                product[:, p * LANES : (p + 1) * LANES]
                .astype(jnp.bfloat16)
                .reshape(count, residues, LANES)
            )


def share_of(blocks_ref, row, part, heads):
    return jnp.concatenate(
        [
            blocks_ref[:, row : row + part, :]
            .astype(jnp.float32)
            .reshape(heads, 2 * part, LANES)
        ],
        axis=0,
    )


def attended_weight_kernel(
    x_ref, grad_ref, wc_ref, wo_ref, blocks_ref, updated_ref, projected_ref, normed_ref, sums_ref
):
    residues, width = x_ref.shape[1], x_ref.shape[2]
    tiles = width // LANES
    normed = normalized(x_ref)[0].astype(jnp.bfloat16)
    normed_ref[...] = normed
    gate = gate_of(f32_dot(normed, wc_ref[:, 3 * width :]))
    grad = grad_ref[...].reshape(-1, width)
    grad_gated = f32_dot(grad, wo_ref[...], NT)
    attended = unpack_heads(blocks_ref, 0, residues, tiles)
    gated = (gate * attended).astype(jnp.bfloat16)
    updated_ref[...] = f32_dot(gated, wo_ref[...]).astype(jnp.bfloat16).reshape(updated_ref.shape)
    projected_ref[:, :width] = unpack_heads(blocks_ref, residues, residues, tiles).astype(
        jnp.bfloat16
    )
    projected_ref[:, width:] = (grad_gated * attended * gate * (1.0 - gate)).astype(jnp.bfloat16)
    sums_ref[:, : 2 * width] = f32_dot(normed, projected_ref[...], TN).astype(jnp.bfloat16)
    sums_ref[:, 2 * width :] = f32_dot(gated, grad, TN).astype(jnp.bfloat16)


def query_weight_kernel(
    place_ref, normed_ref, blocks_ref, pair_weight_ref, attended_sums_ref,
    projected_ref, keep_ref, send_ref, sums_ref,
):
    width = normed_ref.shape[1]
    tiles, residues = width // LANES, (blocks_ref.shape[1] * 2) // 5
    core = place_ref[0]
    for t in range(2):
        projected_ref[:, t * width : (t + 1) * width] = unpack_heads(
            blocks_ref, t * residues, residues, tiles
        ).astype(jnp.bfloat16)
    sums_ref[:, : 2 * width] = f32_dot(normed_ref[...], projected_ref[...], TN).astype(
        jnp.bfloat16
    )
    sums_ref[:, 2 * width : 5 * width] = attended_sums_ref[...]
    heads, channels = pair_weight_ref.shape
    rows = sums_ref.shape[0] // heads
    first = lax.broadcasted_iota(jnp.int32, (rows, channels), 0) == 0
    for h in range(heads):
        row = jnp.broadcast_to(pair_weight_ref[h : h + 1], (rows, channels))
        sums_ref[h * rows : (h + 1) * rows, 5 * width :] = jnp.where(first, row, 0.0).astype(
            jnp.bfloat16
        )
    for which, ref in ((core, keep_ref), (1 - core, send_ref)):
        for block in range(heads // 2):
            start = pl.multiple_of((2 * block + which) * rows, rows)
            ref[block] = sums_ref[pl.ds(start, rows), :]


def core_sum_kernel(place_ref, keep_ref, other_ref, own_ref, *send_refs):
    chip = place_ref[2]
    for flip, ref in enumerate((own_ref, *send_refs)):
        block = jnp.bitwise_xor(chip, flip)
        total = keep_ref[block].astype(jnp.float32) + other_ref[block].astype(jnp.float32)
        ref[...] = total.astype(ref.dtype)


def plane_sum_kernel(own_ref, *refs):
    total = own_ref[...]
    for ref in refs[:-1]:
        total += ref[...].astype(jnp.float32)
    refs[-1][...] = total.astype(refs[-1].dtype)


def pair_weight_kernel(blocks_ref, pair_ref, mean_ref, spread_ref, out_ref, share_ref):
    heads, part = share_ref.shape[0], pair_ref.shape[0] // 2
    share_ref[...] = share_of(blocks_ref, blocks_ref.shape[1] - part, part, heads)

    def rows(step, carry):
        total, shift = carry
        for k in range(8):
            i = step * 8 + k
            scaled = share_ref[:, i, :] * spread_ref[pl.ds(i, 1), :]
            high, low = two_terms(scaled)
            total += f32_dot(jnp.concatenate([high, low], axis=0), pair_ref[i])
            shift += (high.astype(jnp.float32) + low.astype(jnp.float32)) * mean_ref[pl.ds(i, 1), :]
        return total, shift

    channels = pair_ref.shape[2]
    total, shift = lax.fori_loop(
        0,
        pair_ref.shape[0] // 8,
        rows,
        (jnp.zeros((2 * heads, channels), jnp.float32), jnp.zeros((heads, LANES), jnp.float32)),
    )
    out_ref[...] = total[:heads] + total[heads:] - jnp.sum(shift, axis=1, keepdims=True)


def alignment_kernel(x_ref, wc_ref, query_key_ref, value_gate_ref, out_ref):
    normed, spread = normalized(x_ref)
    width = x_ref.shape[2]
    gradient = f32_dot(query_key_ref[...], wc_ref[:, : 2 * width], NT) + f32_dot(
        value_gate_ref[...], wc_ref[:, 2 * width :], NT
    )
    out_ref[...] = (
        layer_norm_backward(gradient, normed, spread).astype(jnp.bfloat16).reshape(out_ref.shape)
    )


def pair_kernel(blocks_row, blocks_ref, pair_ref, weight_ref, bias_ref, mean_ref, spread_ref, out_ref, share_ref):
    heads, channels = weight_ref.shape
    part = pair_ref.shape[0] // 2
    share_ref[...] = share_of(blocks_ref, blocks_row, part, heads)
    first, second = two_terms(centred(weight_ref[...]))
    zero = jnp.zeros((heads, channels), jnp.bfloat16)
    top = lax.broadcasted_iota(jnp.int32, (heads, channels), 0) < 2
    ones = jnp.where(top, 1.0, 0.0).astype(jnp.bfloat16)
    right = jnp.concatenate(
        [
            jnp.concatenate([first, first, second, ones, zero], axis=0),
            jnp.concatenate([zero, zero, zero, zero, ones], axis=0),
        ],
        axis=1,
    )
    row = lax.broadcasted_iota(jnp.int32, (heads, LANES), 0)

    def rows_of_two(value):
        high, low = two_terms(value)
        high, low = high.astype(jnp.float32), low.astype(jnp.float32)
        return jnp.where(row == 0, high, jnp.where(row == 1, low, 0.0)).astype(jnp.bfloat16)

    def rows(step, carry):
        for k in range(8):
            i = step * 8 + k
            gradient = share_ref[:, i, :]
            spread = spread_ref[pl.ds(i, 1), :]
            cross = jnp.sum(gradient * bias_ref[:, i, :], axis=0, keepdims=True) / channels
            slope = spread * spread * cross
            high, low = two_terms(gradient * spread)
            left = jnp.concatenate(
                [
                    high, low, high,
                    rows_of_two(jnp.broadcast_to(slope * mean_ref[pl.ds(i, 1), :], row.shape)),
                    rows_of_two(jnp.broadcast_to(slope, row.shape)),
                ],
                axis=0,
            )
            terms = f32_dot(left, right, TN)
            entries = pair_ref[i].astype(jnp.float32)
            out_ref[i] = (terms[:, :channels] - terms[:, channels:] * entries).astype(jnp.bfloat16)
        return carry

    lax.fori_loop(0, pair_ref.shape[0] // 8, rows, 0)


def call(kernel, outs, *args, scratch=(), place=None, flops=0, after=(), outside=0):
    whole, anywhere = pl.BlockSpec(memory_space=pltpu.VMEM), pl.BlockSpec(memory_space=pl.ANY)
    specs = [anywhere] * outside + [whole] * (len(args) - outside)
    ahead = () if place is None else (place,)
    shapes = [jax.ShapeDtypeStruct(*o) for o in outs]
    moved = sum(math.prod(a.shape) * a.dtype.itemsize for a in list(args) + shapes)
    first = len(ahead) + len(args)
    last = first + len(after)

    def wrapped(*refs):
        given, rest = list(refs[:first]), refs[last:]
        if outside:
            *rest, arrived = rest
            held = rest[len(rest) - outside :]
            rest = rest[: len(rest) - outside]
            copies = []
            for k in range(outside):
                copies.append(
                    pltpu.make_async_copy(given[len(ahead) + k], held[k], arrived.at[k])
                )
                given[len(ahead) + k] = held[k]
            for copy in copies:
                copy.start()
            for copy in copies:
                copy.wait()
        kernel(*given, *rest)

    held = [pltpu.VMEM(a.shape, a.dtype) for a in args[:outside]]
    if outside:
        held.append(pltpu.SemaphoreType.DMA((outside,)))
    return pl.pallas_call(
        wrapped,
        out_shape=shapes,
        in_specs=[pl.BlockSpec(memory_space=pltpu.SMEM)] * len(ahead)
        + specs
        + [anywhere] * len(after),
        out_specs=[whole] * len(shapes),
        scratch_shapes=[*scratch, *held],
        compiler_params=pltpu.CompilerParams(
            vmem_limit_bytes=ARGUMENT_VMEM_LIMIT if outside else VMEM_LIMIT
        ),
        cost_estimate=pl.CostEstimate(flops=flops, bytes_accessed=moved, transcendentals=0),
    )(*ahead, *args, *after)


def swapped(mine, axis_name, distance):
    size = lax.axis_size(axis_name)
    return lax.ppermute(mine, axis_name, [(a, a ^ distance) for a in range(size)])


def fits_heads(alignment_rows, pair_entries, pair_weight):
    channels, heads = pair_weight.shape
    return (
        lax.axis_size("seq") == 4
        and lax.axis_size("res") == heads == 8
        and alignment_rows.shape[0] == 2 * SLOTS
        and alignment_rows.shape[1] == pair_entries.shape[0] == 64
        and alignment_rows.shape[2] == 2 * LANES
        and pair_entries.shape[1] == channels == LANES
    )


def head_body(
    alignment_rows, pair_entries, combined_weight, output_weight, pair_weight, updated_gradient
):
    sequences, residues, width = alignment_rows.shape
    channels, heads = pair_weight.shape
    tokens = sequences * residues
    seq_size, res_size = lax.axis_size("seq"), lax.axis_size("res")
    seq_half = seq_size // 2
    total = residues * res_size
    group = 2 * res_size
    groups = [[g * group + k for k in range(group)] for g in range(seq_half)]
    scale = 1.0 / math.sqrt(width // heads * sequences * seq_size)
    res_index, seq_index = lax.axis_index("res"), lax.axis_index("seq")
    place = jnp.stack([res_index % 2, seq_index // 2, res_index // 2]).astype(jnp.int32)
    bf16, f32 = jnp.bfloat16, jnp.float32

    def across(blocks):
        return lax.all_to_all(blocks, ("seq", "res"), 0, 0, axis_index_groups=groups, tiled=True)

    x, grad, wc, wo = alignment_rows, updated_gradient, combined_weight, output_weight
    (query_blocks,) = call(
        functools.partial(query_kernel, scale), [((group, 2 * residues, LANES), bf16)], x, wc,
        flops=8 * tokens * width * width, outside=2,
    )
    query_blocks = across(query_blocks)
    bias_blocks, bias, mean, spread = call(
        bias_kernel,
        [
            ((group, residues, LANES), bf16),
            ((heads, residues, LANES), f32),
            ((residues, LANES), f32),
            ((residues, LANES), f32),
        ],
        pair_entries, pair_weight.T,
        flops=8 * tokens * width * width, outside=1,
    )
    (value_blocks,) = call(
        value_kernel, [((group, 2 * residues, LANES), bf16)], x, grad, wc, wo,
        flops=8 * tokens * width * width, outside=4,
    )
    query_blocks, bias_blocks, value_blocks = lax.optimization_barrier(
        (query_blocks, bias_blocks, value_blocks)
    )
    bias_blocks = across(bias_blocks)

    def scores(blocks, left_row, right_row, kind):
        return call(
            functools.partial(score_kernel, residues, left_row, right_row),
            [((total // 4, total), f32), ((total // 4, total), kind)],
            blocks, swapped(blocks, "res", 1),
            place=place, flops=2 * total * total * width,
        )

    logit_mine, logit_sent = scores(query_blocks, 0, residues, f32)
    logit_sent, bias_blocks = lax.optimization_barrier((logit_sent, bias_blocks))
    quarter = (total // 4, total)
    (logit_sent,) = call(
        sent_bias_kernel, [(quarter, f32)], bias_blocks, logit_sent, place=place,
        flops=total * total,
    )
    value_blocks, logit_sent = lax.optimization_barrier((value_blocks, logit_sent))
    logit_other = swapped(logit_sent, "seq", seq_half)
    value_blocks = across(value_blocks)
    softmax_out, probs = call(
        softmax_kernel, [(quarter, f32), (quarter, bf16)], bias_blocks, logit_mine, logit_other,
        place=place, flops=total * total,
    )
    probs_far = swapped(probs, "seq", seq_half)
    value_blocks, probs_far = lax.optimization_barrier((value_blocks, probs_far))
    grad_mine, grad_sent = scores(value_blocks, residues, 0, bf16)
    grad_other = swapped(grad_sent, "seq", seq_half)

    def products(quarters, blocks, first_row, second_row, with_share, factor):
        rows = 2 * residues + (residues // 2 if with_share else 0)
        (out,) = call(
            functools.partial(
                product_kernel, residues, factor, first_row, second_row, with_share
            ),
            [((group, rows, LANES), bf16)],
            *quarters, blocks,
            scratch=[pltpu.VMEM((total, total), bf16)],
            place=place, flops=4 * total * total * width,
        )
        return out

    def with_near(mine, far):
        return mine, far, swapped(mine, "res", 1), swapped(far, "res", 1)

    attended = products(with_near(probs, probs_far), value_blocks, 0, residues, False, 1.0)
    attended_blocks = across(attended)
    grad_other = lax.optimization_barrier((attended, grad_other))[1]
    (grad_logits,) = call(
        softmax_gradient_kernel, [(quarter, bf16)], softmax_out, grad_mine, grad_other,
        flops=total * total,
    )
    grad_quarters = with_near(grad_logits, swapped(grad_logits, "seq", seq_half))
    grad_quarters, attended_blocks = lax.optimization_barrier((grad_quarters, attended_blocks))
    grad_blocks = across(products(grad_quarters, query_blocks, residues, 0, True, scale))

    updated, value_gate, normed, attended_sums = call(
        attended_weight_kernel,
        [
            (x.shape, bf16),
            ((tokens, 2 * width), bf16),
            ((tokens, width), bf16),
            ((width, 3 * width), bf16),
        ],
        x, grad, wc, wo, attended_blocks,
        flops=14 * tokens * width * width, outside=4,
    )
    share = pltpu.VMEM((heads, residues, LANES), f32)
    (pair_weight_part,) = call(
        pair_weight_kernel, [((heads, channels), f32)],
        grad_blocks, pair_entries, mean, spread,
        scratch=[share], flops=4 * tokens * width * width,
    )
    columns = 5 * width + channels
    rows = width // res_size
    part_rows = ((res_size // 2, rows, columns), bf16)
    query_key, keep, send = call(
        query_weight_kernel,
        [((tokens, 2 * width), bf16), part_rows, part_rows],
        normed, grad_blocks, pair_weight_part, attended_sums,
        scratch=[pltpu.VMEM((width, columns), bf16)],
        place=place, flops=4 * tokens * width * width,
    )
    own, *sent = call(
        core_sum_kernel,
        [((rows, columns), f32)] + [((rows, columns), bf16)] * 3,
        keep, swapped(send, "res", 1), place=place,
    )
    received = [swapped(t, "res", 2 * flip) for flip, t in enumerate(sent, 1)]
    (pair_gradient,) = call(
        functools.partial(pair_kernel, 2 * residues),
        [(pair_entries.shape, bf16)],
        grad_blocks, pair_entries, pair_weight.T, bias, mean, spread,
        scratch=[share], flops=8 * tokens * width * width,
    )
    received, pair_gradient = lax.optimization_barrier((received, pair_gradient))
    (part,) = call(plane_sum_kernel, [((rows, columns), bf16)], own, *received)
    (alignment_gradient,) = call(
        alignment_kernel, [(x.shape, bf16)], x, wc, query_key, value_gate,
        flops=8 * tokens * width * width,
    )

    def added(mine, other):
        return (mine.astype(f32) + other.astype(f32)).astype(bf16)

    part = added(part, swapped(part, "seq", 1))
    part = added(part, swapped(part, "seq", seq_half))
    whole = lax.all_gather(part, "res", axis=0)
    return (
        updated,
        alignment_gradient,
        pair_gradient,
        whole[:, :, : 4 * width].reshape(wc.shape).astype(f32),
        whole[:, :, 4 * width : 5 * width].reshape(wo.shape).astype(f32),
        whole[:, 0, 5 * width :].T.astype(f32),
    )


def body(alignment_rows, pair_entries, combined_weight, output_weight, pair_weight, updated_gradient):
    chosen = head_body if fits_heads(alignment_rows, pair_entries, pair_weight) else gathered_body
    return chosen(
        alignment_rows, pair_entries, combined_weight, output_weight, pair_weight, updated_gradient
    )


def solution(mesh):
    return jax.shard_map(
        body,
        mesh=mesh,
        in_specs=(
            P("seq", "res", None),
            P("res", "seq", None),
            P(),
            P(),
            P(),
            P("seq", "res", None),
        ),
        out_specs=(
            P("seq", "res", None),
            P("seq", "res", None),
            P("res", "seq", None),
            P(),
            P(),
            P(),
        ),
        check_vma=False,
    )
```

```python
import functools
import math

import jax
import jax.numpy as jnp
from jax import lax
from jax.experimental import pallas as pl
from jax.experimental.pallas import tpu as pltpu
from jax.sharding import PartitionSpec as P

eps_norm = 1e-05


def layer_normalize(values):
    values = values.astype(jnp.float32)
    center = values - jnp.mean(values, axis=-1, keepdims=True)
    broadcast_pair = lax.rsqrt(jnp.mean(center * center, axis=-1, keepdims=True) + eps_norm)
    return (center * broadcast_pair, broadcast_pair)


def layer_norm_backward(normalized_gradient, normalized_rows, broadcast_pair):
    mean_grad = jnp.mean(normalized_gradient, axis=-1, keepdims=True)
    mean_cross = jnp.mean(normalized_gradient * normalized_rows, axis=-1, keepdims=True)
    return broadcast_pair * (normalized_gradient - mean_grad - normalized_rows * mean_cross)


def split_heads(tensor, head_count):
    return tensor.reshape(
        tensor.shape[0], tensor.shape[1], head_count, tensor.shape[2] // head_count
    )


def merge_heads(tensor):
    return tensor.reshape(tensor.shape[0], tensor.shape[1], tensor.shape[2] * tensor.shape[3])


def gathered_body(
    alignment_rows, pair_entries, combined_weight, output_weight, pair_weight, updated_gradient
):
    sequence_count, residue_count, alignment_width = alignment_rows.shape
    head_count = pair_weight.shape[1]
    query_width = output_weight.shape[0]
    head_dim = query_width // head_count
    column_count = pair_entries.shape[1]
    token_count = sequence_count * residue_count
    score_scale = 1.0 / math.sqrt(head_dim * sequence_count * lax.axis_size("seq"))
    normalized_rows, broadcast_pair = layer_normalize(alignment_rows)
    normalized_rows_backward = normalized_rows.astype(jnp.bfloat16).reshape(
        token_count, alignment_width
    )
    projected = jnp.dot(
        normalized_rows_backward, combined_weight, preferred_element_type=jnp.float32
    ).reshape(sequence_count, residue_count, 4 * query_width)
    queries = (projected[..., :query_width] * score_scale).astype(jnp.bfloat16)
    key_rows = projected[..., query_width : 2 * query_width].astype(jnp.bfloat16)
    value_rows = projected[..., 2 * query_width : 3 * query_width].astype(jnp.bfloat16)
    gate_open = jax.nn.sigmoid(projected[..., 3 * query_width :])
    all_keys, all_values = (
        lax.all_gather(key_rows, "res", axis=1, tiled=True),
        lax.all_gather(value_rows, "res", axis=1, tiled=True),
    )
    query_heads = split_heads(queries, head_count)
    key_heads = split_heads(all_keys, head_count)
    value_heads = split_heads(all_values, head_count)
    score_terms = jnp.einsum(
        "sihd,sjhd->hij", query_heads, key_heads, preferred_element_type=jnp.float32
    )
    pair_normed, pair_spread = layer_normalize(pair_entries)
    pair_bias = jnp.einsum("ijc,ch->hij", pair_normed, pair_weight, precision=lax.Precision.HIGHEST)
    col_start = lax.axis_index("seq") * column_count
    own_block = lax.dynamic_slice_in_dim(score_terms, col_start, column_count, 2) + pair_bias
    logits = lax.psum(lax.dynamic_update_slice_in_dim(score_terms, own_block, col_start, 2), "seq")
    row_top = jnp.max(logits, axis=-1, keepdims=True)
    lifted = jnp.exp(logits - row_top)
    softmax_out = lifted / jnp.sum(lifted, axis=-1, keepdims=True)
    softmax_low = softmax_out.astype(jnp.bfloat16)
    attended = merge_heads(
        jnp.einsum("hij,sjhd->sihd", softmax_low, value_heads, preferred_element_type=jnp.float32)
    )
    gated_out = (gate_open * attended).astype(jnp.bfloat16)
    flattened_gated = gated_out.reshape(token_count, query_width)
    updated = (
        jnp.dot(flattened_gated, output_weight, preferred_element_type=jnp.float32)
        .astype(jnp.bfloat16)
        .reshape(sequence_count, residue_count, alignment_width)
    )
    flattened_gradient = updated_gradient.reshape(token_count, alignment_width)
    grad_gated = jnp.dot(
        flattened_gradient, output_weight.T, preferred_element_type=jnp.float32
    ).reshape(sequence_count, residue_count, query_width)
    out_local = jnp.dot(flattened_gated.T, flattened_gradient, preferred_element_type=jnp.float32)
    grad_attended = (grad_gated * gate_open).astype(jnp.bfloat16)
    grad_gate_logit = grad_gated * attended * gate_open * (1.0 - gate_open)
    attended_grad_heads = split_heads(grad_attended, head_count)
    grad_terms = jnp.einsum(
        "sihd,sjhd->hij", attended_grad_heads, value_heads, preferred_element_type=jnp.float32
    )
    grad_probs = lax.psum(grad_terms, "seq")
    row_dot = jnp.sum(softmax_out * grad_probs, axis=-1, keepdims=True)
    grad_logits = softmax_out * (grad_probs - row_dot)
    grad_logits_b = grad_logits.astype(jnp.bfloat16)
    logit_share = lax.dynamic_slice_in_dim(grad_logits, col_start, column_count, 2)
    grad_query_heads = (
        jnp.einsum("hij,sjhd->sihd", grad_logits_b, key_heads, preferred_element_type=jnp.float32)
        * score_scale
    )
    key_part = jnp.einsum(
        "hij,sihd->jshd", grad_logits_b, query_heads, preferred_element_type=jnp.float32
    )
    value_part = jnp.einsum(
        "hij,sihd->jshd", softmax_low, attended_grad_heads, preferred_element_type=jnp.float32
    )
    summed = lax.psum_scatter(
        jnp.concatenate([merge_heads(key_part), merge_heads(value_part)], axis=-1),
        "res",
        scatter_dimension=0,
        tiled=True,
    )
    key_value_grads = jnp.transpose(summed, (1, 0, 2))
    projected_gradient = jnp.concatenate(
        [merge_heads(grad_query_heads), key_value_grads, grad_gate_logit], axis=-1
    )
    projected_gradient = projected_gradient.astype(jnp.bfloat16).reshape(
        token_count, 4 * query_width
    )
    qkvg_local = jnp.dot(
        normalized_rows_backward.T, projected_gradient, preferred_element_type=jnp.float32
    )
    normalized_gradient = jnp.dot(
        projected_gradient, combined_weight.T, preferred_element_type=jnp.float32
    ).reshape(sequence_count, residue_count, alignment_width)
    alignment_gradient = layer_norm_backward(
        normalized_gradient, normalized_rows, broadcast_pair
    ).astype(jnp.bfloat16)
    pair_w_local = jnp.einsum(
        "ijc,hij->ch", pair_normed, logit_share, precision=lax.Precision.HIGHEST
    )
    grad_pair_normed = jnp.einsum(
        "hij,ch->ijc", logit_share, pair_weight, precision=lax.Precision.HIGHEST
    )
    pair_gradient = layer_norm_backward(grad_pair_normed, pair_normed, pair_spread).astype(
        jnp.bfloat16
    )
    combined_weight_gradient, output_weight_gradient, pair_weight_gradient = lax.psum(
        (qkvg_local, out_local, pair_w_local), ("seq", "res")
    )
    return (
        updated,
        alignment_gradient,
        pair_gradient,
        combined_weight_gradient,
        output_weight_gradient,
        pair_weight_gradient,
    )


VMEM_LIMIT = 20 * 1024 * 1024
ARGUMENT_VMEM_LIMIT = 56 * 1024 * 1024
LANES = 128
SLOTS = 4
NT = (((1,), (1,)), ((), ()))
TN = (((0,), (0,)), ((), ()))


def f32_dot(left, right, dims=None):
    if dims is None:
        return jnp.dot(left, right, preferred_element_type=jnp.float32)
    return lax.dot_general(left, right, dims, preferred_element_type=jnp.float32)


def two_terms(values):
    high = values.astype(jnp.bfloat16)
    return high, (values - high.astype(jnp.float32)).astype(jnp.bfloat16)


def slot_select(pieces):
    slot = lax.broadcasted_iota(jnp.int32, pieces[0].shape, 1) // (LANES // SLOTS)
    result = pieces[0]
    for k in range(1, SLOTS):
        result = jnp.where(slot == k, pieces[k], result)
    return result


def pack_heads(out_ref, row, tensor, residues):
    for core in range(2):
        for tile in range(tensor.shape[1] // LANES):
            rolled = []
            for s in range(SLOTS):
                start = (core * SLOTS + s) * residues
                piece = tensor[start : start + residues, tile * LANES : (tile + 1) * LANES]
                rolled.append(pltpu.roll(piece, s * LANES // SLOTS, 1) if s else piece)
            for j in range(SLOTS):
                block = slot_select([rolled[(k - j) % SLOTS] for k in range(SLOTS)])
                out_ref[(tile * SLOTS + j) * 2 + core, row : row + residues, :] = block.astype(
                    jnp.bfloat16
                )


def unpack_heads(in_ref, row, residues, tiles):
    rows = []
    for core in range(2):
        for s in range(SLOTS):
            pieces = []
            for tile in range(tiles):
                blocks = [
                    in_ref[
                        (tile * SLOTS + (k - s) % SLOTS) * 2 + core, row : row + residues, :
                    ].astype(jnp.float32)
                    for k in range(SLOTS)
                ]
                block = slot_select(blocks)
                pieces.append(pltpu.roll(block, LANES - s * LANES // SLOTS, 1) if s else block)
            rows.append(jnp.concatenate(pieces, axis=1))
    return jnp.concatenate(rows, axis=0)


def normalized(x_ref):
    width = x_ref.shape[-1]
    values = x_ref[...].reshape(-1, width).astype(jnp.float32)
    return layer_normalize(values)


def gate_of(logits):
    return 1.0 / (1.0 + jnp.exp(-logits))


def value_kernel(x_ref, grad_ref, wc_ref, wo_ref, out_ref):
    residues, width = x_ref.shape[1], x_ref.shape[2]
    normed = normalized(x_ref)[0].astype(jnp.bfloat16)
    values = f32_dot(normed, wc_ref[:, 2 * width : 3 * width])
    gate = gate_of(f32_dot(normed, wc_ref[:, 3 * width :]))
    grad_gated = f32_dot(grad_ref[...].reshape(-1, width), wo_ref[...], NT)
    pack_heads(out_ref, 0, values, residues)
    pack_heads(out_ref, residues, grad_gated * gate, residues)


def centred(weight):
    return weight - jnp.mean(weight, axis=1, keepdims=True)


def query_kernel(
    scale, arrive, x_ref, wc_ref, pair_ref, weight_ref, out_ref, bias_ref, mean_ref, spread_ref
):
    residues, width = x_ref.shape[1], x_ref.shape[2]
    heads = weight_ref.shape[0]
    normed = normalized(x_ref)[0].astype(jnp.bfloat16)
    pack_heads(out_ref, 0, f32_dot(normed, wc_ref[:, :width]) * scale, residues)
    pack_heads(out_ref, residues, f32_dot(normed, wc_ref[:, width : 2 * width]), residues)

    arrive()
    columns, channels = pair_ref.shape[1], pair_ref.shape[2]
    weight = centred(weight_ref[...])
    first = weight.astype(jnp.bfloat16)
    second, third = two_terms(weight - first.astype(jnp.float32))
    share = jnp.full((heads, channels), 1.0 / channels, jnp.bfloat16)
    left = jnp.concatenate([first, second, third, share], axis=0)
    average = jnp.full((channels, channels), 1.0 / channels, jnp.bfloat16)
    step_rows = 8

    def rows(step, carry):
        start = pl.multiple_of(step * step_rows, step_rows)
        entries = pair_ref[pl.ds(start, step_rows)].reshape(step_rows * columns, channels)
        center = entries.astype(jnp.float32) - f32_dot(entries, average)
        high, low = two_terms(center * center)
        variance = f32_dot(share, high, NT) + f32_dot(share, low, NT)
        spread = lax.rsqrt(variance + eps_norm)
        raw = f32_dot(left, entries, NT)
        bias = spread * (raw[:heads] + raw[heads : 2 * heads] + raw[2 * heads : 3 * heads])
        for k in range(step_rows):
            lanes = slice(k * columns, (k + 1) * columns)
            bias_ref[:, start + k, :] = bias[:, lanes]
            mean_ref[pl.ds(start + k, 1), :] = raw[3 * heads : 3 * heads + 1, lanes]
            spread_ref[pl.ds(start + k, 1), :] = spread[:1, lanes]
        return carry

    lax.fori_loop(0, pair_ref.shape[0] // step_rows, rows, 0)
    half = residues // 2
    for h in range(heads):
        for core in range(2):
            high, low = two_terms(bias_ref[h, core * half : (core + 1) * half, :])
            out_ref[h * 2 + core, 2 * residues : 2 * residues + half, :] = high
            out_ref[h * 2 + core, 2 * residues + half : 3 * residues, :] = low


def lanes_of(blocks_ref, row, residues):
    count = blocks_ref.shape[0] // 2
    planes = [
        blocks_ref[p * count : (p + 1) * count, row : row + residues, :].reshape(-1, LANES)
        for p in range(2)
    ]
    return jnp.concatenate(planes, axis=1)


def score_kernel(
    residues, left_row, right_row, with_bias, place_ref, own_ref, other_ref, mine_ref, sent_ref
):
    core, half = place_ref[0], place_ref[1]
    count = own_ref.shape[0] // 2
    part = residues // 2
    right = jnp.concatenate(
        [lanes_of(own_ref, right_row, residues), lanes_of(other_ref, right_row, residues)], axis=1
    )
    for which, ref in ((half, mine_ref), (1 - half, sent_ref)):
        left = []
        for k in range(count // 2):
            block = which * (count // 2) + k
            rows = pl.ds(pl.multiple_of(left_row + core * part, part), part)
            left.append(
                jnp.concatenate(
                    [
                        r[p * count + block, rows, :]
                        for r in (own_ref, other_ref)
                        for p in range(2)
                    ],
                    axis=1,
                )
            )
        ref[...] = f32_dot(jnp.concatenate(left, axis=0), right, NT).astype(ref.dtype)
        if with_bias:
            for p in range(2):
                columns = pl.ds(pl.multiple_of((half * 2 + p) * LANES, LANES), LANES)
                for k in range(count // 2):
                    block = p * count + which * (count // 2) + k
                    high = own_ref[block, 2 * residues : 2 * residues + part, :]
                    low = own_ref[block, 2 * residues + part : 3 * residues, :]
                    bias = high.astype(jnp.float32) + low.astype(jnp.float32)
                    ref[k * part : (k + 1) * part, columns] += bias


def softmax_kernel(logit_ref, logit_other_ref, grad_ref, grad_other_ref, out_ref, low_ref):
    logits = logit_ref[...] + logit_other_ref[...]
    lifted = jnp.exp(logits - jnp.max(logits, axis=-1, keepdims=True))
    softmax_out = lifted / jnp.sum(lifted, axis=-1, keepdims=True)
    low_ref[...] = softmax_out.astype(jnp.bfloat16)
    grad_probs = grad_ref[...] + grad_other_ref[...].astype(jnp.float32)
    row_dot = jnp.sum(softmax_out * grad_probs, axis=-1, keepdims=True)
    out_ref[...] = (softmax_out * (grad_probs - row_dot)).astype(jnp.bfloat16)


def product_kernel(
    residues, scale, first_row, second_row, with_share,
    place_ref, own_ref, far_ref, near_ref, corner_ref, blocks_ref, out_ref, whole_ref,
):
    core, half = place_ref[0], place_ref[1]
    count = blocks_ref.shape[0] // 2
    part = residues // 2
    quarters = (
        (own_ref, core, half), (far_ref, core, 1 - half),
        (near_ref, 1 - core, half), (corner_ref, 1 - core, 1 - half),
    )
    for ref, c, z in quarters:
        for k in range(count // 2):
            start = (z * (count // 2) + k) * residues + c * part
            whole_ref[pl.ds(pl.multiple_of(start, part), part), :] = ref[k * part : (k + 1) * part, :]
    whole = whole_ref[...]
    if with_share:
        for p in range(2):
            columns = pl.ds(pl.multiple_of((half * 2 + p) * LANES, LANES), LANES)
            for q in range(count):
                rows = pl.ds(pl.multiple_of(q * residues + core * part, part), part)
                out_ref[p * count + q, 2 * residues : 2 * residues + part, :] = whole_ref[rows, columns]
    first = f32_dot(whole, lanes_of(blocks_ref, first_row, residues)) * scale
    second = f32_dot(whole, lanes_of(blocks_ref, second_row, residues), TN)
    for row, product in ((0, first), (residues, second)):
        for p in range(2):
            out_ref[p * count : (p + 1) * count, row : row + residues, :] = (
                product[:, p * LANES : (p + 1) * LANES]
                .astype(jnp.bfloat16)
                .reshape(count, residues, LANES)
            )


def share_of(blocks_ref, row, part, heads):
    return jnp.concatenate(
        [
            blocks_ref[:, row : row + part, :]
            .astype(jnp.float32)
            .reshape(heads, 2 * part, LANES)
        ],
        axis=0,
    )


def query_weight_kernel(x_ref, blocks_ref, pair_weight_ref, projected_ref, sums_ref):
    residues, width = x_ref.shape[1], x_ref.shape[2]
    tiles = width // LANES
    normed = normalized(x_ref)[0].astype(jnp.bfloat16)
    for t in range(2):
        projected_ref[:, t * width : (t + 1) * width] = unpack_heads(
            blocks_ref, t * residues, residues, tiles
        ).astype(jnp.bfloat16)
    sums_ref[:, : 2 * width] = f32_dot(normed, projected_ref[...], TN).astype(jnp.bfloat16)
    heads, channels = pair_weight_ref.shape
    rows = sums_ref.shape[0] // heads
    first = lax.broadcasted_iota(jnp.int32, (rows, channels), 0) == 0
    for h in range(heads):
        row = jnp.broadcast_to(pair_weight_ref[h : h + 1], (rows, channels))
        sums_ref[h * rows : (h + 1) * rows, 2 * width :] = jnp.where(first, row, 0.0).astype(
            jnp.bfloat16
        )


def attended_weight_kernel(
    place_ref, x_ref, grad_ref, wc_ref, wo_ref, query_sums_ref, blocks_ref,
    updated_ref, projected_ref, keep_ref, send_ref, sums_ref,
):
    residues, width = x_ref.shape[1], x_ref.shape[2]
    tiles = width // LANES
    core = place_ref[0]
    normed = normalized(x_ref)[0].astype(jnp.bfloat16)
    gate = gate_of(f32_dot(normed, wc_ref[:, 3 * width :]))
    grad = grad_ref[...].reshape(-1, width)
    grad_gated = f32_dot(grad, wo_ref[...], NT)
    attended = unpack_heads(blocks_ref, 0, residues, tiles)
    gated = (gate * attended).astype(jnp.bfloat16)
    updated_ref[...] = f32_dot(gated, wo_ref[...]).astype(jnp.bfloat16).reshape(updated_ref.shape)
    projected_ref[:, :width] = unpack_heads(blocks_ref, residues, residues, tiles).astype(
        jnp.bfloat16
    )
    projected_ref[:, width:] = (grad_gated * attended * gate * (1.0 - gate)).astype(jnp.bfloat16)
    sums_ref[:, : 2 * width] = f32_dot(normed, projected_ref[...], TN).astype(jnp.bfloat16)
    sums_ref[:, 2 * width : 3 * width] = f32_dot(gated, grad, TN).astype(jnp.bfloat16)
    sums_ref[:, 3 * width :] = query_sums_ref[...]
    rows = keep_ref.shape[1]
    for which, ref in ((core, keep_ref), (1 - core, send_ref)):
        for block in range(keep_ref.shape[0]):
            start = pl.multiple_of((2 * block + which) * rows, rows)
            ref[block] = sums_ref[pl.ds(start, rows), :]


def core_sum_kernel(place_ref, keep_ref, other_ref, own_ref, *send_refs):
    chip = place_ref[2]
    for flip, ref in enumerate((own_ref, *send_refs)):
        block = jnp.bitwise_xor(chip, flip)
        total = keep_ref[block].astype(jnp.float32) + other_ref[block].astype(jnp.float32)
        ref[...] = total.astype(ref.dtype)


def plane_sum_kernel(own_ref, *refs):
    total = own_ref[...]
    for ref in refs[:-1]:
        total += ref[...].astype(jnp.float32)
    refs[-1][...] = total.astype(refs[-1].dtype)


def pair_weight_kernel(blocks_ref, pair_ref, mean_ref, spread_ref, out_ref, share_ref):
    heads, part = share_ref.shape[0], pair_ref.shape[0] // 2
    share_ref[...] = share_of(blocks_ref, blocks_ref.shape[1] - part, part, heads)

    def rows(step, carry):
        total, shift = carry
        for k in range(8):
            i = step * 8 + k
            scaled = share_ref[:, i, :] * spread_ref[pl.ds(i, 1), :]
            high, low = two_terms(scaled)
            total += f32_dot(jnp.concatenate([high, low], axis=0), pair_ref[i])
            shift += (high.astype(jnp.float32) + low.astype(jnp.float32)) * mean_ref[pl.ds(i, 1), :]
        return total, shift

    channels = pair_ref.shape[2]
    total, shift = lax.fori_loop(
        0,
        pair_ref.shape[0] // 8,
        rows,
        (jnp.zeros((2 * heads, channels), jnp.float32), jnp.zeros((heads, LANES), jnp.float32)),
    )
    out_ref[...] = total[:heads] + total[heads:] - jnp.sum(shift, axis=1, keepdims=True)


def alignment_kernel(x_ref, wc_ref, query_key_ref, value_gate_ref, out_ref):
    normed, spread = normalized(x_ref)
    width = x_ref.shape[2]
    gradient = f32_dot(query_key_ref[...], wc_ref[:, : 2 * width], NT) + f32_dot(
        value_gate_ref[...], wc_ref[:, 2 * width :], NT
    )
    out_ref[...] = (
        layer_norm_backward(gradient, normed, spread).astype(jnp.bfloat16).reshape(out_ref.shape)
    )


def pair_kernel(blocks_row, blocks_ref, pair_ref, weight_ref, bias_ref, mean_ref, spread_ref, out_ref, share_ref):
    heads, channels = weight_ref.shape
    part = pair_ref.shape[0] // 2
    share_ref[...] = share_of(blocks_ref, blocks_row, part, heads)
    first, second = two_terms(centred(weight_ref[...]))
    zero = jnp.zeros((heads, channels), jnp.bfloat16)
    top = lax.broadcasted_iota(jnp.int32, (heads, channels), 0) < 2
    ones = jnp.where(top, 1.0, 0.0).astype(jnp.bfloat16)
    right = jnp.concatenate(
        [
            jnp.concatenate([first, first, second, ones, zero], axis=0),
            jnp.concatenate([zero, zero, zero, zero, ones], axis=0),
        ],
        axis=1,
    )
    row = lax.broadcasted_iota(jnp.int32, (heads, LANES), 0)

    def rows_of_two(value):
        high, low = two_terms(value)
        high, low = high.astype(jnp.float32), low.astype(jnp.float32)
        return jnp.where(row == 0, high, jnp.where(row == 1, low, 0.0)).astype(jnp.bfloat16)

    def rows(step, carry):
        for k in range(8):
            i = step * 8 + k
            gradient = share_ref[:, i, :]
            spread = spread_ref[pl.ds(i, 1), :]
            cross = jnp.sum(gradient * bias_ref[:, i, :], axis=0, keepdims=True) / channels
            slope = spread * spread * cross
            high, low = two_terms(gradient * spread)
            left = jnp.concatenate(
                [
                    high, low, high,
                    rows_of_two(jnp.broadcast_to(slope * mean_ref[pl.ds(i, 1), :], row.shape)),
                    rows_of_two(jnp.broadcast_to(slope, row.shape)),
                ],
                axis=0,
            )
            terms = f32_dot(left, right, TN)
            entries = pair_ref[i].astype(jnp.float32)
            out_ref[i] = (terms[:, :channels] - terms[:, channels:] * entries).astype(jnp.bfloat16)
        return carry

    lax.fori_loop(0, pair_ref.shape[0] // 8, rows, 0)


def output_kernel(parts_ref, combined_ref, out_weight_ref, pair_weight_ref):
    width = combined_ref.shape[0]
    rows = parts_ref.shape[1]
    for h in range(parts_ref.shape[0]):
        block = slice(h * rows, (h + 1) * rows)
        part = parts_ref[h].astype(jnp.float32)
        combined_ref[block, 2 * width :] = part[:, : 2 * width]
        out_weight_ref[block, :] = part[:, 2 * width : 3 * width]
        combined_ref[block, : 2 * width] = part[:, 3 * width : 5 * width]
        pair_weight_ref[h : h + 1, :] = part[:1, 5 * width :]


def call(kernel, outs, *args, scratch=(), place=None, flops=0, after=(), outside=0, late=0):
    whole, anywhere = pl.BlockSpec(memory_space=pltpu.VMEM), pl.BlockSpec(memory_space=pl.ANY)
    specs = [anywhere] * outside + [whole] * (len(args) - outside)
    ahead = () if place is None else (place,)
    shapes = [jax.ShapeDtypeStruct(*o) for o in outs]
    moved = sum(math.prod(a.shape) * a.dtype.itemsize for a in list(args) + shapes)
    first = len(ahead) + len(args)
    last = first + len(after)

    def wrapped(*refs):
        given, rest = list(refs[:first]), refs[last:]
        if outside:
            *rest, arrived = rest
            held = rest[len(rest) - outside :]
            rest = rest[: len(rest) - outside]
            copies = []
            for k in range(outside):
                copies.append(
                    pltpu.make_async_copy(given[len(ahead) + k], held[k], arrived.at[k])
                )
                given[len(ahead) + k] = held[k]
            for copy in copies:
                copy.start()
            for copy in copies[: outside - late]:
                copy.wait()
            if late:
                given.insert(0, lambda: [copy.wait() for copy in copies[outside - late :]])
        kernel(*given, *rest)

    held = [pltpu.VMEM(a.shape, a.dtype) for a in args[:outside]]
    if outside:
        held.append(pltpu.SemaphoreType.DMA((outside,)))
    return pl.pallas_call(
        wrapped,
        out_shape=shapes,
        in_specs=[pl.BlockSpec(memory_space=pltpu.SMEM)] * len(ahead)
        + specs
        + [anywhere] * len(after),
        out_specs=[whole] * len(shapes),
        scratch_shapes=[*scratch, *held],
        compiler_params=pltpu.CompilerParams(
            vmem_limit_bytes=ARGUMENT_VMEM_LIMIT if outside else VMEM_LIMIT
        ),
        cost_estimate=pl.CostEstimate(flops=flops, bytes_accessed=moved, transcendentals=0),
    )(*ahead, *args, *after)


def swapped(mine, axis_name, distance):
    size = lax.axis_size(axis_name)
    return lax.ppermute(mine, axis_name, [(a, a ^ distance) for a in range(size)])


def fits_heads(alignment_rows, pair_entries, pair_weight):
    channels, heads = pair_weight.shape
    return (
        lax.axis_size("seq") == 4
        and lax.axis_size("res") == heads == 8
        and alignment_rows.shape[0] == 2 * SLOTS
        and alignment_rows.shape[1] == pair_entries.shape[0] == 64
        and alignment_rows.shape[2] == 2 * LANES
        and pair_entries.shape[1] == channels == LANES
    )


def head_body(
    alignment_rows, pair_entries, combined_weight, output_weight, pair_weight, updated_gradient
):
    sequences, residues, width = alignment_rows.shape
    channels, heads = pair_weight.shape
    tokens = sequences * residues
    seq_size, res_size = lax.axis_size("seq"), lax.axis_size("res")
    seq_half = seq_size // 2
    total = residues * res_size
    group = 2 * res_size
    groups = [[g * group + k for k in range(group)] for g in range(seq_half)]
    scale = 1.0 / math.sqrt(width // heads * sequences * seq_size)
    res_index, seq_index = lax.axis_index("res"), lax.axis_index("seq")
    place = jnp.stack([res_index % 2, seq_index // 2, res_index // 2]).astype(jnp.int32)
    bf16, f32 = jnp.bfloat16, jnp.float32

    def across(blocks):
        return lax.all_to_all(blocks, ("seq", "res"), 0, 0, axis_index_groups=groups, tiled=True)

    x, grad, wc, wo = alignment_rows, updated_gradient, combined_weight, output_weight
    (value_blocks,) = call(
        value_kernel, [((group, 2 * residues, LANES), bf16)], x, grad, wc, wo,
        flops=8 * tokens * width * width, outside=4,
    )
    value_blocks = across(value_blocks)
    query_blocks, bias, mean, spread = call(
        functools.partial(query_kernel, scale),
        [
            ((group, 3 * residues, LANES), bf16),
            ((heads, residues, LANES), f32),
            ((residues, LANES), f32),
            ((residues, LANES), f32),
        ],
        x, wc, pair_entries, pair_weight.T,
        flops=8 * tokens * width * width, outside=3, late=1,
    )
    value_blocks, query_blocks = lax.optimization_barrier((value_blocks, query_blocks))
    query_blocks = across(query_blocks)

    def scores(blocks, left_row, right_row, with_bias, kind):
        return call(
            functools.partial(score_kernel, residues, left_row, right_row, with_bias),
            [((total // 4, total), f32), ((total // 4, total), kind)],
            blocks, swapped(blocks, "res", 1),
            place=place, flops=2 * total * total * width,
        )

    grad_mine, grad_sent = scores(value_blocks, residues, 0, False, bf16)
    grad_other = swapped(grad_sent, "seq", seq_half)
    query_blocks, grad_other = lax.optimization_barrier((query_blocks, grad_other))
    logit_mine, logit_sent = scores(query_blocks, 0, residues, True, f32)
    quarter = ((total // 4, total), bf16)
    grad_logits, probs = call(
        softmax_kernel, [quarter, quarter],
        logit_mine, swapped(logit_sent, "seq", seq_half), grad_mine, grad_other,
        flops=total * total,
    )

    def products(mine, far, blocks, first_row, second_row, with_share, factor):
        rows = 2 * residues + (residues // 2 if with_share else 0)
        (out,) = call(
            functools.partial(
                product_kernel, residues, factor, first_row, second_row, with_share
            ),
            [((group, rows, LANES), bf16)],
            mine, far, swapped(mine, "res", 1), swapped(far, "res", 1), blocks,
            scratch=[pltpu.VMEM((total, total), bf16)],
            place=place, flops=4 * total * total * width,
        )
        return out

    grad_far = swapped(grad_logits, "seq", seq_half)
    grad_far, probs = lax.optimization_barrier((grad_far, probs))
    grad_blocks = across(
        products(grad_logits, grad_far, query_blocks, residues, 0, True, scale)
    )
    attended = products(
        probs, swapped(probs, "seq", seq_half), value_blocks, 0, residues, False, 1.0
    )
    grad_blocks, attended = lax.optimization_barrier((grad_blocks, attended))
    attended_blocks = across(attended)

    share = pltpu.VMEM((heads, residues, LANES), f32)
    (pair_weight_part,) = call(
        pair_weight_kernel, [((heads, channels), f32)],
        grad_blocks, pair_entries, mean, spread,
        scratch=[share], flops=4 * tokens * width * width,
    )
    query_key, query_sums = call(
        query_weight_kernel,
        [((tokens, 2 * width), bf16), ((width, 2 * width + channels), bf16)],
        x, grad_blocks, pair_weight_part,
        flops=4 * tokens * width * width, outside=1,
    )
    (pair_gradient,) = call(
        functools.partial(pair_kernel, 2 * residues),
        [(pair_entries.shape, bf16)],
        grad_blocks, pair_entries, pair_weight.T, bias, mean, spread,
        scratch=[share], flops=8 * tokens * width * width,
    )
    attended_blocks, query_sums, pair_gradient = lax.optimization_barrier(
        (attended_blocks, query_sums, pair_gradient)
    )
    columns = 5 * width + channels
    rows = width // res_size
    part_rows = ((res_size // 2, rows, columns), bf16)
    updated, value_gate, keep, send = call(
        attended_weight_kernel,
        [(x.shape, bf16), ((tokens, 2 * width), bf16), part_rows, part_rows],
        x, grad, wc, wo, query_sums, attended_blocks,
        scratch=[pltpu.VMEM((width, columns), bf16)],
        place=place, flops=14 * tokens * width * width, outside=5,
    )
    own, *sent = call(
        core_sum_kernel,
        [((rows, columns), f32)] + [((rows, columns), bf16)] * 3,
        keep, swapped(send, "res", 1), place=place,
    )
    received = [swapped(t, "res", 2 * flip) for flip, t in enumerate(sent, 1)]
    (alignment_gradient,) = call(
        alignment_kernel, [(x.shape, bf16)], x, wc, query_key, value_gate,
        flops=8 * tokens * width * width, outside=4,
    )
    received, alignment_gradient = lax.optimization_barrier((received, alignment_gradient))
    (part,) = call(plane_sum_kernel, [((rows, columns), bf16)], own, *received)

    def added(mine, other):
        return (mine.astype(f32) + other.astype(f32)).astype(bf16)

    part = added(part, swapped(part, "seq", 1))
    part = added(part, swapped(part, "seq", seq_half))
    combined_gradient, output_gradient, pair_weight_gradient = call(
        output_kernel,
        [(wc.shape, f32), (wo.shape, f32), ((heads, channels), f32)],
        lax.all_gather(part, "res", axis=0),
    )
    return (
        updated,
        alignment_gradient,
        pair_gradient,
        combined_gradient,
        output_gradient,
        pair_weight_gradient.T,
    )


def body(alignment_rows, pair_entries, combined_weight, output_weight, pair_weight, updated_gradient):
    chosen = head_body if fits_heads(alignment_rows, pair_entries, pair_weight) else gathered_body
    return chosen(
        alignment_rows, pair_entries, combined_weight, output_weight, pair_weight, updated_gradient
    )


def solution(mesh):
    return jax.shard_map(
        body,
        mesh=mesh,
        in_specs=(
            P("seq", "res", None),
            P("res", "seq", None),
            P(),
            P(),
            P(),
            P("seq", "res", None),
        ),
        out_specs=(
            P("seq", "res", None),
            P("seq", "res", None),
            P("res", "seq", None),
            P(),
            P(),
            P(),
        ),
        check_vma=False,
    )
```

```python
import functools
import math

import jax
import jax.numpy as jnp
from jax import lax
from jax.experimental import pallas as pl
from jax.experimental.pallas import tpu as pltpu
from jax.sharding import PartitionSpec as P

eps_norm = 1e-05


def layer_normalize(values):
    values = values.astype(jnp.float32)
    center = values - jnp.mean(values, axis=-1, keepdims=True)
    broadcast_pair = lax.rsqrt(jnp.mean(center * center, axis=-1, keepdims=True) + eps_norm)
    return (center * broadcast_pair, broadcast_pair)


def layer_norm_backward(normalized_gradient, normalized_rows, broadcast_pair):
    mean_grad = jnp.mean(normalized_gradient, axis=-1, keepdims=True)
    mean_cross = jnp.mean(normalized_gradient * normalized_rows, axis=-1, keepdims=True)
    return broadcast_pair * (normalized_gradient - mean_grad - normalized_rows * mean_cross)


def split_heads(tensor, head_count):
    return tensor.reshape(
        tensor.shape[0], tensor.shape[1], head_count, tensor.shape[2] // head_count
    )


def merge_heads(tensor):
    return tensor.reshape(tensor.shape[0], tensor.shape[1], tensor.shape[2] * tensor.shape[3])


def gathered_body(
    alignment_rows, pair_entries, combined_weight, output_weight, pair_weight, updated_gradient
):
    sequence_count, residue_count, alignment_width = alignment_rows.shape
    head_count = pair_weight.shape[1]
    query_width = output_weight.shape[0]
    head_dim = query_width // head_count
    column_count = pair_entries.shape[1]
    token_count = sequence_count * residue_count
    score_scale = 1.0 / math.sqrt(head_dim * sequence_count * lax.axis_size("seq"))
    normalized_rows, broadcast_pair = layer_normalize(alignment_rows)
    normalized_rows_backward = normalized_rows.astype(jnp.bfloat16).reshape(
        token_count, alignment_width
    )
    projected = jnp.dot(
        normalized_rows_backward, combined_weight, preferred_element_type=jnp.float32
    ).reshape(sequence_count, residue_count, 4 * query_width)
    queries = (projected[..., :query_width] * score_scale).astype(jnp.bfloat16)
    key_rows = projected[..., query_width : 2 * query_width].astype(jnp.bfloat16)
    value_rows = projected[..., 2 * query_width : 3 * query_width].astype(jnp.bfloat16)
    gate_open = jax.nn.sigmoid(projected[..., 3 * query_width :])
    all_keys, all_values = (
        lax.all_gather(key_rows, "res", axis=1, tiled=True),
        lax.all_gather(value_rows, "res", axis=1, tiled=True),
    )
    query_heads = split_heads(queries, head_count)
    key_heads = split_heads(all_keys, head_count)
    value_heads = split_heads(all_values, head_count)
    score_terms = jnp.einsum(
        "sihd,sjhd->hij", query_heads, key_heads, preferred_element_type=jnp.float32
    )
    pair_normed, pair_spread = layer_normalize(pair_entries)
    pair_bias = jnp.einsum("ijc,ch->hij", pair_normed, pair_weight, precision=lax.Precision.HIGHEST)
    col_start = lax.axis_index("seq") * column_count
    own_block = lax.dynamic_slice_in_dim(score_terms, col_start, column_count, 2) + pair_bias
    logits = lax.psum(lax.dynamic_update_slice_in_dim(score_terms, own_block, col_start, 2), "seq")
    row_top = jnp.max(logits, axis=-1, keepdims=True)
    lifted = jnp.exp(logits - row_top)
    softmax_out = lifted / jnp.sum(lifted, axis=-1, keepdims=True)
    softmax_low = softmax_out.astype(jnp.bfloat16)
    attended = merge_heads(
        jnp.einsum("hij,sjhd->sihd", softmax_low, value_heads, preferred_element_type=jnp.float32)
    )
    gated_out = (gate_open * attended).astype(jnp.bfloat16)
    flattened_gated = gated_out.reshape(token_count, query_width)
    updated = (
        jnp.dot(flattened_gated, output_weight, preferred_element_type=jnp.float32)
        .astype(jnp.bfloat16)
        .reshape(sequence_count, residue_count, alignment_width)
    )
    flattened_gradient = updated_gradient.reshape(token_count, alignment_width)
    grad_gated = jnp.dot(
        flattened_gradient, output_weight.T, preferred_element_type=jnp.float32
    ).reshape(sequence_count, residue_count, query_width)
    out_local = jnp.dot(flattened_gated.T, flattened_gradient, preferred_element_type=jnp.float32)
    grad_attended = (grad_gated * gate_open).astype(jnp.bfloat16)
    grad_gate_logit = grad_gated * attended * gate_open * (1.0 - gate_open)
    attended_grad_heads = split_heads(grad_attended, head_count)
    grad_terms = jnp.einsum(
        "sihd,sjhd->hij", attended_grad_heads, value_heads, preferred_element_type=jnp.float32
    )
    grad_probs = lax.psum(grad_terms, "seq")
    row_dot = jnp.sum(softmax_out * grad_probs, axis=-1, keepdims=True)
    grad_logits = softmax_out * (grad_probs - row_dot)
    grad_logits_b = grad_logits.astype(jnp.bfloat16)
    logit_share = lax.dynamic_slice_in_dim(grad_logits, col_start, column_count, 2)
    grad_query_heads = (
        jnp.einsum("hij,sjhd->sihd", grad_logits_b, key_heads, preferred_element_type=jnp.float32)
        * score_scale
    )
    key_part = jnp.einsum(
        "hij,sihd->jshd", grad_logits_b, query_heads, preferred_element_type=jnp.float32
    )
    value_part = jnp.einsum(
        "hij,sihd->jshd", softmax_low, attended_grad_heads, preferred_element_type=jnp.float32
    )
    summed = lax.psum_scatter(
        jnp.concatenate([merge_heads(key_part), merge_heads(value_part)], axis=-1),
        "res",
        scatter_dimension=0,
        tiled=True,
    )
    key_value_grads = jnp.transpose(summed, (1, 0, 2))
    projected_gradient = jnp.concatenate(
        [merge_heads(grad_query_heads), key_value_grads, grad_gate_logit], axis=-1
    )
    projected_gradient = projected_gradient.astype(jnp.bfloat16).reshape(
        token_count, 4 * query_width
    )
    qkvg_local = jnp.dot(
        normalized_rows_backward.T, projected_gradient, preferred_element_type=jnp.float32
    )
    normalized_gradient = jnp.dot(
        projected_gradient, combined_weight.T, preferred_element_type=jnp.float32
    ).reshape(sequence_count, residue_count, alignment_width)
    alignment_gradient = layer_norm_backward(
        normalized_gradient, normalized_rows, broadcast_pair
    ).astype(jnp.bfloat16)
    pair_w_local = jnp.einsum(
        "ijc,hij->ch", pair_normed, logit_share, precision=lax.Precision.HIGHEST
    )
    grad_pair_normed = jnp.einsum(
        "hij,ch->ijc", logit_share, pair_weight, precision=lax.Precision.HIGHEST
    )
    pair_gradient = layer_norm_backward(grad_pair_normed, pair_normed, pair_spread).astype(
        jnp.bfloat16
    )
    combined_weight_gradient, output_weight_gradient, pair_weight_gradient = lax.psum(
        (qkvg_local, out_local, pair_w_local), ("seq", "res")
    )
    return (
        updated,
        alignment_gradient,
        pair_gradient,
        combined_weight_gradient,
        output_weight_gradient,
        pair_weight_gradient,
    )


VMEM_LIMIT = 20 * 1024 * 1024
ARGUMENT_VMEM_LIMIT = 56 * 1024 * 1024
LANES = 128
SLOTS = 4
NT = (((1,), (1,)), ((), ()))
TN = (((0,), (0,)), ((), ()))


def f32_dot(left, right, dims=None):
    if dims is None:
        return jnp.dot(left, right, preferred_element_type=jnp.float32)
    return lax.dot_general(left, right, dims, preferred_element_type=jnp.float32)


def two_terms(values):
    high = values.astype(jnp.bfloat16)
    return high, (values - high.astype(jnp.float32)).astype(jnp.bfloat16)


def slot_select(pieces):
    slot = lax.broadcasted_iota(jnp.int32, pieces[0].shape, 1) // (LANES // SLOTS)
    result = pieces[0]
    for k in range(1, SLOTS):
        result = jnp.where(slot == k, pieces[k], result)
    return result


def pack_heads(out_ref, row, tensor, residues):
    for core in range(2):
        for tile in range(tensor.shape[1] // LANES):
            rolled = []
            for s in range(SLOTS):
                start = (core * SLOTS + s) * residues
                piece = tensor[start : start + residues, tile * LANES : (tile + 1) * LANES]
                rolled.append(pltpu.roll(piece, s * LANES // SLOTS, 1) if s else piece)
            for j in range(SLOTS):
                block = slot_select([rolled[(k - j) % SLOTS] for k in range(SLOTS)])
                out_ref[(tile * SLOTS + j) * 2 + core, row : row + residues, :] = block.astype(
                    jnp.bfloat16
                )


def unpack_heads(in_ref, row, residues, tiles):
    rows = []
    for core in range(2):
        for s in range(SLOTS):
            pieces = []
            for tile in range(tiles):
                blocks = [
                    in_ref[
                        (tile * SLOTS + (k - s) % SLOTS) * 2 + core, row : row + residues, :
                    ].astype(jnp.float32)
                    for k in range(SLOTS)
                ]
                block = slot_select(blocks)
                pieces.append(pltpu.roll(block, LANES - s * LANES // SLOTS, 1) if s else block)
            rows.append(jnp.concatenate(pieces, axis=1))
    return jnp.concatenate(rows, axis=0)


def normalized(x_ref):
    width = x_ref.shape[-1]
    values = x_ref[...].reshape(-1, width).astype(jnp.float32)
    return layer_normalize(values)


def gate_of(logits):
    return 1.0 / (1.0 + jnp.exp(-logits))


def query_kernel(scale, x_ref, wc_ref, out_ref):
    residues, width = x_ref.shape[1], x_ref.shape[2]
    normed = normalized(x_ref)[0].astype(jnp.bfloat16)
    pack_heads(out_ref, 0, f32_dot(normed, wc_ref[:, :width]) * scale, residues)
    pack_heads(out_ref, residues, f32_dot(normed, wc_ref[:, width : 2 * width]), residues)


def centred(weight):
    return weight - jnp.mean(weight, axis=1, keepdims=True)


def value_kernel(
    arrive, x_ref, grad_ref, wc_ref, wo_ref, pair_ref, weight_ref,
    out_ref, bias_ref, mean_ref, spread_ref,
):
    residues, width = x_ref.shape[1], x_ref.shape[2]
    heads = weight_ref.shape[0]
    normed = normalized(x_ref)[0].astype(jnp.bfloat16)
    values = f32_dot(normed, wc_ref[:, 2 * width : 3 * width])
    gate = gate_of(f32_dot(normed, wc_ref[:, 3 * width :]))
    grad_gated = f32_dot(grad_ref[...].reshape(-1, width), wo_ref[...], NT)
    pack_heads(out_ref, 0, values, residues)
    pack_heads(out_ref, residues, grad_gated * gate, residues)

    arrive()
    columns, channels = pair_ref.shape[1], pair_ref.shape[2]
    weight = centred(weight_ref[...])
    first = weight.astype(jnp.bfloat16)
    second, third = two_terms(weight - first.astype(jnp.float32))
    share = jnp.full((heads, channels), 1.0 / channels, jnp.bfloat16)
    left = jnp.concatenate([first, second, third, share], axis=0)
    average = jnp.full((channels, channels), 1.0 / channels, jnp.bfloat16)
    step_rows = 8

    def rows(step, carry):
        start = pl.multiple_of(step * step_rows, step_rows)
        entries = pair_ref[pl.ds(start, step_rows)].reshape(step_rows * columns, channels)
        center = entries.astype(jnp.float32) - f32_dot(entries, average)
        high, low = two_terms(center * center)
        variance = f32_dot(share, high, NT) + f32_dot(share, low, NT)
        spread = lax.rsqrt(variance + eps_norm)
        raw = f32_dot(left, entries, NT)
        bias = spread * (raw[:heads] + raw[heads : 2 * heads] + raw[2 * heads : 3 * heads])
        for k in range(step_rows):
            lanes = slice(k * columns, (k + 1) * columns)
            bias_ref[:, start + k, :] = bias[:, lanes]
            mean_ref[pl.ds(start + k, 1), :] = raw[3 * heads : 3 * heads + 1, lanes]
            spread_ref[pl.ds(start + k, 1), :] = spread[:1, lanes]
        return carry

    lax.fori_loop(0, pair_ref.shape[0] // step_rows, rows, 0)
    half = residues // 2
    for h in range(heads):
        for core in range(2):
            high, low = two_terms(bias_ref[h, core * half : (core + 1) * half, :])
            out_ref[h * 2 + core, 2 * residues : 2 * residues + half, :] = high
            out_ref[h * 2 + core, 2 * residues + half : 3 * residues, :] = low


def lanes_of(blocks_ref, row, residues):
    count = blocks_ref.shape[0] // 2
    planes = [
        blocks_ref[p * count : (p + 1) * count, row : row + residues, :].reshape(-1, LANES)
        for p in range(2)
    ]
    return jnp.concatenate(planes, axis=1)


def score_kernel(
    residues, left_row, right_row, place_ref, own_ref, other_ref, mine_ref, sent_ref
):
    core, half = place_ref[0], place_ref[1]
    count = own_ref.shape[0] // 2
    part = residues // 2
    right = jnp.concatenate(
        [lanes_of(own_ref, right_row, residues), lanes_of(other_ref, right_row, residues)], axis=1
    )
    for which, ref in ((half, mine_ref), (1 - half, sent_ref)):
        left = []
        for k in range(count // 2):
            block = which * (count // 2) + k
            rows = pl.ds(pl.multiple_of(left_row + core * part, part), part)
            left.append(
                jnp.concatenate(
                    [
                        r[p * count + block, rows, :]
                        for r in (own_ref, other_ref)
                        for p in range(2)
                    ],
                    axis=1,
                )
            )
        ref[...] = f32_dot(jnp.concatenate(left, axis=0), right, NT).astype(ref.dtype)


def bias_kernel(row, place_ref, blocks_ref, mine_ref, sent_ref):
    half = place_ref[1]
    count = blocks_ref.shape[0] // 2
    for which, ref in ((half, mine_ref), (1 - half, sent_ref)):
        for p in range(2):
            for k in range(count // 2):
                block = p * count + which * (count // 2) + k
                ref[p * (count // 2) + k] = blocks_ref[block, row:, :]


def softmax_kernel(
    place_ref, logit_ref, other_ref, bias_ref, bias_other_ref, out_ref, low_ref
):
    half = place_ref[1]
    count, part = bias_ref.shape[0] // 2, bias_ref.shape[1] // 2
    out_ref[...] = logit_ref[...] + other_ref[...]
    for which, ref in ((half, bias_ref), (1 - half, bias_other_ref)):
        for p in range(2):
            columns = pl.ds(pl.multiple_of((which * 2 + p) * LANES, LANES), LANES)
            for k in range(count):
                high = ref[p * count + k, :part, :].astype(jnp.float32)
                low = ref[p * count + k, part:, :].astype(jnp.float32)
                out_ref[k * part : (k + 1) * part, columns] += high + low
    logits = out_ref[...]
    lifted = jnp.exp(logits - jnp.max(logits, axis=-1, keepdims=True))
    softmax_out = lifted / jnp.sum(lifted, axis=-1, keepdims=True)
    out_ref[...] = softmax_out
    low_ref[...] = softmax_out.astype(jnp.bfloat16)


def softmax_gradient_kernel(softmax_ref, grad_ref, other_ref, out_ref):
    softmax_out = softmax_ref[...]
    grad_probs = grad_ref[...] + other_ref[...].astype(jnp.float32)
    row_dot = jnp.sum(softmax_out * grad_probs, axis=-1, keepdims=True)
    out_ref[...] = (softmax_out * (grad_probs - row_dot)).astype(jnp.bfloat16)


def product_kernel(
    residues, scale, first_row, second_row, with_share,
    place_ref, own_ref, far_ref, near_ref, corner_ref, blocks_ref, out_ref, whole_ref,
):
    core, half = place_ref[0], place_ref[1]
    count = blocks_ref.shape[0] // 2
    part = residues // 2
    quarters = (
        (own_ref, core, half), (far_ref, core, 1 - half),
        (near_ref, 1 - core, half), (corner_ref, 1 - core, 1 - half),
    )
    for ref, c, z in quarters:
        for k in range(count // 2):
            start = (z * (count // 2) + k) * residues + c * part
            whole_ref[pl.ds(pl.multiple_of(start, part), part), :] = ref[k * part : (k + 1) * part, :]
    whole = whole_ref[...]
    if with_share:
        for p in range(2):
            columns = pl.ds(pl.multiple_of((half * 2 + p) * LANES, LANES), LANES)
            for q in range(count):
                rows = pl.ds(pl.multiple_of(q * residues + core * part, part), part)
                out_ref[p * count + q, 2 * residues : 2 * residues + part, :] = whole_ref[rows, columns]
    first = f32_dot(whole, lanes_of(blocks_ref, first_row, residues)) * scale
    second = f32_dot(whole, lanes_of(blocks_ref, second_row, residues), TN)
    for row, product in ((0, first), (residues, second)):
        for p in range(2):
            out_ref[p * count : (p + 1) * count, row : row + residues, :] = (
                product[:, p * LANES : (p + 1) * LANES]
                .astype(jnp.bfloat16)
                .reshape(count, residues, LANES)
            )


def share_of(blocks_ref, row, part, heads):
    return jnp.concatenate(
        [
            blocks_ref[:, row : row + part, :]
            .astype(jnp.float32)
            .reshape(heads, 2 * part, LANES)
        ],
        axis=0,
    )


def attended_weight_kernel(
    x_ref, grad_ref, wc_ref, wo_ref, blocks_ref, updated_ref, projected_ref, normed_ref, sums_ref
):
    residues, width = x_ref.shape[1], x_ref.shape[2]
    tiles = width // LANES
    normed = normalized(x_ref)[0].astype(jnp.bfloat16)
    normed_ref[...] = normed
    gate = gate_of(f32_dot(normed, wc_ref[:, 3 * width :]))
    grad = grad_ref[...].reshape(-1, width)
    grad_gated = f32_dot(grad, wo_ref[...], NT)
    attended = unpack_heads(blocks_ref, 0, residues, tiles)
    gated = (gate * attended).astype(jnp.bfloat16)
    updated_ref[...] = f32_dot(gated, wo_ref[...]).astype(jnp.bfloat16).reshape(updated_ref.shape)
    projected_ref[:, :width] = unpack_heads(blocks_ref, residues, residues, tiles).astype(
        jnp.bfloat16
    )
    projected_ref[:, width:] = (grad_gated * attended * gate * (1.0 - gate)).astype(jnp.bfloat16)
    sums_ref[:, : 2 * width] = f32_dot(normed, projected_ref[...], TN).astype(jnp.bfloat16)
    sums_ref[:, 2 * width :] = f32_dot(gated, grad, TN).astype(jnp.bfloat16)


def query_weight_kernel(
    place_ref, normed_ref, blocks_ref, pair_weight_ref, attended_sums_ref,
    projected_ref, keep_ref, send_ref, sums_ref,
):
    width = normed_ref.shape[1]
    tiles, residues = width // LANES, (blocks_ref.shape[1] * 2) // 5
    core = place_ref[0]
    for t in range(2):
        projected_ref[:, t * width : (t + 1) * width] = unpack_heads(
            blocks_ref, t * residues, residues, tiles
        ).astype(jnp.bfloat16)
    sums_ref[:, : 2 * width] = f32_dot(normed_ref[...], projected_ref[...], TN).astype(
        jnp.bfloat16
    )
    sums_ref[:, 2 * width : 5 * width] = attended_sums_ref[...]
    heads, channels = pair_weight_ref.shape
    rows = sums_ref.shape[0] // heads
    first = lax.broadcasted_iota(jnp.int32, (rows, channels), 0) == 0
    for h in range(heads):
        row = jnp.broadcast_to(pair_weight_ref[h : h + 1], (rows, channels))
        sums_ref[h * rows : (h + 1) * rows, 5 * width :] = jnp.where(first, row, 0.0).astype(
            jnp.bfloat16
        )
    for which, ref in ((core, keep_ref), (1 - core, send_ref)):
        for block in range(heads // 2):
            start = pl.multiple_of((2 * block + which) * rows, rows)
            ref[block] = sums_ref[pl.ds(start, rows), :]


def core_sum_kernel(place_ref, keep_ref, other_ref, own_ref, *send_refs):
    chip = place_ref[2]
    for flip, ref in enumerate((own_ref, *send_refs)):
        block = jnp.bitwise_xor(chip, flip)
        total = keep_ref[block].astype(jnp.float32) + other_ref[block].astype(jnp.float32)
        ref[...] = total.astype(ref.dtype)


def plane_sum_kernel(own_ref, *refs):
    total = own_ref[...]
    for ref in refs[:-1]:
        total += ref[...].astype(jnp.float32)
    refs[-1][...] = total.astype(refs[-1].dtype)


def pair_weight_kernel(blocks_ref, pair_ref, mean_ref, spread_ref, out_ref, share_ref):
    heads, part = share_ref.shape[0], pair_ref.shape[0] // 2
    share_ref[...] = share_of(blocks_ref, blocks_ref.shape[1] - part, part, heads)

    def rows(step, carry):
        total, shift = carry
        for k in range(8):
            i = step * 8 + k
            scaled = share_ref[:, i, :] * spread_ref[pl.ds(i, 1), :]
            high, low = two_terms(scaled)
            total += f32_dot(jnp.concatenate([high, low], axis=0), pair_ref[i])
            shift += (high.astype(jnp.float32) + low.astype(jnp.float32)) * mean_ref[pl.ds(i, 1), :]
        return total, shift

    channels = pair_ref.shape[2]
    total, shift = lax.fori_loop(
        0,
        pair_ref.shape[0] // 8,
        rows,
        (jnp.zeros((2 * heads, channels), jnp.float32), jnp.zeros((heads, LANES), jnp.float32)),
    )
    out_ref[...] = total[:heads] + total[heads:] - jnp.sum(shift, axis=1, keepdims=True)


def alignment_kernel(x_ref, wc_ref, query_key_ref, value_gate_ref, out_ref):
    normed, spread = normalized(x_ref)
    width = x_ref.shape[2]
    gradient = f32_dot(query_key_ref[...], wc_ref[:, : 2 * width], NT) + f32_dot(
        value_gate_ref[...], wc_ref[:, 2 * width :], NT
    )
    out_ref[...] = (
        layer_norm_backward(gradient, normed, spread).astype(jnp.bfloat16).reshape(out_ref.shape)
    )


def pair_kernel(blocks_row, blocks_ref, pair_ref, weight_ref, bias_ref, mean_ref, spread_ref, out_ref, share_ref):
    heads, channels = weight_ref.shape
    part = pair_ref.shape[0] // 2
    share_ref[...] = share_of(blocks_ref, blocks_row, part, heads)
    first, second = two_terms(centred(weight_ref[...]))
    zero = jnp.zeros((heads, channels), jnp.bfloat16)
    top = lax.broadcasted_iota(jnp.int32, (heads, channels), 0) < 2
    ones = jnp.where(top, 1.0, 0.0).astype(jnp.bfloat16)
    right = jnp.concatenate(
        [
            jnp.concatenate([first, first, second, ones, zero], axis=0),
            jnp.concatenate([zero, zero, zero, zero, ones], axis=0),
        ],
        axis=1,
    )
    row = lax.broadcasted_iota(jnp.int32, (heads, LANES), 0)

    def rows_of_two(value):
        high, low = two_terms(value)
        high, low = high.astype(jnp.float32), low.astype(jnp.float32)
        return jnp.where(row == 0, high, jnp.where(row == 1, low, 0.0)).astype(jnp.bfloat16)

    def rows(step, carry):
        for k in range(8):
            i = step * 8 + k
            gradient = share_ref[:, i, :]
            spread = spread_ref[pl.ds(i, 1), :]
            cross = jnp.sum(gradient * bias_ref[:, i, :], axis=0, keepdims=True) / channels
            slope = spread * spread * cross
            high, low = two_terms(gradient * spread)
            left = jnp.concatenate(
                [
                    high, low, high,
                    rows_of_two(jnp.broadcast_to(slope * mean_ref[pl.ds(i, 1), :], row.shape)),
                    rows_of_two(jnp.broadcast_to(slope, row.shape)),
                ],
                axis=0,
            )
            terms = f32_dot(left, right, TN)
            entries = pair_ref[i].astype(jnp.float32)
            out_ref[i] = (terms[:, :channels] - terms[:, channels:] * entries).astype(jnp.bfloat16)
        return carry

    lax.fori_loop(0, pair_ref.shape[0] // 8, rows, 0)


def output_kernel(parts_ref, combined_ref, out_weight_ref, pair_weight_ref):
    width = combined_ref.shape[0]
    rows = parts_ref.shape[1]
    for h in range(parts_ref.shape[0]):
        block = slice(h * rows, (h + 1) * rows)
        part = parts_ref[h].astype(jnp.float32)
        combined_ref[block, :] = part[:, : 4 * width]
        out_weight_ref[block, :] = part[:, 4 * width : 5 * width]
        pair_weight_ref[h : h + 1, :] = part[:1, 5 * width :]


def call(kernel, outs, *args, scratch=(), place=None, flops=0, after=(), outside=0, late=0):
    whole, anywhere = pl.BlockSpec(memory_space=pltpu.VMEM), pl.BlockSpec(memory_space=pl.ANY)
    specs = [anywhere] * outside + [whole] * (len(args) - outside)
    ahead = () if place is None else (place,)
    shapes = [jax.ShapeDtypeStruct(*o) for o in outs]
    moved = sum(math.prod(a.shape) * a.dtype.itemsize for a in list(args) + shapes)
    first = len(ahead) + len(args)
    last = first + len(after)

    def wrapped(*refs):
        given, rest = list(refs[:first]), refs[last:]
        if outside:
            *rest, arrived = rest
            held = rest[len(rest) - outside :]
            rest = rest[: len(rest) - outside]
            copies = []
            for k in range(outside):
                copies.append(
                    pltpu.make_async_copy(given[len(ahead) + k], held[k], arrived.at[k])
                )
                given[len(ahead) + k] = held[k]
            for copy in copies:
                copy.start()
            for copy in copies[: outside - late]:
                copy.wait()
            if late:
                given.insert(0, lambda: [copy.wait() for copy in copies[outside - late :]])
        kernel(*given, *rest)

    held = [pltpu.VMEM(a.shape, a.dtype) for a in args[:outside]]
    if outside:
        held.append(pltpu.SemaphoreType.DMA((outside,)))
    return pl.pallas_call(
        wrapped,
        out_shape=shapes,
        in_specs=[pl.BlockSpec(memory_space=pltpu.SMEM)] * len(ahead)
        + specs
        + [anywhere] * len(after),
        out_specs=[whole] * len(shapes),
        scratch_shapes=[*scratch, *held],
        compiler_params=pltpu.CompilerParams(
            vmem_limit_bytes=ARGUMENT_VMEM_LIMIT if outside else VMEM_LIMIT
        ),
        cost_estimate=pl.CostEstimate(flops=flops, bytes_accessed=moved, transcendentals=0),
    )(*ahead, *args, *after)


def swapped(mine, axis_name, distance):
    size = lax.axis_size(axis_name)
    return lax.ppermute(mine, axis_name, [(a, a ^ distance) for a in range(size)])


def fits_heads(alignment_rows, pair_entries, pair_weight):
    channels, heads = pair_weight.shape
    return (
        lax.axis_size("seq") == 4
        and lax.axis_size("res") == heads == 8
        and alignment_rows.shape[0] == 2 * SLOTS
        and alignment_rows.shape[1] == pair_entries.shape[0] == 64
        and alignment_rows.shape[2] == 2 * LANES
        and pair_entries.shape[1] == channels == LANES
    )


def head_body(
    alignment_rows, pair_entries, combined_weight, output_weight, pair_weight, updated_gradient
):
    sequences, residues, width = alignment_rows.shape
    channels, heads = pair_weight.shape
    tokens = sequences * residues
    seq_size, res_size = lax.axis_size("seq"), lax.axis_size("res")
    seq_half = seq_size // 2
    total = residues * res_size
    group = 2 * res_size
    groups = [[g * group + k for k in range(group)] for g in range(seq_half)]
    scale = 1.0 / math.sqrt(width // heads * sequences * seq_size)
    res_index, seq_index = lax.axis_index("res"), lax.axis_index("seq")
    place = jnp.stack([res_index % 2, seq_index // 2, res_index // 2]).astype(jnp.int32)
    bf16, f32 = jnp.bfloat16, jnp.float32

    def across(blocks):
        return lax.all_to_all(blocks, ("seq", "res"), 0, 0, axis_index_groups=groups, tiled=True)

    x, grad, wc, wo = alignment_rows, updated_gradient, combined_weight, output_weight
    (query_blocks,) = call(
        functools.partial(query_kernel, scale), [((group, 2 * residues, LANES), bf16)], x, wc,
        flops=8 * tokens * width * width, outside=2,
    )
    query_blocks = across(query_blocks)
    value_blocks, bias, mean, spread = call(
        value_kernel,
        [
            ((group, 3 * residues, LANES), bf16),
            ((heads, residues, LANES), f32),
            ((residues, LANES), f32),
            ((residues, LANES), f32),
        ],
        x, grad, wc, wo, pair_entries, pair_weight.T,
        flops=8 * tokens * width * width, outside=5, late=1,
    )
    query_blocks, value_blocks = lax.optimization_barrier((query_blocks, value_blocks))
    value_blocks = across(value_blocks)

    def scores(blocks, left_row, right_row, kind):
        return call(
            functools.partial(score_kernel, residues, left_row, right_row),
            [((total // 4, total), f32), ((total // 4, total), kind)],
            blocks, swapped(blocks, "res", 1),
            place=place, flops=2 * total * total * width,
        )

    logit_mine, logit_sent = scores(query_blocks, 0, residues, f32)
    logit_other = swapped(logit_sent, "seq", seq_half)
    value_blocks, logit_other = lax.optimization_barrier((value_blocks, logit_other))
    quarter = (total // 4, total)
    bias_half = ((group // 2, residues, LANES), bf16)
    bias_mine, bias_sent = call(
        functools.partial(bias_kernel, 2 * residues), [bias_half, bias_half], value_blocks,
        place=place,
    )
    bias_other = swapped(bias_sent, "seq", seq_half)
    grad_mine, grad_sent = scores(value_blocks, residues, 0, bf16)
    grad_other = swapped(grad_sent, "seq", seq_half)
    bias_other, grad_mine = lax.optimization_barrier((bias_other, grad_mine))
    softmax_out, probs = call(
        softmax_kernel, [(quarter, f32), (quarter, bf16)],
        logit_mine, logit_other, bias_mine, bias_other,
        place=place, flops=total * total,
    )

    def products(mine, blocks, first_row, second_row, with_share, factor):
        rows = 2 * residues + (residues // 2 if with_share else 0)
        far = swapped(mine, "seq", seq_half)
        (out,) = call(
            functools.partial(
                product_kernel, residues, factor, first_row, second_row, with_share
            ),
            [((group, rows, LANES), bf16)],
            mine, far, swapped(mine, "res", 1), swapped(far, "res", 1), blocks,
            scratch=[pltpu.VMEM((total, total), bf16)],
            place=place, flops=4 * total * total * width,
        )
        return out

    attended = products(probs, value_blocks, 0, residues, False, 1.0)
    (grad_logits,) = call(
        softmax_gradient_kernel, [(quarter, bf16)], softmax_out, grad_mine, grad_other,
        flops=total * total,
    )
    attended, grad_logits = lax.optimization_barrier((attended, grad_logits))
    attended_blocks = across(attended)
    grad_sums = products(grad_logits, query_blocks, residues, 0, True, scale)
    grad_sums, attended_blocks = lax.optimization_barrier((grad_sums, attended_blocks))
    grad_blocks = across(grad_sums)

    updated, value_gate, normed, attended_sums = call(
        attended_weight_kernel,
        [
            (x.shape, bf16),
            ((tokens, 2 * width), bf16),
            ((tokens, width), bf16),
            ((width, 3 * width), bf16),
        ],
        x, grad, wc, wo, attended_blocks,
        flops=14 * tokens * width * width, outside=4,
    )
    share = pltpu.VMEM((heads, residues, LANES), f32)
    (pair_weight_part,) = call(
        pair_weight_kernel, [((heads, channels), f32)],
        grad_blocks, pair_entries, mean, spread,
        scratch=[share], flops=4 * tokens * width * width,
    )
    columns = 5 * width + channels
    rows = width // res_size
    part_rows = ((res_size // 2, rows, columns), bf16)
    query_key, keep, send = call(
        query_weight_kernel,
        [((tokens, 2 * width), bf16), part_rows, part_rows],
        normed, grad_blocks, pair_weight_part, attended_sums,
        scratch=[pltpu.VMEM((width, columns), bf16)],
        place=place, flops=4 * tokens * width * width,
    )
    own, *sent = call(
        core_sum_kernel,
        [((rows, columns), f32)] + [((rows, columns), bf16)] * 3,
        keep, swapped(send, "res", 1), place=place,
    )
    received = [swapped(t, "res", 2 * flip) for flip, t in enumerate(sent, 1)]
    (pair_gradient,) = call(
        functools.partial(pair_kernel, 2 * residues),
        [(pair_entries.shape, bf16)],
        grad_blocks, pair_entries, pair_weight.T, bias, mean, spread,
        scratch=[share], flops=8 * tokens * width * width,
    )
    received, pair_gradient = lax.optimization_barrier((received, pair_gradient))
    (part,) = call(plane_sum_kernel, [((rows, columns), bf16)], own, *received)
    (alignment_gradient,) = call(
        alignment_kernel, [(x.shape, bf16)], x, wc, query_key, value_gate,
        flops=8 * tokens * width * width,
    )

    def added(mine, other):
        return (mine.astype(f32) + other.astype(f32)).astype(bf16)

    part = added(part, swapped(part, "seq", 1))
    part = added(part, swapped(part, "seq", seq_half))
    combined_gradient, output_gradient, pair_weight_gradient = call(
        output_kernel,
        [(wc.shape, f32), (wo.shape, f32), ((heads, channels), f32)],
        lax.all_gather(part, "res", axis=0),
    )
    return (
        updated,
        alignment_gradient,
        pair_gradient,
        combined_gradient,
        output_gradient,
        pair_weight_gradient.T,
    )


def body(alignment_rows, pair_entries, combined_weight, output_weight, pair_weight, updated_gradient):
    chosen = head_body if fits_heads(alignment_rows, pair_entries, pair_weight) else gathered_body
    return chosen(
        alignment_rows, pair_entries, combined_weight, output_weight, pair_weight, updated_gradient
    )


def solution(mesh):
    return jax.shard_map(
        body,
        mesh=mesh,
        in_specs=(
            P("seq", "res", None),
            P("res", "seq", None),
            P(),
            P(),
            P(),
            P("seq", "res", None),
        ),
        out_specs=(
            P("seq", "res", None),
            P("seq", "res", None),
            P("res", "seq", None),
            P(),
            P(),
            P(),
        ),
        check_vma=False,
    )
```

```python
import functools
import math

import jax
import jax.numpy as jnp
from jax import lax
from jax.experimental import pallas as pl
from jax.experimental.pallas import tpu as pltpu
from jax.sharding import PartitionSpec as P

eps_norm = 1e-05


def layer_normalize(values):
    values = values.astype(jnp.float32)
    center = values - jnp.mean(values, axis=-1, keepdims=True)
    broadcast_pair = lax.rsqrt(jnp.mean(center * center, axis=-1, keepdims=True) + eps_norm)
    return (center * broadcast_pair, broadcast_pair)


def layer_norm_backward(normalized_gradient, normalized_rows, broadcast_pair):
    mean_grad = jnp.mean(normalized_gradient, axis=-1, keepdims=True)
    mean_cross = jnp.mean(normalized_gradient * normalized_rows, axis=-1, keepdims=True)
    return broadcast_pair * (normalized_gradient - mean_grad - normalized_rows * mean_cross)


def split_heads(tensor, head_count):
    return tensor.reshape(
        tensor.shape[0], tensor.shape[1], head_count, tensor.shape[2] // head_count
    )


def merge_heads(tensor):
    return tensor.reshape(tensor.shape[0], tensor.shape[1], tensor.shape[2] * tensor.shape[3])


def gathered_body(
    alignment_rows, pair_entries, combined_weight, output_weight, pair_weight, updated_gradient
):
    sequence_count, residue_count, alignment_width = alignment_rows.shape
    head_count = pair_weight.shape[1]
    query_width = output_weight.shape[0]
    head_dim = query_width // head_count
    column_count = pair_entries.shape[1]
    token_count = sequence_count * residue_count
    score_scale = 1.0 / math.sqrt(head_dim * sequence_count * lax.axis_size("seq"))
    normalized_rows, broadcast_pair = layer_normalize(alignment_rows)
    normalized_rows_backward = normalized_rows.astype(jnp.bfloat16).reshape(
        token_count, alignment_width
    )
    projected = jnp.dot(
        normalized_rows_backward, combined_weight, preferred_element_type=jnp.float32
    ).reshape(sequence_count, residue_count, 4 * query_width)
    queries = (projected[..., :query_width] * score_scale).astype(jnp.bfloat16)
    key_rows = projected[..., query_width : 2 * query_width].astype(jnp.bfloat16)
    value_rows = projected[..., 2 * query_width : 3 * query_width].astype(jnp.bfloat16)
    gate_open = jax.nn.sigmoid(projected[..., 3 * query_width :])
    all_keys, all_values = (
        lax.all_gather(key_rows, "res", axis=1, tiled=True),
        lax.all_gather(value_rows, "res", axis=1, tiled=True),
    )
    query_heads = split_heads(queries, head_count)
    key_heads = split_heads(all_keys, head_count)
    value_heads = split_heads(all_values, head_count)
    score_terms = jnp.einsum(
        "sihd,sjhd->hij", query_heads, key_heads, preferred_element_type=jnp.float32
    )
    pair_normed, pair_spread = layer_normalize(pair_entries)
    pair_bias = jnp.einsum("ijc,ch->hij", pair_normed, pair_weight, precision=lax.Precision.HIGHEST)
    col_start = lax.axis_index("seq") * column_count
    own_block = lax.dynamic_slice_in_dim(score_terms, col_start, column_count, 2) + pair_bias
    logits = lax.psum(lax.dynamic_update_slice_in_dim(score_terms, own_block, col_start, 2), "seq")
    row_top = jnp.max(logits, axis=-1, keepdims=True)
    lifted = jnp.exp(logits - row_top)
    softmax_out = lifted / jnp.sum(lifted, axis=-1, keepdims=True)
    softmax_low = softmax_out.astype(jnp.bfloat16)
    attended = merge_heads(
        jnp.einsum("hij,sjhd->sihd", softmax_low, value_heads, preferred_element_type=jnp.float32)
    )
    gated_out = (gate_open * attended).astype(jnp.bfloat16)
    flattened_gated = gated_out.reshape(token_count, query_width)
    updated = (
        jnp.dot(flattened_gated, output_weight, preferred_element_type=jnp.float32)
        .astype(jnp.bfloat16)
        .reshape(sequence_count, residue_count, alignment_width)
    )
    flattened_gradient = updated_gradient.reshape(token_count, alignment_width)
    grad_gated = jnp.dot(
        flattened_gradient, output_weight.T, preferred_element_type=jnp.float32
    ).reshape(sequence_count, residue_count, query_width)
    out_local = jnp.dot(flattened_gated.T, flattened_gradient, preferred_element_type=jnp.float32)
    grad_attended = (grad_gated * gate_open).astype(jnp.bfloat16)
    grad_gate_logit = grad_gated * attended * gate_open * (1.0 - gate_open)
    attended_grad_heads = split_heads(grad_attended, head_count)
    grad_terms = jnp.einsum(
        "sihd,sjhd->hij", attended_grad_heads, value_heads, preferred_element_type=jnp.float32
    )
    grad_probs = lax.psum(grad_terms, "seq")
    row_dot = jnp.sum(softmax_out * grad_probs, axis=-1, keepdims=True)
    grad_logits = softmax_out * (grad_probs - row_dot)
    grad_logits_b = grad_logits.astype(jnp.bfloat16)
    logit_share = lax.dynamic_slice_in_dim(grad_logits, col_start, column_count, 2)
    grad_query_heads = (
        jnp.einsum("hij,sjhd->sihd", grad_logits_b, key_heads, preferred_element_type=jnp.float32)
        * score_scale
    )
    key_part = jnp.einsum(
        "hij,sihd->jshd", grad_logits_b, query_heads, preferred_element_type=jnp.float32
    )
    value_part = jnp.einsum(
        "hij,sihd->jshd", softmax_low, attended_grad_heads, preferred_element_type=jnp.float32
    )
    summed = lax.psum_scatter(
        jnp.concatenate([merge_heads(key_part), merge_heads(value_part)], axis=-1),
        "res",
        scatter_dimension=0,
        tiled=True,
    )
    key_value_grads = jnp.transpose(summed, (1, 0, 2))
    projected_gradient = jnp.concatenate(
        [merge_heads(grad_query_heads), key_value_grads, grad_gate_logit], axis=-1
    )
    projected_gradient = projected_gradient.astype(jnp.bfloat16).reshape(
        token_count, 4 * query_width
    )
    qkvg_local = jnp.dot(
        normalized_rows_backward.T, projected_gradient, preferred_element_type=jnp.float32
    )
    normalized_gradient = jnp.dot(
        projected_gradient, combined_weight.T, preferred_element_type=jnp.float32
    ).reshape(sequence_count, residue_count, alignment_width)
    alignment_gradient = layer_norm_backward(
        normalized_gradient, normalized_rows, broadcast_pair
    ).astype(jnp.bfloat16)
    pair_w_local = jnp.einsum(
        "ijc,hij->ch", pair_normed, logit_share, precision=lax.Precision.HIGHEST
    )
    grad_pair_normed = jnp.einsum(
        "hij,ch->ijc", logit_share, pair_weight, precision=lax.Precision.HIGHEST
    )
    pair_gradient = layer_norm_backward(grad_pair_normed, pair_normed, pair_spread).astype(
        jnp.bfloat16
    )
    combined_weight_gradient, output_weight_gradient, pair_weight_gradient = lax.psum(
        (qkvg_local, out_local, pair_w_local), ("seq", "res")
    )
    return (
        updated,
        alignment_gradient,
        pair_gradient,
        combined_weight_gradient,
        output_weight_gradient,
        pair_weight_gradient,
    )


VMEM_LIMIT = 20 * 1024 * 1024
ARGUMENT_VMEM_LIMIT = 56 * 1024 * 1024
LANES = 128
SLOTS = 4
NT = (((1,), (1,)), ((), ()))
TN = (((0,), (0,)), ((), ()))


def f32_dot(left, right, dims=None):
    if dims is None:
        return jnp.dot(left, right, preferred_element_type=jnp.float32)
    return lax.dot_general(left, right, dims, preferred_element_type=jnp.float32)


def two_terms(values):
    high = values.astype(jnp.bfloat16)
    return high, (values - high.astype(jnp.float32)).astype(jnp.bfloat16)


def slot_select(pieces):
    slot = lax.broadcasted_iota(jnp.int32, pieces[0].shape, 1) // (LANES // SLOTS)
    result = pieces[0]
    for k in range(1, SLOTS):
        result = jnp.where(slot == k, pieces[k], result)
    return result


def pack_heads(out_ref, row, tensor, residues):
    for core in range(2):
        for tile in range(tensor.shape[1] // LANES):
            rolled = []
            for s in range(SLOTS):
                start = (core * SLOTS + s) * residues
                piece = tensor[start : start + residues, tile * LANES : (tile + 1) * LANES]
                rolled.append(pltpu.roll(piece, s * LANES // SLOTS, 1) if s else piece)
            for j in range(SLOTS):
                block = slot_select([rolled[(k - j) % SLOTS] for k in range(SLOTS)])
                out_ref[(tile * SLOTS + j) * 2 + core, row : row + residues, :] = block.astype(
                    jnp.bfloat16
                )


def unpack_heads(in_ref, row, residues, tiles):
    rows = []
    for core in range(2):
        for s in range(SLOTS):
            pieces = []
            for tile in range(tiles):
                blocks = [
                    in_ref[
                        (tile * SLOTS + (k - s) % SLOTS) * 2 + core, row : row + residues, :
                    ].astype(jnp.float32)
                    for k in range(SLOTS)
                ]
                block = slot_select(blocks)
                pieces.append(pltpu.roll(block, LANES - s * LANES // SLOTS, 1) if s else block)
            rows.append(jnp.concatenate(pieces, axis=1))
    return jnp.concatenate(rows, axis=0)


def normalized(x_ref):
    width = x_ref.shape[-1]
    values = x_ref[...].reshape(-1, width).astype(jnp.float32)
    return layer_normalize(values)


def gate_of(logits):
    return 1.0 / (1.0 + jnp.exp(-logits))


def value_kernel(x_ref, grad_ref, wc_ref, wo_ref, out_ref):
    residues, width = x_ref.shape[1], x_ref.shape[2]
    normed = normalized(x_ref)[0].astype(jnp.bfloat16)
    values = f32_dot(normed, wc_ref[:, 2 * width : 3 * width])
    gate = gate_of(f32_dot(normed, wc_ref[:, 3 * width :]))
    grad_gated = f32_dot(grad_ref[...].reshape(-1, width), wo_ref[...], NT)
    pack_heads(out_ref, 0, values, residues)
    pack_heads(out_ref, residues, grad_gated * gate, residues)


def centred(weight):
    return weight - jnp.mean(weight, axis=1, keepdims=True)


def query_kernel(
    scale, arrive, x_ref, wc_ref, pair_ref, weight_ref, out_ref, bias_ref, mean_ref, spread_ref
):
    residues, width = x_ref.shape[1], x_ref.shape[2]
    heads = weight_ref.shape[0]
    normed = normalized(x_ref)[0].astype(jnp.bfloat16)
    pack_heads(out_ref, 0, f32_dot(normed, wc_ref[:, :width]) * scale, residues)
    pack_heads(out_ref, residues, f32_dot(normed, wc_ref[:, width : 2 * width]), residues)

    arrive()
    columns, channels = pair_ref.shape[1], pair_ref.shape[2]
    weight = centred(weight_ref[...])
    first = weight.astype(jnp.bfloat16).astype(jnp.float32)
    second, third = two_terms(weight - first)
    share = jnp.full((heads, channels), 1.0 / channels, jnp.float32)
    right = jnp.concatenate(
        [
            first, second.astype(jnp.float32), third.astype(jnp.float32), share,
            jnp.zeros((channels - 4 * heads, channels), jnp.float32),
        ],
        axis=0,
    ).T
    row = lax.broadcasted_iota(jnp.int32, (channels, channels), 0)
    column = lax.broadcasted_iota(jnp.int32, (channels, channels), 1)
    less_mean = jnp.where(row == column, 1.0, 0.0) - 1.0 / channels
    right = jnp.concatenate([less_mean, right], axis=1).astype(jnp.bfloat16)
    shares = jnp.full((2 * channels, channels), 1.0 / channels, jnp.bfloat16)
    step_rows = 8
    lane = lax.broadcasted_iota(jnp.int32, (step_rows * columns, channels), 1)

    def rows(step, carry):
        start = pl.multiple_of(step * step_rows, step_rows)
        entries = pair_ref[pl.ds(start, step_rows)].reshape(step_rows * columns, channels)
        both = f32_dot(entries, right)
        center = both[:, :channels]
        variance = f32_dot(jnp.concatenate(two_terms(center * center), axis=1), shares)
        turned = jnp.where(lane < 4 * heads, both[:, channels:], variance).T
        spread = lax.rsqrt(turned[4 * heads : 5 * heads] + eps_norm)
        bias = spread * (turned[:heads] + turned[heads : 2 * heads] + turned[2 * heads : 3 * heads])
        for k in range(step_rows):
            lanes = slice(k * columns, (k + 1) * columns)
            bias_ref[:, start + k, :] = bias[:, lanes]
            mean_ref[pl.ds(start + k, 1), :] = turned[3 * heads : 3 * heads + 1, lanes]
            spread_ref[pl.ds(start + k, 1), :] = spread[:1, lanes]
        return carry

    lax.fori_loop(0, pair_ref.shape[0] // step_rows, rows, 0)
    half = residues // 2
    for h in range(heads):
        for core in range(2):
            high, low = two_terms(bias_ref[h, core * half : (core + 1) * half, :])
            out_ref[h * 2 + core, 2 * residues : 2 * residues + half, :] = high
            out_ref[h * 2 + core, 2 * residues + half : 3 * residues, :] = low


def lanes_of(blocks_ref, row, residues):
    count = blocks_ref.shape[0] // 2
    planes = [
        blocks_ref[p * count : (p + 1) * count, row : row + residues, :].reshape(-1, LANES)
        for p in range(2)
    ]
    return jnp.concatenate(planes, axis=1)


def score_kernel(
    residues, left_row, right_row, with_bias, place_ref, own_ref, other_ref, mine_ref, sent_ref
):
    core, half = place_ref[0], place_ref[1]
    count = own_ref.shape[0] // 2
    part = residues // 2
    right = jnp.concatenate(
        [lanes_of(own_ref, right_row, residues), lanes_of(other_ref, right_row, residues)], axis=1
    )
    for which, ref in ((half, mine_ref), (1 - half, sent_ref)):
        left = []
        for k in range(count // 2):
            block = which * (count // 2) + k
            rows = pl.ds(pl.multiple_of(left_row + core * part, part), part)
            left.append(
                jnp.concatenate(
                    [
                        r[p * count + block, rows, :]
                        for r in (own_ref, other_ref)
                        for p in range(2)
                    ],
                    axis=1,
                )
            )
        ref[...] = f32_dot(jnp.concatenate(left, axis=0), right, NT).astype(ref.dtype)
        if with_bias:
            for p in range(2):
                columns = pl.ds(pl.multiple_of((half * 2 + p) * LANES, LANES), LANES)
                for k in range(count // 2):
                    block = p * count + which * (count // 2) + k
                    high = own_ref[block, 2 * residues : 2 * residues + part, :]
                    low = own_ref[block, 2 * residues + part : 3 * residues, :]
                    bias = high.astype(jnp.float32) + low.astype(jnp.float32)
                    ref[k * part : (k + 1) * part, columns] += bias


def softmax_kernel(logit_ref, other_ref, out_ref, low_ref):
    logits = logit_ref[...] + other_ref[...]
    lifted = jnp.exp(logits - jnp.max(logits, axis=-1, keepdims=True))
    softmax_out = lifted / jnp.sum(lifted, axis=-1, keepdims=True)
    out_ref[...] = softmax_out
    low_ref[...] = softmax_out.astype(jnp.bfloat16)


def softmax_gradient_kernel(softmax_ref, grad_ref, other_ref, out_ref):
    softmax_out = softmax_ref[...]
    grad_probs = grad_ref[...] + other_ref[...].astype(jnp.float32)
    row_dot = jnp.sum(softmax_out * grad_probs, axis=-1, keepdims=True)
    out_ref[...] = (softmax_out * (grad_probs - row_dot)).astype(jnp.bfloat16)


def product_kernel(
    residues, scale, first_row, second_row, with_share,
    place_ref, own_ref, far_ref, near_ref, corner_ref, blocks_ref, out_ref, whole_ref,
):
    core, half = place_ref[0], place_ref[1]
    count = blocks_ref.shape[0] // 2
    part = residues // 2
    quarters = (
        (own_ref, core, half), (far_ref, core, 1 - half),
        (near_ref, 1 - core, half), (corner_ref, 1 - core, 1 - half),
    )
    for ref, c, z in quarters:
        for k in range(count // 2):
            start = (z * (count // 2) + k) * residues + c * part
            whole_ref[pl.ds(pl.multiple_of(start, part), part), :] = ref[k * part : (k + 1) * part, :]
    whole = whole_ref[...]
    if with_share:
        for p in range(2):
            columns = pl.ds(pl.multiple_of((half * 2 + p) * LANES, LANES), LANES)
            for q in range(count):
                rows = pl.ds(pl.multiple_of(q * residues + core * part, part), part)
                out_ref[p * count + q, 2 * residues : 2 * residues + part, :] = whole_ref[rows, columns]
    first = f32_dot(whole, lanes_of(blocks_ref, first_row, residues)) * scale
    second = f32_dot(whole, lanes_of(blocks_ref, second_row, residues), TN)
    for row, product in ((0, first), (residues, second)):
        for p in range(2):
            out_ref[p * count : (p + 1) * count, row : row + residues, :] = (
                product[:, p * LANES : (p + 1) * LANES]
                .astype(jnp.bfloat16)
                .reshape(count, residues, LANES)
            )


def share_of(blocks_ref, row, part, heads):
    return jnp.concatenate(
        [
            blocks_ref[:, row : row + part, :]
            .astype(jnp.float32)
            .reshape(heads, 2 * part, LANES)
        ],
        axis=0,
    )


def attended_weight_kernel(
    x_ref, grad_ref, wc_ref, wo_ref, blocks_ref, updated_ref, projected_ref, normed_ref, sums_ref
):
    residues, width = x_ref.shape[1], x_ref.shape[2]
    tiles = width // LANES
    normed = normalized(x_ref)[0].astype(jnp.bfloat16)
    normed_ref[...] = normed
    gate = gate_of(f32_dot(normed, wc_ref[:, 3 * width :]))
    grad = grad_ref[...].reshape(-1, width)
    grad_gated = f32_dot(grad, wo_ref[...], NT)
    attended = unpack_heads(blocks_ref, 0, residues, tiles)
    gated = (gate * attended).astype(jnp.bfloat16)
    updated_ref[...] = f32_dot(gated, wo_ref[...]).astype(jnp.bfloat16).reshape(updated_ref.shape)
    projected_ref[:, :width] = unpack_heads(blocks_ref, residues, residues, tiles).astype(
        jnp.bfloat16
    )
    projected_ref[:, width:] = (grad_gated * attended * gate * (1.0 - gate)).astype(jnp.bfloat16)
    sums_ref[:, : 2 * width] = f32_dot(normed, projected_ref[...], TN).astype(jnp.bfloat16)
    sums_ref[:, 2 * width :] = f32_dot(gated, grad, TN).astype(jnp.bfloat16)


def query_weight_kernel(
    place_ref, normed_ref, blocks_ref, pair_weight_ref, attended_sums_ref,
    projected_ref, keep_ref, send_ref, sums_ref,
):
    width = normed_ref.shape[1]
    tiles, residues = width // LANES, (blocks_ref.shape[1] * 2) // 5
    core = place_ref[0]
    for t in range(2):
        projected_ref[:, t * width : (t + 1) * width] = unpack_heads(
            blocks_ref, t * residues, residues, tiles
        ).astype(jnp.bfloat16)
    sums_ref[:, : 2 * width] = f32_dot(normed_ref[...], projected_ref[...], TN).astype(
        jnp.bfloat16
    )
    sums_ref[:, 2 * width : 5 * width] = attended_sums_ref[...]
    heads, channels = pair_weight_ref.shape
    rows = sums_ref.shape[0] // heads
    first = lax.broadcasted_iota(jnp.int32, (rows, channels), 0) == 0
    for h in range(heads):
        row = jnp.broadcast_to(pair_weight_ref[h : h + 1], (rows, channels))
        sums_ref[h * rows : (h + 1) * rows, 5 * width :] = jnp.where(first, row, 0.0).astype(
            jnp.bfloat16
        )
    for which, ref in ((core, keep_ref), (1 - core, send_ref)):
        for block in range(heads // 2):
            start = pl.multiple_of((2 * block + which) * rows, rows)
            ref[block] = sums_ref[pl.ds(start, rows), :]


def core_sum_kernel(place_ref, keep_ref, other_ref, own_ref, *send_refs):
    chip = place_ref[2]
    for flip, ref in enumerate((own_ref, *send_refs)):
        block = jnp.bitwise_xor(chip, flip)
        total = keep_ref[block].astype(jnp.float32) + other_ref[block].astype(jnp.float32)
        ref[...] = total.astype(ref.dtype)


def plane_sum_kernel(own_ref, *refs):
    total = own_ref[...]
    for ref in refs[:-1]:
        total += ref[...].astype(jnp.float32)
    refs[-1][...] = total.astype(refs[-1].dtype)


def pair_weight_kernel(blocks_ref, pair_ref, mean_ref, spread_ref, out_ref, share_ref):
    heads, part = share_ref.shape[0], pair_ref.shape[0] // 2
    share_ref[...] = share_of(blocks_ref, blocks_ref.shape[1] - part, part, heads)

    def rows(step, carry):
        total, shift = carry
        for k in range(8):
            i = step * 8 + k
            scaled = share_ref[:, i, :] * spread_ref[pl.ds(i, 1), :]
            high, low = two_terms(scaled)
            total += f32_dot(jnp.concatenate([high, low], axis=0), pair_ref[i])
            shift += (high.astype(jnp.float32) + low.astype(jnp.float32)) * mean_ref[pl.ds(i, 1), :]
        return total, shift

    channels = pair_ref.shape[2]
    total, shift = lax.fori_loop(
        0,
        pair_ref.shape[0] // 8,
        rows,
        (jnp.zeros((2 * heads, channels), jnp.float32), jnp.zeros((heads, LANES), jnp.float32)),
    )
    out_ref[...] = total[:heads] + total[heads:] - jnp.sum(shift, axis=1, keepdims=True)


def alignment_kernel(x_ref, wc_ref, query_key_ref, value_gate_ref, out_ref):
    normed, spread = normalized(x_ref)
    width = x_ref.shape[2]
    gradient = f32_dot(query_key_ref[...], wc_ref[:, : 2 * width], NT) + f32_dot(
        value_gate_ref[...], wc_ref[:, 2 * width :], NT
    )
    out_ref[...] = (
        layer_norm_backward(gradient, normed, spread).astype(jnp.bfloat16).reshape(out_ref.shape)
    )


def pair_kernel(blocks_row, blocks_ref, pair_ref, weight_ref, bias_ref, mean_ref, spread_ref, out_ref, share_ref):
    heads, channels = weight_ref.shape
    part = pair_ref.shape[0] // 2
    share_ref[...] = share_of(blocks_ref, blocks_row, part, heads)
    first, second = two_terms(centred(weight_ref[...]))
    zero = jnp.zeros((heads, channels), jnp.bfloat16)
    top = lax.broadcasted_iota(jnp.int32, (heads, channels), 0) < 2
    ones = jnp.where(top, 1.0, 0.0).astype(jnp.bfloat16)
    right = jnp.concatenate(
        [
            jnp.concatenate([first, first, second, ones, zero], axis=0),
            jnp.concatenate([zero, zero, zero, zero, ones], axis=0),
        ],
        axis=1,
    )
    row = lax.broadcasted_iota(jnp.int32, (heads, LANES), 0)

    def rows_of_two(value):
        high, low = two_terms(value)
        high, low = high.astype(jnp.float32), low.astype(jnp.float32)
        return jnp.where(row == 0, high, jnp.where(row == 1, low, 0.0)).astype(jnp.bfloat16)

    def rows(step, carry):
        for k in range(8):
            i = step * 8 + k
            gradient = share_ref[:, i, :]
            spread = spread_ref[pl.ds(i, 1), :]
            cross = jnp.sum(gradient * bias_ref[:, i, :], axis=0, keepdims=True) / channels
            slope = spread * spread * cross
            high, low = two_terms(gradient * spread)
            left = jnp.concatenate(
                [
                    high, low, high,
                    rows_of_two(jnp.broadcast_to(slope * mean_ref[pl.ds(i, 1), :], row.shape)),
                    rows_of_two(jnp.broadcast_to(slope, row.shape)),
                ],
                axis=0,
            )
            terms = f32_dot(left, right, TN)
            entries = pair_ref[i].astype(jnp.float32)
            out_ref[i] = (terms[:, :channels] - terms[:, channels:] * entries).astype(jnp.bfloat16)
        return carry

    lax.fori_loop(0, pair_ref.shape[0] // 8, rows, 0)


def output_kernel(parts_ref, combined_ref, out_weight_ref, pair_weight_ref):
    width = combined_ref.shape[0]
    rows = parts_ref.shape[1]
    for h in range(parts_ref.shape[0]):
        block = slice(h * rows, (h + 1) * rows)
        part = parts_ref[h].astype(jnp.float32)
        combined_ref[block, :] = part[:, : 4 * width]
        out_weight_ref[block, :] = part[:, 4 * width : 5 * width]
        pair_weight_ref[h : h + 1, :] = part[:1, 5 * width :]


def call(kernel, outs, *args, scratch=(), place=None, flops=0, after=(), outside=0, late=0):
    whole, anywhere = pl.BlockSpec(memory_space=pltpu.VMEM), pl.BlockSpec(memory_space=pl.ANY)
    specs = [anywhere] * outside + [whole] * (len(args) - outside)
    ahead = () if place is None else (place,)
    shapes = [jax.ShapeDtypeStruct(*o) for o in outs]
    moved = sum(math.prod(a.shape) * a.dtype.itemsize for a in list(args) + shapes)
    first = len(ahead) + len(args)
    last = first + len(after)

    def wrapped(*refs):
        given, rest = list(refs[:first]), refs[last:]
        if outside:
            *rest, arrived = rest
            held = rest[len(rest) - outside :]
            rest = rest[: len(rest) - outside]
            copies = []
            for k in range(outside):
                copies.append(
                    pltpu.make_async_copy(given[len(ahead) + k], held[k], arrived.at[k])
                )
                given[len(ahead) + k] = held[k]
            for copy in copies:
                copy.start()
            for copy in copies[: outside - late]:
                copy.wait()
            if late:
                given.insert(0, lambda: [copy.wait() for copy in copies[outside - late :]])
        kernel(*given, *rest)

    held = [pltpu.VMEM(a.shape, a.dtype) for a in args[:outside]]
    if outside:
        held.append(pltpu.SemaphoreType.DMA((outside,)))
    return pl.pallas_call(
        wrapped,
        out_shape=shapes,
        in_specs=[pl.BlockSpec(memory_space=pltpu.SMEM)] * len(ahead)
        + specs
        + [anywhere] * len(after),
        out_specs=[whole] * len(shapes),
        scratch_shapes=[*scratch, *held],
        compiler_params=pltpu.CompilerParams(
            vmem_limit_bytes=ARGUMENT_VMEM_LIMIT if outside else VMEM_LIMIT
        ),
        cost_estimate=pl.CostEstimate(flops=flops, bytes_accessed=moved, transcendentals=0),
    )(*ahead, *args, *after)


def swapped(mine, axis_name, distance):
    size = lax.axis_size(axis_name)
    return lax.ppermute(mine, axis_name, [(a, a ^ distance) for a in range(size)])


def fits_heads(alignment_rows, pair_entries, pair_weight):
    channels, heads = pair_weight.shape
    return (
        lax.axis_size("seq") == 4
        and lax.axis_size("res") == heads == 8
        and alignment_rows.shape[0] == 2 * SLOTS
        and alignment_rows.shape[1] == pair_entries.shape[0] == 64
        and alignment_rows.shape[2] == 2 * LANES
        and pair_entries.shape[1] == channels == LANES
    )


def head_body(
    alignment_rows, pair_entries, combined_weight, output_weight, pair_weight, updated_gradient
):
    sequences, residues, width = alignment_rows.shape
    channels, heads = pair_weight.shape
    tokens = sequences * residues
    seq_size, res_size = lax.axis_size("seq"), lax.axis_size("res")
    seq_half = seq_size // 2
    total = residues * res_size
    group = 2 * res_size
    groups = [[g * group + k for k in range(group)] for g in range(seq_half)]
    scale = 1.0 / math.sqrt(width // heads * sequences * seq_size)
    res_index, seq_index = lax.axis_index("res"), lax.axis_index("seq")
    place = jnp.stack([res_index % 2, seq_index // 2, res_index // 2]).astype(jnp.int32)
    bf16, f32 = jnp.bfloat16, jnp.float32

    def across(blocks):
        return lax.all_to_all(blocks, ("seq", "res"), 0, 0, axis_index_groups=groups, tiled=True)

    x, grad, wc, wo = alignment_rows, updated_gradient, combined_weight, output_weight
    query_blocks, bias, mean, spread = call(
        functools.partial(query_kernel, scale),
        [
            ((group, 3 * residues, LANES), bf16),
            ((heads, residues, LANES), f32),
            ((residues, LANES), f32),
            ((residues, LANES), f32),
        ],
        x, wc, pair_entries, pair_weight.T,
        flops=8 * tokens * width * width, outside=3, late=1,
    )
    query_blocks = across(query_blocks)
    def scores(blocks, left_row, right_row, with_bias, kind):
        return call(
            functools.partial(score_kernel, residues, left_row, right_row, with_bias),
            [((total // 4, total), f32), ((total // 4, total), kind)],
            blocks, swapped(blocks, "res", 1),
            place=place, flops=2 * total * total * width,
        )

    (value_blocks,) = call(
        value_kernel, [((group, 2 * residues, LANES), bf16)], x, grad, wc, wo,
        flops=8 * tokens * width * width, outside=4,
    )
    logit_mine, logit_sent = scores(query_blocks, 0, residues, True, f32)
    value_blocks, logit_sent = lax.optimization_barrier((value_blocks, logit_sent))
    logit_other = swapped(logit_sent, "seq", seq_half)
    value_blocks = across(value_blocks)
    quarter = (total // 4, total)
    softmax_out, probs = call(
        softmax_kernel, [(quarter, f32), (quarter, bf16)], logit_mine, logit_other,
        flops=total * total,
    )
    probs_far = swapped(probs, "seq", seq_half)
    value_blocks, probs_far = lax.optimization_barrier((value_blocks, probs_far))
    grad_mine, grad_sent = scores(value_blocks, residues, 0, False, bf16)
    grad_other = swapped(grad_sent, "seq", seq_half)

    def products(quarters, blocks, first_row, second_row, with_share, factor):
        rows = 2 * residues + (residues // 2 if with_share else 0)
        (out,) = call(
            functools.partial(
                product_kernel, residues, factor, first_row, second_row, with_share
            ),
            [((group, rows, LANES), bf16)],
            *quarters, blocks,
            scratch=[pltpu.VMEM((total, total), bf16)],
            place=place, flops=4 * total * total * width,
        )
        return out

    def with_near(mine, far):
        return mine, far, swapped(mine, "res", 1), swapped(far, "res", 1)

    attended = products(with_near(probs, probs_far), value_blocks, 0, residues, False, 1.0)
    attended, grad_sent = lax.optimization_barrier((attended, grad_sent))
    attended_blocks = across(attended)
    grad_other = lax.optimization_barrier((attended, grad_other))[1]
    (grad_logits,) = call(
        softmax_gradient_kernel, [(quarter, bf16)], softmax_out, grad_mine, grad_other,
        flops=total * total,
    )
    grad_quarters = with_near(grad_logits, swapped(grad_logits, "seq", seq_half))
    grad_sums = products(grad_quarters, query_blocks, residues, 0, True, scale)
    grad_sums, attended_blocks = lax.optimization_barrier((grad_sums, attended_blocks))
    grad_blocks = across(grad_sums)

    updated, value_gate, normed, attended_sums = call(
        attended_weight_kernel,
        [
            (x.shape, bf16),
            ((tokens, 2 * width), bf16),
            ((tokens, width), bf16),
            ((width, 3 * width), bf16),
        ],
        x, grad, wc, wo, attended_blocks,
        flops=14 * tokens * width * width, outside=4,
    )
    share = pltpu.VMEM((heads, residues, LANES), f32)
    (pair_weight_part,) = call(
        pair_weight_kernel, [((heads, channels), f32)],
        grad_blocks, pair_entries, mean, spread,
        scratch=[share], flops=4 * tokens * width * width,
    )
    columns = 5 * width + channels
    rows = width // res_size
    part_rows = ((res_size // 2, rows, columns), bf16)
    query_key, keep, send = call(
        query_weight_kernel,
        [((tokens, 2 * width), bf16), part_rows, part_rows],
        normed, grad_blocks, pair_weight_part, attended_sums,
        scratch=[pltpu.VMEM((width, columns), bf16)],
        place=place, flops=4 * tokens * width * width,
    )
    own, *sent = call(
        core_sum_kernel,
        [((rows, columns), f32)] + [((rows, columns), bf16)] * 3,
        keep, swapped(send, "res", 1), place=place,
    )
    received = [swapped(t, "res", 2 * flip) for flip, t in enumerate(sent, 1)]
    (pair_gradient,) = call(
        functools.partial(pair_kernel, 2 * residues),
        [(pair_entries.shape, bf16)],
        grad_blocks, pair_entries, pair_weight.T, bias, mean, spread,
        scratch=[share], flops=8 * tokens * width * width,
    )
    received, pair_gradient = lax.optimization_barrier((received, pair_gradient))
    (part,) = call(plane_sum_kernel, [((rows, columns), bf16)], own, *received)
    (alignment_gradient,) = call(
        alignment_kernel, [(x.shape, bf16)], x, wc, query_key, value_gate,
        flops=8 * tokens * width * width,
    )

    def added(mine, other):
        return (mine.astype(f32) + other.astype(f32)).astype(bf16)

    part = added(part, swapped(part, "seq", 1))
    part = added(part, swapped(part, "seq", seq_half))
    combined_gradient, output_gradient, pair_weight_gradient = call(
        output_kernel,
        [(wc.shape, f32), (wo.shape, f32), ((heads, channels), f32)],
        lax.all_gather(part, "res", axis=0),
    )
    return (
        updated,
        alignment_gradient,
        pair_gradient,
        combined_gradient,
        output_gradient,
        pair_weight_gradient.T,
    )


def body(alignment_rows, pair_entries, combined_weight, output_weight, pair_weight, updated_gradient):
    chosen = head_body if fits_heads(alignment_rows, pair_entries, pair_weight) else gathered_body
    return chosen(
        alignment_rows, pair_entries, combined_weight, output_weight, pair_weight, updated_gradient
    )


def solution(mesh):
    return jax.shard_map(
        body,
        mesh=mesh,
        in_specs=(
            P("seq", "res", None),
            P("res", "seq", None),
            P(),
            P(),
            P(),
            P("seq", "res", None),
        ),
        out_specs=(
            P("seq", "res", None),
            P("seq", "res", None),
            P("res", "seq", None),
            P(),
            P(),
            P(),
        ),
        check_vma=False,
    )
```

```python
import functools
import math

import jax
import jax.numpy as jnp
from jax import lax
from jax.experimental import pallas as pl
from jax.experimental.pallas import tpu as pltpu
from jax.sharding import PartitionSpec as P

eps_norm = 1e-05


def layer_normalize(values):
    values = values.astype(jnp.float32)
    center = values - jnp.mean(values, axis=-1, keepdims=True)
    broadcast_pair = lax.rsqrt(jnp.mean(center * center, axis=-1, keepdims=True) + eps_norm)
    return (center * broadcast_pair, broadcast_pair)


def layer_norm_backward(normalized_gradient, normalized_rows, broadcast_pair):
    mean_grad = jnp.mean(normalized_gradient, axis=-1, keepdims=True)
    mean_cross = jnp.mean(normalized_gradient * normalized_rows, axis=-1, keepdims=True)
    return broadcast_pair * (normalized_gradient - mean_grad - normalized_rows * mean_cross)


def split_heads(tensor, head_count):
    return tensor.reshape(
        tensor.shape[0], tensor.shape[1], head_count, tensor.shape[2] // head_count
    )


def merge_heads(tensor):
    return tensor.reshape(tensor.shape[0], tensor.shape[1], tensor.shape[2] * tensor.shape[3])


def gathered_body(
    alignment_rows, pair_entries, combined_weight, output_weight, pair_weight, updated_gradient
):
    sequence_count, residue_count, alignment_width = alignment_rows.shape
    head_count = pair_weight.shape[1]
    query_width = output_weight.shape[0]
    head_dim = query_width // head_count
    column_count = pair_entries.shape[1]
    token_count = sequence_count * residue_count
    score_scale = 1.0 / math.sqrt(head_dim * sequence_count * lax.axis_size("seq"))
    normalized_rows, broadcast_pair = layer_normalize(alignment_rows)
    normalized_rows_backward = normalized_rows.astype(jnp.bfloat16).reshape(
        token_count, alignment_width
    )
    projected = jnp.dot(
        normalized_rows_backward, combined_weight, preferred_element_type=jnp.float32
    ).reshape(sequence_count, residue_count, 4 * query_width)
    queries = (projected[..., :query_width] * score_scale).astype(jnp.bfloat16)
    key_rows = projected[..., query_width : 2 * query_width].astype(jnp.bfloat16)
    value_rows = projected[..., 2 * query_width : 3 * query_width].astype(jnp.bfloat16)
    gate_open = jax.nn.sigmoid(projected[..., 3 * query_width :])
    all_keys, all_values = (
        lax.all_gather(key_rows, "res", axis=1, tiled=True),
        lax.all_gather(value_rows, "res", axis=1, tiled=True),
    )
    query_heads = split_heads(queries, head_count)
    key_heads = split_heads(all_keys, head_count)
    value_heads = split_heads(all_values, head_count)
    score_terms = jnp.einsum(
        "sihd,sjhd->hij", query_heads, key_heads, preferred_element_type=jnp.float32
    )
    pair_normed, pair_spread = layer_normalize(pair_entries)
    pair_bias = jnp.einsum("ijc,ch->hij", pair_normed, pair_weight, precision=lax.Precision.HIGHEST)
    col_start = lax.axis_index("seq") * column_count
    own_block = lax.dynamic_slice_in_dim(score_terms, col_start, column_count, 2) + pair_bias
    logits = lax.psum(lax.dynamic_update_slice_in_dim(score_terms, own_block, col_start, 2), "seq")
    row_top = jnp.max(logits, axis=-1, keepdims=True)
    lifted = jnp.exp(logits - row_top)
    softmax_out = lifted / jnp.sum(lifted, axis=-1, keepdims=True)
    softmax_low = softmax_out.astype(jnp.bfloat16)
    attended = merge_heads(
        jnp.einsum("hij,sjhd->sihd", softmax_low, value_heads, preferred_element_type=jnp.float32)
    )
    gated_out = (gate_open * attended).astype(jnp.bfloat16)
    flattened_gated = gated_out.reshape(token_count, query_width)
    updated = (
        jnp.dot(flattened_gated, output_weight, preferred_element_type=jnp.float32)
        .astype(jnp.bfloat16)
        .reshape(sequence_count, residue_count, alignment_width)
    )
    flattened_gradient = updated_gradient.reshape(token_count, alignment_width)
    grad_gated = jnp.dot(
        flattened_gradient, output_weight.T, preferred_element_type=jnp.float32
    ).reshape(sequence_count, residue_count, query_width)
    out_local = jnp.dot(flattened_gated.T, flattened_gradient, preferred_element_type=jnp.float32)
    grad_attended = (grad_gated * gate_open).astype(jnp.bfloat16)
    grad_gate_logit = grad_gated * attended * gate_open * (1.0 - gate_open)
    attended_grad_heads = split_heads(grad_attended, head_count)
    grad_terms = jnp.einsum(
        "sihd,sjhd->hij", attended_grad_heads, value_heads, preferred_element_type=jnp.float32
    )
    grad_probs = lax.psum(grad_terms, "seq")
    row_dot = jnp.sum(softmax_out * grad_probs, axis=-1, keepdims=True)
    grad_logits = softmax_out * (grad_probs - row_dot)
    grad_logits_b = grad_logits.astype(jnp.bfloat16)
    logit_share = lax.dynamic_slice_in_dim(grad_logits, col_start, column_count, 2)
    grad_query_heads = (
        jnp.einsum("hij,sjhd->sihd", grad_logits_b, key_heads, preferred_element_type=jnp.float32)
        * score_scale
    )
    key_part = jnp.einsum(
        "hij,sihd->jshd", grad_logits_b, query_heads, preferred_element_type=jnp.float32
    )
    value_part = jnp.einsum(
        "hij,sihd->jshd", softmax_low, attended_grad_heads, preferred_element_type=jnp.float32
    )
    summed = lax.psum_scatter(
        jnp.concatenate([merge_heads(key_part), merge_heads(value_part)], axis=-1),
        "res",
        scatter_dimension=0,
        tiled=True,
    )
    key_value_grads = jnp.transpose(summed, (1, 0, 2))
    projected_gradient = jnp.concatenate(
        [merge_heads(grad_query_heads), key_value_grads, grad_gate_logit], axis=-1
    )
    projected_gradient = projected_gradient.astype(jnp.bfloat16).reshape(
        token_count, 4 * query_width
    )
    qkvg_local = jnp.dot(
        normalized_rows_backward.T, projected_gradient, preferred_element_type=jnp.float32
    )
    normalized_gradient = jnp.dot(
        projected_gradient, combined_weight.T, preferred_element_type=jnp.float32
    ).reshape(sequence_count, residue_count, alignment_width)
    alignment_gradient = layer_norm_backward(
        normalized_gradient, normalized_rows, broadcast_pair
    ).astype(jnp.bfloat16)
    pair_w_local = jnp.einsum(
        "ijc,hij->ch", pair_normed, logit_share, precision=lax.Precision.HIGHEST
    )
    grad_pair_normed = jnp.einsum(
        "hij,ch->ijc", logit_share, pair_weight, precision=lax.Precision.HIGHEST
    )
    pair_gradient = layer_norm_backward(grad_pair_normed, pair_normed, pair_spread).astype(
        jnp.bfloat16
    )
    combined_weight_gradient, output_weight_gradient, pair_weight_gradient = lax.psum(
        (qkvg_local, out_local, pair_w_local), ("seq", "res")
    )
    return (
        updated,
        alignment_gradient,
        pair_gradient,
        combined_weight_gradient,
        output_weight_gradient,
        pair_weight_gradient,
    )


VMEM_LIMIT = 20 * 1024 * 1024
ARGUMENT_VMEM_LIMIT = 56 * 1024 * 1024
LANES = 128
SLOTS = 4
NT = (((1,), (1,)), ((), ()))
TN = (((0,), (0,)), ((), ()))


def f32_dot(left, right, dims=None):
    if dims is None:
        return jnp.dot(left, right, preferred_element_type=jnp.float32)
    return lax.dot_general(left, right, dims, preferred_element_type=jnp.float32)


def two_terms(values):
    high = values.astype(jnp.bfloat16)
    return high, (values - high.astype(jnp.float32)).astype(jnp.bfloat16)


def slot_select(pieces):
    slot = lax.broadcasted_iota(jnp.int32, pieces[0].shape, 1) // (LANES // SLOTS)
    result = pieces[0]
    for k in range(1, SLOTS):
        result = jnp.where(slot == k, pieces[k], result)
    return result


def pack_heads(out_ref, row, tensor, residues):
    for core in range(2):
        for tile in range(tensor.shape[1] // LANES):
            rolled = []
            for s in range(SLOTS):
                start = (core * SLOTS + s) * residues
                piece = tensor[start : start + residues, tile * LANES : (tile + 1) * LANES]
                rolled.append(pltpu.roll(piece, s * LANES // SLOTS, 1) if s else piece)
            for j in range(SLOTS):
                block = slot_select([rolled[(k - j) % SLOTS] for k in range(SLOTS)])
                out_ref[(tile * SLOTS + j) * 2 + core, row : row + residues, :] = block.astype(
                    jnp.bfloat16
                )


def unpack_heads(in_ref, row, residues, tiles):
    rows = []
    for core in range(2):
        for s in range(SLOTS):
            pieces = []
            for tile in range(tiles):
                blocks = [
                    in_ref[
                        (tile * SLOTS + (k - s) % SLOTS) * 2 + core, row : row + residues, :
                    ].astype(jnp.float32)
                    for k in range(SLOTS)
                ]
                block = slot_select(blocks)
                pieces.append(pltpu.roll(block, LANES - s * LANES // SLOTS, 1) if s else block)
            rows.append(jnp.concatenate(pieces, axis=1))
    return jnp.concatenate(rows, axis=0)


def normalized(x_ref):
    width = x_ref.shape[-1]
    values = x_ref[...].reshape(-1, width).astype(jnp.float32)
    return layer_normalize(values)


def gate_of(logits):
    return 1.0 / (1.0 + jnp.exp(-logits))


def value_kernel(x_ref, grad_ref, wc_ref, wo_ref, out_ref):
    residues, width = x_ref.shape[1], x_ref.shape[2]
    normed = normalized(x_ref)[0].astype(jnp.bfloat16)
    values = f32_dot(normed, wc_ref[:, 2 * width : 3 * width])
    gate = gate_of(f32_dot(normed, wc_ref[:, 3 * width :]))
    grad_gated = f32_dot(grad_ref[...].reshape(-1, width), wo_ref[...], NT)
    pack_heads(out_ref, 0, values, residues)
    pack_heads(out_ref, residues, grad_gated * gate, residues)


def centred(weight):
    return weight - jnp.mean(weight, axis=1, keepdims=True)


def query_kernel(
    scale, arrive, x_ref, wc_ref, pair_ref, weight_ref, out_ref, bias_ref, mean_ref, spread_ref
):
    residues, width = x_ref.shape[1], x_ref.shape[2]
    heads = weight_ref.shape[0]
    normed = normalized(x_ref)[0].astype(jnp.bfloat16)
    pack_heads(out_ref, 0, f32_dot(normed, wc_ref[:, :width]) * scale, residues)
    pack_heads(out_ref, residues, f32_dot(normed, wc_ref[:, width : 2 * width]), residues)

    arrive()
    columns, channels = pair_ref.shape[1], pair_ref.shape[2]
    weight = centred(weight_ref[...])
    first = weight.astype(jnp.bfloat16)
    second, third = two_terms(weight - first.astype(jnp.float32))
    share = jnp.full((heads, channels), 1.0 / channels, jnp.bfloat16)
    left = jnp.concatenate([first, second, third, share], axis=0)
    average = jnp.full((channels, channels), 1.0 / channels, jnp.bfloat16)
    step_rows = 8

    def rows(step, carry):
        start = pl.multiple_of(step * step_rows, step_rows)
        entries = pair_ref[pl.ds(start, step_rows)].reshape(step_rows * columns, channels)
        center = entries.astype(jnp.float32) - f32_dot(entries, average)
        high, low = two_terms(center * center)
        variance = f32_dot(share, high, NT) + f32_dot(share, low, NT)
        spread = lax.rsqrt(variance + eps_norm)
        raw = f32_dot(left, entries, NT)
        bias = spread * (raw[:heads] + raw[heads : 2 * heads] + raw[2 * heads : 3 * heads])
        for k in range(step_rows):
            lanes = slice(k * columns, (k + 1) * columns)
            bias_ref[:, start + k, :] = bias[:, lanes]
            mean_ref[pl.ds(start + k, 1), :] = raw[3 * heads : 3 * heads + 1, lanes]
            spread_ref[pl.ds(start + k, 1), :] = spread[:1, lanes]
        return carry

    lax.fori_loop(0, pair_ref.shape[0] // step_rows, rows, 0)
    half = residues // 2
    for h in range(heads):
        for core in range(2):
            high, low = two_terms(bias_ref[h, core * half : (core + 1) * half, :])
            out_ref[h * 2 + core, 2 * residues : 2 * residues + half, :] = high
            out_ref[h * 2 + core, 2 * residues + half : 3 * residues, :] = low


def lanes_of(blocks_ref, row, residues):
    count = blocks_ref.shape[0] // 2
    planes = [
        blocks_ref[p * count : (p + 1) * count, row : row + residues, :].reshape(-1, LANES)
        for p in range(2)
    ]
    return jnp.concatenate(planes, axis=1)


def score_kernel(
    residues, left_row, right_row, with_bias, place_ref, own_ref, other_ref, mine_ref, sent_ref
):
    core, half = place_ref[0], place_ref[1]
    count = own_ref.shape[0] // 2
    part = residues // 2
    right = jnp.concatenate(
        [lanes_of(own_ref, right_row, residues), lanes_of(other_ref, right_row, residues)], axis=1
    )
    for which, ref in ((half, mine_ref), (1 - half, sent_ref)):
        left = []
        for k in range(count // 2):
            block = which * (count // 2) + k
            rows = pl.ds(pl.multiple_of(left_row + core * part, part), part)
            left.append(
                jnp.concatenate(
                    [
                        r[p * count + block, rows, :]
                        for r in (own_ref, other_ref)
                        for p in range(2)
                    ],
                    axis=1,
                )
            )
        ref[...] = f32_dot(jnp.concatenate(left, axis=0), right, NT).astype(ref.dtype)
        if with_bias:
            for p in range(2):
                columns = pl.ds(pl.multiple_of((half * 2 + p) * LANES, LANES), LANES)
                for k in range(count // 2):
                    block = p * count + which * (count // 2) + k
                    high = own_ref[block, 2 * residues : 2 * residues + part, :]
                    low = own_ref[block, 2 * residues + part : 3 * residues, :]
                    bias = high.astype(jnp.float32) + low.astype(jnp.float32)
                    ref[k * part : (k + 1) * part, columns] += bias


def softmax_kernel(logit_ref, other_ref, out_ref, low_ref):
    logits = logit_ref[...] + other_ref[...]
    lifted = jnp.exp(logits - jnp.max(logits, axis=-1, keepdims=True))
    softmax_out = lifted / jnp.sum(lifted, axis=-1, keepdims=True)
    out_ref[...] = softmax_out
    low_ref[...] = softmax_out.astype(jnp.bfloat16)


def softmax_gradient_kernel(softmax_ref, grad_ref, other_ref, out_ref):
    softmax_out = softmax_ref[...]
    grad_probs = grad_ref[...] + other_ref[...].astype(jnp.float32)
    row_dot = jnp.sum(softmax_out * grad_probs, axis=-1, keepdims=True)
    out_ref[...] = (softmax_out * (grad_probs - row_dot)).astype(jnp.bfloat16)


def product_kernel(
    residues, scale, first_row, second_row, with_share,
    place_ref, own_ref, far_ref, near_ref, corner_ref, blocks_ref, out_ref, whole_ref,
):
    core, half = place_ref[0], place_ref[1]
    count = blocks_ref.shape[0] // 2
    part = residues // 2
    quarters = (
        (own_ref, core, half), (far_ref, core, 1 - half),
        (near_ref, 1 - core, half), (corner_ref, 1 - core, 1 - half),
    )
    for ref, c, z in quarters:
        for k in range(count // 2):
            start = (z * (count // 2) + k) * residues + c * part
            whole_ref[pl.ds(pl.multiple_of(start, part), part), :] = ref[k * part : (k + 1) * part, :]
    whole = whole_ref[...]
    if with_share:
        for p in range(2):
            columns = pl.ds(pl.multiple_of((half * 2 + p) * LANES, LANES), LANES)
            for q in range(count):
                rows = pl.ds(pl.multiple_of(q * residues + core * part, part), part)
                out_ref[p * count + q, 2 * residues : 2 * residues + part, :] = whole_ref[rows, columns]
    first = f32_dot(whole, lanes_of(blocks_ref, first_row, residues)) * scale
    second = f32_dot(whole, lanes_of(blocks_ref, second_row, residues), TN)
    for row, product in ((0, first), (residues, second)):
        for p in range(2):
            out_ref[p * count : (p + 1) * count, row : row + residues, :] = (
                product[:, p * LANES : (p + 1) * LANES]
                .astype(jnp.bfloat16)
                .reshape(count, residues, LANES)
            )


def share_of(blocks_ref, row, part, heads):
    return jnp.concatenate(
        [
            blocks_ref[:, row : row + part, :]
            .astype(jnp.float32)
            .reshape(heads, 2 * part, LANES)
        ],
        axis=0,
    )


def attended_weight_kernel(
    x_ref, grad_ref, wc_ref, wo_ref, blocks_ref, updated_ref, projected_ref, normed_ref, sums_ref
):
    residues, width = x_ref.shape[1], x_ref.shape[2]
    tiles = width // LANES
    normed = normalized(x_ref)[0].astype(jnp.bfloat16)
    normed_ref[...] = normed
    gate = gate_of(f32_dot(normed, wc_ref[:, 3 * width :]))
    grad = grad_ref[...].reshape(-1, width)
    grad_gated = f32_dot(grad, wo_ref[...], NT)
    attended = unpack_heads(blocks_ref, 0, residues, tiles)
    gated = (gate * attended).astype(jnp.bfloat16)
    updated_ref[...] = f32_dot(gated, wo_ref[...]).astype(jnp.bfloat16).reshape(updated_ref.shape)
    projected_ref[:, :width] = unpack_heads(blocks_ref, residues, residues, tiles).astype(
        jnp.bfloat16
    )
    projected_ref[:, width:] = (grad_gated * attended * gate * (1.0 - gate)).astype(jnp.bfloat16)
    sums_ref[:, : 2 * width] = f32_dot(normed, projected_ref[...], TN).astype(jnp.bfloat16)
    sums_ref[:, 2 * width :] = f32_dot(gated, grad, TN).astype(jnp.bfloat16)


def query_weight_kernel(
    place_ref, normed_ref, blocks_ref, pair_weight_ref, attended_sums_ref,
    projected_ref, keep_ref, send_ref, sums_ref,
):
    width = normed_ref.shape[1]
    tiles, residues = width // LANES, (blocks_ref.shape[1] * 2) // 5
    core = place_ref[0]
    for t in range(2):
        projected_ref[:, t * width : (t + 1) * width] = unpack_heads(
            blocks_ref, t * residues, residues, tiles
        ).astype(jnp.bfloat16)
    sums_ref[:, : 2 * width] = f32_dot(normed_ref[...], projected_ref[...], TN).astype(
        jnp.bfloat16
    )
    sums_ref[:, 2 * width : 5 * width] = attended_sums_ref[...]
    heads, channels = pair_weight_ref.shape
    rows = sums_ref.shape[0] // heads
    first = lax.broadcasted_iota(jnp.int32, (rows, channels), 0) == 0
    for h in range(heads):
        row = jnp.broadcast_to(pair_weight_ref[h : h + 1], (rows, channels))
        sums_ref[h * rows : (h + 1) * rows, 5 * width :] = jnp.where(first, row, 0.0).astype(
            jnp.bfloat16
        )
    for which, ref in ((core, keep_ref), (1 - core, send_ref)):
        for block in range(heads // 2):
            start = pl.multiple_of((2 * block + which) * rows, rows)
            ref[block] = sums_ref[pl.ds(start, rows), :]


def core_sum_kernel(place_ref, keep_ref, other_ref, own_ref, *send_refs):
    chip = place_ref[2]
    for flip, ref in enumerate((own_ref, *send_refs)):
        block = jnp.bitwise_xor(chip, flip)
        total = keep_ref[block].astype(jnp.float32) + other_ref[block].astype(jnp.float32)
        ref[...] = total.astype(ref.dtype)


def plane_sum_kernel(own_ref, *refs):
    total = own_ref[...]
    for ref in refs[:-1]:
        total += ref[...].astype(jnp.float32)
    refs[-1][...] = total.astype(refs[-1].dtype)


def pair_weight_kernel(blocks_ref, pair_ref, mean_ref, spread_ref, out_ref, share_ref):
    heads, part = share_ref.shape[0], pair_ref.shape[0] // 2
    share_ref[...] = share_of(blocks_ref, blocks_ref.shape[1] - part, part, heads)

    def rows(step, carry):
        total, shift = carry
        for k in range(8):
            i = step * 8 + k
            scaled = share_ref[:, i, :] * spread_ref[pl.ds(i, 1), :]
            high, low = two_terms(scaled)
            total += f32_dot(jnp.concatenate([high, low], axis=0), pair_ref[i])
            shift += (high.astype(jnp.float32) + low.astype(jnp.float32)) * mean_ref[pl.ds(i, 1), :]
        return total, shift

    channels = pair_ref.shape[2]
    total, shift = lax.fori_loop(
        0,
        pair_ref.shape[0] // 8,
        rows,
        (jnp.zeros((2 * heads, channels), jnp.float32), jnp.zeros((heads, LANES), jnp.float32)),
    )
    out_ref[...] = total[:heads] + total[heads:] - jnp.sum(shift, axis=1, keepdims=True)


def alignment_kernel(x_ref, wc_ref, query_key_ref, value_gate_ref, out_ref):
    normed, spread = normalized(x_ref)
    width = x_ref.shape[2]
    gradient = f32_dot(query_key_ref[...], wc_ref[:, : 2 * width], NT) + f32_dot(
        value_gate_ref[...], wc_ref[:, 2 * width :], NT
    )
    out_ref[...] = (
        layer_norm_backward(gradient, normed, spread).astype(jnp.bfloat16).reshape(out_ref.shape)
    )


def pair_kernel(blocks_row, blocks_ref, pair_ref, weight_ref, bias_ref, mean_ref, spread_ref, out_ref, share_ref):
    heads, channels = weight_ref.shape
    part = pair_ref.shape[0] // 2
    share_ref[...] = share_of(blocks_ref, blocks_row, part, heads)
    first, second = two_terms(centred(weight_ref[...]))
    zero = jnp.zeros((heads, channels), jnp.bfloat16)
    top = lax.broadcasted_iota(jnp.int32, (heads, channels), 0) < 2
    ones = jnp.where(top, 1.0, 0.0).astype(jnp.bfloat16)
    right = jnp.concatenate(
        [
            jnp.concatenate([first, first, second, ones, zero], axis=0),
            jnp.concatenate([zero, zero, zero, zero, ones], axis=0),
        ],
        axis=1,
    )
    row = lax.broadcasted_iota(jnp.int32, (heads, LANES), 0)

    def rows_of_two(value):
        high, low = two_terms(value)
        high, low = high.astype(jnp.float32), low.astype(jnp.float32)
        return jnp.where(row == 0, high, jnp.where(row == 1, low, 0.0)).astype(jnp.bfloat16)

    def rows(step, carry):
        for k in range(8):
            i = step * 8 + k
            gradient = share_ref[:, i, :]
            spread = spread_ref[pl.ds(i, 1), :]
            cross = jnp.sum(gradient * bias_ref[:, i, :], axis=0, keepdims=True) / channels
            slope = spread * spread * cross
            high, low = two_terms(gradient * spread)
            left = jnp.concatenate(
                [
                    high, low, high,
                    rows_of_two(jnp.broadcast_to(slope * mean_ref[pl.ds(i, 1), :], row.shape)),
                    rows_of_two(jnp.broadcast_to(slope, row.shape)),
                ],
                axis=0,
            )
            terms = f32_dot(left, right, TN)
            entries = pair_ref[i].astype(jnp.float32)
            out_ref[i] = (terms[:, :channels] - terms[:, channels:] * entries).astype(jnp.bfloat16)
        return carry

    lax.fori_loop(0, pair_ref.shape[0] // 8, rows, 0)


def output_kernel(parts_ref, combined_ref, out_weight_ref, pair_weight_ref):
    width = combined_ref.shape[0]
    rows = parts_ref.shape[1]
    for h in range(parts_ref.shape[0]):
        block = slice(h * rows, (h + 1) * rows)
        part = parts_ref[h].astype(jnp.float32)
        combined_ref[block, :] = part[:, : 4 * width]
        out_weight_ref[block, :] = part[:, 4 * width : 5 * width]
        pair_weight_ref[h : h + 1, :] = part[:1, 5 * width :]


def call(kernel, outs, *args, scratch=(), place=None, flops=0, after=(), outside=0, late=0):
    whole, anywhere = pl.BlockSpec(memory_space=pltpu.VMEM), pl.BlockSpec(memory_space=pl.ANY)
    specs = [anywhere] * outside + [whole] * (len(args) - outside)
    ahead = () if place is None else (place,)
    shapes = [jax.ShapeDtypeStruct(*o) for o in outs]
    moved = sum(math.prod(a.shape) * a.dtype.itemsize for a in list(args) + shapes)
    first = len(ahead) + len(args)
    last = first + len(after)

    def wrapped(*refs):
        given, rest = list(refs[:first]), refs[last:]
        if outside:
            *rest, arrived = rest
            held = rest[len(rest) - outside :]
            rest = rest[: len(rest) - outside]
            copies = []
            for k in range(outside):
                copies.append(
                    pltpu.make_async_copy(given[len(ahead) + k], held[k], arrived.at[k])
                )
                given[len(ahead) + k] = held[k]
            for copy in copies:
                copy.start()
            for copy in copies[: outside - late]:
                copy.wait()
            if late:
                given.insert(0, lambda: [copy.wait() for copy in copies[outside - late :]])
        kernel(*given, *rest)

    held = [pltpu.VMEM(a.shape, a.dtype) for a in args[:outside]]
    if outside:
        held.append(pltpu.SemaphoreType.DMA((outside,)))
    return pl.pallas_call(
        wrapped,
        out_shape=shapes,
        in_specs=[pl.BlockSpec(memory_space=pltpu.SMEM)] * len(ahead)
        + specs
        + [anywhere] * len(after),
        out_specs=[whole] * len(shapes),
        scratch_shapes=[*scratch, *held],
        compiler_params=pltpu.CompilerParams(
            vmem_limit_bytes=ARGUMENT_VMEM_LIMIT if outside else VMEM_LIMIT
        ),
        cost_estimate=pl.CostEstimate(flops=flops, bytes_accessed=moved, transcendentals=0),
    )(*ahead, *args, *after)


def swapped(mine, axis_name, distance):
    size = lax.axis_size(axis_name)
    return lax.ppermute(mine, axis_name, [(a, a ^ distance) for a in range(size)])


def fits_heads(alignment_rows, pair_entries, pair_weight):
    channels, heads = pair_weight.shape
    return (
        lax.axis_size("seq") == 4
        and lax.axis_size("res") == heads == 8
        and alignment_rows.shape[0] == 2 * SLOTS
        and alignment_rows.shape[1] == pair_entries.shape[0] == 64
        and alignment_rows.shape[2] == 2 * LANES
        and pair_entries.shape[1] == channels == LANES
    )


def head_body(
    alignment_rows, pair_entries, combined_weight, output_weight, pair_weight, updated_gradient
):
    sequences, residues, width = alignment_rows.shape
    channels, heads = pair_weight.shape
    tokens = sequences * residues
    seq_size, res_size = lax.axis_size("seq"), lax.axis_size("res")
    seq_half = seq_size // 2
    total = residues * res_size
    group = 2 * res_size
    groups = [[g * group + k for k in range(group)] for g in range(seq_half)]
    scale = 1.0 / math.sqrt(width // heads * sequences * seq_size)
    res_index, seq_index = lax.axis_index("res"), lax.axis_index("seq")
    place = jnp.stack([res_index % 2, seq_index // 2, res_index // 2]).astype(jnp.int32)
    bf16, f32 = jnp.bfloat16, jnp.float32

    def across(blocks):
        return lax.all_to_all(blocks, ("seq", "res"), 0, 0, axis_index_groups=groups, tiled=True)

    x, grad, wc, wo = alignment_rows, updated_gradient, combined_weight, output_weight
    query_blocks, bias, mean, spread = call(
        functools.partial(query_kernel, scale),
        [
            ((group, 3 * residues, LANES), bf16),
            ((heads, residues, LANES), f32),
            ((residues, LANES), f32),
            ((residues, LANES), f32),
        ],
        x, wc, pair_entries, pair_weight.T,
        flops=8 * tokens * width * width, outside=3, late=1,
    )
    query_blocks = across(query_blocks)
    (value_blocks,) = call(
        value_kernel, [((group, 2 * residues, LANES), bf16)], x, grad, wc, wo,
        flops=8 * tokens * width * width, outside=4,
    )
    query_blocks, value_blocks = lax.optimization_barrier((query_blocks, value_blocks))
    value_blocks = across(value_blocks)

    def scores(blocks, left_row, right_row, with_bias, kind):
        return call(
            functools.partial(score_kernel, residues, left_row, right_row, with_bias),
            [((total // 4, total), f32), ((total // 4, total), kind)],
            blocks, swapped(blocks, "res", 1),
            place=place, flops=2 * total * total * width,
        )

    logit_mine, logit_sent = scores(query_blocks, 0, residues, True, f32)
    logit_other = swapped(logit_sent, "seq", seq_half)
    quarter = (total // 4, total)
    softmax_out, probs = call(
        softmax_kernel, [(quarter, f32), (quarter, bf16)], logit_mine, logit_other,
        flops=total * total,
    )
    value_blocks, probs = lax.optimization_barrier((value_blocks, probs))
    probs_far = swapped(probs, "seq", seq_half)
    grad_mine, grad_sent = scores(value_blocks, residues, 0, False, bf16)
    grad_other = swapped(grad_sent, "seq", seq_half)

    def products(quarters, blocks, first_row, second_row, with_share, factor):
        rows = 2 * residues + (residues // 2 if with_share else 0)
        (out,) = call(
            functools.partial(
                product_kernel, residues, factor, first_row, second_row, with_share
            ),
            [((group, rows, LANES), bf16)],
            *quarters, blocks,
            scratch=[pltpu.VMEM((total, total), bf16)],
            place=place, flops=4 * total * total * width,
        )
        return out

    def with_near(mine, far):
        return mine, far, swapped(mine, "res", 1), swapped(far, "res", 1)

    attended = products(with_near(probs, probs_far), value_blocks, 0, residues, False, 1.0)
    attended, grad_other = lax.optimization_barrier((attended, grad_other))
    attended_blocks = across(attended)
    (grad_logits,) = call(
        softmax_gradient_kernel, [(quarter, bf16)], softmax_out, grad_mine, grad_other,
        flops=total * total,
    )
    grad_quarters = with_near(grad_logits, swapped(grad_logits, "seq", seq_half))
    grad_sums = products(grad_quarters, query_blocks, residues, 0, True, scale)
    grad_sums, attended_blocks = lax.optimization_barrier((grad_sums, attended_blocks))
    grad_blocks = across(grad_sums)

    updated, value_gate, normed, attended_sums = call(
        attended_weight_kernel,
        [
            (x.shape, bf16),
            ((tokens, 2 * width), bf16),
            ((tokens, width), bf16),
            ((width, 3 * width), bf16),
        ],
        x, grad, wc, wo, attended_blocks,
        flops=14 * tokens * width * width, outside=4,
    )
    share = pltpu.VMEM((heads, residues, LANES), f32)
    (pair_weight_part,) = call(
        pair_weight_kernel, [((heads, channels), f32)],
        grad_blocks, pair_entries, mean, spread,
        scratch=[share], flops=4 * tokens * width * width,
    )
    columns = 5 * width + channels
    rows = width // res_size
    part_rows = ((res_size // 2, rows, columns), bf16)
    query_key, keep, send = call(
        query_weight_kernel,
        [((tokens, 2 * width), bf16), part_rows, part_rows],
        normed, grad_blocks, pair_weight_part, attended_sums,
        scratch=[pltpu.VMEM((width, columns), bf16)],
        place=place, flops=4 * tokens * width * width,
    )
    own, *sent = call(
        core_sum_kernel,
        [((rows, columns), f32)] + [((rows, columns), bf16)] * 3,
        keep, swapped(send, "res", 1), place=place,
    )
    received = [swapped(t, "res", 2 * flip) for flip, t in enumerate(sent, 1)]
    (pair_gradient,) = call(
        functools.partial(pair_kernel, 2 * residues),
        [(pair_entries.shape, bf16)],
        grad_blocks, pair_entries, pair_weight.T, bias, mean, spread,
        scratch=[share], flops=8 * tokens * width * width,
    )
    (alignment_gradient,) = call(
        alignment_kernel, [(x.shape, bf16)], x, wc, query_key, value_gate,
        flops=8 * tokens * width * width,
    )
    received, alignment_gradient = lax.optimization_barrier((received, alignment_gradient))
    (part,) = call(plane_sum_kernel, [((rows, columns), bf16)], own, *received)

    def added(mine, other):
        return (mine.astype(f32) + other.astype(f32)).astype(bf16)

    part = added(part, swapped(part, "seq", 1))
    other_half = swapped(part, "seq", seq_half)
    other_half, pair_gradient = lax.optimization_barrier((other_half, pair_gradient))
    part = added(part, other_half)
    combined_gradient, output_gradient, pair_weight_gradient = call(
        output_kernel,
        [(wc.shape, f32), (wo.shape, f32), ((heads, channels), f32)],
        lax.all_gather(part, "res", axis=0),
    )
    return (
        updated,
        alignment_gradient,
        pair_gradient,
        combined_gradient,
        output_gradient,
        pair_weight_gradient.T,
    )


def body(alignment_rows, pair_entries, combined_weight, output_weight, pair_weight, updated_gradient):
    chosen = head_body if fits_heads(alignment_rows, pair_entries, pair_weight) else gathered_body
    return chosen(
        alignment_rows, pair_entries, combined_weight, output_weight, pair_weight, updated_gradient
    )


def solution(mesh):
    return jax.shard_map(
        body,
        mesh=mesh,
        in_specs=(
            P("seq", "res", None),
            P("res", "seq", None),
            P(),
            P(),
            P(),
            P("seq", "res", None),
        ),
        out_specs=(
            P("seq", "res", None),
            P("seq", "res", None),
            P("res", "seq", None),
            P(),
            P(),
            P(),
        ),
        check_vma=False,
    )
```

```python
import functools
import math

import jax
import jax.numpy as jnp
from jax import lax
from jax.experimental import pallas as pl
from jax.experimental.pallas import tpu as pltpu
from jax.sharding import PartitionSpec as P

eps_norm = 1e-05


def layer_normalize(values):
    values = values.astype(jnp.float32)
    center = values - jnp.mean(values, axis=-1, keepdims=True)
    broadcast_pair = lax.rsqrt(jnp.mean(center * center, axis=-1, keepdims=True) + eps_norm)
    return (center * broadcast_pair, broadcast_pair)


def layer_norm_backward(normalized_gradient, normalized_rows, broadcast_pair):
    mean_grad = jnp.mean(normalized_gradient, axis=-1, keepdims=True)
    mean_cross = jnp.mean(normalized_gradient * normalized_rows, axis=-1, keepdims=True)
    return broadcast_pair * (normalized_gradient - mean_grad - normalized_rows * mean_cross)


def split_heads(tensor, head_count):
    return tensor.reshape(
        tensor.shape[0], tensor.shape[1], head_count, tensor.shape[2] // head_count
    )


def merge_heads(tensor):
    return tensor.reshape(tensor.shape[0], tensor.shape[1], tensor.shape[2] * tensor.shape[3])


def gathered_body(
    alignment_rows, pair_entries, combined_weight, output_weight, pair_weight, updated_gradient
):
    sequence_count, residue_count, alignment_width = alignment_rows.shape
    head_count = pair_weight.shape[1]
    query_width = output_weight.shape[0]
    head_dim = query_width // head_count
    column_count = pair_entries.shape[1]
    token_count = sequence_count * residue_count
    score_scale = 1.0 / math.sqrt(head_dim * sequence_count * lax.axis_size("seq"))
    normalized_rows, broadcast_pair = layer_normalize(alignment_rows)
    normalized_rows_backward = normalized_rows.astype(jnp.bfloat16).reshape(
        token_count, alignment_width
    )
    projected = jnp.dot(
        normalized_rows_backward, combined_weight, preferred_element_type=jnp.float32
    ).reshape(sequence_count, residue_count, 4 * query_width)
    queries = (projected[..., :query_width] * score_scale).astype(jnp.bfloat16)
    key_rows = projected[..., query_width : 2 * query_width].astype(jnp.bfloat16)
    value_rows = projected[..., 2 * query_width : 3 * query_width].astype(jnp.bfloat16)
    gate_open = jax.nn.sigmoid(projected[..., 3 * query_width :])
    all_keys, all_values = (
        lax.all_gather(key_rows, "res", axis=1, tiled=True),
        lax.all_gather(value_rows, "res", axis=1, tiled=True),
    )
    query_heads = split_heads(queries, head_count)
    key_heads = split_heads(all_keys, head_count)
    value_heads = split_heads(all_values, head_count)
    score_terms = jnp.einsum(
        "sihd,sjhd->hij", query_heads, key_heads, preferred_element_type=jnp.float32
    )
    pair_normed, pair_spread = layer_normalize(pair_entries)
    pair_bias = jnp.einsum("ijc,ch->hij", pair_normed, pair_weight, precision=lax.Precision.HIGHEST)
    col_start = lax.axis_index("seq") * column_count
    own_block = lax.dynamic_slice_in_dim(score_terms, col_start, column_count, 2) + pair_bias
    logits = lax.psum(lax.dynamic_update_slice_in_dim(score_terms, own_block, col_start, 2), "seq")
    row_top = jnp.max(logits, axis=-1, keepdims=True)
    lifted = jnp.exp(logits - row_top)
    softmax_out = lifted / jnp.sum(lifted, axis=-1, keepdims=True)
    softmax_low = softmax_out.astype(jnp.bfloat16)
    attended = merge_heads(
        jnp.einsum("hij,sjhd->sihd", softmax_low, value_heads, preferred_element_type=jnp.float32)
    )
    gated_out = (gate_open * attended).astype(jnp.bfloat16)
    flattened_gated = gated_out.reshape(token_count, query_width)
    updated = (
        jnp.dot(flattened_gated, output_weight, preferred_element_type=jnp.float32)
        .astype(jnp.bfloat16)
        .reshape(sequence_count, residue_count, alignment_width)
    )
    flattened_gradient = updated_gradient.reshape(token_count, alignment_width)
    grad_gated = jnp.dot(
        flattened_gradient, output_weight.T, preferred_element_type=jnp.float32
    ).reshape(sequence_count, residue_count, query_width)
    out_local = jnp.dot(flattened_gated.T, flattened_gradient, preferred_element_type=jnp.float32)
    grad_attended = (grad_gated * gate_open).astype(jnp.bfloat16)
    grad_gate_logit = grad_gated * attended * gate_open * (1.0 - gate_open)
    attended_grad_heads = split_heads(grad_attended, head_count)
    grad_terms = jnp.einsum(
        "sihd,sjhd->hij", attended_grad_heads, value_heads, preferred_element_type=jnp.float32
    )
    grad_probs = lax.psum(grad_terms, "seq")
    row_dot = jnp.sum(softmax_out * grad_probs, axis=-1, keepdims=True)
    grad_logits = softmax_out * (grad_probs - row_dot)
    grad_logits_b = grad_logits.astype(jnp.bfloat16)
    logit_share = lax.dynamic_slice_in_dim(grad_logits, col_start, column_count, 2)
    grad_query_heads = (
        jnp.einsum("hij,sjhd->sihd", grad_logits_b, key_heads, preferred_element_type=jnp.float32)
        * score_scale
    )
    key_part = jnp.einsum(
        "hij,sihd->jshd", grad_logits_b, query_heads, preferred_element_type=jnp.float32
    )
    value_part = jnp.einsum(
        "hij,sihd->jshd", softmax_low, attended_grad_heads, preferred_element_type=jnp.float32
    )
    summed = lax.psum_scatter(
        jnp.concatenate([merge_heads(key_part), merge_heads(value_part)], axis=-1),
        "res",
        scatter_dimension=0,
        tiled=True,
    )
    key_value_grads = jnp.transpose(summed, (1, 0, 2))
    projected_gradient = jnp.concatenate(
        [merge_heads(grad_query_heads), key_value_grads, grad_gate_logit], axis=-1
    )
    projected_gradient = projected_gradient.astype(jnp.bfloat16).reshape(
        token_count, 4 * query_width
    )
    qkvg_local = jnp.dot(
        normalized_rows_backward.T, projected_gradient, preferred_element_type=jnp.float32
    )
    normalized_gradient = jnp.dot(
        projected_gradient, combined_weight.T, preferred_element_type=jnp.float32
    ).reshape(sequence_count, residue_count, alignment_width)
    alignment_gradient = layer_norm_backward(
        normalized_gradient, normalized_rows, broadcast_pair
    ).astype(jnp.bfloat16)
    pair_w_local = jnp.einsum(
        "ijc,hij->ch", pair_normed, logit_share, precision=lax.Precision.HIGHEST
    )
    grad_pair_normed = jnp.einsum(
        "hij,ch->ijc", logit_share, pair_weight, precision=lax.Precision.HIGHEST
    )
    pair_gradient = layer_norm_backward(grad_pair_normed, pair_normed, pair_spread).astype(
        jnp.bfloat16
    )
    combined_weight_gradient, output_weight_gradient, pair_weight_gradient = lax.psum(
        (qkvg_local, out_local, pair_w_local), ("seq", "res")
    )
    return (
        updated,
        alignment_gradient,
        pair_gradient,
        combined_weight_gradient,
        output_weight_gradient,
        pair_weight_gradient,
    )


VMEM_LIMIT = 20 * 1024 * 1024
ARGUMENT_VMEM_LIMIT = 56 * 1024 * 1024
LANES = 128
SLOTS = 4
NT = (((1,), (1,)), ((), ()))
TN = (((0,), (0,)), ((), ()))


def f32_dot(left, right, dims=None):
    if dims is None:
        return jnp.dot(left, right, preferred_element_type=jnp.float32)
    return lax.dot_general(left, right, dims, preferred_element_type=jnp.float32)


def two_terms(values):
    high = values.astype(jnp.bfloat16)
    return high, (values - high.astype(jnp.float32)).astype(jnp.bfloat16)


def slot_select(pieces):
    slot = lax.broadcasted_iota(jnp.int32, pieces[0].shape, 1) // (LANES // SLOTS)
    result = pieces[0]
    for k in range(1, SLOTS):
        result = jnp.where(slot == k, pieces[k], result)
    return result


def pack_heads(out_ref, row, tensor, residues):
    for core in range(2):
        for tile in range(tensor.shape[1] // LANES):
            rolled = []
            for s in range(SLOTS):
                start = (core * SLOTS + s) * residues
                piece = tensor[start : start + residues, tile * LANES : (tile + 1) * LANES]
                rolled.append(pltpu.roll(piece, s * LANES // SLOTS, 1) if s else piece)
            for j in range(SLOTS):
                block = slot_select([rolled[(k - j) % SLOTS] for k in range(SLOTS)])
                out_ref[(tile * SLOTS + j) * 2 + core, row : row + residues, :] = block.astype(
                    jnp.bfloat16
                )


def unpack_heads(in_ref, row, residues, tiles):
    rows = []
    for core in range(2):
        for s in range(SLOTS):
            pieces = []
            for tile in range(tiles):
                blocks = [
                    in_ref[
                        (tile * SLOTS + (k - s) % SLOTS) * 2 + core, row : row + residues, :
                    ].astype(jnp.float32)
                    for k in range(SLOTS)
                ]
                block = slot_select(blocks)
                pieces.append(pltpu.roll(block, LANES - s * LANES // SLOTS, 1) if s else block)
            rows.append(jnp.concatenate(pieces, axis=1))
    return jnp.concatenate(rows, axis=0)


def normalized(x_ref):
    width = x_ref.shape[-1]
    values = x_ref[...].reshape(-1, width).astype(jnp.float32)
    return layer_normalize(values)


def gate_of(logits):
    return 1.0 / (1.0 + jnp.exp(-logits))


def value_kernel(x_ref, grad_ref, wc_ref, wo_ref, out_ref):
    residues, width = x_ref.shape[1], x_ref.shape[2]
    normed = normalized(x_ref)[0].astype(jnp.bfloat16)
    values = f32_dot(normed, wc_ref[:, 2 * width : 3 * width])
    gate = gate_of(f32_dot(normed, wc_ref[:, 3 * width :]))
    grad_gated = f32_dot(grad_ref[...].reshape(-1, width), wo_ref[...], NT)
    pack_heads(out_ref, 0, values, residues)
    pack_heads(out_ref, residues, grad_gated * gate, residues)


def centred(weight):
    return weight - jnp.mean(weight, axis=1, keepdims=True)


def query_kernel(
    scale, arrive, x_ref, wc_ref, pair_ref, weight_ref, out_ref, bias_ref, mean_ref, spread_ref
):
    residues, width = x_ref.shape[1], x_ref.shape[2]
    heads = weight_ref.shape[0]
    normed = normalized(x_ref)[0].astype(jnp.bfloat16)
    pack_heads(out_ref, 0, f32_dot(normed, wc_ref[:, :width]) * scale, residues)
    pack_heads(out_ref, residues, f32_dot(normed, wc_ref[:, width : 2 * width]), residues)

    arrive()
    columns, channels = pair_ref.shape[1], pair_ref.shape[2]
    weight = centred(weight_ref[...])
    first = weight.astype(jnp.bfloat16)
    second, third = two_terms(weight - first.astype(jnp.float32))
    share = jnp.full((heads, channels), 1.0 / channels, jnp.bfloat16)
    left = jnp.concatenate([first, second, third, share], axis=0)
    average = jnp.full((channels, channels), 1.0 / channels, jnp.bfloat16)
    step_rows = 16

    def rows(step, carry):
        start = pl.multiple_of(step * step_rows, step_rows)
        entries = pair_ref[pl.ds(start, step_rows)].reshape(step_rows * columns, channels)
        center = entries.astype(jnp.float32) - f32_dot(entries, average)
        high, low = two_terms(center * center)
        variance = f32_dot(share, high, NT) + f32_dot(share, low, NT)
        spread = lax.rsqrt(variance + eps_norm)
        raw = f32_dot(left, entries, NT)
        bias = spread * (raw[:heads] + raw[heads : 2 * heads] + raw[2 * heads : 3 * heads])
        for k in range(step_rows):
            lanes = slice(k * columns, (k + 1) * columns)
            bias_ref[:, start + k, :] = bias[:, lanes]
            mean_ref[pl.ds(start + k, 1), :] = raw[3 * heads : 3 * heads + 1, lanes]
            spread_ref[pl.ds(start + k, 1), :] = spread[:1, lanes]
        return carry

    lax.fori_loop(0, pair_ref.shape[0] // step_rows, rows, 0)
    half = residues // 2
    for h in range(heads):
        for core in range(2):
            high, low = two_terms(bias_ref[h, core * half : (core + 1) * half, :])
            out_ref[h * 2 + core, 2 * residues : 2 * residues + half, :] = high
            out_ref[h * 2 + core, 2 * residues + half : 3 * residues, :] = low


def lanes_of(blocks_ref, row, residues):
    count = blocks_ref.shape[0] // 2
    planes = [
        blocks_ref[p * count : (p + 1) * count, row : row + residues, :].reshape(-1, LANES)
        for p in range(2)
    ]
    return jnp.concatenate(planes, axis=1)


def score_kernel(
    residues, left_row, right_row, with_bias, place_ref, own_ref, other_ref, mine_ref, sent_ref
):
    core, half = place_ref[0], place_ref[1]
    count = own_ref.shape[0] // 2
    part = residues // 2
    right = jnp.concatenate(
        [lanes_of(own_ref, right_row, residues), lanes_of(other_ref, right_row, residues)], axis=1
    )
    for which, ref in ((half, mine_ref), (1 - half, sent_ref)):
        left = []
        for k in range(count // 2):
            block = which * (count // 2) + k
            rows = pl.ds(pl.multiple_of(left_row + core * part, part), part)
            left.append(
                jnp.concatenate(
                    [
                        r[p * count + block, rows, :]
                        for r in (own_ref, other_ref)
                        for p in range(2)
                    ],
                    axis=1,
                )
            )
        ref[...] = f32_dot(jnp.concatenate(left, axis=0), right, NT).astype(ref.dtype)
        if with_bias:
            for p in range(2):
                columns = pl.ds(pl.multiple_of((half * 2 + p) * LANES, LANES), LANES)
                for k in range(count // 2):
                    block = p * count + which * (count // 2) + k
                    high = own_ref[block, 2 * residues : 2 * residues + part, :]
                    low = own_ref[block, 2 * residues + part : 3 * residues, :]
                    bias = high.astype(jnp.float32) + low.astype(jnp.float32)
                    ref[k * part : (k + 1) * part, columns] += bias


def softmax_kernel(logit_ref, other_ref, out_ref, low_ref):
    logits = logit_ref[...] + other_ref[...]
    lifted = jnp.exp(logits - jnp.max(logits, axis=-1, keepdims=True))
    softmax_out = lifted / jnp.sum(lifted, axis=-1, keepdims=True)
    out_ref[...] = softmax_out
    low_ref[...] = softmax_out.astype(jnp.bfloat16)


def softmax_gradient_kernel(softmax_ref, grad_ref, other_ref, out_ref):
    softmax_out = softmax_ref[...]
    grad_probs = grad_ref[...] + other_ref[...].astype(jnp.float32)
    row_dot = jnp.sum(softmax_out * grad_probs, axis=-1, keepdims=True)
    out_ref[...] = (softmax_out * (grad_probs - row_dot)).astype(jnp.bfloat16)


def product_kernel(
    residues, scale, first_row, second_row, with_share,
    place_ref, own_ref, far_ref, near_ref, corner_ref, blocks_ref, out_ref, whole_ref,
):
    core, half = place_ref[0], place_ref[1]
    count = blocks_ref.shape[0] // 2
    part = residues // 2
    quarters = (
        (own_ref, core, half), (far_ref, core, 1 - half),
        (near_ref, 1 - core, half), (corner_ref, 1 - core, 1 - half),
    )
    for ref, c, z in quarters:
        for k in range(count // 2):
            start = (z * (count // 2) + k) * residues + c * part
            whole_ref[pl.ds(pl.multiple_of(start, part), part), :] = ref[k * part : (k + 1) * part, :]
    whole = whole_ref[...]
    if with_share:
        for p in range(2):
            columns = pl.ds(pl.multiple_of((half * 2 + p) * LANES, LANES), LANES)
            for q in range(count):
                rows = pl.ds(pl.multiple_of(q * residues + core * part, part), part)
                out_ref[p * count + q, 2 * residues : 2 * residues + part, :] = whole_ref[rows, columns]
    first = f32_dot(whole, lanes_of(blocks_ref, first_row, residues)) * scale
    second = f32_dot(whole, lanes_of(blocks_ref, second_row, residues), TN)
    for row, product in ((0, first), (residues, second)):
        for p in range(2):
            out_ref[p * count : (p + 1) * count, row : row + residues, :] = (
                product[:, p * LANES : (p + 1) * LANES]
                .astype(jnp.bfloat16)
                .reshape(count, residues, LANES)
            )


def share_of(blocks_ref, row, part, heads):
    return jnp.concatenate(
        [
            blocks_ref[:, row : row + part, :]
            .astype(jnp.float32)
            .reshape(heads, 2 * part, LANES)
        ],
        axis=0,
    )


def attended_weight_kernel(
    x_ref, grad_ref, wc_ref, wo_ref, blocks_ref, updated_ref, projected_ref, normed_ref, sums_ref
):
    residues, width = x_ref.shape[1], x_ref.shape[2]
    tiles = width // LANES
    normed = normalized(x_ref)[0].astype(jnp.bfloat16)
    normed_ref[...] = normed
    gate = gate_of(f32_dot(normed, wc_ref[:, 3 * width :]))
    grad = grad_ref[...].reshape(-1, width)
    grad_gated = f32_dot(grad, wo_ref[...], NT)
    attended = unpack_heads(blocks_ref, 0, residues, tiles)
    gated = (gate * attended).astype(jnp.bfloat16)
    updated_ref[...] = f32_dot(gated, wo_ref[...]).astype(jnp.bfloat16).reshape(updated_ref.shape)
    projected_ref[:, :width] = unpack_heads(blocks_ref, residues, residues, tiles).astype(
        jnp.bfloat16
    )
    projected_ref[:, width:] = (grad_gated * attended * gate * (1.0 - gate)).astype(jnp.bfloat16)
    sums_ref[:, : 2 * width] = f32_dot(normed, projected_ref[...], TN).astype(jnp.bfloat16)
    sums_ref[:, 2 * width :] = f32_dot(gated, grad, TN).astype(jnp.bfloat16)


def query_weight_kernel(
    place_ref, normed_ref, blocks_ref, attended_sums_ref,
    projected_ref, keep_ref, send_ref, sums_ref,
):
    width = normed_ref.shape[1]
    tiles, residues = width // LANES, (blocks_ref.shape[1] * 2) // 5
    core = place_ref[0]
    for t in range(2):
        projected_ref[:, t * width : (t + 1) * width] = unpack_heads(
            blocks_ref, t * residues, residues, tiles
        ).astype(jnp.bfloat16)
    sums_ref[:, : 2 * width] = f32_dot(normed_ref[...], projected_ref[...], TN).astype(
        jnp.bfloat16
    )
    sums_ref[:, 2 * width :] = attended_sums_ref[...]
    rows = keep_ref.shape[1]
    for which, ref in ((core, keep_ref), (1 - core, send_ref)):
        for block in range(keep_ref.shape[0]):
            start = pl.multiple_of((2 * block + which) * rows, rows)
            ref[block] = sums_ref[pl.ds(start, rows), :]


def core_sum_kernel(place_ref, keep_ref, other_ref, own_ref, *send_refs):
    chip = place_ref[2]
    for flip, ref in enumerate((own_ref, *send_refs)):
        block = jnp.bitwise_xor(chip, flip)
        total = keep_ref[block].astype(jnp.float32) + other_ref[block].astype(jnp.float32)
        ref[...] = total.astype(ref.dtype)


def plane_sum_kernel(own_ref, pair_weight_ref, *refs):
    *received, out_ref = refs
    total = own_ref[...]
    for ref in received:
        total += ref[...].astype(jnp.float32)
    count = own_ref.shape[1]
    heads = pair_weight_ref.shape[0]
    out_ref[:, :count] = total.astype(out_ref.dtype)
    rest = jnp.zeros((out_ref.shape[0] - heads, out_ref.shape[1] - count), jnp.float32)
    out_ref[:, count:] = jnp.concatenate([pair_weight_ref[...], rest], axis=0).astype(
        out_ref.dtype
    )


def pair_weight_kernel(blocks_ref, pair_ref, mean_ref, spread_ref, out_ref, share_ref):
    heads, part = share_ref.shape[0], pair_ref.shape[0] // 2
    share_ref[...] = share_of(blocks_ref, blocks_ref.shape[1] - part, part, heads)

    def rows(step, carry):
        total, shift = carry
        for k in range(8):
            i = step * 8 + k
            scaled = share_ref[:, i, :] * spread_ref[pl.ds(i, 1), :]
            high, low = two_terms(scaled)
            total += f32_dot(jnp.concatenate([high, low], axis=0), pair_ref[i])
            shift += (high.astype(jnp.float32) + low.astype(jnp.float32)) * mean_ref[pl.ds(i, 1), :]
        return total, shift

    channels = pair_ref.shape[2]
    total, shift = lax.fori_loop(
        0,
        pair_ref.shape[0] // 8,
        rows,
        (jnp.zeros((2 * heads, channels), jnp.float32), jnp.zeros((heads, LANES), jnp.float32)),
    )
    out_ref[...] = total[:heads] + total[heads:] - jnp.sum(shift, axis=1, keepdims=True)


def alignment_kernel(x_ref, wc_ref, query_key_ref, value_gate_ref, out_ref):
    normed, spread = normalized(x_ref)
    width = x_ref.shape[2]
    gradient = f32_dot(query_key_ref[...], wc_ref[:, : 2 * width], NT) + f32_dot(
        value_gate_ref[...], wc_ref[:, 2 * width :], NT
    )
    out_ref[...] = (
        layer_norm_backward(gradient, normed, spread).astype(jnp.bfloat16).reshape(out_ref.shape)
    )


def pair_kernel(blocks_row, blocks_ref, pair_ref, weight_ref, bias_ref, mean_ref, spread_ref, out_ref, share_ref):
    heads, channels = weight_ref.shape
    part = pair_ref.shape[0] // 2
    share_ref[...] = share_of(blocks_ref, blocks_row, part, heads)
    first, second = two_terms(centred(weight_ref[...]))
    zero = jnp.zeros((heads, channels), jnp.bfloat16)
    top = lax.broadcasted_iota(jnp.int32, (heads, channels), 0) < 2
    ones = jnp.where(top, 1.0, 0.0).astype(jnp.bfloat16)
    right = jnp.concatenate(
        [
            jnp.concatenate([first, first, second, ones, zero], axis=0),
            jnp.concatenate([zero, zero, zero, zero, ones], axis=0),
        ],
        axis=1,
    )
    row = lax.broadcasted_iota(jnp.int32, (heads, LANES), 0)

    def rows_of_two(value):
        high, low = two_terms(value)
        high, low = high.astype(jnp.float32), low.astype(jnp.float32)
        return jnp.where(row == 0, high, jnp.where(row == 1, low, 0.0)).astype(jnp.bfloat16)

    def rows(step, carry):
        for k in range(8):
            i = step * 8 + k
            gradient = share_ref[:, i, :]
            spread = spread_ref[pl.ds(i, 1), :]
            cross = jnp.sum(gradient * bias_ref[:, i, :], axis=0, keepdims=True) / channels
            slope = spread * spread * cross
            high, low = two_terms(gradient * spread)
            left = jnp.concatenate(
                [
                    high, low, high,
                    rows_of_two(jnp.broadcast_to(slope * mean_ref[pl.ds(i, 1), :], row.shape)),
                    rows_of_two(jnp.broadcast_to(slope, row.shape)),
                ],
                axis=0,
            )
            terms = f32_dot(left, right, TN)
            entries = pair_ref[i].astype(jnp.float32)
            out_ref[i] = (terms[:, :channels] - terms[:, channels:] * entries).astype(jnp.bfloat16)
        return carry

    lax.fori_loop(0, pair_ref.shape[0] // 8, rows, 0)


def output_kernel(parts_ref, combined_ref, out_weight_ref, pair_weight_ref):
    width = combined_ref.shape[0]
    rows = parts_ref.shape[1]
    for h in range(parts_ref.shape[0]):
        block = slice(h * rows, (h + 1) * rows)
        part = parts_ref[h].astype(jnp.float32)
        combined_ref[block, :] = part[:, : 4 * width]
        out_weight_ref[block, :] = part[:, 4 * width : 5 * width]
        share = part[: pair_weight_ref.shape[0], 5 * width :]
        pair_weight_ref[...] = share if h == 0 else pair_weight_ref[...] + share


def call(kernel, outs, *args, scratch=(), place=None, flops=0, after=(), outside=0, late=0):
    whole, anywhere = pl.BlockSpec(memory_space=pltpu.VMEM), pl.BlockSpec(memory_space=pl.ANY)
    specs = [anywhere] * outside + [whole] * (len(args) - outside)
    ahead = () if place is None else (place,)
    shapes = [jax.ShapeDtypeStruct(*o) for o in outs]
    moved = sum(math.prod(a.shape) * a.dtype.itemsize for a in list(args) + shapes)
    first = len(ahead) + len(args)
    last = first + len(after)

    def wrapped(*refs):
        given, rest = list(refs[:first]), refs[last:]
        if outside:
            *rest, arrived = rest
            held = rest[len(rest) - outside :]
            rest = rest[: len(rest) - outside]
            copies = []
            for k in range(outside):
                copies.append(
                    pltpu.make_async_copy(given[len(ahead) + k], held[k], arrived.at[k])
                )
                given[len(ahead) + k] = held[k]
            for copy in copies:
                copy.start()
            for copy in copies[: outside - late]:
                copy.wait()
            if late:
                given.insert(0, lambda: [copy.wait() for copy in copies[outside - late :]])
        kernel(*given, *rest)

    held = [pltpu.VMEM(a.shape, a.dtype) for a in args[:outside]]
    if outside:
        held.append(pltpu.SemaphoreType.DMA((outside,)))
    return pl.pallas_call(
        wrapped,
        out_shape=shapes,
        in_specs=[pl.BlockSpec(memory_space=pltpu.SMEM)] * len(ahead)
        + specs
        + [anywhere] * len(after),
        out_specs=[whole] * len(shapes),
        scratch_shapes=[*scratch, *held],
        compiler_params=pltpu.CompilerParams(
            vmem_limit_bytes=ARGUMENT_VMEM_LIMIT if outside else VMEM_LIMIT
        ),
        cost_estimate=pl.CostEstimate(flops=flops, bytes_accessed=moved, transcendentals=0),
    )(*ahead, *args, *after)


def swapped(mine, axis_name, distance):
    size = lax.axis_size(axis_name)
    return lax.ppermute(mine, axis_name, [(a, a ^ distance) for a in range(size)])


def fits_heads(alignment_rows, pair_entries, pair_weight):
    channels, heads = pair_weight.shape
    return (
        lax.axis_size("seq") == 4
        and lax.axis_size("res") == heads == 8
        and alignment_rows.shape[0] == 2 * SLOTS
        and alignment_rows.shape[1] == pair_entries.shape[0] == 64
        and alignment_rows.shape[2] == 2 * LANES
        and pair_entries.shape[1] == channels == LANES
    )


def head_body(
    alignment_rows, pair_entries, combined_weight, output_weight, pair_weight, updated_gradient
):
    sequences, residues, width = alignment_rows.shape
    channels, heads = pair_weight.shape
    tokens = sequences * residues
    seq_size, res_size = lax.axis_size("seq"), lax.axis_size("res")
    seq_half = seq_size // 2
    total = residues * res_size
    group = 2 * res_size
    groups = [[g * group + k for k in range(group)] for g in range(seq_half)]
    scale = 1.0 / math.sqrt(width // heads * sequences * seq_size)
    res_index, seq_index = lax.axis_index("res"), lax.axis_index("seq")
    place = jnp.stack([res_index % 2, seq_index // 2, res_index // 2]).astype(jnp.int32)
    bf16, f32 = jnp.bfloat16, jnp.float32

    def across(blocks):
        return lax.all_to_all(blocks, ("seq", "res"), 0, 0, axis_index_groups=groups, tiled=True)

    x, grad, wc, wo = alignment_rows, updated_gradient, combined_weight, output_weight
    query_blocks, bias, mean, spread = call(
        functools.partial(query_kernel, scale),
        [
            ((group, 3 * residues, LANES), bf16),
            ((heads, residues, LANES), f32),
            ((residues, LANES), f32),
            ((residues, LANES), f32),
        ],
        x, wc, pair_entries, pair_weight.T,
        flops=8 * tokens * width * width, outside=3, late=1,
    )
    query_blocks = across(query_blocks)
    (value_blocks,) = call(
        value_kernel, [((group, 2 * residues, LANES), bf16)], x, grad, wc, wo,
        flops=8 * tokens * width * width, outside=4,
    )
    query_blocks, value_blocks = lax.optimization_barrier((query_blocks, value_blocks))
    value_blocks = across(value_blocks)

    def scores(blocks, left_row, right_row, with_bias, kind):
        return call(
            functools.partial(score_kernel, residues, left_row, right_row, with_bias),
            [((total // 4, total), f32), ((total // 4, total), kind)],
            blocks, swapped(blocks, "res", 1),
            place=place, flops=2 * total * total * width,
        )

    logit_mine, logit_sent = scores(query_blocks, 0, residues, True, f32)
    logit_other = swapped(logit_sent, "seq", seq_half)
    quarter = (total // 4, total)
    softmax_out, probs = call(
        softmax_kernel, [(quarter, f32), (quarter, bf16)], logit_mine, logit_other,
        flops=total * total,
    )
    value_blocks, probs = lax.optimization_barrier((value_blocks, probs))
    probs_far = swapped(probs, "seq", seq_half)
    grad_mine, grad_sent = scores(value_blocks, residues, 0, False, bf16)
    grad_other = swapped(grad_sent, "seq", seq_half)
    probs_far = lax.optimization_barrier((probs_far, grad_sent))[0]

    def products(quarters, blocks, first_row, second_row, with_share, factor):
        rows = 2 * residues + (residues // 2 if with_share else 0)
        (out,) = call(
            functools.partial(
                product_kernel, residues, factor, first_row, second_row, with_share
            ),
            [((group, rows, LANES), bf16)],
            *quarters, blocks,
            scratch=[pltpu.VMEM((total, total), bf16)],
            place=place, flops=4 * total * total * width,
        )
        return out

    def with_near(mine, far):
        return mine, far, swapped(mine, "res", 1), swapped(far, "res", 1)

    attended = products(with_near(probs, probs_far), value_blocks, 0, residues, False, 1.0)
    attended_blocks = across(attended)
    grad_other = lax.optimization_barrier((attended, grad_other))[1]
    (grad_logits,) = call(
        softmax_gradient_kernel, [(quarter, bf16)], softmax_out, grad_mine, grad_other,
        flops=total * total,
    )
    grad_quarters = with_near(grad_logits, swapped(grad_logits, "seq", seq_half))
    grad_sums = products(grad_quarters, query_blocks, residues, 0, True, scale)
    grad_sums, attended_blocks = lax.optimization_barrier((grad_sums, attended_blocks))
    grad_blocks = across(grad_sums)

    updated, value_gate, normed, attended_sums = call(
        attended_weight_kernel,
        [
            (x.shape, bf16),
            ((tokens, 2 * width), bf16),
            ((tokens, width), bf16),
            ((width, 3 * width), bf16),
        ],
        x, grad, wc, wo, attended_blocks,
        flops=14 * tokens * width * width, outside=4,
    )
    share = pltpu.VMEM((heads, residues, LANES), f32)
    columns = 5 * width
    rows = width // res_size
    part_rows = ((res_size // 2, rows, columns), bf16)
    query_key, keep, send = call(
        query_weight_kernel,
        [((tokens, 2 * width), bf16), part_rows, part_rows],
        normed, grad_blocks, attended_sums,
        scratch=[pltpu.VMEM((width, columns), bf16)],
        place=place, flops=4 * tokens * width * width,
    )
    own, *sent = call(
        core_sum_kernel,
        [((rows, columns), f32)] + [((rows, columns), bf16)] * 3,
        keep, swapped(send, "res", 1), place=place,
    )
    received = [swapped(t, "res", 2 * flip) for flip, t in enumerate(sent, 1)]
    (pair_weight_part,) = call(
        pair_weight_kernel, [((heads, channels), f32)],
        grad_blocks, pair_entries, mean, spread,
        scratch=[share], flops=4 * tokens * width * width, after=(sent[0],),
    )
    (pair_gradient,) = call(
        functools.partial(pair_kernel, 2 * residues),
        [(pair_entries.shape, bf16)],
        grad_blocks, pair_entries, pair_weight.T, bias, mean, spread,
        scratch=[share], flops=8 * tokens * width * width,
    )
    received, pair_weight_part = lax.optimization_barrier((received, pair_weight_part))
    (part,) = call(
        plane_sum_kernel, [((rows, columns + channels), bf16)], own, pair_weight_part, *received
    )
    (alignment_gradient,) = call(
        alignment_kernel, [(x.shape, bf16)], x, wc, query_key, value_gate,
        flops=8 * tokens * width * width,
    )

    def added(mine, other):
        return (mine.astype(f32) + other.astype(f32)).astype(bf16)

    other_plane = swapped(part, "seq", 1)
    other_plane, alignment_gradient = lax.optimization_barrier((other_plane, alignment_gradient))
    part = added(part, other_plane)
    other_half = swapped(part, "seq", seq_half)
    other_half, pair_gradient = lax.optimization_barrier((other_half, pair_gradient))
    part = added(part, other_half)
    combined_gradient, output_gradient, pair_weight_gradient = call(
        output_kernel,
        [(wc.shape, f32), (wo.shape, f32), ((heads, channels), f32)],
        lax.all_gather(part, "res", axis=0),
    )
    return (
        updated,
        alignment_gradient,
        pair_gradient,
        combined_gradient,
        output_gradient,
        pair_weight_gradient.T,
    )


def body(alignment_rows, pair_entries, combined_weight, output_weight, pair_weight, updated_gradient):
    chosen = head_body if fits_heads(alignment_rows, pair_entries, pair_weight) else gathered_body
    return chosen(
        alignment_rows, pair_entries, combined_weight, output_weight, pair_weight, updated_gradient
    )


def solution(mesh):
    return jax.shard_map(
        body,
        mesh=mesh,
        in_specs=(
            P("seq", "res", None),
            P("res", "seq", None),
            P(),
            P(),
            P(),
            P("seq", "res", None),
        ),
        out_specs=(
            P("seq", "res", None),
            P("seq", "res", None),
            P("res", "seq", None),
            P(),
            P(),
            P(),
        ),
        check_vma=False,
    )
```

```python
import functools
import math

import jax
import jax.numpy as jnp
from jax import lax
from jax.experimental import pallas as pl
from jax.experimental.pallas import tpu as pltpu
from jax.sharding import PartitionSpec as P

eps_norm = 1e-05


def layer_normalize(values):
    values = values.astype(jnp.float32)
    center = values - jnp.mean(values, axis=-1, keepdims=True)
    broadcast_pair = lax.rsqrt(jnp.mean(center * center, axis=-1, keepdims=True) + eps_norm)
    return (center * broadcast_pair, broadcast_pair)


def layer_norm_backward(normalized_gradient, normalized_rows, broadcast_pair):
    mean_grad = jnp.mean(normalized_gradient, axis=-1, keepdims=True)
    mean_cross = jnp.mean(normalized_gradient * normalized_rows, axis=-1, keepdims=True)
    return broadcast_pair * (normalized_gradient - mean_grad - normalized_rows * mean_cross)


def split_heads(tensor, head_count):
    return tensor.reshape(
        tensor.shape[0], tensor.shape[1], head_count, tensor.shape[2] // head_count
    )


def merge_heads(tensor):
    return tensor.reshape(tensor.shape[0], tensor.shape[1], tensor.shape[2] * tensor.shape[3])


def gathered_body(
    alignment_rows, pair_entries, combined_weight, output_weight, pair_weight, updated_gradient
):
    sequence_count, residue_count, alignment_width = alignment_rows.shape
    head_count = pair_weight.shape[1]
    query_width = output_weight.shape[0]
    head_dim = query_width // head_count
    column_count = pair_entries.shape[1]
    token_count = sequence_count * residue_count
    score_scale = 1.0 / math.sqrt(head_dim * sequence_count * lax.axis_size("seq"))
    normalized_rows, broadcast_pair = layer_normalize(alignment_rows)
    normalized_rows_backward = normalized_rows.astype(jnp.bfloat16).reshape(
        token_count, alignment_width
    )
    projected = jnp.dot(
        normalized_rows_backward, combined_weight, preferred_element_type=jnp.float32
    ).reshape(sequence_count, residue_count, 4 * query_width)
    queries = (projected[..., :query_width] * score_scale).astype(jnp.bfloat16)
    key_rows = projected[..., query_width : 2 * query_width].astype(jnp.bfloat16)
    value_rows = projected[..., 2 * query_width : 3 * query_width].astype(jnp.bfloat16)
    gate_open = jax.nn.sigmoid(projected[..., 3 * query_width :])
    all_keys, all_values = (
        lax.all_gather(key_rows, "res", axis=1, tiled=True),
        lax.all_gather(value_rows, "res", axis=1, tiled=True),
    )
    query_heads = split_heads(queries, head_count)
    key_heads = split_heads(all_keys, head_count)
    value_heads = split_heads(all_values, head_count)
    score_terms = jnp.einsum(
        "sihd,sjhd->hij", query_heads, key_heads, preferred_element_type=jnp.float32
    )
    pair_normed, pair_spread = layer_normalize(pair_entries)
    pair_bias = jnp.einsum("ijc,ch->hij", pair_normed, pair_weight, precision=lax.Precision.HIGHEST)
    col_start = lax.axis_index("seq") * column_count
    own_block = lax.dynamic_slice_in_dim(score_terms, col_start, column_count, 2) + pair_bias
    logits = lax.psum(lax.dynamic_update_slice_in_dim(score_terms, own_block, col_start, 2), "seq")
    row_top = jnp.max(logits, axis=-1, keepdims=True)
    lifted = jnp.exp(logits - row_top)
    softmax_out = lifted / jnp.sum(lifted, axis=-1, keepdims=True)
    softmax_low = softmax_out.astype(jnp.bfloat16)
    attended = merge_heads(
        jnp.einsum("hij,sjhd->sihd", softmax_low, value_heads, preferred_element_type=jnp.float32)
    )
    gated_out = (gate_open * attended).astype(jnp.bfloat16)
    flattened_gated = gated_out.reshape(token_count, query_width)
    updated = (
        jnp.dot(flattened_gated, output_weight, preferred_element_type=jnp.float32)
        .astype(jnp.bfloat16)
        .reshape(sequence_count, residue_count, alignment_width)
    )
    flattened_gradient = updated_gradient.reshape(token_count, alignment_width)
    grad_gated = jnp.dot(
        flattened_gradient, output_weight.T, preferred_element_type=jnp.float32
    ).reshape(sequence_count, residue_count, query_width)
    out_local = jnp.dot(flattened_gated.T, flattened_gradient, preferred_element_type=jnp.float32)
    grad_attended = (grad_gated * gate_open).astype(jnp.bfloat16)
    grad_gate_logit = grad_gated * attended * gate_open * (1.0 - gate_open)
    attended_grad_heads = split_heads(grad_attended, head_count)
    grad_terms = jnp.einsum(
        "sihd,sjhd->hij", attended_grad_heads, value_heads, preferred_element_type=jnp.float32
    )
    grad_probs = lax.psum(grad_terms, "seq")
    row_dot = jnp.sum(softmax_out * grad_probs, axis=-1, keepdims=True)
    grad_logits = softmax_out * (grad_probs - row_dot)
    grad_logits_b = grad_logits.astype(jnp.bfloat16)
    logit_share = lax.dynamic_slice_in_dim(grad_logits, col_start, column_count, 2)
    grad_query_heads = (
        jnp.einsum("hij,sjhd->sihd", grad_logits_b, key_heads, preferred_element_type=jnp.float32)
        * score_scale
    )
    key_part = jnp.einsum(
        "hij,sihd->jshd", grad_logits_b, query_heads, preferred_element_type=jnp.float32
    )
    value_part = jnp.einsum(
        "hij,sihd->jshd", softmax_low, attended_grad_heads, preferred_element_type=jnp.float32
    )
    summed = lax.psum_scatter(
        jnp.concatenate([merge_heads(key_part), merge_heads(value_part)], axis=-1),
        "res",
        scatter_dimension=0,
        tiled=True,
    )
    key_value_grads = jnp.transpose(summed, (1, 0, 2))
    projected_gradient = jnp.concatenate(
        [merge_heads(grad_query_heads), key_value_grads, grad_gate_logit], axis=-1
    )
    projected_gradient = projected_gradient.astype(jnp.bfloat16).reshape(
        token_count, 4 * query_width
    )
    qkvg_local = jnp.dot(
        normalized_rows_backward.T, projected_gradient, preferred_element_type=jnp.float32
    )
    normalized_gradient = jnp.dot(
        projected_gradient, combined_weight.T, preferred_element_type=jnp.float32
    ).reshape(sequence_count, residue_count, alignment_width)
    alignment_gradient = layer_norm_backward(
        normalized_gradient, normalized_rows, broadcast_pair
    ).astype(jnp.bfloat16)
    pair_w_local = jnp.einsum(
        "ijc,hij->ch", pair_normed, logit_share, precision=lax.Precision.HIGHEST
    )
    grad_pair_normed = jnp.einsum(
        "hij,ch->ijc", logit_share, pair_weight, precision=lax.Precision.HIGHEST
    )
    pair_gradient = layer_norm_backward(grad_pair_normed, pair_normed, pair_spread).astype(
        jnp.bfloat16
    )
    combined_weight_gradient, output_weight_gradient, pair_weight_gradient = lax.psum(
        (qkvg_local, out_local, pair_w_local), ("seq", "res")
    )
    return (
        updated,
        alignment_gradient,
        pair_gradient,
        combined_weight_gradient,
        output_weight_gradient,
        pair_weight_gradient,
    )


VMEM_LIMIT = 20 * 1024 * 1024
ARGUMENT_VMEM_LIMIT = 56 * 1024 * 1024
LANES = 128
SLOTS = 4
NT = (((1,), (1,)), ((), ()))
TN = (((0,), (0,)), ((), ()))


def f32_dot(left, right, dims=None):
    if dims is None:
        return jnp.dot(left, right, preferred_element_type=jnp.float32)
    return lax.dot_general(left, right, dims, preferred_element_type=jnp.float32)


def two_terms(values):
    high = values.astype(jnp.bfloat16)
    return high, (values - high.astype(jnp.float32)).astype(jnp.bfloat16)


def slot_select(pieces):
    slot = lax.broadcasted_iota(jnp.int32, pieces[0].shape, 1) // (LANES // SLOTS)
    result = pieces[0]
    for k in range(1, SLOTS):
        result = jnp.where(slot == k, pieces[k], result)
    return result


def pack_heads(out_ref, row, tensor, residues):
    for core in range(2):
        for tile in range(tensor.shape[1] // LANES):
            rolled = []
            for s in range(SLOTS):
                start = (core * SLOTS + s) * residues
                piece = tensor[start : start + residues, tile * LANES : (tile + 1) * LANES]
                rolled.append(pltpu.roll(piece, s * LANES // SLOTS, 1) if s else piece)
            for j in range(SLOTS):
                block = slot_select([rolled[(k - j) % SLOTS] for k in range(SLOTS)])
                out_ref[(tile * SLOTS + j) * 2 + core, row : row + residues, :] = block.astype(
                    jnp.bfloat16
                )


def unpack_heads(in_ref, row, residues, tiles):
    rows = []
    for core in range(2):
        for s in range(SLOTS):
            pieces = []
            for tile in range(tiles):
                blocks = [
                    in_ref[
                        (tile * SLOTS + (k - s) % SLOTS) * 2 + core, row : row + residues, :
                    ].astype(jnp.float32)
                    for k in range(SLOTS)
                ]
                block = slot_select(blocks)
                pieces.append(pltpu.roll(block, LANES - s * LANES // SLOTS, 1) if s else block)
            rows.append(jnp.concatenate(pieces, axis=1))
    return jnp.concatenate(rows, axis=0)


def normalized(x_ref):
    width = x_ref.shape[-1]
    values = x_ref[...].reshape(-1, width).astype(jnp.float32)
    return layer_normalize(values)


def gate_of(logits):
    return 1.0 / (1.0 + jnp.exp(-logits))


def value_kernel(x_ref, grad_ref, wc_ref, wo_ref, out_ref):
    residues, width = x_ref.shape[1], x_ref.shape[2]
    normed = normalized(x_ref)[0].astype(jnp.bfloat16)
    values = f32_dot(normed, wc_ref[:, 2 * width : 3 * width])
    gate = gate_of(f32_dot(normed, wc_ref[:, 3 * width :]))
    grad_gated = f32_dot(grad_ref[...].reshape(-1, width), wo_ref[...], NT)
    pack_heads(out_ref, 0, values, residues)
    pack_heads(out_ref, residues, grad_gated * gate, residues)


def centred(weight):
    return weight - jnp.mean(weight, axis=1, keepdims=True)


def query_kernel(
    scale, arrive, x_ref, wc_ref, pair_ref, weight_ref, out_ref, bias_ref, mean_ref, spread_ref
):
    residues, width = x_ref.shape[1], x_ref.shape[2]
    heads = weight_ref.shape[0]
    normed = normalized(x_ref)[0].astype(jnp.bfloat16)
    pack_heads(out_ref, 0, f32_dot(normed, wc_ref[:, :width]) * scale, residues)
    pack_heads(out_ref, residues, f32_dot(normed, wc_ref[:, width : 2 * width]), residues)

    arrive()
    columns, channels = pair_ref.shape[1], pair_ref.shape[2]
    weight = centred(weight_ref[...])
    first = weight.astype(jnp.bfloat16)
    second, third = two_terms(weight - first.astype(jnp.float32))
    share = jnp.full((heads, channels), 1.0 / channels, jnp.bfloat16)
    left = jnp.concatenate([first, second, third, share], axis=0)
    average = jnp.full((channels, channels), 1.0 / channels, jnp.bfloat16)
    step_rows = 32

    def rows(step, carry):
        start = pl.multiple_of(step * step_rows, step_rows)
        entries = pair_ref[pl.ds(start, step_rows)].reshape(step_rows * columns, channels)
        center = entries.astype(jnp.float32) - f32_dot(entries, average)
        high, low = two_terms(center * center)
        variance = f32_dot(share, high, NT) + f32_dot(share, low, NT)
        spread = lax.rsqrt(variance + eps_norm)
        raw = f32_dot(left, entries, NT)
        bias = spread * (raw[:heads] + raw[heads : 2 * heads] + raw[2 * heads : 3 * heads])
        for k in range(step_rows):
            lanes = slice(k * columns, (k + 1) * columns)
            bias_ref[:, start + k, :] = bias[:, lanes]
            mean_ref[pl.ds(start + k, 1), :] = raw[3 * heads : 3 * heads + 1, lanes]
            spread_ref[pl.ds(start + k, 1), :] = spread[:1, lanes]
        return carry

    lax.fori_loop(0, pair_ref.shape[0] // step_rows, rows, 0)
    half = residues // 2
    for h in range(heads):
        for core in range(2):
            high, low = two_terms(bias_ref[h, core * half : (core + 1) * half, :])
            out_ref[h * 2 + core, 2 * residues : 2 * residues + half, :] = high
            out_ref[h * 2 + core, 2 * residues + half : 3 * residues, :] = low


def lanes_of(blocks_ref, row, residues):
    count = blocks_ref.shape[0] // 2
    planes = [
        blocks_ref[p * count : (p + 1) * count, row : row + residues, :].reshape(-1, LANES)
        for p in range(2)
    ]
    return jnp.concatenate(planes, axis=1)


def score_kernel(
    residues, left_row, right_row, with_bias, place_ref, own_ref, other_ref, mine_ref, sent_ref
):
    core, half = place_ref[0], place_ref[1]
    count = own_ref.shape[0] // 2
    part = residues // 2
    right = jnp.concatenate(
        [lanes_of(own_ref, right_row, residues), lanes_of(other_ref, right_row, residues)], axis=1
    )
    for which, ref in ((half, mine_ref), (1 - half, sent_ref)):
        left = []
        for k in range(count // 2):
            block = which * (count // 2) + k
            rows = pl.ds(pl.multiple_of(left_row + core * part, part), part)
            left.append(
                jnp.concatenate(
                    [
                        r[p * count + block, rows, :]
                        for r in (own_ref, other_ref)
                        for p in range(2)
                    ],
                    axis=1,
                )
            )
        ref[...] = f32_dot(jnp.concatenate(left, axis=0), right, NT).astype(ref.dtype)
        if with_bias:
            for p in range(2):
                columns = pl.ds(pl.multiple_of((half * 2 + p) * LANES, LANES), LANES)
                for k in range(count // 2):
                    block = p * count + which * (count // 2) + k
                    high = own_ref[block, 2 * residues : 2 * residues + part, :]
                    low = own_ref[block, 2 * residues + part : 3 * residues, :]
                    bias = high.astype(jnp.float32) + low.astype(jnp.float32)
                    ref[k * part : (k + 1) * part, columns] += bias


def softmax_kernel(logit_ref, other_ref, out_ref, low_ref):
    logits = logit_ref[...] + other_ref[...]
    lifted = jnp.exp(logits - jnp.max(logits, axis=-1, keepdims=True))
    softmax_out = lifted / jnp.sum(lifted, axis=-1, keepdims=True)
    out_ref[...] = softmax_out
    low_ref[...] = softmax_out.astype(jnp.bfloat16)


def softmax_gradient_kernel(softmax_ref, grad_ref, other_ref, out_ref):
    softmax_out = softmax_ref[...]
    grad_probs = grad_ref[...] + other_ref[...].astype(jnp.float32)
    row_dot = jnp.sum(softmax_out * grad_probs, axis=-1, keepdims=True)
    out_ref[...] = (softmax_out * (grad_probs - row_dot)).astype(jnp.bfloat16)


def product_kernel(
    residues, scale, first_row, second_row, with_share,
    place_ref, own_ref, far_ref, near_ref, corner_ref, blocks_ref, out_ref, whole_ref,
):
    core, half = place_ref[0], place_ref[1]
    count = blocks_ref.shape[0] // 2
    part = residues // 2
    quarters = (
        (own_ref, core, half), (far_ref, core, 1 - half),
        (near_ref, 1 - core, half), (corner_ref, 1 - core, 1 - half),
    )
    for ref, c, z in quarters:
        for k in range(count // 2):
            start = (z * (count // 2) + k) * residues + c * part
            whole_ref[pl.ds(pl.multiple_of(start, part), part), :] = ref[k * part : (k + 1) * part, :]
    whole = whole_ref[...]
    if with_share:
        for p in range(2):
            columns = pl.ds(pl.multiple_of((half * 2 + p) * LANES, LANES), LANES)
            for q in range(count):
                rows = pl.ds(pl.multiple_of(q * residues + core * part, part), part)
                out_ref[p * count + q, 2 * residues : 2 * residues + part, :] = whole_ref[rows, columns]
    first = f32_dot(whole, lanes_of(blocks_ref, first_row, residues)) * scale
    second = f32_dot(whole, lanes_of(blocks_ref, second_row, residues), TN)
    for row, product in ((0, first), (residues, second)):
        for p in range(2):
            out_ref[p * count : (p + 1) * count, row : row + residues, :] = (
                product[:, p * LANES : (p + 1) * LANES]
                .astype(jnp.bfloat16)
                .reshape(count, residues, LANES)
            )


def share_of(blocks_ref, row, part, heads):
    return jnp.concatenate(
        [
            blocks_ref[:, row : row + part, :]
            .astype(jnp.float32)
            .reshape(heads, 2 * part, LANES)
        ],
        axis=0,
    )


def attended_weight_kernel(
    x_ref, grad_ref, wc_ref, wo_ref, blocks_ref, updated_ref, projected_ref, normed_ref, sums_ref
):
    residues, width = x_ref.shape[1], x_ref.shape[2]
    tiles = width // LANES
    normed = normalized(x_ref)[0].astype(jnp.bfloat16)
    normed_ref[...] = normed
    gate = gate_of(f32_dot(normed, wc_ref[:, 3 * width :]))
    grad = grad_ref[...].reshape(-1, width)
    grad_gated = f32_dot(grad, wo_ref[...], NT)
    attended = unpack_heads(blocks_ref, 0, residues, tiles)
    gated = (gate * attended).astype(jnp.bfloat16)
    updated_ref[...] = f32_dot(gated, wo_ref[...]).astype(jnp.bfloat16).reshape(updated_ref.shape)
    projected_ref[:, :width] = unpack_heads(blocks_ref, residues, residues, tiles).astype(
        jnp.bfloat16
    )
    projected_ref[:, width:] = (grad_gated * attended * gate * (1.0 - gate)).astype(jnp.bfloat16)
    sums_ref[:, : 2 * width] = f32_dot(normed, projected_ref[...], TN).astype(jnp.bfloat16)
    sums_ref[:, 2 * width :] = f32_dot(gated, grad, TN).astype(jnp.bfloat16)


def query_weight_kernel(
    arrive, place_ref, normed_ref, attended_sums_ref, blocks_ref,
    projected_ref, keep_ref, send_ref, sums_ref,
):
    width = normed_ref.shape[1]
    tiles, residues = width // LANES, (blocks_ref.shape[1] * 2) // 5
    core = place_ref[0]
    for t in range(2):
        projected_ref[:, t * width : (t + 1) * width] = unpack_heads(
            blocks_ref, t * residues, residues, tiles
        ).astype(jnp.bfloat16)
    arrive()
    sums_ref[:, : 2 * width] = f32_dot(normed_ref[...], projected_ref[...], TN).astype(
        jnp.bfloat16
    )
    sums_ref[:, 2 * width :] = attended_sums_ref[...]
    rows = keep_ref.shape[1]
    for which, ref in ((core, keep_ref), (1 - core, send_ref)):
        for block in range(keep_ref.shape[0]):
            start = pl.multiple_of((2 * block + which) * rows, rows)
            ref[block] = sums_ref[pl.ds(start, rows), :]


def core_sum_kernel(place_ref, keep_ref, other_ref, own_ref, *send_refs):
    chip = place_ref[2]
    for flip, ref in enumerate((own_ref, *send_refs)):
        block = jnp.bitwise_xor(chip, flip)
        total = keep_ref[block].astype(jnp.float32) + other_ref[block].astype(jnp.float32)
        ref[...] = total.astype(ref.dtype)


def plane_sum_kernel(own_ref, pair_weight_ref, *refs):
    *received, out_ref = refs
    total = own_ref[...]
    for ref in received:
        total += ref[...].astype(jnp.float32)
    count = own_ref.shape[1]
    heads = pair_weight_ref.shape[0]
    out_ref[:, :count] = total.astype(out_ref.dtype)
    rest = jnp.zeros((out_ref.shape[0] - heads, out_ref.shape[1] - count), jnp.float32)
    out_ref[:, count:] = jnp.concatenate([pair_weight_ref[...], rest], axis=0).astype(
        out_ref.dtype
    )


def pair_weight_kernel(blocks_ref, pair_ref, mean_ref, spread_ref, out_ref, share_ref):
    heads, part = share_ref.shape[0], pair_ref.shape[0] // 2
    share_ref[...] = share_of(blocks_ref, blocks_ref.shape[1] - part, part, heads)

    def rows(step, carry):
        total, shift = carry
        for k in range(8):
            i = step * 8 + k
            scaled = share_ref[:, i, :] * spread_ref[pl.ds(i, 1), :]
            high, low = two_terms(scaled)
            total += f32_dot(jnp.concatenate([high, low], axis=0), pair_ref[i])
            shift += (high.astype(jnp.float32) + low.astype(jnp.float32)) * mean_ref[pl.ds(i, 1), :]
        return total, shift

    channels = pair_ref.shape[2]
    total, shift = lax.fori_loop(
        0,
        pair_ref.shape[0] // 8,
        rows,
        (jnp.zeros((2 * heads, channels), jnp.float32), jnp.zeros((heads, LANES), jnp.float32)),
    )
    out_ref[...] = total[:heads] + total[heads:] - jnp.sum(shift, axis=1, keepdims=True)


def alignment_kernel(x_ref, wc_ref, query_key_ref, value_gate_ref, out_ref):
    normed, spread = normalized(x_ref)
    width = x_ref.shape[2]
    gradient = f32_dot(query_key_ref[...], wc_ref[:, : 2 * width], NT) + f32_dot(
        value_gate_ref[...], wc_ref[:, 2 * width :], NT
    )
    out_ref[...] = (
        layer_norm_backward(gradient, normed, spread).astype(jnp.bfloat16).reshape(out_ref.shape)
    )


def pair_kernel(blocks_row, blocks_ref, pair_ref, weight_ref, bias_ref, mean_ref, spread_ref, out_ref, share_ref):
    heads, channels = weight_ref.shape
    part = pair_ref.shape[0] // 2
    share_ref[...] = share_of(blocks_ref, blocks_row, part, heads)
    first, second = two_terms(centred(weight_ref[...]))
    zero = jnp.zeros((heads, channels), jnp.bfloat16)
    top = lax.broadcasted_iota(jnp.int32, (heads, channels), 0) < 2
    ones = jnp.where(top, 1.0, 0.0).astype(jnp.bfloat16)
    right = jnp.concatenate(
        [
            jnp.concatenate([first, first, second, ones, zero], axis=0),
            jnp.concatenate([zero, zero, zero, zero, ones], axis=0),
        ],
        axis=1,
    )
    row = lax.broadcasted_iota(jnp.int32, (heads, LANES), 0)

    def rows_of_two(value):
        high, low = two_terms(value)
        high, low = high.astype(jnp.float32), low.astype(jnp.float32)
        return jnp.where(row == 0, high, jnp.where(row == 1, low, 0.0)).astype(jnp.bfloat16)

    def rows(step, carry):
        for k in range(8):
            i = step * 8 + k
            gradient = share_ref[:, i, :]
            spread = spread_ref[pl.ds(i, 1), :]
            cross = jnp.sum(gradient * bias_ref[:, i, :], axis=0, keepdims=True) / channels
            slope = spread * spread * cross
            high, low = two_terms(gradient * spread)
            left = jnp.concatenate(
                [
                    high, low, high,
                    rows_of_two(jnp.broadcast_to(slope * mean_ref[pl.ds(i, 1), :], row.shape)),
                    rows_of_two(jnp.broadcast_to(slope, row.shape)),
                ],
                axis=0,
            )
            terms = f32_dot(left, right, TN)
            entries = pair_ref[i].astype(jnp.float32)
            out_ref[i] = (terms[:, :channels] - terms[:, channels:] * entries).astype(jnp.bfloat16)
        return carry

    lax.fori_loop(0, pair_ref.shape[0] // 8, rows, 0)


def output_kernel(parts_ref, combined_ref, out_weight_ref, pair_weight_ref):
    width = combined_ref.shape[0]
    rows = parts_ref.shape[1]
    for h in range(parts_ref.shape[0]):
        block = slice(h * rows, (h + 1) * rows)
        part = parts_ref[h].astype(jnp.float32)
        combined_ref[block, :] = part[:, : 4 * width]
        out_weight_ref[block, :] = part[:, 4 * width : 5 * width]
        share = part[: pair_weight_ref.shape[0], 5 * width :]
        pair_weight_ref[...] = share if h == 0 else pair_weight_ref[...] + share


def call(kernel, outs, *args, scratch=(), place=None, flops=0, after=(), outside=0, late=0):
    whole, anywhere = pl.BlockSpec(memory_space=pltpu.VMEM), pl.BlockSpec(memory_space=pl.ANY)
    specs = [anywhere] * outside + [whole] * (len(args) - outside)
    ahead = () if place is None else (place,)
    shapes = [jax.ShapeDtypeStruct(*o) for o in outs]
    moved = sum(math.prod(a.shape) * a.dtype.itemsize for a in list(args) + shapes)
    first = len(ahead) + len(args)
    last = first + len(after)

    def wrapped(*refs):
        given, rest = list(refs[:first]), refs[last:]
        if outside:
            *rest, arrived = rest
            held = rest[len(rest) - outside :]
            rest = rest[: len(rest) - outside]
            copies = []
            for k in range(outside):
                copies.append(
                    pltpu.make_async_copy(given[len(ahead) + k], held[k], arrived.at[k])
                )
                given[len(ahead) + k] = held[k]
            for copy in copies:
                copy.start()
            for copy in copies[: outside - late]:
                copy.wait()
            if late:
                given.insert(0, lambda: [copy.wait() for copy in copies[outside - late :]])
        kernel(*given, *rest)

    held = [pltpu.VMEM(a.shape, a.dtype) for a in args[:outside]]
    if outside:
        held.append(pltpu.SemaphoreType.DMA((outside,)))
    return pl.pallas_call(
        wrapped,
        out_shape=shapes,
        in_specs=[pl.BlockSpec(memory_space=pltpu.SMEM)] * len(ahead)
        + specs
        + [anywhere] * len(after),
        out_specs=[whole] * len(shapes),
        scratch_shapes=[*scratch, *held],
        compiler_params=pltpu.CompilerParams(
            vmem_limit_bytes=ARGUMENT_VMEM_LIMIT if outside else VMEM_LIMIT
        ),
        cost_estimate=pl.CostEstimate(flops=flops, bytes_accessed=moved, transcendentals=0),
    )(*ahead, *args, *after)


def swapped(mine, axis_name, distance):
    size = lax.axis_size(axis_name)
    return lax.ppermute(mine, axis_name, [(a, a ^ distance) for a in range(size)])


def fits_heads(alignment_rows, pair_entries, pair_weight):
    channels, heads = pair_weight.shape
    return (
        lax.axis_size("seq") == 4
        and lax.axis_size("res") == heads == 8
        and alignment_rows.shape[0] == 2 * SLOTS
        and alignment_rows.shape[1] == pair_entries.shape[0] == 64
        and alignment_rows.shape[2] == 2 * LANES
        and pair_entries.shape[1] == channels == LANES
    )


def head_body(
    alignment_rows, pair_entries, combined_weight, output_weight, pair_weight, updated_gradient
):
    sequences, residues, width = alignment_rows.shape
    channels, heads = pair_weight.shape
    tokens = sequences * residues
    seq_size, res_size = lax.axis_size("seq"), lax.axis_size("res")
    seq_half = seq_size // 2
    total = residues * res_size
    group = 2 * res_size
    groups = [[g * group + k for k in range(group)] for g in range(seq_half)]
    scale = 1.0 / math.sqrt(width // heads * sequences * seq_size)
    res_index, seq_index = lax.axis_index("res"), lax.axis_index("seq")
    place = jnp.stack([res_index % 2, seq_index // 2, res_index // 2]).astype(jnp.int32)
    bf16, f32 = jnp.bfloat16, jnp.float32

    def across(blocks):
        return lax.all_to_all(blocks, ("seq", "res"), 0, 0, axis_index_groups=groups, tiled=True)

    x, grad, wc, wo = alignment_rows, updated_gradient, combined_weight, output_weight
    query_blocks, bias, mean, spread = call(
        functools.partial(query_kernel, scale),
        [
            ((group, 3 * residues, LANES), bf16),
            ((heads, residues, LANES), f32),
            ((residues, LANES), f32),
            ((residues, LANES), f32),
        ],
        x, wc, pair_entries, pair_weight.T,
        flops=8 * tokens * width * width, outside=3, late=1,
    )
    query_blocks = across(query_blocks)
    (value_blocks,) = call(
        value_kernel, [((group, 2 * residues, LANES), bf16)], x, grad, wc, wo,
        flops=8 * tokens * width * width, outside=4,
    )
    query_blocks, value_blocks = lax.optimization_barrier((query_blocks, value_blocks))
    value_blocks = across(value_blocks)

    def scores(blocks, left_row, right_row, with_bias, kind):
        return call(
            functools.partial(score_kernel, residues, left_row, right_row, with_bias),
            [((total // 4, total), f32), ((total // 4, total), kind)],
            blocks, swapped(blocks, "res", 1),
            place=place, flops=2 * total * total * width,
        )

    logit_mine, logit_sent = scores(query_blocks, 0, residues, True, f32)
    logit_other = swapped(logit_sent, "seq", seq_half)
    quarter = (total // 4, total)
    softmax_out, probs = call(
        softmax_kernel, [(quarter, f32), (quarter, bf16)], logit_mine, logit_other,
        flops=total * total,
    )
    value_blocks, probs = lax.optimization_barrier((value_blocks, probs))
    probs_far = swapped(probs, "seq", seq_half)
    grad_mine, grad_sent = scores(value_blocks, residues, 0, False, bf16)
    grad_other = swapped(grad_sent, "seq", seq_half)
    probs_far, grad_other = lax.optimization_barrier((probs_far, grad_other))

    def products(quarters, blocks, first_row, second_row, with_share, factor):
        rows = 2 * residues + (residues // 2 if with_share else 0)
        (out,) = call(
            functools.partial(
                product_kernel, residues, factor, first_row, second_row, with_share
            ),
            [((group, rows, LANES), bf16)],
            *quarters, blocks,
            scratch=[pltpu.VMEM((total, total), bf16)],
            place=place, flops=4 * total * total * width,
        )
        return out

    def with_near(mine, far):
        return mine, far, swapped(mine, "res", 1), swapped(far, "res", 1)

    attended = products(with_near(probs, probs_far), value_blocks, 0, residues, False, 1.0)
    attended_blocks = across(attended)
    grad_other = lax.optimization_barrier((attended, grad_other))[1]
    (grad_logits,) = call(
        softmax_gradient_kernel, [(quarter, bf16)], softmax_out, grad_mine, grad_other,
        flops=total * total,
    )
    grad_quarters = with_near(grad_logits, swapped(grad_logits, "seq", seq_half))
    grad_sums = products(grad_quarters, query_blocks, residues, 0, True, scale)
    grad_sums, attended_blocks = lax.optimization_barrier((grad_sums, attended_blocks))
    grad_blocks = across(grad_sums)

    updated, value_gate, normed, attended_sums = call(
        attended_weight_kernel,
        [
            (x.shape, bf16),
            ((tokens, 2 * width), bf16),
            ((tokens, width), bf16),
            ((width, 3 * width), bf16),
        ],
        x, grad, wc, wo, attended_blocks,
        flops=14 * tokens * width * width, outside=4,
    )
    share = pltpu.VMEM((heads, residues, LANES), f32)
    columns = 5 * width
    rows = width // res_size
    part_rows = ((res_size // 2, rows, columns), bf16)
    query_key, keep, send = call(
        query_weight_kernel,
        [((tokens, 2 * width), bf16), part_rows, part_rows],
        normed, attended_sums, grad_blocks,
        scratch=[pltpu.VMEM((width, columns), bf16)],
        place=place, flops=4 * tokens * width * width, outside=2, late=2,
    )
    own, *sent = call(
        core_sum_kernel,
        [((rows, columns), f32)] + [((rows, columns), bf16)] * 3,
        keep, swapped(send, "res", 1), place=place,
    )
    received = [swapped(t, "res", 2 * flip) for flip, t in enumerate(sent, 1)]
    (pair_weight_part,) = call(
        pair_weight_kernel, [((heads, channels), f32)],
        grad_blocks, pair_entries, mean, spread,
        scratch=[share], flops=4 * tokens * width * width, after=(sent[0],),
    )
    (pair_gradient,) = call(
        functools.partial(pair_kernel, 2 * residues),
        [(pair_entries.shape, bf16)],
        grad_blocks, pair_entries, pair_weight.T, bias, mean, spread,
        scratch=[share], flops=8 * tokens * width * width,
    )
    received, pair_weight_part = lax.optimization_barrier((received, pair_weight_part))
    (part,) = call(
        plane_sum_kernel, [((rows, columns + channels), bf16)], own, pair_weight_part, *received
    )
    (alignment_gradient,) = call(
        alignment_kernel, [(x.shape, bf16)], x, wc, query_key, value_gate,
        flops=8 * tokens * width * width,
    )

    def added(mine, other):
        return (mine.astype(f32) + other.astype(f32)).astype(bf16)

    other_plane = swapped(part, "seq", 1)
    other_plane, alignment_gradient = lax.optimization_barrier((other_plane, alignment_gradient))
    part = added(part, other_plane)
    other_half = swapped(part, "seq", seq_half)
    other_half, pair_gradient = lax.optimization_barrier((other_half, pair_gradient))
    part = added(part, other_half)
    combined_gradient, output_gradient, pair_weight_gradient = call(
        output_kernel,
        [(wc.shape, f32), (wo.shape, f32), ((heads, channels), f32)],
        lax.all_gather(part, "res", axis=0),
    )
    return (
        updated,
        alignment_gradient,
        pair_gradient,
        combined_gradient,
        output_gradient,
        pair_weight_gradient.T,
    )


def body(alignment_rows, pair_entries, combined_weight, output_weight, pair_weight, updated_gradient):
    chosen = head_body if fits_heads(alignment_rows, pair_entries, pair_weight) else gathered_body
    return chosen(
        alignment_rows, pair_entries, combined_weight, output_weight, pair_weight, updated_gradient
    )


def solution(mesh):
    return jax.shard_map(
        body,
        mesh=mesh,
        in_specs=(
            P("seq", "res", None),
            P("res", "seq", None),
            P(),
            P(),
            P(),
            P("seq", "res", None),
        ),
        out_specs=(
            P("seq", "res", None),
            P("seq", "res", None),
            P("res", "seq", None),
            P(),
            P(),
            P(),
        ),
        check_vma=False,
    )
```

```python
import functools
import math

import jax
import jax.numpy as jnp
from jax import lax
from jax.experimental import pallas as pl
from jax.experimental.pallas import tpu as pltpu
from jax.sharding import PartitionSpec as P

eps_norm = 1e-05


def layer_normalize(values):
    values = values.astype(jnp.float32)
    center = values - jnp.mean(values, axis=-1, keepdims=True)
    broadcast_pair = lax.rsqrt(jnp.mean(center * center, axis=-1, keepdims=True) + eps_norm)
    return (center * broadcast_pair, broadcast_pair)


def layer_norm_backward(normalized_gradient, normalized_rows, broadcast_pair):
    mean_grad = jnp.mean(normalized_gradient, axis=-1, keepdims=True)
    mean_cross = jnp.mean(normalized_gradient * normalized_rows, axis=-1, keepdims=True)
    return broadcast_pair * (normalized_gradient - mean_grad - normalized_rows * mean_cross)


def split_heads(tensor, head_count):
    return tensor.reshape(
        tensor.shape[0], tensor.shape[1], head_count, tensor.shape[2] // head_count
    )


def merge_heads(tensor):
    return tensor.reshape(tensor.shape[0], tensor.shape[1], tensor.shape[2] * tensor.shape[3])


def gathered_body(
    alignment_rows, pair_entries, combined_weight, output_weight, pair_weight, updated_gradient
):
    sequence_count, residue_count, alignment_width = alignment_rows.shape
    head_count = pair_weight.shape[1]
    query_width = output_weight.shape[0]
    head_dim = query_width // head_count
    column_count = pair_entries.shape[1]
    token_count = sequence_count * residue_count
    score_scale = 1.0 / math.sqrt(head_dim * sequence_count * lax.axis_size("seq"))
    normalized_rows, broadcast_pair = layer_normalize(alignment_rows)
    normalized_rows_backward = normalized_rows.astype(jnp.bfloat16).reshape(
        token_count, alignment_width
    )
    projected = jnp.dot(
        normalized_rows_backward, combined_weight, preferred_element_type=jnp.float32
    ).reshape(sequence_count, residue_count, 4 * query_width)
    queries = (projected[..., :query_width] * score_scale).astype(jnp.bfloat16)
    key_rows = projected[..., query_width : 2 * query_width].astype(jnp.bfloat16)
    value_rows = projected[..., 2 * query_width : 3 * query_width].astype(jnp.bfloat16)
    gate_open = jax.nn.sigmoid(projected[..., 3 * query_width :])
    all_keys, all_values = (
        lax.all_gather(key_rows, "res", axis=1, tiled=True),
        lax.all_gather(value_rows, "res", axis=1, tiled=True),
    )
    query_heads = split_heads(queries, head_count)
    key_heads = split_heads(all_keys, head_count)
    value_heads = split_heads(all_values, head_count)
    score_terms = jnp.einsum(
        "sihd,sjhd->hij", query_heads, key_heads, preferred_element_type=jnp.float32
    )
    pair_normed, pair_spread = layer_normalize(pair_entries)
    pair_bias = jnp.einsum("ijc,ch->hij", pair_normed, pair_weight, precision=lax.Precision.HIGHEST)
    col_start = lax.axis_index("seq") * column_count
    own_block = lax.dynamic_slice_in_dim(score_terms, col_start, column_count, 2) + pair_bias
    logits = lax.psum(lax.dynamic_update_slice_in_dim(score_terms, own_block, col_start, 2), "seq")
    row_top = jnp.max(logits, axis=-1, keepdims=True)
    lifted = jnp.exp(logits - row_top)
    softmax_out = lifted / jnp.sum(lifted, axis=-1, keepdims=True)
    softmax_low = softmax_out.astype(jnp.bfloat16)
    attended = merge_heads(
        jnp.einsum("hij,sjhd->sihd", softmax_low, value_heads, preferred_element_type=jnp.float32)
    )
    gated_out = (gate_open * attended).astype(jnp.bfloat16)
    flattened_gated = gated_out.reshape(token_count, query_width)
    updated = (
        jnp.dot(flattened_gated, output_weight, preferred_element_type=jnp.float32)
        .astype(jnp.bfloat16)
        .reshape(sequence_count, residue_count, alignment_width)
    )
    flattened_gradient = updated_gradient.reshape(token_count, alignment_width)
    grad_gated = jnp.dot(
        flattened_gradient, output_weight.T, preferred_element_type=jnp.float32
    ).reshape(sequence_count, residue_count, query_width)
    out_local = jnp.dot(flattened_gated.T, flattened_gradient, preferred_element_type=jnp.float32)
    grad_attended = (grad_gated * gate_open).astype(jnp.bfloat16)
    grad_gate_logit = grad_gated * attended * gate_open * (1.0 - gate_open)
    attended_grad_heads = split_heads(grad_attended, head_count)
    grad_terms = jnp.einsum(
        "sihd,sjhd->hij", attended_grad_heads, value_heads, preferred_element_type=jnp.float32
    )
    grad_probs = lax.psum(grad_terms, "seq")
    row_dot = jnp.sum(softmax_out * grad_probs, axis=-1, keepdims=True)
    grad_logits = softmax_out * (grad_probs - row_dot)
    grad_logits_b = grad_logits.astype(jnp.bfloat16)
    logit_share = lax.dynamic_slice_in_dim(grad_logits, col_start, column_count, 2)
    grad_query_heads = (
        jnp.einsum("hij,sjhd->sihd", grad_logits_b, key_heads, preferred_element_type=jnp.float32)
        * score_scale
    )
    key_part = jnp.einsum(
        "hij,sihd->jshd", grad_logits_b, query_heads, preferred_element_type=jnp.float32
    )
    value_part = jnp.einsum(
        "hij,sihd->jshd", softmax_low, attended_grad_heads, preferred_element_type=jnp.float32
    )
    summed = lax.psum_scatter(
        jnp.concatenate([merge_heads(key_part), merge_heads(value_part)], axis=-1),
        "res",
        scatter_dimension=0,
        tiled=True,
    )
    key_value_grads = jnp.transpose(summed, (1, 0, 2))
    projected_gradient = jnp.concatenate(
        [merge_heads(grad_query_heads), key_value_grads, grad_gate_logit], axis=-1
    )
    projected_gradient = projected_gradient.astype(jnp.bfloat16).reshape(
        token_count, 4 * query_width
    )
    qkvg_local = jnp.dot(
        normalized_rows_backward.T, projected_gradient, preferred_element_type=jnp.float32
    )
    normalized_gradient = jnp.dot(
        projected_gradient, combined_weight.T, preferred_element_type=jnp.float32
    ).reshape(sequence_count, residue_count, alignment_width)
    alignment_gradient = layer_norm_backward(
        normalized_gradient, normalized_rows, broadcast_pair
    ).astype(jnp.bfloat16)
    pair_w_local = jnp.einsum(
        "ijc,hij->ch", pair_normed, logit_share, precision=lax.Precision.HIGHEST
    )
    grad_pair_normed = jnp.einsum(
        "hij,ch->ijc", logit_share, pair_weight, precision=lax.Precision.HIGHEST
    )
    pair_gradient = layer_norm_backward(grad_pair_normed, pair_normed, pair_spread).astype(
        jnp.bfloat16
    )
    combined_weight_gradient, output_weight_gradient, pair_weight_gradient = lax.psum(
        (qkvg_local, out_local, pair_w_local), ("seq", "res")
    )
    return (
        updated,
        alignment_gradient,
        pair_gradient,
        combined_weight_gradient,
        output_weight_gradient,
        pair_weight_gradient,
    )


VMEM_LIMIT = 20 * 1024 * 1024
ARGUMENT_VMEM_LIMIT = 56 * 1024 * 1024
LANES = 128
SLOTS = 4
NT = (((1,), (1,)), ((), ()))
TN = (((0,), (0,)), ((), ()))


def f32_dot(left, right, dims=None):
    if dims is None:
        return jnp.dot(left, right, preferred_element_type=jnp.float32)
    return lax.dot_general(left, right, dims, preferred_element_type=jnp.float32)


def two_terms(values):
    high = values.astype(jnp.bfloat16)
    return high, (values - high.astype(jnp.float32)).astype(jnp.bfloat16)


def slot_select(pieces):
    slot = lax.broadcasted_iota(jnp.int32, pieces[0].shape, 1) // (LANES // SLOTS)
    result = pieces[0]
    for k in range(1, SLOTS):
        result = jnp.where(slot == k, pieces[k], result)
    return result


def pack_heads(out_ref, row, tensor, residues):
    for core in range(2):
        for tile in range(tensor.shape[1] // LANES):
            rolled = []
            for s in range(SLOTS):
                start = (core * SLOTS + s) * residues
                piece = tensor[start : start + residues, tile * LANES : (tile + 1) * LANES]
                rolled.append(pltpu.roll(piece, s * LANES // SLOTS, 1) if s else piece)
            for j in range(SLOTS):
                block = slot_select([rolled[(k - j) % SLOTS] for k in range(SLOTS)])
                out_ref[(tile * SLOTS + j) * 2 + core, row : row + residues, :] = block.astype(
                    jnp.bfloat16
                )


def unpack_heads(in_ref, row, residues, tiles):
    rows = []
    for core in range(2):
        for s in range(SLOTS):
            pieces = []
            for tile in range(tiles):
                blocks = [
                    in_ref[
                        (tile * SLOTS + (k - s) % SLOTS) * 2 + core, row : row + residues, :
                    ].astype(jnp.float32)
                    for k in range(SLOTS)
                ]
                block = slot_select(blocks)
                pieces.append(pltpu.roll(block, LANES - s * LANES // SLOTS, 1) if s else block)
            rows.append(jnp.concatenate(pieces, axis=1))
    return jnp.concatenate(rows, axis=0)


def normalized(x_ref):
    width = x_ref.shape[-1]
    values = x_ref[...].reshape(-1, width).astype(jnp.float32)
    return layer_normalize(values)


def gate_of(logits):
    return 1.0 / (1.0 + jnp.exp(-logits))


def value_kernel(x_ref, grad_ref, wc_ref, wo_ref, out_ref):
    residues, width = x_ref.shape[1], x_ref.shape[2]
    normed = normalized(x_ref)[0].astype(jnp.bfloat16)
    values = f32_dot(normed, wc_ref[:, 2 * width : 3 * width])
    gate = gate_of(f32_dot(normed, wc_ref[:, 3 * width :]))
    grad_gated = f32_dot(grad_ref[...].reshape(-1, width), wo_ref[...], NT)
    pack_heads(out_ref, 0, values, residues)
    pack_heads(out_ref, residues, grad_gated * gate, residues)


def centred(weight):
    return weight - jnp.mean(weight, axis=1, keepdims=True)


def query_kernel(
    scale, arrive, x_ref, wc_ref, pair_ref, weight_ref, out_ref, bias_ref, mean_ref, spread_ref
):
    residues, width = x_ref.shape[1], x_ref.shape[2]
    heads = weight_ref.shape[0]
    normed = normalized(x_ref)[0].astype(jnp.bfloat16)
    pack_heads(out_ref, 0, f32_dot(normed, wc_ref[:, :width]) * scale, residues)
    pack_heads(out_ref, residues, f32_dot(normed, wc_ref[:, width : 2 * width]), residues)

    arrive()
    columns, channels = pair_ref.shape[1], pair_ref.shape[2]
    weight = centred(weight_ref[...])
    first = weight.astype(jnp.bfloat16)
    second, third = two_terms(weight - first.astype(jnp.float32))
    share = jnp.full((heads, channels), 1.0 / channels, jnp.bfloat16)
    left = jnp.concatenate([first, second, third, share], axis=0)
    average = jnp.full((channels, channels), 1.0 / channels, jnp.bfloat16)
    step_rows = 64

    def rows(step, carry):
        start = pl.multiple_of(step * step_rows, step_rows)
        entries = pair_ref[pl.ds(start, step_rows)].reshape(step_rows * columns, channels)
        center = entries.astype(jnp.float32) - f32_dot(entries, average)
        high, low = two_terms(center * center)
        variance = f32_dot(share, high, NT) + f32_dot(share, low, NT)
        spread = lax.rsqrt(variance + eps_norm)
        raw = f32_dot(left, entries, NT)
        bias = spread * (raw[:heads] + raw[heads : 2 * heads] + raw[2 * heads : 3 * heads])
        for k in range(step_rows):
            lanes = slice(k * columns, (k + 1) * columns)
            bias_ref[:, start + k, :] = bias[:, lanes]
            mean_ref[pl.ds(start + k, 1), :] = raw[3 * heads : 3 * heads + 1, lanes]
            spread_ref[pl.ds(start + k, 1), :] = spread[:1, lanes]
        return carry

    lax.fori_loop(0, pair_ref.shape[0] // step_rows, rows, 0)
    half = residues // 2
    for h in range(heads):
        for core in range(2):
            high, low = two_terms(bias_ref[h, core * half : (core + 1) * half, :])
            out_ref[h * 2 + core, 2 * residues : 2 * residues + half, :] = high
            out_ref[h * 2 + core, 2 * residues + half : 3 * residues, :] = low


def lanes_of(blocks_ref, row, residues):
    count = blocks_ref.shape[0] // 2
    planes = [
        blocks_ref[p * count : (p + 1) * count, row : row + residues, :].reshape(-1, LANES)
        for p in range(2)
    ]
    return jnp.concatenate(planes, axis=1)


def score_kernel(
    residues, left_row, right_row, with_bias, place_ref, own_ref, other_ref, mine_ref, sent_ref
):
    core, half = place_ref[0], place_ref[1]
    count = own_ref.shape[0] // 2
    part = residues // 2
    right = jnp.concatenate(
        [lanes_of(own_ref, right_row, residues), lanes_of(other_ref, right_row, residues)], axis=1
    )
    for which, ref in ((half, mine_ref), (1 - half, sent_ref)):
        left = []
        for k in range(count // 2):
            block = which * (count // 2) + k
            rows = pl.ds(pl.multiple_of(left_row + core * part, part), part)
            left.append(
                jnp.concatenate(
                    [
                        r[p * count + block, rows, :]
                        for r in (own_ref, other_ref)
                        for p in range(2)
                    ],
                    axis=1,
                )
            )
        ref[...] = f32_dot(jnp.concatenate(left, axis=0), right, NT).astype(ref.dtype)
        if with_bias:
            for p in range(2):
                columns = pl.ds(pl.multiple_of((half * 2 + p) * LANES, LANES), LANES)
                for k in range(count // 2):
                    block = p * count + which * (count // 2) + k
                    high = own_ref[block, 2 * residues : 2 * residues + part, :]
                    low = own_ref[block, 2 * residues + part : 3 * residues, :]
                    bias = high.astype(jnp.float32) + low.astype(jnp.float32)
                    ref[k * part : (k + 1) * part, columns] += bias


def softmax_kernel(logit_ref, other_ref, out_ref, low_ref):
    logits = logit_ref[...] + other_ref[...]
    lifted = jnp.exp(logits - jnp.max(logits, axis=-1, keepdims=True))
    softmax_out = lifted / jnp.sum(lifted, axis=-1, keepdims=True)
    out_ref[...] = softmax_out
    low_ref[...] = softmax_out.astype(jnp.bfloat16)


def softmax_gradient_kernel(softmax_ref, grad_ref, other_ref, out_ref):
    softmax_out = softmax_ref[...]
    grad_probs = grad_ref[...] + other_ref[...].astype(jnp.float32)
    row_dot = jnp.sum(softmax_out * grad_probs, axis=-1, keepdims=True)
    out_ref[...] = (softmax_out * (grad_probs - row_dot)).astype(jnp.bfloat16)


def product_kernel(
    residues, scale, first_row, second_row, with_share,
    place_ref, own_ref, far_ref, near_ref, corner_ref, blocks_ref, out_ref, whole_ref,
):
    core, half = place_ref[0], place_ref[1]
    count = blocks_ref.shape[0] // 2
    part = residues // 2
    quarters = (
        (own_ref, core, half), (far_ref, core, 1 - half),
        (near_ref, 1 - core, half), (corner_ref, 1 - core, 1 - half),
    )
    for ref, c, z in quarters:
        for k in range(count // 2):
            start = (z * (count // 2) + k) * residues + c * part
            whole_ref[pl.ds(pl.multiple_of(start, part), part), :] = ref[k * part : (k + 1) * part, :]
    whole = whole_ref[...]
    if with_share:
        for p in range(2):
            columns = pl.ds(pl.multiple_of((half * 2 + p) * LANES, LANES), LANES)
            for q in range(count):
                rows = pl.ds(pl.multiple_of(q * residues + core * part, part), part)
                out_ref[p * count + q, 2 * residues : 2 * residues + part, :] = whole_ref[rows, columns]
    first = f32_dot(whole, lanes_of(blocks_ref, first_row, residues)) * scale
    second = f32_dot(whole, lanes_of(blocks_ref, second_row, residues), TN)
    for row, product in ((0, first), (residues, second)):
        for p in range(2):
            out_ref[p * count : (p + 1) * count, row : row + residues, :] = (
                product[:, p * LANES : (p + 1) * LANES]
                .astype(jnp.bfloat16)
                .reshape(count, residues, LANES)
            )


def share_of(blocks_ref, row, part, heads):
    return jnp.concatenate(
        [
            blocks_ref[:, row : row + part, :]
            .astype(jnp.float32)
            .reshape(heads, 2 * part, LANES)
        ],
        axis=0,
    )


def attended_weight_kernel(
    x_ref, grad_ref, wc_ref, wo_ref, blocks_ref, updated_ref, projected_ref, normed_ref, sums_ref
):
    residues, width = x_ref.shape[1], x_ref.shape[2]
    tiles = width // LANES
    normed = normalized(x_ref)[0].astype(jnp.bfloat16)
    normed_ref[...] = normed
    gate = gate_of(f32_dot(normed, wc_ref[:, 3 * width :]))
    grad = grad_ref[...].reshape(-1, width)
    grad_gated = f32_dot(grad, wo_ref[...], NT)
    attended = unpack_heads(blocks_ref, 0, residues, tiles)
    gated = (gate * attended).astype(jnp.bfloat16)
    updated_ref[...] = f32_dot(gated, wo_ref[...]).astype(jnp.bfloat16).reshape(updated_ref.shape)
    projected_ref[:, :width] = unpack_heads(blocks_ref, residues, residues, tiles).astype(
        jnp.bfloat16
    )
    projected_ref[:, width:] = (grad_gated * attended * gate * (1.0 - gate)).astype(jnp.bfloat16)
    sums_ref[:, : 2 * width] = f32_dot(normed, projected_ref[...], TN).astype(jnp.bfloat16)
    sums_ref[:, 2 * width :] = f32_dot(gated, grad, TN).astype(jnp.bfloat16)


def query_weight_kernel(
    arrive, place_ref, normed_ref, attended_sums_ref, blocks_ref,
    projected_ref, keep_ref, send_ref, sums_ref,
):
    width = normed_ref.shape[1]
    tiles, residues = width // LANES, (blocks_ref.shape[1] * 2) // 5
    core = place_ref[0]
    for t in range(2):
        projected_ref[:, t * width : (t + 1) * width] = unpack_heads(
            blocks_ref, t * residues, residues, tiles
        ).astype(jnp.bfloat16)
    arrive()
    sums_ref[:, : 2 * width] = f32_dot(normed_ref[...], projected_ref[...], TN).astype(
        jnp.bfloat16
    )
    sums_ref[:, 2 * width :] = attended_sums_ref[...]
    rows = keep_ref.shape[1]
    for which, ref in ((core, keep_ref), (1 - core, send_ref)):
        for block in range(keep_ref.shape[0]):
            start = pl.multiple_of((2 * block + which) * rows, rows)
            ref[block] = sums_ref[pl.ds(start, rows), :]


def core_sum_kernel(place_ref, keep_ref, other_ref, own_ref, *send_refs):
    chip = place_ref[2]
    for flip, ref in enumerate((own_ref, *send_refs)):
        block = jnp.bitwise_xor(chip, flip)
        total = keep_ref[block].astype(jnp.float32) + other_ref[block].astype(jnp.float32)
        ref[...] = total.astype(ref.dtype)


def plane_sum_kernel(own_ref, pair_weight_ref, *refs):
    *received, out_ref = refs
    total = own_ref[...]
    for ref in received:
        total += ref[...].astype(jnp.float32)
    count = own_ref.shape[1]
    heads = pair_weight_ref.shape[0]
    out_ref[:, :count] = total.astype(out_ref.dtype)
    rest = jnp.zeros((out_ref.shape[0] - heads, out_ref.shape[1] - count), jnp.float32)
    out_ref[:, count:] = jnp.concatenate([pair_weight_ref[...], rest], axis=0).astype(
        out_ref.dtype
    )


def pair_weight_kernel(blocks_ref, pair_ref, mean_ref, spread_ref, out_ref, share_ref):
    heads, part = share_ref.shape[0], pair_ref.shape[0] // 2
    share_ref[...] = share_of(blocks_ref, blocks_ref.shape[1] - part, part, heads)

    def rows(step, carry):
        total, shift = carry
        for k in range(8):
            i = step * 8 + k
            scaled = share_ref[:, i, :] * spread_ref[pl.ds(i, 1), :]
            high, low = two_terms(scaled)
            total += f32_dot(jnp.concatenate([high, low], axis=0), pair_ref[i])
            shift += (high.astype(jnp.float32) + low.astype(jnp.float32)) * mean_ref[pl.ds(i, 1), :]
        return total, shift

    channels = pair_ref.shape[2]
    total, shift = lax.fori_loop(
        0,
        pair_ref.shape[0] // 8,
        rows,
        (jnp.zeros((2 * heads, channels), jnp.float32), jnp.zeros((heads, LANES), jnp.float32)),
    )
    out_ref[...] = total[:heads] + total[heads:] - jnp.sum(shift, axis=1, keepdims=True)


def alignment_kernel(x_ref, wc_ref, query_key_ref, value_gate_ref, out_ref):
    normed, spread = normalized(x_ref)
    width = x_ref.shape[2]
    gradient = f32_dot(query_key_ref[...], wc_ref[:, : 2 * width], NT) + f32_dot(
        value_gate_ref[...], wc_ref[:, 2 * width :], NT
    )
    out_ref[...] = (
        layer_norm_backward(gradient, normed, spread).astype(jnp.bfloat16).reshape(out_ref.shape)
    )


def pair_kernel(blocks_row, blocks_ref, pair_ref, weight_ref, bias_ref, mean_ref, spread_ref, out_ref, share_ref):
    heads, channels = weight_ref.shape
    part = pair_ref.shape[0] // 2
    share_ref[...] = share_of(blocks_ref, blocks_row, part, heads)
    first, second = two_terms(centred(weight_ref[...]))
    zero = jnp.zeros((heads, channels), jnp.bfloat16)
    top = lax.broadcasted_iota(jnp.int32, (heads, channels), 0) < 2
    ones = jnp.where(top, 1.0, 0.0).astype(jnp.bfloat16)
    right = jnp.concatenate(
        [
            jnp.concatenate([first, first, second, ones, zero], axis=0),
            jnp.concatenate([zero, zero, zero, zero, ones], axis=0),
        ],
        axis=1,
    )
    row = lax.broadcasted_iota(jnp.int32, (heads, LANES), 0)

    def rows_of_two(value):
        high, low = two_terms(value)
        high, low = high.astype(jnp.float32), low.astype(jnp.float32)
        return jnp.where(row == 0, high, jnp.where(row == 1, low, 0.0)).astype(jnp.bfloat16)

    def rows(step, carry):
        for k in range(8):
            i = step * 8 + k
            gradient = share_ref[:, i, :]
            spread = spread_ref[pl.ds(i, 1), :]
            cross = jnp.sum(gradient * bias_ref[:, i, :], axis=0, keepdims=True) / channels
            slope = spread * spread * cross
            high, low = two_terms(gradient * spread)
            left = jnp.concatenate(
                [
                    high, low, high,
                    rows_of_two(jnp.broadcast_to(slope * mean_ref[pl.ds(i, 1), :], row.shape)),
                    rows_of_two(jnp.broadcast_to(slope, row.shape)),
                ],
                axis=0,
            )
            terms = f32_dot(left, right, TN)
            entries = pair_ref[i].astype(jnp.float32)
            out_ref[i] = (terms[:, :channels] - terms[:, channels:] * entries).astype(jnp.bfloat16)
        return carry

    lax.fori_loop(0, pair_ref.shape[0] // 8, rows, 0)


def output_kernel(parts_ref, combined_ref, out_weight_ref, pair_weight_ref):
    width = combined_ref.shape[0]
    rows = parts_ref.shape[1]
    for h in range(parts_ref.shape[0]):
        block = slice(h * rows, (h + 1) * rows)
        part = parts_ref[h].astype(jnp.float32)
        combined_ref[block, :] = part[:, : 4 * width]
        out_weight_ref[block, :] = part[:, 4 * width : 5 * width]
        share = part[: pair_weight_ref.shape[0], 5 * width :]
        pair_weight_ref[...] = share if h == 0 else pair_weight_ref[...] + share


def call(kernel, outs, *args, scratch=(), place=None, flops=0, after=(), outside=0, late=0, limit=None):
    whole, anywhere = pl.BlockSpec(memory_space=pltpu.VMEM), pl.BlockSpec(memory_space=pl.ANY)
    specs = [anywhere] * outside + [whole] * (len(args) - outside)
    ahead = () if place is None else (place,)
    shapes = [jax.ShapeDtypeStruct(*o) for o in outs]
    moved = sum(math.prod(a.shape) * a.dtype.itemsize for a in list(args) + shapes)
    first = len(ahead) + len(args)
    last = first + len(after)

    def wrapped(*refs):
        given, rest = list(refs[:first]), refs[last:]
        if outside:
            *rest, arrived = rest
            held = rest[len(rest) - outside :]
            rest = rest[: len(rest) - outside]
            copies = []
            for k in range(outside):
                copies.append(
                    pltpu.make_async_copy(given[len(ahead) + k], held[k], arrived.at[k])
                )
                given[len(ahead) + k] = held[k]
            for copy in copies:
                copy.start()
            for copy in copies[: outside - late]:
                copy.wait()
            if late:
                given.insert(0, lambda: [copy.wait() for copy in copies[outside - late :]])
        kernel(*given, *rest)

    held = [pltpu.VMEM(a.shape, a.dtype) for a in args[:outside]]
    if outside:
        held.append(pltpu.SemaphoreType.DMA((outside,)))
    return pl.pallas_call(
        wrapped,
        out_shape=shapes,
        in_specs=[pl.BlockSpec(memory_space=pltpu.SMEM)] * len(ahead)
        + specs
        + [anywhere] * len(after),
        out_specs=[whole] * len(shapes),
        scratch_shapes=[*scratch, *held],
        compiler_params=pltpu.CompilerParams(
            vmem_limit_bytes=limit or (ARGUMENT_VMEM_LIMIT if outside else VMEM_LIMIT)
        ),
        cost_estimate=pl.CostEstimate(flops=flops, bytes_accessed=moved, transcendentals=0),
    )(*ahead, *args, *after)


def swapped(mine, axis_name, distance):
    size = lax.axis_size(axis_name)
    return lax.ppermute(mine, axis_name, [(a, a ^ distance) for a in range(size)])


def fits_heads(alignment_rows, pair_entries, pair_weight):
    channels, heads = pair_weight.shape
    return (
        lax.axis_size("seq") == 4
        and lax.axis_size("res") == heads == 8
        and alignment_rows.shape[0] == 2 * SLOTS
        and alignment_rows.shape[1] == pair_entries.shape[0] == 64
        and alignment_rows.shape[2] == 2 * LANES
        and pair_entries.shape[1] == channels == LANES
    )


def head_body(
    alignment_rows, pair_entries, combined_weight, output_weight, pair_weight, updated_gradient
):
    sequences, residues, width = alignment_rows.shape
    channels, heads = pair_weight.shape
    tokens = sequences * residues
    seq_size, res_size = lax.axis_size("seq"), lax.axis_size("res")
    seq_half = seq_size // 2
    total = residues * res_size
    group = 2 * res_size
    groups = [[g * group + k for k in range(group)] for g in range(seq_half)]
    scale = 1.0 / math.sqrt(width // heads * sequences * seq_size)
    res_index, seq_index = lax.axis_index("res"), lax.axis_index("seq")
    place = jnp.stack([res_index % 2, seq_index // 2, res_index // 2]).astype(jnp.int32)
    bf16, f32 = jnp.bfloat16, jnp.float32

    def across(blocks):
        return lax.all_to_all(blocks, ("seq", "res"), 0, 0, axis_index_groups=groups, tiled=True)

    x, grad, wc, wo = alignment_rows, updated_gradient, combined_weight, output_weight
    query_blocks, bias, mean, spread = call(
        functools.partial(query_kernel, scale),
        [
            ((group, 3 * residues, LANES), bf16),
            ((heads, residues, LANES), f32),
            ((residues, LANES), f32),
            ((residues, LANES), f32),
        ],
        x, wc, pair_entries, pair_weight.T,
        flops=8 * tokens * width * width, outside=3, late=1,
    )
    query_blocks = across(query_blocks)
    (value_blocks,) = call(
        value_kernel, [((group, 2 * residues, LANES), bf16)], x, grad, wc, wo,
        flops=8 * tokens * width * width, outside=4,
    )
    query_blocks, value_blocks = lax.optimization_barrier((query_blocks, value_blocks))
    value_blocks = across(value_blocks)

    def scores(blocks, left_row, right_row, with_bias, kind):
        return call(
            functools.partial(score_kernel, residues, left_row, right_row, with_bias),
            [((total // 4, total), f32), ((total // 4, total), kind)],
            blocks, swapped(blocks, "res", 1),
            place=place, flops=2 * total * total * width,
        )

    logit_mine, logit_sent = scores(query_blocks, 0, residues, True, f32)
    logit_other = swapped(logit_sent, "seq", seq_half)
    quarter = (total // 4, total)
    softmax_out, probs = call(
        softmax_kernel, [(quarter, f32), (quarter, bf16)], logit_mine, logit_other,
        flops=total * total,
    )
    probs_far = swapped(probs, "seq", seq_half)
    value_blocks, probs_far = lax.optimization_barrier((value_blocks, probs_far))
    grad_mine, grad_sent = scores(value_blocks, residues, 0, False, bf16)
    grad_other = swapped(grad_sent, "seq", seq_half)

    def products(quarters, blocks, first_row, second_row, with_share, factor):
        rows = 2 * residues + (residues // 2 if with_share else 0)
        (out,) = call(
            functools.partial(
                product_kernel, residues, factor, first_row, second_row, with_share
            ),
            [((group, rows, LANES), bf16)],
            *quarters, blocks,
            scratch=[pltpu.VMEM((total, total), bf16)],
            place=place, flops=4 * total * total * width,
        )
        return out

    def with_near(mine, far):
        return mine, far, swapped(mine, "res", 1), swapped(far, "res", 1)

    attended = products(with_near(probs, probs_far), value_blocks, 0, residues, False, 1.0)
    attended, grad_other = lax.optimization_barrier((attended, grad_other))
    attended_blocks = across(attended)
    (grad_logits,) = call(
        softmax_gradient_kernel, [(quarter, bf16)], softmax_out, grad_mine, grad_other,
        flops=total * total,
    )
    grad_quarters = with_near(grad_logits, swapped(grad_logits, "seq", seq_half))
    grad_sums = products(grad_quarters, query_blocks, residues, 0, True, scale)
    grad_sums, attended_blocks = lax.optimization_barrier((grad_sums, attended_blocks))
    grad_blocks = across(grad_sums)

    updated, value_gate, normed, attended_sums = call(
        attended_weight_kernel,
        [
            (x.shape, bf16),
            ((tokens, 2 * width), bf16),
            ((tokens, width), bf16),
            ((width, 3 * width), bf16),
        ],
        x, grad, wc, wo, attended_blocks,
        flops=14 * tokens * width * width, outside=4,
    )
    share = pltpu.VMEM((heads, residues, LANES), f32)
    columns = 5 * width
    rows = width // res_size
    part_rows = ((res_size // 2, rows, columns), bf16)
    query_key, keep, send = call(
        query_weight_kernel,
        [((tokens, 2 * width), bf16), part_rows, part_rows],
        normed, attended_sums, grad_blocks,
        scratch=[pltpu.VMEM((width, columns), bf16)],
        place=place, flops=4 * tokens * width * width, outside=2, late=2, limit=VMEM_LIMIT,
    )
    own, *sent = call(
        core_sum_kernel,
        [((rows, columns), f32)] + [((rows, columns), bf16)] * 3,
        keep, swapped(send, "res", 1), place=place,
    )
    received = [swapped(t, "res", 2 * flip) for flip, t in enumerate(sent, 1)]
    (pair_weight_part,) = call(
        pair_weight_kernel, [((heads, channels), f32)],
        grad_blocks, pair_entries, mean, spread,
        scratch=[share], flops=4 * tokens * width * width, after=(sent[0],),
    )
    (pair_gradient,) = call(
        functools.partial(pair_kernel, 2 * residues),
        [(pair_entries.shape, bf16)],
        grad_blocks, pair_entries, pair_weight.T, bias, mean, spread,
        scratch=[share], flops=8 * tokens * width * width,
    )
    received, pair_weight_part = lax.optimization_barrier((received, pair_weight_part))
    (part,) = call(
        plane_sum_kernel, [((rows, columns + channels), bf16)], own, pair_weight_part, *received
    )
    (alignment_gradient,) = call(
        alignment_kernel, [(x.shape, bf16)], x, wc, query_key, value_gate,
        flops=8 * tokens * width * width,
    )

    def added(mine, other):
        return (mine.astype(f32) + other.astype(f32)).astype(bf16)

    other_plane = swapped(part, "seq", 1)
    other_plane, alignment_gradient = lax.optimization_barrier((other_plane, alignment_gradient))
    part = added(part, other_plane)
    other_half = swapped(part, "seq", seq_half)
    other_half, pair_gradient = lax.optimization_barrier((other_half, pair_gradient))
    part = added(part, other_half)
    combined_gradient, output_gradient, pair_weight_gradient = call(
        output_kernel,
        [(wc.shape, f32), (wo.shape, f32), ((heads, channels), f32)],
        lax.all_gather(part, "res", axis=0),
    )
    return (
        updated,
        alignment_gradient,
        pair_gradient,
        combined_gradient,
        output_gradient,
        pair_weight_gradient.T,
    )


def body(alignment_rows, pair_entries, combined_weight, output_weight, pair_weight, updated_gradient):
    chosen = head_body if fits_heads(alignment_rows, pair_entries, pair_weight) else gathered_body
    return chosen(
        alignment_rows, pair_entries, combined_weight, output_weight, pair_weight, updated_gradient
    )


def solution(mesh):
    return jax.shard_map(
        body,
        mesh=mesh,
        in_specs=(
            P("seq", "res", None),
            P("res", "seq", None),
            P(),
            P(),
            P(),
            P("seq", "res", None),
        ),
        out_specs=(
            P("seq", "res", None),
            P("seq", "res", None),
            P("res", "seq", None),
            P(),
            P(),
            P(),
        ),
        check_vma=False,
    )
```

```python
import functools
import math

import jax
import jax.numpy as jnp
from jax import lax
from jax.experimental import pallas as pl
from jax.experimental.pallas import tpu as pltpu
from jax.sharding import PartitionSpec as P

eps_norm = 1e-05


def layer_normalize(values):
    values = values.astype(jnp.float32)
    center = values - jnp.mean(values, axis=-1, keepdims=True)
    broadcast_pair = lax.rsqrt(jnp.mean(center * center, axis=-1, keepdims=True) + eps_norm)
    return (center * broadcast_pair, broadcast_pair)


def layer_norm_backward(normalized_gradient, normalized_rows, broadcast_pair):
    mean_grad = jnp.mean(normalized_gradient, axis=-1, keepdims=True)
    mean_cross = jnp.mean(normalized_gradient * normalized_rows, axis=-1, keepdims=True)
    return broadcast_pair * (normalized_gradient - mean_grad - normalized_rows * mean_cross)


def split_heads(tensor, head_count):
    return tensor.reshape(
        tensor.shape[0], tensor.shape[1], head_count, tensor.shape[2] // head_count
    )


def merge_heads(tensor):
    return tensor.reshape(tensor.shape[0], tensor.shape[1], tensor.shape[2] * tensor.shape[3])


def gathered_body(
    alignment_rows, pair_entries, combined_weight, output_weight, pair_weight, updated_gradient
):
    sequence_count, residue_count, alignment_width = alignment_rows.shape
    head_count = pair_weight.shape[1]
    query_width = output_weight.shape[0]
    head_dim = query_width // head_count
    column_count = pair_entries.shape[1]
    token_count = sequence_count * residue_count
    score_scale = 1.0 / math.sqrt(head_dim * sequence_count * lax.axis_size("seq"))
    normalized_rows, broadcast_pair = layer_normalize(alignment_rows)
    normalized_rows_backward = normalized_rows.astype(jnp.bfloat16).reshape(
        token_count, alignment_width
    )
    projected = jnp.dot(
        normalized_rows_backward, combined_weight, preferred_element_type=jnp.float32
    ).reshape(sequence_count, residue_count, 4 * query_width)
    queries = (projected[..., :query_width] * score_scale).astype(jnp.bfloat16)
    key_rows = projected[..., query_width : 2 * query_width].astype(jnp.bfloat16)
    value_rows = projected[..., 2 * query_width : 3 * query_width].astype(jnp.bfloat16)
    gate_open = jax.nn.sigmoid(projected[..., 3 * query_width :])
    all_keys, all_values = (
        lax.all_gather(key_rows, "res", axis=1, tiled=True),
        lax.all_gather(value_rows, "res", axis=1, tiled=True),
    )
    query_heads = split_heads(queries, head_count)
    key_heads = split_heads(all_keys, head_count)
    value_heads = split_heads(all_values, head_count)
    score_terms = jnp.einsum(
        "sihd,sjhd->hij", query_heads, key_heads, preferred_element_type=jnp.float32
    )
    pair_normed, pair_spread = layer_normalize(pair_entries)
    pair_bias = jnp.einsum("ijc,ch->hij", pair_normed, pair_weight, precision=lax.Precision.HIGHEST)
    col_start = lax.axis_index("seq") * column_count
    own_block = lax.dynamic_slice_in_dim(score_terms, col_start, column_count, 2) + pair_bias
    logits = lax.psum(lax.dynamic_update_slice_in_dim(score_terms, own_block, col_start, 2), "seq")
    row_top = jnp.max(logits, axis=-1, keepdims=True)
    lifted = jnp.exp(logits - row_top)
    softmax_out = lifted / jnp.sum(lifted, axis=-1, keepdims=True)
    softmax_low = softmax_out.astype(jnp.bfloat16)
    attended = merge_heads(
        jnp.einsum("hij,sjhd->sihd", softmax_low, value_heads, preferred_element_type=jnp.float32)
    )
    gated_out = (gate_open * attended).astype(jnp.bfloat16)
    flattened_gated = gated_out.reshape(token_count, query_width)
    updated = (
        jnp.dot(flattened_gated, output_weight, preferred_element_type=jnp.float32)
        .astype(jnp.bfloat16)
        .reshape(sequence_count, residue_count, alignment_width)
    )
    flattened_gradient = updated_gradient.reshape(token_count, alignment_width)
    grad_gated = jnp.dot(
        flattened_gradient, output_weight.T, preferred_element_type=jnp.float32
    ).reshape(sequence_count, residue_count, query_width)
    out_local = jnp.dot(flattened_gated.T, flattened_gradient, preferred_element_type=jnp.float32)
    grad_attended = (grad_gated * gate_open).astype(jnp.bfloat16)
    grad_gate_logit = grad_gated * attended * gate_open * (1.0 - gate_open)
    attended_grad_heads = split_heads(grad_attended, head_count)
    grad_terms = jnp.einsum(
        "sihd,sjhd->hij", attended_grad_heads, value_heads, preferred_element_type=jnp.float32
    )
    grad_probs = lax.psum(grad_terms, "seq")
    row_dot = jnp.sum(softmax_out * grad_probs, axis=-1, keepdims=True)
    grad_logits = softmax_out * (grad_probs - row_dot)
    grad_logits_b = grad_logits.astype(jnp.bfloat16)
    logit_share = lax.dynamic_slice_in_dim(grad_logits, col_start, column_count, 2)
    grad_query_heads = (
        jnp.einsum("hij,sjhd->sihd", grad_logits_b, key_heads, preferred_element_type=jnp.float32)
        * score_scale
    )
    key_part = jnp.einsum(
        "hij,sihd->jshd", grad_logits_b, query_heads, preferred_element_type=jnp.float32
    )
    value_part = jnp.einsum(
        "hij,sihd->jshd", softmax_low, attended_grad_heads, preferred_element_type=jnp.float32
    )
    summed = lax.psum_scatter(
        jnp.concatenate([merge_heads(key_part), merge_heads(value_part)], axis=-1),
        "res",
        scatter_dimension=0,
        tiled=True,
    )
    key_value_grads = jnp.transpose(summed, (1, 0, 2))
    projected_gradient = jnp.concatenate(
        [merge_heads(grad_query_heads), key_value_grads, grad_gate_logit], axis=-1
    )
    projected_gradient = projected_gradient.astype(jnp.bfloat16).reshape(
        token_count, 4 * query_width
    )
    qkvg_local = jnp.dot(
        normalized_rows_backward.T, projected_gradient, preferred_element_type=jnp.float32
    )
    normalized_gradient = jnp.dot(
        projected_gradient, combined_weight.T, preferred_element_type=jnp.float32
    ).reshape(sequence_count, residue_count, alignment_width)
    alignment_gradient = layer_norm_backward(
        normalized_gradient, normalized_rows, broadcast_pair
    ).astype(jnp.bfloat16)
    pair_w_local = jnp.einsum(
        "ijc,hij->ch", pair_normed, logit_share, precision=lax.Precision.HIGHEST
    )
    grad_pair_normed = jnp.einsum(
        "hij,ch->ijc", logit_share, pair_weight, precision=lax.Precision.HIGHEST
    )
    pair_gradient = layer_norm_backward(grad_pair_normed, pair_normed, pair_spread).astype(
        jnp.bfloat16
    )
    combined_weight_gradient, output_weight_gradient, pair_weight_gradient = lax.psum(
        (qkvg_local, out_local, pair_w_local), ("seq", "res")
    )
    return (
        updated,
        alignment_gradient,
        pair_gradient,
        combined_weight_gradient,
        output_weight_gradient,
        pair_weight_gradient,
    )


VMEM_LIMIT = 20 * 1024 * 1024
ARGUMENT_VMEM_LIMIT = 56 * 1024 * 1024
LANES = 128
SLOTS = 4
NT = (((1,), (1,)), ((), ()))
TN = (((0,), (0,)), ((), ()))


def f32_dot(left, right, dims=None):
    if dims is None:
        return jnp.dot(left, right, preferred_element_type=jnp.float32)
    return lax.dot_general(left, right, dims, preferred_element_type=jnp.float32)


def two_terms(values):
    high = values.astype(jnp.bfloat16)
    return high, (values - high.astype(jnp.float32)).astype(jnp.bfloat16)


def slot_select(pieces):
    slot = lax.broadcasted_iota(jnp.int32, pieces[0].shape, 1) // (LANES // SLOTS)
    result = pieces[0]
    for k in range(1, SLOTS):
        result = jnp.where(slot == k, pieces[k], result)
    return result


def pack_heads(out_ref, row, tensor, residues):
    for core in range(2):
        for tile in range(tensor.shape[1] // LANES):
            rolled = []
            for s in range(SLOTS):
                start = (core * SLOTS + s) * residues
                piece = tensor[start : start + residues, tile * LANES : (tile + 1) * LANES]
                rolled.append(pltpu.roll(piece, s * LANES // SLOTS, 1) if s else piece)
            for j in range(SLOTS):
                block = slot_select([rolled[(k - j) % SLOTS] for k in range(SLOTS)])
                out_ref[(tile * SLOTS + j) * 2 + core, row : row + residues, :] = block.astype(
                    jnp.bfloat16
                )


def unpack_heads(in_ref, row, residues, tiles):
    rows = []
    for core in range(2):
        for s in range(SLOTS):
            pieces = []
            for tile in range(tiles):
                blocks = [
                    in_ref[
                        (tile * SLOTS + (k - s) % SLOTS) * 2 + core, row : row + residues, :
                    ].astype(jnp.float32)
                    for k in range(SLOTS)
                ]
                block = slot_select(blocks)
                pieces.append(pltpu.roll(block, LANES - s * LANES // SLOTS, 1) if s else block)
            rows.append(jnp.concatenate(pieces, axis=1))
    return jnp.concatenate(rows, axis=0)


def normalized(x_ref):
    width = x_ref.shape[-1]
    values = x_ref[...].reshape(-1, width).astype(jnp.float32)
    return layer_normalize(values)


def gate_of(logits):
    return 1.0 / (1.0 + jnp.exp(-logits))


def value_kernel(x_ref, grad_ref, wc_ref, wo_ref, out_ref):
    residues, width = x_ref.shape[1], x_ref.shape[2]
    normed = normalized(x_ref)[0].astype(jnp.bfloat16)
    values = f32_dot(normed, wc_ref[:, 2 * width : 3 * width])
    gate = gate_of(f32_dot(normed, wc_ref[:, 3 * width :]))
    grad_gated = f32_dot(grad_ref[...].reshape(-1, width), wo_ref[...], NT)
    pack_heads(out_ref, 0, values, residues)
    pack_heads(out_ref, residues, grad_gated * gate, residues)


def centred(weight):
    return weight - jnp.mean(weight, axis=1, keepdims=True)


def query_kernel(
    scale, arrive, x_ref, wc_ref, pair_ref, weight_ref, out_ref, bias_ref, mean_ref, spread_ref
):
    residues, width = x_ref.shape[1], x_ref.shape[2]
    heads = weight_ref.shape[0]
    normed = normalized(x_ref)[0].astype(jnp.bfloat16)
    pack_heads(out_ref, 0, f32_dot(normed, wc_ref[:, :width]) * scale, residues)
    pack_heads(out_ref, residues, f32_dot(normed, wc_ref[:, width : 2 * width]), residues)

    arrive()
    columns, channels = pair_ref.shape[1], pair_ref.shape[2]
    weight = centred(weight_ref[...])
    first = weight.astype(jnp.bfloat16)
    second, third = two_terms(weight - first.astype(jnp.float32))
    share = jnp.full((heads, channels), 1.0 / channels, jnp.bfloat16)
    left = jnp.concatenate([first, second, third, share], axis=0)
    average = jnp.full((channels, channels), 1.0 / channels, jnp.bfloat16)
    step_rows = 64

    def rows(step, carry):
        start = pl.multiple_of(step * step_rows, step_rows)
        entries = pair_ref[pl.ds(start, step_rows)].reshape(step_rows * columns, channels)
        center = entries.astype(jnp.float32) - f32_dot(entries, average)
        high, low = two_terms(center * center)
        variance = f32_dot(share, high, NT) + f32_dot(share, low, NT)
        spread = lax.rsqrt(variance + eps_norm)
        raw = f32_dot(left, entries, NT)
        bias = spread * (raw[:heads] + raw[heads : 2 * heads] + raw[2 * heads : 3 * heads])
        for k in range(step_rows):
            lanes = slice(k * columns, (k + 1) * columns)
            bias_ref[:, start + k, :] = bias[:, lanes]
            mean_ref[pl.ds(start + k, 1), :] = raw[3 * heads : 3 * heads + 1, lanes]
            spread_ref[pl.ds(start + k, 1), :] = spread[:1, lanes]
        return carry

    lax.fori_loop(0, pair_ref.shape[0] // step_rows, rows, 0)
    half = residues // 2
    for h in range(heads):
        for core in range(2):
            high, low = two_terms(bias_ref[h, core * half : (core + 1) * half, :])
            out_ref[h * 2 + core, 2 * residues : 2 * residues + half, :] = high
            out_ref[h * 2 + core, 2 * residues + half : 3 * residues, :] = low


def lanes_of(blocks_ref, row, residues):
    count = blocks_ref.shape[0] // 2
    planes = [
        blocks_ref[p * count : (p + 1) * count, row : row + residues, :].reshape(-1, LANES)
        for p in range(2)
    ]
    return jnp.concatenate(planes, axis=1)


def score_kernel(
    residues, left_row, right_row, with_bias, place_ref, own_ref, other_ref, mine_ref, sent_ref
):
    core, half = place_ref[0], place_ref[1]
    count = own_ref.shape[0] // 2
    part = residues // 2
    right = jnp.concatenate(
        [lanes_of(own_ref, right_row, residues), lanes_of(other_ref, right_row, residues)], axis=1
    )
    for which, ref in ((half, mine_ref), (1 - half, sent_ref)):
        left = []
        for k in range(count // 2):
            block = which * (count // 2) + k
            rows = pl.ds(pl.multiple_of(left_row + core * part, part), part)
            left.append(
                jnp.concatenate(
                    [
                        r[p * count + block, rows, :]
                        for r in (own_ref, other_ref)
                        for p in range(2)
                    ],
                    axis=1,
                )
            )
        ref[...] = f32_dot(jnp.concatenate(left, axis=0), right, NT).astype(ref.dtype)
        if with_bias:
            for p in range(2):
                columns = pl.ds(pl.multiple_of((half * 2 + p) * LANES, LANES), LANES)
                for k in range(count // 2):
                    block = p * count + which * (count // 2) + k
                    high = own_ref[block, 2 * residues : 2 * residues + part, :]
                    low = own_ref[block, 2 * residues + part : 3 * residues, :]
                    bias = high.astype(jnp.float32) + low.astype(jnp.float32)
                    ref[k * part : (k + 1) * part, columns] += bias


def softmax_kernel(logit_ref, other_ref, out_ref, low_ref):
    logits = logit_ref[...] + other_ref[...]
    lifted = jnp.exp(logits - jnp.max(logits, axis=-1, keepdims=True))
    softmax_out = lifted / jnp.sum(lifted, axis=-1, keepdims=True)
    out_ref[...] = softmax_out
    low_ref[...] = softmax_out.astype(jnp.bfloat16)


def grad_score_kernel(
    residues, left_row, right_row, place_ref, own_ref, other_ref, full_ref, sent_ref
):
    core = place_ref[0]
    count = own_ref.shape[0] // 2
    part = residues // 2
    right = jnp.concatenate(
        [lanes_of(own_ref, right_row, residues), lanes_of(other_ref, right_row, residues)], axis=1
    )
    rows = pl.ds(pl.multiple_of(left_row + core * part, part), part)
    left = [
        jnp.concatenate(
            [r[p * count + k, rows, :] for r in (own_ref, other_ref) for p in range(2)], axis=1
        )
        for k in range(count)
    ]
    terms = f32_dot(jnp.concatenate(left, axis=0), right, NT)
    full_ref[...] = terms
    sent_ref[...] = terms.astype(jnp.bfloat16)


def softmax_gradient_kernel(
    place_ref, softmax_ref, far_ref, grad_ref, other_ref, out_ref, out_far_ref
):
    half = place_ref[1]
    count = softmax_ref.shape[0]
    for which, probs, ref in ((half, softmax_ref, out_ref), (1 - half, far_ref, out_far_ref)):
        rows = pl.ds(pl.multiple_of(which * count, count), count)
        softmax_out = probs[...].astype(jnp.float32)
        grad_probs = grad_ref[rows, :] + other_ref[rows, :].astype(jnp.float32)
        row_dot = jnp.sum(softmax_out * grad_probs, axis=-1, keepdims=True)
        ref[...] = (softmax_out * (grad_probs - row_dot)).astype(jnp.bfloat16)


def product_kernel(
    residues, scale, first_row, second_row, with_share,
    place_ref, own_ref, far_ref, near_ref, corner_ref, blocks_ref, out_ref, whole_ref,
):
    core, half = place_ref[0], place_ref[1]
    count = blocks_ref.shape[0] // 2
    part = residues // 2
    quarters = (
        (own_ref, core, half), (far_ref, core, 1 - half),
        (near_ref, 1 - core, half), (corner_ref, 1 - core, 1 - half),
    )
    for ref, c, z in quarters:
        for k in range(count // 2):
            start = (z * (count // 2) + k) * residues + c * part
            whole_ref[pl.ds(pl.multiple_of(start, part), part), :] = ref[k * part : (k + 1) * part, :]
    whole = whole_ref[...]
    if with_share:
        for p in range(2):
            columns = pl.ds(pl.multiple_of((half * 2 + p) * LANES, LANES), LANES)
            for q in range(count):
                rows = pl.ds(pl.multiple_of(q * residues + core * part, part), part)
                out_ref[p * count + q, 2 * residues : 2 * residues + part, :] = whole_ref[rows, columns]
    first = f32_dot(whole, lanes_of(blocks_ref, first_row, residues)) * scale
    second = f32_dot(whole, lanes_of(blocks_ref, second_row, residues), TN)
    for row, product in ((0, first), (residues, second)):
        for p in range(2):
            out_ref[p * count : (p + 1) * count, row : row + residues, :] = (
                product[:, p * LANES : (p + 1) * LANES]
                .astype(jnp.bfloat16)
                .reshape(count, residues, LANES)
            )


def share_of(blocks_ref, row, part, heads):
    return jnp.concatenate(
        [
            blocks_ref[:, row : row + part, :]
            .astype(jnp.float32)
            .reshape(heads, 2 * part, LANES)
        ],
        axis=0,
    )


def attended_weight_kernel(
    x_ref, grad_ref, wc_ref, wo_ref, blocks_ref, updated_ref, projected_ref, normed_ref, sums_ref
):
    residues, width = x_ref.shape[1], x_ref.shape[2]
    tiles = width // LANES
    normed = normalized(x_ref)[0].astype(jnp.bfloat16)
    normed_ref[...] = normed
    gate = gate_of(f32_dot(normed, wc_ref[:, 3 * width :]))
    grad = grad_ref[...].reshape(-1, width)
    grad_gated = f32_dot(grad, wo_ref[...], NT)
    attended = unpack_heads(blocks_ref, 0, residues, tiles)
    gated = (gate * attended).astype(jnp.bfloat16)
    updated_ref[...] = f32_dot(gated, wo_ref[...]).astype(jnp.bfloat16).reshape(updated_ref.shape)
    projected_ref[:, :width] = unpack_heads(blocks_ref, residues, residues, tiles).astype(
        jnp.bfloat16
    )
    projected_ref[:, width:] = (grad_gated * attended * gate * (1.0 - gate)).astype(jnp.bfloat16)
    sums_ref[:, : 2 * width] = f32_dot(normed, projected_ref[...], TN).astype(jnp.bfloat16)
    sums_ref[:, 2 * width :] = f32_dot(gated, grad, TN).astype(jnp.bfloat16)


def query_weight_kernel(
    place_ref, normed_ref, attended_sums_ref, blocks_ref,
    projected_ref, keep_ref, send_ref, sums_ref,
):
    width = normed_ref.shape[1]
    tiles, residues = width // LANES, (blocks_ref.shape[1] * 2) // 5
    core = place_ref[0]
    for t in range(2):
        projected_ref[:, t * width : (t + 1) * width] = unpack_heads(
            blocks_ref, t * residues, residues, tiles
        ).astype(jnp.bfloat16)
    sums_ref[:, : 2 * width] = f32_dot(normed_ref[...], projected_ref[...], TN).astype(
        jnp.bfloat16
    )
    sums_ref[:, 2 * width :] = attended_sums_ref[...]
    rows = keep_ref.shape[1]
    for which, ref in ((core, keep_ref), (1 - core, send_ref)):
        for block in range(keep_ref.shape[0]):
            start = pl.multiple_of((2 * block + which) * rows, rows)
            ref[block] = sums_ref[pl.ds(start, rows), :]


def core_sum_kernel(place_ref, keep_ref, other_ref, own_ref, *send_refs):
    chip = place_ref[2]
    for flip, ref in enumerate((own_ref, *send_refs)):
        block = jnp.bitwise_xor(chip, flip)
        total = keep_ref[block].astype(jnp.float32) + other_ref[block].astype(jnp.float32)
        ref[...] = total.astype(ref.dtype)


def plane_sum_kernel(own_ref, pair_weight_ref, *refs):
    *received, out_ref = refs
    total = own_ref[...]
    for ref in received:
        total += ref[...].astype(jnp.float32)
    count = own_ref.shape[1]
    heads = pair_weight_ref.shape[0]
    out_ref[:, :count] = total.astype(out_ref.dtype)
    rest = jnp.zeros((out_ref.shape[0] - heads, out_ref.shape[1] - count), jnp.float32)
    out_ref[:, count:] = jnp.concatenate([pair_weight_ref[...], rest], axis=0).astype(
        out_ref.dtype
    )


def pair_weight_kernel(blocks_ref, pair_ref, mean_ref, spread_ref, out_ref, share_ref):
    heads, part = share_ref.shape[0], pair_ref.shape[0] // 2
    share_ref[...] = share_of(blocks_ref, blocks_ref.shape[1] - part, part, heads)

    def rows(step, carry):
        total, shift = carry
        for k in range(8):
            i = step * 8 + k
            scaled = share_ref[:, i, :] * spread_ref[pl.ds(i, 1), :]
            high, low = two_terms(scaled)
            total += f32_dot(jnp.concatenate([high, low], axis=0), pair_ref[i])
            shift += (high.astype(jnp.float32) + low.astype(jnp.float32)) * mean_ref[pl.ds(i, 1), :]
        return total, shift

    channels = pair_ref.shape[2]
    total, shift = lax.fori_loop(
        0,
        pair_ref.shape[0] // 8,
        rows,
        (jnp.zeros((2 * heads, channels), jnp.float32), jnp.zeros((heads, LANES), jnp.float32)),
    )
    out_ref[...] = total[:heads] + total[heads:] - jnp.sum(shift, axis=1, keepdims=True)


def alignment_kernel(x_ref, wc_ref, query_key_ref, value_gate_ref, out_ref):
    normed, spread = normalized(x_ref)
    width = x_ref.shape[2]
    gradient = f32_dot(query_key_ref[...], wc_ref[:, : 2 * width], NT) + f32_dot(
        value_gate_ref[...], wc_ref[:, 2 * width :], NT
    )
    out_ref[...] = (
        layer_norm_backward(gradient, normed, spread).astype(jnp.bfloat16).reshape(out_ref.shape)
    )


def pair_kernel(blocks_row, blocks_ref, pair_ref, weight_ref, bias_ref, mean_ref, spread_ref, out_ref, share_ref):
    heads, channels = weight_ref.shape
    part = pair_ref.shape[0] // 2
    share_ref[...] = share_of(blocks_ref, blocks_row, part, heads)
    first, second = two_terms(centred(weight_ref[...]))
    zero = jnp.zeros((heads, channels), jnp.bfloat16)
    top = lax.broadcasted_iota(jnp.int32, (heads, channels), 0) < 2
    ones = jnp.where(top, 1.0, 0.0).astype(jnp.bfloat16)
    right = jnp.concatenate(
        [
            jnp.concatenate([first, first, second, ones, zero], axis=0),
            jnp.concatenate([zero, zero, zero, zero, ones], axis=0),
        ],
        axis=1,
    )
    row = lax.broadcasted_iota(jnp.int32, (heads, LANES), 0)

    def rows_of_two(value):
        high, low = two_terms(value)
        high, low = high.astype(jnp.float32), low.astype(jnp.float32)
        return jnp.where(row == 0, high, jnp.where(row == 1, low, 0.0)).astype(jnp.bfloat16)

    def rows(step, carry):
        for k in range(8):
            i = step * 8 + k
            gradient = share_ref[:, i, :]
            spread = spread_ref[pl.ds(i, 1), :]
            cross = jnp.sum(gradient * bias_ref[:, i, :], axis=0, keepdims=True) / channels
            slope = spread * spread * cross
            high, low = two_terms(gradient * spread)
            left = jnp.concatenate(
                [
                    high, low, high,
                    rows_of_two(jnp.broadcast_to(slope * mean_ref[pl.ds(i, 1), :], row.shape)),
                    rows_of_two(jnp.broadcast_to(slope, row.shape)),
                ],
                axis=0,
            )
            terms = f32_dot(left, right, TN)
            entries = pair_ref[i].astype(jnp.float32)
            out_ref[i] = (terms[:, :channels] - terms[:, channels:] * entries).astype(jnp.bfloat16)
        return carry

    lax.fori_loop(0, pair_ref.shape[0] // 8, rows, 0)


def output_kernel(parts_ref, combined_ref, out_weight_ref, pair_weight_ref):
    width = combined_ref.shape[0]
    rows = parts_ref.shape[1]
    for h in range(parts_ref.shape[0]):
        block = slice(h * rows, (h + 1) * rows)
        part = parts_ref[h].astype(jnp.float32)
        combined_ref[block, :] = part[:, : 4 * width]
        out_weight_ref[block, :] = part[:, 4 * width : 5 * width]
        share = part[: pair_weight_ref.shape[0], 5 * width :]
        pair_weight_ref[...] = share if h == 0 else pair_weight_ref[...] + share


def call(kernel, outs, *args, scratch=(), place=None, flops=0, after=(), outside=0, late=0):
    whole, anywhere = pl.BlockSpec(memory_space=pltpu.VMEM), pl.BlockSpec(memory_space=pl.ANY)
    specs = [anywhere] * outside + [whole] * (len(args) - outside)
    ahead = () if place is None else (place,)
    shapes = [jax.ShapeDtypeStruct(*o) for o in outs]
    moved = sum(math.prod(a.shape) * a.dtype.itemsize for a in list(args) + shapes)
    first = len(ahead) + len(args)
    last = first + len(after)

    def wrapped(*refs):
        given, rest = list(refs[:first]), refs[last:]
        if outside:
            *rest, arrived = rest
            held = rest[len(rest) - outside :]
            rest = rest[: len(rest) - outside]
            copies = []
            for k in range(outside):
                copies.append(
                    pltpu.make_async_copy(given[len(ahead) + k], held[k], arrived.at[k])
                )
                given[len(ahead) + k] = held[k]
            for copy in copies:
                copy.start()
            for copy in copies[: outside - late]:
                copy.wait()
            if late:
                given.insert(0, lambda: [copy.wait() for copy in copies[outside - late :]])
        kernel(*given, *rest)

    held = [pltpu.VMEM(a.shape, a.dtype) for a in args[:outside]]
    if outside:
        held.append(pltpu.SemaphoreType.DMA((outside,)))
    return pl.pallas_call(
        wrapped,
        out_shape=shapes,
        in_specs=[pl.BlockSpec(memory_space=pltpu.SMEM)] * len(ahead)
        + specs
        + [anywhere] * len(after),
        out_specs=[whole] * len(shapes),
        scratch_shapes=[*scratch, *held],
        compiler_params=pltpu.CompilerParams(
            vmem_limit_bytes=ARGUMENT_VMEM_LIMIT if outside else VMEM_LIMIT
        ),
        cost_estimate=pl.CostEstimate(flops=flops, bytes_accessed=moved, transcendentals=0),
    )(*ahead, *args, *after)


def swapped(mine, axis_name, distance):
    size = lax.axis_size(axis_name)
    return lax.ppermute(mine, axis_name, [(a, a ^ distance) for a in range(size)])


def fits_heads(alignment_rows, pair_entries, pair_weight):
    channels, heads = pair_weight.shape
    return (
        lax.axis_size("seq") == 4
        and lax.axis_size("res") == heads == 8
        and alignment_rows.shape[0] == 2 * SLOTS
        and alignment_rows.shape[1] == pair_entries.shape[0] == 64
        and alignment_rows.shape[2] == 2 * LANES
        and pair_entries.shape[1] == channels == LANES
    )


def head_body(
    alignment_rows, pair_entries, combined_weight, output_weight, pair_weight, updated_gradient
):
    sequences, residues, width = alignment_rows.shape
    channels, heads = pair_weight.shape
    tokens = sequences * residues
    seq_size, res_size = lax.axis_size("seq"), lax.axis_size("res")
    seq_half = seq_size // 2
    total = residues * res_size
    group = 2 * res_size
    groups = [[g * group + k for k in range(group)] for g in range(seq_half)]
    scale = 1.0 / math.sqrt(width // heads * sequences * seq_size)
    res_index, seq_index = lax.axis_index("res"), lax.axis_index("seq")
    place = jnp.stack([res_index % 2, seq_index // 2, res_index // 2]).astype(jnp.int32)
    bf16, f32 = jnp.bfloat16, jnp.float32

    def across(blocks):
        return lax.all_to_all(blocks, ("seq", "res"), 0, 0, axis_index_groups=groups, tiled=True)

    x, grad, wc, wo = alignment_rows, updated_gradient, combined_weight, output_weight
    (value_blocks,) = call(
        value_kernel, [((group, 2 * residues, LANES), bf16)], x, grad, wc, wo,
        flops=8 * tokens * width * width, outside=4,
    )
    value_blocks = across(value_blocks)
    query_blocks, bias, mean, spread = call(
        functools.partial(query_kernel, scale),
        [
            ((group, 3 * residues, LANES), bf16),
            ((heads, residues, LANES), f32),
            ((residues, LANES), f32),
            ((residues, LANES), f32),
        ],
        x, wc, pair_entries, pair_weight.T,
        flops=8 * tokens * width * width, outside=3, late=1,
    )
    value_blocks, query_blocks = lax.optimization_barrier((value_blocks, query_blocks))
    query_blocks = across(query_blocks)

    quarter, half_rows = (total // 4, total), (total // 2, total)
    grad_full, grad_sent = call(
        functools.partial(grad_score_kernel, residues, residues, 0),
        [(half_rows, f32), (half_rows, bf16)],
        value_blocks, swapped(value_blocks, "res", 1),
        place=place, flops=2 * total * total * width,
    )
    grad_other = swapped(grad_sent, "seq", seq_half)
    query_blocks, grad_other = lax.optimization_barrier((query_blocks, grad_other))
    logit_mine, logit_sent = call(
        functools.partial(score_kernel, residues, 0, residues, True),
        [(quarter, f32), (quarter, f32)],
        query_blocks, swapped(query_blocks, "res", 1),
        place=place, flops=2 * total * total * width,
    )
    softmax_out, probs = call(
        softmax_kernel, [(quarter, f32), (quarter, bf16)],
        logit_mine, swapped(logit_sent, "seq", seq_half),
        flops=total * total,
    )

    def products(mine, far, blocks, first_row, second_row, with_share, factor):
        rows = 2 * residues + (residues // 2 if with_share else 0)
        (out,) = call(
            functools.partial(
                product_kernel, residues, factor, first_row, second_row, with_share
            ),
            [((group, rows, LANES), bf16)],
            mine, far, swapped(mine, "res", 1), swapped(far, "res", 1), blocks,
            scratch=[pltpu.VMEM((total, total), bf16)],
            place=place, flops=4 * total * total * width,
        )
        return out

    probs_far = swapped(probs, "seq", seq_half)
    attended = products(probs, probs_far, value_blocks, 0, residues, False, 1.0)
    attended_blocks = across(attended)
    softmax_out = lax.optimization_barrier((attended, softmax_out))[1]
    grad_logits, grad_far = call(
        softmax_gradient_kernel, [(quarter, bf16), (quarter, bf16)],
        softmax_out, probs_far, grad_full, grad_other,
        place=place, flops=total * total,
    )
    grad_sums = products(grad_logits, grad_far, query_blocks, residues, 0, True, scale)
    grad_sums, attended_blocks = lax.optimization_barrier((grad_sums, attended_blocks))
    grad_blocks = across(grad_sums)

    updated, value_gate, normed, attended_sums = call(
        attended_weight_kernel,
        [
            (x.shape, bf16),
            ((tokens, 2 * width), bf16),
            ((tokens, width), bf16),
            ((width, 3 * width), bf16),
        ],
        x, grad, wc, wo, attended_blocks,
        flops=14 * tokens * width * width, outside=4,
    )
    share = pltpu.VMEM((heads, residues, LANES), f32)
    columns = 5 * width
    rows = width // res_size
    part_rows = ((res_size // 2, rows, columns), bf16)
    (pair_weight_part,) = call(
        pair_weight_kernel, [((heads, channels), f32)],
        grad_blocks, pair_entries, mean, spread,
        scratch=[share], flops=4 * tokens * width * width,
    )
    query_key, keep, send = call(
        query_weight_kernel,
        [((tokens, 2 * width), bf16), part_rows, part_rows],
        normed, attended_sums, grad_blocks,
        scratch=[pltpu.VMEM((width, columns), bf16)],
        place=place, flops=4 * tokens * width * width, after=(pair_weight_part,),
    )
    own, *sent = call(
        core_sum_kernel,
        [((rows, columns), f32)] + [((rows, columns), bf16)] * 3,
        keep, swapped(send, "res", 1), place=place,
    )
    received = [swapped(t, "res", 2 * flip) for flip, t in enumerate(sent, 1)]
    (pair_gradient,) = call(
        functools.partial(pair_kernel, 2 * residues),
        [(pair_entries.shape, bf16)],
        grad_blocks, pair_entries, pair_weight.T, bias, mean, spread,
        scratch=[share], flops=8 * tokens * width * width,
    )
    (alignment_gradient,) = call(
        alignment_kernel, [(x.shape, bf16)], x, wc, query_key, value_gate,
        flops=8 * tokens * width * width,
    )
    received, alignment_gradient = lax.optimization_barrier((received, alignment_gradient))
    (part,) = call(
        plane_sum_kernel, [((rows, columns + channels), bf16)], own, pair_weight_part, *received
    )
    def added(mine, other):
        return (mine.astype(f32) + other.astype(f32)).astype(bf16)

    other_plane = swapped(part, "seq", 1)
    part = added(part, other_plane)
    other_half = swapped(part, "seq", seq_half)
    other_half, pair_gradient = lax.optimization_barrier((other_half, pair_gradient))
    part = added(part, other_half)
    combined_gradient, output_gradient, pair_weight_gradient = call(
        output_kernel,
        [(wc.shape, f32), (wo.shape, f32), ((heads, channels), f32)],
        lax.all_gather(part, "res", axis=0),
    )
    return (
        updated,
        alignment_gradient,
        pair_gradient,
        combined_gradient,
        output_gradient,
        pair_weight_gradient.T,
    )


def body(alignment_rows, pair_entries, combined_weight, output_weight, pair_weight, updated_gradient):
    chosen = head_body if fits_heads(alignment_rows, pair_entries, pair_weight) else gathered_body
    return chosen(
        alignment_rows, pair_entries, combined_weight, output_weight, pair_weight, updated_gradient
    )


def solution(mesh):
    return jax.shard_map(
        body,
        mesh=mesh,
        in_specs=(
            P("seq", "res", None),
            P("res", "seq", None),
            P(),
            P(),
            P(),
            P("seq", "res", None),
        ),
        out_specs=(
            P("seq", "res", None),
            P("seq", "res", None),
            P("res", "seq", None),
            P(),
            P(),
            P(),
        ),
        check_vma=False,
    )
```

```python
import functools
import math

import jax
import jax.numpy as jnp
from jax import lax
from jax.experimental import pallas as pl
from jax.experimental.pallas import tpu as pltpu
from jax.sharding import PartitionSpec as P

eps_norm = 1e-05


def layer_normalize(values):
    values = values.astype(jnp.float32)
    center = values - jnp.mean(values, axis=-1, keepdims=True)
    broadcast_pair = lax.rsqrt(jnp.mean(center * center, axis=-1, keepdims=True) + eps_norm)
    return (center * broadcast_pair, broadcast_pair)


def layer_norm_backward(normalized_gradient, normalized_rows, broadcast_pair):
    mean_grad = jnp.mean(normalized_gradient, axis=-1, keepdims=True)
    mean_cross = jnp.mean(normalized_gradient * normalized_rows, axis=-1, keepdims=True)
    return broadcast_pair * (normalized_gradient - mean_grad - normalized_rows * mean_cross)


def split_heads(tensor, head_count):
    return tensor.reshape(
        tensor.shape[0], tensor.shape[1], head_count, tensor.shape[2] // head_count
    )


def merge_heads(tensor):
    return tensor.reshape(tensor.shape[0], tensor.shape[1], tensor.shape[2] * tensor.shape[3])


def gathered_body(
    alignment_rows, pair_entries, combined_weight, output_weight, pair_weight, updated_gradient
):
    sequence_count, residue_count, alignment_width = alignment_rows.shape
    head_count = pair_weight.shape[1]
    query_width = output_weight.shape[0]
    head_dim = query_width // head_count
    column_count = pair_entries.shape[1]
    token_count = sequence_count * residue_count
    score_scale = 1.0 / math.sqrt(head_dim * sequence_count * lax.axis_size("seq"))
    normalized_rows, broadcast_pair = layer_normalize(alignment_rows)
    normalized_rows_backward = normalized_rows.astype(jnp.bfloat16).reshape(
        token_count, alignment_width
    )
    projected = jnp.dot(
        normalized_rows_backward, combined_weight, preferred_element_type=jnp.float32
    ).reshape(sequence_count, residue_count, 4 * query_width)
    queries = (projected[..., :query_width] * score_scale).astype(jnp.bfloat16)
    key_rows = projected[..., query_width : 2 * query_width].astype(jnp.bfloat16)
    value_rows = projected[..., 2 * query_width : 3 * query_width].astype(jnp.bfloat16)
    gate_open = jax.nn.sigmoid(projected[..., 3 * query_width :])
    all_keys, all_values = (
        lax.all_gather(key_rows, "res", axis=1, tiled=True),
        lax.all_gather(value_rows, "res", axis=1, tiled=True),
    )
    query_heads = split_heads(queries, head_count)
    key_heads = split_heads(all_keys, head_count)
    value_heads = split_heads(all_values, head_count)
    score_terms = jnp.einsum(
        "sihd,sjhd->hij", query_heads, key_heads, preferred_element_type=jnp.float32
    )
    pair_normed, pair_spread = layer_normalize(pair_entries)
    pair_bias = jnp.einsum("ijc,ch->hij", pair_normed, pair_weight, precision=lax.Precision.HIGHEST)
    col_start = lax.axis_index("seq") * column_count
    own_block = lax.dynamic_slice_in_dim(score_terms, col_start, column_count, 2) + pair_bias
    logits = lax.psum(lax.dynamic_update_slice_in_dim(score_terms, own_block, col_start, 2), "seq")
    row_top = jnp.max(logits, axis=-1, keepdims=True)
    lifted = jnp.exp(logits - row_top)
    softmax_out = lifted / jnp.sum(lifted, axis=-1, keepdims=True)
    softmax_low = softmax_out.astype(jnp.bfloat16)
    attended = merge_heads(
        jnp.einsum("hij,sjhd->sihd", softmax_low, value_heads, preferred_element_type=jnp.float32)
    )
    gated_out = (gate_open * attended).astype(jnp.bfloat16)
    flattened_gated = gated_out.reshape(token_count, query_width)
    updated = (
        jnp.dot(flattened_gated, output_weight, preferred_element_type=jnp.float32)
        .astype(jnp.bfloat16)
        .reshape(sequence_count, residue_count, alignment_width)
    )
    flattened_gradient = updated_gradient.reshape(token_count, alignment_width)
    grad_gated = jnp.dot(
        flattened_gradient, output_weight.T, preferred_element_type=jnp.float32
    ).reshape(sequence_count, residue_count, query_width)
    out_local = jnp.dot(flattened_gated.T, flattened_gradient, preferred_element_type=jnp.float32)
    grad_attended = (grad_gated * gate_open).astype(jnp.bfloat16)
    grad_gate_logit = grad_gated * attended * gate_open * (1.0 - gate_open)
    attended_grad_heads = split_heads(grad_attended, head_count)
    grad_terms = jnp.einsum(
        "sihd,sjhd->hij", attended_grad_heads, value_heads, preferred_element_type=jnp.float32
    )
    grad_probs = lax.psum(grad_terms, "seq")
    row_dot = jnp.sum(softmax_out * grad_probs, axis=-1, keepdims=True)
    grad_logits = softmax_out * (grad_probs - row_dot)
    grad_logits_b = grad_logits.astype(jnp.bfloat16)
    logit_share = lax.dynamic_slice_in_dim(grad_logits, col_start, column_count, 2)
    grad_query_heads = (
        jnp.einsum("hij,sjhd->sihd", grad_logits_b, key_heads, preferred_element_type=jnp.float32)
        * score_scale
    )
    key_part = jnp.einsum(
        "hij,sihd->jshd", grad_logits_b, query_heads, preferred_element_type=jnp.float32
    )
    value_part = jnp.einsum(
        "hij,sihd->jshd", softmax_low, attended_grad_heads, preferred_element_type=jnp.float32
    )
    summed = lax.psum_scatter(
        jnp.concatenate([merge_heads(key_part), merge_heads(value_part)], axis=-1),
        "res",
        scatter_dimension=0,
        tiled=True,
    )
    key_value_grads = jnp.transpose(summed, (1, 0, 2))
    projected_gradient = jnp.concatenate(
        [merge_heads(grad_query_heads), key_value_grads, grad_gate_logit], axis=-1
    )
    projected_gradient = projected_gradient.astype(jnp.bfloat16).reshape(
        token_count, 4 * query_width
    )
    qkvg_local = jnp.dot(
        normalized_rows_backward.T, projected_gradient, preferred_element_type=jnp.float32
    )
    normalized_gradient = jnp.dot(
        projected_gradient, combined_weight.T, preferred_element_type=jnp.float32
    ).reshape(sequence_count, residue_count, alignment_width)
    alignment_gradient = layer_norm_backward(
        normalized_gradient, normalized_rows, broadcast_pair
    ).astype(jnp.bfloat16)
    pair_w_local = jnp.einsum(
        "ijc,hij->ch", pair_normed, logit_share, precision=lax.Precision.HIGHEST
    )
    grad_pair_normed = jnp.einsum(
        "hij,ch->ijc", logit_share, pair_weight, precision=lax.Precision.HIGHEST
    )
    pair_gradient = layer_norm_backward(grad_pair_normed, pair_normed, pair_spread).astype(
        jnp.bfloat16
    )
    combined_weight_gradient, output_weight_gradient, pair_weight_gradient = lax.psum(
        (qkvg_local, out_local, pair_w_local), ("seq", "res")
    )
    return (
        updated,
        alignment_gradient,
        pair_gradient,
        combined_weight_gradient,
        output_weight_gradient,
        pair_weight_gradient,
    )


VMEM_LIMIT = 20 * 1024 * 1024
ARGUMENT_VMEM_LIMIT = 56 * 1024 * 1024
LANES = 128
SLOTS = 4
NT = (((1,), (1,)), ((), ()))
TN = (((0,), (0,)), ((), ()))


def f32_dot(left, right, dims=None):
    if dims is None:
        return jnp.dot(left, right, preferred_element_type=jnp.float32)
    return lax.dot_general(left, right, dims, preferred_element_type=jnp.float32)


def two_terms(values):
    high = values.astype(jnp.bfloat16)
    return high, (values - high.astype(jnp.float32)).astype(jnp.bfloat16)


def slot_select(pieces):
    slot = lax.broadcasted_iota(jnp.int32, pieces[0].shape, 1) // (LANES // SLOTS)
    result = pieces[0]
    for k in range(1, SLOTS):
        result = jnp.where(slot == k, pieces[k], result)
    return result


def pack_heads(out_ref, row, tensor, residues):
    for core in range(2):
        for tile in range(tensor.shape[1] // LANES):
            rolled = []
            for s in range(SLOTS):
                start = (core * SLOTS + s) * residues
                piece = tensor[start : start + residues, tile * LANES : (tile + 1) * LANES]
                rolled.append(pltpu.roll(piece, s * LANES // SLOTS, 1) if s else piece)
            for j in range(SLOTS):
                block = slot_select([rolled[(k - j) % SLOTS] for k in range(SLOTS)])
                out_ref[(tile * SLOTS + j) * 2 + core, row : row + residues, :] = block.astype(
                    jnp.bfloat16
                )


def unpack_heads(in_ref, row, residues, tiles):
    rows = []
    for core in range(2):
        for s in range(SLOTS):
            pieces = []
            for tile in range(tiles):
                blocks = [
                    in_ref[
                        (tile * SLOTS + (k - s) % SLOTS) * 2 + core, row : row + residues, :
                    ].astype(jnp.float32)
                    for k in range(SLOTS)
                ]
                block = slot_select(blocks)
                pieces.append(pltpu.roll(block, LANES - s * LANES // SLOTS, 1) if s else block)
            rows.append(jnp.concatenate(pieces, axis=1))
    return jnp.concatenate(rows, axis=0)


def normalized(x_ref):
    width = x_ref.shape[-1]
    values = x_ref[...].reshape(-1, width).astype(jnp.float32)
    return layer_normalize(values)


def gate_of(logits):
    return 1.0 / (1.0 + jnp.exp(-logits))


def query_kernel(scale, x_ref, wc_ref, out_ref):
    residues, width = x_ref.shape[1], x_ref.shape[2]
    normed = normalized(x_ref)[0].astype(jnp.bfloat16)
    pack_heads(out_ref, 0, f32_dot(normed, wc_ref[:, :width]) * scale, residues)
    pack_heads(out_ref, residues, f32_dot(normed, wc_ref[:, width : 2 * width]), residues)


def centred(weight):
    return weight - jnp.mean(weight, axis=1, keepdims=True)


def value_kernel(
    arrive, x_ref, grad_ref, wc_ref, wo_ref, pair_ref, weight_ref,
    out_ref, bias_ref, mean_ref, spread_ref,
):
    residues, width = x_ref.shape[1], x_ref.shape[2]
    heads = weight_ref.shape[0]
    normed = normalized(x_ref)[0].astype(jnp.bfloat16)
    values = f32_dot(normed, wc_ref[:, 2 * width : 3 * width])
    gate = gate_of(f32_dot(normed, wc_ref[:, 3 * width :]))
    grad_gated = f32_dot(grad_ref[...].reshape(-1, width), wo_ref[...], NT)
    pack_heads(out_ref, 0, values, residues)
    pack_heads(out_ref, residues, grad_gated * gate, residues)

    arrive()
    columns, channels = pair_ref.shape[1], pair_ref.shape[2]
    weight = centred(weight_ref[...])
    first = weight.astype(jnp.bfloat16)
    second, third = two_terms(weight - first.astype(jnp.float32))
    share = jnp.full((heads, channels), 1.0 / channels, jnp.bfloat16)
    left = jnp.concatenate([first, second, third, share], axis=0)
    average = jnp.full((channels, channels), 1.0 / channels, jnp.bfloat16)
    step_rows = 64

    def rows(step, carry):
        start = pl.multiple_of(step * step_rows, step_rows)
        entries = pair_ref[pl.ds(start, step_rows)].reshape(step_rows * columns, channels)
        center = entries.astype(jnp.float32) - f32_dot(entries, average)
        high, low = two_terms(center * center)
        variance = f32_dot(share, high, NT) + f32_dot(share, low, NT)
        spread = lax.rsqrt(variance + eps_norm)
        raw = f32_dot(left, entries, NT)
        bias = spread * (raw[:heads] + raw[heads : 2 * heads] + raw[2 * heads : 3 * heads])
        for k in range(step_rows):
            lanes = slice(k * columns, (k + 1) * columns)
            bias_ref[:, start + k, :] = bias[:, lanes]
            mean_ref[pl.ds(start + k, 1), :] = raw[3 * heads : 3 * heads + 1, lanes]
            spread_ref[pl.ds(start + k, 1), :] = spread[:1, lanes]
        return carry

    lax.fori_loop(0, pair_ref.shape[0] // step_rows, rows, 0)
    half = residues // 2
    for h in range(heads):
        for core in range(2):
            high, low = two_terms(bias_ref[h, core * half : (core + 1) * half, :])
            out_ref[h * 2 + core, 2 * residues : 2 * residues + half, :] = high
            out_ref[h * 2 + core, 2 * residues + half : 3 * residues, :] = low


def lanes_of(blocks_ref, row, residues):
    count = blocks_ref.shape[0] // 2
    planes = [
        blocks_ref[p * count : (p + 1) * count, row : row + residues, :].reshape(-1, LANES)
        for p in range(2)
    ]
    return jnp.concatenate(planes, axis=1)


def score_kernel(
    residues, left_row, right_row, place_ref, own_ref, other_ref, mine_ref, sent_ref
):
    core, half = place_ref[0], place_ref[1]
    count = own_ref.shape[0] // 2
    part = residues // 2
    right = jnp.concatenate(
        [lanes_of(own_ref, right_row, residues), lanes_of(other_ref, right_row, residues)], axis=1
    )
    for which, ref in ((half, mine_ref), (1 - half, sent_ref)):
        left = []
        for k in range(count // 2):
            block = which * (count // 2) + k
            rows = pl.ds(pl.multiple_of(left_row + core * part, part), part)
            left.append(
                jnp.concatenate(
                    [
                        r[p * count + block, rows, :]
                        for r in (own_ref, other_ref)
                        for p in range(2)
                    ],
                    axis=1,
                )
            )
        ref[...] = f32_dot(jnp.concatenate(left, axis=0), right, NT).astype(ref.dtype)


def bias_kernel(row, place_ref, blocks_ref, mine_ref, sent_ref):
    half = place_ref[1]
    count = blocks_ref.shape[0] // 2
    for which, ref in ((half, mine_ref), (1 - half, sent_ref)):
        for p in range(2):
            for k in range(count // 2):
                block = p * count + which * (count // 2) + k
                ref[p * (count // 2) + k] = blocks_ref[block, row:, :]


def softmax_kernel(
    place_ref, logit_ref, other_ref, bias_ref, bias_other_ref, out_ref, low_ref
):
    half = place_ref[1]
    count, part = bias_ref.shape[0] // 2, bias_ref.shape[1] // 2
    out_ref[...] = logit_ref[...] + other_ref[...]
    for which, ref in ((half, bias_ref), (1 - half, bias_other_ref)):
        for p in range(2):
            columns = pl.ds(pl.multiple_of((which * 2 + p) * LANES, LANES), LANES)
            for k in range(count):
                high = ref[p * count + k, :part, :].astype(jnp.float32)
                low = ref[p * count + k, part:, :].astype(jnp.float32)
                out_ref[k * part : (k + 1) * part, columns] += high + low
    logits = out_ref[...]
    lifted = jnp.exp(logits - jnp.max(logits, axis=-1, keepdims=True))
    softmax_out = lifted / jnp.sum(lifted, axis=-1, keepdims=True)
    out_ref[...] = softmax_out
    low_ref[...] = softmax_out.astype(jnp.bfloat16)


def grad_score_kernel(
    residues, left_row, right_row, place_ref, own_ref, other_ref, full_ref, sent_ref
):
    core = place_ref[0]
    count = own_ref.shape[0] // 2
    part = residues // 2
    right = jnp.concatenate(
        [lanes_of(own_ref, right_row, residues), lanes_of(other_ref, right_row, residues)], axis=1
    )
    rows = pl.ds(pl.multiple_of(left_row + core * part, part), part)
    left = [
        jnp.concatenate(
            [r[p * count + k, rows, :] for r in (own_ref, other_ref) for p in range(2)], axis=1
        )
        for k in range(count)
    ]
    terms = f32_dot(jnp.concatenate(left, axis=0), right, NT)
    full_ref[...] = terms
    sent_ref[...] = terms.astype(jnp.bfloat16)


def softmax_gradient_kernel(
    place_ref, softmax_ref, far_ref, grad_ref, other_ref, out_ref, out_far_ref
):
    half = place_ref[1]
    count = softmax_ref.shape[0]
    for which, probs, ref in ((half, softmax_ref, out_ref), (1 - half, far_ref, out_far_ref)):
        rows = pl.ds(pl.multiple_of(which * count, count), count)
        softmax_out = probs[...].astype(jnp.float32)
        grad_probs = grad_ref[rows, :] + other_ref[rows, :].astype(jnp.float32)
        row_dot = jnp.sum(softmax_out * grad_probs, axis=-1, keepdims=True)
        ref[...] = (softmax_out * (grad_probs - row_dot)).astype(jnp.bfloat16)


def product_kernel(
    residues, scale, first_row, second_row, with_share,
    place_ref, own_ref, far_ref, near_ref, corner_ref, blocks_ref, out_ref, whole_ref,
):
    core, half = place_ref[0], place_ref[1]
    count = blocks_ref.shape[0] // 2
    part = residues // 2
    quarters = (
        (own_ref, core, half), (far_ref, core, 1 - half),
        (near_ref, 1 - core, half), (corner_ref, 1 - core, 1 - half),
    )
    for ref, c, z in quarters:
        for k in range(count // 2):
            start = (z * (count // 2) + k) * residues + c * part
            whole_ref[pl.ds(pl.multiple_of(start, part), part), :] = ref[k * part : (k + 1) * part, :]
    whole = whole_ref[...]
    if with_share:
        for p in range(2):
            columns = pl.ds(pl.multiple_of((half * 2 + p) * LANES, LANES), LANES)
            for q in range(count):
                rows = pl.ds(pl.multiple_of(q * residues + core * part, part), part)
                out_ref[p * count + q, 2 * residues : 2 * residues + part, :] = whole_ref[rows, columns]
    first = f32_dot(whole, lanes_of(blocks_ref, first_row, residues)) * scale
    second = f32_dot(whole, lanes_of(blocks_ref, second_row, residues), TN)
    for row, product in ((0, first), (residues, second)):
        for p in range(2):
            out_ref[p * count : (p + 1) * count, row : row + residues, :] = (
                product[:, p * LANES : (p + 1) * LANES]
                .astype(jnp.bfloat16)
                .reshape(count, residues, LANES)
            )


def share_of(blocks_ref, row, part, heads):
    return jnp.concatenate(
        [
            blocks_ref[:, row : row + part, :]
            .astype(jnp.float32)
            .reshape(heads, 2 * part, LANES)
        ],
        axis=0,
    )


def attended_weight_kernel(
    x_ref, grad_ref, wc_ref, wo_ref, blocks_ref, updated_ref, projected_ref, normed_ref, sums_ref
):
    residues, width = x_ref.shape[1], x_ref.shape[2]
    tiles = width // LANES
    normed = normalized(x_ref)[0].astype(jnp.bfloat16)
    normed_ref[...] = normed
    gate = gate_of(f32_dot(normed, wc_ref[:, 3 * width :]))
    grad = grad_ref[...].reshape(-1, width)
    grad_gated = f32_dot(grad, wo_ref[...], NT)
    attended = unpack_heads(blocks_ref, 0, residues, tiles)
    gated = (gate * attended).astype(jnp.bfloat16)
    updated_ref[...] = f32_dot(gated, wo_ref[...]).astype(jnp.bfloat16).reshape(updated_ref.shape)
    projected_ref[:, :width] = unpack_heads(blocks_ref, residues, residues, tiles).astype(
        jnp.bfloat16
    )
    projected_ref[:, width:] = (grad_gated * attended * gate * (1.0 - gate)).astype(jnp.bfloat16)
    sums_ref[:, : 2 * width] = f32_dot(normed, projected_ref[...], TN).astype(jnp.bfloat16)
    sums_ref[:, 2 * width :] = f32_dot(gated, grad, TN).astype(jnp.bfloat16)


def query_weight_kernel(
    place_ref, normed_ref, attended_sums_ref, blocks_ref,
    projected_ref, keep_ref, send_ref, sums_ref,
):
    width = normed_ref.shape[1]
    tiles, residues = width // LANES, (blocks_ref.shape[1] * 2) // 5
    core = place_ref[0]
    for t in range(2):
        projected_ref[:, t * width : (t + 1) * width] = unpack_heads(
            blocks_ref, t * residues, residues, tiles
        ).astype(jnp.bfloat16)
    sums_ref[:, : 2 * width] = f32_dot(normed_ref[...], projected_ref[...], TN).astype(
        jnp.bfloat16
    )
    sums_ref[:, 2 * width :] = attended_sums_ref[...]
    rows = keep_ref.shape[1]
    for which, ref in ((core, keep_ref), (1 - core, send_ref)):
        for block in range(keep_ref.shape[0]):
            start = pl.multiple_of((2 * block + which) * rows, rows)
            ref[block] = sums_ref[pl.ds(start, rows), :]


def core_sum_kernel(place_ref, keep_ref, other_ref, own_ref, *send_refs):
    chip = place_ref[2]
    for flip, ref in enumerate((own_ref, *send_refs)):
        block = jnp.bitwise_xor(chip, flip)
        total = keep_ref[block].astype(jnp.float32) + other_ref[block].astype(jnp.float32)
        ref[...] = total.astype(ref.dtype)


def plane_sum_kernel(own_ref, pair_weight_ref, *refs):
    *received, out_ref = refs
    total = own_ref[...]
    for ref in received:
        total += ref[...].astype(jnp.float32)
    count = own_ref.shape[1]
    heads = pair_weight_ref.shape[0]
    out_ref[:, :count] = total.astype(out_ref.dtype)
    rest = jnp.zeros((out_ref.shape[0] - heads, out_ref.shape[1] - count), jnp.float32)
    out_ref[:, count:] = jnp.concatenate([pair_weight_ref[...], rest], axis=0).astype(
        out_ref.dtype
    )


def pair_weight_kernel(blocks_ref, pair_ref, mean_ref, spread_ref, out_ref, share_ref):
    heads, part = share_ref.shape[0], pair_ref.shape[0] // 2
    share_ref[...] = share_of(blocks_ref, blocks_ref.shape[1] - part, part, heads)

    def rows(step, carry):
        total, shift = carry
        for k in range(8):
            i = step * 8 + k
            scaled = share_ref[:, i, :] * spread_ref[pl.ds(i, 1), :]
            high, low = two_terms(scaled)
            total += f32_dot(jnp.concatenate([high, low], axis=0), pair_ref[i])
            shift += (high.astype(jnp.float32) + low.astype(jnp.float32)) * mean_ref[pl.ds(i, 1), :]
        return total, shift

    channels = pair_ref.shape[2]
    total, shift = lax.fori_loop(
        0,
        pair_ref.shape[0] // 8,
        rows,
        (jnp.zeros((2 * heads, channels), jnp.float32), jnp.zeros((heads, LANES), jnp.float32)),
    )
    out_ref[...] = total[:heads] + total[heads:] - jnp.sum(shift, axis=1, keepdims=True)


def alignment_kernel(x_ref, wc_ref, query_key_ref, value_gate_ref, out_ref):
    normed, spread = normalized(x_ref)
    width = x_ref.shape[2]
    gradient = f32_dot(query_key_ref[...], wc_ref[:, : 2 * width], NT) + f32_dot(
        value_gate_ref[...], wc_ref[:, 2 * width :], NT
    )
    out_ref[...] = (
        layer_norm_backward(gradient, normed, spread).astype(jnp.bfloat16).reshape(out_ref.shape)
    )


def pair_kernel(blocks_row, blocks_ref, pair_ref, weight_ref, bias_ref, mean_ref, spread_ref, out_ref, share_ref):
    heads, channels = weight_ref.shape
    part = pair_ref.shape[0] // 2
    share_ref[...] = share_of(blocks_ref, blocks_row, part, heads)
    first, second = two_terms(centred(weight_ref[...]))
    zero = jnp.zeros((heads, channels), jnp.bfloat16)
    top = lax.broadcasted_iota(jnp.int32, (heads, channels), 0) < 2
    ones = jnp.where(top, 1.0, 0.0).astype(jnp.bfloat16)
    right = jnp.concatenate(
        [
            jnp.concatenate([first, first, second, ones, zero], axis=0),
            jnp.concatenate([zero, zero, zero, zero, ones], axis=0),
        ],
        axis=1,
    )
    row = lax.broadcasted_iota(jnp.int32, (heads, LANES), 0)

    def rows_of_two(value):
        high, low = two_terms(value)
        high, low = high.astype(jnp.float32), low.astype(jnp.float32)
        return jnp.where(row == 0, high, jnp.where(row == 1, low, 0.0)).astype(jnp.bfloat16)

    def rows(step, carry):
        for k in range(8):
            i = step * 8 + k
            gradient = share_ref[:, i, :]
            spread = spread_ref[pl.ds(i, 1), :]
            cross = jnp.sum(gradient * bias_ref[:, i, :], axis=0, keepdims=True) / channels
            slope = spread * spread * cross
            high, low = two_terms(gradient * spread)
            left = jnp.concatenate(
                [
                    high, low, high,
                    rows_of_two(jnp.broadcast_to(slope * mean_ref[pl.ds(i, 1), :], row.shape)),
                    rows_of_two(jnp.broadcast_to(slope, row.shape)),
                ],
                axis=0,
            )
            terms = f32_dot(left, right, TN)
            entries = pair_ref[i].astype(jnp.float32)
            out_ref[i] = (terms[:, :channels] - terms[:, channels:] * entries).astype(jnp.bfloat16)
        return carry

    lax.fori_loop(0, pair_ref.shape[0] // 8, rows, 0)


def output_kernel(parts_ref, combined_ref, out_weight_ref, pair_weight_ref):
    width = combined_ref.shape[0]
    rows = parts_ref.shape[1]
    for h in range(parts_ref.shape[0]):
        block = slice(h * rows, (h + 1) * rows)
        part = parts_ref[h].astype(jnp.float32)
        combined_ref[block, :] = part[:, : 4 * width]
        out_weight_ref[block, :] = part[:, 4 * width : 5 * width]
        share = part[: pair_weight_ref.shape[0], 5 * width :]
        pair_weight_ref[...] = share if h == 0 else pair_weight_ref[...] + share


def call(kernel, outs, *args, scratch=(), place=None, flops=0, after=(), outside=0, late=0):
    whole, anywhere = pl.BlockSpec(memory_space=pltpu.VMEM), pl.BlockSpec(memory_space=pl.ANY)
    specs = [anywhere] * outside + [whole] * (len(args) - outside)
    ahead = () if place is None else (place,)
    shapes = [jax.ShapeDtypeStruct(*o) for o in outs]
    moved = sum(math.prod(a.shape) * a.dtype.itemsize for a in list(args) + shapes)
    first = len(ahead) + len(args)
    last = first + len(after)

    def wrapped(*refs):
        given, rest = list(refs[:first]), refs[last:]
        if outside:
            *rest, arrived = rest
            held = rest[len(rest) - outside :]
            rest = rest[: len(rest) - outside]
            copies = []
            for k in range(outside):
                copies.append(
                    pltpu.make_async_copy(given[len(ahead) + k], held[k], arrived.at[k])
                )
                given[len(ahead) + k] = held[k]
            for copy in copies:
                copy.start()
            for copy in copies[: outside - late]:
                copy.wait()
            if late:
                given.insert(0, lambda: [copy.wait() for copy in copies[outside - late :]])
        kernel(*given, *rest)

    held = [pltpu.VMEM(a.shape, a.dtype) for a in args[:outside]]
    if outside:
        held.append(pltpu.SemaphoreType.DMA((outside,)))
    return pl.pallas_call(
        wrapped,
        out_shape=shapes,
        in_specs=[pl.BlockSpec(memory_space=pltpu.SMEM)] * len(ahead)
        + specs
        + [anywhere] * len(after),
        out_specs=[whole] * len(shapes),
        scratch_shapes=[*scratch, *held],
        compiler_params=pltpu.CompilerParams(
            vmem_limit_bytes=ARGUMENT_VMEM_LIMIT if outside else VMEM_LIMIT
        ),
        cost_estimate=pl.CostEstimate(flops=flops, bytes_accessed=moved, transcendentals=0),
    )(*ahead, *args, *after)


def swapped(mine, axis_name, distance):
    size = lax.axis_size(axis_name)
    return lax.ppermute(mine, axis_name, [(a, a ^ distance) for a in range(size)])


def fits_heads(alignment_rows, pair_entries, pair_weight):
    channels, heads = pair_weight.shape
    return (
        lax.axis_size("seq") == 4
        and lax.axis_size("res") == heads == 8
        and alignment_rows.shape[0] == 2 * SLOTS
        and alignment_rows.shape[1] == pair_entries.shape[0] == 64
        and alignment_rows.shape[2] == 2 * LANES
        and pair_entries.shape[1] == channels == LANES
    )


def head_body(
    alignment_rows, pair_entries, combined_weight, output_weight, pair_weight, updated_gradient
):
    sequences, residues, width = alignment_rows.shape
    channels, heads = pair_weight.shape
    tokens = sequences * residues
    seq_size, res_size = lax.axis_size("seq"), lax.axis_size("res")
    seq_half = seq_size // 2
    total = residues * res_size
    group = 2 * res_size
    groups = [[g * group + k for k in range(group)] for g in range(seq_half)]
    scale = 1.0 / math.sqrt(width // heads * sequences * seq_size)
    res_index, seq_index = lax.axis_index("res"), lax.axis_index("seq")
    place = jnp.stack([res_index % 2, seq_index // 2, res_index // 2]).astype(jnp.int32)
    bf16, f32 = jnp.bfloat16, jnp.float32

    def across(blocks):
        return lax.all_to_all(blocks, ("seq", "res"), 0, 0, axis_index_groups=groups, tiled=True)

    x, grad, wc, wo = alignment_rows, updated_gradient, combined_weight, output_weight
    (query_blocks,) = call(
        functools.partial(query_kernel, scale), [((group, 2 * residues, LANES), bf16)], x, wc,
        flops=8 * tokens * width * width, outside=2,
    )
    query_blocks = across(query_blocks)
    value_blocks, bias, mean, spread = call(
        value_kernel,
        [
            ((group, 3 * residues, LANES), bf16),
            ((heads, residues, LANES), f32),
            ((residues, LANES), f32),
            ((residues, LANES), f32),
        ],
        x, grad, wc, wo, pair_entries, pair_weight.T,
        flops=8 * tokens * width * width, outside=5, late=1,
    )
    query_blocks, value_blocks = lax.optimization_barrier((query_blocks, value_blocks))
    value_blocks = across(value_blocks)

    quarter, half_rows = (total // 4, total), (total // 2, total)
    logit_mine, logit_sent = call(
        functools.partial(score_kernel, residues, 0, residues),
        [(quarter, f32), (quarter, f32)],
        query_blocks, swapped(query_blocks, "res", 1),
        place=place, flops=2 * total * total * width,
    )
    logit_other = swapped(logit_sent, "seq", seq_half)
    value_blocks, logit_other = lax.optimization_barrier((value_blocks, logit_other))
    bias_half = ((group // 2, residues, LANES), bf16)
    bias_mine, bias_sent = call(
        functools.partial(bias_kernel, 2 * residues), [bias_half, bias_half], value_blocks,
        place=place,
    )
    bias_other = swapped(bias_sent, "seq", seq_half)
    grad_full, grad_sent = call(
        functools.partial(grad_score_kernel, residues, residues, 0),
        [(half_rows, f32), (half_rows, bf16)],
        value_blocks, swapped(value_blocks, "res", 1),
        place=place, flops=2 * total * total * width,
    )
    grad_other = swapped(grad_sent, "seq", seq_half)
    bias_other, grad_full = lax.optimization_barrier((bias_other, grad_full))
    softmax_out, probs = call(
        softmax_kernel, [(quarter, f32), (quarter, bf16)],
        logit_mine, logit_other, bias_mine, bias_other,
        place=place, flops=total * total,
    )

    def products(mine, far, blocks, first_row, second_row, with_share, factor):
        rows = 2 * residues + (residues // 2 if with_share else 0)
        (out,) = call(
            functools.partial(
                product_kernel, residues, factor, first_row, second_row, with_share
            ),
            [((group, rows, LANES), bf16)],
            mine, far, swapped(mine, "res", 1), swapped(far, "res", 1), blocks,
            scratch=[pltpu.VMEM((total, total), bf16)],
            place=place, flops=4 * total * total * width,
        )
        return out

    probs_far = swapped(probs, "seq", seq_half)
    attended = products(probs, probs_far, value_blocks, 0, residues, False, 1.0)
    attended_blocks = across(attended)
    softmax_out = lax.optimization_barrier((attended, softmax_out))[1]
    grad_logits, grad_far = call(
        softmax_gradient_kernel, [(quarter, bf16), (quarter, bf16)],
        softmax_out, probs_far, grad_full, grad_other,
        place=place, flops=total * total,
    )
    grad_sums = products(grad_logits, grad_far, query_blocks, residues, 0, True, scale)
    grad_sums, attended_blocks = lax.optimization_barrier((grad_sums, attended_blocks))
    grad_blocks = across(grad_sums)

    updated, value_gate, normed, attended_sums = call(
        attended_weight_kernel,
        [
            (x.shape, bf16),
            ((tokens, 2 * width), bf16),
            ((tokens, width), bf16),
            ((width, 3 * width), bf16),
        ],
        x, grad, wc, wo, attended_blocks,
        flops=14 * tokens * width * width, outside=4,
    )
    share = pltpu.VMEM((heads, residues, LANES), f32)
    columns = 5 * width
    rows = width // res_size
    part_rows = ((res_size // 2, rows, columns), bf16)
    (pair_weight_part,) = call(
        pair_weight_kernel, [((heads, channels), f32)],
        grad_blocks, pair_entries, mean, spread,
        scratch=[share], flops=4 * tokens * width * width,
    )
    query_key, keep, send = call(
        query_weight_kernel,
        [((tokens, 2 * width), bf16), part_rows, part_rows],
        normed, attended_sums, grad_blocks,
        scratch=[pltpu.VMEM((width, columns), bf16)],
        place=place, flops=4 * tokens * width * width, after=(pair_weight_part,),
    )
    own, *sent = call(
        core_sum_kernel,
        [((rows, columns), f32)] + [((rows, columns), bf16)] * 3,
        keep, swapped(send, "res", 1), place=place,
    )
    received = [swapped(t, "res", 2 * flip) for flip, t in enumerate(sent, 1)]
    (pair_gradient,) = call(
        functools.partial(pair_kernel, 2 * residues),
        [(pair_entries.shape, bf16)],
        grad_blocks, pair_entries, pair_weight.T, bias, mean, spread,
        scratch=[share], flops=8 * tokens * width * width,
    )
    (alignment_gradient,) = call(
        alignment_kernel, [(x.shape, bf16)], x, wc, query_key, value_gate,
        flops=8 * tokens * width * width,
    )
    received, alignment_gradient = lax.optimization_barrier((received, alignment_gradient))
    (part,) = call(
        plane_sum_kernel, [((rows, columns + channels), bf16)], own, pair_weight_part, *received
    )
    def added(mine, other):
        return (mine.astype(f32) + other.astype(f32)).astype(bf16)

    other_plane = swapped(part, "seq", 1)
    part = added(part, other_plane)
    other_half = swapped(part, "seq", seq_half)
    other_half, pair_gradient = lax.optimization_barrier((other_half, pair_gradient))
    part = added(part, other_half)
    combined_gradient, output_gradient, pair_weight_gradient = call(
        output_kernel,
        [(wc.shape, f32), (wo.shape, f32), ((heads, channels), f32)],
        lax.all_gather(part, "res", axis=0),
    )
    return (
        updated,
        alignment_gradient,
        pair_gradient,
        combined_gradient,
        output_gradient,
        pair_weight_gradient.T,
    )


def body(alignment_rows, pair_entries, combined_weight, output_weight, pair_weight, updated_gradient):
    chosen = head_body if fits_heads(alignment_rows, pair_entries, pair_weight) else gathered_body
    return chosen(
        alignment_rows, pair_entries, combined_weight, output_weight, pair_weight, updated_gradient
    )


def solution(mesh):
    return jax.shard_map(
        body,
        mesh=mesh,
        in_specs=(
            P("seq", "res", None),
            P("res", "seq", None),
            P(),
            P(),
            P(),
            P("seq", "res", None),
        ),
        out_specs=(
            P("seq", "res", None),
            P("seq", "res", None),
            P("res", "seq", None),
            P(),
            P(),
            P(),
        ),
        check_vma=False,
    )
```

```python
import functools
import math

import jax
import jax.numpy as jnp
from jax import lax
from jax.experimental import pallas as pl
from jax.experimental.pallas import tpu as pltpu
from jax.sharding import PartitionSpec as P

eps_norm = 1e-05


def layer_normalize(values):
    values = values.astype(jnp.float32)
    center = values - jnp.mean(values, axis=-1, keepdims=True)
    broadcast_pair = lax.rsqrt(jnp.mean(center * center, axis=-1, keepdims=True) + eps_norm)
    return (center * broadcast_pair, broadcast_pair)


def layer_norm_backward(normalized_gradient, normalized_rows, broadcast_pair):
    mean_grad = jnp.mean(normalized_gradient, axis=-1, keepdims=True)
    mean_cross = jnp.mean(normalized_gradient * normalized_rows, axis=-1, keepdims=True)
    return broadcast_pair * (normalized_gradient - mean_grad - normalized_rows * mean_cross)


def split_heads(tensor, head_count):
    return tensor.reshape(
        tensor.shape[0], tensor.shape[1], head_count, tensor.shape[2] // head_count
    )


def merge_heads(tensor):
    return tensor.reshape(tensor.shape[0], tensor.shape[1], tensor.shape[2] * tensor.shape[3])


def gathered_body(
    alignment_rows, pair_entries, combined_weight, output_weight, pair_weight, updated_gradient
):
    sequence_count, residue_count, alignment_width = alignment_rows.shape
    head_count = pair_weight.shape[1]
    query_width = output_weight.shape[0]
    head_dim = query_width // head_count
    column_count = pair_entries.shape[1]
    token_count = sequence_count * residue_count
    score_scale = 1.0 / math.sqrt(head_dim * sequence_count * lax.axis_size("seq"))
    normalized_rows, broadcast_pair = layer_normalize(alignment_rows)
    normalized_rows_backward = normalized_rows.astype(jnp.bfloat16).reshape(
        token_count, alignment_width
    )
    projected = jnp.dot(
        normalized_rows_backward, combined_weight, preferred_element_type=jnp.float32
    ).reshape(sequence_count, residue_count, 4 * query_width)
    queries = (projected[..., :query_width] * score_scale).astype(jnp.bfloat16)
    key_rows = projected[..., query_width : 2 * query_width].astype(jnp.bfloat16)
    value_rows = projected[..., 2 * query_width : 3 * query_width].astype(jnp.bfloat16)
    gate_open = jax.nn.sigmoid(projected[..., 3 * query_width :])
    all_keys, all_values = (
        lax.all_gather(key_rows, "res", axis=1, tiled=True),
        lax.all_gather(value_rows, "res", axis=1, tiled=True),
    )
    query_heads = split_heads(queries, head_count)
    key_heads = split_heads(all_keys, head_count)
    value_heads = split_heads(all_values, head_count)
    score_terms = jnp.einsum(
        "sihd,sjhd->hij", query_heads, key_heads, preferred_element_type=jnp.float32
    )
    pair_normed, pair_spread = layer_normalize(pair_entries)
    pair_bias = jnp.einsum("ijc,ch->hij", pair_normed, pair_weight, precision=lax.Precision.HIGHEST)
    col_start = lax.axis_index("seq") * column_count
    own_block = lax.dynamic_slice_in_dim(score_terms, col_start, column_count, 2) + pair_bias
    logits = lax.psum(lax.dynamic_update_slice_in_dim(score_terms, own_block, col_start, 2), "seq")
    row_top = jnp.max(logits, axis=-1, keepdims=True)
    lifted = jnp.exp(logits - row_top)
    softmax_out = lifted / jnp.sum(lifted, axis=-1, keepdims=True)
    softmax_low = softmax_out.astype(jnp.bfloat16)
    attended = merge_heads(
        jnp.einsum("hij,sjhd->sihd", softmax_low, value_heads, preferred_element_type=jnp.float32)
    )
    gated_out = (gate_open * attended).astype(jnp.bfloat16)
    flattened_gated = gated_out.reshape(token_count, query_width)
    updated = (
        jnp.dot(flattened_gated, output_weight, preferred_element_type=jnp.float32)
        .astype(jnp.bfloat16)
        .reshape(sequence_count, residue_count, alignment_width)
    )
    flattened_gradient = updated_gradient.reshape(token_count, alignment_width)
    grad_gated = jnp.dot(
        flattened_gradient, output_weight.T, preferred_element_type=jnp.float32
    ).reshape(sequence_count, residue_count, query_width)
    out_local = jnp.dot(flattened_gated.T, flattened_gradient, preferred_element_type=jnp.float32)
    grad_attended = (grad_gated * gate_open).astype(jnp.bfloat16)
    grad_gate_logit = grad_gated * attended * gate_open * (1.0 - gate_open)
    attended_grad_heads = split_heads(grad_attended, head_count)
    grad_terms = jnp.einsum(
        "sihd,sjhd->hij", attended_grad_heads, value_heads, preferred_element_type=jnp.float32
    )
    grad_probs = lax.psum(grad_terms, "seq")
    row_dot = jnp.sum(softmax_out * grad_probs, axis=-1, keepdims=True)
    grad_logits = softmax_out * (grad_probs - row_dot)
    grad_logits_b = grad_logits.astype(jnp.bfloat16)
    logit_share = lax.dynamic_slice_in_dim(grad_logits, col_start, column_count, 2)
    grad_query_heads = (
        jnp.einsum("hij,sjhd->sihd", grad_logits_b, key_heads, preferred_element_type=jnp.float32)
        * score_scale
    )
    key_part = jnp.einsum(
        "hij,sihd->jshd", grad_logits_b, query_heads, preferred_element_type=jnp.float32
    )
    value_part = jnp.einsum(
        "hij,sihd->jshd", softmax_low, attended_grad_heads, preferred_element_type=jnp.float32
    )
    summed = lax.psum_scatter(
        jnp.concatenate([merge_heads(key_part), merge_heads(value_part)], axis=-1),
        "res",
        scatter_dimension=0,
        tiled=True,
    )
    key_value_grads = jnp.transpose(summed, (1, 0, 2))
    projected_gradient = jnp.concatenate(
        [merge_heads(grad_query_heads), key_value_grads, grad_gate_logit], axis=-1
    )
    projected_gradient = projected_gradient.astype(jnp.bfloat16).reshape(
        token_count, 4 * query_width
    )
    qkvg_local = jnp.dot(
        normalized_rows_backward.T, projected_gradient, preferred_element_type=jnp.float32
    )
    normalized_gradient = jnp.dot(
        projected_gradient, combined_weight.T, preferred_element_type=jnp.float32
    ).reshape(sequence_count, residue_count, alignment_width)
    alignment_gradient = layer_norm_backward(
        normalized_gradient, normalized_rows, broadcast_pair
    ).astype(jnp.bfloat16)
    pair_w_local = jnp.einsum(
        "ijc,hij->ch", pair_normed, logit_share, precision=lax.Precision.HIGHEST
    )
    grad_pair_normed = jnp.einsum(
        "hij,ch->ijc", logit_share, pair_weight, precision=lax.Precision.HIGHEST
    )
    pair_gradient = layer_norm_backward(grad_pair_normed, pair_normed, pair_spread).astype(
        jnp.bfloat16
    )
    combined_weight_gradient, output_weight_gradient, pair_weight_gradient = lax.psum(
        (qkvg_local, out_local, pair_w_local), ("seq", "res")
    )
    return (
        updated,
        alignment_gradient,
        pair_gradient,
        combined_weight_gradient,
        output_weight_gradient,
        pair_weight_gradient,
    )


VMEM_LIMIT = 20 * 1024 * 1024
ARGUMENT_VMEM_LIMIT = 56 * 1024 * 1024
LANES = 128
SLOTS = 4
NT = (((1,), (1,)), ((), ()))
TN = (((0,), (0,)), ((), ()))


def f32_dot(left, right, dims=None):
    if dims is None:
        return jnp.dot(left, right, preferred_element_type=jnp.float32)
    return lax.dot_general(left, right, dims, preferred_element_type=jnp.float32)


def two_terms(values):
    high = values.astype(jnp.bfloat16)
    return high, (values - high.astype(jnp.float32)).astype(jnp.bfloat16)


def slot_select(pieces):
    slot = lax.broadcasted_iota(jnp.int32, pieces[0].shape, 1) // (LANES // SLOTS)
    result = pieces[0]
    for k in range(1, SLOTS):
        result = jnp.where(slot == k, pieces[k], result)
    return result


def pack_heads(out_ref, row, tensor, residues):
    for core in range(2):
        for tile in range(tensor.shape[1] // LANES):
            rolled = []
            for s in range(SLOTS):
                start = (core * SLOTS + s) * residues
                piece = tensor[start : start + residues, tile * LANES : (tile + 1) * LANES]
                rolled.append(pltpu.roll(piece, s * LANES // SLOTS, 1) if s else piece)
            for j in range(SLOTS):
                block = slot_select([rolled[(k - j) % SLOTS] for k in range(SLOTS)])
                out_ref[(tile * SLOTS + j) * 2 + core, row : row + residues, :] = block.astype(
                    jnp.bfloat16
                )


def unpack_heads(in_ref, row, residues, tiles):
    rows = []
    for core in range(2):
        for s in range(SLOTS):
            pieces = []
            for tile in range(tiles):
                blocks = [
                    in_ref[
                        (tile * SLOTS + (k - s) % SLOTS) * 2 + core, row : row + residues, :
                    ].astype(jnp.float32)
                    for k in range(SLOTS)
                ]
                block = slot_select(blocks)
                pieces.append(pltpu.roll(block, LANES - s * LANES // SLOTS, 1) if s else block)
            rows.append(jnp.concatenate(pieces, axis=1))
    return jnp.concatenate(rows, axis=0)


def normalized(x_ref):
    width = x_ref.shape[-1]
    values = x_ref[...].reshape(-1, width).astype(jnp.float32)
    return layer_normalize(values)


def gate_of(logits):
    return 1.0 / (1.0 + jnp.exp(-logits))


def value_kernel(x_ref, grad_ref, wc_ref, wo_ref, out_ref):
    residues, width = x_ref.shape[1], x_ref.shape[2]
    normed = normalized(x_ref)[0].astype(jnp.bfloat16)
    values = f32_dot(normed, wc_ref[:, 2 * width : 3 * width])
    gate = gate_of(f32_dot(normed, wc_ref[:, 3 * width :]))
    grad_gated = f32_dot(grad_ref[...].reshape(-1, width), wo_ref[...], NT)
    pack_heads(out_ref, 0, values, residues)
    pack_heads(out_ref, residues, grad_gated * gate, residues)


def centred(weight):
    return weight - jnp.mean(weight, axis=1, keepdims=True)


def query_kernel(
    scale, arrive, x_ref, wc_ref, pair_ref, weight_ref, out_ref, bias_ref, mean_ref, spread_ref
):
    residues, width = x_ref.shape[1], x_ref.shape[2]
    heads = weight_ref.shape[0]
    normed = normalized(x_ref)[0].astype(jnp.bfloat16)
    pack_heads(out_ref, 0, f32_dot(normed, wc_ref[:, :width]) * scale, residues)
    pack_heads(out_ref, residues, f32_dot(normed, wc_ref[:, width : 2 * width]), residues)

    arrive()
    columns, channels = pair_ref.shape[1], pair_ref.shape[2]
    weight = centred(weight_ref[...])
    first = weight.astype(jnp.bfloat16)
    second, third = two_terms(weight - first.astype(jnp.float32))
    share = jnp.full((heads, channels), 1.0 / channels, jnp.bfloat16)
    left = jnp.concatenate([first, second, third, share], axis=0)
    average = jnp.full((channels, channels), 1.0 / channels, jnp.bfloat16)
    step_rows = 64

    def rows(step, carry):
        start = pl.multiple_of(step * step_rows, step_rows)
        entries = pair_ref[pl.ds(start, step_rows)].reshape(step_rows * columns, channels)
        center = entries.astype(jnp.float32) - f32_dot(entries, average)
        high, low = two_terms(center * center)
        variance = f32_dot(share, high, NT) + f32_dot(share, low, NT)
        spread = lax.rsqrt(variance + eps_norm)
        raw = f32_dot(left, entries, NT)
        bias = spread * (raw[:heads] + raw[heads : 2 * heads] + raw[2 * heads : 3 * heads])
        for k in range(step_rows):
            lanes = slice(k * columns, (k + 1) * columns)
            bias_ref[:, start + k, :] = bias[:, lanes]
            mean_ref[pl.ds(start + k, 1), :] = raw[3 * heads : 3 * heads + 1, lanes]
            spread_ref[pl.ds(start + k, 1), :] = spread[:1, lanes]
        return carry

    lax.fori_loop(0, pair_ref.shape[0] // step_rows, rows, 0)
    half = residues // 2
    for h in range(heads):
        for core in range(2):
            high, low = two_terms(bias_ref[h, core * half : (core + 1) * half, :])
            out_ref[h * 2 + core, 2 * residues : 2 * residues + half, :] = high
            out_ref[h * 2 + core, 2 * residues + half : 3 * residues, :] = low


def lanes_of(blocks_ref, row, residues):
    count = blocks_ref.shape[0] // 2
    planes = [
        blocks_ref[p * count : (p + 1) * count, row : row + residues, :].reshape(-1, LANES)
        for p in range(2)
    ]
    return jnp.concatenate(planes, axis=1)


def score_kernel(
    residues, left_row, right_row, with_bias, place_ref, own_ref, other_ref, mine_ref, sent_ref
):
    core, half = place_ref[0], place_ref[1]
    count = own_ref.shape[0] // 2
    part = residues // 2
    right = jnp.concatenate(
        [lanes_of(own_ref, right_row, residues), lanes_of(other_ref, right_row, residues)], axis=1
    )
    for which, ref in ((half, mine_ref), (1 - half, sent_ref)):
        left = []
        for k in range(count // 2):
            block = which * (count // 2) + k
            rows = pl.ds(pl.multiple_of(left_row + core * part, part), part)
            left.append(
                jnp.concatenate(
                    [
                        r[p * count + block, rows, :]
                        for r in (own_ref, other_ref)
                        for p in range(2)
                    ],
                    axis=1,
                )
            )
        ref[...] = f32_dot(jnp.concatenate(left, axis=0), right, NT).astype(ref.dtype)
        if with_bias:
            for p in range(2):
                columns = pl.ds(pl.multiple_of((half * 2 + p) * LANES, LANES), LANES)
                for k in range(count // 2):
                    block = p * count + which * (count // 2) + k
                    high = own_ref[block, 2 * residues : 2 * residues + part, :]
                    low = own_ref[block, 2 * residues + part : 3 * residues, :]
                    bias = high.astype(jnp.float32) + low.astype(jnp.float32)
                    ref[k * part : (k + 1) * part, columns] += bias


def softmax_kernel(logit_ref, other_ref, out_ref, low_ref):
    logits = logit_ref[...] + other_ref[...]
    lifted = jnp.exp(logits - jnp.max(logits, axis=-1, keepdims=True))
    softmax_out = lifted / jnp.sum(lifted, axis=-1, keepdims=True)
    out_ref[...] = softmax_out
    low_ref[...] = softmax_out.astype(jnp.bfloat16)


def grad_score_kernel(
    residues, left_row, right_row, place_ref, own_ref, other_ref, full_ref, sent_ref
):
    core = place_ref[0]
    count = own_ref.shape[0] // 2
    part = residues // 2
    right = jnp.concatenate(
        [lanes_of(own_ref, right_row, residues), lanes_of(other_ref, right_row, residues)], axis=1
    )
    rows = pl.ds(pl.multiple_of(left_row + core * part, part), part)
    left = [
        jnp.concatenate(
            [r[p * count + k, rows, :] for r in (own_ref, other_ref) for p in range(2)], axis=1
        )
        for k in range(count)
    ]
    terms = f32_dot(jnp.concatenate(left, axis=0), right, NT)
    full_ref[...] = terms
    sent_ref[...] = terms.astype(jnp.bfloat16)


def softmax_gradient_kernel(
    place_ref, softmax_ref, far_ref, grad_ref, other_ref, out_ref, out_far_ref
):
    half = place_ref[1]
    count = softmax_ref.shape[0]
    for which, probs, ref in ((half, softmax_ref, out_ref), (1 - half, far_ref, out_far_ref)):
        rows = pl.ds(pl.multiple_of(which * count, count), count)
        softmax_out = probs[...].astype(jnp.float32)
        grad_probs = grad_ref[rows, :] + other_ref[rows, :].astype(jnp.float32)
        row_dot = jnp.sum(softmax_out * grad_probs, axis=-1, keepdims=True)
        ref[...] = (softmax_out * (grad_probs - row_dot)).astype(jnp.bfloat16)


def product_kernel(
    residues, scale, first_row, second_row, with_share,
    place_ref, own_ref, far_ref, near_ref, corner_ref, blocks_ref, out_ref, whole_ref,
):
    core, half = place_ref[0], place_ref[1]
    count = blocks_ref.shape[0] // 2
    part = residues // 2
    quarters = (
        (own_ref, core, half), (far_ref, core, 1 - half),
        (near_ref, 1 - core, half), (corner_ref, 1 - core, 1 - half),
    )
    for ref, c, z in quarters:
        for k in range(count // 2):
            start = (z * (count // 2) + k) * residues + c * part
            whole_ref[pl.ds(pl.multiple_of(start, part), part), :] = ref[k * part : (k + 1) * part, :]
    whole = whole_ref[...]
    if with_share:
        for p in range(2):
            columns = pl.ds(pl.multiple_of((half * 2 + p) * LANES, LANES), LANES)
            for q in range(count):
                rows = pl.ds(pl.multiple_of(q * residues + core * part, part), part)
                out_ref[p * count + q, 2 * residues : 2 * residues + part, :] = whole_ref[rows, columns]
    first = f32_dot(whole, lanes_of(blocks_ref, first_row, residues)) * scale
    second = f32_dot(whole, lanes_of(blocks_ref, second_row, residues), TN)
    for row, product in ((0, first), (residues, second)):
        for p in range(2):
            out_ref[p * count : (p + 1) * count, row : row + residues, :] = (
                product[:, p * LANES : (p + 1) * LANES]
                .astype(jnp.bfloat16)
                .reshape(count, residues, LANES)
            )


def share_of(blocks_ref, row, part, heads):
    return jnp.concatenate(
        [
            blocks_ref[:, row : row + part, :]
            .astype(jnp.float32)
            .reshape(heads, 2 * part, LANES)
        ],
        axis=0,
    )


def attended_weight_kernel(
    x_ref, grad_ref, wc_ref, wo_ref, blocks_ref, updated_ref, projected_ref, normed_ref, sums_ref
):
    residues, width = x_ref.shape[1], x_ref.shape[2]
    tiles = width // LANES
    normed = normalized(x_ref)[0].astype(jnp.bfloat16)
    normed_ref[...] = normed
    gate = gate_of(f32_dot(normed, wc_ref[:, 3 * width :]))
    grad = grad_ref[...].reshape(-1, width)
    grad_gated = f32_dot(grad, wo_ref[...], NT)
    attended = unpack_heads(blocks_ref, 0, residues, tiles)
    gated = (gate * attended).astype(jnp.bfloat16)
    updated_ref[...] = f32_dot(gated, wo_ref[...]).astype(jnp.bfloat16).reshape(updated_ref.shape)
    projected_ref[:, :width] = unpack_heads(blocks_ref, residues, residues, tiles).astype(
        jnp.bfloat16
    )
    projected_ref[:, width:] = (grad_gated * attended * gate * (1.0 - gate)).astype(jnp.bfloat16)
    sums_ref[:, : 2 * width] = f32_dot(normed, projected_ref[...], TN).astype(jnp.bfloat16)
    sums_ref[:, 2 * width :] = f32_dot(gated, grad, TN).astype(jnp.bfloat16)


def query_weight_kernel(
    place_ref, normed_ref, attended_sums_ref, blocks_ref,
    projected_ref, keep_ref, send_ref, sums_ref,
):
    width = normed_ref.shape[1]
    tiles, residues = width // LANES, (blocks_ref.shape[1] * 2) // 5
    core = place_ref[0]
    for t in range(2):
        projected_ref[:, t * width : (t + 1) * width] = unpack_heads(
            blocks_ref, t * residues, residues, tiles
        ).astype(jnp.bfloat16)
    sums_ref[:, : 2 * width] = f32_dot(normed_ref[...], projected_ref[...], TN).astype(
        jnp.bfloat16
    )
    sums_ref[:, 2 * width :] = attended_sums_ref[...]
    rows = keep_ref.shape[1]
    for which, ref in ((core, keep_ref), (1 - core, send_ref)):
        for block in range(keep_ref.shape[0]):
            start = pl.multiple_of((2 * block + which) * rows, rows)
            ref[block] = sums_ref[pl.ds(start, rows), :]


def core_sum_kernel(place_ref, keep_ref, other_ref, own_ref, *send_refs):
    chip = place_ref[2]
    for flip, ref in enumerate((own_ref, *send_refs)):
        block = jnp.bitwise_xor(chip, flip)
        total = keep_ref[block].astype(jnp.float32) + other_ref[block].astype(jnp.float32)
        ref[...] = total.astype(ref.dtype)


def plane_sum_kernel(own_ref, pair_weight_ref, *refs):
    *received, out_ref = refs
    total = own_ref[...]
    for ref in received:
        total += ref[...].astype(jnp.float32)
    count = own_ref.shape[1]
    heads = pair_weight_ref.shape[0]
    out_ref[:, :count] = total.astype(out_ref.dtype)
    rest = jnp.zeros((out_ref.shape[0] - heads, out_ref.shape[1] - count), jnp.float32)
    out_ref[:, count:] = jnp.concatenate([pair_weight_ref[...], rest], axis=0).astype(
        out_ref.dtype
    )


def pair_weight_kernel(blocks_ref, pair_ref, mean_ref, spread_ref, out_ref, share_ref):
    heads, part = share_ref.shape[0], pair_ref.shape[0] // 2
    share_ref[...] = share_of(blocks_ref, blocks_ref.shape[1] - part, part, heads)

    def rows(step, carry):
        total, shift = carry
        for k in range(8):
            i = step * 8 + k
            scaled = share_ref[:, i, :] * spread_ref[pl.ds(i, 1), :]
            high, low = two_terms(scaled)
            total += f32_dot(jnp.concatenate([high, low], axis=0), pair_ref[i])
            shift += (high.astype(jnp.float32) + low.astype(jnp.float32)) * mean_ref[pl.ds(i, 1), :]
        return total, shift

    channels = pair_ref.shape[2]
    total, shift = lax.fori_loop(
        0,
        pair_ref.shape[0] // 8,
        rows,
        (jnp.zeros((2 * heads, channels), jnp.float32), jnp.zeros((heads, LANES), jnp.float32)),
    )
    out_ref[...] = total[:heads] + total[heads:] - jnp.sum(shift, axis=1, keepdims=True)


def alignment_kernel(x_ref, wc_ref, query_key_ref, value_gate_ref, out_ref):
    normed, spread = normalized(x_ref)
    width = x_ref.shape[2]
    gradient = f32_dot(query_key_ref[...], wc_ref[:, : 2 * width], NT) + f32_dot(
        value_gate_ref[...], wc_ref[:, 2 * width :], NT
    )
    out_ref[...] = (
        layer_norm_backward(gradient, normed, spread).astype(jnp.bfloat16).reshape(out_ref.shape)
    )


def pair_kernel(blocks_row, blocks_ref, pair_ref, weight_ref, bias_ref, mean_ref, spread_ref, out_ref, share_ref):
    heads, channels = weight_ref.shape
    part = pair_ref.shape[0] // 2
    share_ref[...] = share_of(blocks_ref, blocks_row, part, heads)
    first, second = two_terms(centred(weight_ref[...]))
    zero = jnp.zeros((heads, channels), jnp.bfloat16)
    top = lax.broadcasted_iota(jnp.int32, (heads, channels), 0) < 2
    ones = jnp.where(top, 1.0, 0.0).astype(jnp.bfloat16)
    right = jnp.concatenate(
        [
            jnp.concatenate([first, first, second, ones, zero], axis=0),
            jnp.concatenate([zero, zero, zero, zero, ones], axis=0),
        ],
        axis=1,
    )
    row = lax.broadcasted_iota(jnp.int32, (heads, LANES), 0)

    def rows_of_two(value):
        high, low = two_terms(value)
        high, low = high.astype(jnp.float32), low.astype(jnp.float32)
        return jnp.where(row == 0, high, jnp.where(row == 1, low, 0.0)).astype(jnp.bfloat16)

    def rows(step, carry):
        for k in range(8):
            i = step * 8 + k
            gradient = share_ref[:, i, :]
            spread = spread_ref[pl.ds(i, 1), :]
            cross = jnp.sum(gradient * bias_ref[:, i, :], axis=0, keepdims=True) / channels
            slope = spread * spread * cross
            high, low = two_terms(gradient * spread)
            left = jnp.concatenate(
                [
                    high, low, high,
                    rows_of_two(jnp.broadcast_to(slope * mean_ref[pl.ds(i, 1), :], row.shape)),
                    rows_of_two(jnp.broadcast_to(slope, row.shape)),
                ],
                axis=0,
            )
            terms = f32_dot(left, right, TN)
            entries = pair_ref[i].astype(jnp.float32)
            out_ref[i] = (terms[:, :channels] - terms[:, channels:] * entries).astype(jnp.bfloat16)
        return carry

    lax.fori_loop(0, pair_ref.shape[0] // 8, rows, 0)


def output_kernel(place_ref, *refs):
    *parts, combined_ref, out_weight_ref, pair_weight_ref, shares_ref = refs
    core, chip = place_ref[0], place_ref[2]
    width = combined_ref.shape[0]
    rows = parts[0].shape[0]
    heads = pair_weight_ref.shape[0]
    for k, ref in enumerate(parts):
        owner = jnp.bitwise_xor(chip, k // 2) * 2 + jnp.bitwise_xor(core, k % 2)
        block = pl.ds(pl.multiple_of(owner * rows, rows), rows)
        part = ref[...].astype(jnp.float32)
        combined_ref[block, :] = part[:, : 4 * width]
        out_weight_ref[block, :] = part[:, 4 * width : 5 * width]
        shares_ref[owner] = part[:heads, 5 * width :]
    total = shares_ref[0]
    for k in range(1, len(parts)):
        total += shares_ref[k]
    pair_weight_ref[...] = total


def call(kernel, outs, *args, scratch=(), place=None, flops=0, after=(), outside=0, late=0):
    whole, anywhere = pl.BlockSpec(memory_space=pltpu.VMEM), pl.BlockSpec(memory_space=pl.ANY)
    specs = [anywhere] * outside + [whole] * (len(args) - outside)
    ahead = () if place is None else (place,)
    shapes = [jax.ShapeDtypeStruct(*o) for o in outs]
    moved = sum(math.prod(a.shape) * a.dtype.itemsize for a in list(args) + shapes)
    first = len(ahead) + len(args)
    last = first + len(after)

    def wrapped(*refs):
        given, rest = list(refs[:first]), refs[last:]
        if outside:
            *rest, arrived = rest
            held = rest[len(rest) - outside :]
            rest = rest[: len(rest) - outside]
            copies = []
            for k in range(outside):
                copies.append(
                    pltpu.make_async_copy(given[len(ahead) + k], held[k], arrived.at[k])
                )
                given[len(ahead) + k] = held[k]
            for copy in copies:
                copy.start()
            for copy in copies[: outside - late]:
                copy.wait()
            if late:
                given.insert(0, lambda: [copy.wait() for copy in copies[outside - late :]])
        kernel(*given, *rest)

    held = [pltpu.VMEM(a.shape, a.dtype) for a in args[:outside]]
    if outside:
        held.append(pltpu.SemaphoreType.DMA((outside,)))
    return pl.pallas_call(
        wrapped,
        out_shape=shapes,
        in_specs=[pl.BlockSpec(memory_space=pltpu.SMEM)] * len(ahead)
        + specs
        + [anywhere] * len(after),
        out_specs=[whole] * len(shapes),
        scratch_shapes=[*scratch, *held],
        compiler_params=pltpu.CompilerParams(
            vmem_limit_bytes=ARGUMENT_VMEM_LIMIT if outside else VMEM_LIMIT
        ),
        cost_estimate=pl.CostEstimate(flops=flops, bytes_accessed=moved, transcendentals=0),
    )(*ahead, *args, *after)


def swapped(mine, axis_name, distance):
    size = lax.axis_size(axis_name)
    return lax.ppermute(mine, axis_name, [(a, a ^ distance) for a in range(size)])


def fits_heads(alignment_rows, pair_entries, pair_weight):
    channels, heads = pair_weight.shape
    return (
        lax.axis_size("seq") == 4
        and lax.axis_size("res") == heads == 8
        and alignment_rows.shape[0] == 2 * SLOTS
        and alignment_rows.shape[1] == pair_entries.shape[0] == 64
        and alignment_rows.shape[2] == 2 * LANES
        and pair_entries.shape[1] == channels == LANES
    )


def head_body(
    alignment_rows, pair_entries, combined_weight, output_weight, pair_weight, updated_gradient
):
    sequences, residues, width = alignment_rows.shape
    channels, heads = pair_weight.shape
    tokens = sequences * residues
    seq_size, res_size = lax.axis_size("seq"), lax.axis_size("res")
    seq_half = seq_size // 2
    total = residues * res_size
    group = 2 * res_size
    groups = [[g * group + k for k in range(group)] for g in range(seq_half)]
    scale = 1.0 / math.sqrt(width // heads * sequences * seq_size)
    res_index, seq_index = lax.axis_index("res"), lax.axis_index("seq")
    place = jnp.stack([res_index % 2, seq_index // 2, res_index // 2]).astype(jnp.int32)
    bf16, f32 = jnp.bfloat16, jnp.float32

    def across(blocks):
        return lax.all_to_all(blocks, ("seq", "res"), 0, 0, axis_index_groups=groups, tiled=True)

    x, grad, wc, wo = alignment_rows, updated_gradient, combined_weight, output_weight
    (value_blocks,) = call(
        value_kernel, [((group, 2 * residues, LANES), bf16)], x, grad, wc, wo,
        flops=8 * tokens * width * width, outside=4,
    )
    value_blocks = across(value_blocks)
    query_blocks, bias, mean, spread = call(
        functools.partial(query_kernel, scale),
        [
            ((group, 3 * residues, LANES), bf16),
            ((heads, residues, LANES), f32),
            ((residues, LANES), f32),
            ((residues, LANES), f32),
        ],
        x, wc, pair_entries, pair_weight.T,
        flops=8 * tokens * width * width, outside=3, late=1,
    )
    value_blocks, query_blocks = lax.optimization_barrier((value_blocks, query_blocks))
    query_blocks = across(query_blocks)

    quarter, half_rows = (total // 4, total), (total // 2, total)
    grad_full, grad_sent = call(
        functools.partial(grad_score_kernel, residues, residues, 0),
        [(half_rows, f32), (half_rows, bf16)],
        value_blocks, swapped(value_blocks, "res", 1),
        place=place, flops=2 * total * total * width,
    )
    grad_other = swapped(grad_sent, "seq", seq_half)
    query_blocks, grad_other = lax.optimization_barrier((query_blocks, grad_other))
    logit_mine, logit_sent = call(
        functools.partial(score_kernel, residues, 0, residues, True),
        [(quarter, f32), (quarter, f32)],
        query_blocks, swapped(query_blocks, "res", 1),
        place=place, flops=2 * total * total * width,
    )
    softmax_out, probs = call(
        softmax_kernel, [(quarter, f32), (quarter, bf16)],
        logit_mine, swapped(logit_sent, "seq", seq_half),
        flops=total * total,
    )

    def products(mine, far, blocks, first_row, second_row, with_share, factor):
        rows = 2 * residues + (residues // 2 if with_share else 0)
        (out,) = call(
            functools.partial(
                product_kernel, residues, factor, first_row, second_row, with_share
            ),
            [((group, rows, LANES), bf16)],
            mine, far, swapped(mine, "res", 1), swapped(far, "res", 1), blocks,
            scratch=[pltpu.VMEM((total, total), bf16)],
            place=place, flops=4 * total * total * width,
        )
        return out

    probs_far = swapped(probs, "seq", seq_half)
    attended = products(probs, probs_far, value_blocks, 0, residues, False, 1.0)
    attended_blocks = across(attended)
    softmax_out = lax.optimization_barrier((attended, softmax_out))[1]
    grad_logits, grad_far = call(
        softmax_gradient_kernel, [(quarter, bf16), (quarter, bf16)],
        softmax_out, probs_far, grad_full, grad_other,
        place=place, flops=total * total,
    )
    grad_sums = products(grad_logits, grad_far, query_blocks, residues, 0, True, scale)
    grad_sums, attended_blocks = lax.optimization_barrier((grad_sums, attended_blocks))
    grad_blocks = across(grad_sums)

    updated, value_gate, normed, attended_sums = call(
        attended_weight_kernel,
        [
            (x.shape, bf16),
            ((tokens, 2 * width), bf16),
            ((tokens, width), bf16),
            ((width, 3 * width), bf16),
        ],
        x, grad, wc, wo, attended_blocks,
        flops=14 * tokens * width * width, outside=4,
    )
    share = pltpu.VMEM((heads, residues, LANES), f32)
    columns = 5 * width
    rows = width // res_size
    part_rows = ((res_size // 2, rows, columns), bf16)
    (pair_weight_part,) = call(
        pair_weight_kernel, [((heads, channels), f32)],
        grad_blocks, pair_entries, mean, spread,
        scratch=[share], flops=4 * tokens * width * width,
    )
    query_key, keep, send = call(
        query_weight_kernel,
        [((tokens, 2 * width), bf16), part_rows, part_rows],
        normed, attended_sums, grad_blocks,
        scratch=[pltpu.VMEM((width, columns), bf16)],
        place=place, flops=4 * tokens * width * width, after=(pair_weight_part,),
    )
    own, *sent = call(
        core_sum_kernel,
        [((rows, columns), f32)] + [((rows, columns), bf16)] * 3,
        keep, swapped(send, "res", 1), place=place,
    )
    received = [swapped(t, "res", 2 * flip) for flip, t in enumerate(sent, 1)]
    (pair_gradient,) = call(
        functools.partial(pair_kernel, 2 * residues),
        [(pair_entries.shape, bf16)],
        grad_blocks, pair_entries, pair_weight.T, bias, mean, spread,
        scratch=[share], flops=8 * tokens * width * width,
    )
    (alignment_gradient,) = call(
        alignment_kernel, [(x.shape, bf16)], x, wc, query_key, value_gate,
        flops=8 * tokens * width * width,
    )
    received, alignment_gradient = lax.optimization_barrier((received, alignment_gradient))
    (part,) = call(
        plane_sum_kernel, [((rows, columns + channels), bf16)], own, pair_weight_part, *received
    )
    def added(mine, other):
        return (mine.astype(f32) + other.astype(f32)).astype(bf16)

    other_plane = swapped(part, "seq", 1)
    part = added(part, other_plane)
    other_half = swapped(part, "seq", seq_half)
    other_half, pair_gradient = lax.optimization_barrier((other_half, pair_gradient))
    part = added(part, other_half)
    chips = [part] + [swapped(part, "res", 2 * flip) for flip in range(1, res_size // 2)]
    parts = [t for chip in chips for t in (chip, swapped(chip, "res", 1))]
    combined_gradient, output_gradient, pair_weight_gradient = call(
        output_kernel,
        [(wc.shape, f32), (wo.shape, f32), ((heads, channels), f32)],
        *parts,
        scratch=[pltpu.VMEM((len(parts), heads, channels), f32)],
        place=place,
    )
    return (
        updated,
        alignment_gradient,
        pair_gradient,
        combined_gradient,
        output_gradient,
        pair_weight_gradient.T,
    )


def body(alignment_rows, pair_entries, combined_weight, output_weight, pair_weight, updated_gradient):
    chosen = head_body if fits_heads(alignment_rows, pair_entries, pair_weight) else gathered_body
    return chosen(
        alignment_rows, pair_entries, combined_weight, output_weight, pair_weight, updated_gradient
    )


def solution(mesh):
    return jax.shard_map(
        body,
        mesh=mesh,
        in_specs=(
            P("seq", "res", None),
            P("res", "seq", None),
            P(),
            P(),
            P(),
            P("seq", "res", None),
        ),
        out_specs=(
            P("seq", "res", None),
            P("seq", "res", None),
            P("res", "seq", None),
            P(),
            P(),
            P(),
        ),
        check_vma=False,
    )
```

```python
import functools
import math

import jax
import jax.numpy as jnp
from jax import lax
from jax.experimental import pallas as pl
from jax.experimental.pallas import tpu as pltpu
from jax.sharding import PartitionSpec as P

eps_norm = 1e-05


def layer_normalize(values):
    values = values.astype(jnp.float32)
    center = values - jnp.mean(values, axis=-1, keepdims=True)
    broadcast_pair = lax.rsqrt(jnp.mean(center * center, axis=-1, keepdims=True) + eps_norm)
    return (center * broadcast_pair, broadcast_pair)


def layer_norm_backward(normalized_gradient, normalized_rows, broadcast_pair):
    mean_grad = jnp.mean(normalized_gradient, axis=-1, keepdims=True)
    mean_cross = jnp.mean(normalized_gradient * normalized_rows, axis=-1, keepdims=True)
    return broadcast_pair * (normalized_gradient - mean_grad - normalized_rows * mean_cross)


def split_heads(tensor, head_count):
    return tensor.reshape(
        tensor.shape[0], tensor.shape[1], head_count, tensor.shape[2] // head_count
    )


def merge_heads(tensor):
    return tensor.reshape(tensor.shape[0], tensor.shape[1], tensor.shape[2] * tensor.shape[3])


def gathered_body(
    alignment_rows, pair_entries, combined_weight, output_weight, pair_weight, updated_gradient
):
    sequence_count, residue_count, alignment_width = alignment_rows.shape
    head_count = pair_weight.shape[1]
    query_width = output_weight.shape[0]
    head_dim = query_width // head_count
    column_count = pair_entries.shape[1]
    token_count = sequence_count * residue_count
    score_scale = 1.0 / math.sqrt(head_dim * sequence_count * lax.axis_size("seq"))
    normalized_rows, broadcast_pair = layer_normalize(alignment_rows)
    normalized_rows_backward = normalized_rows.astype(jnp.bfloat16).reshape(
        token_count, alignment_width
    )
    projected = jnp.dot(
        normalized_rows_backward, combined_weight, preferred_element_type=jnp.float32
    ).reshape(sequence_count, residue_count, 4 * query_width)
    queries = (projected[..., :query_width] * score_scale).astype(jnp.bfloat16)
    key_rows = projected[..., query_width : 2 * query_width].astype(jnp.bfloat16)
    value_rows = projected[..., 2 * query_width : 3 * query_width].astype(jnp.bfloat16)
    gate_open = jax.nn.sigmoid(projected[..., 3 * query_width :])
    all_keys, all_values = (
        lax.all_gather(key_rows, "res", axis=1, tiled=True),
        lax.all_gather(value_rows, "res", axis=1, tiled=True),
    )
    query_heads = split_heads(queries, head_count)
    key_heads = split_heads(all_keys, head_count)
    value_heads = split_heads(all_values, head_count)
    score_terms = jnp.einsum(
        "sihd,sjhd->hij", query_heads, key_heads, preferred_element_type=jnp.float32
    )
    pair_normed, pair_spread = layer_normalize(pair_entries)
    pair_bias = jnp.einsum("ijc,ch->hij", pair_normed, pair_weight, precision=lax.Precision.HIGHEST)
    col_start = lax.axis_index("seq") * column_count
    own_block = lax.dynamic_slice_in_dim(score_terms, col_start, column_count, 2) + pair_bias
    logits = lax.psum(lax.dynamic_update_slice_in_dim(score_terms, own_block, col_start, 2), "seq")
    row_top = jnp.max(logits, axis=-1, keepdims=True)
    lifted = jnp.exp(logits - row_top)
    softmax_out = lifted / jnp.sum(lifted, axis=-1, keepdims=True)
    softmax_low = softmax_out.astype(jnp.bfloat16)
    attended = merge_heads(
        jnp.einsum("hij,sjhd->sihd", softmax_low, value_heads, preferred_element_type=jnp.float32)
    )
    gated_out = (gate_open * attended).astype(jnp.bfloat16)
    flattened_gated = gated_out.reshape(token_count, query_width)
    updated = (
        jnp.dot(flattened_gated, output_weight, preferred_element_type=jnp.float32)
        .astype(jnp.bfloat16)
        .reshape(sequence_count, residue_count, alignment_width)
    )
    flattened_gradient = updated_gradient.reshape(token_count, alignment_width)
    grad_gated = jnp.dot(
        flattened_gradient, output_weight.T, preferred_element_type=jnp.float32
    ).reshape(sequence_count, residue_count, query_width)
    out_local = jnp.dot(flattened_gated.T, flattened_gradient, preferred_element_type=jnp.float32)
    grad_attended = (grad_gated * gate_open).astype(jnp.bfloat16)
    grad_gate_logit = grad_gated * attended * gate_open * (1.0 - gate_open)
    attended_grad_heads = split_heads(grad_attended, head_count)
    grad_terms = jnp.einsum(
        "sihd,sjhd->hij", attended_grad_heads, value_heads, preferred_element_type=jnp.float32
    )
    grad_probs = lax.psum(grad_terms, "seq")
    row_dot = jnp.sum(softmax_out * grad_probs, axis=-1, keepdims=True)
    grad_logits = softmax_out * (grad_probs - row_dot)
    grad_logits_b = grad_logits.astype(jnp.bfloat16)
    logit_share = lax.dynamic_slice_in_dim(grad_logits, col_start, column_count, 2)
    grad_query_heads = (
        jnp.einsum("hij,sjhd->sihd", grad_logits_b, key_heads, preferred_element_type=jnp.float32)
        * score_scale
    )
    key_part = jnp.einsum(
        "hij,sihd->jshd", grad_logits_b, query_heads, preferred_element_type=jnp.float32
    )
    value_part = jnp.einsum(
        "hij,sihd->jshd", softmax_low, attended_grad_heads, preferred_element_type=jnp.float32
    )
    summed = lax.psum_scatter(
        jnp.concatenate([merge_heads(key_part), merge_heads(value_part)], axis=-1),
        "res",
        scatter_dimension=0,
        tiled=True,
    )
    key_value_grads = jnp.transpose(summed, (1, 0, 2))
    projected_gradient = jnp.concatenate(
        [merge_heads(grad_query_heads), key_value_grads, grad_gate_logit], axis=-1
    )
    projected_gradient = projected_gradient.astype(jnp.bfloat16).reshape(
        token_count, 4 * query_width
    )
    qkvg_local = jnp.dot(
        normalized_rows_backward.T, projected_gradient, preferred_element_type=jnp.float32
    )
    normalized_gradient = jnp.dot(
        projected_gradient, combined_weight.T, preferred_element_type=jnp.float32
    ).reshape(sequence_count, residue_count, alignment_width)
    alignment_gradient = layer_norm_backward(
        normalized_gradient, normalized_rows, broadcast_pair
    ).astype(jnp.bfloat16)
    pair_w_local = jnp.einsum(
        "ijc,hij->ch", pair_normed, logit_share, precision=lax.Precision.HIGHEST
    )
    grad_pair_normed = jnp.einsum(
        "hij,ch->ijc", logit_share, pair_weight, precision=lax.Precision.HIGHEST
    )
    pair_gradient = layer_norm_backward(grad_pair_normed, pair_normed, pair_spread).astype(
        jnp.bfloat16
    )
    combined_weight_gradient, output_weight_gradient, pair_weight_gradient = lax.psum(
        (qkvg_local, out_local, pair_w_local), ("seq", "res")
    )
    return (
        updated,
        alignment_gradient,
        pair_gradient,
        combined_weight_gradient,
        output_weight_gradient,
        pair_weight_gradient,
    )


VMEM_LIMIT = 20 * 1024 * 1024
ARGUMENT_VMEM_LIMIT = 56 * 1024 * 1024
LANES = 128
SLOTS = 4
NT = (((1,), (1,)), ((), ()))
TN = (((0,), (0,)), ((), ()))


def f32_dot(left, right, dims=None):
    if dims is None:
        return jnp.dot(left, right, preferred_element_type=jnp.float32)
    return lax.dot_general(left, right, dims, preferred_element_type=jnp.float32)


def two_terms(values):
    high = values.astype(jnp.bfloat16)
    return high, (values - high.astype(jnp.float32)).astype(jnp.bfloat16)


def slot_select(pieces):
    slot = lax.broadcasted_iota(jnp.int32, pieces[0].shape, 1) // (LANES // SLOTS)
    result = pieces[0]
    for k in range(1, SLOTS):
        result = jnp.where(slot == k, pieces[k], result)
    return result


def pack_heads(out_ref, row, tensor, residues):
    for core in range(2):
        for tile in range(tensor.shape[1] // LANES):
            rolled = []
            for s in range(SLOTS):
                start = (core * SLOTS + s) * residues
                piece = tensor[start : start + residues, tile * LANES : (tile + 1) * LANES]
                rolled.append(pltpu.roll(piece, s * LANES // SLOTS, 1) if s else piece)
            for j in range(SLOTS):
                block = slot_select([rolled[(k - j) % SLOTS] for k in range(SLOTS)])
                out_ref[(tile * SLOTS + j) * 2 + core, row : row + residues, :] = block.astype(
                    jnp.bfloat16
                )


def unpack_heads(in_ref, row, residues, tiles):
    rows = []
    for core in range(2):
        for s in range(SLOTS):
            pieces = []
            for tile in range(tiles):
                blocks = [
                    in_ref[
                        (tile * SLOTS + (k - s) % SLOTS) * 2 + core, row : row + residues, :
                    ].astype(jnp.float32)
                    for k in range(SLOTS)
                ]
                block = slot_select(blocks)
                pieces.append(pltpu.roll(block, LANES - s * LANES // SLOTS, 1) if s else block)
            rows.append(jnp.concatenate(pieces, axis=1))
    return jnp.concatenate(rows, axis=0)


def normalized(x_ref):
    width = x_ref.shape[-1]
    values = x_ref[...].reshape(-1, width).astype(jnp.float32)
    return layer_normalize(values)


def gate_of(logits):
    return 1.0 / (1.0 + jnp.exp(-logits))


def query_kernel(scale, x_ref, wc_ref, out_ref):
    residues, width = x_ref.shape[1], x_ref.shape[2]
    normed = normalized(x_ref)[0].astype(jnp.bfloat16)
    pack_heads(out_ref, 0, f32_dot(normed, wc_ref[:, :width]) * scale, residues)
    pack_heads(out_ref, residues, f32_dot(normed, wc_ref[:, width : 2 * width]), residues)


def centred(weight):
    return weight - jnp.mean(weight, axis=1, keepdims=True)


def value_kernel(
    arrive, x_ref, grad_ref, wc_ref, wo_ref, pair_ref, weight_ref,
    out_ref, bias_ref, mean_ref, spread_ref,
):
    residues, width = x_ref.shape[1], x_ref.shape[2]
    heads = weight_ref.shape[0]
    normed = normalized(x_ref)[0].astype(jnp.bfloat16)
    values = f32_dot(normed, wc_ref[:, 2 * width : 3 * width])
    gate = gate_of(f32_dot(normed, wc_ref[:, 3 * width :]))
    grad_gated = f32_dot(grad_ref[...].reshape(-1, width), wo_ref[...], NT)
    pack_heads(out_ref, 0, values, residues)
    pack_heads(out_ref, residues, grad_gated * gate, residues)

    arrive()
    columns, channels = pair_ref.shape[1], pair_ref.shape[2]
    weight = centred(weight_ref[...])
    first = weight.astype(jnp.bfloat16)
    second, third = two_terms(weight - first.astype(jnp.float32))
    share = jnp.full((heads, channels), 1.0 / channels, jnp.bfloat16)
    left = jnp.concatenate([first, second, third, share], axis=0)
    average = jnp.full((channels, channels), 1.0 / channels, jnp.bfloat16)
    step_rows = 64

    def rows(step, carry):
        start = pl.multiple_of(step * step_rows, step_rows)
        entries = pair_ref[pl.ds(start, step_rows)].reshape(step_rows * columns, channels)
        center = entries.astype(jnp.float32) - f32_dot(entries, average)
        high, low = two_terms(center * center)
        variance = f32_dot(share, high, NT) + f32_dot(share, low, NT)
        spread = lax.rsqrt(variance + eps_norm)
        raw = f32_dot(left, entries, NT)
        bias = spread * (raw[:heads] + raw[heads : 2 * heads] + raw[2 * heads : 3 * heads])
        for k in range(step_rows):
            lanes = slice(k * columns, (k + 1) * columns)
            bias_ref[:, start + k, :] = bias[:, lanes]
            mean_ref[pl.ds(start + k, 1), :] = raw[3 * heads : 3 * heads + 1, lanes]
            spread_ref[pl.ds(start + k, 1), :] = spread[:1, lanes]
        return carry

    lax.fori_loop(0, pair_ref.shape[0] // step_rows, rows, 0)
    half = residues // 2
    for h in range(heads):
        for core in range(2):
            high, low = two_terms(bias_ref[h, core * half : (core + 1) * half, :])
            out_ref[h * 2 + core, 2 * residues : 2 * residues + half, :] = high
            out_ref[h * 2 + core, 2 * residues + half : 3 * residues, :] = low


def lanes_of(blocks_ref, row, residues):
    count = blocks_ref.shape[0] // 2
    planes = [
        blocks_ref[p * count : (p + 1) * count, row : row + residues, :].reshape(-1, LANES)
        for p in range(2)
    ]
    return jnp.concatenate(planes, axis=1)


def score_kernel(
    residues, left_row, right_row, place_ref, own_ref, other_ref, mine_ref, sent_ref
):
    core, half = place_ref[0], place_ref[1]
    count = own_ref.shape[0] // 2
    part = residues // 2
    right = jnp.concatenate(
        [lanes_of(own_ref, right_row, residues), lanes_of(other_ref, right_row, residues)], axis=1
    )
    for which, ref in ((half, mine_ref), (1 - half, sent_ref)):
        left = []
        for k in range(count // 2):
            block = which * (count // 2) + k
            rows = pl.ds(pl.multiple_of(left_row + core * part, part), part)
            left.append(
                jnp.concatenate(
                    [
                        r[p * count + block, rows, :]
                        for r in (own_ref, other_ref)
                        for p in range(2)
                    ],
                    axis=1,
                )
            )
        ref[...] = f32_dot(jnp.concatenate(left, axis=0), right, NT).astype(ref.dtype)


def bias_kernel(row, place_ref, blocks_ref, mine_ref, sent_ref):
    half = place_ref[1]
    count = blocks_ref.shape[0] // 2
    for which, ref in ((half, mine_ref), (1 - half, sent_ref)):
        for p in range(2):
            for k in range(count // 2):
                block = p * count + which * (count // 2) + k
                ref[p * (count // 2) + k] = blocks_ref[block, row:, :]


def softmax_kernel(
    place_ref, logit_ref, other_ref, bias_ref, bias_other_ref, out_ref, low_ref
):
    half = place_ref[1]
    count, part = bias_ref.shape[0] // 2, bias_ref.shape[1] // 2
    out_ref[...] = logit_ref[...] + other_ref[...]
    for which, ref in ((half, bias_ref), (1 - half, bias_other_ref)):
        for p in range(2):
            columns = pl.ds(pl.multiple_of((which * 2 + p) * LANES, LANES), LANES)
            for k in range(count):
                high = ref[p * count + k, :part, :].astype(jnp.float32)
                low = ref[p * count + k, part:, :].astype(jnp.float32)
                out_ref[k * part : (k + 1) * part, columns] += high + low
    logits = out_ref[...]
    lifted = jnp.exp(logits - jnp.max(logits, axis=-1, keepdims=True))
    softmax_out = lifted / jnp.sum(lifted, axis=-1, keepdims=True)
    out_ref[...] = softmax_out
    low_ref[...] = softmax_out.astype(jnp.bfloat16)


def grad_score_kernel(residues, left_row, right_row, place_ref, own_ref, other_ref, out_ref):
    core = place_ref[0]
    count = own_ref.shape[0] // 2
    part = residues // 2
    right = jnp.concatenate(
        [lanes_of(own_ref, right_row, residues), lanes_of(other_ref, right_row, residues)], axis=1
    )
    rows = pl.ds(pl.multiple_of(left_row + core * part, part), part)
    left = [
        jnp.concatenate(
            [r[p * count + k, rows, :] for r in (own_ref, other_ref) for p in range(2)], axis=1
        )
        for k in range(count)
    ]
    out_ref[...] = f32_dot(jnp.concatenate(left, axis=0), right, NT).astype(jnp.bfloat16)


def softmax_gradient_kernel(place_ref, softmax_ref, far_ref, grad_ref, out_ref, out_far_ref):
    half = place_ref[1]
    count = softmax_ref.shape[0]
    for which, probs, ref in ((half, softmax_ref, out_ref), (1 - half, far_ref, out_far_ref)):
        rows = pl.ds(pl.multiple_of(which * count, count), count)
        softmax_out = probs[...].astype(jnp.float32)
        grad_probs = grad_ref[rows, :].astype(jnp.float32)
        row_dot = jnp.sum(softmax_out * grad_probs, axis=-1, keepdims=True)
        ref[...] = (softmax_out * (grad_probs - row_dot)).astype(jnp.bfloat16)


def product_kernel(
    residues, scale, first_row, second_row, with_share,
    place_ref, own_ref, far_ref, near_ref, corner_ref, blocks_ref, out_ref, whole_ref,
):
    core, half = place_ref[0], place_ref[1]
    count = blocks_ref.shape[0] // 2
    part = residues // 2
    quarters = (
        (own_ref, core, half), (far_ref, core, 1 - half),
        (near_ref, 1 - core, half), (corner_ref, 1 - core, 1 - half),
    )
    for ref, c, z in quarters:
        for k in range(count // 2):
            start = (z * (count // 2) + k) * residues + c * part
            whole_ref[pl.ds(pl.multiple_of(start, part), part), :] = ref[k * part : (k + 1) * part, :]
    whole = whole_ref[...]
    if with_share:
        for p in range(2):
            columns = pl.ds(pl.multiple_of((half * 2 + p) * LANES, LANES), LANES)
            for q in range(count):
                rows = pl.ds(pl.multiple_of(q * residues + core * part, part), part)
                out_ref[p * count + q, 2 * residues : 2 * residues + part, :] = whole_ref[rows, columns]
    first = f32_dot(whole, lanes_of(blocks_ref, first_row, residues)) * scale
    second = f32_dot(whole, lanes_of(blocks_ref, second_row, residues), TN)
    for row, product in ((0, first), (residues, second)):
        for p in range(2):
            out_ref[p * count : (p + 1) * count, row : row + residues, :] = (
                product[:, p * LANES : (p + 1) * LANES]
                .astype(jnp.bfloat16)
                .reshape(count, residues, LANES)
            )


def share_of(blocks_ref, row, part, heads):
    return jnp.concatenate(
        [
            blocks_ref[:, row : row + part, :]
            .astype(jnp.float32)
            .reshape(heads, 2 * part, LANES)
        ],
        axis=0,
    )


def attended_weight_kernel(
    x_ref, grad_ref, wc_ref, wo_ref, blocks_ref, updated_ref, projected_ref, normed_ref, sums_ref
):
    residues, width = x_ref.shape[1], x_ref.shape[2]
    tiles = width // LANES
    normed = normalized(x_ref)[0].astype(jnp.bfloat16)
    normed_ref[...] = normed
    gate = gate_of(f32_dot(normed, wc_ref[:, 3 * width :]))
    grad = grad_ref[...].reshape(-1, width)
    grad_gated = f32_dot(grad, wo_ref[...], NT)
    attended = unpack_heads(blocks_ref, 0, residues, tiles)
    gated = (gate * attended).astype(jnp.bfloat16)
    updated_ref[...] = f32_dot(gated, wo_ref[...]).astype(jnp.bfloat16).reshape(updated_ref.shape)
    projected_ref[:, :width] = unpack_heads(blocks_ref, residues, residues, tiles).astype(
        jnp.bfloat16
    )
    projected_ref[:, width:] = (grad_gated * attended * gate * (1.0 - gate)).astype(jnp.bfloat16)
    sums_ref[:, : 2 * width] = f32_dot(normed, projected_ref[...], TN).astype(jnp.bfloat16)
    sums_ref[:, 2 * width :] = f32_dot(gated, grad, TN).astype(jnp.bfloat16)


def query_weight_kernel(
    place_ref, normed_ref, attended_sums_ref, blocks_ref,
    projected_ref, keep_ref, send_ref, sums_ref,
):
    width = normed_ref.shape[1]
    tiles, residues = width // LANES, (blocks_ref.shape[1] * 2) // 5
    core = place_ref[0]
    for t in range(2):
        projected_ref[:, t * width : (t + 1) * width] = unpack_heads(
            blocks_ref, t * residues, residues, tiles
        ).astype(jnp.bfloat16)
    sums_ref[:, : 2 * width] = f32_dot(normed_ref[...], projected_ref[...], TN).astype(
        jnp.bfloat16
    )
    sums_ref[:, 2 * width :] = attended_sums_ref[...]
    rows = keep_ref.shape[1]
    for which, ref in ((core, keep_ref), (1 - core, send_ref)):
        for block in range(keep_ref.shape[0]):
            start = pl.multiple_of((2 * block + which) * rows, rows)
            ref[block] = sums_ref[pl.ds(start, rows), :]


def core_sum_kernel(place_ref, keep_ref, other_ref, own_ref, *send_refs):
    chip = place_ref[2]
    for flip, ref in enumerate((own_ref, *send_refs)):
        block = jnp.bitwise_xor(chip, flip)
        total = keep_ref[block].astype(jnp.float32) + other_ref[block].astype(jnp.float32)
        ref[...] = total.astype(ref.dtype)


def plane_sum_kernel(own_ref, pair_weight_ref, *refs):
    *received, out_ref = refs
    total = own_ref[...]
    for ref in received:
        total += ref[...].astype(jnp.float32)
    count = own_ref.shape[1]
    heads = pair_weight_ref.shape[0]
    out_ref[:, :count] = total.astype(out_ref.dtype)
    rest = jnp.zeros((out_ref.shape[0] - heads, out_ref.shape[1] - count), jnp.float32)
    out_ref[:, count:] = jnp.concatenate([pair_weight_ref[...], rest], axis=0).astype(
        out_ref.dtype
    )


def pair_weight_kernel(blocks_ref, pair_ref, mean_ref, spread_ref, out_ref, share_ref):
    heads, part = share_ref.shape[0], pair_ref.shape[0] // 2
    share_ref[...] = share_of(blocks_ref, blocks_ref.shape[1] - part, part, heads)

    def rows(step, carry):
        total, shift = carry
        for k in range(8):
            i = step * 8 + k
            scaled = share_ref[:, i, :] * spread_ref[pl.ds(i, 1), :]
            high, low = two_terms(scaled)
            total += f32_dot(jnp.concatenate([high, low], axis=0), pair_ref[i])
            shift += (high.astype(jnp.float32) + low.astype(jnp.float32)) * mean_ref[pl.ds(i, 1), :]
        return total, shift

    channels = pair_ref.shape[2]
    total, shift = lax.fori_loop(
        0,
        pair_ref.shape[0] // 8,
        rows,
        (jnp.zeros((2 * heads, channels), jnp.float32), jnp.zeros((heads, LANES), jnp.float32)),
    )
    out_ref[...] = total[:heads] + total[heads:] - jnp.sum(shift, axis=1, keepdims=True)


def alignment_kernel(x_ref, wc_ref, query_key_ref, value_gate_ref, out_ref):
    normed, spread = normalized(x_ref)
    width = x_ref.shape[2]
    gradient = f32_dot(query_key_ref[...], wc_ref[:, : 2 * width], NT) + f32_dot(
        value_gate_ref[...], wc_ref[:, 2 * width :], NT
    )
    out_ref[...] = (
        layer_norm_backward(gradient, normed, spread).astype(jnp.bfloat16).reshape(out_ref.shape)
    )


def pair_kernel(blocks_row, blocks_ref, pair_ref, weight_ref, bias_ref, mean_ref, spread_ref, out_ref, share_ref):
    heads, channels = weight_ref.shape
    part = pair_ref.shape[0] // 2
    share_ref[...] = share_of(blocks_ref, blocks_row, part, heads)
    first, second = two_terms(centred(weight_ref[...]))
    zero = jnp.zeros((heads, channels), jnp.bfloat16)
    top = lax.broadcasted_iota(jnp.int32, (heads, channels), 0) < 2
    ones = jnp.where(top, 1.0, 0.0).astype(jnp.bfloat16)
    right = jnp.concatenate(
        [
            jnp.concatenate([first, first, second, ones, zero], axis=0),
            jnp.concatenate([zero, zero, zero, zero, ones], axis=0),
        ],
        axis=1,
    )
    row = lax.broadcasted_iota(jnp.int32, (heads, LANES), 0)

    def rows_of_two(value):
        high, low = two_terms(value)
        high, low = high.astype(jnp.float32), low.astype(jnp.float32)
        return jnp.where(row == 0, high, jnp.where(row == 1, low, 0.0)).astype(jnp.bfloat16)

    def rows(step, carry):
        for k in range(8):
            i = step * 8 + k
            gradient = share_ref[:, i, :]
            spread = spread_ref[pl.ds(i, 1), :]
            cross = jnp.sum(gradient * bias_ref[:, i, :], axis=0, keepdims=True) / channels
            slope = spread * spread * cross
            high, low = two_terms(gradient * spread)
            left = jnp.concatenate(
                [
                    high, low, high,
                    rows_of_two(jnp.broadcast_to(slope * mean_ref[pl.ds(i, 1), :], row.shape)),
                    rows_of_two(jnp.broadcast_to(slope, row.shape)),
                ],
                axis=0,
            )
            terms = f32_dot(left, right, TN)
            entries = pair_ref[i].astype(jnp.float32)
            out_ref[i] = (terms[:, :channels] - terms[:, channels:] * entries).astype(jnp.bfloat16)
        return carry

    lax.fori_loop(0, pair_ref.shape[0] // 8, rows, 0)


def output_kernel(place_ref, *refs):
    *parts, combined_ref, out_weight_ref, pair_weight_ref, shares_ref = refs
    core, chip = place_ref[0], place_ref[2]
    width = combined_ref.shape[0]
    rows = parts[0].shape[0]
    heads = pair_weight_ref.shape[0]
    for k, ref in enumerate(parts):
        owner = jnp.bitwise_xor(chip, k // 2) * 2 + jnp.bitwise_xor(core, k % 2)
        block = pl.ds(pl.multiple_of(owner * rows, rows), rows)
        part = ref[...].astype(jnp.float32)
        combined_ref[block, :] = part[:, : 4 * width]
        out_weight_ref[block, :] = part[:, 4 * width : 5 * width]
        shares_ref[owner] = part[:heads, 5 * width :]
    total = shares_ref[0]
    for k in range(1, len(parts)):
        total += shares_ref[k]
    pair_weight_ref[...] = total


def call(kernel, outs, *args, scratch=(), place=None, flops=0, after=(), outside=0, late=0):
    whole, anywhere = pl.BlockSpec(memory_space=pltpu.VMEM), pl.BlockSpec(memory_space=pl.ANY)
    specs = [anywhere] * outside + [whole] * (len(args) - outside)
    ahead = () if place is None else (place,)
    shapes = [jax.ShapeDtypeStruct(*o) for o in outs]
    moved = sum(math.prod(a.shape) * a.dtype.itemsize for a in list(args) + shapes)
    first = len(ahead) + len(args)
    last = first + len(after)

    def wrapped(*refs):
        given, rest = list(refs[:first]), refs[last:]
        if outside:
            *rest, arrived = rest
            held = rest[len(rest) - outside :]
            rest = rest[: len(rest) - outside]
            copies = []
            for k in range(outside):
                copies.append(
                    pltpu.make_async_copy(given[len(ahead) + k], held[k], arrived.at[k])
                )
                given[len(ahead) + k] = held[k]
            for copy in copies:
                copy.start()
            for copy in copies[: outside - late]:
                copy.wait()
            if late:
                given.insert(0, lambda: [copy.wait() for copy in copies[outside - late :]])
        kernel(*given, *rest)

    held = [pltpu.VMEM(a.shape, a.dtype) for a in args[:outside]]
    if outside:
        held.append(pltpu.SemaphoreType.DMA((outside,)))
    return pl.pallas_call(
        wrapped,
        out_shape=shapes,
        in_specs=[pl.BlockSpec(memory_space=pltpu.SMEM)] * len(ahead)
        + specs
        + [anywhere] * len(after),
        out_specs=[whole] * len(shapes),
        scratch_shapes=[*scratch, *held],
        compiler_params=pltpu.CompilerParams(
            vmem_limit_bytes=ARGUMENT_VMEM_LIMIT if outside else VMEM_LIMIT
        ),
        cost_estimate=pl.CostEstimate(flops=flops, bytes_accessed=moved, transcendentals=0),
    )(*ahead, *args, *after)


def swapped(mine, axis_name, distance):
    size = lax.axis_size(axis_name)
    return lax.ppermute(mine, axis_name, [(a, a ^ distance) for a in range(size)])


def fits_heads(alignment_rows, pair_entries, pair_weight):
    channels, heads = pair_weight.shape
    return (
        lax.axis_size("seq") == 4
        and lax.axis_size("res") == heads == 8
        and alignment_rows.shape[0] == 2 * SLOTS
        and alignment_rows.shape[1] == pair_entries.shape[0] == 64
        and alignment_rows.shape[2] == 2 * LANES
        and pair_entries.shape[1] == channels == LANES
    )


def head_body(
    alignment_rows, pair_entries, combined_weight, output_weight, pair_weight, updated_gradient
):
    sequences, residues, width = alignment_rows.shape
    channels, heads = pair_weight.shape
    tokens = sequences * residues
    seq_size, res_size = lax.axis_size("seq"), lax.axis_size("res")
    seq_half = seq_size // 2
    total = residues * res_size
    group = 2 * res_size
    groups = [[g * group + k for k in range(group)] for g in range(seq_half)]
    scale = 1.0 / math.sqrt(width // heads * sequences * seq_size)
    res_index, seq_index = lax.axis_index("res"), lax.axis_index("seq")
    place = jnp.stack([res_index % 2, seq_index // 2, res_index // 2]).astype(jnp.int32)
    bf16, f32 = jnp.bfloat16, jnp.float32

    def across(blocks):
        return lax.all_to_all(blocks, ("seq", "res"), 0, 0, axis_index_groups=groups, tiled=True)

    x, grad, wc, wo = alignment_rows, updated_gradient, combined_weight, output_weight
    (query_blocks,) = call(
        functools.partial(query_kernel, scale), [((group, 2 * residues, LANES), bf16)], x, wc,
        flops=8 * tokens * width * width, outside=2,
    )
    query_blocks = across(query_blocks)
    value_blocks, bias, mean, spread = call(
        value_kernel,
        [
            ((group, 3 * residues, LANES), bf16),
            ((heads, residues, LANES), f32),
            ((residues, LANES), f32),
            ((residues, LANES), f32),
        ],
        x, grad, wc, wo, pair_entries, pair_weight.T,
        flops=8 * tokens * width * width, outside=5, late=1,
    )
    query_blocks, value_blocks = lax.optimization_barrier((query_blocks, value_blocks))
    value_blocks = across(value_blocks)

    quarter = (total // 4, total)
    logit_mine, logit_sent = call(
        functools.partial(score_kernel, residues, 0, residues),
        [(quarter, f32), (quarter, f32)],
        query_blocks, swapped(query_blocks, "res", 1),
        place=place, flops=2 * total * total * width,
    )
    logit_other = swapped(logit_sent, "seq", seq_half)
    value_blocks, logit_other = lax.optimization_barrier((value_blocks, logit_other))
    bias_half = ((group // 2, residues, LANES), bf16)
    bias_mine, bias_sent = call(
        functools.partial(bias_kernel, 2 * residues), [bias_half, bias_half], value_blocks,
        place=place,
    )
    bias_other = swapped(bias_sent, "seq", seq_half)
    (grad_terms,) = call(
        functools.partial(grad_score_kernel, residues, residues, 0), [((total // 2, total), bf16)],
        value_blocks, swapped(value_blocks, "res", 1),
        place=place, flops=2 * total * total * width,
    )
    halves = [[k, k + seq_half] for k in range(seq_half)]
    grad_probs = lax.psum(grad_terms, "seq", axis_index_groups=halves)
    bias_other, grad_terms = lax.optimization_barrier((bias_other, grad_terms))
    softmax_out, probs = call(
        softmax_kernel, [(quarter, f32), (quarter, bf16)],
        logit_mine, logit_other, bias_mine, bias_other,
        place=place, flops=total * total,
    )

    def products(mine, far, blocks, first_row, second_row, with_share, factor):
        rows = 2 * residues + (residues // 2 if with_share else 0)
        (out,) = call(
            functools.partial(
                product_kernel, residues, factor, first_row, second_row, with_share
            ),
            [((group, rows, LANES), bf16)],
            mine, far, swapped(mine, "res", 1), swapped(far, "res", 1), blocks,
            scratch=[pltpu.VMEM((total, total), bf16)],
            place=place, flops=4 * total * total * width,
        )
        return out

    probs_far = swapped(probs, "seq", seq_half)
    attended = products(probs, probs_far, value_blocks, 0, residues, False, 1.0)
    attended_blocks = across(attended)
    softmax_out = lax.optimization_barrier((attended, softmax_out))[1]
    grad_logits, grad_far = call(
        softmax_gradient_kernel, [(quarter, bf16), (quarter, bf16)],
        softmax_out, probs_far, grad_probs,
        place=place, flops=total * total,
    )
    grad_sums = products(grad_logits, grad_far, query_blocks, residues, 0, True, scale)
    grad_sums, attended_blocks = lax.optimization_barrier((grad_sums, attended_blocks))
    grad_blocks = across(grad_sums)

    updated, value_gate, normed, attended_sums = call(
        attended_weight_kernel,
        [
            (x.shape, bf16),
            ((tokens, 2 * width), bf16),
            ((tokens, width), bf16),
            ((width, 3 * width), bf16),
        ],
        x, grad, wc, wo, attended_blocks,
        flops=14 * tokens * width * width, outside=4,
    )
    share = pltpu.VMEM((heads, residues, LANES), f32)
    columns = 5 * width
    rows = width // res_size
    part_rows = ((res_size // 2, rows, columns), bf16)
    (pair_weight_part,) = call(
        pair_weight_kernel, [((heads, channels), f32)],
        grad_blocks, pair_entries, mean, spread,
        scratch=[share], flops=4 * tokens * width * width,
    )
    query_key, keep, send = call(
        query_weight_kernel,
        [((tokens, 2 * width), bf16), part_rows, part_rows],
        normed, attended_sums, grad_blocks,
        scratch=[pltpu.VMEM((width, columns), bf16)],
        place=place, flops=4 * tokens * width * width, after=(pair_weight_part,),
    )
    own, *sent = call(
        core_sum_kernel,
        [((rows, columns), f32)] + [((rows, columns), bf16)] * 3,
        keep, swapped(send, "res", 1), place=place,
    )
    received = [swapped(t, "res", 2 * flip) for flip, t in enumerate(sent, 1)]
    (pair_gradient,) = call(
        functools.partial(pair_kernel, 2 * residues),
        [(pair_entries.shape, bf16)],
        grad_blocks, pair_entries, pair_weight.T, bias, mean, spread,
        scratch=[share], flops=8 * tokens * width * width,
    )
    (alignment_gradient,) = call(
        alignment_kernel, [(x.shape, bf16)], x, wc, query_key, value_gate,
        flops=8 * tokens * width * width,
    )
    received, alignment_gradient = lax.optimization_barrier((received, alignment_gradient))
    (part,) = call(
        plane_sum_kernel, [((rows, columns + channels), bf16)], own, pair_weight_part, *received
    )
    def added(mine, other):
        return (mine.astype(f32) + other.astype(f32)).astype(bf16)

    other_plane = swapped(part, "seq", 1)
    part = added(part, other_plane)
    other_half = swapped(part, "seq", seq_half)
    other_half, pair_gradient = lax.optimization_barrier((other_half, pair_gradient))
    part = added(part, other_half)
    chips = [part] + [swapped(part, "res", 2 * flip) for flip in range(1, res_size // 2)]
    parts = [t for chip in chips for t in (chip, swapped(chip, "res", 1))]
    combined_gradient, output_gradient, pair_weight_gradient = call(
        output_kernel,
        [(wc.shape, f32), (wo.shape, f32), ((heads, channels), f32)],
        *parts,
        scratch=[pltpu.VMEM((len(parts), heads, channels), f32)],
        place=place,
    )
    return (
        updated,
        alignment_gradient,
        pair_gradient,
        combined_gradient,
        output_gradient,
        pair_weight_gradient.T,
    )


def body(alignment_rows, pair_entries, combined_weight, output_weight, pair_weight, updated_gradient):
    chosen = head_body if fits_heads(alignment_rows, pair_entries, pair_weight) else gathered_body
    return chosen(
        alignment_rows, pair_entries, combined_weight, output_weight, pair_weight, updated_gradient
    )


def solution(mesh):
    return jax.shard_map(
        body,
        mesh=mesh,
        in_specs=(
            P("seq", "res", None),
            P("res", "seq", None),
            P(),
            P(),
            P(),
            P("seq", "res", None),
        ),
        out_specs=(
            P("seq", "res", None),
            P("seq", "res", None),
            P("res", "seq", None),
            P(),
            P(),
            P(),
        ),
        check_vma=False,
    )
```

```python
import functools
import math

import jax
import jax.numpy as jnp
from jax import lax
from jax.experimental import pallas as pl
from jax.experimental.pallas import tpu as pltpu
from jax.sharding import PartitionSpec as P

eps_norm = 1e-05


def layer_normalize(values):
    values = values.astype(jnp.float32)
    center = values - jnp.mean(values, axis=-1, keepdims=True)
    broadcast_pair = lax.rsqrt(jnp.mean(center * center, axis=-1, keepdims=True) + eps_norm)
    return (center * broadcast_pair, broadcast_pair)


def layer_norm_backward(normalized_gradient, normalized_rows, broadcast_pair):
    mean_grad = jnp.mean(normalized_gradient, axis=-1, keepdims=True)
    mean_cross = jnp.mean(normalized_gradient * normalized_rows, axis=-1, keepdims=True)
    return broadcast_pair * (normalized_gradient - mean_grad - normalized_rows * mean_cross)


def split_heads(tensor, head_count):
    return tensor.reshape(
        tensor.shape[0], tensor.shape[1], head_count, tensor.shape[2] // head_count
    )


def merge_heads(tensor):
    return tensor.reshape(tensor.shape[0], tensor.shape[1], tensor.shape[2] * tensor.shape[3])


def gathered_body(
    alignment_rows, pair_entries, combined_weight, output_weight, pair_weight, updated_gradient
):
    sequence_count, residue_count, alignment_width = alignment_rows.shape
    head_count = pair_weight.shape[1]
    query_width = output_weight.shape[0]
    head_dim = query_width // head_count
    column_count = pair_entries.shape[1]
    token_count = sequence_count * residue_count
    score_scale = 1.0 / math.sqrt(head_dim * sequence_count * lax.axis_size("seq"))
    normalized_rows, broadcast_pair = layer_normalize(alignment_rows)
    normalized_rows_backward = normalized_rows.astype(jnp.bfloat16).reshape(
        token_count, alignment_width
    )
    projected = jnp.dot(
        normalized_rows_backward, combined_weight, preferred_element_type=jnp.float32
    ).reshape(sequence_count, residue_count, 4 * query_width)
    queries = (projected[..., :query_width] * score_scale).astype(jnp.bfloat16)
    key_rows = projected[..., query_width : 2 * query_width].astype(jnp.bfloat16)
    value_rows = projected[..., 2 * query_width : 3 * query_width].astype(jnp.bfloat16)
    gate_open = jax.nn.sigmoid(projected[..., 3 * query_width :])
    all_keys, all_values = (
        lax.all_gather(key_rows, "res", axis=1, tiled=True),
        lax.all_gather(value_rows, "res", axis=1, tiled=True),
    )
    query_heads = split_heads(queries, head_count)
    key_heads = split_heads(all_keys, head_count)
    value_heads = split_heads(all_values, head_count)
    score_terms = jnp.einsum(
        "sihd,sjhd->hij", query_heads, key_heads, preferred_element_type=jnp.float32
    )
    pair_normed, pair_spread = layer_normalize(pair_entries)
    pair_bias = jnp.einsum("ijc,ch->hij", pair_normed, pair_weight, precision=lax.Precision.HIGHEST)
    col_start = lax.axis_index("seq") * column_count
    own_block = lax.dynamic_slice_in_dim(score_terms, col_start, column_count, 2) + pair_bias
    logits = lax.psum(lax.dynamic_update_slice_in_dim(score_terms, own_block, col_start, 2), "seq")
    row_top = jnp.max(logits, axis=-1, keepdims=True)
    lifted = jnp.exp(logits - row_top)
    softmax_out = lifted / jnp.sum(lifted, axis=-1, keepdims=True)
    softmax_low = softmax_out.astype(jnp.bfloat16)
    attended = merge_heads(
        jnp.einsum("hij,sjhd->sihd", softmax_low, value_heads, preferred_element_type=jnp.float32)
    )
    gated_out = (gate_open * attended).astype(jnp.bfloat16)
    flattened_gated = gated_out.reshape(token_count, query_width)
    updated = (
        jnp.dot(flattened_gated, output_weight, preferred_element_type=jnp.float32)
        .astype(jnp.bfloat16)
        .reshape(sequence_count, residue_count, alignment_width)
    )
    flattened_gradient = updated_gradient.reshape(token_count, alignment_width)
    grad_gated = jnp.dot(
        flattened_gradient, output_weight.T, preferred_element_type=jnp.float32
    ).reshape(sequence_count, residue_count, query_width)
    out_local = jnp.dot(flattened_gated.T, flattened_gradient, preferred_element_type=jnp.float32)
    grad_attended = (grad_gated * gate_open).astype(jnp.bfloat16)
    grad_gate_logit = grad_gated * attended * gate_open * (1.0 - gate_open)
    attended_grad_heads = split_heads(grad_attended, head_count)
    grad_terms = jnp.einsum(
        "sihd,sjhd->hij", attended_grad_heads, value_heads, preferred_element_type=jnp.float32
    )
    grad_probs = lax.psum(grad_terms, "seq")
    row_dot = jnp.sum(softmax_out * grad_probs, axis=-1, keepdims=True)
    grad_logits = softmax_out * (grad_probs - row_dot)
    grad_logits_b = grad_logits.astype(jnp.bfloat16)
    logit_share = lax.dynamic_slice_in_dim(grad_logits, col_start, column_count, 2)
    grad_query_heads = (
        jnp.einsum("hij,sjhd->sihd", grad_logits_b, key_heads, preferred_element_type=jnp.float32)
        * score_scale
    )
    key_part = jnp.einsum(
        "hij,sihd->jshd", grad_logits_b, query_heads, preferred_element_type=jnp.float32
    )
    value_part = jnp.einsum(
        "hij,sihd->jshd", softmax_low, attended_grad_heads, preferred_element_type=jnp.float32
    )
    summed = lax.psum_scatter(
        jnp.concatenate([merge_heads(key_part), merge_heads(value_part)], axis=-1),
        "res",
        scatter_dimension=0,
        tiled=True,
    )
    key_value_grads = jnp.transpose(summed, (1, 0, 2))
    projected_gradient = jnp.concatenate(
        [merge_heads(grad_query_heads), key_value_grads, grad_gate_logit], axis=-1
    )
    projected_gradient = projected_gradient.astype(jnp.bfloat16).reshape(
        token_count, 4 * query_width
    )
    qkvg_local = jnp.dot(
        normalized_rows_backward.T, projected_gradient, preferred_element_type=jnp.float32
    )
    normalized_gradient = jnp.dot(
        projected_gradient, combined_weight.T, preferred_element_type=jnp.float32
    ).reshape(sequence_count, residue_count, alignment_width)
    alignment_gradient = layer_norm_backward(
        normalized_gradient, normalized_rows, broadcast_pair
    ).astype(jnp.bfloat16)
    pair_w_local = jnp.einsum(
        "ijc,hij->ch", pair_normed, logit_share, precision=lax.Precision.HIGHEST
    )
    grad_pair_normed = jnp.einsum(
        "hij,ch->ijc", logit_share, pair_weight, precision=lax.Precision.HIGHEST
    )
    pair_gradient = layer_norm_backward(grad_pair_normed, pair_normed, pair_spread).astype(
        jnp.bfloat16
    )
    combined_weight_gradient, output_weight_gradient, pair_weight_gradient = lax.psum(
        (qkvg_local, out_local, pair_w_local), ("seq", "res")
    )
    return (
        updated,
        alignment_gradient,
        pair_gradient,
        combined_weight_gradient,
        output_weight_gradient,
        pair_weight_gradient,
    )


VMEM_LIMIT = 20 * 1024 * 1024
ARGUMENT_VMEM_LIMIT = 56 * 1024 * 1024
LANES = 128
SLOTS = 4
NT = (((1,), (1,)), ((), ()))
TN = (((0,), (0,)), ((), ()))


def f32_dot(left, right, dims=None):
    if dims is None:
        return jnp.dot(left, right, preferred_element_type=jnp.float32)
    return lax.dot_general(left, right, dims, preferred_element_type=jnp.float32)


def two_terms(values):
    high = values.astype(jnp.bfloat16)
    return high, (values - high.astype(jnp.float32)).astype(jnp.bfloat16)


def slot_select(pieces):
    slot = lax.broadcasted_iota(jnp.int32, pieces[0].shape, 1) // (LANES // SLOTS)
    result = pieces[0]
    for k in range(1, SLOTS):
        result = jnp.where(slot == k, pieces[k], result)
    return result


def pack_heads(out_ref, row, tensor, residues):
    for core in range(2):
        for tile in range(tensor.shape[1] // LANES):
            rolled = []
            for s in range(SLOTS):
                start = (core * SLOTS + s) * residues
                piece = tensor[start : start + residues, tile * LANES : (tile + 1) * LANES]
                rolled.append(pltpu.roll(piece, s * LANES // SLOTS, 1) if s else piece)
            for j in range(SLOTS):
                block = slot_select([rolled[(k - j) % SLOTS] for k in range(SLOTS)])
                out_ref[(tile * SLOTS + j) * 2 + core, row : row + residues, :] = block.astype(
                    jnp.bfloat16
                )


def unpack_heads(in_ref, row, residues, tiles):
    rows = []
    for core in range(2):
        for s in range(SLOTS):
            pieces = []
            for tile in range(tiles):
                blocks = [
                    in_ref[
                        (tile * SLOTS + (k - s) % SLOTS) * 2 + core, row : row + residues, :
                    ].astype(jnp.float32)
                    for k in range(SLOTS)
                ]
                block = slot_select(blocks)
                pieces.append(pltpu.roll(block, LANES - s * LANES // SLOTS, 1) if s else block)
            rows.append(jnp.concatenate(pieces, axis=1))
    return jnp.concatenate(rows, axis=0)


def normalized(x_ref):
    width = x_ref.shape[-1]
    values = x_ref[...].reshape(-1, width).astype(jnp.float32)
    return layer_normalize(values)


def gate_of(logits):
    return 1.0 / (1.0 + jnp.exp(-logits))


def value_kernel(x_ref, grad_ref, wc_ref, wo_ref, out_ref):
    residues, width = x_ref.shape[1], x_ref.shape[2]
    normed = normalized(x_ref)[0].astype(jnp.bfloat16)
    values = f32_dot(normed, wc_ref[:, 2 * width : 3 * width])
    gate = gate_of(f32_dot(normed, wc_ref[:, 3 * width :]))
    grad_gated = f32_dot(grad_ref[...].reshape(-1, width), wo_ref[...], NT)
    pack_heads(out_ref, 0, values, residues)
    pack_heads(out_ref, residues, grad_gated * gate, residues)


def centred(weight):
    return weight - jnp.mean(weight, axis=1, keepdims=True)


def query_kernel(
    scale, arrive, x_ref, wc_ref, pair_ref, weight_ref, out_ref, bias_ref, mean_ref, spread_ref
):
    residues, width = x_ref.shape[1], x_ref.shape[2]
    heads = weight_ref.shape[0]
    normed = normalized(x_ref)[0].astype(jnp.bfloat16)
    pack_heads(out_ref, 0, f32_dot(normed, wc_ref[:, :width]) * scale, residues)
    pack_heads(out_ref, residues, f32_dot(normed, wc_ref[:, width : 2 * width]), residues)

    arrive()
    columns, channels = pair_ref.shape[1], pair_ref.shape[2]
    weight = centred(weight_ref[...])
    first = weight.astype(jnp.bfloat16)
    second, third = two_terms(weight - first.astype(jnp.float32))
    share = jnp.full((heads, channels), 1.0 / channels, jnp.bfloat16)
    left = jnp.concatenate([first, second, third, share], axis=0)
    average = jnp.full((channels, channels), 1.0 / channels, jnp.bfloat16)
    step_rows = 64

    def rows(step, carry):
        start = pl.multiple_of(step * step_rows, step_rows)
        entries = pair_ref[pl.ds(start, step_rows)].reshape(step_rows * columns, channels)
        center = entries.astype(jnp.float32) - f32_dot(entries, average)
        high, low = two_terms(center * center)
        variance = f32_dot(share, high, NT) + f32_dot(share, low, NT)
        spread = lax.rsqrt(variance + eps_norm)
        raw = f32_dot(left, entries, NT)
        bias = spread * (raw[:heads] + raw[heads : 2 * heads] + raw[2 * heads : 3 * heads])
        for k in range(step_rows):
            lanes = slice(k * columns, (k + 1) * columns)
            bias_ref[:, start + k, :] = bias[:, lanes]
            mean_ref[pl.ds(start + k, 1), :] = raw[3 * heads : 3 * heads + 1, lanes]
            spread_ref[pl.ds(start + k, 1), :] = spread[:1, lanes]
        return carry

    lax.fori_loop(0, pair_ref.shape[0] // step_rows, rows, 0)
    half = residues // 2
    for h in range(heads):
        for core in range(2):
            high, low = two_terms(bias_ref[h, core * half : (core + 1) * half, :])
            out_ref[h * 2 + core, 2 * residues : 2 * residues + half, :] = high
            out_ref[h * 2 + core, 2 * residues + half : 3 * residues, :] = low


def lanes_of(blocks_ref, row, residues):
    count = blocks_ref.shape[0] // 2
    planes = [
        blocks_ref[p * count : (p + 1) * count, row : row + residues, :].reshape(-1, LANES)
        for p in range(2)
    ]
    return jnp.concatenate(planes, axis=1)


def score_kernel(
    residues, left_row, right_row, sent, place_ref, own_ref, other_ref, out_ref
):
    core, half = place_ref[0], place_ref[1]
    count = own_ref.shape[0] // 2
    part = residues // 2
    right = jnp.concatenate(
        [lanes_of(own_ref, right_row, residues), lanes_of(other_ref, right_row, residues)], axis=1
    )
    which = 1 - half if sent else half
    left = []
    for k in range(count // 2):
        block = which * (count // 2) + k
        rows = pl.ds(pl.multiple_of(left_row + core * part, part), part)
        left.append(
            jnp.concatenate(
                [
                    r[p * count + block, rows, :]
                    for r in (own_ref, other_ref)
                    for p in range(2)
                ],
                axis=1,
            )
        )
    out_ref[...] = f32_dot(jnp.concatenate(left, axis=0), right, NT)
    for p in range(2):
        columns = pl.ds(pl.multiple_of((half * 2 + p) * LANES, LANES), LANES)
        for k in range(count // 2):
            block = p * count + which * (count // 2) + k
            high = own_ref[block, 2 * residues : 2 * residues + part, :]
            low = own_ref[block, 2 * residues + part : 3 * residues, :]
            bias = high.astype(jnp.float32) + low.astype(jnp.float32)
            out_ref[k * part : (k + 1) * part, columns] += bias


def softmax_kernel(logit_ref, other_ref, out_ref, low_ref):
    logits = logit_ref[...] + other_ref[...]
    lifted = jnp.exp(logits - jnp.max(logits, axis=-1, keepdims=True))
    softmax_out = lifted / jnp.sum(lifted, axis=-1, keepdims=True)
    out_ref[...] = softmax_out
    low_ref[...] = softmax_out.astype(jnp.bfloat16)


def grad_score_kernel(
    residues, left_row, right_row, place_ref, own_ref, other_ref, full_ref, sent_ref
):
    core = place_ref[0]
    count = own_ref.shape[0] // 2
    part = residues // 2
    right = jnp.concatenate(
        [lanes_of(own_ref, right_row, residues), lanes_of(other_ref, right_row, residues)], axis=1
    )
    rows = pl.ds(pl.multiple_of(left_row + core * part, part), part)
    left = [
        jnp.concatenate(
            [r[p * count + k, rows, :] for r in (own_ref, other_ref) for p in range(2)], axis=1
        )
        for k in range(count)
    ]
    terms = f32_dot(jnp.concatenate(left, axis=0), right, NT)
    full_ref[...] = terms
    sent_ref[...] = terms.astype(jnp.bfloat16)


def softmax_gradient_kernel(
    place_ref, softmax_ref, far_ref, grad_ref, other_ref, out_ref, out_far_ref
):
    half = place_ref[1]
    count = softmax_ref.shape[0]
    for which, probs, ref in ((half, softmax_ref, out_ref), (1 - half, far_ref, out_far_ref)):
        rows = pl.ds(pl.multiple_of(which * count, count), count)
        softmax_out = probs[...].astype(jnp.float32)
        grad_probs = grad_ref[rows, :] + other_ref[rows, :].astype(jnp.float32)
        row_dot = jnp.sum(softmax_out * grad_probs, axis=-1, keepdims=True)
        ref[...] = (softmax_out * (grad_probs - row_dot)).astype(jnp.bfloat16)


def product_kernel(
    residues, scale, first_row, second_row, with_share,
    place_ref, own_ref, far_ref, near_ref, corner_ref, blocks_ref, out_ref, whole_ref,
):
    core, half = place_ref[0], place_ref[1]
    count = blocks_ref.shape[0] // 2
    part = residues // 2
    quarters = (
        (own_ref, core, half), (far_ref, core, 1 - half),
        (near_ref, 1 - core, half), (corner_ref, 1 - core, 1 - half),
    )
    for ref, c, z in quarters:
        for k in range(count // 2):
            start = (z * (count // 2) + k) * residues + c * part
            whole_ref[pl.ds(pl.multiple_of(start, part), part), :] = ref[k * part : (k + 1) * part, :]
    whole = whole_ref[...]
    if with_share:
        for p in range(2):
            columns = pl.ds(pl.multiple_of((half * 2 + p) * LANES, LANES), LANES)
            for q in range(count):
                rows = pl.ds(pl.multiple_of(q * residues + core * part, part), part)
                out_ref[p * count + q, 2 * residues : 2 * residues + part, :] = whole_ref[rows, columns]
    first = f32_dot(whole, lanes_of(blocks_ref, first_row, residues)) * scale
    second = f32_dot(whole, lanes_of(blocks_ref, second_row, residues), TN)
    for row, product in ((0, first), (residues, second)):
        for p in range(2):
            out_ref[p * count : (p + 1) * count, row : row + residues, :] = (
                product[:, p * LANES : (p + 1) * LANES]
                .astype(jnp.bfloat16)
                .reshape(count, residues, LANES)
            )


def share_of(blocks_ref, row, part, heads):
    return jnp.concatenate(
        [
            blocks_ref[:, row : row + part, :]
            .astype(jnp.float32)
            .reshape(heads, 2 * part, LANES)
        ],
        axis=0,
    )


def split_rows(core, sums_ref, keep_ref, send_ref):
    rows = keep_ref.shape[1]
    for which, ref in ((core, keep_ref), (1 - core, send_ref)):
        for block in range(keep_ref.shape[0]):
            start = pl.multiple_of((2 * block + which) * rows, rows)
            ref[block] = sums_ref[pl.ds(start, rows), :]


def attended_weight_kernel(
    place_ref, x_ref, grad_ref, wc_ref, wo_ref, blocks_ref,
    updated_ref, projected_ref, normed_ref, keep_ref, send_ref, sums_ref,
):
    residues, width = x_ref.shape[1], x_ref.shape[2]
    tiles = width // LANES
    normed = normalized(x_ref)[0].astype(jnp.bfloat16)
    normed_ref[...] = normed
    gate = gate_of(f32_dot(normed, wc_ref[:, 3 * width :]))
    grad = grad_ref[...].reshape(-1, width)
    grad_gated = f32_dot(grad, wo_ref[...], NT)
    attended = unpack_heads(blocks_ref, 0, residues, tiles)
    gated = (gate * attended).astype(jnp.bfloat16)
    updated_ref[...] = f32_dot(gated, wo_ref[...]).astype(jnp.bfloat16).reshape(updated_ref.shape)
    projected_ref[:, :width] = unpack_heads(blocks_ref, residues, residues, tiles).astype(
        jnp.bfloat16
    )
    projected_ref[:, width:] = (grad_gated * attended * gate * (1.0 - gate)).astype(jnp.bfloat16)
    sums_ref[:, : 2 * width] = f32_dot(normed, projected_ref[...], TN).astype(jnp.bfloat16)
    sums_ref[:, 2 * width :] = f32_dot(gated, grad, TN).astype(jnp.bfloat16)
    split_rows(place_ref[0], sums_ref, keep_ref, send_ref)


def query_weight_kernel(
    place_ref, normed_ref, blocks_ref, projected_ref, keep_ref, send_ref, sums_ref
):
    width = normed_ref.shape[1]
    tiles, residues = width // LANES, (blocks_ref.shape[1] * 2) // 5
    for t in range(2):
        projected_ref[:, t * width : (t + 1) * width] = unpack_heads(
            blocks_ref, t * residues, residues, tiles
        ).astype(jnp.bfloat16)
    sums_ref[...] = f32_dot(normed_ref[...], projected_ref[...], TN).astype(jnp.bfloat16)
    split_rows(place_ref[0], sums_ref, keep_ref, send_ref)


def core_sum_kernel(place_ref, keep_ref, other_ref, own_ref, *send_refs):
    chip = place_ref[2]
    for flip, ref in enumerate((own_ref, *send_refs)):
        block = jnp.bitwise_xor(chip, flip)
        total = keep_ref[block].astype(jnp.float32) + other_ref[block].astype(jnp.float32)
        ref[...] = total.astype(ref.dtype)


def plane_sum_kernel(own_ref, *refs):
    total = own_ref[...]
    for ref in refs[:-1]:
        total += ref[...].astype(jnp.float32)
    refs[-1][...] = total.astype(refs[-1].dtype)


def plane_pair_sum_kernel(own_ref, pair_weight_ref, *refs):
    *received, out_ref = refs
    total = own_ref[...]
    for ref in received:
        total += ref[...].astype(jnp.float32)
    count = own_ref.shape[1]
    heads = pair_weight_ref.shape[0]
    out_ref[:, :count] = total.astype(out_ref.dtype)
    rest = jnp.zeros((out_ref.shape[0] - heads, out_ref.shape[1] - count), jnp.float32)
    out_ref[:, count:] = jnp.concatenate([pair_weight_ref[...], rest], axis=0).astype(
        out_ref.dtype
    )


def join_kernel(query_ref, query_other_ref, value_ref, value_other_ref, out_ref):
    query = query_ref[...].astype(jnp.float32) + query_other_ref[...].astype(jnp.float32)
    value = value_ref[...].astype(jnp.float32) + value_other_ref[...].astype(jnp.float32)
    channels = query.shape[1] + value.shape[1] - out_ref.shape[1] + LANES
    count = query.shape[1] - channels
    out_ref[:, :count] = query[:, :count].astype(out_ref.dtype)
    out_ref[:, count : count + value.shape[1]] = value.astype(out_ref.dtype)
    out_ref[:, count + value.shape[1] :] = query[:, count:].astype(out_ref.dtype)


def pair_weight_kernel(blocks_ref, pair_ref, mean_ref, spread_ref, out_ref, share_ref):
    heads, part = share_ref.shape[0], pair_ref.shape[0] // 2
    share_ref[...] = share_of(blocks_ref, blocks_ref.shape[1] - part, part, heads)

    def rows(step, carry):
        total, shift = carry
        for k in range(8):
            i = step * 8 + k
            scaled = share_ref[:, i, :] * spread_ref[pl.ds(i, 1), :]
            high, low = two_terms(scaled)
            total += f32_dot(jnp.concatenate([high, low], axis=0), pair_ref[i])
            shift += (high.astype(jnp.float32) + low.astype(jnp.float32)) * mean_ref[pl.ds(i, 1), :]
        return total, shift

    channels = pair_ref.shape[2]
    total, shift = lax.fori_loop(
        0,
        pair_ref.shape[0] // 8,
        rows,
        (jnp.zeros((2 * heads, channels), jnp.float32), jnp.zeros((heads, LANES), jnp.float32)),
    )
    out_ref[...] = total[:heads] + total[heads:] - jnp.sum(shift, axis=1, keepdims=True)


def alignment_kernel(x_ref, wc_ref, query_key_ref, value_gate_ref, out_ref):
    normed, spread = normalized(x_ref)
    width = x_ref.shape[2]
    gradient = f32_dot(query_key_ref[...], wc_ref[:, : 2 * width], NT) + f32_dot(
        value_gate_ref[...], wc_ref[:, 2 * width :], NT
    )
    out_ref[...] = (
        layer_norm_backward(gradient, normed, spread).astype(jnp.bfloat16).reshape(out_ref.shape)
    )


def pair_kernel(blocks_row, blocks_ref, pair_ref, weight_ref, bias_ref, mean_ref, spread_ref, out_ref, share_ref):
    heads, channels = weight_ref.shape
    part = pair_ref.shape[0] // 2
    share_ref[...] = share_of(blocks_ref, blocks_row, part, heads)
    first, second = two_terms(centred(weight_ref[...]))
    zero = jnp.zeros((heads, channels), jnp.bfloat16)
    top = lax.broadcasted_iota(jnp.int32, (heads, channels), 0) < 2
    ones = jnp.where(top, 1.0, 0.0).astype(jnp.bfloat16)
    right = jnp.concatenate(
        [
            jnp.concatenate([first, first, second, ones, zero], axis=0),
            jnp.concatenate([zero, zero, zero, zero, ones], axis=0),
        ],
        axis=1,
    )
    row = lax.broadcasted_iota(jnp.int32, (heads, LANES), 0)

    def rows_of_two(value):
        high, low = two_terms(value)
        high, low = high.astype(jnp.float32), low.astype(jnp.float32)
        return jnp.where(row == 0, high, jnp.where(row == 1, low, 0.0)).astype(jnp.bfloat16)

    def rows(step, carry):
        for k in range(8):
            i = step * 8 + k
            gradient = share_ref[:, i, :]
            spread = spread_ref[pl.ds(i, 1), :]
            cross = jnp.sum(gradient * bias_ref[:, i, :], axis=0, keepdims=True) / channels
            slope = spread * spread * cross
            high, low = two_terms(gradient * spread)
            left = jnp.concatenate(
                [
                    high, low, high,
                    rows_of_two(jnp.broadcast_to(slope * mean_ref[pl.ds(i, 1), :], row.shape)),
                    rows_of_two(jnp.broadcast_to(slope, row.shape)),
                ],
                axis=0,
            )
            terms = f32_dot(left, right, TN)
            entries = pair_ref[i].astype(jnp.float32)
            out_ref[i] = (terms[:, :channels] - terms[:, channels:] * entries).astype(jnp.bfloat16)
        return carry

    lax.fori_loop(0, pair_ref.shape[0] // 8, rows, 0)


def output_kernel(place_ref, *refs):
    *parts, combined_ref, out_weight_ref, pair_weight_ref, shares_ref = refs
    core, chip = place_ref[0], place_ref[2]
    width = combined_ref.shape[0]
    rows = parts[0].shape[0]
    heads = pair_weight_ref.shape[0]
    for k, ref in enumerate(parts):
        owner = jnp.bitwise_xor(chip, k // 2) * 2 + jnp.bitwise_xor(core, k % 2)
        block = pl.ds(pl.multiple_of(owner * rows, rows), rows)
        part = ref[...].astype(jnp.float32)
        combined_ref[block, :] = part[:, : 4 * width]
        out_weight_ref[block, :] = part[:, 4 * width : 5 * width]
        shares_ref[owner] = part[:heads, 5 * width :]
    total = shares_ref[0]
    for k in range(1, len(parts)):
        total += shares_ref[k]
    pair_weight_ref[...] = total


def call(kernel, outs, *args, scratch=(), place=None, flops=0, after=(), outside=0, late=0):
    whole, anywhere = pl.BlockSpec(memory_space=pltpu.VMEM), pl.BlockSpec(memory_space=pl.ANY)
    specs = [anywhere] * outside + [whole] * (len(args) - outside)
    ahead = () if place is None else (place,)
    shapes = [jax.ShapeDtypeStruct(*o) for o in outs]
    moved = sum(math.prod(a.shape) * a.dtype.itemsize for a in list(args) + shapes)
    first = len(ahead) + len(args)
    last = first + len(after)

    def wrapped(*refs):
        given, rest = list(refs[:first]), refs[last:]
        if outside:
            *rest, arrived = rest
            held = rest[len(rest) - outside :]
            rest = rest[: len(rest) - outside]
            copies = []
            for k in range(outside):
                copies.append(
                    pltpu.make_async_copy(given[len(ahead) + k], held[k], arrived.at[k])
                )
                given[len(ahead) + k] = held[k]
            for copy in copies:
                copy.start()
            for copy in copies[: outside - late]:
                copy.wait()
            if late:
                given.insert(0, lambda: [copy.wait() for copy in copies[outside - late :]])
        kernel(*given, *rest)

    held = [pltpu.VMEM(a.shape, a.dtype) for a in args[:outside]]
    if outside:
        held.append(pltpu.SemaphoreType.DMA((outside,)))
    return pl.pallas_call(
        wrapped,
        out_shape=shapes,
        in_specs=[pl.BlockSpec(memory_space=pltpu.SMEM)] * len(ahead)
        + specs
        + [anywhere] * len(after),
        out_specs=[whole] * len(shapes),
        scratch_shapes=[*scratch, *held],
        compiler_params=pltpu.CompilerParams(
            vmem_limit_bytes=ARGUMENT_VMEM_LIMIT if outside else VMEM_LIMIT
        ),
        cost_estimate=pl.CostEstimate(flops=flops, bytes_accessed=moved, transcendentals=0),
    )(*ahead, *args, *after)


def swapped(mine, axis_name, distance):
    size = lax.axis_size(axis_name)
    return lax.ppermute(mine, axis_name, [(a, a ^ distance) for a in range(size)])


def fits_heads(alignment_rows, pair_entries, pair_weight):
    channels, heads = pair_weight.shape
    return (
        lax.axis_size("seq") == 4
        and lax.axis_size("res") == heads == 8
        and alignment_rows.shape[0] == 2 * SLOTS
        and alignment_rows.shape[1] == pair_entries.shape[0] == 64
        and alignment_rows.shape[2] == 2 * LANES
        and pair_entries.shape[1] == channels == LANES
    )


def head_body(
    alignment_rows, pair_entries, combined_weight, output_weight, pair_weight, updated_gradient
):
    sequences, residues, width = alignment_rows.shape
    channels, heads = pair_weight.shape
    tokens = sequences * residues
    seq_size, res_size = lax.axis_size("seq"), lax.axis_size("res")
    seq_half = seq_size // 2
    total = residues * res_size
    group = 2 * res_size
    groups = [[g * group + k for k in range(group)] for g in range(seq_half)]
    scale = 1.0 / math.sqrt(width // heads * sequences * seq_size)
    res_index, seq_index = lax.axis_index("res"), lax.axis_index("seq")
    place = jnp.stack([res_index % 2, seq_index // 2, res_index // 2]).astype(jnp.int32)
    bf16, f32 = jnp.bfloat16, jnp.float32

    def across(blocks):
        return lax.all_to_all(blocks, ("seq", "res"), 0, 0, axis_index_groups=groups, tiled=True)

    x, grad, wc, wo = alignment_rows, updated_gradient, combined_weight, output_weight
    (value_blocks,) = call(
        value_kernel, [((group, 2 * residues, LANES), bf16)], x, grad, wc, wo,
        flops=8 * tokens * width * width, outside=4,
    )
    value_blocks = across(value_blocks)
    query_blocks, bias, mean, spread = call(
        functools.partial(query_kernel, scale),
        [
            ((group, 3 * residues, LANES), bf16),
            ((heads, residues, LANES), f32),
            ((residues, LANES), f32),
            ((residues, LANES), f32),
        ],
        x, wc, pair_entries, pair_weight.T,
        flops=8 * tokens * width * width, outside=3, late=1,
    )
    value_blocks, query_blocks = lax.optimization_barrier((value_blocks, query_blocks))
    query_blocks = across(query_blocks)

    quarter, half_rows = (total // 4, total), (total // 2, total)
    grad_full, grad_sent = call(
        functools.partial(grad_score_kernel, residues, residues, 0),
        [(half_rows, f32), (half_rows, bf16)],
        value_blocks, swapped(value_blocks, "res", 1),
        place=place, flops=2 * total * total * width,
    )
    grad_other = swapped(grad_sent, "seq", seq_half)
    query_blocks, grad_other = lax.optimization_barrier((query_blocks, grad_other))
    query_other = swapped(query_blocks, "res", 1)

    def scores(sent):
        return call(
            functools.partial(score_kernel, residues, 0, residues, sent), [(quarter, f32)],
            query_blocks, query_other,
            place=place, flops=total * total * width,
        )[0]

    logit_sent, logit_mine = scores(True), scores(False)
    softmax_out, probs = call(
        softmax_kernel, [(quarter, f32), (quarter, bf16)],
        logit_mine, swapped(logit_sent, "seq", seq_half),
        flops=total * total,
    )

    def products(mine, far, blocks, first_row, second_row, with_share, factor):
        rows = 2 * residues + (residues // 2 if with_share else 0)
        (out,) = call(
            functools.partial(
                product_kernel, residues, factor, first_row, second_row, with_share
            ),
            [((group, rows, LANES), bf16)],
            mine, far, swapped(mine, "res", 1), swapped(far, "res", 1), blocks,
            scratch=[pltpu.VMEM((total, total), bf16)],
            place=place, flops=4 * total * total * width,
        )
        return out

    probs_far = swapped(probs, "seq", seq_half)
    attended = products(probs, probs_far, value_blocks, 0, residues, False, 1.0)
    attended_blocks = across(attended)
    softmax_out = lax.optimization_barrier((attended, softmax_out))[1]
    grad_logits, grad_far = call(
        softmax_gradient_kernel, [(quarter, bf16), (quarter, bf16)],
        softmax_out, probs_far, grad_full, grad_other,
        place=place, flops=total * total,
    )
    grad_sums = products(grad_logits, grad_far, query_blocks, residues, 0, True, scale)
    grad_sums, attended_blocks = lax.optimization_barrier((grad_sums, attended_blocks))
    grad_blocks = across(grad_sums)

    rows = width // res_size

    def part_rows(columns):
        return [((res_size // 2, rows, columns), bf16)] * 2

    def chip_sums(keep, send):
        columns = keep.shape[2]
        own, *sent = call(
            core_sum_kernel,
            [((rows, columns), f32)] + [((rows, columns), bf16)] * 3,
            keep, swapped(send, "res", 1), place=place,
        )
        return own, [swapped(t, "res", 2 * flip) for flip, t in enumerate(sent, 1)]

    updated, value_gate, normed, keep, send = call(
        attended_weight_kernel,
        [(x.shape, bf16), ((tokens, 2 * width), bf16), ((tokens, width), bf16)]
        + part_rows(3 * width),
        x, grad, wc, wo, attended_blocks,
        scratch=[pltpu.VMEM((width, 3 * width), bf16)],
        place=place, flops=14 * tokens * width * width, outside=4,
    )
    value_own, value_received = chip_sums(keep, send)
    grad_blocks, value_received = lax.optimization_barrier((grad_blocks, value_received))
    (value_part,) = call(
        plane_sum_kernel, [((rows, 3 * width), bf16)], value_own, *value_received
    )
    share = pltpu.VMEM((heads, residues, LANES), f32)
    (pair_weight_part,) = call(
        pair_weight_kernel, [((heads, channels), f32)],
        grad_blocks, pair_entries, mean, spread,
        scratch=[share], flops=4 * tokens * width * width,
    )
    query_key, keep, send = call(
        query_weight_kernel,
        [((tokens, 2 * width), bf16)] + part_rows(2 * width),
        normed, grad_blocks,
        scratch=[pltpu.VMEM((width, 2 * width), bf16)],
        place=place, flops=4 * tokens * width * width, after=(pair_weight_part,),
    )
    query_own, query_received = chip_sums(keep, send)
    (pair_gradient,) = call(
        functools.partial(pair_kernel, 2 * residues),
        [(pair_entries.shape, bf16)],
        grad_blocks, pair_entries, pair_weight.T, bias, mean, spread,
        scratch=[share], flops=8 * tokens * width * width,
    )
    (alignment_gradient,) = call(
        alignment_kernel, [(x.shape, bf16)], x, wc, query_key, value_gate,
        flops=8 * tokens * width * width,
    )
    query_received, alignment_gradient = lax.optimization_barrier(
        (query_received, alignment_gradient)
    )
    (query_part,) = call(
        plane_pair_sum_kernel, [((rows, 2 * width + channels), bf16)],
        query_own, pair_weight_part, *query_received,
    )

    def added(mine, other):
        return (mine.astype(f32) + other.astype(f32)).astype(bf16)

    value_part = added(value_part, swapped(value_part, "seq", 1))
    value_other = swapped(value_part, "seq", seq_half)
    query_part = added(query_part, swapped(query_part, "seq", 1))
    query_other = swapped(query_part, "seq", seq_half)
    query_other, pair_gradient = lax.optimization_barrier((query_other, pair_gradient))
    (part,) = call(
        join_kernel, [((rows, 5 * width + channels), bf16)],
        query_part, query_other, value_part, value_other,
    )
    chips = [part] + [swapped(part, "res", 2 * flip) for flip in range(1, res_size // 2)]
    parts = [t for chip in chips for t in (chip, swapped(chip, "res", 1))]
    combined_gradient, output_gradient, pair_weight_gradient = call(
        output_kernel,
        [(wc.shape, f32), (wo.shape, f32), ((heads, channels), f32)],
        *parts,
        scratch=[pltpu.VMEM((len(parts), heads, channels), f32)],
        place=place,
    )
    return (
        updated,
        alignment_gradient,
        pair_gradient,
        combined_gradient,
        output_gradient,
        pair_weight_gradient.T,
    )


def body(alignment_rows, pair_entries, combined_weight, output_weight, pair_weight, updated_gradient):
    chosen = head_body if fits_heads(alignment_rows, pair_entries, pair_weight) else gathered_body
    return chosen(
        alignment_rows, pair_entries, combined_weight, output_weight, pair_weight, updated_gradient
    )


def solution(mesh):
    return jax.shard_map(
        body,
        mesh=mesh,
        in_specs=(
            P("seq", "res", None),
            P("res", "seq", None),
            P(),
            P(),
            P(),
            P("seq", "res", None),
        ),
        out_specs=(
            P("seq", "res", None),
            P("seq", "res", None),
            P("res", "seq", None),
            P(),
            P(),
            P(),
        ),
        check_vma=False,
    )
```

```python
import functools
import math

import jax
import jax.numpy as jnp
from jax import lax
from jax.experimental import pallas as pl
from jax.experimental.pallas import tpu as pltpu
from jax.sharding import PartitionSpec as P

eps_norm = 1e-05


def layer_normalize(values):
    values = values.astype(jnp.float32)
    center = values - jnp.mean(values, axis=-1, keepdims=True)
    broadcast_pair = lax.rsqrt(jnp.mean(center * center, axis=-1, keepdims=True) + eps_norm)
    return (center * broadcast_pair, broadcast_pair)


def layer_norm_backward(normalized_gradient, normalized_rows, broadcast_pair):
    mean_grad = jnp.mean(normalized_gradient, axis=-1, keepdims=True)
    mean_cross = jnp.mean(normalized_gradient * normalized_rows, axis=-1, keepdims=True)
    return broadcast_pair * (normalized_gradient - mean_grad - normalized_rows * mean_cross)


def split_heads(tensor, head_count):
    return tensor.reshape(
        tensor.shape[0], tensor.shape[1], head_count, tensor.shape[2] // head_count
    )


def merge_heads(tensor):
    return tensor.reshape(tensor.shape[0], tensor.shape[1], tensor.shape[2] * tensor.shape[3])


def gathered_body(
    alignment_rows, pair_entries, combined_weight, output_weight, pair_weight, updated_gradient
):
    sequence_count, residue_count, alignment_width = alignment_rows.shape
    head_count = pair_weight.shape[1]
    query_width = output_weight.shape[0]
    head_dim = query_width // head_count
    column_count = pair_entries.shape[1]
    token_count = sequence_count * residue_count
    score_scale = 1.0 / math.sqrt(head_dim * sequence_count * lax.axis_size("seq"))
    normalized_rows, broadcast_pair = layer_normalize(alignment_rows)
    normalized_rows_backward = normalized_rows.astype(jnp.bfloat16).reshape(
        token_count, alignment_width
    )
    projected = jnp.dot(
        normalized_rows_backward, combined_weight, preferred_element_type=jnp.float32
    ).reshape(sequence_count, residue_count, 4 * query_width)
    queries = (projected[..., :query_width] * score_scale).astype(jnp.bfloat16)
    key_rows = projected[..., query_width : 2 * query_width].astype(jnp.bfloat16)
    value_rows = projected[..., 2 * query_width : 3 * query_width].astype(jnp.bfloat16)
    gate_open = jax.nn.sigmoid(projected[..., 3 * query_width :])
    all_keys, all_values = (
        lax.all_gather(key_rows, "res", axis=1, tiled=True),
        lax.all_gather(value_rows, "res", axis=1, tiled=True),
    )
    query_heads = split_heads(queries, head_count)
    key_heads = split_heads(all_keys, head_count)
    value_heads = split_heads(all_values, head_count)
    score_terms = jnp.einsum(
        "sihd,sjhd->hij", query_heads, key_heads, preferred_element_type=jnp.float32
    )
    pair_normed, pair_spread = layer_normalize(pair_entries)
    pair_bias = jnp.einsum("ijc,ch->hij", pair_normed, pair_weight, precision=lax.Precision.HIGHEST)
    col_start = lax.axis_index("seq") * column_count
    own_block = lax.dynamic_slice_in_dim(score_terms, col_start, column_count, 2) + pair_bias
    logits = lax.psum(lax.dynamic_update_slice_in_dim(score_terms, own_block, col_start, 2), "seq")
    row_top = jnp.max(logits, axis=-1, keepdims=True)
    lifted = jnp.exp(logits - row_top)
    softmax_out = lifted / jnp.sum(lifted, axis=-1, keepdims=True)
    softmax_low = softmax_out.astype(jnp.bfloat16)
    attended = merge_heads(
        jnp.einsum("hij,sjhd->sihd", softmax_low, value_heads, preferred_element_type=jnp.float32)
    )
    gated_out = (gate_open * attended).astype(jnp.bfloat16)
    flattened_gated = gated_out.reshape(token_count, query_width)
    updated = (
        jnp.dot(flattened_gated, output_weight, preferred_element_type=jnp.float32)
        .astype(jnp.bfloat16)
        .reshape(sequence_count, residue_count, alignment_width)
    )
    flattened_gradient = updated_gradient.reshape(token_count, alignment_width)
    grad_gated = jnp.dot(
        flattened_gradient, output_weight.T, preferred_element_type=jnp.float32
    ).reshape(sequence_count, residue_count, query_width)
    out_local = jnp.dot(flattened_gated.T, flattened_gradient, preferred_element_type=jnp.float32)
    grad_attended = (grad_gated * gate_open).astype(jnp.bfloat16)
    grad_gate_logit = grad_gated * attended * gate_open * (1.0 - gate_open)
    attended_grad_heads = split_heads(grad_attended, head_count)
    grad_terms = jnp.einsum(
        "sihd,sjhd->hij", attended_grad_heads, value_heads, preferred_element_type=jnp.float32
    )
    grad_probs = lax.psum(grad_terms, "seq")
    row_dot = jnp.sum(softmax_out * grad_probs, axis=-1, keepdims=True)
    grad_logits = softmax_out * (grad_probs - row_dot)
    grad_logits_b = grad_logits.astype(jnp.bfloat16)
    logit_share = lax.dynamic_slice_in_dim(grad_logits, col_start, column_count, 2)
    grad_query_heads = (
        jnp.einsum("hij,sjhd->sihd", grad_logits_b, key_heads, preferred_element_type=jnp.float32)
        * score_scale
    )
    key_part = jnp.einsum(
        "hij,sihd->jshd", grad_logits_b, query_heads, preferred_element_type=jnp.float32
    )
    value_part = jnp.einsum(
        "hij,sihd->jshd", softmax_low, attended_grad_heads, preferred_element_type=jnp.float32
    )
    summed = lax.psum_scatter(
        jnp.concatenate([merge_heads(key_part), merge_heads(value_part)], axis=-1),
        "res",
        scatter_dimension=0,
        tiled=True,
    )
    key_value_grads = jnp.transpose(summed, (1, 0, 2))
    projected_gradient = jnp.concatenate(
        [merge_heads(grad_query_heads), key_value_grads, grad_gate_logit], axis=-1
    )
    projected_gradient = projected_gradient.astype(jnp.bfloat16).reshape(
        token_count, 4 * query_width
    )
    qkvg_local = jnp.dot(
        normalized_rows_backward.T, projected_gradient, preferred_element_type=jnp.float32
    )
    normalized_gradient = jnp.dot(
        projected_gradient, combined_weight.T, preferred_element_type=jnp.float32
    ).reshape(sequence_count, residue_count, alignment_width)
    alignment_gradient = layer_norm_backward(
        normalized_gradient, normalized_rows, broadcast_pair
    ).astype(jnp.bfloat16)
    pair_w_local = jnp.einsum(
        "ijc,hij->ch", pair_normed, logit_share, precision=lax.Precision.HIGHEST
    )
    grad_pair_normed = jnp.einsum(
        "hij,ch->ijc", logit_share, pair_weight, precision=lax.Precision.HIGHEST
    )
    pair_gradient = layer_norm_backward(grad_pair_normed, pair_normed, pair_spread).astype(
        jnp.bfloat16
    )
    combined_weight_gradient, output_weight_gradient, pair_weight_gradient = lax.psum(
        (qkvg_local, out_local, pair_w_local), ("seq", "res")
    )
    return (
        updated,
        alignment_gradient,
        pair_gradient,
        combined_weight_gradient,
        output_weight_gradient,
        pair_weight_gradient,
    )


VMEM_LIMIT = 20 * 1024 * 1024
ARGUMENT_VMEM_LIMIT = 56 * 1024 * 1024
LANES = 128
SLOTS = 4
NT = (((1,), (1,)), ((), ()))
TN = (((0,), (0,)), ((), ()))


def f32_dot(left, right, dims=None):
    if dims is None:
        return jnp.dot(left, right, preferred_element_type=jnp.float32)
    return lax.dot_general(left, right, dims, preferred_element_type=jnp.float32)


def two_terms(values):
    high = values.astype(jnp.bfloat16)
    return high, (values - high.astype(jnp.float32)).astype(jnp.bfloat16)


def slot_select(pieces):
    slot = lax.broadcasted_iota(jnp.int32, pieces[0].shape, 1) // (LANES // SLOTS)
    result = pieces[0]
    for k in range(1, SLOTS):
        result = jnp.where(slot == k, pieces[k], result)
    return result


def pack_heads(out_ref, row, tensor, residues):
    for core in range(2):
        for tile in range(tensor.shape[1] // LANES):
            rolled = []
            for s in range(SLOTS):
                start = (core * SLOTS + s) * residues
                piece = tensor[start : start + residues, tile * LANES : (tile + 1) * LANES]
                rolled.append(pltpu.roll(piece, s * LANES // SLOTS, 1) if s else piece)
            for j in range(SLOTS):
                block = slot_select([rolled[(k - j) % SLOTS] for k in range(SLOTS)])
                out_ref[(tile * SLOTS + j) * 2 + core, row : row + residues, :] = block.astype(
                    jnp.bfloat16
                )


def unpack_heads(in_ref, row, residues, tiles):
    rows = []
    for core in range(2):
        for s in range(SLOTS):
            pieces = []
            for tile in range(tiles):
                blocks = [
                    in_ref[
                        (tile * SLOTS + (k - s) % SLOTS) * 2 + core, row : row + residues, :
                    ].astype(jnp.float32)
                    for k in range(SLOTS)
                ]
                block = slot_select(blocks)
                pieces.append(pltpu.roll(block, LANES - s * LANES // SLOTS, 1) if s else block)
            rows.append(jnp.concatenate(pieces, axis=1))
    return jnp.concatenate(rows, axis=0)


def normalized(x_ref):
    width = x_ref.shape[-1]
    values = x_ref[...].reshape(-1, width).astype(jnp.float32)
    return layer_normalize(values)


def gate_of(logits):
    return 1.0 / (1.0 + jnp.exp(-logits))


def value_kernel(x_ref, grad_ref, wc_ref, wo_ref, out_ref):
    residues, width = x_ref.shape[1], x_ref.shape[2]
    normed = normalized(x_ref)[0].astype(jnp.bfloat16)
    values = f32_dot(normed, wc_ref[:, 2 * width : 3 * width])
    gate = gate_of(f32_dot(normed, wc_ref[:, 3 * width :]))
    grad_gated = f32_dot(grad_ref[...].reshape(-1, width), wo_ref[...], NT)
    pack_heads(out_ref, 0, values, residues)
    pack_heads(out_ref, residues, grad_gated * gate, residues)


def centred(weight):
    return weight - jnp.mean(weight, axis=1, keepdims=True)


def query_kernel(
    scale, arrive, x_ref, wc_ref, pair_ref, weight_ref, out_ref, bias_ref, mean_ref, spread_ref
):
    residues, width = x_ref.shape[1], x_ref.shape[2]
    heads = weight_ref.shape[0]
    normed = normalized(x_ref)[0].astype(jnp.bfloat16)
    pack_heads(out_ref, 0, f32_dot(normed, wc_ref[:, :width]) * scale, residues)
    pack_heads(out_ref, residues, f32_dot(normed, wc_ref[:, width : 2 * width]), residues)

    arrive()
    columns, channels = pair_ref.shape[1], pair_ref.shape[2]
    weight = centred(weight_ref[...])
    first = weight.astype(jnp.bfloat16)
    second, third = two_terms(weight - first.astype(jnp.float32))
    share = jnp.full((heads, channels), 1.0 / channels, jnp.bfloat16)
    left = jnp.concatenate([first, second, third, share], axis=0)
    average = jnp.full((channels, channels), 1.0 / channels, jnp.bfloat16)
    step_rows = 64

    def rows(step, carry):
        start = pl.multiple_of(step * step_rows, step_rows)
        entries = pair_ref[pl.ds(start, step_rows)].reshape(step_rows * columns, channels)
        center = entries.astype(jnp.float32) - f32_dot(entries, average)
        high, low = two_terms(center * center)
        variance = f32_dot(share, high, NT) + f32_dot(share, low, NT)
        spread = lax.rsqrt(variance + eps_norm)
        raw = f32_dot(left, entries, NT)
        bias = spread * (raw[:heads] + raw[heads : 2 * heads] + raw[2 * heads : 3 * heads])
        for k in range(step_rows):
            lanes = slice(k * columns, (k + 1) * columns)
            bias_ref[:, start + k, :] = bias[:, lanes]
            mean_ref[pl.ds(start + k, 1), :] = raw[3 * heads : 3 * heads + 1, lanes]
            spread_ref[pl.ds(start + k, 1), :] = spread[:1, lanes]
        return carry

    lax.fori_loop(0, pair_ref.shape[0] // step_rows, rows, 0)
    half = residues // 2
    for h in range(heads):
        for core in range(2):
            high, low = two_terms(bias_ref[h, core * half : (core + 1) * half, :])
            out_ref[h * 2 + core, 2 * residues : 2 * residues + half, :] = high
            out_ref[h * 2 + core, 2 * residues + half : 3 * residues, :] = low


def lanes_of(blocks_ref, row, residues):
    count = blocks_ref.shape[0] // 2
    planes = [
        blocks_ref[p * count : (p + 1) * count, row : row + residues, :].reshape(-1, LANES)
        for p in range(2)
    ]
    return jnp.concatenate(planes, axis=1)


def score_kernel(
    residues, left_row, right_row, sent, with_bias, place_ref, own_ref, other_ref, out_ref
):
    core, half = place_ref[0], place_ref[1]
    count = own_ref.shape[0] // 2
    part = residues // 2
    right = jnp.concatenate(
        [lanes_of(own_ref, right_row, residues), lanes_of(other_ref, right_row, residues)], axis=1
    )
    which = 1 - half if sent else half
    left = []
    for k in range(count // 2):
        block = which * (count // 2) + k
        rows = pl.ds(pl.multiple_of(left_row + core * part, part), part)
        left.append(
            jnp.concatenate(
                [
                    r[p * count + block, rows, :]
                    for r in (own_ref, other_ref)
                    for p in range(2)
                ],
                axis=1,
            )
        )
    terms = f32_dot(jnp.concatenate(left, axis=0), right, NT)
    out_ref[...] = terms.astype(out_ref.dtype)
    for p in range(2 if with_bias else 0):
        columns = pl.ds(pl.multiple_of((half * 2 + p) * LANES, LANES), LANES)
        for k in range(count // 2):
            block = p * count + which * (count // 2) + k
            high = own_ref[block, 2 * residues : 2 * residues + part, :]
            low = own_ref[block, 2 * residues + part : 3 * residues, :]
            bias = high.astype(jnp.float32) + low.astype(jnp.float32)
            out_ref[k * part : (k + 1) * part, columns] += bias


def softmax_kernel(logit_ref, logit_other_ref, grad_ref, grad_other_ref, out_ref, low_ref):
    logits = logit_ref[...] + logit_other_ref[...]
    lifted = jnp.exp(logits - jnp.max(logits, axis=-1, keepdims=True))
    softmax_out = lifted / jnp.sum(lifted, axis=-1, keepdims=True)
    low_ref[...] = softmax_out.astype(jnp.bfloat16)
    grad_probs = grad_ref[...] + grad_other_ref[...].astype(jnp.float32)
    row_dot = jnp.sum(softmax_out * grad_probs, axis=-1, keepdims=True)
    out_ref[...] = (softmax_out * (grad_probs - row_dot)).astype(jnp.bfloat16)


def product_kernel(
    residues, scale, first_row, second_row, with_share,
    place_ref, own_ref, far_ref, near_ref, corner_ref, blocks_ref, out_ref, whole_ref,
):
    core, half = place_ref[0], place_ref[1]
    count = blocks_ref.shape[0] // 2
    part = residues // 2
    quarters = (
        (own_ref, core, half), (far_ref, core, 1 - half),
        (near_ref, 1 - core, half), (corner_ref, 1 - core, 1 - half),
    )
    for ref, c, z in quarters:
        for k in range(count // 2):
            start = (z * (count // 2) + k) * residues + c * part
            whole_ref[pl.ds(pl.multiple_of(start, part), part), :] = ref[k * part : (k + 1) * part, :]
    whole = whole_ref[...]
    if with_share:
        for p in range(2):
            columns = pl.ds(pl.multiple_of((half * 2 + p) * LANES, LANES), LANES)
            for q in range(count):
                rows = pl.ds(pl.multiple_of(q * residues + core * part, part), part)
                out_ref[p * count + q, 2 * residues : 2 * residues + part, :] = whole_ref[rows, columns]
    first = f32_dot(whole, lanes_of(blocks_ref, first_row, residues)) * scale
    second = f32_dot(whole, lanes_of(blocks_ref, second_row, residues), TN)
    for row, product in ((0, first), (residues, second)):
        for p in range(2):
            out_ref[p * count : (p + 1) * count, row : row + residues, :] = (
                product[:, p * LANES : (p + 1) * LANES]
                .astype(jnp.bfloat16)
                .reshape(count, residues, LANES)
            )


def share_of(blocks_ref, row, part, heads):
    return jnp.concatenate(
        [
            blocks_ref[:, row : row + part, :]
            .astype(jnp.float32)
            .reshape(heads, 2 * part, LANES)
        ],
        axis=0,
    )


def attended_weight_kernel(
    x_ref, grad_ref, wc_ref, wo_ref, blocks_ref, updated_ref, projected_ref, normed_ref, sums_ref
):
    residues, width = x_ref.shape[1], x_ref.shape[2]
    tiles = width // LANES
    normed = normalized(x_ref)[0].astype(jnp.bfloat16)
    normed_ref[...] = normed
    gate = gate_of(f32_dot(normed, wc_ref[:, 3 * width :]))
    grad = grad_ref[...].reshape(-1, width)
    grad_gated = f32_dot(grad, wo_ref[...], NT)
    attended = unpack_heads(blocks_ref, 0, residues, tiles)
    gated = (gate * attended).astype(jnp.bfloat16)
    updated_ref[...] = f32_dot(gated, wo_ref[...]).astype(jnp.bfloat16).reshape(updated_ref.shape)
    projected_ref[:, :width] = unpack_heads(blocks_ref, residues, residues, tiles).astype(
        jnp.bfloat16
    )
    projected_ref[:, width:] = (grad_gated * attended * gate * (1.0 - gate)).astype(jnp.bfloat16)
    sums_ref[:, : 2 * width] = f32_dot(normed, projected_ref[...], TN).astype(jnp.bfloat16)
    sums_ref[:, 2 * width :] = f32_dot(gated, grad, TN).astype(jnp.bfloat16)


def query_weight_kernel(
    place_ref, normed_ref, attended_sums_ref, blocks_ref,
    projected_ref, keep_ref, send_ref, sums_ref,
):
    width = normed_ref.shape[1]
    tiles, residues = width // LANES, (blocks_ref.shape[1] * 2) // 5
    core = place_ref[0]
    for t in range(2):
        projected_ref[:, t * width : (t + 1) * width] = unpack_heads(
            blocks_ref, t * residues, residues, tiles
        ).astype(jnp.bfloat16)
    sums_ref[:, : 2 * width] = f32_dot(normed_ref[...], projected_ref[...], TN).astype(
        jnp.bfloat16
    )
    sums_ref[:, 2 * width :] = attended_sums_ref[...]
    rows = keep_ref.shape[1]
    for which, ref in ((core, keep_ref), (1 - core, send_ref)):
        for block in range(keep_ref.shape[0]):
            start = pl.multiple_of((2 * block + which) * rows, rows)
            ref[block] = sums_ref[pl.ds(start, rows), :]


def core_sum_kernel(place_ref, keep_ref, other_ref, own_ref, *send_refs):
    chip = place_ref[2]
    for flip, ref in enumerate((own_ref, *send_refs)):
        block = jnp.bitwise_xor(chip, flip)
        total = keep_ref[block].astype(jnp.float32) + other_ref[block].astype(jnp.float32)
        ref[...] = total.astype(ref.dtype)


def plane_sum_kernel(own_ref, pair_weight_ref, *refs):
    *received, out_ref = refs
    total = own_ref[...]
    for ref in received:
        total += ref[...].astype(jnp.float32)
    count = own_ref.shape[1]
    heads = pair_weight_ref.shape[0]
    out_ref[:, :count] = total.astype(out_ref.dtype)
    rest = jnp.zeros((out_ref.shape[0] - heads, out_ref.shape[1] - count), jnp.float32)
    out_ref[:, count:] = jnp.concatenate([pair_weight_ref[...], rest], axis=0).astype(
        out_ref.dtype
    )


def pair_weight_kernel(blocks_ref, pair_ref, mean_ref, spread_ref, out_ref, share_ref):
    heads, part = share_ref.shape[0], pair_ref.shape[0] // 2
    share_ref[...] = share_of(blocks_ref, blocks_ref.shape[1] - part, part, heads)

    def rows(step, carry):
        total, shift = carry
        for k in range(8):
            i = step * 8 + k
            scaled = share_ref[:, i, :] * spread_ref[pl.ds(i, 1), :]
            high, low = two_terms(scaled)
            total += f32_dot(jnp.concatenate([high, low], axis=0), pair_ref[i])
            shift += (high.astype(jnp.float32) + low.astype(jnp.float32)) * mean_ref[pl.ds(i, 1), :]
        return total, shift

    channels = pair_ref.shape[2]
    total, shift = lax.fori_loop(
        0,
        pair_ref.shape[0] // 8,
        rows,
        (jnp.zeros((2 * heads, channels), jnp.float32), jnp.zeros((heads, LANES), jnp.float32)),
    )
    out_ref[...] = total[:heads] + total[heads:] - jnp.sum(shift, axis=1, keepdims=True)


def alignment_kernel(x_ref, wc_ref, query_key_ref, value_gate_ref, out_ref):
    normed, spread = normalized(x_ref)
    width = x_ref.shape[2]
    gradient = f32_dot(query_key_ref[...], wc_ref[:, : 2 * width], NT) + f32_dot(
        value_gate_ref[...], wc_ref[:, 2 * width :], NT
    )
    out_ref[...] = (
        layer_norm_backward(gradient, normed, spread).astype(jnp.bfloat16).reshape(out_ref.shape)
    )


def pair_kernel(blocks_row, blocks_ref, pair_ref, weight_ref, bias_ref, mean_ref, spread_ref, out_ref, share_ref):
    heads, channels = weight_ref.shape
    part = pair_ref.shape[0] // 2
    share_ref[...] = share_of(blocks_ref, blocks_row, part, heads)
    first, second = two_terms(centred(weight_ref[...]))
    zero = jnp.zeros((heads, channels), jnp.bfloat16)
    top = lax.broadcasted_iota(jnp.int32, (heads, channels), 0) < 2
    ones = jnp.where(top, 1.0, 0.0).astype(jnp.bfloat16)
    right = jnp.concatenate(
        [
            jnp.concatenate([first, first, second, ones, zero], axis=0),
            jnp.concatenate([zero, zero, zero, zero, ones], axis=0),
        ],
        axis=1,
    )
    row = lax.broadcasted_iota(jnp.int32, (heads, LANES), 0)

    def rows_of_two(value):
        high, low = two_terms(value)
        high, low = high.astype(jnp.float32), low.astype(jnp.float32)
        return jnp.where(row == 0, high, jnp.where(row == 1, low, 0.0)).astype(jnp.bfloat16)

    def rows(step, carry):
        for k in range(8):
            i = step * 8 + k
            gradient = share_ref[:, i, :]
            spread = spread_ref[pl.ds(i, 1), :]
            cross = jnp.sum(gradient * bias_ref[:, i, :], axis=0, keepdims=True) / channels
            slope = spread * spread * cross
            high, low = two_terms(gradient * spread)
            left = jnp.concatenate(
                [
                    high, low, high,
                    rows_of_two(jnp.broadcast_to(slope * mean_ref[pl.ds(i, 1), :], row.shape)),
                    rows_of_two(jnp.broadcast_to(slope, row.shape)),
                ],
                axis=0,
            )
            terms = f32_dot(left, right, TN)
            entries = pair_ref[i].astype(jnp.float32)
            out_ref[i] = (terms[:, :channels] - terms[:, channels:] * entries).astype(jnp.bfloat16)
        return carry

    lax.fori_loop(0, pair_ref.shape[0] // 8, rows, 0)


def output_kernel(place_ref, *refs):
    *parts, combined_ref, out_weight_ref, pair_weight_ref, shares_ref = refs
    core, chip = place_ref[0], place_ref[2]
    width = combined_ref.shape[0]
    rows = parts[0].shape[0]
    heads = pair_weight_ref.shape[0]
    for k, ref in enumerate(parts):
        owner = jnp.bitwise_xor(chip, k // 2) * 2 + jnp.bitwise_xor(core, k % 2)
        block = pl.ds(pl.multiple_of(owner * rows, rows), rows)
        part = ref[...].astype(jnp.float32)
        combined_ref[block, :] = part[:, : 4 * width]
        out_weight_ref[block, :] = part[:, 4 * width : 5 * width]
        shares_ref[owner] = part[:heads, 5 * width :]
    total = shares_ref[0]
    for k in range(1, len(parts)):
        total += shares_ref[k]
    pair_weight_ref[...] = total


def call(kernel, outs, *args, scratch=(), place=None, flops=0, after=(), outside=0, late=0):
    whole, anywhere = pl.BlockSpec(memory_space=pltpu.VMEM), pl.BlockSpec(memory_space=pl.ANY)
    specs = [anywhere] * outside + [whole] * (len(args) - outside)
    ahead = () if place is None else (place,)
    shapes = [jax.ShapeDtypeStruct(*o) for o in outs]
    moved = sum(math.prod(a.shape) * a.dtype.itemsize for a in list(args) + shapes)
    first = len(ahead) + len(args)
    last = first + len(after)

    def wrapped(*refs):
        given, rest = list(refs[:first]), refs[last:]
        if outside:
            *rest, arrived = rest
            held = rest[len(rest) - outside :]
            rest = rest[: len(rest) - outside]
            copies = []
            for k in range(outside):
                copies.append(
                    pltpu.make_async_copy(given[len(ahead) + k], held[k], arrived.at[k])
                )
                given[len(ahead) + k] = held[k]
            for copy in copies:
                copy.start()
            for copy in copies[: outside - late]:
                copy.wait()
            if late:
                given.insert(0, lambda: [copy.wait() for copy in copies[outside - late :]])
        kernel(*given, *rest)

    held = [pltpu.VMEM(a.shape, a.dtype) for a in args[:outside]]
    if outside:
        held.append(pltpu.SemaphoreType.DMA((outside,)))
    return pl.pallas_call(
        wrapped,
        out_shape=shapes,
        in_specs=[pl.BlockSpec(memory_space=pltpu.SMEM)] * len(ahead)
        + specs
        + [anywhere] * len(after),
        out_specs=[whole] * len(shapes),
        scratch_shapes=[*scratch, *held],
        compiler_params=pltpu.CompilerParams(
            vmem_limit_bytes=ARGUMENT_VMEM_LIMIT if outside else VMEM_LIMIT
        ),
        cost_estimate=pl.CostEstimate(flops=flops, bytes_accessed=moved, transcendentals=0),
    )(*ahead, *args, *after)


def swapped(mine, axis_name, distance):
    size = lax.axis_size(axis_name)
    return lax.ppermute(mine, axis_name, [(a, a ^ distance) for a in range(size)])


def fits_heads(alignment_rows, pair_entries, pair_weight):
    channels, heads = pair_weight.shape
    return (
        lax.axis_size("seq") == 4
        and lax.axis_size("res") == heads == 8
        and alignment_rows.shape[0] == 2 * SLOTS
        and alignment_rows.shape[1] == pair_entries.shape[0] == 64
        and alignment_rows.shape[2] == 2 * LANES
        and pair_entries.shape[1] == channels == LANES
    )


def head_body(
    alignment_rows, pair_entries, combined_weight, output_weight, pair_weight, updated_gradient
):
    sequences, residues, width = alignment_rows.shape
    channels, heads = pair_weight.shape
    tokens = sequences * residues
    seq_size, res_size = lax.axis_size("seq"), lax.axis_size("res")
    seq_half = seq_size // 2
    total = residues * res_size
    group = 2 * res_size
    groups = [[g * group + k for k in range(group)] for g in range(seq_half)]
    scale = 1.0 / math.sqrt(width // heads * sequences * seq_size)
    res_index, seq_index = lax.axis_index("res"), lax.axis_index("seq")
    place = jnp.stack([res_index % 2, seq_index // 2, res_index // 2]).astype(jnp.int32)
    bf16, f32 = jnp.bfloat16, jnp.float32

    def across(blocks):
        return lax.all_to_all(blocks, ("seq", "res"), 0, 0, axis_index_groups=groups, tiled=True)

    x, grad, wc, wo = alignment_rows, updated_gradient, combined_weight, output_weight
    (value_blocks,) = call(
        value_kernel, [((group, 2 * residues, LANES), bf16)], x, grad, wc, wo,
        flops=8 * tokens * width * width, outside=4,
    )
    value_blocks = across(value_blocks)
    query_blocks, bias, mean, spread = call(
        functools.partial(query_kernel, scale),
        [
            ((group, 3 * residues, LANES), bf16),
            ((heads, residues, LANES), f32),
            ((residues, LANES), f32),
            ((residues, LANES), f32),
        ],
        x, wc, pair_entries, pair_weight.T,
        flops=8 * tokens * width * width, outside=3, late=1,
    )
    value_blocks, query_blocks = lax.optimization_barrier((value_blocks, query_blocks))
    query_blocks = across(query_blocks)

    quarter = (total // 4, total)

    def scores(blocks, other, left_row, right_row, sent, with_bias, kind):
        return call(
            functools.partial(score_kernel, residues, left_row, right_row, sent, with_bias),
            [(quarter, kind)],
            blocks, other,
            place=place, flops=total * total * width,
        )[0]

    value_other = swapped(value_blocks, "res", 1)
    grad_sent = scores(value_blocks, value_other, residues, 0, True, False, bf16)
    grad_mine = scores(value_blocks, value_other, residues, 0, False, False, f32)
    grad_other = swapped(grad_sent, "seq", seq_half)
    query_blocks, grad_other = lax.optimization_barrier((query_blocks, grad_other))
    query_other = swapped(query_blocks, "res", 1)
    logit_sent = scores(query_blocks, query_other, 0, residues, True, True, f32)
    logit_mine = scores(query_blocks, query_other, 0, residues, False, True, f32)
    grad_logits, probs = call(
        softmax_kernel, [(quarter, bf16), (quarter, bf16)],
        logit_mine, swapped(logit_sent, "seq", seq_half), grad_mine, grad_other,
        flops=total * total,
    )

    def products(mine, far, blocks, first_row, second_row, with_share, factor):
        rows = 2 * residues + (residues // 2 if with_share else 0)
        (out,) = call(
            functools.partial(
                product_kernel, residues, factor, first_row, second_row, with_share
            ),
            [((group, rows, LANES), bf16)],
            mine, far, swapped(mine, "res", 1), swapped(far, "res", 1), blocks,
            scratch=[pltpu.VMEM((total, total), bf16)],
            place=place, flops=4 * total * total * width,
        )
        return out

    probs_far = swapped(probs, "seq", seq_half)
    grad_far = swapped(grad_logits, "seq", seq_half)
    attended = products(probs, probs_far, value_blocks, 0, residues, False, 1.0)
    attended_blocks = across(attended)
    grad_sums = products(grad_logits, grad_far, query_blocks, residues, 0, True, scale)
    grad_sums, attended_blocks = lax.optimization_barrier((grad_sums, attended_blocks))
    grad_blocks = across(grad_sums)

    updated, value_gate, normed, attended_sums = call(
        attended_weight_kernel,
        [
            (x.shape, bf16),
            ((tokens, 2 * width), bf16),
            ((tokens, width), bf16),
            ((width, 3 * width), bf16),
        ],
        x, grad, wc, wo, attended_blocks,
        flops=14 * tokens * width * width, outside=4,
    )
    share = pltpu.VMEM((heads, residues, LANES), f32)
    columns = 5 * width
    rows = width // res_size
    part_rows = ((res_size // 2, rows, columns), bf16)
    (pair_weight_part,) = call(
        pair_weight_kernel, [((heads, channels), f32)],
        grad_blocks, pair_entries, mean, spread,
        scratch=[share], flops=4 * tokens * width * width,
    )
    query_key, keep, send = call(
        query_weight_kernel,
        [((tokens, 2 * width), bf16), part_rows, part_rows],
        normed, attended_sums, grad_blocks,
        scratch=[pltpu.VMEM((width, columns), bf16)],
        place=place, flops=4 * tokens * width * width, after=(pair_weight_part,),
    )
    own, *sent = call(
        core_sum_kernel,
        [((rows, columns), f32)] + [((rows, columns), bf16)] * 3,
        keep, swapped(send, "res", 1), place=place,
    )
    received = [swapped(t, "res", 2 * flip) for flip, t in enumerate(sent, 1)]
    (pair_gradient,) = call(
        functools.partial(pair_kernel, 2 * residues),
        [(pair_entries.shape, bf16)],
        grad_blocks, pair_entries, pair_weight.T, bias, mean, spread,
        scratch=[share], flops=8 * tokens * width * width,
    )
    (alignment_gradient,) = call(
        alignment_kernel, [(x.shape, bf16)], x, wc, query_key, value_gate,
        flops=8 * tokens * width * width,
    )
    received, alignment_gradient = lax.optimization_barrier((received, alignment_gradient))
    (part,) = call(
        plane_sum_kernel, [((rows, columns + channels), bf16)], own, pair_weight_part, *received
    )
    def added(mine, other):
        return (mine.astype(f32) + other.astype(f32)).astype(bf16)

    other_plane = swapped(part, "seq", 1)
    part = added(part, other_plane)
    other_half = swapped(part, "seq", seq_half)
    other_half, pair_gradient = lax.optimization_barrier((other_half, pair_gradient))
    part = added(part, other_half)
    chips = [part] + [swapped(part, "res", 2 * flip) for flip in range(1, res_size // 2)]
    parts = [t for chip in chips for t in (chip, swapped(chip, "res", 1))]
    combined_gradient, output_gradient, pair_weight_gradient = call(
        output_kernel,
        [(wc.shape, f32), (wo.shape, f32), ((heads, channels), f32)],
        *parts,
        scratch=[pltpu.VMEM((len(parts), heads, channels), f32)],
        place=place,
    )
    return (
        updated,
        alignment_gradient,
        pair_gradient,
        combined_gradient,
        output_gradient,
        pair_weight_gradient.T,
    )


def body(alignment_rows, pair_entries, combined_weight, output_weight, pair_weight, updated_gradient):
    chosen = head_body if fits_heads(alignment_rows, pair_entries, pair_weight) else gathered_body
    return chosen(
        alignment_rows, pair_entries, combined_weight, output_weight, pair_weight, updated_gradient
    )


def solution(mesh):
    return jax.shard_map(
        body,
        mesh=mesh,
        in_specs=(
            P("seq", "res", None),
            P("res", "seq", None),
            P(),
            P(),
            P(),
            P("seq", "res", None),
        ),
        out_specs=(
            P("seq", "res", None),
            P("seq", "res", None),
            P("res", "seq", None),
            P(),
            P(),
            P(),
        ),
        check_vma=False,
    )
```

```python
import functools
import math

import jax
import jax.numpy as jnp
from jax import lax
from jax.experimental import pallas as pl
from jax.experimental.pallas import tpu as pltpu
from jax.sharding import PartitionSpec as P

eps_norm = 1e-05


def layer_normalize(values):
    values = values.astype(jnp.float32)
    center = values - jnp.mean(values, axis=-1, keepdims=True)
    broadcast_pair = lax.rsqrt(jnp.mean(center * center, axis=-1, keepdims=True) + eps_norm)
    return (center * broadcast_pair, broadcast_pair)


def layer_norm_backward(normalized_gradient, normalized_rows, broadcast_pair):
    mean_grad = jnp.mean(normalized_gradient, axis=-1, keepdims=True)
    mean_cross = jnp.mean(normalized_gradient * normalized_rows, axis=-1, keepdims=True)
    return broadcast_pair * (normalized_gradient - mean_grad - normalized_rows * mean_cross)


def split_heads(tensor, head_count):
    return tensor.reshape(
        tensor.shape[0], tensor.shape[1], head_count, tensor.shape[2] // head_count
    )


def merge_heads(tensor):
    return tensor.reshape(tensor.shape[0], tensor.shape[1], tensor.shape[2] * tensor.shape[3])


def gathered_body(
    alignment_rows, pair_entries, combined_weight, output_weight, pair_weight, updated_gradient
):
    sequence_count, residue_count, alignment_width = alignment_rows.shape
    head_count = pair_weight.shape[1]
    query_width = output_weight.shape[0]
    head_dim = query_width // head_count
    column_count = pair_entries.shape[1]
    token_count = sequence_count * residue_count
    score_scale = 1.0 / math.sqrt(head_dim * sequence_count * lax.axis_size("seq"))
    normalized_rows, broadcast_pair = layer_normalize(alignment_rows)
    normalized_rows_backward = normalized_rows.astype(jnp.bfloat16).reshape(
        token_count, alignment_width
    )
    projected = jnp.dot(
        normalized_rows_backward, combined_weight, preferred_element_type=jnp.float32
    ).reshape(sequence_count, residue_count, 4 * query_width)
    queries = (projected[..., :query_width] * score_scale).astype(jnp.bfloat16)
    key_rows = projected[..., query_width : 2 * query_width].astype(jnp.bfloat16)
    value_rows = projected[..., 2 * query_width : 3 * query_width].astype(jnp.bfloat16)
    gate_open = jax.nn.sigmoid(projected[..., 3 * query_width :])
    all_keys, all_values = (
        lax.all_gather(key_rows, "res", axis=1, tiled=True),
        lax.all_gather(value_rows, "res", axis=1, tiled=True),
    )
    query_heads = split_heads(queries, head_count)
    key_heads = split_heads(all_keys, head_count)
    value_heads = split_heads(all_values, head_count)
    score_terms = jnp.einsum(
        "sihd,sjhd->hij", query_heads, key_heads, preferred_element_type=jnp.float32
    )
    pair_normed, pair_spread = layer_normalize(pair_entries)
    pair_bias = jnp.einsum("ijc,ch->hij", pair_normed, pair_weight, precision=lax.Precision.HIGHEST)
    col_start = lax.axis_index("seq") * column_count
    own_block = lax.dynamic_slice_in_dim(score_terms, col_start, column_count, 2) + pair_bias
    logits = lax.psum(lax.dynamic_update_slice_in_dim(score_terms, own_block, col_start, 2), "seq")
    row_top = jnp.max(logits, axis=-1, keepdims=True)
    lifted = jnp.exp(logits - row_top)
    softmax_out = lifted / jnp.sum(lifted, axis=-1, keepdims=True)
    softmax_low = softmax_out.astype(jnp.bfloat16)
    attended = merge_heads(
        jnp.einsum("hij,sjhd->sihd", softmax_low, value_heads, preferred_element_type=jnp.float32)
    )
    gated_out = (gate_open * attended).astype(jnp.bfloat16)
    flattened_gated = gated_out.reshape(token_count, query_width)
    updated = (
        jnp.dot(flattened_gated, output_weight, preferred_element_type=jnp.float32)
        .astype(jnp.bfloat16)
        .reshape(sequence_count, residue_count, alignment_width)
    )
    flattened_gradient = updated_gradient.reshape(token_count, alignment_width)
    grad_gated = jnp.dot(
        flattened_gradient, output_weight.T, preferred_element_type=jnp.float32
    ).reshape(sequence_count, residue_count, query_width)
    out_local = jnp.dot(flattened_gated.T, flattened_gradient, preferred_element_type=jnp.float32)
    grad_attended = (grad_gated * gate_open).astype(jnp.bfloat16)
    grad_gate_logit = grad_gated * attended * gate_open * (1.0 - gate_open)
    attended_grad_heads = split_heads(grad_attended, head_count)
    grad_terms = jnp.einsum(
        "sihd,sjhd->hij", attended_grad_heads, value_heads, preferred_element_type=jnp.float32
    )
    grad_probs = lax.psum(grad_terms, "seq")
    row_dot = jnp.sum(softmax_out * grad_probs, axis=-1, keepdims=True)
    grad_logits = softmax_out * (grad_probs - row_dot)
    grad_logits_b = grad_logits.astype(jnp.bfloat16)
    logit_share = lax.dynamic_slice_in_dim(grad_logits, col_start, column_count, 2)
    grad_query_heads = (
        jnp.einsum("hij,sjhd->sihd", grad_logits_b, key_heads, preferred_element_type=jnp.float32)
        * score_scale
    )
    key_part = jnp.einsum(
        "hij,sihd->jshd", grad_logits_b, query_heads, preferred_element_type=jnp.float32
    )
    value_part = jnp.einsum(
        "hij,sihd->jshd", softmax_low, attended_grad_heads, preferred_element_type=jnp.float32
    )
    summed = lax.psum_scatter(
        jnp.concatenate([merge_heads(key_part), merge_heads(value_part)], axis=-1),
        "res",
        scatter_dimension=0,
        tiled=True,
    )
    key_value_grads = jnp.transpose(summed, (1, 0, 2))
    projected_gradient = jnp.concatenate(
        [merge_heads(grad_query_heads), key_value_grads, grad_gate_logit], axis=-1
    )
    projected_gradient = projected_gradient.astype(jnp.bfloat16).reshape(
        token_count, 4 * query_width
    )
    qkvg_local = jnp.dot(
        normalized_rows_backward.T, projected_gradient, preferred_element_type=jnp.float32
    )
    normalized_gradient = jnp.dot(
        projected_gradient, combined_weight.T, preferred_element_type=jnp.float32
    ).reshape(sequence_count, residue_count, alignment_width)
    alignment_gradient = layer_norm_backward(
        normalized_gradient, normalized_rows, broadcast_pair
    ).astype(jnp.bfloat16)
    pair_w_local = jnp.einsum(
        "ijc,hij->ch", pair_normed, logit_share, precision=lax.Precision.HIGHEST
    )
    grad_pair_normed = jnp.einsum(
        "hij,ch->ijc", logit_share, pair_weight, precision=lax.Precision.HIGHEST
    )
    pair_gradient = layer_norm_backward(grad_pair_normed, pair_normed, pair_spread).astype(
        jnp.bfloat16
    )
    combined_weight_gradient, output_weight_gradient, pair_weight_gradient = lax.psum(
        (qkvg_local, out_local, pair_w_local), ("seq", "res")
    )
    return (
        updated,
        alignment_gradient,
        pair_gradient,
        combined_weight_gradient,
        output_weight_gradient,
        pair_weight_gradient,
    )


VMEM_LIMIT = 20 * 1024 * 1024
ARGUMENT_VMEM_LIMIT = 56 * 1024 * 1024
LANES = 128
SLOTS = 4
NT = (((1,), (1,)), ((), ()))
TN = (((0,), (0,)), ((), ()))


def f32_dot(left, right, dims=None):
    if dims is None:
        return jnp.dot(left, right, preferred_element_type=jnp.float32)
    return lax.dot_general(left, right, dims, preferred_element_type=jnp.float32)


def two_terms(values):
    high = values.astype(jnp.bfloat16)
    return high, (values - high.astype(jnp.float32)).astype(jnp.bfloat16)


def slot_select(pieces):
    slot = lax.broadcasted_iota(jnp.int32, pieces[0].shape, 1) // (LANES // SLOTS)
    result = pieces[0]
    for k in range(1, SLOTS):
        result = jnp.where(slot == k, pieces[k], result)
    return result


def pack_heads(out_ref, row, tensor, residues):
    for core in range(2):
        for tile in range(tensor.shape[1] // LANES):
            rolled = []
            for s in range(SLOTS):
                start = (core * SLOTS + s) * residues
                piece = tensor[start : start + residues, tile * LANES : (tile + 1) * LANES]
                rolled.append(pltpu.roll(piece, s * LANES // SLOTS, 1) if s else piece)
            for j in range(SLOTS):
                block = slot_select([rolled[(k - j) % SLOTS] for k in range(SLOTS)])
                out_ref[(tile * SLOTS + j) * 2 + core, row : row + residues, :] = block.astype(
                    jnp.bfloat16
                )


def unpack_heads(in_ref, row, residues, tiles):
    rows = []
    for core in range(2):
        for s in range(SLOTS):
            pieces = []
            for tile in range(tiles):
                blocks = [
                    in_ref[
                        (tile * SLOTS + (k - s) % SLOTS) * 2 + core, row : row + residues, :
                    ].astype(jnp.float32)
                    for k in range(SLOTS)
                ]
                block = slot_select(blocks)
                pieces.append(pltpu.roll(block, LANES - s * LANES // SLOTS, 1) if s else block)
            rows.append(jnp.concatenate(pieces, axis=1))
    return jnp.concatenate(rows, axis=0)


def normalized(x_ref):
    width = x_ref.shape[-1]
    values = x_ref[...].reshape(-1, width).astype(jnp.float32)
    return layer_normalize(values)


def gate_of(logits):
    return 1.0 / (1.0 + jnp.exp(-logits))


def value_kernel(x_ref, grad_ref, wc_ref, wo_ref, out_ref):
    residues, width = x_ref.shape[1], x_ref.shape[2]
    normed = normalized(x_ref)[0].astype(jnp.bfloat16)
    values = f32_dot(normed, wc_ref[:, 2 * width : 3 * width])
    gate = gate_of(f32_dot(normed, wc_ref[:, 3 * width :]))
    grad_gated = f32_dot(grad_ref[...].reshape(-1, width), wo_ref[...], NT)
    pack_heads(out_ref, 0, values, residues)
    pack_heads(out_ref, residues, grad_gated * gate, residues)


def centred(weight):
    return weight - jnp.mean(weight, axis=1, keepdims=True)


def query_kernel(
    scale, arrive, x_ref, wc_ref, pair_ref, weight_ref, out_ref, bias_ref, mean_ref, spread_ref
):
    residues, width = x_ref.shape[1], x_ref.shape[2]
    heads = weight_ref.shape[0]
    normed = normalized(x_ref)[0].astype(jnp.bfloat16)
    pack_heads(out_ref, 0, f32_dot(normed, wc_ref[:, :width]) * scale, residues)
    pack_heads(out_ref, residues, f32_dot(normed, wc_ref[:, width : 2 * width]), residues)

    arrive()
    columns, channels = pair_ref.shape[1], pair_ref.shape[2]
    weight = centred(weight_ref[...])
    first = weight.astype(jnp.bfloat16)
    second, third = two_terms(weight - first.astype(jnp.float32))
    share = jnp.full((heads, channels), 1.0 / channels, jnp.bfloat16)
    left = jnp.concatenate([first, second, third, share], axis=0)
    average = jnp.full((channels, channels), 1.0 / channels, jnp.bfloat16)
    step_rows = 64

    def rows(step, carry):
        start = pl.multiple_of(step * step_rows, step_rows)
        entries = pair_ref[pl.ds(start, step_rows)].reshape(step_rows * columns, channels)
        center = entries.astype(jnp.float32) - f32_dot(entries, average)
        high, low = two_terms(center * center)
        variance = f32_dot(share, high, NT) + f32_dot(share, low, NT)
        spread = lax.rsqrt(variance + eps_norm)
        raw = f32_dot(left, entries, NT)
        bias = spread * (raw[:heads] + raw[heads : 2 * heads] + raw[2 * heads : 3 * heads])
        for k in range(step_rows):
            lanes = slice(k * columns, (k + 1) * columns)
            bias_ref[:, start + k, :] = bias[:, lanes]
            mean_ref[pl.ds(start + k, 1), :] = raw[3 * heads : 3 * heads + 1, lanes]
            spread_ref[pl.ds(start + k, 1), :] = spread[:1, lanes]
        return carry

    lax.fori_loop(0, pair_ref.shape[0] // step_rows, rows, 0)
    half = residues // 2
    for h in range(heads):
        for core in range(2):
            high, low = two_terms(bias_ref[h, core * half : (core + 1) * half, :])
            out_ref[h * 2 + core, 2 * residues : 2 * residues + half, :] = high
            out_ref[h * 2 + core, 2 * residues + half : 3 * residues, :] = low


def lanes_of(blocks_ref, row, residues):
    count = blocks_ref.shape[0] // 2
    planes = [
        blocks_ref[p * count : (p + 1) * count, row : row + residues, :].reshape(-1, LANES)
        for p in range(2)
    ]
    return jnp.concatenate(planes, axis=1)


def score_kernel(
    residues, left_row, right_row, sent, place_ref, own_ref, other_ref, out_ref
):
    core, half = place_ref[0], place_ref[1]
    count = own_ref.shape[0] // 2
    part = residues // 2
    right = jnp.concatenate(
        [lanes_of(own_ref, right_row, residues), lanes_of(other_ref, right_row, residues)], axis=1
    )
    which = 1 - half if sent else half
    left = []
    for k in range(count // 2):
        block = which * (count // 2) + k
        rows = pl.ds(pl.multiple_of(left_row + core * part, part), part)
        left.append(
            jnp.concatenate(
                [
                    r[p * count + block, rows, :]
                    for r in (own_ref, other_ref)
                    for p in range(2)
                ],
                axis=1,
            )
        )
    out_ref[...] = f32_dot(jnp.concatenate(left, axis=0), right, NT)
    for p in range(2):
        columns = pl.ds(pl.multiple_of((half * 2 + p) * LANES, LANES), LANES)
        for k in range(count // 2):
            block = p * count + which * (count // 2) + k
            high = own_ref[block, 2 * residues : 2 * residues + part, :]
            low = own_ref[block, 2 * residues + part : 3 * residues, :]
            bias = high.astype(jnp.float32) + low.astype(jnp.float32)
            out_ref[k * part : (k + 1) * part, columns] += bias


def softmax_kernel(logit_ref, other_ref, out_ref, low_ref):
    logits = logit_ref[...] + other_ref[...]
    lifted = jnp.exp(logits - jnp.max(logits, axis=-1, keepdims=True))
    softmax_out = lifted / jnp.sum(lifted, axis=-1, keepdims=True)
    out_ref[...] = softmax_out
    low_ref[...] = softmax_out.astype(jnp.bfloat16)


def grad_score_kernel(
    residues, left_row, right_row, place_ref, own_ref, other_ref, full_ref, sent_ref
):
    core = place_ref[0]
    count = own_ref.shape[0] // 2
    part = residues // 2
    right = jnp.concatenate(
        [lanes_of(own_ref, right_row, residues), lanes_of(other_ref, right_row, residues)], axis=1
    )
    rows = pl.ds(pl.multiple_of(left_row + core * part, part), part)
    left = [
        jnp.concatenate(
            [r[p * count + k, rows, :] for r in (own_ref, other_ref) for p in range(2)], axis=1
        )
        for k in range(count)
    ]
    terms = f32_dot(jnp.concatenate(left, axis=0), right, NT)
    full_ref[...] = terms
    sent_ref[...] = terms.astype(jnp.bfloat16)


def softmax_gradient_kernel(
    place_ref, softmax_ref, far_ref, grad_ref, other_ref, out_ref, out_far_ref
):
    half = place_ref[1]
    count = softmax_ref.shape[0]
    for which, probs, ref in ((half, softmax_ref, out_ref), (1 - half, far_ref, out_far_ref)):
        rows = pl.ds(pl.multiple_of(which * count, count), count)
        softmax_out = probs[...].astype(jnp.float32)
        grad_probs = grad_ref[rows, :] + other_ref[rows, :].astype(jnp.float32)
        row_dot = jnp.sum(softmax_out * grad_probs, axis=-1, keepdims=True)
        ref[...] = (softmax_out * (grad_probs - row_dot)).astype(jnp.bfloat16)


def product_kernel(
    residues, scale, first_row, second_row, with_share,
    place_ref, own_ref, far_ref, near_ref, corner_ref, blocks_ref, out_ref, whole_ref,
):
    core, half = place_ref[0], place_ref[1]
    count = blocks_ref.shape[0] // 2
    part = residues // 2
    quarters = (
        (own_ref, core, half), (far_ref, core, 1 - half),
        (near_ref, 1 - core, half), (corner_ref, 1 - core, 1 - half),
    )
    for ref, c, z in quarters:
        for k in range(count // 2):
            start = (z * (count // 2) + k) * residues + c * part
            whole_ref[pl.ds(pl.multiple_of(start, part), part), :] = ref[k * part : (k + 1) * part, :]
    whole = whole_ref[...]
    if with_share:
        for p in range(2):
            columns = pl.ds(pl.multiple_of((half * 2 + p) * LANES, LANES), LANES)
            for q in range(count):
                rows = pl.ds(pl.multiple_of(q * residues + core * part, part), part)
                out_ref[p * count + q, 2 * residues : 2 * residues + part, :] = whole_ref[rows, columns]
    first = f32_dot(whole, lanes_of(blocks_ref, first_row, residues)) * scale
    second = f32_dot(whole, lanes_of(blocks_ref, second_row, residues), TN)
    for row, product in ((0, first), (residues, second)):
        for p in range(2):
            out_ref[p * count : (p + 1) * count, row : row + residues, :] = (
                product[:, p * LANES : (p + 1) * LANES]
                .astype(jnp.bfloat16)
                .reshape(count, residues, LANES)
            )


def share_of(blocks_ref, row, part, heads):
    return jnp.concatenate(
        [
            blocks_ref[:, row : row + part, :]
            .astype(jnp.float32)
            .reshape(heads, 2 * part, LANES)
        ],
        axis=0,
    )


def attended_weight_kernel(
    x_ref, grad_ref, wc_ref, wo_ref, blocks_ref, updated_ref, projected_ref, normed_ref, sums_ref
):
    residues, width = x_ref.shape[1], x_ref.shape[2]
    tiles = width // LANES
    normed = normalized(x_ref)[0].astype(jnp.bfloat16)
    normed_ref[...] = normed
    gate = gate_of(f32_dot(normed, wc_ref[:, 3 * width :]))
    grad = grad_ref[...].reshape(-1, width)
    grad_gated = f32_dot(grad, wo_ref[...], NT)
    attended = unpack_heads(blocks_ref, 0, residues, tiles)
    gated = (gate * attended).astype(jnp.bfloat16)
    updated_ref[...] = f32_dot(gated, wo_ref[...]).astype(jnp.bfloat16).reshape(updated_ref.shape)
    projected_ref[:, :width] = unpack_heads(blocks_ref, residues, residues, tiles).astype(
        jnp.bfloat16
    )
    projected_ref[:, width:] = (grad_gated * attended * gate * (1.0 - gate)).astype(jnp.bfloat16)
    sums_ref[:, : 2 * width] = f32_dot(normed, projected_ref[...], TN).astype(jnp.bfloat16)
    sums_ref[:, 2 * width :] = f32_dot(gated, grad, TN).astype(jnp.bfloat16)


def query_weight_kernel(
    place_ref, normed_ref, attended_sums_ref, blocks_ref,
    projected_ref, keep_ref, send_ref, sums_ref,
):
    width = normed_ref.shape[1]
    tiles, residues = width // LANES, (blocks_ref.shape[1] * 2) // 5
    core = place_ref[0]
    for t in range(2):
        projected_ref[:, t * width : (t + 1) * width] = unpack_heads(
            blocks_ref, t * residues, residues, tiles
        ).astype(jnp.bfloat16)
    sums_ref[:, : 2 * width] = f32_dot(normed_ref[...], projected_ref[...], TN).astype(
        jnp.bfloat16
    )
    sums_ref[:, 2 * width :] = attended_sums_ref[...]
    rows = keep_ref.shape[1]
    for which, ref in ((core, keep_ref), (1 - core, send_ref)):
        for block in range(keep_ref.shape[0]):
            start = pl.multiple_of((2 * block + which) * rows, rows)
            ref[block] = sums_ref[pl.ds(start, rows), :]


def core_sum_kernel(place_ref, keep_ref, other_ref, own_ref, *send_refs):
    chip = place_ref[2]
    for flip, ref in enumerate((own_ref, *send_refs)):
        block = jnp.bitwise_xor(chip, flip)
        total = keep_ref[block].astype(jnp.float32) + other_ref[block].astype(jnp.float32)
        ref[...] = total.astype(ref.dtype)


def plane_sum_kernel(own_ref, pair_weight_ref, *refs):
    *received, out_ref = refs
    total = own_ref[...]
    for ref in received:
        total += ref[...].astype(jnp.float32)
    count = own_ref.shape[1]
    heads = pair_weight_ref.shape[0]
    out_ref[:, :count] = total.astype(out_ref.dtype)
    rest = jnp.zeros((out_ref.shape[0] - heads, out_ref.shape[1] - count), jnp.float32)
    out_ref[:, count:] = jnp.concatenate([pair_weight_ref[...], rest], axis=0).astype(
        out_ref.dtype
    )


def pair_weight_kernel(blocks_ref, pair_ref, mean_ref, spread_ref, out_ref, share_ref):
    heads, part = share_ref.shape[0], pair_ref.shape[0] // 2
    share_ref[...] = share_of(blocks_ref, blocks_ref.shape[1] - part, part, heads)

    def rows(step, carry):
        total, shift = carry
        for k in range(8):
            i = step * 8 + k
            scaled = share_ref[:, i, :] * spread_ref[pl.ds(i, 1), :]
            high, low = two_terms(scaled)
            total += f32_dot(jnp.concatenate([high, low], axis=0), pair_ref[i])
            shift += (high.astype(jnp.float32) + low.astype(jnp.float32)) * mean_ref[pl.ds(i, 1), :]
        return total, shift

    channels = pair_ref.shape[2]
    total, shift = lax.fori_loop(
        0,
        pair_ref.shape[0] // 8,
        rows,
        (jnp.zeros((2 * heads, channels), jnp.float32), jnp.zeros((heads, LANES), jnp.float32)),
    )
    out_ref[...] = total[:heads] + total[heads:] - jnp.sum(shift, axis=1, keepdims=True)


def alignment_kernel(x_ref, wc_ref, query_key_ref, value_gate_ref, out_ref):
    normed, spread = normalized(x_ref)
    width = x_ref.shape[2]
    gradient = f32_dot(query_key_ref[...], wc_ref[:, : 2 * width], NT) + f32_dot(
        value_gate_ref[...], wc_ref[:, 2 * width :], NT
    )
    out_ref[...] = (
        layer_norm_backward(gradient, normed, spread).astype(jnp.bfloat16).reshape(out_ref.shape)
    )


def pair_kernel(blocks_row, blocks_ref, pair_ref, weight_ref, bias_ref, mean_ref, spread_ref, out_ref, share_ref):
    heads, channels = weight_ref.shape
    part = pair_ref.shape[0] // 2
    share_ref[...] = share_of(blocks_ref, blocks_row, part, heads)
    first, second = two_terms(centred(weight_ref[...]))
    zero = jnp.zeros((heads, channels), jnp.bfloat16)
    top = lax.broadcasted_iota(jnp.int32, (heads, channels), 0) < 2
    ones = jnp.where(top, 1.0, 0.0).astype(jnp.bfloat16)
    right = jnp.concatenate(
        [
            jnp.concatenate([first, first, second, ones, zero], axis=0),
            jnp.concatenate([zero, zero, zero, zero, ones], axis=0),
        ],
        axis=1,
    )
    row = lax.broadcasted_iota(jnp.int32, (heads, LANES), 0)

    def rows_of_two(value):
        high, low = two_terms(value)
        high, low = high.astype(jnp.float32), low.astype(jnp.float32)
        return jnp.where(row == 0, high, jnp.where(row == 1, low, 0.0)).astype(jnp.bfloat16)

    def rows(step, carry):
        for k in range(8):
            i = step * 8 + k
            gradient = share_ref[:, i, :]
            spread = spread_ref[pl.ds(i, 1), :]
            cross = jnp.sum(gradient * bias_ref[:, i, :], axis=0, keepdims=True) / channels
            slope = spread * spread * cross
            high, low = two_terms(gradient * spread)
            left = jnp.concatenate(
                [
                    high, low, high,
                    rows_of_two(jnp.broadcast_to(slope * mean_ref[pl.ds(i, 1), :], row.shape)),
                    rows_of_two(jnp.broadcast_to(slope, row.shape)),
                ],
                axis=0,
            )
            terms = f32_dot(left, right, TN)
            entries = pair_ref[i].astype(jnp.float32)
            out_ref[i] = (terms[:, :channels] - terms[:, channels:] * entries).astype(jnp.bfloat16)
        return carry

    lax.fori_loop(0, pair_ref.shape[0] // 8, rows, 0)


def output_kernel(place_ref, *refs):
    *parts, combined_ref, out_weight_ref, pair_weight_ref, shares_ref = refs
    core, chip = place_ref[0], place_ref[2]
    width = combined_ref.shape[0]
    rows = parts[0].shape[0]
    heads = pair_weight_ref.shape[0]
    for k, ref in enumerate(parts):
        owner = jnp.bitwise_xor(chip, k // 2) * 2 + jnp.bitwise_xor(core, k % 2)
        block = pl.ds(pl.multiple_of(owner * rows, rows), rows)
        part = ref[...].astype(jnp.float32)
        combined_ref[block, :] = part[:, : 4 * width]
        out_weight_ref[block, :] = part[:, 4 * width : 5 * width]
        shares_ref[owner] = part[:heads, 5 * width :]
    total = shares_ref[0]
    for k in range(1, len(parts)):
        total += shares_ref[k]
    pair_weight_ref[...] = total


def call(kernel, outs, *args, scratch=(), place=None, flops=0, after=(), outside=0, late=0):
    whole, anywhere = pl.BlockSpec(memory_space=pltpu.VMEM), pl.BlockSpec(memory_space=pl.ANY)
    specs = [anywhere] * outside + [whole] * (len(args) - outside)
    ahead = () if place is None else (place,)
    shapes = [jax.ShapeDtypeStruct(*o) for o in outs]
    moved = sum(math.prod(a.shape) * a.dtype.itemsize for a in list(args) + shapes)
    first = len(ahead) + len(args)
    last = first + len(after)

    def wrapped(*refs):
        given, rest = list(refs[:first]), refs[last:]
        if outside:
            *rest, arrived = rest
            held = rest[len(rest) - outside :]
            rest = rest[: len(rest) - outside]
            copies = []
            for k in range(outside):
                copies.append(
                    pltpu.make_async_copy(given[len(ahead) + k], held[k], arrived.at[k])
                )
                given[len(ahead) + k] = held[k]
            for copy in copies:
                copy.start()
            for copy in copies[: outside - late]:
                copy.wait()
            if late:
                given.insert(0, lambda: [copy.wait() for copy in copies[outside - late :]])
        kernel(*given, *rest)

    held = [pltpu.VMEM(a.shape, a.dtype) for a in args[:outside]]
    if outside:
        held.append(pltpu.SemaphoreType.DMA((outside,)))
    return pl.pallas_call(
        wrapped,
        out_shape=shapes,
        in_specs=[pl.BlockSpec(memory_space=pltpu.SMEM)] * len(ahead)
        + specs
        + [anywhere] * len(after),
        out_specs=[whole] * len(shapes),
        scratch_shapes=[*scratch, *held],
        compiler_params=pltpu.CompilerParams(
            vmem_limit_bytes=ARGUMENT_VMEM_LIMIT if outside else VMEM_LIMIT
        ),
        cost_estimate=pl.CostEstimate(flops=flops, bytes_accessed=moved, transcendentals=0),
    )(*ahead, *args, *after)


def swapped(mine, axis_name, distance):
    size = lax.axis_size(axis_name)
    return lax.ppermute(mine, axis_name, [(a, a ^ distance) for a in range(size)])


def fits_heads(alignment_rows, pair_entries, pair_weight):
    channels, heads = pair_weight.shape
    return (
        lax.axis_size("seq") == 4
        and lax.axis_size("res") == heads == 8
        and alignment_rows.shape[0] == 2 * SLOTS
        and alignment_rows.shape[1] == pair_entries.shape[0] == 64
        and alignment_rows.shape[2] == 2 * LANES
        and pair_entries.shape[1] == channels == LANES
    )


def head_body(
    alignment_rows, pair_entries, combined_weight, output_weight, pair_weight, updated_gradient
):
    sequences, residues, width = alignment_rows.shape
    channels, heads = pair_weight.shape
    tokens = sequences * residues
    seq_size, res_size = lax.axis_size("seq"), lax.axis_size("res")
    seq_half = seq_size // 2
    total = residues * res_size
    group = 2 * res_size
    groups = [[g * group + k for k in range(group)] for g in range(seq_half)]
    scale = 1.0 / math.sqrt(width // heads * sequences * seq_size)
    res_index, seq_index = lax.axis_index("res"), lax.axis_index("seq")
    place = jnp.stack([res_index % 2, seq_index // 2, res_index // 2]).astype(jnp.int32)
    bf16, f32 = jnp.bfloat16, jnp.float32

    def across(blocks):
        return lax.all_to_all(blocks, ("seq", "res"), 0, 0, axis_index_groups=groups, tiled=True)

    x, grad, wc, wo = alignment_rows, updated_gradient, combined_weight, output_weight
    (value_blocks,) = call(
        value_kernel, [((group, 2 * residues, LANES), bf16)], x, grad, wc, wo,
        flops=8 * tokens * width * width, outside=4,
    )
    value_blocks = across(value_blocks)
    query_blocks, bias, mean, spread = call(
        functools.partial(query_kernel, scale),
        [
            ((group, 3 * residues, LANES), bf16),
            ((heads, residues, LANES), f32),
            ((residues, LANES), f32),
            ((residues, LANES), f32),
        ],
        x, wc, pair_entries, pair_weight.T,
        flops=8 * tokens * width * width, outside=3, late=1,
    )
    value_blocks, query_blocks = lax.optimization_barrier((value_blocks, query_blocks))
    query_blocks = across(query_blocks)

    quarter, half_rows = (total // 4, total), (total // 2, total)
    grad_full, grad_sent = call(
        functools.partial(grad_score_kernel, residues, residues, 0),
        [(half_rows, f32), (half_rows, bf16)],
        value_blocks, swapped(value_blocks, "res", 1),
        place=place, flops=2 * total * total * width,
    )
    grad_other = swapped(grad_sent, "seq", seq_half)
    query_blocks, grad_other = lax.optimization_barrier((query_blocks, grad_other))
    query_other = swapped(query_blocks, "res", 1)

    def scores(sent):
        return call(
            functools.partial(score_kernel, residues, 0, residues, sent), [(quarter, f32)],
            query_blocks, query_other,
            place=place, flops=total * total * width,
        )[0]

    logit_sent, logit_mine = scores(True), scores(False)
    softmax_out, probs = call(
        softmax_kernel, [(quarter, f32), (quarter, bf16)],
        logit_mine, swapped(logit_sent, "seq", seq_half),
        flops=total * total,
    )

    def products(mine, far, blocks, first_row, second_row, with_share, factor):
        rows = 2 * residues + (residues // 2 if with_share else 0)
        (out,) = call(
            functools.partial(
                product_kernel, residues, factor, first_row, second_row, with_share
            ),
            [((group, rows, LANES), bf16)],
            mine, far, swapped(mine, "res", 1), swapped(far, "res", 1), blocks,
            scratch=[pltpu.VMEM((total, total), bf16)],
            place=place, flops=4 * total * total * width,
        )
        return out

    probs_far = swapped(probs, "seq", seq_half)
    attended = products(probs, probs_far, value_blocks, 0, residues, False, 1.0)
    attended_blocks = across(attended)
    softmax_out = lax.optimization_barrier((attended, softmax_out))[1]
    grad_logits, grad_far = call(
        softmax_gradient_kernel, [(quarter, bf16), (quarter, bf16)],
        softmax_out, probs_far, grad_full, grad_other,
        place=place, flops=total * total,
    )
    grad_sums = products(grad_logits, grad_far, query_blocks, residues, 0, True, scale)
    grad_sums, attended_blocks = lax.optimization_barrier((grad_sums, attended_blocks))
    grad_blocks = across(grad_sums)

    updated, value_gate, normed, attended_sums = call(
        attended_weight_kernel,
        [
            (x.shape, bf16),
            ((tokens, 2 * width), bf16),
            ((tokens, width), bf16),
            ((width, 3 * width), bf16),
        ],
        x, grad, wc, wo, attended_blocks,
        flops=14 * tokens * width * width, outside=4,
    )
    share = pltpu.VMEM((heads, residues, LANES), f32)
    columns = 5 * width
    rows = width // res_size
    part_rows = ((res_size // 2, rows, columns), bf16)
    (pair_weight_part,) = call(
        pair_weight_kernel, [((heads, channels), f32)],
        grad_blocks, pair_entries, mean, spread,
        scratch=[share], flops=4 * tokens * width * width,
    )
    query_key, keep, send = call(
        query_weight_kernel,
        [((tokens, 2 * width), bf16), part_rows, part_rows],
        normed, attended_sums, grad_blocks,
        scratch=[pltpu.VMEM((width, columns), bf16)],
        place=place, flops=4 * tokens * width * width, after=(pair_weight_part,),
    )
    own, *sent = call(
        core_sum_kernel,
        [((rows, columns), f32)] + [((rows, columns), bf16)] * 3,
        keep, swapped(send, "res", 1), place=place,
    )
    received = [swapped(t, "res", 2 * flip) for flip, t in enumerate(sent, 1)]
    (pair_gradient,) = call(
        functools.partial(pair_kernel, 2 * residues),
        [(pair_entries.shape, bf16)],
        grad_blocks, pair_entries, pair_weight.T, bias, mean, spread,
        scratch=[share], flops=8 * tokens * width * width,
    )
    (alignment_gradient,) = call(
        alignment_kernel, [(x.shape, bf16)], x, wc, query_key, value_gate,
        flops=8 * tokens * width * width,
    )
    received, alignment_gradient = lax.optimization_barrier((received, alignment_gradient))
    (part,) = call(
        plane_sum_kernel, [((rows, columns + channels), bf16)], own, pair_weight_part, *received
    )
    def added(mine, other):
        return (mine.astype(f32) + other.astype(f32)).astype(bf16)

    other_plane = swapped(part, "seq", 1)
    part = added(part, other_plane)
    other_half = swapped(part, "seq", seq_half)
    other_half, pair_gradient = lax.optimization_barrier((other_half, pair_gradient))
    part = added(part, other_half)
    beside = swapped(part, "res", 2)
    chips = [part, beside, swapped(part, "res", 4), swapped(beside, "res", 4)]
    parts = [t for chip in chips for t in (chip, swapped(chip, "res", 1))]
    combined_gradient, output_gradient, pair_weight_gradient = call(
        output_kernel,
        [(wc.shape, f32), (wo.shape, f32), ((heads, channels), f32)],
        *parts,
        scratch=[pltpu.VMEM((len(parts), heads, channels), f32)],
        place=place,
    )
    return (
        updated,
        alignment_gradient,
        pair_gradient,
        combined_gradient,
        output_gradient,
        pair_weight_gradient.T,
    )


def body(alignment_rows, pair_entries, combined_weight, output_weight, pair_weight, updated_gradient):
    chosen = head_body if fits_heads(alignment_rows, pair_entries, pair_weight) else gathered_body
    return chosen(
        alignment_rows, pair_entries, combined_weight, output_weight, pair_weight, updated_gradient
    )


def solution(mesh):
    return jax.shard_map(
        body,
        mesh=mesh,
        in_specs=(
            P("seq", "res", None),
            P("res", "seq", None),
            P(),
            P(),
            P(),
            P("seq", "res", None),
        ),
        out_specs=(
            P("seq", "res", None),
            P("seq", "res", None),
            P("res", "seq", None),
            P(),
            P(),
            P(),
        ),
        check_vma=False,
    )
```

```python
import functools
import math

import jax
import jax.numpy as jnp
from jax import lax
from jax.experimental import pallas as pl
from jax.experimental.pallas import tpu as pltpu
from jax.sharding import PartitionSpec as P

eps_norm = 1e-05


def layer_normalize(values):
    values = values.astype(jnp.float32)
    center = values - jnp.mean(values, axis=-1, keepdims=True)
    broadcast_pair = lax.rsqrt(jnp.mean(center * center, axis=-1, keepdims=True) + eps_norm)
    return (center * broadcast_pair, broadcast_pair)


def layer_norm_backward(normalized_gradient, normalized_rows, broadcast_pair):
    mean_grad = jnp.mean(normalized_gradient, axis=-1, keepdims=True)
    mean_cross = jnp.mean(normalized_gradient * normalized_rows, axis=-1, keepdims=True)
    return broadcast_pair * (normalized_gradient - mean_grad - normalized_rows * mean_cross)


def split_heads(tensor, head_count):
    return tensor.reshape(
        tensor.shape[0], tensor.shape[1], head_count, tensor.shape[2] // head_count
    )


def merge_heads(tensor):
    return tensor.reshape(tensor.shape[0], tensor.shape[1], tensor.shape[2] * tensor.shape[3])


def gathered_body(
    alignment_rows, pair_entries, combined_weight, output_weight, pair_weight, updated_gradient
):
    sequence_count, residue_count, alignment_width = alignment_rows.shape
    head_count = pair_weight.shape[1]
    query_width = output_weight.shape[0]
    head_dim = query_width // head_count
    column_count = pair_entries.shape[1]
    token_count = sequence_count * residue_count
    score_scale = 1.0 / math.sqrt(head_dim * sequence_count * lax.axis_size("seq"))
    normalized_rows, broadcast_pair = layer_normalize(alignment_rows)
    normalized_rows_backward = normalized_rows.astype(jnp.bfloat16).reshape(
        token_count, alignment_width
    )
    projected = jnp.dot(
        normalized_rows_backward, combined_weight, preferred_element_type=jnp.float32
    ).reshape(sequence_count, residue_count, 4 * query_width)
    queries = (projected[..., :query_width] * score_scale).astype(jnp.bfloat16)
    key_rows = projected[..., query_width : 2 * query_width].astype(jnp.bfloat16)
    value_rows = projected[..., 2 * query_width : 3 * query_width].astype(jnp.bfloat16)
    gate_open = jax.nn.sigmoid(projected[..., 3 * query_width :])
    all_keys, all_values = (
        lax.all_gather(key_rows, "res", axis=1, tiled=True),
        lax.all_gather(value_rows, "res", axis=1, tiled=True),
    )
    query_heads = split_heads(queries, head_count)
    key_heads = split_heads(all_keys, head_count)
    value_heads = split_heads(all_values, head_count)
    score_terms = jnp.einsum(
        "sihd,sjhd->hij", query_heads, key_heads, preferred_element_type=jnp.float32
    )
    pair_normed, pair_spread = layer_normalize(pair_entries)
    pair_bias = jnp.einsum("ijc,ch->hij", pair_normed, pair_weight, precision=lax.Precision.HIGHEST)
    col_start = lax.axis_index("seq") * column_count
    own_block = lax.dynamic_slice_in_dim(score_terms, col_start, column_count, 2) + pair_bias
    logits = lax.psum(lax.dynamic_update_slice_in_dim(score_terms, own_block, col_start, 2), "seq")
    row_top = jnp.max(logits, axis=-1, keepdims=True)
    lifted = jnp.exp(logits - row_top)
    softmax_out = lifted / jnp.sum(lifted, axis=-1, keepdims=True)
    softmax_low = softmax_out.astype(jnp.bfloat16)
    attended = merge_heads(
        jnp.einsum("hij,sjhd->sihd", softmax_low, value_heads, preferred_element_type=jnp.float32)
    )
    gated_out = (gate_open * attended).astype(jnp.bfloat16)
    flattened_gated = gated_out.reshape(token_count, query_width)
    updated = (
        jnp.dot(flattened_gated, output_weight, preferred_element_type=jnp.float32)
        .astype(jnp.bfloat16)
        .reshape(sequence_count, residue_count, alignment_width)
    )
    flattened_gradient = updated_gradient.reshape(token_count, alignment_width)
    grad_gated = jnp.dot(
        flattened_gradient, output_weight.T, preferred_element_type=jnp.float32
    ).reshape(sequence_count, residue_count, query_width)
    out_local = jnp.dot(flattened_gated.T, flattened_gradient, preferred_element_type=jnp.float32)
    grad_attended = (grad_gated * gate_open).astype(jnp.bfloat16)
    grad_gate_logit = grad_gated * attended * gate_open * (1.0 - gate_open)
    attended_grad_heads = split_heads(grad_attended, head_count)
    grad_terms = jnp.einsum(
        "sihd,sjhd->hij", attended_grad_heads, value_heads, preferred_element_type=jnp.float32
    )
    grad_probs = lax.psum(grad_terms, "seq")
    row_dot = jnp.sum(softmax_out * grad_probs, axis=-1, keepdims=True)
    grad_logits = softmax_out * (grad_probs - row_dot)
    grad_logits_b = grad_logits.astype(jnp.bfloat16)
    logit_share = lax.dynamic_slice_in_dim(grad_logits, col_start, column_count, 2)
    grad_query_heads = (
        jnp.einsum("hij,sjhd->sihd", grad_logits_b, key_heads, preferred_element_type=jnp.float32)
        * score_scale
    )
    key_part = jnp.einsum(
        "hij,sihd->jshd", grad_logits_b, query_heads, preferred_element_type=jnp.float32
    )
    value_part = jnp.einsum(
        "hij,sihd->jshd", softmax_low, attended_grad_heads, preferred_element_type=jnp.float32
    )
    summed = lax.psum_scatter(
        jnp.concatenate([merge_heads(key_part), merge_heads(value_part)], axis=-1),
        "res",
        scatter_dimension=0,
        tiled=True,
    )
    key_value_grads = jnp.transpose(summed, (1, 0, 2))
    projected_gradient = jnp.concatenate(
        [merge_heads(grad_query_heads), key_value_grads, grad_gate_logit], axis=-1
    )
    projected_gradient = projected_gradient.astype(jnp.bfloat16).reshape(
        token_count, 4 * query_width
    )
    qkvg_local = jnp.dot(
        normalized_rows_backward.T, projected_gradient, preferred_element_type=jnp.float32
    )
    normalized_gradient = jnp.dot(
        projected_gradient, combined_weight.T, preferred_element_type=jnp.float32
    ).reshape(sequence_count, residue_count, alignment_width)
    alignment_gradient = layer_norm_backward(
        normalized_gradient, normalized_rows, broadcast_pair
    ).astype(jnp.bfloat16)
    pair_w_local = jnp.einsum(
        "ijc,hij->ch", pair_normed, logit_share, precision=lax.Precision.HIGHEST
    )
    grad_pair_normed = jnp.einsum(
        "hij,ch->ijc", logit_share, pair_weight, precision=lax.Precision.HIGHEST
    )
    pair_gradient = layer_norm_backward(grad_pair_normed, pair_normed, pair_spread).astype(
        jnp.bfloat16
    )
    combined_weight_gradient, output_weight_gradient, pair_weight_gradient = lax.psum(
        (qkvg_local, out_local, pair_w_local), ("seq", "res")
    )
    return (
        updated,
        alignment_gradient,
        pair_gradient,
        combined_weight_gradient,
        output_weight_gradient,
        pair_weight_gradient,
    )


VMEM_LIMIT = 20 * 1024 * 1024
ARGUMENT_VMEM_LIMIT = 56 * 1024 * 1024
LANES = 128
SLOTS = 4
NT = (((1,), (1,)), ((), ()))
TN = (((0,), (0,)), ((), ()))


def f32_dot(left, right, dims=None):
    if dims is None:
        return jnp.dot(left, right, preferred_element_type=jnp.float32)
    return lax.dot_general(left, right, dims, preferred_element_type=jnp.float32)


def two_terms(values):
    high = values.astype(jnp.bfloat16)
    return high, (values - high.astype(jnp.float32)).astype(jnp.bfloat16)


def slot_select(pieces):
    slot = lax.broadcasted_iota(jnp.int32, pieces[0].shape, 1) // (LANES // SLOTS)
    result = pieces[0]
    for k in range(1, SLOTS):
        result = jnp.where(slot == k, pieces[k], result)
    return result


def pack_heads(out_ref, row, tensor, residues):
    for core in range(2):
        for tile in range(tensor.shape[1] // LANES):
            rolled = []
            for s in range(SLOTS):
                start = (core * SLOTS + s) * residues
                piece = tensor[start : start + residues, tile * LANES : (tile + 1) * LANES]
                rolled.append(pltpu.roll(piece, s * LANES // SLOTS, 1) if s else piece)
            for j in range(SLOTS):
                block = slot_select([rolled[(k - j) % SLOTS] for k in range(SLOTS)])
                out_ref[(tile * SLOTS + j) * 2 + core, row : row + residues, :] = block.astype(
                    jnp.bfloat16
                )


def unpack_heads(in_ref, row, residues, tiles):
    rows = []
    for core in range(2):
        for s in range(SLOTS):
            pieces = []
            for tile in range(tiles):
                blocks = [
                    in_ref[
                        (tile * SLOTS + (k - s) % SLOTS) * 2 + core, row : row + residues, :
                    ].astype(jnp.float32)
                    for k in range(SLOTS)
                ]
                block = slot_select(blocks)
                pieces.append(pltpu.roll(block, LANES - s * LANES // SLOTS, 1) if s else block)
            rows.append(jnp.concatenate(pieces, axis=1))
    return jnp.concatenate(rows, axis=0)


def normalized(x_ref):
    width = x_ref.shape[-1]
    values = x_ref[...].reshape(-1, width).astype(jnp.float32)
    return layer_normalize(values)


def gate_of(logits):
    return 1.0 / (1.0 + jnp.exp(-logits))


def value_kernel(arrive, x_ref, grad_ref, wc_ref, wo_ref, out_ref):
    residues, width = x_ref.shape[1], x_ref.shape[2]
    normed = normalized(x_ref)[0].astype(jnp.bfloat16)
    arrive()
    values = f32_dot(normed, wc_ref[:, 2 * width : 3 * width])
    gate = gate_of(f32_dot(normed, wc_ref[:, 3 * width :]))
    grad_gated = f32_dot(grad_ref[...].reshape(-1, width), wo_ref[...], NT)
    pack_heads(out_ref, 0, values, residues)
    pack_heads(out_ref, residues, grad_gated * gate, residues)


def centred(weight):
    return weight - jnp.mean(weight, axis=1, keepdims=True)


def query_kernel(
    scale, arrive, x_ref, wc_ref, pair_ref, weight_ref, out_ref, bias_ref, mean_ref, spread_ref
):
    residues, width = x_ref.shape[1], x_ref.shape[2]
    heads = weight_ref.shape[0]
    normed = normalized(x_ref)[0].astype(jnp.bfloat16)
    pack_heads(out_ref, 0, f32_dot(normed, wc_ref[:, :width]) * scale, residues)
    pack_heads(out_ref, residues, f32_dot(normed, wc_ref[:, width : 2 * width]), residues)

    arrive()
    columns, channels = pair_ref.shape[1], pair_ref.shape[2]
    weight = centred(weight_ref[...])
    first = weight.astype(jnp.bfloat16)
    second, third = two_terms(weight - first.astype(jnp.float32))
    share = jnp.full((heads, channels), 1.0 / channels, jnp.bfloat16)
    left = jnp.concatenate([first, second, third, share], axis=0)
    average = jnp.full((channels, channels), 1.0 / channels, jnp.bfloat16)
    step_rows = 64

    def rows(step, carry):
        start = pl.multiple_of(step * step_rows, step_rows)
        entries = pair_ref[pl.ds(start, step_rows)].reshape(step_rows * columns, channels)
        center = entries.astype(jnp.float32) - f32_dot(entries, average)
        high, low = two_terms(center * center)
        variance = f32_dot(share, high, NT) + f32_dot(share, low, NT)
        spread = lax.rsqrt(variance + eps_norm)
        raw = f32_dot(left, entries, NT)
        bias = spread * (raw[:heads] + raw[heads : 2 * heads] + raw[2 * heads : 3 * heads])
        for k in range(step_rows):
            lanes = slice(k * columns, (k + 1) * columns)
            bias_ref[:, start + k, :] = bias[:, lanes]
            mean_ref[pl.ds(start + k, 1), :] = raw[3 * heads : 3 * heads + 1, lanes]
            spread_ref[pl.ds(start + k, 1), :] = spread[:1, lanes]
        return carry

    lax.fori_loop(0, pair_ref.shape[0] // step_rows, rows, 0)
    half = residues // 2
    for h in range(heads):
        for core in range(2):
            high, low = two_terms(bias_ref[h, core * half : (core + 1) * half, :])
            out_ref[h * 2 + core, 2 * residues : 2 * residues + half, :] = high
            out_ref[h * 2 + core, 2 * residues + half : 3 * residues, :] = low


def lanes_of(blocks_ref, row, residues):
    count = blocks_ref.shape[0] // 2
    planes = [
        blocks_ref[p * count : (p + 1) * count, row : row + residues, :].reshape(-1, LANES)
        for p in range(2)
    ]
    return jnp.concatenate(planes, axis=1)


def score_kernel(
    residues, left_row, right_row, with_bias, place_ref, own_ref, other_ref, mine_ref, sent_ref
):
    core, half = place_ref[0], place_ref[1]
    count = own_ref.shape[0] // 2
    part = residues // 2
    right = jnp.concatenate(
        [lanes_of(own_ref, right_row, residues), lanes_of(other_ref, right_row, residues)], axis=1
    )
    for which, ref in ((half, mine_ref), (1 - half, sent_ref)):
        left = []
        for k in range(count // 2):
            block = which * (count // 2) + k
            rows = pl.ds(pl.multiple_of(left_row + core * part, part), part)
            left.append(
                jnp.concatenate(
                    [
                        r[p * count + block, rows, :]
                        for r in (own_ref, other_ref)
                        for p in range(2)
                    ],
                    axis=1,
                )
            )
        ref[...] = f32_dot(jnp.concatenate(left, axis=0), right, NT).astype(ref.dtype)
        if with_bias:
            for p in range(2):
                columns = pl.ds(pl.multiple_of((half * 2 + p) * LANES, LANES), LANES)
                for k in range(count // 2):
                    block = p * count + which * (count // 2) + k
                    high = own_ref[block, 2 * residues : 2 * residues + part, :]
                    low = own_ref[block, 2 * residues + part : 3 * residues, :]
                    bias = high.astype(jnp.float32) + low.astype(jnp.float32)
                    ref[k * part : (k + 1) * part, columns] += bias


def softmax_kernel(logit_ref, other_ref, out_ref, low_ref):
    logits = logit_ref[...] + other_ref[...]
    lifted = jnp.exp(logits - jnp.max(logits, axis=-1, keepdims=True))
    softmax_out = lifted / jnp.sum(lifted, axis=-1, keepdims=True)
    out_ref[...] = softmax_out
    low_ref[...] = softmax_out.astype(jnp.bfloat16)


def grad_score_kernel(
    residues, left_row, right_row, place_ref, own_ref, other_ref, full_ref, sent_ref
):
    core = place_ref[0]
    count = own_ref.shape[0] // 2
    part = residues // 2
    right = jnp.concatenate(
        [lanes_of(own_ref, right_row, residues), lanes_of(other_ref, right_row, residues)], axis=1
    )
    rows = pl.ds(pl.multiple_of(left_row + core * part, part), part)
    left = [
        jnp.concatenate(
            [r[p * count + k, rows, :] for r in (own_ref, other_ref) for p in range(2)], axis=1
        )
        for k in range(count)
    ]
    terms = f32_dot(jnp.concatenate(left, axis=0), right, NT)
    full_ref[...] = terms
    sent_ref[...] = terms.astype(jnp.bfloat16)


def softmax_gradient_kernel(
    place_ref, softmax_ref, far_ref, grad_ref, other_ref, out_ref, out_far_ref
):
    half = place_ref[1]
    count = softmax_ref.shape[0]
    for which, probs, ref in ((half, softmax_ref, out_ref), (1 - half, far_ref, out_far_ref)):
        rows = pl.ds(pl.multiple_of(which * count, count), count)
        softmax_out = probs[...].astype(jnp.float32)
        grad_probs = grad_ref[rows, :] + other_ref[rows, :].astype(jnp.float32)
        row_dot = jnp.sum(softmax_out * grad_probs, axis=-1, keepdims=True)
        ref[...] = (softmax_out * (grad_probs - row_dot)).astype(jnp.bfloat16)


def product_kernel(
    residues, scale, first_row, second_row, with_share,
    place_ref, own_ref, far_ref, near_ref, corner_ref, blocks_ref, out_ref, whole_ref,
):
    core, half = place_ref[0], place_ref[1]
    count = blocks_ref.shape[0] // 2
    part = residues // 2
    quarters = (
        (own_ref, core, half), (far_ref, core, 1 - half),
        (near_ref, 1 - core, half), (corner_ref, 1 - core, 1 - half),
    )
    for ref, c, z in quarters:
        for k in range(count // 2):
            start = (z * (count // 2) + k) * residues + c * part
            whole_ref[pl.ds(pl.multiple_of(start, part), part), :] = ref[k * part : (k + 1) * part, :]
    whole = whole_ref[...]
    if with_share:
        for p in range(2):
            columns = pl.ds(pl.multiple_of((half * 2 + p) * LANES, LANES), LANES)
            for q in range(count):
                rows = pl.ds(pl.multiple_of(q * residues + core * part, part), part)
                out_ref[p * count + q, 2 * residues : 2 * residues + part, :] = whole_ref[rows, columns]
    first = f32_dot(whole, lanes_of(blocks_ref, first_row, residues)) * scale
    second = f32_dot(whole, lanes_of(blocks_ref, second_row, residues), TN)
    for row, product in ((0, first), (residues, second)):
        for p in range(2):
            out_ref[p * count : (p + 1) * count, row : row + residues, :] = (
                product[:, p * LANES : (p + 1) * LANES]
                .astype(jnp.bfloat16)
                .reshape(count, residues, LANES)
            )


def share_of(blocks_ref, row, part, heads):
    return jnp.concatenate(
        [
            blocks_ref[:, row : row + part, :]
            .astype(jnp.float32)
            .reshape(heads, 2 * part, LANES)
        ],
        axis=0,
    )


def attended_weight_kernel(
    x_ref, grad_ref, wc_ref, wo_ref, blocks_ref, updated_ref, projected_ref, normed_ref, sums_ref
):
    residues, width = x_ref.shape[1], x_ref.shape[2]
    tiles = width // LANES
    normed = normalized(x_ref)[0].astype(jnp.bfloat16)
    normed_ref[...] = normed
    gate = gate_of(f32_dot(normed, wc_ref[:, 3 * width :]))
    grad = grad_ref[...].reshape(-1, width)
    grad_gated = f32_dot(grad, wo_ref[...], NT)
    attended = unpack_heads(blocks_ref, 0, residues, tiles)
    gated = (gate * attended).astype(jnp.bfloat16)
    updated_ref[...] = f32_dot(gated, wo_ref[...]).astype(jnp.bfloat16).reshape(updated_ref.shape)
    projected_ref[:, :width] = unpack_heads(blocks_ref, residues, residues, tiles).astype(
        jnp.bfloat16
    )
    projected_ref[:, width:] = (grad_gated * attended * gate * (1.0 - gate)).astype(jnp.bfloat16)
    sums_ref[:, : 2 * width] = f32_dot(normed, projected_ref[...], TN).astype(jnp.bfloat16)
    sums_ref[:, 2 * width :] = f32_dot(gated, grad, TN).astype(jnp.bfloat16)


def query_weight_kernel(
    place_ref, normed_ref, attended_sums_ref, blocks_ref,
    projected_ref, keep_ref, send_ref, sums_ref,
):
    width = normed_ref.shape[1]
    tiles, residues = width // LANES, (blocks_ref.shape[1] * 2) // 5
    core = place_ref[0]
    for t in range(2):
        projected_ref[:, t * width : (t + 1) * width] = unpack_heads(
            blocks_ref, t * residues, residues, tiles
        ).astype(jnp.bfloat16)
    sums_ref[:, : 2 * width] = f32_dot(normed_ref[...], projected_ref[...], TN).astype(
        jnp.bfloat16
    )
    sums_ref[:, 2 * width :] = attended_sums_ref[...]
    rows = keep_ref.shape[1]
    for which, ref in ((core, keep_ref), (1 - core, send_ref)):
        for block in range(keep_ref.shape[0]):
            start = pl.multiple_of((2 * block + which) * rows, rows)
            ref[block] = sums_ref[pl.ds(start, rows), :]


def core_sum_kernel(place_ref, keep_ref, other_ref, own_ref, *send_refs):
    chip = place_ref[2]
    for flip, ref in enumerate((own_ref, *send_refs)):
        block = jnp.bitwise_xor(chip, flip)
        total = keep_ref[block].astype(jnp.float32) + other_ref[block].astype(jnp.float32)
        ref[...] = total.astype(ref.dtype)


def plane_sum_kernel(own_ref, pair_weight_ref, *refs):
    *received, out_ref = refs
    total = own_ref[...]
    for ref in received:
        total += ref[...].astype(jnp.float32)
    count = own_ref.shape[1]
    heads = pair_weight_ref.shape[0]
    out_ref[:, :count] = total.astype(out_ref.dtype)
    rest = jnp.zeros((out_ref.shape[0] - heads, out_ref.shape[1] - count), jnp.float32)
    out_ref[:, count:] = jnp.concatenate([pair_weight_ref[...], rest], axis=0).astype(
        out_ref.dtype
    )


def pair_weight_kernel(blocks_ref, pair_ref, mean_ref, spread_ref, out_ref, share_ref):
    heads, part = share_ref.shape[0], pair_ref.shape[0] // 2
    share_ref[...] = share_of(blocks_ref, blocks_ref.shape[1] - part, part, heads)

    columns, channels = pair_ref.shape[1], pair_ref.shape[2]
    step_rows = 16

    def rows(step, carry):
        total, shift = carry
        start = pl.multiple_of(step * step_rows, step_rows)
        left = []
        for k in range(step_rows):
            i = start + k
            high, low = two_terms(share_ref[:, i, :] * spread_ref[pl.ds(i, 1), :])
            left.append(jnp.concatenate([high, low], axis=0))
            shift += (high.astype(jnp.float32) + low.astype(jnp.float32)) * mean_ref[pl.ds(i, 1), :]
        entries = pair_ref[pl.ds(start, step_rows)].reshape(step_rows * columns, channels)
        return total + f32_dot(jnp.concatenate(left, axis=1), entries), shift

    total, shift = lax.fori_loop(
        0,
        pair_ref.shape[0] // step_rows,
        rows,
        (jnp.zeros((2 * heads, channels), jnp.float32), jnp.zeros((heads, LANES), jnp.float32)),
    )
    out_ref[...] = total[:heads] + total[heads:] - jnp.sum(shift, axis=1, keepdims=True)


def alignment_kernel(x_ref, wc_ref, query_key_ref, value_gate_ref, out_ref):
    normed, spread = normalized(x_ref)
    width = x_ref.shape[2]
    gradient = f32_dot(query_key_ref[...], wc_ref[:, : 2 * width], NT) + f32_dot(
        value_gate_ref[...], wc_ref[:, 2 * width :], NT
    )
    out_ref[...] = (
        layer_norm_backward(gradient, normed, spread).astype(jnp.bfloat16).reshape(out_ref.shape)
    )


def pair_kernel(blocks_row, blocks_ref, pair_ref, weight_ref, bias_ref, mean_ref, spread_ref, out_ref, share_ref):
    heads, channels = weight_ref.shape
    part = pair_ref.shape[0] // 2
    share_ref[...] = share_of(blocks_ref, blocks_row, part, heads)
    first, second = two_terms(centred(weight_ref[...]))
    zero = jnp.zeros((heads, channels), jnp.bfloat16)
    top = lax.broadcasted_iota(jnp.int32, (heads, channels), 0) < 2
    ones = jnp.where(top, 1.0, 0.0).astype(jnp.bfloat16)
    right = jnp.concatenate(
        [
            jnp.concatenate([first, first, second, ones, zero], axis=0),
            jnp.concatenate([zero, zero, zero, zero, ones], axis=0),
        ],
        axis=1,
    )
    row = lax.broadcasted_iota(jnp.int32, (heads, LANES), 0)

    def rows_of_two(value):
        high, low = two_terms(value)
        high, low = high.astype(jnp.float32), low.astype(jnp.float32)
        return jnp.where(row == 0, high, jnp.where(row == 1, low, 0.0)).astype(jnp.bfloat16)

    def rows(step, carry):
        for k in range(8):
            i = step * 8 + k
            gradient = share_ref[:, i, :]
            spread = spread_ref[pl.ds(i, 1), :]
            cross = jnp.sum(gradient * bias_ref[:, i, :], axis=0, keepdims=True) / channels
            slope = spread * spread * cross
            high, low = two_terms(gradient * spread)
            left = jnp.concatenate(
                [
                    high, low, high,
                    rows_of_two(jnp.broadcast_to(slope * mean_ref[pl.ds(i, 1), :], row.shape)),
                    rows_of_two(jnp.broadcast_to(slope, row.shape)),
                ],
                axis=0,
            )
            terms = f32_dot(left, right, TN)
            entries = pair_ref[i].astype(jnp.float32)
            out_ref[i] = (terms[:, :channels] - terms[:, channels:] * entries).astype(jnp.bfloat16)
        return carry

    lax.fori_loop(0, pair_ref.shape[0] // 8, rows, 0)


def output_kernel(place_ref, *refs):
    *parts, combined_ref, out_weight_ref, pair_weight_ref, shares_ref = refs
    core, chip = place_ref[0], place_ref[2]
    width = combined_ref.shape[0]
    rows = parts[0].shape[0]
    heads = pair_weight_ref.shape[0]
    for k, ref in enumerate(parts):
        owner = jnp.bitwise_xor(chip, k // 2) * 2 + jnp.bitwise_xor(core, k % 2)
        block = pl.ds(pl.multiple_of(owner * rows, rows), rows)
        part = ref[...].astype(jnp.float32)
        combined_ref[block, :] = part[:, : 4 * width]
        out_weight_ref[block, :] = part[:, 4 * width : 5 * width]
        shares_ref[owner] = part[:heads, 5 * width :]
    total = shares_ref[0]
    for k in range(1, len(parts)):
        total += shares_ref[k]
    pair_weight_ref[...] = total


def call(kernel, outs, *args, scratch=(), place=None, flops=0, after=(), outside=0, late=0):
    whole, anywhere = pl.BlockSpec(memory_space=pltpu.VMEM), pl.BlockSpec(memory_space=pl.ANY)
    specs = [anywhere] * outside + [whole] * (len(args) - outside)
    ahead = () if place is None else (place,)
    shapes = [jax.ShapeDtypeStruct(*o) for o in outs]
    moved = sum(math.prod(a.shape) * a.dtype.itemsize for a in list(args) + shapes)
    first = len(ahead) + len(args)
    last = first + len(after)

    def wrapped(*refs):
        given, rest = list(refs[:first]), refs[last:]
        if outside:
            *rest, arrived = rest
            held = rest[len(rest) - outside :]
            rest = rest[: len(rest) - outside]
            copies = []
            for k in range(outside):
                copies.append(
                    pltpu.make_async_copy(given[len(ahead) + k], held[k], arrived.at[k])
                )
                given[len(ahead) + k] = held[k]
            for copy in copies:
                copy.start()
            for copy in copies[: outside - late]:
                copy.wait()
            if late:
                given.insert(0, lambda: [copy.wait() for copy in copies[outside - late :]])
        kernel(*given, *rest)

    held = [pltpu.VMEM(a.shape, a.dtype) for a in args[:outside]]
    if outside:
        held.append(pltpu.SemaphoreType.DMA((outside,)))
    return pl.pallas_call(
        wrapped,
        out_shape=shapes,
        in_specs=[pl.BlockSpec(memory_space=pltpu.SMEM)] * len(ahead)
        + specs
        + [anywhere] * len(after),
        out_specs=[whole] * len(shapes),
        scratch_shapes=[*scratch, *held],
        compiler_params=pltpu.CompilerParams(
            vmem_limit_bytes=ARGUMENT_VMEM_LIMIT if outside else VMEM_LIMIT
        ),
        cost_estimate=pl.CostEstimate(flops=flops, bytes_accessed=moved, transcendentals=0),
    )(*ahead, *args, *after)


def swapped(mine, axis_name, distance):
    size = lax.axis_size(axis_name)
    return lax.ppermute(mine, axis_name, [(a, a ^ distance) for a in range(size)])


def fits_heads(alignment_rows, pair_entries, pair_weight):
    channels, heads = pair_weight.shape
    return (
        lax.axis_size("seq") == 4
        and lax.axis_size("res") == heads == 8
        and alignment_rows.shape[0] == 2 * SLOTS
        and alignment_rows.shape[1] == pair_entries.shape[0] == 64
        and alignment_rows.shape[2] == 2 * LANES
        and pair_entries.shape[1] == channels == LANES
    )


def head_body(
    alignment_rows, pair_entries, combined_weight, output_weight, pair_weight, updated_gradient
):
    sequences, residues, width = alignment_rows.shape
    channels, heads = pair_weight.shape
    tokens = sequences * residues
    seq_size, res_size = lax.axis_size("seq"), lax.axis_size("res")
    seq_half = seq_size // 2
    total = residues * res_size
    group = 2 * res_size
    groups = [[g * group + k for k in range(group)] for g in range(seq_half)]
    scale = 1.0 / math.sqrt(width // heads * sequences * seq_size)
    res_index, seq_index = lax.axis_index("res"), lax.axis_index("seq")
    place = jnp.stack([res_index % 2, seq_index // 2, res_index // 2]).astype(jnp.int32)
    bf16, f32 = jnp.bfloat16, jnp.float32

    def across(blocks):
        return lax.all_to_all(blocks, ("seq", "res"), 0, 0, axis_index_groups=groups, tiled=True)

    x, grad, wc, wo = alignment_rows, updated_gradient, combined_weight, output_weight
    (value_blocks,) = call(
        value_kernel, [((group, 2 * residues, LANES), bf16)], x, grad, wc, wo,
        flops=8 * tokens * width * width, outside=4, late=3,
    )
    value_blocks = across(value_blocks)
    query_blocks, bias, mean, spread = call(
        functools.partial(query_kernel, scale),
        [
            ((group, 3 * residues, LANES), bf16),
            ((heads, residues, LANES), f32),
            ((residues, LANES), f32),
            ((residues, LANES), f32),
        ],
        x, wc, pair_entries, pair_weight.T,
        flops=8 * tokens * width * width, outside=3, late=1,
    )
    value_blocks, query_blocks = lax.optimization_barrier((value_blocks, query_blocks))
    query_blocks = across(query_blocks)

    quarter, half_rows = (total // 4, total), (total // 2, total)
    grad_full, grad_sent = call(
        functools.partial(grad_score_kernel, residues, residues, 0),
        [(half_rows, f32), (half_rows, bf16)],
        value_blocks, swapped(value_blocks, "res", 1),
        place=place, flops=2 * total * total * width,
    )
    grad_other = swapped(grad_sent, "seq", seq_half)
    query_blocks, grad_other = lax.optimization_barrier((query_blocks, grad_other))
    logit_mine, logit_sent = call(
        functools.partial(score_kernel, residues, 0, residues, True),
        [(quarter, f32), (quarter, f32)],
        query_blocks, swapped(query_blocks, "res", 1),
        place=place, flops=2 * total * total * width,
    )
    softmax_out, probs = call(
        softmax_kernel, [(quarter, f32), (quarter, bf16)],
        logit_mine, swapped(logit_sent, "seq", seq_half),
        flops=total * total,
    )

    def products(mine, far, blocks, first_row, second_row, with_share, factor):
        rows = 2 * residues + (residues // 2 if with_share else 0)
        (out,) = call(
            functools.partial(
                product_kernel, residues, factor, first_row, second_row, with_share
            ),
            [((group, rows, LANES), bf16)],
            mine, far, swapped(mine, "res", 1), swapped(far, "res", 1), blocks,
            scratch=[pltpu.VMEM((total, total), bf16)],
            place=place, flops=4 * total * total * width,
        )
        return out

    probs_far = swapped(probs, "seq", seq_half)
    attended = products(probs, probs_far, value_blocks, 0, residues, False, 1.0)
    attended_blocks = across(attended)
    softmax_out = lax.optimization_barrier((attended, softmax_out))[1]
    grad_logits, grad_far = call(
        softmax_gradient_kernel, [(quarter, bf16), (quarter, bf16)],
        softmax_out, probs_far, grad_full, grad_other,
        place=place, flops=total * total,
    )
    grad_sums = products(grad_logits, grad_far, query_blocks, residues, 0, True, scale)
    grad_sums, attended_blocks = lax.optimization_barrier((grad_sums, attended_blocks))
    grad_blocks = across(grad_sums)

    updated, value_gate, normed, attended_sums = call(
        attended_weight_kernel,
        [
            (x.shape, bf16),
            ((tokens, 2 * width), bf16),
            ((tokens, width), bf16),
            ((width, 3 * width), bf16),
        ],
        x, grad, wc, wo, attended_blocks,
        flops=14 * tokens * width * width, outside=4,
    )
    share = pltpu.VMEM((heads, residues, LANES), f32)
    columns = 5 * width
    rows = width // res_size
    part_rows = ((res_size // 2, rows, columns), bf16)
    (pair_weight_part,) = call(
        pair_weight_kernel, [((heads, channels), f32)],
        grad_blocks, pair_entries, mean, spread,
        scratch=[share], flops=4 * tokens * width * width,
    )
    query_key, keep, send = call(
        query_weight_kernel,
        [((tokens, 2 * width), bf16), part_rows, part_rows],
        normed, attended_sums, grad_blocks,
        scratch=[pltpu.VMEM((width, columns), bf16)],
        place=place, flops=4 * tokens * width * width, after=(pair_weight_part,),
    )
    own, *sent = call(
        core_sum_kernel,
        [((rows, columns), f32)] + [((rows, columns), bf16)] * 3,
        keep, swapped(send, "res", 1), place=place,
    )
    received = [swapped(t, "res", 2 * flip) for flip, t in enumerate(sent, 1)]
    (pair_gradient,) = call(
        functools.partial(pair_kernel, 2 * residues),
        [(pair_entries.shape, bf16)],
        grad_blocks, pair_entries, pair_weight.T, bias, mean, spread,
        scratch=[share], flops=8 * tokens * width * width,
    )
    (alignment_gradient,) = call(
        alignment_kernel, [(x.shape, bf16)], x, wc, query_key, value_gate,
        flops=8 * tokens * width * width,
    )
    received, alignment_gradient = lax.optimization_barrier((received, alignment_gradient))
    (part,) = call(
        plane_sum_kernel, [((rows, columns + channels), bf16)], own, pair_weight_part, *received
    )
    def added(mine, other):
        return (mine.astype(f32) + other.astype(f32)).astype(bf16)

    other_plane = swapped(part, "seq", 1)
    part = added(part, other_plane)
    other_half = swapped(part, "seq", seq_half)
    other_half, pair_gradient = lax.optimization_barrier((other_half, pair_gradient))
    part = added(part, other_half)
    chips = [part] + [swapped(part, "res", 2 * flip) for flip in range(1, res_size // 2)]
    parts = [t for chip in chips for t in (chip, swapped(chip, "res", 1))]
    combined_gradient, output_gradient, pair_weight_gradient = call(
        output_kernel,
        [(wc.shape, f32), (wo.shape, f32), ((heads, channels), f32)],
        *parts,
        scratch=[pltpu.VMEM((len(parts), heads, channels), f32)],
        place=place,
    )
    return (
        updated,
        alignment_gradient,
        pair_gradient,
        combined_gradient,
        output_gradient,
        pair_weight_gradient.T,
    )


def body(alignment_rows, pair_entries, combined_weight, output_weight, pair_weight, updated_gradient):
    chosen = head_body if fits_heads(alignment_rows, pair_entries, pair_weight) else gathered_body
    return chosen(
        alignment_rows, pair_entries, combined_weight, output_weight, pair_weight, updated_gradient
    )


def solution(mesh):
    return jax.shard_map(
        body,
        mesh=mesh,
        in_specs=(
            P("seq", "res", None),
            P("res", "seq", None),
            P(),
            P(),
            P(),
            P("seq", "res", None),
        ),
        out_specs=(
            P("seq", "res", None),
            P("seq", "res", None),
            P("res", "seq", None),
            P(),
            P(),
            P(),
        ),
        check_vma=False,
    )
```

```python
import functools
import math

import jax
import jax.numpy as jnp
from jax import lax
from jax.experimental import pallas as pl
from jax.experimental.pallas import tpu as pltpu
from jax.sharding import PartitionSpec as P

eps_norm = 1e-05


def layer_normalize(values):
    values = values.astype(jnp.float32)
    center = values - jnp.mean(values, axis=-1, keepdims=True)
    broadcast_pair = lax.rsqrt(jnp.mean(center * center, axis=-1, keepdims=True) + eps_norm)
    return (center * broadcast_pair, broadcast_pair)


def layer_norm_backward(normalized_gradient, normalized_rows, broadcast_pair):
    mean_grad = jnp.mean(normalized_gradient, axis=-1, keepdims=True)
    mean_cross = jnp.mean(normalized_gradient * normalized_rows, axis=-1, keepdims=True)
    return broadcast_pair * (normalized_gradient - mean_grad - normalized_rows * mean_cross)


def split_heads(tensor, head_count):
    return tensor.reshape(
        tensor.shape[0], tensor.shape[1], head_count, tensor.shape[2] // head_count
    )


def merge_heads(tensor):
    return tensor.reshape(tensor.shape[0], tensor.shape[1], tensor.shape[2] * tensor.shape[3])


def gathered_body(
    alignment_rows, pair_entries, combined_weight, output_weight, pair_weight, updated_gradient
):
    sequence_count, residue_count, alignment_width = alignment_rows.shape
    head_count = pair_weight.shape[1]
    query_width = output_weight.shape[0]
    head_dim = query_width // head_count
    column_count = pair_entries.shape[1]
    token_count = sequence_count * residue_count
    score_scale = 1.0 / math.sqrt(head_dim * sequence_count * lax.axis_size("seq"))
    normalized_rows, broadcast_pair = layer_normalize(alignment_rows)
    normalized_rows_backward = normalized_rows.astype(jnp.bfloat16).reshape(
        token_count, alignment_width
    )
    projected = jnp.dot(
        normalized_rows_backward, combined_weight, preferred_element_type=jnp.float32
    ).reshape(sequence_count, residue_count, 4 * query_width)
    queries = (projected[..., :query_width] * score_scale).astype(jnp.bfloat16)
    key_rows = projected[..., query_width : 2 * query_width].astype(jnp.bfloat16)
    value_rows = projected[..., 2 * query_width : 3 * query_width].astype(jnp.bfloat16)
    gate_open = jax.nn.sigmoid(projected[..., 3 * query_width :])
    all_keys, all_values = (
        lax.all_gather(key_rows, "res", axis=1, tiled=True),
        lax.all_gather(value_rows, "res", axis=1, tiled=True),
    )
    query_heads = split_heads(queries, head_count)
    key_heads = split_heads(all_keys, head_count)
    value_heads = split_heads(all_values, head_count)
    score_terms = jnp.einsum(
        "sihd,sjhd->hij", query_heads, key_heads, preferred_element_type=jnp.float32
    )
    pair_normed, pair_spread = layer_normalize(pair_entries)
    pair_bias = jnp.einsum("ijc,ch->hij", pair_normed, pair_weight, precision=lax.Precision.HIGHEST)
    col_start = lax.axis_index("seq") * column_count
    own_block = lax.dynamic_slice_in_dim(score_terms, col_start, column_count, 2) + pair_bias
    logits = lax.psum(lax.dynamic_update_slice_in_dim(score_terms, own_block, col_start, 2), "seq")
    row_top = jnp.max(logits, axis=-1, keepdims=True)
    lifted = jnp.exp(logits - row_top)
    softmax_out = lifted / jnp.sum(lifted, axis=-1, keepdims=True)
    softmax_low = softmax_out.astype(jnp.bfloat16)
    attended = merge_heads(
        jnp.einsum("hij,sjhd->sihd", softmax_low, value_heads, preferred_element_type=jnp.float32)
    )
    gated_out = (gate_open * attended).astype(jnp.bfloat16)
    flattened_gated = gated_out.reshape(token_count, query_width)
    updated = (
        jnp.dot(flattened_gated, output_weight, preferred_element_type=jnp.float32)
        .astype(jnp.bfloat16)
        .reshape(sequence_count, residue_count, alignment_width)
    )
    flattened_gradient = updated_gradient.reshape(token_count, alignment_width)
    grad_gated = jnp.dot(
        flattened_gradient, output_weight.T, preferred_element_type=jnp.float32
    ).reshape(sequence_count, residue_count, query_width)
    out_local = jnp.dot(flattened_gated.T, flattened_gradient, preferred_element_type=jnp.float32)
    grad_attended = (grad_gated * gate_open).astype(jnp.bfloat16)
    grad_gate_logit = grad_gated * attended * gate_open * (1.0 - gate_open)
    attended_grad_heads = split_heads(grad_attended, head_count)
    grad_terms = jnp.einsum(
        "sihd,sjhd->hij", attended_grad_heads, value_heads, preferred_element_type=jnp.float32
    )
    grad_probs = lax.psum(grad_terms, "seq")
    row_dot = jnp.sum(softmax_out * grad_probs, axis=-1, keepdims=True)
    grad_logits = softmax_out * (grad_probs - row_dot)
    grad_logits_b = grad_logits.astype(jnp.bfloat16)
    logit_share = lax.dynamic_slice_in_dim(grad_logits, col_start, column_count, 2)
    grad_query_heads = (
        jnp.einsum("hij,sjhd->sihd", grad_logits_b, key_heads, preferred_element_type=jnp.float32)
        * score_scale
    )
    key_part = jnp.einsum(
        "hij,sihd->jshd", grad_logits_b, query_heads, preferred_element_type=jnp.float32
    )
    value_part = jnp.einsum(
        "hij,sihd->jshd", softmax_low, attended_grad_heads, preferred_element_type=jnp.float32
    )
    summed = lax.psum_scatter(
        jnp.concatenate([merge_heads(key_part), merge_heads(value_part)], axis=-1),
        "res",
        scatter_dimension=0,
        tiled=True,
    )
    key_value_grads = jnp.transpose(summed, (1, 0, 2))
    projected_gradient = jnp.concatenate(
        [merge_heads(grad_query_heads), key_value_grads, grad_gate_logit], axis=-1
    )
    projected_gradient = projected_gradient.astype(jnp.bfloat16).reshape(
        token_count, 4 * query_width
    )
    qkvg_local = jnp.dot(
        normalized_rows_backward.T, projected_gradient, preferred_element_type=jnp.float32
    )
    normalized_gradient = jnp.dot(
        projected_gradient, combined_weight.T, preferred_element_type=jnp.float32
    ).reshape(sequence_count, residue_count, alignment_width)
    alignment_gradient = layer_norm_backward(
        normalized_gradient, normalized_rows, broadcast_pair
    ).astype(jnp.bfloat16)
    pair_w_local = jnp.einsum(
        "ijc,hij->ch", pair_normed, logit_share, precision=lax.Precision.HIGHEST
    )
    grad_pair_normed = jnp.einsum(
        "hij,ch->ijc", logit_share, pair_weight, precision=lax.Precision.HIGHEST
    )
    pair_gradient = layer_norm_backward(grad_pair_normed, pair_normed, pair_spread).astype(
        jnp.bfloat16
    )
    combined_weight_gradient, output_weight_gradient, pair_weight_gradient = lax.psum(
        (qkvg_local, out_local, pair_w_local), ("seq", "res")
    )
    return (
        updated,
        alignment_gradient,
        pair_gradient,
        combined_weight_gradient,
        output_weight_gradient,
        pair_weight_gradient,
    )


VMEM_LIMIT = 20 * 1024 * 1024
ARGUMENT_VMEM_LIMIT = 56 * 1024 * 1024
LANES = 128
SLOTS = 4
NT = (((1,), (1,)), ((), ()))
TN = (((0,), (0,)), ((), ()))


def f32_dot(left, right, dims=None):
    if dims is None:
        return jnp.dot(left, right, preferred_element_type=jnp.float32)
    return lax.dot_general(left, right, dims, preferred_element_type=jnp.float32)


def two_terms(values):
    high = values.astype(jnp.bfloat16)
    return high, (values - high.astype(jnp.float32)).astype(jnp.bfloat16)


def slot_select(pieces):
    slot = lax.broadcasted_iota(jnp.int32, pieces[0].shape, 1) // (LANES // SLOTS)
    result = pieces[0]
    for k in range(1, SLOTS):
        result = jnp.where(slot == k, pieces[k], result)
    return result


def pack_heads(out_ref, row, tensor, residues):
    for core in range(2):
        for tile in range(tensor.shape[1] // LANES):
            rolled = []
            for s in range(SLOTS):
                start = (core * SLOTS + s) * residues
                piece = tensor[start : start + residues, tile * LANES : (tile + 1) * LANES]
                rolled.append(pltpu.roll(piece, s * LANES // SLOTS, 1) if s else piece)
            for j in range(SLOTS):
                block = slot_select([rolled[(k - j) % SLOTS] for k in range(SLOTS)])
                out_ref[(tile * SLOTS + j) * 2 + core, row : row + residues, :] = block.astype(
                    jnp.bfloat16
                )


def unpack_heads(in_ref, row, residues, tiles):
    rows = []
    for core in range(2):
        for s in range(SLOTS):
            pieces = []
            for tile in range(tiles):
                blocks = [
                    in_ref[
                        (tile * SLOTS + (k - s) % SLOTS) * 2 + core, row : row + residues, :
                    ].astype(jnp.float32)
                    for k in range(SLOTS)
                ]
                block = slot_select(blocks)
                pieces.append(pltpu.roll(block, LANES - s * LANES // SLOTS, 1) if s else block)
            rows.append(jnp.concatenate(pieces, axis=1))
    return jnp.concatenate(rows, axis=0)


def normalized(x_ref):
    width = x_ref.shape[-1]
    values = x_ref[...].reshape(-1, width).astype(jnp.float32)
    return layer_normalize(values)


def gate_of(logits):
    return 1.0 / (1.0 + jnp.exp(-logits))


def value_kernel(arrive, x_ref, grad_ref, wc_ref, wo_ref, out_ref):
    residues, width = x_ref.shape[1], x_ref.shape[2]
    normed = normalized(x_ref)[0].astype(jnp.bfloat16)
    arrive()
    values = f32_dot(normed, wc_ref[:, 2 * width : 3 * width])
    gate = gate_of(f32_dot(normed, wc_ref[:, 3 * width :]))
    grad_gated = f32_dot(grad_ref[...].reshape(-1, width), wo_ref[...], NT)
    pack_heads(out_ref, 0, values, residues)
    pack_heads(out_ref, residues, grad_gated * gate, residues)


def centred(weight):
    return weight - jnp.mean(weight, axis=1, keepdims=True)


def query_kernel(
    scale, arrive, x_ref, wc_ref, pair_ref, weight_ref, out_ref, bias_ref, mean_ref, spread_ref
):
    residues, width = x_ref.shape[1], x_ref.shape[2]
    heads = weight_ref.shape[0]
    normed = normalized(x_ref)[0].astype(jnp.bfloat16)
    pack_heads(out_ref, 0, f32_dot(normed, wc_ref[:, :width]) * scale, residues)
    pack_heads(out_ref, residues, f32_dot(normed, wc_ref[:, width : 2 * width]), residues)

    arrive()
    columns, channels = pair_ref.shape[1], pair_ref.shape[2]
    weight = centred(weight_ref[...])
    first = weight.astype(jnp.bfloat16)
    second, third = two_terms(weight - first.astype(jnp.float32))
    share = jnp.full((heads, channels), 1.0 / channels, jnp.bfloat16)
    left = jnp.concatenate([first, second, third, share], axis=0)
    average = jnp.full((channels, channels), 1.0 / channels, jnp.bfloat16)
    step_rows = 64

    def rows(step, carry):
        start = pl.multiple_of(step * step_rows, step_rows)
        entries = pair_ref[pl.ds(start, step_rows)].reshape(step_rows * columns, channels)
        center = entries.astype(jnp.float32) - f32_dot(entries, average)
        high, low = two_terms(center * center)
        variance = f32_dot(share, high, NT) + f32_dot(share, low, NT)
        spread = lax.rsqrt(variance + eps_norm)
        raw = f32_dot(left, entries, NT)
        bias = spread * (raw[:heads] + raw[heads : 2 * heads] + raw[2 * heads : 3 * heads])
        for k in range(step_rows):
            lanes = slice(k * columns, (k + 1) * columns)
            bias_ref[:, start + k, :] = bias[:, lanes]
            mean_ref[pl.ds(start + k, 1), :] = raw[3 * heads : 3 * heads + 1, lanes]
            spread_ref[pl.ds(start + k, 1), :] = spread[:1, lanes]
        return carry

    lax.fori_loop(0, pair_ref.shape[0] // step_rows, rows, 0)
    half = residues // 2
    for h in range(heads):
        for core in range(2):
            high, low = two_terms(bias_ref[h, core * half : (core + 1) * half, :])
            out_ref[h * 2 + core, 2 * residues : 2 * residues + half, :] = high
            out_ref[h * 2 + core, 2 * residues + half : 3 * residues, :] = low


def lanes_of(blocks_ref, row, residues):
    count = blocks_ref.shape[0] // 2
    planes = [
        blocks_ref[p * count : (p + 1) * count, row : row + residues, :].reshape(-1, LANES)
        for p in range(2)
    ]
    return jnp.concatenate(planes, axis=1)


def score_kernel(
    residues, left_row, right_row, sent, place_ref, own_ref, other_ref, out_ref
):
    core, half = place_ref[0], place_ref[1]
    count = own_ref.shape[0] // 2
    part = residues // 2
    right = jnp.concatenate(
        [lanes_of(own_ref, right_row, residues), lanes_of(other_ref, right_row, residues)], axis=1
    )
    which = 1 - half if sent else half
    left = []
    for k in range(count // 2):
        block = which * (count // 2) + k
        rows = pl.ds(pl.multiple_of(left_row + core * part, part), part)
        left.append(
            jnp.concatenate(
                [
                    r[p * count + block, rows, :]
                    for r in (own_ref, other_ref)
                    for p in range(2)
                ],
                axis=1,
            )
        )
    out_ref[...] = f32_dot(jnp.concatenate(left, axis=0), right, NT)
    for p in range(2):
        columns = pl.ds(pl.multiple_of((half * 2 + p) * LANES, LANES), LANES)
        for k in range(count // 2):
            block = p * count + which * (count // 2) + k
            high = own_ref[block, 2 * residues : 2 * residues + part, :]
            low = own_ref[block, 2 * residues + part : 3 * residues, :]
            bias = high.astype(jnp.float32) + low.astype(jnp.float32)
            out_ref[k * part : (k + 1) * part, columns] += bias


def softmax_kernel(logit_ref, other_ref, out_ref, low_ref):
    logits = logit_ref[...] + other_ref[...]
    lifted = jnp.exp(logits - jnp.max(logits, axis=-1, keepdims=True))
    softmax_out = lifted / jnp.sum(lifted, axis=-1, keepdims=True)
    out_ref[...] = softmax_out
    low_ref[...] = softmax_out.astype(jnp.bfloat16)


def grad_score_kernel(
    residues, left_row, right_row, place_ref, own_ref, other_ref, full_ref, sent_ref
):
    core = place_ref[0]
    count = own_ref.shape[0] // 2
    part = residues // 2
    right = jnp.concatenate(
        [lanes_of(own_ref, right_row, residues), lanes_of(other_ref, right_row, residues)], axis=1
    )
    rows = pl.ds(pl.multiple_of(left_row + core * part, part), part)
    left = [
        jnp.concatenate(
            [r[p * count + k, rows, :] for r in (own_ref, other_ref) for p in range(2)], axis=1
        )
        for k in range(count)
    ]
    terms = f32_dot(jnp.concatenate(left, axis=0), right, NT)
    full_ref[...] = terms
    sent_ref[...] = terms.astype(jnp.bfloat16)


def softmax_gradient_kernel(
    place_ref, softmax_ref, far_ref, grad_ref, other_ref, out_ref, out_far_ref
):
    half = place_ref[1]
    count = softmax_ref.shape[0]
    for which, probs, ref in ((half, softmax_ref, out_ref), (1 - half, far_ref, out_far_ref)):
        rows = pl.ds(pl.multiple_of(which * count, count), count)
        softmax_out = probs[...].astype(jnp.float32)
        grad_probs = grad_ref[rows, :] + other_ref[rows, :].astype(jnp.float32)
        row_dot = jnp.sum(softmax_out * grad_probs, axis=-1, keepdims=True)
        ref[...] = (softmax_out * (grad_probs - row_dot)).astype(jnp.bfloat16)


def product_kernel(
    residues, scale, first_row, second_row, with_share,
    place_ref, own_ref, far_ref, near_ref, corner_ref, blocks_ref, out_ref, whole_ref,
):
    core, half = place_ref[0], place_ref[1]
    count = blocks_ref.shape[0] // 2
    part = residues // 2
    quarters = (
        (own_ref, core, half), (far_ref, core, 1 - half),
        (near_ref, 1 - core, half), (corner_ref, 1 - core, 1 - half),
    )
    for ref, c, z in quarters:
        for k in range(count // 2):
            start = (z * (count // 2) + k) * residues + c * part
            whole_ref[pl.ds(pl.multiple_of(start, part), part), :] = ref[k * part : (k + 1) * part, :]
    whole = whole_ref[...]
    if with_share:
        for p in range(2):
            columns = pl.ds(pl.multiple_of((half * 2 + p) * LANES, LANES), LANES)
            for q in range(count):
                rows = pl.ds(pl.multiple_of(q * residues + core * part, part), part)
                out_ref[p * count + q, 2 * residues : 2 * residues + part, :] = whole_ref[rows, columns]
    first = f32_dot(whole, lanes_of(blocks_ref, first_row, residues)) * scale
    second = f32_dot(whole, lanes_of(blocks_ref, second_row, residues), TN)
    for row, product in ((0, first), (residues, second)):
        for p in range(2):
            out_ref[p * count : (p + 1) * count, row : row + residues, :] = (
                product[:, p * LANES : (p + 1) * LANES]
                .astype(jnp.bfloat16)
                .reshape(count, residues, LANES)
            )


def share_of(blocks_ref, row, part, heads):
    return jnp.concatenate(
        [
            blocks_ref[:, row : row + part, :]
            .astype(jnp.float32)
            .reshape(heads, 2 * part, LANES)
        ],
        axis=0,
    )


def attended_weight_kernel(
    x_ref, grad_ref, wc_ref, wo_ref, blocks_ref, updated_ref, projected_ref, normed_ref, sums_ref
):
    residues, width = x_ref.shape[1], x_ref.shape[2]
    tiles = width // LANES
    normed = normalized(x_ref)[0].astype(jnp.bfloat16)
    normed_ref[...] = normed
    gate = gate_of(f32_dot(normed, wc_ref[:, 3 * width :]))
    grad = grad_ref[...].reshape(-1, width)
    grad_gated = f32_dot(grad, wo_ref[...], NT)
    attended = unpack_heads(blocks_ref, 0, residues, tiles)
    gated = (gate * attended).astype(jnp.bfloat16)
    updated_ref[...] = f32_dot(gated, wo_ref[...]).astype(jnp.bfloat16).reshape(updated_ref.shape)
    projected_ref[:, :width] = unpack_heads(blocks_ref, residues, residues, tiles).astype(
        jnp.bfloat16
    )
    projected_ref[:, width:] = (grad_gated * attended * gate * (1.0 - gate)).astype(jnp.bfloat16)
    sums_ref[:, : 2 * width] = f32_dot(normed, projected_ref[...], TN).astype(jnp.bfloat16)
    sums_ref[:, 2 * width :] = f32_dot(gated, grad, TN).astype(jnp.bfloat16)


def query_weight_kernel(
    place_ref, normed_ref, attended_sums_ref, blocks_ref,
    projected_ref, keep_ref, send_ref, sums_ref,
):
    width = normed_ref.shape[1]
    tiles, residues = width // LANES, (blocks_ref.shape[1] * 2) // 5
    core = place_ref[0]
    for t in range(2):
        projected_ref[:, t * width : (t + 1) * width] = unpack_heads(
            blocks_ref, t * residues, residues, tiles
        ).astype(jnp.bfloat16)
    sums_ref[:, : 2 * width] = f32_dot(normed_ref[...], projected_ref[...], TN).astype(
        jnp.bfloat16
    )
    sums_ref[:, 2 * width :] = attended_sums_ref[...]
    rows = keep_ref.shape[1]
    for which, ref in ((core, keep_ref), (1 - core, send_ref)):
        for block in range(keep_ref.shape[0]):
            start = pl.multiple_of((2 * block + which) * rows, rows)
            ref[block] = sums_ref[pl.ds(start, rows), :]


def core_sum_kernel(place_ref, keep_ref, other_ref, own_ref, *send_refs):
    chip = place_ref[2]
    for flip, ref in enumerate((own_ref, *send_refs)):
        block = jnp.bitwise_xor(chip, flip)
        total = keep_ref[block].astype(jnp.float32) + other_ref[block].astype(jnp.float32)
        ref[...] = total.astype(ref.dtype)


def plane_sum_kernel(own_ref, pair_weight_ref, *refs):
    *received, out_ref = refs
    total = own_ref[...]
    for ref in received:
        total += ref[...].astype(jnp.float32)
    count = own_ref.shape[1]
    heads = pair_weight_ref.shape[0]
    out_ref[:, :count] = total.astype(out_ref.dtype)
    rest = jnp.zeros((out_ref.shape[0] - heads, out_ref.shape[1] - count), jnp.float32)
    out_ref[:, count:] = jnp.concatenate([pair_weight_ref[...], rest], axis=0).astype(
        out_ref.dtype
    )


def pair_weight_kernel(blocks_ref, pair_ref, mean_ref, spread_ref, out_ref, share_ref):
    heads, part = share_ref.shape[0], pair_ref.shape[0] // 2
    share_ref[...] = share_of(blocks_ref, blocks_ref.shape[1] - part, part, heads)

    columns, channels = pair_ref.shape[1], pair_ref.shape[2]
    step_rows = 16

    def rows(step, carry):
        total, shift = carry
        start = pl.multiple_of(step * step_rows, step_rows)
        left = []
        for k in range(step_rows):
            i = start + k
            high, low = two_terms(share_ref[:, i, :] * spread_ref[pl.ds(i, 1), :])
            left.append(jnp.concatenate([high, low], axis=0))
            shift += (high.astype(jnp.float32) + low.astype(jnp.float32)) * mean_ref[pl.ds(i, 1), :]
        entries = pair_ref[pl.ds(start, step_rows)].reshape(step_rows * columns, channels)
        return total + f32_dot(jnp.concatenate(left, axis=1), entries), shift

    total, shift = lax.fori_loop(
        0,
        pair_ref.shape[0] // step_rows,
        rows,
        (jnp.zeros((2 * heads, channels), jnp.float32), jnp.zeros((heads, LANES), jnp.float32)),
    )
    out_ref[...] = total[:heads] + total[heads:] - jnp.sum(shift, axis=1, keepdims=True)


def alignment_kernel(x_ref, wc_ref, query_key_ref, value_gate_ref, out_ref):
    normed, spread = normalized(x_ref)
    width = x_ref.shape[2]
    gradient = f32_dot(query_key_ref[...], wc_ref[:, : 2 * width], NT) + f32_dot(
        value_gate_ref[...], wc_ref[:, 2 * width :], NT
    )
    out_ref[...] = (
        layer_norm_backward(gradient, normed, spread).astype(jnp.bfloat16).reshape(out_ref.shape)
    )


def pair_kernel(blocks_row, blocks_ref, pair_ref, weight_ref, bias_ref, mean_ref, spread_ref, out_ref, share_ref):
    heads, channels = weight_ref.shape
    part = pair_ref.shape[0] // 2
    share_ref[...] = share_of(blocks_ref, blocks_row, part, heads)
    first, second = two_terms(centred(weight_ref[...]))
    zero = jnp.zeros((heads, channels), jnp.bfloat16)
    top = lax.broadcasted_iota(jnp.int32, (heads, channels), 0) < 2
    ones = jnp.where(top, 1.0, 0.0).astype(jnp.bfloat16)
    right = jnp.concatenate(
        [
            jnp.concatenate([first, first, second, ones, zero], axis=0),
            jnp.concatenate([zero, zero, zero, zero, ones], axis=0),
        ],
        axis=1,
    )
    row = lax.broadcasted_iota(jnp.int32, (heads, LANES), 0)

    def rows_of_two(value):
        high, low = two_terms(value)
        high, low = high.astype(jnp.float32), low.astype(jnp.float32)
        return jnp.where(row == 0, high, jnp.where(row == 1, low, 0.0)).astype(jnp.bfloat16)

    def rows(step, carry):
        for k in range(8):
            i = step * 8 + k
            gradient = share_ref[:, i, :]
            spread = spread_ref[pl.ds(i, 1), :]
            cross = jnp.sum(gradient * bias_ref[:, i, :], axis=0, keepdims=True) / channels
            slope = spread * spread * cross
            high, low = two_terms(gradient * spread)
            left = jnp.concatenate(
                [
                    high, low, high,
                    rows_of_two(jnp.broadcast_to(slope * mean_ref[pl.ds(i, 1), :], row.shape)),
                    rows_of_two(jnp.broadcast_to(slope, row.shape)),
                ],
                axis=0,
            )
            terms = f32_dot(left, right, TN)
            entries = pair_ref[i].astype(jnp.float32)
            out_ref[i] = (terms[:, :channels] - terms[:, channels:] * entries).astype(jnp.bfloat16)
        return carry

    lax.fori_loop(0, pair_ref.shape[0] // 8, rows, 0)


def output_kernel(place_ref, *refs):
    *parts, combined_ref, out_weight_ref, pair_weight_ref, shares_ref = refs
    core, chip = place_ref[0], place_ref[2]
    width = combined_ref.shape[0]
    rows = parts[0].shape[0]
    heads = pair_weight_ref.shape[0]
    for k, ref in enumerate(parts):
        owner = jnp.bitwise_xor(chip, k // 2) * 2 + jnp.bitwise_xor(core, k % 2)
        block = pl.ds(pl.multiple_of(owner * rows, rows), rows)
        part = ref[...].astype(jnp.float32)
        combined_ref[block, :] = part[:, : 4 * width]
        out_weight_ref[block, :] = part[:, 4 * width : 5 * width]
        shares_ref[owner] = part[:heads, 5 * width :]
    total = shares_ref[0]
    for k in range(1, len(parts)):
        total += shares_ref[k]
    pair_weight_ref[...] = total


def call(kernel, outs, *args, scratch=(), place=None, flops=0, after=(), outside=0, late=0):
    whole, anywhere = pl.BlockSpec(memory_space=pltpu.VMEM), pl.BlockSpec(memory_space=pl.ANY)
    specs = [anywhere] * outside + [whole] * (len(args) - outside)
    ahead = () if place is None else (place,)
    shapes = [jax.ShapeDtypeStruct(*o) for o in outs]
    moved = sum(math.prod(a.shape) * a.dtype.itemsize for a in list(args) + shapes)
    first = len(ahead) + len(args)
    last = first + len(after)

    def wrapped(*refs):
        given, rest = list(refs[:first]), refs[last:]
        if outside:
            *rest, arrived = rest
            held = rest[len(rest) - outside :]
            rest = rest[: len(rest) - outside]
            copies = []
            for k in range(outside):
                copies.append(
                    pltpu.make_async_copy(given[len(ahead) + k], held[k], arrived.at[k])
                )
                given[len(ahead) + k] = held[k]
            for copy in copies:
                copy.start()
            for copy in copies[: outside - late]:
                copy.wait()
            if late:
                given.insert(0, lambda: [copy.wait() for copy in copies[outside - late :]])
        kernel(*given, *rest)

    held = [pltpu.VMEM(a.shape, a.dtype) for a in args[:outside]]
    if outside:
        held.append(pltpu.SemaphoreType.DMA((outside,)))
    return pl.pallas_call(
        wrapped,
        out_shape=shapes,
        in_specs=[pl.BlockSpec(memory_space=pltpu.SMEM)] * len(ahead)
        + specs
        + [anywhere] * len(after),
        out_specs=[whole] * len(shapes),
        scratch_shapes=[*scratch, *held],
        compiler_params=pltpu.CompilerParams(
            vmem_limit_bytes=ARGUMENT_VMEM_LIMIT if outside else VMEM_LIMIT
        ),
        cost_estimate=pl.CostEstimate(flops=flops, bytes_accessed=moved, transcendentals=0),
    )(*ahead, *args, *after)


def swapped(mine, axis_name, distance):
    size = lax.axis_size(axis_name)
    return lax.ppermute(mine, axis_name, [(a, a ^ distance) for a in range(size)])


def fits_heads(alignment_rows, pair_entries, pair_weight):
    channels, heads = pair_weight.shape
    return (
        lax.axis_size("seq") == 4
        and lax.axis_size("res") == heads == 8
        and alignment_rows.shape[0] == 2 * SLOTS
        and alignment_rows.shape[1] == pair_entries.shape[0] == 64
        and alignment_rows.shape[2] == 2 * LANES
        and pair_entries.shape[1] == channels == LANES
    )


def head_body(
    alignment_rows, pair_entries, combined_weight, output_weight, pair_weight, updated_gradient
):
    sequences, residues, width = alignment_rows.shape
    channels, heads = pair_weight.shape
    tokens = sequences * residues
    seq_size, res_size = lax.axis_size("seq"), lax.axis_size("res")
    seq_half = seq_size // 2
    total = residues * res_size
    group = 2 * res_size
    groups = [[g * group + k for k in range(group)] for g in range(seq_half)]
    scale = 1.0 / math.sqrt(width // heads * sequences * seq_size)
    res_index, seq_index = lax.axis_index("res"), lax.axis_index("seq")
    place = jnp.stack([res_index % 2, seq_index // 2, res_index // 2]).astype(jnp.int32)
    bf16, f32 = jnp.bfloat16, jnp.float32

    def across(blocks):
        return lax.all_to_all(blocks, ("seq", "res"), 0, 0, axis_index_groups=groups, tiled=True)

    x, grad, wc, wo = alignment_rows, updated_gradient, combined_weight, output_weight
    (value_blocks,) = call(
        value_kernel, [((group, 2 * residues, LANES), bf16)], x, grad, wc, wo,
        flops=8 * tokens * width * width, outside=4, late=3,
    )
    value_blocks = across(value_blocks)
    query_blocks, bias, mean, spread = call(
        functools.partial(query_kernel, scale),
        [
            ((group, 3 * residues, LANES), bf16),
            ((heads, residues, LANES), f32),
            ((residues, LANES), f32),
            ((residues, LANES), f32),
        ],
        x, wc, pair_entries, pair_weight.T,
        flops=8 * tokens * width * width, outside=3, late=1,
    )
    value_blocks, query_blocks = lax.optimization_barrier((value_blocks, query_blocks))
    query_blocks = across(query_blocks)

    quarter, half_rows = (total // 4, total), (total // 2, total)
    grad_full, grad_sent = call(
        functools.partial(grad_score_kernel, residues, residues, 0),
        [(half_rows, f32), (half_rows, bf16)],
        value_blocks, swapped(value_blocks, "res", 1),
        place=place, flops=2 * total * total * width,
    )
    grad_other = swapped(grad_sent, "seq", seq_half)
    query_blocks, grad_other = lax.optimization_barrier((query_blocks, grad_other))
    query_other = swapped(query_blocks, "res", 1)

    def scores(sent):
        return call(
            functools.partial(score_kernel, residues, 0, residues, sent), [(quarter, f32)],
            query_blocks, query_other,
            place=place, flops=total * total * width,
        )[0]

    logit_sent, logit_mine = scores(True), scores(False)
    softmax_out, probs = call(
        softmax_kernel, [(quarter, f32), (quarter, bf16)],
        logit_mine, swapped(logit_sent, "seq", seq_half),
        flops=total * total,
    )

    def products(mine, far, blocks, first_row, second_row, with_share, factor):
        rows = 2 * residues + (residues // 2 if with_share else 0)
        (out,) = call(
            functools.partial(
                product_kernel, residues, factor, first_row, second_row, with_share
            ),
            [((group, rows, LANES), bf16)],
            mine, far, swapped(mine, "res", 1), swapped(far, "res", 1), blocks,
            scratch=[pltpu.VMEM((total, total), bf16)],
            place=place, flops=4 * total * total * width,
        )
        return out

    probs_far = swapped(probs, "seq", seq_half)
    attended = products(probs, probs_far, value_blocks, 0, residues, False, 1.0)
    attended_blocks = across(attended)
    softmax_out = lax.optimization_barrier((attended, softmax_out))[1]
    grad_logits, grad_far = call(
        softmax_gradient_kernel, [(quarter, bf16), (quarter, bf16)],
        softmax_out, probs_far, grad_full, grad_other,
        place=place, flops=total * total,
    )
    grad_sums = products(grad_logits, grad_far, query_blocks, residues, 0, True, scale)
    grad_sums, attended_blocks = lax.optimization_barrier((grad_sums, attended_blocks))
    grad_blocks = across(grad_sums)

    updated, value_gate, normed, attended_sums = call(
        attended_weight_kernel,
        [
            (x.shape, bf16),
            ((tokens, 2 * width), bf16),
            ((tokens, width), bf16),
            ((width, 3 * width), bf16),
        ],
        x, grad, wc, wo, attended_blocks,
        flops=14 * tokens * width * width, outside=4,
    )
    share = pltpu.VMEM((heads, residues, LANES), f32)
    columns = 5 * width
    rows = width // res_size
    part_rows = ((res_size // 2, rows, columns), bf16)
    (pair_weight_part,) = call(
        pair_weight_kernel, [((heads, channels), f32)],
        grad_blocks, pair_entries, mean, spread,
        scratch=[share], flops=4 * tokens * width * width,
    )
    query_key, keep, send = call(
        query_weight_kernel,
        [((tokens, 2 * width), bf16), part_rows, part_rows],
        normed, attended_sums, grad_blocks,
        scratch=[pltpu.VMEM((width, columns), bf16)],
        place=place, flops=4 * tokens * width * width, after=(pair_weight_part,),
    )
    own, *sent = call(
        core_sum_kernel,
        [((rows, columns), f32)] + [((rows, columns), bf16)] * 3,
        keep, swapped(send, "res", 1), place=place,
    )
    received = [swapped(t, "res", 2 * flip) for flip, t in enumerate(sent, 1)]
    (pair_gradient,) = call(
        functools.partial(pair_kernel, 2 * residues),
        [(pair_entries.shape, bf16)],
        grad_blocks, pair_entries, pair_weight.T, bias, mean, spread,
        scratch=[share], flops=8 * tokens * width * width,
    )
    (alignment_gradient,) = call(
        alignment_kernel, [(x.shape, bf16)], x, wc, query_key, value_gate,
        flops=8 * tokens * width * width,
    )
    received, alignment_gradient = lax.optimization_barrier((received, alignment_gradient))
    (part,) = call(
        plane_sum_kernel, [((rows, columns + channels), bf16)], own, pair_weight_part, *received
    )
    def added(mine, other):
        return (mine.astype(f32) + other.astype(f32)).astype(bf16)

    other_plane = swapped(part, "seq", 1)
    part = added(part, other_plane)
    other_half = swapped(part, "seq", seq_half)
    other_half, pair_gradient = lax.optimization_barrier((other_half, pair_gradient))
    part = added(part, other_half)
    chips = [part] + [swapped(part, "res", 2 * flip) for flip in range(1, res_size // 2)]
    parts = [t for chip in chips for t in (chip, swapped(chip, "res", 1))]
    combined_gradient, output_gradient, pair_weight_gradient = call(
        output_kernel,
        [(wc.shape, f32), (wo.shape, f32), ((heads, channels), f32)],
        *parts,
        scratch=[pltpu.VMEM((len(parts), heads, channels), f32)],
        place=place,
    )
    return (
        updated,
        alignment_gradient,
        pair_gradient,
        combined_gradient,
        output_gradient,
        pair_weight_gradient.T,
    )


def body(alignment_rows, pair_entries, combined_weight, output_weight, pair_weight, updated_gradient):
    chosen = head_body if fits_heads(alignment_rows, pair_entries, pair_weight) else gathered_body
    return chosen(
        alignment_rows, pair_entries, combined_weight, output_weight, pair_weight, updated_gradient
    )


def solution(mesh):
    return jax.shard_map(
        body,
        mesh=mesh,
        in_specs=(
            P("seq", "res", None),
            P("res", "seq", None),
            P(),
            P(),
            P(),
            P("seq", "res", None),
        ),
        out_specs=(
            P("seq", "res", None),
            P("seq", "res", None),
            P("res", "seq", None),
            P(),
            P(),
            P(),
        ),
        check_vma=False,
    )
```
